128 devices in a mesh: row: 8 (over x, core), col: 16 (over y, z).
Axes of the slice: x: 4, y: 4, z: 4, core: 2. Of those that a mesh axis runs over, the one named last changes fastest.
Arguments:
- latent: bfloat16 [16, 32, 32, 16], P(None, 'row', 'col'), may hold values from -6 to 6
- condition: bfloat16 [16, 1024], replicated, may hold values from -6 to 6
- caption: bfloat16 [16, 256, 4096], P('col'), may hold values from -6 to 6
- cap_len: int32 [16], replicated, may hold values from 8 to 256, as said below
- cotangent: bfloat16 [16, 32, 32, 16], P(None, 'row', 'col'), may hold values from -6 to 6
- embed_weight: bfloat16 [3, 3, 16, 1536], replicated, may hold values from -0.5 to 0.5
- modulate_weight: bfloat16 [1024, 6144], P(None, ('row', 'col')), may hold values from -0.1875 to 0.1875
- norm_gains: float32 [7, 1536], replicated, may hold values from 0.1 to 1.9
- cross_gate: float32 [24], replicated, may hold values from -1.5 to 1.5
- qkv_weight: bfloat16 [3, 1536, 1536], P(None, 'col', 'row'), may hold values from -0.15625 to 0.15625
- text_kv_weight: bfloat16 [2, 4096, 1536], P(None, 'col', 'row'), may hold values from -0.09375 to 0.09375
- out_weight: bfloat16 [1536, 1536], P('row', 'col'), may hold values from -0.15625 to 0.15625
- gate_up_weight: bfloat16 [2, 1536, 4096], P(None, 'col', 'row'), may hold values from -0.15625 to 0.15625
- down_weight: bfloat16 [4096, 1536], P('row', 'col'), may hold values from -0.09375 to 0.09375
- unpatch_weight: bfloat16 [3, 3, 1536, 16], replicated, may hold values from -0.0546875 to 0.0546875
Outputs:
- activation: bfloat16 [16, 32, 32, 16], P(None, 'row', 'col')
- latent_grad: bfloat16 [16, 32, 32, 16], P(None, 'row', 'col')
- embed_grad: float32 [3, 3, 16, 1536], replicated
- modulate_grad: float32 [1024, 6144], P(None, ('row', 'col'))
- gains_grad: float32 [7, 1536], replicated
- gate_grad: float32 [24], replicated
- qkv_grad: float32 [3, 1536, 1536], P(None, 'col', 'row')
- text_kv_grad: float32 [2, 4096, 1536], P(None, 'col', 'row')
- out_grad: float32 [1536, 1536], P('row', 'col')
- gate_up_grad: float32 [2, 1536, 4096], P(None, 'col', 'row')
- down_grad: float32 [4096, 1536], P('row', 'col')
- unpatch_grad: float32 [3, 3, 1536, 16], replicated
The draws below stay inside these ranges and needn't reach their ends.
Inputs may be any that keep to these rules, and one draw needn't show every extreme that they name: `cap_len`: every image has 8 to 256 caption tokens; in every draw one image has exactly 256 and another exactly 8.
All inputs are finite; a program needn't handle non-finite values.
Results may differ from the reference program's by a relative error of at most 0.025.
Values may be sent and summed in bfloat16 or wider, within the bound.
No kernel may reach another device: no remote copies, remote signals or barrier semaphores. Data moves between devices by JAX's collectives and lax.ppermute only.
A program may use at most 256 MiB of HBM per device.

```python
import jax
import jax.numpy as jnp
from jax import lax

D = 1536
HEADS = 24
HD = 64
FF = 4096
TEXT = 4096
CONDW = 1024
PCH = 16
GRID = 32
LT = 256
LMIN = 8
IMAGES = 16


def draw_cap_len(key, part):
    key = jax.random.fold_in(key, 7)
    subkeys = jax.random.split(key, 3)
    uniform_draw = jax.random.randint(subkeys[0], (IMAGES,), 0, 1024)
    skewed = uniform_draw * uniform_draw // 1024 * uniform_draw // 1024
    lengths = LMIN + (LT - LMIN) * skewed // 1023
    longest = jax.random.randint(subkeys[1], (), 0, IMAGES)
    shortest = (longest + 1 + jax.random.randint(subkeys[2], (), 0, IMAGES - 1)) % IMAGES
    image_index = jnp.arange(IMAGES)
    lengths = jnp.where(image_index == longest, LT, jnp.where(image_index == shortest, LMIN, lengths))
    return lengths.astype(jnp.int32)


def level_of(own_key, extent, cuts, smallest, top_value):
    level = 1.0
    for dim, blocks in cuts:
        draws = jax.random.uniform(jax.random.fold_in(jax.random.fold_in(own_key, 6), dim), (blocks,), jnp.float32, smallest / len(cuts), top_value / len(cuts))
        level = level * jnp.repeat(jnp.exp(draws), extent[dim] // blocks).reshape((-1,) + (1,) * (len(extent) - 1 - dim))
    return level


def centred(rng, shape, width, bound, cuts=(), held_as=jnp.bfloat16):
    array = width * jax.random.normal(rng, shape, jnp.float32)
    if cuts:
        array = array * level_of(rng, shape, cuts, -0.22, 0.18)
    return jnp.clip(array, -bound, bound).astype(held_as)


def setup_inputs(seed: int = 0) -> dict:
    key_list = jax.random.split(jax.random.key(seed), 16)
    latent = centred(key_list[0], (IMAGES, GRID, GRID, PCH), 1.0, 6.0, ((1, 8), (2, 16)))
    condition = centred(key_list[1], (IMAGES, CONDW), 1.0, 6.0)
    caption = centred(key_list[2], (IMAGES, LT, TEXT), 1.0, 6.0, ((0, 16),))
    cap_len = draw_cap_len(jax.random.fold_in(key_list[15], 71), 0)
    cotangent = centred(key_list[4], (IMAGES, GRID, GRID, PCH), 1.0, 6.0, ((1, 8), (2, 16)))
    embed_weight = centred(key_list[5], (3, 3, PCH, D), (9 * PCH) ** -0.5, 0.5)
    modulate_weight = centred(key_list[6], (CONDW, 4 * D), CONDW ** -0.5, 0.1875, ((1, 128),))
    norm_gains = jnp.clip(1.0 + 0.18 * jax.random.normal(key_list[7], (7, D), jnp.float32), 0.1, 1.9)
    cross_gate = jnp.clip(jax.random.uniform(key_list[8], (HEADS,), jnp.float32, -1.5, 1.5), -1.5, 1.5)
    qkv_weight = centred(key_list[9], (3, D, D), D ** -0.5, 0.15625, ((1, 16), (2, 8)))
    text_kv_weight = centred(key_list[10], (2, TEXT, D), TEXT ** -0.5, 0.09375, ((1, 16), (2, 8)))
    out_weight = centred(key_list[11], (D, D), D ** -0.5, 0.15625, ((0, 8), (1, 16)))
    gate_up_weight = centred(key_list[12], (2, D, FF), D ** -0.5, 0.15625, ((1, 16), (2, 8)))
    down_weight = centred(key_list[13], (FF, D), FF ** -0.5, 0.09375, ((0, 8), (1, 16)))
    unpatch_weight = centred(key_list[14], (3, 3, D, PCH), (9 * D) ** -0.5, 0.0546875)
    return dict(latent=latent, condition=condition, caption=caption, cap_len=cap_len, cotangent=cotangent, embed_weight=embed_weight, modulate_weight=modulate_weight, norm_gains=norm_gains, cross_gate=cross_gate, qkv_weight=qkv_weight, text_kv_weight=text_kv_weight, out_weight=out_weight, gate_up_weight=gate_up_weight, down_weight=down_weight, unpatch_weight=unpatch_weight)


HIGHEST_PRECISION = lax.Precision.HIGHEST
EPSILON = 1e-06
ROPE_BASE = 10000.0
MASKED = -1e+30

@jax.custom_vjp
def low(v):
    return lax.optimization_barrier(v.astype(jnp.bfloat16)).astype(jnp.float32)

@jax.custom_vjp
def low_back(v):
    return v

def low_keep(v):
    return (low(v), None)

def low_pass(kept, grad):
    return (grad,)

def back_keep(v):
    return (v, None)

def back_low(kept, grad):
    return (low(grad),)
low.defvjp(low_keep, low_pass)
low_back.defvjp(back_keep, back_low)

def rms_norm(values):
    return values * lax.rsqrt(lax.optimization_barrier(jnp.mean(values * values, axis=-1, keepdims=True)) + EPSILON)

def head_norm(values, scale_gain, head_size):
    per_head = values.reshape(values.shape[:-1] + (values.shape[-1] // head_size, head_size))
    return (rms_norm(per_head) * scale_gain.reshape(per_head.shape[-2:])).reshape(values.shape)

def modulate_in(resid, scale_gain, shift_scale):
    return rms_norm(resid) * scale_gain * (1.0 + shift_scale[:, None, :])

def gated(resid, branch, scale_gain, gate_values):
    return resid + jnp.tanh(gate_values)[:, None, :] * rms_norm(branch) * scale_gain

def swiglu(gate_part, up_part):
    return jax.nn.silu(gate_part) * up_part

def rope_angles(position, quarter):
    frequency = ROPE_BASE ** (-jnp.arange(quarter, dtype=jnp.float32) / quarter)
    angle_grid = position.astype(jnp.float32)[..., None, None] * frequency
    return (jnp.cos(angle_grid), jnp.sin(angle_grid))

def rotate(values, row_table, col_table):
    quarter = values.shape[-1] // 4
    row_even = values[..., :quarter]
    row_odd = values[..., quarter:2 * quarter]
    col_even = values[..., 2 * quarter:3 * quarter]
    col_odd = values[..., 3 * quarter:]
    return jnp.concatenate([row_even * row_table[0] - row_odd * row_table[1], row_even * row_table[1] + row_odd * row_table[0], col_even * col_table[0] - col_odd * col_table[1], col_even * col_table[1] + col_odd * col_table[0]], axis=-1)

def conv_taps(field, kernel):
    grid_rows = field.shape[1]
    grid_cols = field.shape[2]
    padded = jnp.pad(field, ((0, 0), (1, 1), (1, 1), (0, 0)))
    result = jnp.zeros(field.shape[:3] + (kernel.shape[3],), field.dtype)
    for row_tap in range(3):
        for col_tap in range(3):
            window = padded[:, row_tap:row_tap + grid_rows, col_tap:col_tap + grid_cols, :]
            result = result + jnp.einsum('gijc,ce->gije', window, kernel[row_tap, col_tap], precision=HIGHEST_PRECISION)
    return result

def softmax_rows(scores):
    row_peak = lax.optimization_barrier(jnp.max(scores, axis=-1, keepdims=True))
    exponent = jnp.exp(scores - row_peak)
    return exponent / lax.optimization_barrier(jnp.sum(exponent, axis=-1, keepdims=True))

def head_attention(pieces):
    query_rows, key_rows, value_rows, text_key_rows, text_value_rows, text_mask, gate_value = pieces
    score_scale = HD ** (-0.5)
    scores = low_back(jnp.dot(query_rows, key_rows.T, precision=HIGHEST_PRECISION) * score_scale)
    own_out = jnp.dot(low(softmax_rows(scores)), value_rows, precision=HIGHEST_PRECISION)
    text_raw_scores = low_back(jnp.dot(query_rows, text_key_rows.T, precision=HIGHEST_PRECISION) * score_scale)
    text_scores = jnp.where(text_mask[None, :], text_raw_scores, MASKED)
    text_out = jnp.dot(low(softmax_rows(text_scores)), text_value_rows, precision=HIGHEST_PRECISION)
    return low(low_back(own_out + gate_value * text_out))

def block(params, latent, condition, caption, text_mask):
    embed_weight, modulate_weight, norm_gains, cross_gate, qkv_weight, text_kv_weight, out_weight, gate_up_weight, down_weight, unpatch_weight = params
    group_size = latent.shape[0]
    tokens_image = GRID * GRID
    x_first = low_back(conv_taps(latent, embed_weight)).reshape(group_size, tokens_image, D)
    modulation = jnp.dot(low(jax.nn.silu(condition)), modulate_weight, precision=HIGHEST_PRECISION).reshape(group_size, 4, D)
    h_first = low(modulate_in(x_first, norm_gains[0], modulation[:, 0]))
    qkv_raw = jnp.einsum('gnd,sde->sgne', h_first, qkv_weight, precision=HIGHEST_PRECISION)
    token_place = jnp.arange(tokens_image)
    row_table = rope_angles(token_place // GRID, HD // 4)
    col_table = rope_angles(token_place % GRID, HD // 4)

    def query_side(raw, scale_gain):
        normed = head_norm(low_back(raw), scale_gain, HD).reshape(group_size, tokens_image, HEADS, HD)
        return low(low_back(rotate(normed, row_table, col_table)))
    queries = query_side(qkv_raw[0], norm_gains[4])
    key_heads = query_side(qkv_raw[1], norm_gains[5])
    value_heads = low(low_back(qkv_raw[2])).reshape(group_size, tokens_image, HEADS, HD)
    text_raw = jnp.einsum('gtc,sce->sgte', caption, text_kv_weight, precision=HIGHEST_PRECISION)
    text_keys = low(head_norm(low_back(text_raw[0]), norm_gains[6], HD)).reshape(group_size, LT, HEADS, HD)
    text_values = low(low_back(text_raw[1])).reshape(group_size, LT, HEADS, HD)

    def heads_first(tensor_in):
        return tensor_in.transpose(0, 2, 1, 3).reshape(group_size * HEADS, tensor_in.shape[1], HD)
    mixed = lax.map(jax.checkpoint(head_attention), (heads_first(queries), heads_first(key_heads), heads_first(value_heads), heads_first(text_keys), heads_first(text_values), jnp.repeat(text_mask, HEADS, axis=0), jnp.tile(jnp.tanh(cross_gate), group_size)))
    mixed = mixed.reshape(group_size, HEADS, tokens_image, HD).transpose(0, 2, 1, 3).reshape(group_size, tokens_image, D)
    attn_out = low_back(jnp.einsum('gnd,de->gne', mixed, out_weight, precision=HIGHEST_PRECISION))
    x_mid = gated(x_first, attn_out, norm_gains[1], modulation[:, 1])
    h_second = low(modulate_in(x_mid, norm_gains[2], modulation[:, 2]))
    gate_up = jnp.einsum('gnd,sdf->sgnf', h_second, gate_up_weight, precision=HIGHEST_PRECISION)
    hidden = low(swiglu(low_back(gate_up[0]), low_back(gate_up[1])))
    ffn_out = low_back(jnp.einsum('gnf,fd->gnd', hidden, down_weight, precision=HIGHEST_PRECISION))
    x_last = gated(x_mid, ffn_out, norm_gains[3], modulation[:, 3])
    return conv_taps(low(x_last).reshape(group_size, GRID, GRID, D), unpatch_weight)

def reference(latent, condition, caption, cap_len, cotangent, embed_weight, modulate_weight, norm_gains, cross_gate, qkv_weight, text_kv_weight, out_weight, gate_up_weight, down_weight, unpatch_weight):
    params = tuple((weight.astype(jnp.float32) for weight in (embed_weight, modulate_weight, norm_gains, cross_gate, qkv_weight, text_kv_weight, out_weight, gate_up_weight, down_weight, unpatch_weight)))
    text_mask = jnp.arange(LT)[None, :] < cap_len[:, None]
    group_size = 4
    group_count = IMAGES // group_size

    def regroup(tensor_in):
        return tensor_in.reshape((group_count, group_size) + tensor_in.shape[1:])

    def one_group(totals, inputs):
        latent_group, condition_group, caption_group, mask_group, cotangent_group = inputs

        def forward(param_set, latent_in):
            return block(param_set, latent_in, condition_group, caption_group, mask_group)
        activation, pull = jax.vjp(forward, params, latent_group)
        param_grads, latent_grad = pull(cotangent_group)
        return (jax.tree.map(jnp.add, totals, param_grads), (activation, latent_grad))
    initial = jax.tree.map(jnp.zeros_like, params)
    totals, (activation, latent_grad) = lax.scan(one_group, initial, (regroup(latent.astype(jnp.float32)), regroup(condition.astype(jnp.float32)), regroup(caption.astype(jnp.float32)), regroup(text_mask), regroup(cotangent.astype(jnp.float32))))
    activation = activation.reshape(IMAGES, GRID, GRID, PCH).astype(jnp.bfloat16)
    latent_grad = latent_grad.reshape(IMAGES, GRID, GRID, PCH).astype(jnp.bfloat16)
    return (activation, latent_grad, totals[0], totals[1], totals[2], totals[3], totals[4], totals[5], totals[6], totals[7], totals[8], totals[9])
```

```python
import math
from functools import partial

import jax
import jax.numpy as jnp
import numpy as np
from jax import lax
from jax.experimental import pallas as pl
from jax.experimental.pallas import tpu as pltpu
from jax.sharding import PartitionSpec as P

HEADS = 24
HD = 64
GRID = 32
TOKENS = GRID * GRID
EPSILON = 1e-06
ROPE_BASE = 10000.0
MASKED = -1e30
F32 = jnp.float32
BF16 = jnp.bfloat16
ROWS = 8
COLS = 16
QUERY_BLOCK = 256


def dot(left, right, contract):
    return lax.dot_general(
        left, right, ((contract[:1], contract[1:]), ((), ())), preferred_element_type=F32
    )


def row_pairs(dx, dc):
    return [
        (((x + dx) % 4) * 2 + (c + dc) % 2, x * 2 + c) for x in range(4) for c in range(2)
    ]


def row_pairs_to(dx, dc):
    return [(dst, src) for src, dst in row_pairs(dx, dc)]


def gather_near(piece):
    quad = jnp.stack([piece] + [lax.ppermute(piece, "row", row_pairs(d, 0)) for d in (1, 2, 3)])
    other = lax.ppermute(quad, "row", row_pairs(0, 1))
    return jnp.concatenate([quad, other])


def scatter_near(parts):
    other = lax.ppermute(parts[4:], "row", row_pairs(0, 1))
    near = parts[:4].astype(F32) + other.astype(F32)
    low = near.astype(BF16)
    total = near[0]
    for d in (1, 2, 3):
        total = total + lax.ppermute(low[d], "row", row_pairs_to(d, 0)).astype(F32)
    return total


def rope_tables():
    quarter = HD // 4
    frequency = np.float32(ROPE_BASE) ** (-np.arange(quarter, dtype=np.float32) / np.float32(quarter))
    place = np.arange(TOKENS)
    row = frequency[:, None] * (place // GRID).astype(np.float32)[None, :]
    col = frequency[:, None] * (place % GRID).astype(np.float32)[None, :]
    return np.stack([np.cos(row), np.sin(row), np.cos(col), np.sin(col)]).astype(np.float32)


def turn(v, table, sign):
    a, b, c, d = (v[k * 16 : (k + 1) * 16] for k in range(4))
    cr, sr, cc, sc = table[0], table[1] * sign, table[2], table[3] * sign
    return jnp.concatenate([a * cr - b * sr, a * sr + b * cr, c * cc - d * sc, c * sc + d * cc], 0)


def column_rms(v):
    return lax.rsqrt(jnp.mean(v * v, axis=0, keepdims=True) + EPSILON)


def normed(v, gain):
    return v * column_rms(v) * gain


def column_rms_back(v, u):
    scale = column_rms(v)
    return (u - v * (jnp.mean(u * v, axis=0, keepdims=True) * scale * scale)) * scale


def attend_kernel(
    cap_ref, gate_ref, raw_ref, text_ref, gain_ref, table_ref, mixed_ref, lse_ref
):
    table = table_ref[...]
    head = pl.program_id(0)
    gate = gate_ref[head]
    q = turn(normed(raw_ref[0], gain_ref[0]), table, 1.0).astype(BF16) * jnp.asarray(0.125, BF16)
    k = turn(normed(raw_ref[1], gain_ref[1]), table, 1.0).astype(BF16)
    v = raw_ref[2].astype(BF16)
    tk = normed(text_ref[0], gain_ref[2]).astype(BF16)
    tv = text_ref[1].astype(BF16)
    slots = tk.shape[1]
    mask = lax.broadcasted_iota(jnp.int32, (slots, QUERY_BLOCK), 0) < cap_ref[0]
    for first in range(0, TOKENS, QUERY_BLOCK):
        qb = q[:, first : first + QUERY_BLOCK]
        e = jnp.exp(dot(k, qb, (0, 0)))
        total = jnp.sum(e, axis=0, keepdims=True)
        own = dot(v, e.astype(BF16), (1, 0)) / total
        te = jnp.exp(jnp.where(mask, dot(tk, qb, (0, 0)), MASKED))
        text_total = jnp.sum(te, axis=0, keepdims=True)
        text = dot(tv, te.astype(BF16), (1, 0)) / text_total
        mixed_ref[:, first : first + QUERY_BLOCK] = (own + gate * text).astype(BF16)
        lse_ref[0:1, first : first + QUERY_BLOCK] = jnp.log(total)
        lse_ref[1:2, first : first + QUERY_BLOCK] = jnp.log(text_total)


def attend(raw, text_raw, gains, table, cap, gates):
    heads = raw.shape[1]
    slots = text_raw.shape[3]
    return pl.pallas_call(
        attend_kernel,
        grid_spec=pltpu.PrefetchScalarGridSpec(
            num_scalar_prefetch=2,
            grid=(heads,),
            in_specs=[
                pl.BlockSpec((3, None, HD, TOKENS), lambda h, *_: (0, h, 0, 0)),
                pl.BlockSpec((2, None, HD, slots), lambda h, *_: (0, h, 0, 0)),
                pl.BlockSpec((3, None, HD, 1), lambda h, *_: (0, h, 0, 0)),
                pl.BlockSpec((4, 16, TOKENS), lambda h, *_: (0, 0, 0)),
            ],
            out_specs=[
                pl.BlockSpec((None, HD, TOKENS), lambda h, *_: (h, 0, 0)),
                pl.BlockSpec((None, 8, TOKENS), lambda h, *_: (h, 0, 0)),
            ],
        ),
        out_shape=[
            jax.ShapeDtypeStruct((heads, HD, TOKENS), BF16),
            jax.ShapeDtypeStruct((heads, 8, TOKENS), F32),
        ],
        compiler_params=pltpu.CompilerParams(vmem_limit_bytes=48 * 2**20),
        cost_estimate=pl.CostEstimate(
            flops=heads * 4 * HD * TOKENS * (TOKENS + slots),
            bytes_accessed=heads * HD * TOKENS * 16,
            transcendentals=heads * TOKENS * (TOKENS + slots),
        ),
    )(cap, gates, raw, text_raw, gains, table)


def attend_back_kernel(
    cap_ref, gate_ref, raw_ref, text_ref, gain_ref, table_ref, lse_ref, grad_ref,
    d_raw_ref, d_text_ref, d_gain_ref, dv_ref, dk_ref, dq_ref, dtv_ref, dtk_ref,
):
    table = table_ref[...]
    head = pl.program_id(0)
    gate = gate_ref[head]
    q = turn(normed(raw_ref[0], gain_ref[0]), table, 1.0).astype(BF16) * jnp.asarray(0.125, BF16)
    k = turn(normed(raw_ref[1], gain_ref[1]), table, 1.0).astype(BF16)
    v = raw_ref[2].astype(BF16)
    tk = normed(text_ref[0], gain_ref[2]).astype(BF16)
    tv = text_ref[1].astype(BF16)
    slots = tk.shape[1]
    mask = lax.broadcasted_iota(jnp.int32, (slots, QUERY_BLOCK), 0) < cap_ref[0]
    gate_sum = jnp.zeros((HD, QUERY_BLOCK), F32)
    for first in range(0, TOKENS, QUERY_BLOCK):
        here = slice(first, first + QUERY_BLOCK)
        qb = q[:, here]
        gb = grad_ref[:, here]
        p = jnp.exp(dot(k, qb, (0, 0)) - lse_ref[0:1, here])
        dv = dot(gb, p.astype(BF16), (1, 1))
        pd = p * dot(v, gb, (0, 0))
        ds = (pd - p * jnp.sum(pd, axis=0, keepdims=True)).astype(BF16)
        dq = dot(k, ds, (1, 0))
        dk = dot(qb, ds, (1, 1))
        tp = jnp.exp(jnp.where(mask, dot(tk, qb, (0, 0)), MASKED) - lse_ref[1:2, here])
        tpb = tp.astype(BF16)
        dtv = dot(gb, tpb, (1, 1))
        gate_sum = gate_sum + gb.astype(F32) * dot(tv, tpb, (1, 0))
        tpd = tp * dot(tv, gb, (0, 0)) * gate
        dts = (tpd - tp * jnp.sum(tpd, axis=0, keepdims=True)).astype(BF16)
        dq_ref[:, here] = dq + dot(tk, dts, (1, 0))
        dtk = dot(qb, dts, (1, 1))
        if first == 0:
            dv_ref[...] = dv
            dk_ref[...] = dk
            dtv_ref[...] = dtv
            dtk_ref[...] = dtk
        else:
            dv_ref[...] += dv
            dk_ref[...] += dk
            dtv_ref[...] += dtv
            dtk_ref[...] += dtk

    def raw_back(which, d_turned):
        spun = turn(d_turned.astype(BF16).astype(F32), table, -1.0)
        values = raw_ref[which]
        d_raw_ref[which] = column_rms_back(values, spun * gain_ref[which]).astype(BF16)
        d_gain_ref[which] = jnp.sum(values * column_rms(values) * spun, axis=1, keepdims=True)

    raw_back(0, dq_ref[...] * 0.125)
    raw_back(1, dk_ref[...])
    d_raw_ref[2] = dv_ref[...].astype(BF16)
    values = text_ref[0]
    d_tk = dtk_ref[...]
    d_text_ref[0] = column_rms_back(values, d_tk * gain_ref[2]).astype(BF16)
    d_gain_ref[2] = jnp.sum(values * column_rms(values) * d_tk, axis=1, keepdims=True)
    d_text_ref[1] = (dtv_ref[...] * gate).astype(BF16)
    d_gain_ref[3] = jnp.sum(gate_sum, axis=1, keepdims=True)


def attend_back(raw, text_raw, gains, table, lse, grads, cap, gates):
    heads = raw.shape[1]
    slots = text_raw.shape[3]
    return pl.pallas_call(
        attend_back_kernel,
        grid_spec=pltpu.PrefetchScalarGridSpec(
            num_scalar_prefetch=2,
            grid=(heads,),
            in_specs=[
                pl.BlockSpec((3, None, HD, TOKENS), lambda h, *_: (0, h, 0, 0)),
                pl.BlockSpec((2, None, HD, slots), lambda h, *_: (0, h, 0, 0)),
                pl.BlockSpec((3, None, HD, 1), lambda h, *_: (0, h, 0, 0)),
                pl.BlockSpec((4, 16, TOKENS), lambda h, *_: (0, 0, 0)),
                pl.BlockSpec((None, 8, TOKENS), lambda h, *_: (h, 0, 0)),
                pl.BlockSpec((None, HD, TOKENS), lambda h, *_: (h, 0, 0)),
            ],
            out_specs=[
                pl.BlockSpec((3, None, HD, TOKENS), lambda h, *_: (0, h, 0, 0)),
                pl.BlockSpec((2, None, HD, slots), lambda h, *_: (0, h, 0, 0)),
                pl.BlockSpec((4, None, HD, 1), lambda h, *_: (0, h, 0, 0)),
            ],
            scratch_shapes=[
                pltpu.VMEM((HD, TOKENS), F32),
                pltpu.VMEM((HD, TOKENS), F32),
                pltpu.VMEM((HD, TOKENS), F32),
                pltpu.VMEM((HD, slots), F32),
                pltpu.VMEM((HD, slots), F32),
            ],
        ),
        out_shape=[
            jax.ShapeDtypeStruct((3, heads, HD, TOKENS), BF16),
            jax.ShapeDtypeStruct((2, heads, HD, slots), BF16),
            jax.ShapeDtypeStruct((4, heads, HD, 1), F32),
        ],
        compiler_params=pltpu.CompilerParams(vmem_limit_bytes=48 * 2**20),
        cost_estimate=pl.CostEstimate(
            flops=heads * 10 * HD * TOKENS * (TOKENS + slots),
            bytes_accessed=heads * HD * TOKENS * 24,
            transcendentals=heads * TOKENS * (TOKENS + slots),
        ),
    )(cap, gates, raw, text_raw, gains, table, lse, grads)


def grid_shift(field, di, dj):
    step = di * GRID + dj
    reach = GRID + 1
    padded = jnp.pad(field, ((0, 0), (reach, reach)))
    moved = lax.slice_in_dim(padded, reach + step, reach + step + TOKENS, axis=1)
    if dj == 0:
        return moved
    column = np.arange(TOKENS) % GRID + dj
    inside = jnp.asarray(((column >= 0) & (column < GRID)).astype(np.float32), field.dtype)
    return moved * inside


def taps_of(field, sign):
    return jnp.concatenate(
        [grid_shift(field, sign * (a - 1), sign * (b - 1)) for a in range(3) for b in range(3)], 0
    )


def taps_sum(taps, sign):
    channels = taps.shape[0] // 9
    total = 0.0
    for a in range(3):
        for b in range(3):
            first = (a * 3 + b) * channels
            total = total + grid_shift(
                taps[first : first + channels], sign * (a - 1), sign * (b - 1)
            )
    return total


def row_rms(v):
    return lax.rsqrt(jnp.mean(v * v, axis=-1, keepdims=True) + EPSILON)


def row_rms_back(v, scale, u):
    return (u - v * (jnp.mean(u * v, axis=-1, keepdims=True) * scale * scale)) * scale


def local(
    latent, condition, caption, cap_len, cotangent, embed_weight, modulate_weight, norm_gains,
    cross_gate, qkv_weight, text_kv_weight, out_weight, gate_up_weight, down_weight, unpatch_weight,
):
    channels = latent.shape[3]
    width = embed_weight.shape[3]
    local_width = qkv_weight.shape[2]
    heads = local_width // HD
    hidden_width = down_weight.shape[0]
    row_at = lax.axis_index("row")
    col_at = lax.axis_index("col")
    block = TOKENS // ROWS
    tile = latent.shape[1] * latent.shape[2] * channels

    qkv_whole = lax.all_to_all(
        jnp.broadcast_to(qkv_weight, (COLS,) + qkv_weight.shape), "col", 0, 0
    )
    qkv_whole = qkv_whole.transpose(1, 0, 2, 3).reshape(3, width, local_width)
    text_whole = lax.all_gather(text_kv_weight, "col", axis=1, tiled=True)
    out_rows = lax.all_gather(out_weight, "col", axis=1, tiled=True)
    out_whole = gather_near(out_rows).reshape(width, width)
    gate_up_whole = lax.all_gather(gate_up_weight, "col", axis=1, tiled=True)
    down_whole = lax.all_gather(down_weight, "col", axis=1, tiled=True)

    cond_low = jax.nn.silu(condition.astype(F32)).astype(BF16)
    mod_piece = jnp.dot(cond_low, modulate_weight, preferred_element_type=F32)
    mod_columns = mod_piece.shape[1]
    images = latent.shape[0]
    packed = jnp.concatenate(
        [
            latent.reshape(images, tile).astype(F32),
            cotangent.reshape(images, tile).astype(F32),
            jnp.pad(mod_piece, ((0, 0), (0, 128 - mod_columns))),
        ],
        axis=1,
    )
    packed = lax.all_to_all(packed, "col", 0, 0, tiled=True)
    packed = lax.all_gather(packed, "row", axis=0)

    def image_of(values):
        return (
            values.reshape(ROWS, COLS, 4, 2, channels).transpose(4, 0, 2, 1, 3).reshape(channels, TOKENS)
        )

    latent_image = image_of(packed[:, :, :tile])
    cotangent_image = image_of(packed[:, :, tile : 2 * tile])
    modulation = packed[:, :, 2 * tile : 2 * tile + mod_columns].reshape(4, 1, width)
    scale_attn, gate_attn, scale_ffn, gate_ffn = (modulation[k] for k in range(4))
    gains = [norm_gains[k][None, :] for k in range(4)]
    gate_attn = jnp.tanh(gate_attn)
    gate_ffn = jnp.tanh(gate_ffn)

    patches = taps_of(latent_image, 1).astype(BF16)
    x_first = dot(patches, embed_weight.reshape(9 * channels, width), (0, 0))
    first_scale = row_rms(x_first)
    h_first = (x_first * first_scale * (gains[0] * (1.0 + scale_attn))).astype(BF16)

    raw = jnp.einsum("sde,nd->sen", qkv_whole, h_first, preferred_element_type=F32).reshape(
        3, heads, HD, TOKENS
    )
    caption_rows = caption[0]
    text_raw = jnp.einsum(
        "sce,tc->set", text_whole, caption_rows, preferred_element_type=F32
    ).reshape(2, heads, HD, caption_rows.shape[0])
    head_gains = lax.dynamic_slice(norm_gains, (4, row_at * local_width), (3, local_width)).reshape(
        3, heads, HD, 1
    )
    head_gates = jnp.tanh(lax.dynamic_slice_in_dim(cross_gate, row_at * heads, heads))
    cap = lax.dynamic_slice_in_dim(cap_len, col_at, 1)
    table = jnp.asarray(rope_tables())
    mixed, lse = attend(raw, text_raw, head_gains, table, cap, head_gates)

    mixed_all = gather_near(mixed.reshape(local_width, TOKENS)).reshape(width, TOKENS)
    attn_out = dot(mixed_all, out_whole, (0, 0))
    attn_scale = row_rms(attn_out)
    x_mid = x_first + (gate_attn * gains[1]) * (attn_out * attn_scale)
    mid_scale = row_rms(x_mid)
    h_second = (x_mid * mid_scale * (gains[2] * (1.0 + scale_ffn))).astype(BF16)

    gate_pre = jnp.dot(h_second, gate_up_whole[0], preferred_element_type=F32)
    up_pre = jnp.dot(h_second, gate_up_whole[1], preferred_element_type=F32)
    hidden = (jax.nn.silu(gate_pre) * up_pre).astype(BF16)
    ffn_part = jnp.dot(hidden, down_whole, preferred_element_type=F32).astype(BF16)
    ffn_out = lax.psum_scatter(ffn_part, "row", scatter_dimension=0, tiled=True).astype(F32)

    cot_taps = taps_of(cotangent_image, -1).astype(BF16)
    unpatch_back = unpatch_weight.transpose(0, 1, 3, 2).reshape(9 * channels, width)
    d_last = dot(cot_taps, unpatch_back, (0, 0))
    own_cot = lax.dynamic_slice_in_dim(cot_taps, row_at * block, block, 1)
    d_last_own = lax.dynamic_slice_in_dim(d_last, row_at * block, block, 0)
    x_mid_own = lax.dynamic_slice_in_dim(x_mid, row_at * block, block, 0)
    ffn_scale = row_rms(ffn_out)
    ffn_normed = ffn_out * ffn_scale
    d_ffn_own = row_rms_back(ffn_out, ffn_scale, gate_ffn * gains[3] * d_last_own).astype(BF16)
    d_ffn = lax.all_gather(d_ffn_own, "row", axis=0, tiled=True)
    last_low = (x_mid_own + gate_ffn * gains[3] * ffn_normed).astype(BF16)
    last_taps = dot(unpatch_back, last_low, (1, 1))
    unpatch_sum = dot(own_cot, last_low, (1, 0))
    ffn_terms = jnp.sum(ffn_normed * d_last_own, axis=0)
    d_gain_three = gate_ffn[0] * ffn_terms
    d_gate_ffn = (1.0 - gate_ffn[0] * gate_ffn[0]) * gains[3][0] * ffn_terms
    activation_image = taps_sum(
        lax.dynamic_update_slice(
            jnp.zeros((9 * channels, TOKENS), F32), last_taps, (0, row_at * block)
        ),
        1,
    )

    d_hidden = dot(d_ffn, down_whole, (1, 1))
    down_sum = dot(hidden, d_ffn, (0, 0))
    sigma = jax.nn.sigmoid(gate_pre)
    d_gate_pre = (d_hidden * up_pre * sigma * (1.0 + gate_pre * (1.0 - sigma))).astype(BF16)
    d_up_pre = (d_hidden * gate_pre * sigma).astype(BF16)
    gate_sum = dot(h_second, d_gate_pre, (0, 0))
    up_sum = dot(h_second, d_up_pre, (0, 0))
    d_h_second = dot(d_gate_pre, gate_up_whole[0], (1, 1)) + dot(
        d_up_pre, gate_up_whole[1], (1, 1)
    )
    own_rows = (lax.broadcasted_iota(jnp.int32, (TOKENS, 1), 0) // block) == row_at
    mid_terms = x_mid * mid_scale * d_h_second
    mid_sums = jnp.sum(mid_terms, axis=0)
    d_gain_two = (1.0 + scale_ffn[0]) * mid_sums
    d_scale_ffn = gains[2][0] * mid_sums
    d_mid = row_rms_back(
        x_mid, mid_scale, (gains[2] * (1.0 + scale_ffn)) * d_h_second
    ) + jnp.where(own_rows, d_last, 0.0)
    attn_terms = jnp.sum(attn_out * attn_scale * d_mid, axis=0)
    d_gain_one = gate_attn[0] * attn_terms
    d_gate_attn = (1.0 - gate_attn[0] * gate_attn[0]) * gains[1][0] * attn_terms
    d_attn = row_rms_back(attn_out, attn_scale, (gate_attn * gains[1]) * d_mid).astype(BF16)
    d_mixed_parts = dot(out_whole, d_attn, (1, 1)).astype(BF16)
    d_mixed = scatter_near(d_mixed_parts.reshape(ROWS, local_width, TOKENS)).astype(BF16)
    out_parts = dot(mixed_all, d_attn, (1, 0)).astype(BF16)
    out_sum = scatter_near(out_parts.reshape(ROWS, local_width, width)).astype(BF16)

    d_raw, d_text, d_head = attend_back(
        raw, text_raw, head_gains, table, lse, d_mixed.reshape(heads, HD, TOKENS), cap, head_gates
    )
    d_text = d_text.reshape(2, local_width, -1)
    text_sum = jnp.einsum("tc,set->sce", caption_rows, d_text, preferred_element_type=F32)
    d_qkv = d_raw.reshape(3, local_width, TOKENS)
    qkv_sum = jnp.einsum("nd,sen->dse", h_first, d_qkv, preferred_element_type=F32)
    d_h_first = sum(dot(d_qkv[s], qkv_whole[s], (0, 1)) for s in range(3))
    first_sums = jnp.sum(x_first * first_scale * d_h_first, axis=0)
    d_gain_zero = (1.0 + scale_attn[0]) * first_sums
    d_scale_attn = gains[0][0] * first_sums
    d_first = (
        d_mid + row_rms_back(x_first, first_scale, (gains[0] * (1.0 + scale_attn)) * d_h_first)
    ).astype(BF16)
    embed_sum = dot(patches, d_first, (1, 0))
    embed_back = embed_weight.reshape(9 * channels, width)
    latent_taps = dot(embed_back, d_first, (1, 1))
    latent_image_grad = taps_sum(latent_taps, -1)

    d_modulation = jnp.stack([d_scale_attn, d_gate_attn, d_scale_ffn, d_gate_ffn])

    def blocks_of(values):
        return values.reshape(channels, ROWS, block).transpose(1, 0, 2).reshape(ROWS, -1)

    row_pack = jnp.concatenate(
        [blocks_of(activation_image), blocks_of(latent_image_grad), d_modulation.reshape(ROWS, -1)],
        axis=1,
    )
    row_pack = jnp.sum(lax.all_to_all(row_pack, "row", 0, 0, tiled=True), axis=0)
    field = channels * block

    def tiles_of(values):
        return (
            values.reshape(channels, 4, COLS, 2).transpose(2, 1, 3, 0).reshape(COLS, -1)
        )

    col_pack = jnp.concatenate(
        [
            tiles_of(row_pack[:field]),
            tiles_of(row_pack[field : 2 * field]),
            row_pack[2 * field :].reshape(COLS, mod_columns),
        ],
        axis=1,
    )
    col_pack = lax.all_to_all(col_pack, "col", 0, 0, tiled=True)
    activation = col_pack[:, :tile].reshape(latent.shape).astype(BF16)
    latent_grad = col_pack[:, tile : 2 * tile].reshape(latent.shape).astype(BF16)
    modulate_grad = lax.dot_general(
        cond_low.astype(F32),
        col_pack[:, 2 * tile :],
        (((0,), (0,)), ((), ())),
        precision=lax.Precision.HIGHEST,
        preferred_element_type=F32,
    )

    head_place = row_at * local_width
    head_rows = lax.dynamic_update_slice(
        jnp.zeros((3, width), F32), d_head[:3].reshape(3, local_width), (0, head_place)
    )
    gate_part = jnp.sum(d_head[3], axis=(1, 2)) * (1.0 - head_gates * head_gates)
    gate_row = lax.dynamic_update_slice(jnp.zeros((1, width), F32), gate_part[None], (0, row_at * heads))
    shared = jnp.concatenate(
        [
            embed_sum,
            unpatch_sum,
            jnp.stack([d_gain_zero, d_gain_one, d_gain_two, d_gain_three]),
            head_rows,
            gate_row,
            jnp.zeros((24, width), F32),
        ]
    )
    shared = shared.astype(BF16).reshape(ROWS, 480, 128)
    shared = jnp.sum(lax.all_to_all(shared, "row", 0, 0).astype(F32), axis=0)
    shared = shared.astype(BF16).reshape(COLS, 30, 128)
    shared = jnp.sum(lax.all_to_all(shared, "col", 0, 0).astype(F32), axis=0).astype(BF16)
    shared = lax.all_gather(shared, "col", axis=0)
    shared = lax.all_gather(shared, "row", axis=0).reshape(320, width).astype(F32)
    taps = 9 * channels
    embed_grad = shared[:taps].reshape(embed_weight.shape)
    unpatch_grad = shared[taps : 2 * taps].reshape(3, 3, channels, width).transpose(0, 1, 3, 2)
    gains_grad = shared[2 * taps : 2 * taps + 7]
    gate_grad = shared[2 * taps + 7, :HEADS]

    def over_col(values, axis):
        return lax.psum_scatter(
            values.astype(BF16), "col", scatter_dimension=axis, tiled=True
        ).astype(F32)

    gate_up_grad = over_col(jnp.stack([gate_sum.astype(BF16), up_sum.astype(BF16)]), 1)
    down_grad = over_col(down_sum, 1)
    text_kv_grad = over_col(text_sum, 1)
    out_grad = over_col(out_sum, 1)
    qkv_parts = qkv_sum.astype(BF16).reshape(COLS, width // COLS, 3 * local_width)
    qkv_grad = jnp.sum(lax.all_to_all(qkv_parts, "col", 0, 0).astype(F32), axis=0)
    qkv_grad = qkv_grad.reshape(width // COLS, 3, local_width).transpose(1, 0, 2)
    return (
        activation, latent_grad, embed_grad, modulate_grad, gains_grad, gate_grad,
        qkv_grad, text_kv_grad, out_grad, gate_up_grad, down_grad, unpatch_grad,
    )


def solution(mesh):
    placed = (
        P(None, "row", "col", None),
        P(),
        P("col", None, None),
        P(),
        P(None, "row", "col", None),
        P(),
        P(None, ("row", "col")),
        P(),
        P(),
        P(None, "col", "row"),
        P(None, "col", "row"),
        P("row", "col"),
        P(None, "col", "row"),
        P("row", "col"),
        P(),
    )
    return jax.shard_map(
        local,
        mesh=mesh,
        in_specs=placed,
        out_specs=(
            P(None, "row", "col", None),
            P(None, "row", "col", None),
            P(),
            P(None, ("row", "col")),
            P(),
            P(),
            P(None, "col", "row"),
            P(None, "col", "row"),
            P("row", "col"),
            P(None, "col", "row"),
            P("row", "col"),
            P(),
        ),
        check_vma=False,
    )
```

```python
import math
from functools import partial

import jax
import jax.numpy as jnp
import numpy as np
from jax import lax
from jax.experimental import pallas as pl
from jax.experimental.pallas import tpu as pltpu
from jax.sharding import PartitionSpec as P

HEADS = 24
HD = 64
GRID = 32
TOKENS = GRID * GRID
EPSILON = 1e-06
ROPE_BASE = 10000.0
MASKED = -1e30
F32 = jnp.float32
BF16 = jnp.bfloat16
ROWS = 8
COLS = 16
QUERY_BLOCK = 256
BLOCK = TOKENS // ROWS
PAIR = 2 * BLOCK
VMEM = 56 * 2**20


def dot(left, right, contract):
    return lax.dot_general(
        left, right, ((contract[:1], contract[1:]), ((), ())), preferred_element_type=F32
    )


def row_pairs(dx, dc):
    return [
        (((x + dx) % 4) * 2 + (c + dc) % 2, x * 2 + c) for x in range(4) for c in range(2)
    ]


def row_pairs_to(dx, dc):
    return [(dst, src) for src, dst in row_pairs(dx, dc)]


def gather_near(piece):
    quad = jnp.stack([piece] + [lax.ppermute(piece, "row", row_pairs(d, 0)) for d in (1, 2, 3)])
    return quad, lax.ppermute(quad, "row", row_pairs(0, 1))


def scatter_near(own, other):
    other = lax.ppermute(other, "row", row_pairs(0, 1))
    near = [(own[d].astype(F32) + other[d].astype(F32)).astype(BF16) for d in range(4)]
    return [near[0]] + [lax.ppermute(near[d], "row", row_pairs_to(d, 0)) for d in (1, 2, 3)]


def send_all(piece, axis):
    copies = jnp.broadcast_to(piece, (lax.axis_size(axis),) + piece.shape)
    return lax.all_to_all(copies, axis, 0, 0)


def after(value, *others):
    return lax.optimization_barrier((value,) + others)[0]


def rope_tables():
    quarter = HD // 4
    frequency = np.float32(ROPE_BASE) ** (-np.arange(quarter, dtype=np.float32) / np.float32(quarter))
    place = np.arange(TOKENS)
    row = frequency[:, None] * (place // GRID).astype(np.float32)[None, :]
    col = frequency[:, None] * (place % GRID).astype(np.float32)[None, :]
    return np.stack([np.cos(row), np.sin(row), np.cos(col), np.sin(col)]).astype(np.float32)


def turn(v, table, sign):
    a, b, c, d = (v[k * 16 : (k + 1) * 16] for k in range(4))
    cr, sr, cc, sc = table[0], table[1] * sign, table[2], table[3] * sign
    return jnp.concatenate([a * cr - b * sr, a * sr + b * cr, c * cc - d * sc, c * sc + d * cc], 0)


def column_rms(v):
    return lax.rsqrt(jnp.mean(v * v, axis=0, keepdims=True) + EPSILON)


def normed(v, gain):
    return v * column_rms(v) * gain


def column_rms_back(v, u):
    scale = column_rms(v)
    return (u - v * (jnp.mean(u * v, axis=0, keepdims=True) * scale * scale)) * scale


def whole(shape):
    zeros = (0,) * len(shape)
    return pl.BlockSpec(shape, lambda *_: zeros, pipeline_mode=pl.Buffered(1))


def lane_block(rows, lanes):
    return pl.BlockSpec((rows, lanes), lambda t, *_: (0, t))


def row_block(rows, lanes):
    return pl.BlockSpec((rows, lanes), lambda t, *_: (t, 0))


def params():
    return pltpu.CompilerParams(vmem_limit_bytes=VMEM, dimension_semantics=("arbitrary",))


def attend_kernel(
    cap_ref, gate_ref, raw_ref, text_ref, gain_ref, table_ref, mixed_ref, lse_ref,
    q_ref, k_ref, v_ref, tk_ref, tv_ref,
):
    step = pl.program_id(0)
    heads = raw_ref.shape[1]

    @pl.when(step == 0)
    def _():
        table = table_ref[...]
        for h in range(heads):
            q = turn(normed(raw_ref[0, h], gain_ref[0, h]), table, 1.0).astype(BF16)
            q_ref[h] = q * jnp.asarray(0.125, BF16)
            k_ref[h] = turn(normed(raw_ref[1, h], gain_ref[1, h]), table, 1.0).astype(BF16)
            v_ref[h] = raw_ref[2, h].astype(BF16)
            tk_ref[h] = normed(text_ref[0, h], gain_ref[2, h]).astype(BF16)
            tv_ref[h] = text_ref[1, h].astype(BF16)

    slots = tk_ref.shape[2]
    mask = lax.broadcasted_iota(jnp.int32, (slots, QUERY_BLOCK), 0) < cap_ref[0]
    here = pl.ds(pl.multiple_of(step * QUERY_BLOCK, QUERY_BLOCK), QUERY_BLOCK)
    outs = []
    for h in range(heads):
        qb = q_ref[h, :, here]
        e = jnp.exp(dot(k_ref[h], qb, (0, 0)))
        total = jnp.sum(e, axis=0, keepdims=True)
        own = dot(v_ref[h], e.astype(BF16), (1, 0)) / total
        te = jnp.exp(jnp.where(mask, dot(tk_ref[h], qb, (0, 0)), MASKED))
        text_total = jnp.sum(te, axis=0, keepdims=True)
        text = dot(tv_ref[h], te.astype(BF16), (1, 0)) / text_total
        outs.append(own + gate_ref[h] * text)
        lse_ref[h, 0:1] = jnp.log(total)
        lse_ref[h, 1:2] = jnp.log(text_total)
    mixed_ref[...] = jnp.concatenate(outs, 0).T.astype(BF16)


def attend(raw, text_raw, gains, table, cap, gates):
    heads = raw.shape[1]
    slots = text_raw.shape[3]
    return pl.pallas_call(
        attend_kernel,
        grid_spec=pltpu.PrefetchScalarGridSpec(
            num_scalar_prefetch=2,
            grid=(TOKENS // QUERY_BLOCK,),
            in_specs=[
                whole((3, heads, HD, TOKENS)),
                whole((2, heads, HD, slots)),
                whole((3, heads, HD, 1)),
                whole((4, 16, TOKENS)),
            ],
            out_specs=[
                row_block(QUERY_BLOCK, heads * HD),
                pl.BlockSpec((heads, 8, QUERY_BLOCK), lambda t, *_: (0, 0, t)),
            ],
            scratch_shapes=[
                pltpu.VMEM((heads, HD, TOKENS), BF16),
                pltpu.VMEM((heads, HD, TOKENS), BF16),
                pltpu.VMEM((heads, HD, TOKENS), BF16),
                pltpu.VMEM((heads, HD, slots), BF16),
                pltpu.VMEM((heads, HD, slots), BF16),
            ],
        ),
        out_shape=[
            jax.ShapeDtypeStruct((TOKENS, heads * HD), BF16),
            jax.ShapeDtypeStruct((heads, 8, TOKENS), F32),
        ],
        compiler_params=params(),
        cost_estimate=pl.CostEstimate(
            flops=heads * 4 * HD * TOKENS * (TOKENS + slots),
            bytes_accessed=heads * HD * TOKENS * 16,
            transcendentals=heads * TOKENS * (TOKENS + slots),
        ),
        name="attend",
    )(cap, gates, raw, text_raw, gains, table)


def attend_back_kernel(
    cap_ref, gate_ref, raw_ref, text_ref, gain_ref, table_ref, lse_ref, grad_ref,
    d_raw_ref, d_text_ref, d_gain_ref, dv_ref, dk_ref, dq_ref, dtv_ref, dtk_ref,
):
    table = table_ref[...]
    head = pl.program_id(0)
    gate = gate_ref[head]
    q = turn(normed(raw_ref[0], gain_ref[0]), table, 1.0).astype(BF16) * jnp.asarray(0.125, BF16)
    k = turn(normed(raw_ref[1], gain_ref[1]), table, 1.0).astype(BF16)
    v = raw_ref[2].astype(BF16)
    tk = normed(text_ref[0], gain_ref[2]).astype(BF16)
    tv = text_ref[1].astype(BF16)
    slots = tk.shape[1]
    mask = lax.broadcasted_iota(jnp.int32, (slots, QUERY_BLOCK), 0) < cap_ref[0]
    gate_sum = jnp.zeros((HD, QUERY_BLOCK), F32)
    for first in range(0, TOKENS, QUERY_BLOCK):
        here = slice(first, first + QUERY_BLOCK)
        qb = q[:, here]
        gb = grad_ref[:, here]
        p = jnp.exp(dot(k, qb, (0, 0)) - lse_ref[0:1, here])
        dv = dot(gb, p.astype(BF16), (1, 1))
        pd = p * dot(v, gb, (0, 0))
        ds = (pd - p * jnp.sum(pd, axis=0, keepdims=True)).astype(BF16)
        dq = dot(k, ds, (1, 0))
        dk = dot(qb, ds, (1, 1))
        tp = jnp.exp(jnp.where(mask, dot(tk, qb, (0, 0)), MASKED) - lse_ref[1:2, here])
        tpb = tp.astype(BF16)
        dtv = dot(gb, tpb, (1, 1))
        gate_sum = gate_sum + gb.astype(F32) * dot(tv, tpb, (1, 0))
        tpd = tp * dot(tv, gb, (0, 0)) * gate
        dts = (tpd - tp * jnp.sum(tpd, axis=0, keepdims=True)).astype(BF16)
        dq_ref[:, here] = dq + dot(tk, dts, (1, 0))
        dtk = dot(qb, dts, (1, 1))
        if first == 0:
            dv_ref[...] = dv
            dk_ref[...] = dk
            dtv_ref[...] = dtv
            dtk_ref[...] = dtk
        else:
            dv_ref[...] += dv
            dk_ref[...] += dk
            dtv_ref[...] += dtv
            dtk_ref[...] += dtk

    def raw_back(which, d_turned):
        spun = turn(d_turned.astype(BF16).astype(F32), table, -1.0)
        values = raw_ref[which]
        d_raw_ref[which] = column_rms_back(values, spun * gain_ref[which]).astype(BF16)
        d_gain_ref[which] = jnp.sum(values * column_rms(values) * spun, axis=1, keepdims=True)

    raw_back(0, dq_ref[...] * 0.125)
    raw_back(1, dk_ref[...])
    d_raw_ref[2] = dv_ref[...].astype(BF16)
    values = text_ref[0]
    d_tk = dtk_ref[...]
    d_text_ref[0] = column_rms_back(values, d_tk * gain_ref[2]).astype(BF16)
    d_gain_ref[2] = jnp.sum(values * column_rms(values) * d_tk, axis=1, keepdims=True)
    d_text_ref[1] = (dtv_ref[...] * gate).astype(BF16)
    d_gain_ref[3] = jnp.sum(gate_sum, axis=1, keepdims=True)


def attend_back(raw, text_raw, gains, table, lse, grads, cap, gates):
    heads = raw.shape[1]
    slots = text_raw.shape[3]
    return pl.pallas_call(
        attend_back_kernel,
        grid_spec=pltpu.PrefetchScalarGridSpec(
            num_scalar_prefetch=2,
            grid=(heads,),
            in_specs=[
                pl.BlockSpec((3, None, HD, TOKENS), lambda h, *_: (0, h, 0, 0)),
                pl.BlockSpec((2, None, HD, slots), lambda h, *_: (0, h, 0, 0)),
                pl.BlockSpec((3, None, HD, 1), lambda h, *_: (0, h, 0, 0)),
                pl.BlockSpec((4, 16, TOKENS), lambda h, *_: (0, 0, 0)),
                pl.BlockSpec((None, 8, TOKENS), lambda h, *_: (h, 0, 0)),
                pl.BlockSpec((None, HD, TOKENS), lambda h, *_: (h, 0, 0)),
            ],
            out_specs=[
                pl.BlockSpec((3, None, HD, TOKENS), lambda h, *_: (0, h, 0, 0)),
                pl.BlockSpec((2, None, HD, slots), lambda h, *_: (0, h, 0, 0)),
                pl.BlockSpec((4, None, HD, 1), lambda h, *_: (0, h, 0, 0)),
            ],
            scratch_shapes=[
                pltpu.VMEM((HD, TOKENS), F32),
                pltpu.VMEM((HD, TOKENS), F32),
                pltpu.VMEM((HD, TOKENS), F32),
                pltpu.VMEM((HD, slots), F32),
                pltpu.VMEM((HD, slots), F32),
            ],
        ),
        out_shape=[
            jax.ShapeDtypeStruct((3, heads, HD, TOKENS), BF16),
            jax.ShapeDtypeStruct((2, heads, HD, slots), BF16),
            jax.ShapeDtypeStruct((4, heads, HD, 1), F32),
        ],
        compiler_params=pltpu.CompilerParams(vmem_limit_bytes=48 * 2**20),
        cost_estimate=pl.CostEstimate(
            flops=heads * 10 * HD * TOKENS * (TOKENS + slots),
            bytes_accessed=heads * HD * TOKENS * 24,
            transcendentals=heads * TOKENS * (TOKENS + slots),
        ),
    )(cap, gates, raw, text_raw, gains, table, lse, grads)


def tile_places(chunk_first):
    r, c, k = np.meshgrid(np.arange(ROWS), np.arange(COLS), np.arange(8), indexing="ij")
    token = r * BLOCK + (k // 2) * GRID + c * 2 + k % 2
    source = (k * ROWS + r) * COLS + c if chunk_first else (r * COLS + c) * 8 + k
    places = np.zeros((TOKENS, TOKENS), np.float32)
    places[source.ravel(), token.ravel()] = 1.0
    return jnp.asarray(places, BF16)


def grid_shift(field, di, dj):
    step = di * GRID + dj
    moved = pltpu.roll(field, (-step) % TOKENS, 1) if step else field
    place = lax.broadcasted_iota(jnp.int32, field.shape, 1)
    row = place // GRID + di
    col = place % GRID + dj
    inside = (row >= 0) & (row < GRID) & (col >= 0) & (col < GRID)
    return jnp.where(inside, moved, 0.0)


def image_kernel(packed_ref, place_ref, patch_ref, cot_ref):
    for which, sign, out_ref in ((0, 1, patch_ref), (1, -1, cot_ref)):
        turned = packed_ref[:, which * 128 : (which + 1) * 128].T
        chunks = jnp.concatenate([turned[k * 16 : (k + 1) * 16] for k in range(8)], 1)
        image = dot(chunks.astype(BF16), place_ref[...], (1, 0))
        for a in range(3):
            for b in range(3):
                first = (a * 3 + b) * 16
                out_ref[first : first + 16] = grid_shift(
                    image, sign * (a - 1), sign * (b - 1)
                ).astype(BF16)


def image_taps(packed):
    out = jax.ShapeDtypeStruct((144, TOKENS), BF16)
    return pl.pallas_call(
        image_kernel,
        out_shape=[out, out],
        compiler_params=pltpu.CompilerParams(vmem_limit_bytes=VMEM),
        name="image_taps",
    )(packed, tile_places(True))


def field_of(taps, place, sign):
    total = jnp.zeros((16, TOKENS), F32)
    for a in range(3):
        for b in range(3):
            first = (a * 3 + b) * 16
            total = total + grid_shift(taps[first : first + 16], sign * (a - 1), sign * (b - 1))
    tiles = dot(total.astype(BF16), place, (1, 1))
    return [tiles[:, r * BLOCK : (r + 1) * BLOCK] for r in range(ROWS)]


def row_rms(v):
    return lax.rsqrt(jnp.mean(v * v, axis=-1, keepdims=True) + EPSILON)


def row_rms_back(v, scale, u):
    return (u - v * (jnp.mean(u * v, axis=-1, keepdims=True) * scale * scale)) * scale


def qkv_kernel(patch_ref, embed_ref, vec_ref, weight_ref, raw_ref, joined_ref, out_ref, turn_ref):
    width = embed_ref.shape[1]
    part = width // COLS

    @pl.when(pl.program_id(0) == 0)
    def _():
        for c in range(COLS):
            here = slice(c * part, (c + 1) * part)
            for s in range(3):
                joined_ref[s, here] = weight_ref[c, s]
            turn_ref[here] = weight_ref[c, 3]
        out_ref[...] = turn_ref[...].T

    x = dot(patch_ref[...], embed_ref[...], (0, 0))
    h = (x * row_rms(x) * vec_ref[0:1]).astype(BF16)
    for s in range(3):
        raw_ref[s] = dot(h, joined_ref[s], (1, 0)).T


def qkv_project(patches, embed, vec, weight):
    width = embed.shape[1]
    part = weight.shape[3]
    return pl.pallas_call(
        qkv_kernel,
        grid=(TOKENS // PAIR,),
        in_specs=[
            lane_block(144, PAIR),
            whole(embed.shape),
            whole(vec.shape),
            whole(weight.shape),
        ],
        out_specs=[
            pl.BlockSpec((3, part, PAIR), lambda t: (0, 0, t)),
            pl.BlockSpec((3, width, part), lambda t: (0, 0, 0)),
            pl.BlockSpec((part, width), lambda t: (0, 0)),
        ],
        out_shape=[
            jax.ShapeDtypeStruct((3, part, TOKENS), F32),
            jax.ShapeDtypeStruct((3, width, part), BF16),
            jax.ShapeDtypeStruct((part, width), BF16),
        ],
        scratch_shapes=[pltpu.VMEM((width, part), BF16)],
        compiler_params=params(),
        cost_estimate=pl.CostEstimate(
            flops=2 * TOKENS * width * (3 * part + 144), bytes_accessed=8 * 2**20, transcendentals=0
        ),
        name="qkv_project",
    )(patches, embed, vec, weight)


def halves(core, first, second):
    return jnp.where(core == 0, first, second)


def forward_kernel(
    at_ref, near_ref, far_ref, out_near_ref, out_far_ref, patch_ref, embed_ref, vec_ref, ffn_ref,
    attn_ref, second_ref, gate_up_ref, hidden_ref, own_ref, other_ref,
):
    core = at_ref[1]
    hidden_width = hidden_ref.shape[1]
    x = dot(patch_ref[...], embed_ref[...], (0, 0))
    attn = dot(near_ref[0], out_near_ref[0], (1, 0))
    for k in range(1, 4):
        attn = attn + dot(near_ref[k], out_near_ref[k], (1, 0))
    for k in range(4):
        attn = attn + dot(far_ref[k], out_far_ref[k], (1, 0))
    attn_ref[...] = attn
    mid = x + vec_ref[1:2] * (attn * row_rms(attn))
    second = (mid * row_rms(mid) * vec_ref[2:3]).astype(BF16)
    second_ref[...] = second
    gate_up = dot(second, ffn_ref[:, : 2 * hidden_width], (1, 0))
    gate_up_ref[...] = gate_up
    gate = gate_up[:, :hidden_width]
    hidden = (gate * jax.nn.sigmoid(gate) * gate_up[:, hidden_width:]).astype(BF16)
    hidden_ref[...] = hidden
    part = dot(hidden, ffn_ref[:, 2 * hidden_width :], (1, 1)).astype(BF16)
    own_ref[0] = halves(core, part[:BLOCK], part[BLOCK:])
    other_ref[0] = halves(core, part[BLOCK:], part[:BLOCK])


def forward(at, mixed, out_whole, patches, embed, vec, ffn):
    width = embed.shape[1]
    part = mixed[0].shape[2]
    hidden_width = ffn.shape[1] // 3
    by_chip = pl.BlockSpec((1, BLOCK, width), lambda t, at: ((t - at[0] + 4) % 4, 0, 0))
    return pl.pallas_call(
        forward_kernel,
        grid_spec=pltpu.PrefetchScalarGridSpec(
            num_scalar_prefetch=1,
            grid=(4,),
            in_specs=[
                pl.BlockSpec((4, PAIR, part), lambda t, at: (0, t, 0)),
                pl.BlockSpec((4, PAIR, part), lambda t, at: (0, t, 0)),
                whole((4, part, width)),
                whole((4, part, width)),
                lane_block(144, PAIR),
                whole(embed.shape),
                whole(vec.shape),
                whole(ffn.shape),
            ],
            out_specs=[
                row_block(PAIR, width),
                row_block(PAIR, width),
                row_block(PAIR, 2 * hidden_width),
                row_block(PAIR, hidden_width),
                by_chip,
                by_chip,
            ],
        ),
        out_shape=[
            jax.ShapeDtypeStruct((TOKENS, width), F32),
            jax.ShapeDtypeStruct((TOKENS, width), BF16),
            jax.ShapeDtypeStruct((TOKENS, 2 * hidden_width), F32),
            jax.ShapeDtypeStruct((TOKENS, hidden_width), BF16),
            jax.ShapeDtypeStruct((4, BLOCK, width), BF16),
            jax.ShapeDtypeStruct((4, BLOCK, width), BF16),
        ],
        compiler_params=params(),
        cost_estimate=pl.CostEstimate(
            flops=2 * TOKENS * width * (width + 3 * hidden_width),
            bytes_accessed=28 * 2**20,
            transcendentals=TOKENS * hidden_width,
        ),
        name="forward",
    )(at, *mixed, *out_whole, patches, embed, vec, ffn)


def own_kernel(
    at_ref, p0_ref, p1_ref, p2_ref, p3_ref, attn_ref, patch_ref, cot_ref, embed_ref, unpatch_ref,
    vec_ref, d_ffn_ref, taps_ref, unpatch_sum_ref, sums_ref,
):
    ffn = sum(p[...].astype(F32) for p in (p0_ref, p1_ref, p2_ref, p3_ref))
    d_last = dot(cot_ref[...], unpatch_ref[...], (0, 0))
    scale = row_rms(ffn)
    gated = vec_ref[3:4]
    d_ffn_ref[...] = row_rms_back(ffn, scale, gated * d_last).astype(BF16)
    normed_ffn = ffn * scale
    sums_ref[...] = jnp.broadcast_to(
        jnp.sum(normed_ffn * d_last, axis=0, keepdims=True), sums_ref.shape
    )
    attn = attn_ref[...]
    x = dot(patch_ref[...], embed_ref[...], (0, 0))
    last = (x + vec_ref[1:2] * (attn * row_rms(attn)) + gated * normed_ffn).astype(BF16)
    taps_ref[...] = dot(unpatch_ref[...], last, (1, 1))
    unpatch_sum_ref[...] = dot(cot_ref[...], last, (1, 0))


def own_block(at, pieces, attn, patches, cot_taps, embed, unpatch, vec):
    width = embed.shape[1]
    piece = pl.BlockSpec((BLOCK, width), lambda t, at: (0, 0))
    lanes = pl.BlockSpec((144, BLOCK), lambda t, at: (0, 2 * at[0] + at[1]))
    return pl.pallas_call(
        own_kernel,
        grid_spec=pltpu.PrefetchScalarGridSpec(
            num_scalar_prefetch=1,
            grid=(1,),
            in_specs=[piece] * 4
            + [
                pl.BlockSpec((BLOCK, width), lambda t, at: (2 * at[0] + at[1], 0)),
                lanes,
                lanes,
                whole(embed.shape),
                whole(unpatch.shape),
                whole(vec.shape),
            ],
            out_specs=[
                piece,
                pl.BlockSpec((144, BLOCK), lambda t, at: (0, 0)),
                pl.BlockSpec((144, width), lambda t, at: (0, 0)),
                pl.BlockSpec((8, width), lambda t, at: (0, 0)),
            ],
        ),
        out_shape=[
            jax.ShapeDtypeStruct((BLOCK, width), BF16),
            jax.ShapeDtypeStruct((144, BLOCK), F32),
            jax.ShapeDtypeStruct((144, width), F32),
            jax.ShapeDtypeStruct((8, width), F32),
        ],
        compiler_params=params(),
        name="own_block",
    )(at, *pieces, attn, patches, cot_taps, embed, unpatch, vec)


def backward_kernel(
    at_ref, own_ref, other_ref, ffn_ref, out_near_ref, out_far_ref, gate_up_ref, attn_ref,
    patch_ref, embed_ref, cot_ref, unpatch_ref, vec_ref,
    d_ffn_ref, d_gate_up_ref, d_attn_ref, d_mid_ref, mixed_own_ref, mixed_other_ref, sums_ref,
):
    step = pl.program_id(0)
    chip, core = at_ref[0], at_ref[1]
    hidden_width = d_gate_up_ref.shape[1] // 2
    own, other = own_ref[0], other_ref[0]
    d_ffn = jnp.concatenate([halves(core, own, other), halves(core, other, own)], 0)
    d_ffn_ref[...] = d_ffn
    d_hidden = dot(d_ffn, ffn_ref[:, 2 * hidden_width :], (1, 0))
    gate = gate_up_ref[:, :hidden_width]
    up = gate_up_ref[:, hidden_width:]
    sigma = jax.nn.sigmoid(gate)
    silu = gate * sigma
    d_gate = d_hidden * up * (sigma + silu * (1.0 - sigma))
    d_gate_up = jnp.concatenate([d_gate.astype(BF16), (d_hidden * silu).astype(BF16)], 1)
    d_gate_up_ref[...] = d_gate_up
    d_second = dot(d_gate_up, ffn_ref[:, : 2 * hidden_width], (1, 1))

    x = dot(patch_ref[...], embed_ref[...], (0, 0))
    attn = attn_ref[...]
    attn_scale = row_rms(attn)
    attn_normed = attn * attn_scale
    mid = x + vec_ref[1:2] * attn_normed
    mid_scale = row_rms(mid)
    mid_sum = jnp.sum(mid * mid_scale * d_second, axis=0, keepdims=True)
    d_last = dot(cot_ref[...], unpatch_ref[...], (0, 0))
    place = lax.broadcasted_iota(jnp.int32, (PAIR, 1), 0) // BLOCK
    mine = (place == core) & (step == chip)
    d_mid = row_rms_back(mid, mid_scale, vec_ref[2:3] * d_second) + jnp.where(mine, d_last, 0.0)
    d_mid_ref[...] = d_mid
    attn_sum = jnp.sum(attn_normed * d_mid, axis=0, keepdims=True)
    d_attn = row_rms_back(attn, attn_scale, vec_ref[1:2] * d_mid).astype(BF16)
    d_attn_ref[...] = d_attn
    for k in range(4):
        mixed_own_ref[k] = dot(out_near_ref[k], d_attn, (1, 1)).astype(BF16)
        mixed_other_ref[k] = dot(out_far_ref[k], d_attn, (1, 1)).astype(BF16)

    @pl.when(step == 0)
    def _():
        sums_ref[...] = jnp.zeros_like(sums_ref)

    sums_ref[0:1] += mid_sum
    sums_ref[1:2] += attn_sum


def backward(at, d_ffn, ffn, out_whole, gate_up, attn, patches, embed, cot_taps, unpatch, vec):
    width = embed.shape[1]
    part = out_whole[0].shape[1]
    hidden_width = ffn.shape[1] // 3
    by_chip = pl.BlockSpec((1, BLOCK, width), lambda t, at: ((t - at[0] + 4) % 4, 0, 0))
    parts = pl.BlockSpec((4, part, PAIR), lambda t, at: (0, 0, t))
    return pl.pallas_call(
        backward_kernel,
        grid_spec=pltpu.PrefetchScalarGridSpec(
            num_scalar_prefetch=1,
            grid=(4,),
            in_specs=[
                by_chip,
                by_chip,
                whole(ffn.shape),
                whole((4, part, width)),
                whole((4, part, width)),
                row_block(PAIR, 2 * hidden_width),
                row_block(PAIR, width),
                lane_block(144, PAIR),
                whole(embed.shape),
                lane_block(144, PAIR),
                whole(unpatch.shape),
                whole(vec.shape),
            ],
            out_specs=[
                row_block(PAIR, width),
                row_block(PAIR, 2 * hidden_width),
                row_block(PAIR, width),
                row_block(PAIR, width),
                parts,
                parts,
                pl.BlockSpec((8, width), lambda t, at: (0, 0)),
            ],
        ),
        out_shape=[
            jax.ShapeDtypeStruct((TOKENS, width), BF16),
            jax.ShapeDtypeStruct((TOKENS, 2 * hidden_width), BF16),
            jax.ShapeDtypeStruct((TOKENS, width), BF16),
            jax.ShapeDtypeStruct((TOKENS, width), F32),
            jax.ShapeDtypeStruct((4, part, TOKENS), BF16),
            jax.ShapeDtypeStruct((4, part, TOKENS), BF16),
            jax.ShapeDtypeStruct((8, width), F32),
        ],
        compiler_params=params(),
        cost_estimate=pl.CostEstimate(
            flops=2 * TOKENS * width * (width + 3 * hidden_width),
            bytes_accessed=36 * 2**20,
            transcendentals=TOKENS * hidden_width,
        ),
        name="backward",
    )(at, *d_ffn, ffn, *out_whole, gate_up, attn, patches, embed, cot_taps, unpatch, vec)


def ffn_grad_kernel(second_ref, d_gate_up_ref, d_ffn_ref, hidden_ref, out_ref):
    split = d_gate_up_ref.shape[1]
    out_ref[:, :split] = dot(second_ref[...], d_gate_up_ref[...], (0, 0)).astype(BF16)
    out_ref[:, split:] = dot(d_ffn_ref[...], hidden_ref[...], (0, 0)).astype(BF16)


def ffn_grads(second, d_gate_up, d_ffn, hidden):
    width = second.shape[1]
    lanes = d_gate_up.shape[1] + hidden.shape[1]
    return pl.pallas_call(
        ffn_grad_kernel,
        grid=(width // 256,),
        in_specs=[
            lane_block(TOKENS, 256),
            whole(d_gate_up.shape),
            lane_block(TOKENS, 256),
            whole(hidden.shape),
        ],
        out_specs=row_block(256, lanes),
        out_shape=jax.ShapeDtypeStruct((width, lanes), BF16),
        compiler_params=params(),
        cost_estimate=pl.CostEstimate(
            flops=2 * TOKENS * width * lanes, bytes_accessed=14 * 2**20, transcendentals=0
        ),
        name="ffn_grads",
    )(second, d_gate_up, d_ffn, hidden)


def first_kernel(
    patch_ref, embed_ref, vec_ref, weight_ref, d_raw_ref, d_mid_ref, place_ref,
    qkv_ref, embed_sum_ref, field_ref, sums_ref, qkv_acc, taps_acc,
):
    step = pl.program_id(0)
    last = pl.num_programs(0) - 1
    part = weight_ref.shape[1] // COLS
    x = dot(patch_ref[...], embed_ref[...], (0, 0))
    scale = row_rms(x)
    x_normed = x * scale
    h = (x_normed * vec_ref[0:1]).astype(BF16)
    d_h = dot(d_raw_ref[0], weight_ref[0], (0, 1))
    for s in (1, 2):
        d_h = d_h + dot(d_raw_ref[s], weight_ref[s], (0, 1))

    @pl.when(step == 0)
    def _():
        qkv_acc[...] = jnp.zeros_like(qkv_acc)
        embed_sum_ref[...] = jnp.zeros_like(embed_sum_ref)
        sums_ref[...] = jnp.zeros_like(sums_ref)

    for s in range(3):
        qkv_acc[s] += dot(d_raw_ref[s], h, (1, 0))
    sums_ref[0:1] += jnp.sum(x_normed * d_h, axis=0, keepdims=True)
    d_first = (d_mid_ref[...] + row_rms_back(x, scale, vec_ref[0:1] * d_h)).astype(BF16)
    embed_sum_ref[...] += dot(patch_ref[...], d_first, (1, 0))
    here = pl.ds(pl.multiple_of(step * PAIR, PAIR), PAIR)
    taps_acc[:, here] = dot(embed_ref[...], d_first, (1, 1))

    @pl.when(step == last)
    def _():
        for s in range(3):
            turned = qkv_acc[s].T.astype(BF16)
            for c in range(COLS):
                qkv_ref[c, s] = turned[c * part : (c + 1) * part]
        for r, tile in enumerate(field_of(taps_acc[...], place_ref[...], -1)):
            field_ref[r] = tile


def first_back(patches, embed, vec, weight, d_raw, d_mid, place):
    width = embed.shape[1]
    part = weight.shape[2]
    return pl.pallas_call(
        first_kernel,
        grid=(TOKENS // PAIR,),
        in_specs=[
            lane_block(144, PAIR),
            whole(embed.shape),
            whole(vec.shape),
            whole(weight.shape),
            pl.BlockSpec((3, part, PAIR), lambda t: (0, 0, t)),
            row_block(PAIR, width),
            whole(place.shape),
        ],
        out_specs=[
            pl.BlockSpec((COLS, 3, width // COLS, part), lambda t: (0, 0, 0, 0)),
            pl.BlockSpec((144, width), lambda t: (0, 0)),
            pl.BlockSpec((ROWS, 16, BLOCK), lambda t: (0, 0, 0)),
            pl.BlockSpec((8, width), lambda t: (0, 0)),
        ],
        out_shape=[
            jax.ShapeDtypeStruct((COLS, 3, width // COLS, part), BF16),
            jax.ShapeDtypeStruct((144, width), F32),
            jax.ShapeDtypeStruct((ROWS, 16, BLOCK), F32),
            jax.ShapeDtypeStruct((8, width), F32),
        ],
        scratch_shapes=[pltpu.VMEM((3, part, width), F32), pltpu.VMEM((144, TOKENS), F32)],
        compiler_params=params(),
        cost_estimate=pl.CostEstimate(
            flops=2 * TOKENS * width * (6 * part + 3 * 144),
            bytes_accessed=16 * 2**20,
            transcendentals=0,
        ),
        name="first_back",
    )(patches, embed, vec, weight, d_raw, d_mid, place)


def field_kernel(taps_ref, place_ref, field_ref):
    for r, tile in enumerate(field_of(taps_ref[...], place_ref[...], 1)):
        field_ref[r] = tile


def local(
    latent, condition, caption, cap_len, cotangent, embed_weight, modulate_weight, norm_gains,
    cross_gate, qkv_weight, text_kv_weight, out_weight, gate_up_weight, down_weight, unpatch_weight,
):
    images, _, _, channels = latent.shape
    width = embed_weight.shape[3]
    local_width = qkv_weight.shape[2]
    heads = local_width // HD
    hidden_width = down_weight.shape[0]
    taps = 9 * channels
    row_at = lax.axis_index("row")
    col_at = lax.axis_index("col")
    at = jnp.stack([row_at // 2, row_at % 2]).astype(jnp.int32)
    tile = latent.shape[1] * latent.shape[2] * channels

    cond_low = jax.nn.silu(condition.astype(F32)).astype(BF16)
    mod_piece = jnp.dot(cond_low, modulate_weight, preferred_element_type=F32)
    mod_columns = mod_piece.shape[1]
    packed = jnp.concatenate(
        [
            latent.reshape(images, tile).astype(F32),
            cotangent.reshape(images, tile).astype(F32),
            jnp.pad(mod_piece, ((0, 0), (0, 128 - mod_columns))),
        ],
        axis=1,
    )
    packed = lax.all_to_all(packed, "col", 0, 0, tiled=True)
    head_piece = after(jnp.concatenate([qkv_weight, out_weight.T[None]]), packed)
    packed = send_all(packed, "row").reshape(ROWS * COLS, -1)

    head_pieces = send_all(head_piece, "col")
    text_piece = jnp.concatenate([text_kv_weight[0], text_kv_weight[1]], axis=1)
    text_whole = lax.all_gather(text_piece, "col", axis=0, tiled=True)
    ffn_piece = jnp.concatenate([gate_up_weight[0], gate_up_weight[1], down_weight.T], axis=1)
    ffn_whole = lax.all_gather(ffn_piece, "col", axis=0, tiled=True)

    patches, cot_taps = image_taps(packed)
    modulation = packed[:, 2 * tile : 2 * tile + mod_columns].reshape(4, width)
    attn_gate = jnp.tanh(modulation[1])
    ffn_gate = jnp.tanh(modulation[3])
    vec = jnp.stack(
        [
            norm_gains[0] * (1.0 + modulation[0]),
            norm_gains[1] * attn_gate,
            norm_gains[2] * (1.0 + modulation[2]),
            norm_gains[3] * ffn_gate,
        ]
    )
    vec = jnp.pad(vec, ((0, 4), (0, 0)))
    embed = embed_weight.reshape(taps, width)
    unpatch = unpatch_weight.transpose(0, 1, 3, 2).reshape(taps, width)
    raw, qkv_whole, out_rows = qkv_project(patches, embed, vec, head_pieces)
    out_whole = gather_near(out_rows)
    raw = raw.reshape(3, heads, HD, TOKENS)
    caption_rows = caption[0]
    text_raw = dot(text_whole, caption_rows, (0, 1)).reshape(2, heads, HD, caption_rows.shape[0])
    head_gains = lax.dynamic_slice(norm_gains, (4, row_at * local_width), (3, local_width)).reshape(
        3, heads, HD, 1
    )
    head_gates = jnp.tanh(lax.dynamic_slice_in_dim(cross_gate, row_at * heads, heads))
    cap = lax.dynamic_slice_in_dim(cap_len, col_at, 1)
    table = jnp.asarray(rope_tables())
    mixed, lse = attend(raw, text_raw, head_gains, table, cap, head_gates)

    mixed_whole = gather_near(mixed)
    attn, second, gate_up, hidden, ffn_own, ffn_other = forward(
        at, mixed_whole, out_whole, patches, embed, vec, ffn_whole
    )
    d_ffn_own, last_taps, unpatch_sum, own_sums = own_block(
        at, scatter_near(ffn_own, ffn_other), attn, patches, cot_taps, embed, unpatch, vec
    )
    d_ffn, d_gate_up, d_attn, d_mid, mixed_own, mixed_other, back_sums = backward(
        at, gather_near(d_ffn_own), ffn_whole, out_whole, gate_up, attn, patches, embed, cot_taps,
        unpatch, vec,
    )
    mixed_terms = scatter_near(mixed_own, mixed_other)
    d_mixed = sum(term.astype(F32) for term in mixed_terms).astype(BF16)
    ffn_sum = ffn_grads(after(second, mixed_terms[0]), d_gate_up, d_ffn, hidden)
    d_attn = after(d_attn, ffn_sum)
    out_parts = [
        jnp.einsum("kne,nd->ked", pieces, d_attn, preferred_element_type=F32).astype(BF16)
        for pieces in mixed_whole
    ]

    d_mixed = after(d_mixed, ffn_sum, *out_parts)
    d_raw, d_text, d_head = attend_back(
        raw, text_raw, head_gains, table, lse, d_mixed.reshape(heads, HD, TOKENS), cap, head_gates
    )
    text_sum = dot(caption_rows, d_text.reshape(2 * local_width, -1), (0, 1)).astype(BF16)
    d_raw = after(d_raw, text_sum)
    place = tile_places(False)
    qkv_parts, embed_sum, latent_field, first_sums = first_back(
        patches, embed, vec, qkv_whole, d_raw.reshape(3, local_width, TOKENS), d_mid, place
    )
    activation_field = pl.pallas_call(
        field_kernel,
        out_shape=jax.ShapeDtypeStruct((ROWS, channels, BLOCK), F32),
        compiler_params=pltpu.CompilerParams(vmem_limit_bytes=VMEM),
        name="activation_field",
    )(
        lax.dynamic_update_slice(jnp.zeros((taps, TOKENS), F32), last_taps, (0, row_at * BLOCK)),
        place,
    )

    terms = jnp.stack([first_sums[0], back_sums[1], back_sums[0], own_sums[0]])
    one = jnp.ones_like(attn_gate)
    d_modulation = terms * jnp.stack(
        [
            norm_gains[0],
            norm_gains[1] * (1.0 - attn_gate * attn_gate),
            norm_gains[2],
            norm_gains[3] * (1.0 - ffn_gate * ffn_gate),
        ]
    )
    d_gains = terms * jnp.stack([one + modulation[0], attn_gate, one + modulation[2], ffn_gate])
    head_rows = lax.dynamic_update_slice(
        jnp.zeros((3, width), F32), d_head[:3].reshape(3, local_width), (0, row_at * local_width)
    )
    gate_part = jnp.sum(d_head[3], axis=(1, 2)) * (1.0 - head_gates * head_gates)
    gate_row = lax.dynamic_update_slice(
        jnp.zeros((1, width), F32), gate_part[None], (0, row_at * heads)
    )
    shared = jnp.concatenate(
        [embed_sum, unpatch_sum, d_gains, head_rows, gate_row, jnp.zeros((24, width), F32)]
    )
    per_row = shared.shape[0] * width // (ROWS * 128)
    row_pack = jnp.concatenate(
        [
            shared.astype(BF16).reshape(ROWS, per_row, 128),
            activation_field.astype(BF16),
            latent_field.astype(BF16),
            jnp.pad(d_modulation.astype(BF16).reshape(ROWS, 6, 128), ((0, 0), (0, 10), (0, 0))),
        ],
        axis=1,
    )
    row_pack = jnp.sum(lax.all_to_all(row_pack, "row", 0, 0).astype(F32), axis=0)
    fields = row_pack[per_row : per_row + 2 * channels]
    fields = fields.T.reshape(COLS, 8, 2 * channels)
    mod_sums = row_pack[per_row + 2 * channels : per_row + 2 * channels + 6]
    fields = jnp.concatenate([fields, mod_sums.reshape(COLS, 8, 6)], axis=2)
    fields = lax.all_to_all(fields, "col", 0, 0)
    activation = fields[:, :, :channels].reshape(latent.shape).astype(BF16)
    latent_grad = fields[:, :, channels : 2 * channels].reshape(latent.shape).astype(BF16)
    modulate_grad = lax.dot_general(
        cond_low.astype(F32),
        fields[:, :, 2 * channels :].reshape(images, mod_columns),
        (((0,), (0,)), ((), ())),
        precision=lax.Precision.HIGHEST,
        preferred_element_type=F32,
    )
    shared = row_pack[:per_row].astype(BF16).reshape(COLS, per_row // COLS, 128)
    shared = jnp.sum(lax.all_to_all(shared, "col", 0, 0).astype(F32), axis=0).astype(BF16)
    shared = send_all(send_all(shared, "col"), "row").reshape(-1, width).astype(F32)
    embed_grad = shared[:taps].reshape(embed_weight.shape)
    unpatch_grad = shared[taps : 2 * taps].reshape(3, 3, channels, width).transpose(0, 1, 3, 2)
    gains_grad = shared[2 * taps : 2 * taps + 7]
    gate_grad = shared[2 * taps + 7, :HEADS]

    ffn_total = lax.psum_scatter(ffn_sum, "col", scatter_dimension=0, tiled=True).astype(F32)
    gate_up_grad = jnp.stack([ffn_total[:, :hidden_width], ffn_total[:, hidden_width : 2 * hidden_width]])
    down_grad = ffn_total[:, 2 * hidden_width :].T
    text_total = lax.psum_scatter(text_sum, "col", scatter_dimension=0, tiled=True).astype(F32)
    text_kv_grad = jnp.stack([text_total[:, :local_width], text_total[:, local_width:]])
    out_sum = sum(term.astype(F32) for term in scatter_near(*out_parts)).astype(BF16)
    out_sum = out_sum.reshape(local_width, COLS, width // COLS).transpose(1, 0, 2)
    out_grad = jnp.sum(lax.all_to_all(out_sum, "col", 0, 0).astype(F32), axis=0)
    qkv_grad = jnp.sum(lax.all_to_all(qkv_parts, "col", 0, 0).astype(F32), axis=0)
    return (
        activation, latent_grad, embed_grad, modulate_grad, gains_grad, gate_grad,
        qkv_grad, text_kv_grad, out_grad, gate_up_grad, down_grad, unpatch_grad,
    )


def solution(mesh):
    placed = (
        P(None, "row", "col", None),
        P(),
        P("col", None, None),
        P(),
        P(None, "row", "col", None),
        P(),
        P(None, ("row", "col")),
        P(),
        P(),
        P(None, "col", "row"),
        P(None, "col", "row"),
        P("row", "col"),
        P(None, "col", "row"),
        P("row", "col"),
        P(),
    )
    return jax.shard_map(
        local,
        mesh=mesh,
        in_specs=placed,
        out_specs=(
            P(None, "row", "col", None),
            P(None, "row", "col", None),
            P(),
            P(None, ("row", "col")),
            P(),
            P(),
            P(None, "col", "row"),
            P(None, "col", "row"),
            P("row", "col"),
            P(None, "col", "row"),
            P("row", "col"),
            P(),
        ),
        check_vma=False,
    )
```

```python
import math
from functools import partial

import jax
import jax.numpy as jnp
import numpy as np
from jax import lax
from jax.experimental import pallas as pl
from jax.experimental.pallas import tpu as pltpu
from jax.sharding import PartitionSpec as P

HEADS = 24
HD = 64
GRID = 32
TOKENS = GRID * GRID
EPSILON = 1e-06
ROPE_BASE = 10000.0
MASKED = -1e30
F32 = jnp.float32
BF16 = jnp.bfloat16
ROWS = 8
COLS = 16
QUERY_BLOCK = 256
BLOCK = TOKENS // ROWS
PAIR = 2 * BLOCK
VMEM = 56 * 2**20


def dot(left, right, contract):
    return lax.dot_general(
        left, right, ((contract[:1], contract[1:]), ((), ())), preferred_element_type=F32
    )


def row_pairs(dx, dc):
    return [
        (((x + dx) % 4) * 2 + (c + dc) % 2, x * 2 + c) for x in range(4) for c in range(2)
    ]


def row_pairs_to(dx, dc):
    return [(dst, src) for src, dst in row_pairs(dx, dc)]


def gather_near(piece):
    quad = jnp.stack([piece] + [lax.ppermute(piece, "row", row_pairs(d, 0)) for d in (1, 2, 3)])
    return quad, lax.ppermute(quad, "row", row_pairs(0, 1))


def sum_cores(own, other):
    other = lax.ppermute(other, "row", row_pairs(0, 1))
    return [(own[d].astype(F32) + other[d].astype(F32)).astype(BF16) for d in range(4)]


def to_chips(near):
    return [near[0]] + [lax.ppermute(near[d], "row", row_pairs_to(d, 0)) for d in (1, 2, 3)]


def send_all(piece, axis):
    copies = jnp.broadcast_to(piece, (lax.axis_size(axis),) + piece.shape)
    return lax.all_to_all(copies, axis, 0, 0)


def after(value, *others):
    return lax.optimization_barrier((value,) + others)[0]


def rope_tables():
    quarter = HD // 4
    frequency = np.float32(ROPE_BASE) ** (-np.arange(quarter, dtype=np.float32) / np.float32(quarter))
    place = np.arange(TOKENS)
    row = frequency[:, None] * (place // GRID).astype(np.float32)[None, :]
    col = frequency[:, None] * (place % GRID).astype(np.float32)[None, :]
    return np.stack([np.cos(row), np.sin(row), np.cos(col), np.sin(col)]).astype(np.float32)


def turn(v, table, sign):
    a, b, c, d = (v[k * 16 : (k + 1) * 16] for k in range(4))
    cr, sr, cc, sc = table[0], table[1] * sign, table[2], table[3] * sign
    return jnp.concatenate([a * cr - b * sr, a * sr + b * cr, c * cc - d * sc, c * sc + d * cc], 0)


def column_rms(v):
    return lax.rsqrt(jnp.mean(v * v, axis=0, keepdims=True) + EPSILON)


def normed(v, gain):
    return v * column_rms(v) * gain


def column_rms_back(v, u):
    scale = column_rms(v)
    return (u - v * (jnp.mean(u * v, axis=0, keepdims=True) * scale * scale)) * scale


def whole(shape):
    zeros = (0,) * len(shape)
    return pl.BlockSpec(shape, lambda *_: zeros, pipeline_mode=pl.Buffered(1))


def lane_block(rows, lanes):
    return pl.BlockSpec((rows, lanes), lambda t, *_: (0, t))


def row_block(rows, lanes):
    return pl.BlockSpec((rows, lanes), lambda t, *_: (t, 0))


def params():
    return pltpu.CompilerParams(vmem_limit_bytes=VMEM, dimension_semantics=("arbitrary",))


def attend_kernel(
    cap_ref, gate_ref, raw_ref, text_ref, gain_ref, table_ref, mixed_ref, lse_ref,
    q_ref, k_ref, v_ref, tk_ref, tv_ref,
):
    step = pl.program_id(0)
    heads = raw_ref.shape[1]

    @pl.when(step == 0)
    def _():
        table = table_ref[...]
        for h in range(heads):
            q = turn(normed(raw_ref[0, h], gain_ref[0, h]), table, 1.0).astype(BF16)
            q_ref[h] = q * jnp.asarray(0.125, BF16)
            k_ref[h] = turn(normed(raw_ref[1, h], gain_ref[1, h]), table, 1.0).astype(BF16)
            v_ref[h] = raw_ref[2, h].astype(BF16)
            tk_ref[h] = normed(text_ref[0, h], gain_ref[2, h]).astype(BF16)
            tv_ref[h] = text_ref[1, h].astype(BF16)

    slots = tk_ref.shape[2]
    mask = lax.broadcasted_iota(jnp.int32, (slots, QUERY_BLOCK), 0) < cap_ref[0]
    here = pl.ds(pl.multiple_of(step * QUERY_BLOCK, QUERY_BLOCK), QUERY_BLOCK)
    outs = []
    for h in range(heads):
        qb = q_ref[h, :, here]
        e = jnp.exp(dot(k_ref[h], qb, (0, 0)))
        total = jnp.sum(e, axis=0, keepdims=True)
        own = dot(v_ref[h], e.astype(BF16), (1, 0)) / total
        te = jnp.exp(jnp.where(mask, dot(tk_ref[h], qb, (0, 0)), MASKED))
        text_total = jnp.sum(te, axis=0, keepdims=True)
        text = dot(tv_ref[h], te.astype(BF16), (1, 0)) / text_total
        outs.append(own + gate_ref[h] * text)
        lse_ref[h, 0:1] = jnp.log(total)
        lse_ref[h, 1:2] = jnp.log(text_total)
    mixed_ref[...] = jnp.concatenate(outs, 0).astype(BF16)


def attend(raw, text_raw, gains, table, cap, gates):
    heads = raw.shape[1]
    slots = text_raw.shape[3]
    return pl.pallas_call(
        attend_kernel,
        grid_spec=pltpu.PrefetchScalarGridSpec(
            num_scalar_prefetch=2,
            grid=(TOKENS // QUERY_BLOCK,),
            in_specs=[
                whole((3, heads, HD, TOKENS)),
                whole((2, heads, HD, slots)),
                whole((3, heads, HD, 1)),
                whole((4, 16, TOKENS)),
            ],
            out_specs=[
                lane_block(heads * HD, QUERY_BLOCK),
                pl.BlockSpec((heads, 8, QUERY_BLOCK), lambda t, *_: (0, 0, t)),
            ],
            scratch_shapes=[
                pltpu.VMEM((heads, HD, TOKENS), BF16),
                pltpu.VMEM((heads, HD, TOKENS), BF16),
                pltpu.VMEM((heads, HD, TOKENS), BF16),
                pltpu.VMEM((heads, HD, slots), BF16),
                pltpu.VMEM((heads, HD, slots), BF16),
            ],
        ),
        out_shape=[
            jax.ShapeDtypeStruct((heads * HD, TOKENS), BF16),
            jax.ShapeDtypeStruct((heads, 8, TOKENS), F32),
        ],
        compiler_params=params(),
        cost_estimate=pl.CostEstimate(
            flops=heads * 4 * HD * TOKENS * (TOKENS + slots),
            bytes_accessed=heads * HD * TOKENS * 16,
            transcendentals=heads * TOKENS * (TOKENS + slots),
        ),
        name="attend",
    )(cap, gates, raw, text_raw, gains, table)


def attend_back_kernel(
    cap_ref, gate_ref, raw_ref, text_ref, gain_ref, table_ref, lse_ref, grad_ref,
    d_raw_ref, d_text_ref, d_gain_ref, dv_ref, dk_ref, dq_ref, dtv_ref, dtk_ref,
):
    table = table_ref[...]
    head = pl.program_id(0)
    gate = gate_ref[head]
    q = turn(normed(raw_ref[0], gain_ref[0]), table, 1.0).astype(BF16) * jnp.asarray(0.125, BF16)
    k = turn(normed(raw_ref[1], gain_ref[1]), table, 1.0).astype(BF16)
    v = raw_ref[2].astype(BF16)
    tk = normed(text_ref[0], gain_ref[2]).astype(BF16)
    tv = text_ref[1].astype(BF16)
    slots = tk.shape[1]
    mask = lax.broadcasted_iota(jnp.int32, (slots, QUERY_BLOCK), 0) < cap_ref[0]
    gate_sum = jnp.zeros((HD, QUERY_BLOCK), F32)
    for first in range(0, TOKENS, QUERY_BLOCK):
        here = slice(first, first + QUERY_BLOCK)
        qb = q[:, here]
        gb = grad_ref[:, here]
        p = jnp.exp(dot(k, qb, (0, 0)) - lse_ref[0:1, here])
        dv = dot(gb, p.astype(BF16), (1, 1))
        pd = p * dot(v, gb, (0, 0))
        ds = (pd - p * jnp.sum(pd, axis=0, keepdims=True)).astype(BF16)
        dq = dot(k, ds, (1, 0))
        dk = dot(qb, ds, (1, 1))
        tp = jnp.exp(jnp.where(mask, dot(tk, qb, (0, 0)), MASKED) - lse_ref[1:2, here])
        tpb = tp.astype(BF16)
        dtv = dot(gb, tpb, (1, 1))
        gate_sum = gate_sum + gb.astype(F32) * dot(tv, tpb, (1, 0))
        tpd = tp * dot(tv, gb, (0, 0)) * gate
        dts = (tpd - tp * jnp.sum(tpd, axis=0, keepdims=True)).astype(BF16)
        dq_ref[:, here] = dq + dot(tk, dts, (1, 0))
        dtk = dot(qb, dts, (1, 1))
        if first == 0:
            dv_ref[...] = dv
            dk_ref[...] = dk
            dtv_ref[...] = dtv
            dtk_ref[...] = dtk
        else:
            dv_ref[...] += dv
            dk_ref[...] += dk
            dtv_ref[...] += dtv
            dtk_ref[...] += dtk

    def raw_back(which, d_turned):
        spun = turn(d_turned.astype(BF16).astype(F32), table, -1.0)
        values = raw_ref[which]
        d_raw_ref[which] = column_rms_back(values, spun * gain_ref[which]).astype(BF16)
        d_gain_ref[which] = jnp.sum(values * column_rms(values) * spun, axis=1, keepdims=True)

    raw_back(0, dq_ref[...] * 0.125)
    raw_back(1, dk_ref[...])
    d_raw_ref[2] = dv_ref[...].astype(BF16)
    values = text_ref[0]
    d_tk = dtk_ref[...]
    d_text_ref[0] = column_rms_back(values, d_tk * gain_ref[2]).astype(BF16)
    d_gain_ref[2] = jnp.sum(values * column_rms(values) * d_tk, axis=1, keepdims=True)
    d_text_ref[1] = (dtv_ref[...] * gate).astype(BF16)
    d_gain_ref[3] = jnp.sum(gate_sum, axis=1, keepdims=True)


def attend_back(raw, text_raw, gains, table, lse, grads, cap, gates):
    heads = raw.shape[1]
    slots = text_raw.shape[3]
    return pl.pallas_call(
        attend_back_kernel,
        grid_spec=pltpu.PrefetchScalarGridSpec(
            num_scalar_prefetch=2,
            grid=(heads,),
            in_specs=[
                pl.BlockSpec((3, None, HD, TOKENS), lambda h, *_: (0, h, 0, 0)),
                pl.BlockSpec((2, None, HD, slots), lambda h, *_: (0, h, 0, 0)),
                pl.BlockSpec((3, None, HD, 1), lambda h, *_: (0, h, 0, 0)),
                pl.BlockSpec((4, 16, TOKENS), lambda h, *_: (0, 0, 0)),
                pl.BlockSpec((None, 8, TOKENS), lambda h, *_: (h, 0, 0)),
                pl.BlockSpec((None, HD, TOKENS), lambda h, *_: (h, 0, 0)),
            ],
            out_specs=[
                pl.BlockSpec((3, None, HD, TOKENS), lambda h, *_: (0, h, 0, 0)),
                pl.BlockSpec((2, None, HD, slots), lambda h, *_: (0, h, 0, 0)),
                pl.BlockSpec((4, None, HD, 1), lambda h, *_: (0, h, 0, 0)),
            ],
            scratch_shapes=[
                pltpu.VMEM((HD, TOKENS), F32),
                pltpu.VMEM((HD, TOKENS), F32),
                pltpu.VMEM((HD, TOKENS), F32),
                pltpu.VMEM((HD, slots), F32),
                pltpu.VMEM((HD, slots), F32),
            ],
        ),
        out_shape=[
            jax.ShapeDtypeStruct((3, heads, HD, TOKENS), BF16),
            jax.ShapeDtypeStruct((2, heads, HD, slots), BF16),
            jax.ShapeDtypeStruct((4, heads, HD, 1), F32),
        ],
        compiler_params=pltpu.CompilerParams(vmem_limit_bytes=48 * 2**20),
        cost_estimate=pl.CostEstimate(
            flops=heads * 10 * HD * TOKENS * (TOKENS + slots),
            bytes_accessed=heads * HD * TOKENS * 24,
            transcendentals=heads * TOKENS * (TOKENS + slots),
        ),
    )(cap, gates, raw, text_raw, gains, table, lse, grads)


def tile_places(chunk_first):
    r, c, k = np.meshgrid(np.arange(ROWS), np.arange(COLS), np.arange(8), indexing="ij")
    token = r * BLOCK + (k // 2) * GRID + c * 2 + k % 2
    source = (k * ROWS + r) * COLS + c if chunk_first else (r * COLS + c) * 8 + k
    places = np.zeros((TOKENS, TOKENS), np.float32)
    places[source.ravel(), token.ravel()] = 1.0
    return jnp.asarray(places, BF16)


def grid_shift(field, di, dj):
    step = di * GRID + dj
    moved = pltpu.roll(field, (-step) % TOKENS, 1) if step else field
    place = lax.broadcasted_iota(jnp.int32, field.shape, 1)
    row = place // GRID + di
    col = place % GRID + dj
    inside = (row >= 0) & (row < GRID) & (col >= 0) & (col < GRID)
    return jnp.where(inside, moved, 0.0)


def image_kernel(packed_ref, place_ref, patch_ref, cot_ref):
    for which, sign, out_ref in ((0, 1, patch_ref), (1, -1, cot_ref)):
        tiles = jnp.concatenate([packed_ref[r, which] for r in range(ROWS)], 0)
        turned = tiles.astype(F32).T
        chunks = jnp.concatenate([turned[k * 16 : (k + 1) * 16] for k in range(8)], 1)
        image = dot(chunks.astype(BF16), place_ref[...], (1, 0))
        for a in range(3):
            for b in range(3):
                first = (a * 3 + b) * 16
                out_ref[first : first + 16] = grid_shift(
                    image, sign * (a - 1), sign * (b - 1)
                ).astype(BF16)


def image_taps(packed):
    out = jax.ShapeDtypeStruct((144, TOKENS), BF16)
    return pl.pallas_call(
        image_kernel,
        out_shape=[out, out],
        compiler_params=pltpu.CompilerParams(vmem_limit_bytes=VMEM),
        name="image_taps",
    )(packed, tile_places(True))


def field_of(taps, place, sign):
    total = jnp.zeros((16, TOKENS), F32)
    for a in range(3):
        for b in range(3):
            first = (a * 3 + b) * 16
            total = total + grid_shift(taps[first : first + 16], sign * (a - 1), sign * (b - 1))
    tiles = dot(total.astype(BF16), place, (1, 1))
    return [tiles[:, r * BLOCK : (r + 1) * BLOCK] for r in range(ROWS)]


def row_rms(v):
    return lax.rsqrt(jnp.mean(v * v, axis=-1, keepdims=True) + EPSILON)


def row_rms_back(v, scale, u):
    return (u - v * (jnp.mean(u * v, axis=-1, keepdims=True) * scale * scale)) * scale


def qkv_kernel(patch_ref, embed_ref, vec_ref, weight_ref, raw_ref, joined_ref, out_ref, turn_ref):
    width = embed_ref.shape[1]
    part = width // COLS

    @pl.when(pl.program_id(0) == 0)
    def _():
        for c in range(COLS):
            here = slice(c * part, (c + 1) * part)
            for s in range(3):
                joined_ref[s, here] = weight_ref[c, s * part : (s + 1) * part]
            turn_ref[here] = weight_ref[c, 3 * part : 4 * part]
        out_ref[...] = turn_ref[...].T

    x = dot(patch_ref[...], embed_ref[...], (0, 0))
    h = (x * row_rms(x) * vec_ref[0:1]).astype(BF16)
    for s in range(3):
        raw_ref[s] = dot(h, joined_ref[s], (1, 0)).T


def qkv_project(patches, embed, vec, weight):
    width = embed.shape[1]
    part = weight.shape[2]
    return pl.pallas_call(
        qkv_kernel,
        grid=(TOKENS // PAIR,),
        in_specs=[
            lane_block(144, PAIR),
            whole(embed.shape),
            whole(vec.shape),
            whole(weight.shape),
        ],
        out_specs=[
            pl.BlockSpec((3, part, PAIR), lambda t: (0, 0, t)),
            pl.BlockSpec((3, width, part), lambda t: (0, 0, 0)),
            pl.BlockSpec((part, width), lambda t: (0, 0)),
        ],
        out_shape=[
            jax.ShapeDtypeStruct((3, part, TOKENS), F32),
            jax.ShapeDtypeStruct((3, width, part), BF16),
            jax.ShapeDtypeStruct((part, width), BF16),
        ],
        scratch_shapes=[pltpu.VMEM((width, part), BF16)],
        compiler_params=params(),
        cost_estimate=pl.CostEstimate(
            flops=2 * TOKENS * width * (3 * part + 144), bytes_accessed=8 * 2**20, transcendentals=0
        ),
        name="qkv_project",
    )(patches, embed, vec, weight)


def halves(core, first, second):
    return jnp.where(core == 0, first, second)


def forward_kernel(
    at_ref, near_ref, far_ref, out_near_ref, out_far_ref, patch_ref, embed_ref, vec_ref, ffn_ref,
    attn_ref, second_ref, gate_up_ref, hidden_ref, own_ref, other_ref,
):
    core = at_ref[1]
    hidden_width = hidden_ref.shape[1]
    x = dot(patch_ref[...], embed_ref[...], (0, 0))
    attn = dot(near_ref[0], out_near_ref[0], (0, 0))
    for k in range(1, 4):
        attn = attn + dot(near_ref[k], out_near_ref[k], (0, 0))
    for k in range(4):
        attn = attn + dot(far_ref[k], out_far_ref[k], (0, 0))
    attn_ref[...] = attn
    mid = x + vec_ref[1:2] * (attn * row_rms(attn))
    second = (mid * row_rms(mid) * vec_ref[2:3]).astype(BF16)
    second_ref[...] = second
    gate_up = dot(second, ffn_ref[:, : 2 * hidden_width], (1, 0))
    gate_up_ref[...] = gate_up
    gate = gate_up[:, :hidden_width]
    hidden = (gate * jax.nn.sigmoid(gate) * gate_up[:, hidden_width:]).astype(BF16)
    hidden_ref[...] = hidden
    part = dot(hidden, ffn_ref[:, 2 * hidden_width :], (1, 1)).astype(BF16)
    own_ref[0] = halves(core, part[:BLOCK], part[BLOCK:])
    other_ref[0] = halves(core, part[BLOCK:], part[:BLOCK])


def forward(at, mixed, out_whole, patches, embed, vec, ffn):
    width = embed.shape[1]
    part = mixed[0].shape[1]
    hidden_width = ffn.shape[1] // 3
    by_chip = pl.BlockSpec((1, BLOCK, width), lambda t, at: ((t - at[0] + 4) % 4, 0, 0))
    return pl.pallas_call(
        forward_kernel,
        grid_spec=pltpu.PrefetchScalarGridSpec(
            num_scalar_prefetch=1,
            grid=(4,),
            in_specs=[
                pl.BlockSpec((4, part, PAIR), lambda t, at: (0, 0, t)),
                pl.BlockSpec((4, part, PAIR), lambda t, at: (0, 0, t)),
                whole((4, part, width)),
                whole((4, part, width)),
                lane_block(144, PAIR),
                whole(embed.shape),
                whole(vec.shape),
                whole(ffn.shape),
            ],
            out_specs=[
                row_block(PAIR, width),
                row_block(PAIR, width),
                row_block(PAIR, 2 * hidden_width),
                row_block(PAIR, hidden_width),
                by_chip,
                by_chip,
            ],
        ),
        out_shape=[
            jax.ShapeDtypeStruct((TOKENS, width), F32),
            jax.ShapeDtypeStruct((TOKENS, width), BF16),
            jax.ShapeDtypeStruct((TOKENS, 2 * hidden_width), F32),
            jax.ShapeDtypeStruct((TOKENS, hidden_width), BF16),
            jax.ShapeDtypeStruct((4, BLOCK, width), BF16),
            jax.ShapeDtypeStruct((4, BLOCK, width), BF16),
        ],
        compiler_params=params(),
        cost_estimate=pl.CostEstimate(
            flops=2 * TOKENS * width * (width + 3 * hidden_width),
            bytes_accessed=28 * 2**20,
            transcendentals=TOKENS * hidden_width,
        ),
        name="forward",
    )(at, *mixed, *out_whole, patches, embed, vec, ffn)


def own_kernel(
    at_ref, p0_ref, p1_ref, p2_ref, p3_ref, attn_ref, patch_ref, cot_ref, embed_ref, unpatch_ref,
    vec_ref, d_ffn_ref, taps_ref, unpatch_sum_ref, sums_ref,
):
    ffn = sum(p[...].astype(F32) for p in (p0_ref, p1_ref, p2_ref, p3_ref))
    d_last = dot(cot_ref[...], unpatch_ref[...], (0, 0))
    scale = row_rms(ffn)
    gated = vec_ref[3:4]
    d_ffn_ref[...] = row_rms_back(ffn, scale, gated * d_last).astype(BF16)
    normed_ffn = ffn * scale
    sums_ref[...] = jnp.broadcast_to(
        jnp.sum(normed_ffn * d_last, axis=0, keepdims=True), sums_ref.shape
    )
    attn = attn_ref[...]
    x = dot(patch_ref[...], embed_ref[...], (0, 0))
    last = (x + vec_ref[1:2] * (attn * row_rms(attn)) + gated * normed_ffn).astype(BF16)
    taps_ref[...] = dot(unpatch_ref[...], last, (1, 1))
    unpatch_sum_ref[...] = dot(cot_ref[...], last, (1, 0))


def own_block(at, pieces, attn, patches, cot_taps, embed, unpatch, vec):
    width = embed.shape[1]
    piece = pl.BlockSpec((BLOCK, width), lambda t, at: (0, 0))
    lanes = pl.BlockSpec((144, BLOCK), lambda t, at: (0, 2 * at[0] + at[1]))
    return pl.pallas_call(
        own_kernel,
        grid_spec=pltpu.PrefetchScalarGridSpec(
            num_scalar_prefetch=1,
            grid=(1,),
            in_specs=[piece] * 4
            + [
                pl.BlockSpec((BLOCK, width), lambda t, at: (2 * at[0] + at[1], 0)),
                lanes,
                lanes,
                whole(embed.shape),
                whole(unpatch.shape),
                whole(vec.shape),
            ],
            out_specs=[
                piece,
                pl.BlockSpec((144, BLOCK), lambda t, at: (0, 0)),
                pl.BlockSpec((144, width), lambda t, at: (0, 0)),
                pl.BlockSpec((8, width), lambda t, at: (0, 0)),
            ],
        ),
        out_shape=[
            jax.ShapeDtypeStruct((BLOCK, width), BF16),
            jax.ShapeDtypeStruct((144, BLOCK), F32),
            jax.ShapeDtypeStruct((144, width), F32),
            jax.ShapeDtypeStruct((8, width), F32),
        ],
        compiler_params=params(),
        name="own_block",
    )(at, *pieces, attn, patches, cot_taps, embed, unpatch, vec)


def backward_kernel(
    at_ref, own_ref, other_ref, ffn_ref, out_near_ref, out_far_ref, gate_up_ref, attn_ref,
    patch_ref, embed_ref, cot_ref, unpatch_ref, vec_ref,
    d_ffn_ref, d_gate_up_ref, d_attn_ref, d_mid_ref, mixed_own_ref, mixed_other_ref, sums_ref,
):
    step = pl.program_id(0)
    chip, core = at_ref[0], at_ref[1]
    hidden_width = d_gate_up_ref.shape[1] // 2
    own, other = own_ref[0], other_ref[0]
    d_ffn = jnp.concatenate([halves(core, own, other), halves(core, other, own)], 0)
    d_ffn_ref[...] = d_ffn
    d_hidden = dot(d_ffn, ffn_ref[:, 2 * hidden_width :], (1, 0))
    gate = gate_up_ref[:, :hidden_width]
    up = gate_up_ref[:, hidden_width:]
    sigma = jax.nn.sigmoid(gate)
    silu = gate * sigma
    d_gate = d_hidden * up * (sigma + silu * (1.0 - sigma))
    d_gate_up = jnp.concatenate([d_gate.astype(BF16), (d_hidden * silu).astype(BF16)], 1)
    d_gate_up_ref[...] = d_gate_up
    d_second = dot(d_gate_up, ffn_ref[:, : 2 * hidden_width], (1, 1))

    x = dot(patch_ref[...], embed_ref[...], (0, 0))
    attn = attn_ref[...]
    attn_scale = row_rms(attn)
    attn_normed = attn * attn_scale
    mid = x + vec_ref[1:2] * attn_normed
    mid_scale = row_rms(mid)
    mid_sum = jnp.sum(mid * mid_scale * d_second, axis=0, keepdims=True)
    d_last = dot(cot_ref[...], unpatch_ref[...], (0, 0))
    place = lax.broadcasted_iota(jnp.int32, (PAIR, 1), 0) // BLOCK
    mine = (place == core) & (step == chip)
    d_mid = row_rms_back(mid, mid_scale, vec_ref[2:3] * d_second) + jnp.where(mine, d_last, 0.0)
    d_mid_ref[...] = d_mid
    attn_sum = jnp.sum(attn_normed * d_mid, axis=0, keepdims=True)
    d_attn = row_rms_back(attn, attn_scale, vec_ref[1:2] * d_mid).astype(BF16)
    d_attn_ref[...] = d_attn
    for k in range(4):
        mixed_own_ref[k] = dot(out_near_ref[k], d_attn, (1, 1)).astype(BF16)
        mixed_other_ref[k] = dot(out_far_ref[k], d_attn, (1, 1)).astype(BF16)

    @pl.when(step == 0)
    def _():
        sums_ref[...] = jnp.zeros_like(sums_ref)

    sums_ref[0:1] += mid_sum
    sums_ref[1:2] += attn_sum


def backward(at, d_ffn, ffn, out_whole, gate_up, attn, patches, embed, cot_taps, unpatch, vec):
    width = embed.shape[1]
    part = out_whole[0].shape[1]
    hidden_width = ffn.shape[1] // 3
    by_chip = pl.BlockSpec((1, BLOCK, width), lambda t, at: ((t - at[0] + 4) % 4, 0, 0))
    parts = pl.BlockSpec((4, part, PAIR), lambda t, at: (0, 0, t))
    return pl.pallas_call(
        backward_kernel,
        grid_spec=pltpu.PrefetchScalarGridSpec(
            num_scalar_prefetch=1,
            grid=(4,),
            in_specs=[
                by_chip,
                by_chip,
                whole(ffn.shape),
                whole((4, part, width)),
                whole((4, part, width)),
                row_block(PAIR, 2 * hidden_width),
                row_block(PAIR, width),
                lane_block(144, PAIR),
                whole(embed.shape),
                lane_block(144, PAIR),
                whole(unpatch.shape),
                whole(vec.shape),
            ],
            out_specs=[
                row_block(PAIR, width),
                row_block(PAIR, 2 * hidden_width),
                row_block(PAIR, width),
                row_block(PAIR, width),
                parts,
                parts,
                pl.BlockSpec((8, width), lambda t, at: (0, 0)),
            ],
        ),
        out_shape=[
            jax.ShapeDtypeStruct((TOKENS, width), BF16),
            jax.ShapeDtypeStruct((TOKENS, 2 * hidden_width), BF16),
            jax.ShapeDtypeStruct((TOKENS, width), BF16),
            jax.ShapeDtypeStruct((TOKENS, width), F32),
            jax.ShapeDtypeStruct((4, part, TOKENS), BF16),
            jax.ShapeDtypeStruct((4, part, TOKENS), BF16),
            jax.ShapeDtypeStruct((8, width), F32),
        ],
        compiler_params=params(),
        cost_estimate=pl.CostEstimate(
            flops=2 * TOKENS * width * (width + 3 * hidden_width),
            bytes_accessed=36 * 2**20,
            transcendentals=TOKENS * hidden_width,
        ),
        name="backward",
    )(at, *d_ffn, ffn, *out_whole, gate_up, attn, patches, embed, cot_taps, unpatch, vec)


def ffn_grad_kernel(second_ref, d_gate_up_ref, d_ffn_ref, hidden_ref, out_ref):
    split = d_gate_up_ref.shape[1]
    out_ref[:, :split] = dot(second_ref[...], d_gate_up_ref[...], (0, 0)).astype(BF16)
    out_ref[:, split:] = dot(d_ffn_ref[...], hidden_ref[...], (0, 0)).astype(BF16)


def ffn_grads(second, d_gate_up, d_ffn, hidden):
    width = second.shape[1]
    lanes = d_gate_up.shape[1] + hidden.shape[1]
    return pl.pallas_call(
        ffn_grad_kernel,
        grid=(width // 256,),
        in_specs=[
            lane_block(TOKENS, 256),
            whole(d_gate_up.shape),
            lane_block(TOKENS, 256),
            whole(hidden.shape),
        ],
        out_specs=row_block(256, lanes),
        out_shape=jax.ShapeDtypeStruct((width, lanes), BF16),
        compiler_params=params(),
        cost_estimate=pl.CostEstimate(
            flops=2 * TOKENS * width * lanes, bytes_accessed=14 * 2**20, transcendentals=0
        ),
        name="ffn_grads",
    )(second, d_gate_up, d_ffn, hidden)


def first_kernel(
    patch_ref, embed_ref, vec_ref, weight_ref, d_raw_ref, d_mid_ref, place_ref, out_sum_ref,
    qkv_ref, embed_sum_ref, field_ref, sums_ref, qkv_acc, taps_acc,
):
    step = pl.program_id(0)
    last = pl.num_programs(0) - 1
    part = weight_ref.shape[1] // COLS
    x = dot(patch_ref[...], embed_ref[...], (0, 0))
    scale = row_rms(x)
    x_normed = x * scale
    h = (x_normed * vec_ref[0:1]).astype(BF16)
    d_h = dot(d_raw_ref[0], weight_ref[0], (0, 1))
    for s in (1, 2):
        d_h = d_h + dot(d_raw_ref[s], weight_ref[s], (0, 1))

    @pl.when(step == 0)
    def _():
        qkv_acc[...] = jnp.zeros_like(qkv_acc)
        embed_sum_ref[...] = jnp.zeros_like(embed_sum_ref)
        sums_ref[...] = jnp.zeros_like(sums_ref)

    for s in range(3):
        qkv_acc[s] += dot(d_raw_ref[s], h, (1, 0))
    sums_ref[0:1] += jnp.sum(x_normed * d_h, axis=0, keepdims=True)
    d_first = (d_mid_ref[...] + row_rms_back(x, scale, vec_ref[0:1] * d_h)).astype(BF16)
    embed_sum_ref[...] += dot(patch_ref[...], d_first, (1, 0))
    here = pl.ds(pl.multiple_of(step * PAIR, PAIR), PAIR)
    taps_acc[:, here] = dot(embed_ref[...], d_first, (1, 1))

    @pl.when(step == last)
    def _():
        for s in range(4):
            turned = (qkv_acc[s] if s < 3 else out_sum_ref[...]).T.astype(BF16)
            for c in range(COLS):
                qkv_ref[c, s * part : (s + 1) * part] = turned[c * part : (c + 1) * part]
        for r, tile in enumerate(field_of(taps_acc[...], place_ref[...], -1)):
            field_ref[r] = tile


def first_back(patches, embed, vec, weight, d_raw, d_mid, place, out_sum):
    width = embed.shape[1]
    part = weight.shape[2]
    return pl.pallas_call(
        first_kernel,
        grid=(TOKENS // PAIR,),
        in_specs=[
            lane_block(144, PAIR),
            whole(embed.shape),
            whole(vec.shape),
            whole(weight.shape),
            pl.BlockSpec((3, part, PAIR), lambda t: (0, 0, t)),
            row_block(PAIR, width),
            whole(place.shape),
            whole(out_sum.shape),
        ],
        out_specs=[
            pl.BlockSpec((COLS, 4 * width // COLS, part), lambda t: (0, 0, 0)),
            pl.BlockSpec((144, width), lambda t: (0, 0)),
            pl.BlockSpec((ROWS, 16, BLOCK), lambda t: (0, 0, 0)),
            pl.BlockSpec((8, width), lambda t: (0, 0)),
        ],
        out_shape=[
            jax.ShapeDtypeStruct((COLS, 4 * width // COLS, part), BF16),
            jax.ShapeDtypeStruct((144, width), F32),
            jax.ShapeDtypeStruct((ROWS, 16, BLOCK), F32),
            jax.ShapeDtypeStruct((8, width), F32),
        ],
        scratch_shapes=[pltpu.VMEM((3, part, width), F32), pltpu.VMEM((144, TOKENS), F32)],
        compiler_params=params(),
        cost_estimate=pl.CostEstimate(
            flops=2 * TOKENS * width * (6 * part + 3 * 144),
            bytes_accessed=16 * 2**20,
            transcendentals=0,
        ),
        name="first_back",
    )(patches, embed, vec, weight, d_raw, d_mid, place, out_sum)


def field_kernel(taps_ref, place_ref, field_ref):
    for r, tile in enumerate(field_of(taps_ref[...], place_ref[...], 1)):
        field_ref[r] = tile


def local(
    latent, condition, caption, cap_len, cotangent, embed_weight, modulate_weight, norm_gains,
    cross_gate, qkv_weight, text_kv_weight, out_weight, gate_up_weight, down_weight, unpatch_weight,
):
    images, _, _, channels = latent.shape
    width = embed_weight.shape[3]
    local_width = qkv_weight.shape[2]
    heads = local_width // HD
    hidden_width = down_weight.shape[0]
    taps = 9 * channels
    row_at = lax.axis_index("row")
    col_at = lax.axis_index("col")
    at = jnp.stack([row_at // 2, row_at % 2]).astype(jnp.int32)
    tile = latent.shape[1] * latent.shape[2] * channels

    cond_low = jax.nn.silu(condition.astype(F32)).astype(BF16)
    mod_piece = jnp.dot(cond_low, modulate_weight, preferred_element_type=F32)
    mod_columns = mod_piece.shape[1]
    mod_high = mod_piece.astype(BF16)
    mod_low = (mod_piece - mod_high.astype(F32)).astype(BF16)

    def one_row(values):
        return jnp.pad(values, ((0, 0), (0, local_width - values.shape[1])))[:, None]

    packed = jnp.concatenate(
        [
            one_row(latent.reshape(images, tile)),
            one_row(cotangent.reshape(images, tile)),
            one_row(mod_high),
            one_row(mod_low),
            jnp.zeros((images, 12, local_width), BF16),
        ],
        axis=1,
    )

    head_piece = jnp.concatenate(
        [qkv_weight.reshape(-1, local_width), out_weight.T], axis=0
    )
    piece_rows = head_piece.shape[0]
    head_piece = jnp.broadcast_to(head_piece, (COLS,) + head_piece.shape)
    head_pieces = lax.all_to_all(jnp.concatenate([head_piece, packed], axis=1), "col", 0, 0)
    packed = head_pieces[:, piece_rows : piece_rows + 4, :tile].transpose(1, 0, 2)
    packed = send_all(packed, "row")

    text_piece = jnp.concatenate([text_kv_weight[0], text_kv_weight[1]], axis=1)
    text_whole = lax.all_gather(text_piece, "col", axis=0, tiled=True)
    ffn_piece = jnp.concatenate([gate_up_weight[0], gate_up_weight[1], down_weight.T], axis=1)
    ffn_whole = lax.all_gather(after(ffn_piece, text_whole), "col", axis=0, tiled=True)

    patches, cot_taps = image_taps(packed)
    modulation = packed[:, 2].astype(F32) + packed[:, 3].astype(F32)
    modulation = modulation[:, :, :mod_columns].reshape(4, width)
    attn_gate = jnp.tanh(modulation[1])
    ffn_gate = jnp.tanh(modulation[3])
    vec = jnp.stack(
        [
            norm_gains[0] * (1.0 + modulation[0]),
            norm_gains[1] * attn_gate,
            norm_gains[2] * (1.0 + modulation[2]),
            norm_gains[3] * ffn_gate,
        ]
    )
    vec = jnp.pad(vec, ((0, 4), (0, 0)))
    embed = embed_weight.reshape(taps, width)
    unpatch = unpatch_weight.transpose(0, 1, 3, 2).reshape(taps, width)
    raw, qkv_whole, out_rows = qkv_project(patches, embed, vec, head_pieces)
    out_whole = gather_near(out_rows)
    raw = raw.reshape(3, heads, HD, TOKENS)
    caption_rows = caption[0]
    text_raw = dot(text_whole, caption_rows, (0, 1)).reshape(2, heads, HD, caption_rows.shape[0])
    head_gains = lax.dynamic_slice(norm_gains, (4, row_at * local_width), (3, local_width)).reshape(
        3, heads, HD, 1
    )
    head_gates = jnp.tanh(lax.dynamic_slice_in_dim(cross_gate, row_at * heads, heads))
    cap = lax.dynamic_slice_in_dim(cap_len, col_at, 1)
    table = jnp.asarray(rope_tables())
    mixed, lse = attend(raw, text_raw, head_gains, table, cap, head_gates)

    mixed_whole = gather_near(mixed)
    attn, second, gate_up, hidden, ffn_own, ffn_other = forward(
        at, mixed_whole, out_whole, patches, embed, vec, ffn_whole
    )
    d_ffn_own, last_taps, unpatch_sum, own_sums = own_block(
        at, to_chips(sum_cores(ffn_own, ffn_other)), attn, patches, cot_taps, embed, unpatch, vec
    )
    d_ffn, d_gate_up, d_attn, d_mid, mixed_own, mixed_other, back_sums = backward(
        at, gather_near(d_ffn_own), ffn_whole, out_whole, gate_up, attn, patches, embed, cot_taps,
        unpatch, vec,
    )
    mixed_near = sum_cores(mixed_own, mixed_other)
    mixed_terms = to_chips(mixed_near)
    ffn_sum = ffn_grads(after(second, *mixed_near), d_gate_up, d_ffn, hidden)
    ffn_sum = ffn_sum.reshape(COLS, width // COLS, -1)
    ffn_total = lax.all_to_all(ffn_sum, "col", 0, 0)
    d_attn = after(d_attn, ffn_sum)
    out_parts = [
        jnp.einsum("ken,nd->ked", pieces, d_attn, preferred_element_type=F32).astype(BF16)
        for pieces in mixed_whole
    ]
    reached = lax.optimization_barrier((*mixed_terms, *sum_cores(*out_parts)))
    d_mixed = sum(term.astype(F32) for term in reached[:4]).astype(BF16)
    out_terms = to_chips(reached[4:])

    d_raw, d_text, d_head = attend_back(
        raw, text_raw, head_gains, table, lse, d_mixed.reshape(heads, HD, TOKENS), cap, head_gates
    )
    text_sum = dot(caption_rows, d_text.reshape(2 * local_width, -1), (0, 1)).astype(BF16)
    d_raw = after(d_raw, text_sum)
    place = tile_places(False)
    out_sum = sum(term.astype(F32) for term in out_terms)
    head_parts, embed_sum, latent_field, first_sums = first_back(
        patches, embed, vec, qkv_whole, d_raw.reshape(3, local_width, TOKENS), d_mid, place, out_sum
    )
    activation_field = pl.pallas_call(
        field_kernel,
        out_shape=jax.ShapeDtypeStruct((ROWS, channels, BLOCK), F32),
        compiler_params=pltpu.CompilerParams(vmem_limit_bytes=VMEM),
        name="activation_field",
    )(
        lax.dynamic_update_slice(jnp.zeros((taps, TOKENS), F32), last_taps, (0, row_at * BLOCK)),
        place,
    )

    terms = jnp.stack([first_sums[0], back_sums[1], back_sums[0], own_sums[0]])
    one = jnp.ones_like(attn_gate)
    d_modulation = terms * jnp.stack(
        [
            norm_gains[0],
            norm_gains[1] * (1.0 - attn_gate * attn_gate),
            norm_gains[2],
            norm_gains[3] * (1.0 - ffn_gate * ffn_gate),
        ]
    )
    d_gains = terms * jnp.stack([one + modulation[0], attn_gate, one + modulation[2], ffn_gate])
    head_rows = lax.dynamic_update_slice(
        jnp.zeros((3, width), F32), d_head[:3].reshape(3, local_width), (0, row_at * local_width)
    )
    gate_part = jnp.sum(d_head[3], axis=(1, 2)) * (1.0 - head_gates * head_gates)
    gate_row = lax.dynamic_update_slice(
        jnp.zeros((1, width), F32), gate_part[None], (0, row_at * heads)
    )
    shared = jnp.concatenate(
        [embed_sum, unpatch_sum, d_gains, head_rows, gate_row, jnp.zeros((24, width), F32)]
    )
    per_row = shared.shape[0] * width // (ROWS * 128)
    row_pack = jnp.concatenate(
        [
            shared.astype(BF16).reshape(ROWS, per_row, 128),
            activation_field.astype(BF16),
            latent_field.astype(BF16),
            jnp.pad(d_modulation.astype(BF16).reshape(ROWS, 6, 128), ((0, 0), (0, 10), (0, 0))),
        ],
        axis=1,
    )
    row_pack = jnp.sum(lax.all_to_all(row_pack, "row", 0, 0).astype(F32), axis=0)
    fields = row_pack[per_row : per_row + 2 * channels]
    fields = fields.T.reshape(COLS, 8, 2 * channels)
    mod_sums = row_pack[per_row + 2 * channels : per_row + 2 * channels + 6]
    fields = jnp.concatenate([fields, mod_sums.reshape(COLS, 8, 6)], axis=2).astype(BF16)
    fields = jnp.pad(fields, ((0, 0), (0, 4), (0, local_width - fields.shape[2])))
    shared = row_pack[:per_row].astype(BF16).reshape(COLS, -1, local_width)
    shared_rows = shared.shape[1]
    col_pack = lax.all_to_all(jnp.concatenate([head_parts, shared, fields], axis=1), "col", 0, 0)
    fields = col_pack[:, piece_rows + shared_rows : piece_rows + shared_rows + 8]
    shared = jnp.sum(col_pack[:, piece_rows : piece_rows + shared_rows].astype(F32), axis=0)
    shared = send_all(send_all(shared.astype(BF16), "col"), "row").reshape(-1, width).astype(F32)
    activation = fields[:, :, :channels].reshape(latent.shape)
    latent_grad = fields[:, :, channels : 2 * channels].reshape(latent.shape)
    modulate_grad = lax.dot_general(
        cond_low.astype(F32),
        fields[:, :, 2 * channels : 2 * channels + 6].reshape(images, mod_columns).astype(F32),
        (((0,), (0,)), ((), ())),
        precision=lax.Precision.HIGHEST,
        preferred_element_type=F32,
    )
    embed_grad = shared[:taps].reshape(embed_weight.shape)
    unpatch_grad = shared[taps : 2 * taps].reshape(3, 3, channels, width).transpose(0, 1, 3, 2)
    gains_grad = shared[2 * taps : 2 * taps + 7]
    gate_grad = shared[2 * taps + 7, :HEADS]

    ffn_total = jnp.sum(ffn_total.astype(F32), axis=0)
    gate_up_grad = jnp.stack(
        [ffn_total[:, :hidden_width], ffn_total[:, hidden_width : 2 * hidden_width]]
    )
    down_grad = ffn_total[:, 2 * hidden_width :].T
    text_total = lax.psum_scatter(text_sum, "col", scatter_dimension=0, tiled=True).astype(F32)
    text_kv_grad = jnp.stack([text_total[:, :local_width], text_total[:, local_width:]])
    head_total = jnp.sum(col_pack[:, :piece_rows].astype(F32), axis=0)
    qkv_rows = piece_rows * 3 // 4
    qkv_grad = head_total[:qkv_rows].reshape(qkv_weight.shape)
    out_grad = head_total[qkv_rows:].T
    return (
        activation, latent_grad, embed_grad, modulate_grad, gains_grad, gate_grad,
        qkv_grad, text_kv_grad, out_grad, gate_up_grad, down_grad, unpatch_grad,
    )


def solution(mesh):
    placed = (
        P(None, "row", "col", None),
        P(),
        P("col", None, None),
        P(),
        P(None, "row", "col", None),
        P(),
        P(None, ("row", "col")),
        P(),
        P(),
        P(None, "col", "row"),
        P(None, "col", "row"),
        P("row", "col"),
        P(None, "col", "row"),
        P("row", "col"),
        P(),
    )
    return jax.shard_map(
        local,
        mesh=mesh,
        in_specs=placed,
        out_specs=(
            P(None, "row", "col", None),
            P(None, "row", "col", None),
            P(),
            P(None, ("row", "col")),
            P(),
            P(),
            P(None, "col", "row"),
            P(None, "col", "row"),
            P("row", "col"),
            P(None, "col", "row"),
            P("row", "col"),
            P(),
        ),
        check_vma=False,
    )
```

```python
import math
from functools import partial

import jax
import jax.numpy as jnp
import numpy as np
from jax import lax
from jax.experimental import pallas as pl
from jax.experimental.pallas import tpu as pltpu
from jax.sharding import PartitionSpec as P

HEADS = 24
HD = 64
GRID = 32
TOKENS = GRID * GRID
EPSILON = 1e-06
ROPE_BASE = 10000.0
MASKED = -1e30
F32 = jnp.float32
BF16 = jnp.bfloat16
ROWS = 8
COLS = 16
QUERY_BLOCK = 256
BLOCK = TOKENS // ROWS
PAIR = 2 * BLOCK
VMEM = 56 * 2**20
SHARED = 320
CHUNK = 512
LIGHT = pl.CostEstimate(flops=1, bytes_accessed=1, transcendentals=0)


def dot(left, right, contract):
    return lax.dot_general(
        left, right, ((contract[:1], contract[1:]), ((), ())), preferred_element_type=F32
    )


def row_pairs(dx, dc):
    return [
        (((x + dx) % 4) * 2 + (c + dc) % 2, x * 2 + c) for x in range(4) for c in range(2)
    ]


def row_pairs_to(dx, dc):
    return [(dst, src) for src, dst in row_pairs(dx, dc)]


def gather_near(piece):
    quad = jnp.stack([piece] + [lax.ppermute(piece, "row", row_pairs(d, 0)) for d in (1, 2, 3)])
    return quad, lax.ppermute(quad, "row", row_pairs(0, 1))


def sum_cores(own, other):
    other = lax.ppermute(other, "row", row_pairs(0, 1))
    return [(own[d].astype(F32) + other[d].astype(F32)).astype(BF16) for d in range(4)]


def to_chips(near):
    return [near[0]] + [lax.ppermute(near[d], "row", row_pairs_to(d, 0)) for d in (1, 2, 3)]


def col_pairs_to(dy, dz):
    return [(y * 4 + z, (y + dy) % 4 * 4 + (z + dz) % 4) for y in range(4) for z in range(4)]


def scatter_col(parts):
    near = parts[0].astype(F32)
    for d in (1, 2, 3):
        near = near + lax.ppermute(parts[d], "col", col_pairs_to(0, d)).astype(F32)
    near = near.astype(BF16)
    total = near[0].astype(F32)
    for d in (1, 2, 3):
        total = total + lax.ppermute(near[d], "col", col_pairs_to(d, 0)).astype(F32)
    return total


def send_all(piece, axis):
    copies = jnp.broadcast_to(piece, (lax.axis_size(axis),) + piece.shape)
    return lax.all_to_all(copies, axis, 0, 0)


def after(value, *others):
    return lax.optimization_barrier((value,) + others)[0]


def rope_tables():
    quarter = HD // 4
    frequency = np.float32(ROPE_BASE) ** (-np.arange(quarter, dtype=np.float32) / np.float32(quarter))
    place = np.arange(TOKENS)
    row = frequency[:, None] * (place // GRID).astype(np.float32)[None, :]
    col = frequency[:, None] * (place % GRID).astype(np.float32)[None, :]
    return np.stack([np.cos(row), np.sin(row), np.cos(col), np.sin(col)]).astype(np.float32)


def turn(v, table, sign):
    a, b, c, d = (v[k * 16 : (k + 1) * 16] for k in range(4))
    cr, sr, cc, sc = table[0], table[1] * sign, table[2], table[3] * sign
    return jnp.concatenate([a * cr - b * sr, a * sr + b * cr, c * cc - d * sc, c * sc + d * cc], 0)


def column_rms(v):
    return lax.rsqrt(jnp.mean(v * v, axis=0, keepdims=True) + EPSILON)


def normed(v, gain):
    return v * column_rms(v) * gain


def column_rms_back(v, u):
    scale = column_rms(v)
    return (u - v * (jnp.mean(u * v, axis=0, keepdims=True) * scale * scale)) * scale


def whole(shape):
    zeros = (0,) * len(shape)
    return pl.BlockSpec(shape, lambda *_: zeros, pipeline_mode=pl.Buffered(1))


def lane_block(rows, lanes):
    return pl.BlockSpec((rows, lanes), lambda t, *_: (0, t))


def row_block(rows, lanes):
    return pl.BlockSpec((rows, lanes), lambda t, *_: (t, 0))


def params():
    return pltpu.CompilerParams(vmem_limit_bytes=VMEM, dimension_semantics=("arbitrary",))


def attend_kernel(
    cap_ref, gate_ref, raw_ref, text_ref, gain_ref, table_ref, mixed_ref, lse_ref,
    q_ref, k_ref, v_ref, tk_ref, tv_ref,
):
    step = pl.program_id(0)
    heads = raw_ref.shape[1]

    @pl.when(step == 0)
    def _():
        table = table_ref[...]
        for h in range(heads):
            q = turn(normed(raw_ref[0, h], gain_ref[0, h]), table, 1.0).astype(BF16)
            q_ref[h] = q * jnp.asarray(0.125, BF16)
            k_ref[h] = turn(normed(raw_ref[1, h], gain_ref[1, h]), table, 1.0).astype(BF16)
            v_ref[h] = raw_ref[2, h].astype(BF16)
            tk_ref[h] = normed(text_ref[0, h], gain_ref[2, h]).astype(BF16)
            tv_ref[h] = text_ref[1, h].astype(BF16)

    slots = tk_ref.shape[2]
    mask = lax.broadcasted_iota(jnp.int32, (slots, QUERY_BLOCK), 0) < cap_ref[0]
    here = pl.ds(pl.multiple_of(step * QUERY_BLOCK, QUERY_BLOCK), QUERY_BLOCK)
    outs = []
    for h in range(heads):
        qb = q_ref[h, :, here]
        e = jnp.exp(dot(k_ref[h], qb, (0, 0)))
        total = jnp.sum(e, axis=0, keepdims=True)
        own = dot(v_ref[h], e.astype(BF16), (1, 0)) / total
        te = jnp.exp(jnp.where(mask, dot(tk_ref[h], qb, (0, 0)), MASKED))
        text_total = jnp.sum(te, axis=0, keepdims=True)
        text = dot(tv_ref[h], te.astype(BF16), (1, 0)) / text_total
        outs.append(own + gate_ref[h] * text)
        lse_ref[h, 0:1] = jnp.log(total)
        lse_ref[h, 1:2] = jnp.log(text_total)
    mixed_ref[...] = jnp.concatenate(outs, 0).astype(BF16)


def attend(raw, text_raw, gains, table, cap, gates):
    heads = raw.shape[1]
    slots = text_raw.shape[3]
    return pl.pallas_call(
        attend_kernel,
        grid_spec=pltpu.PrefetchScalarGridSpec(
            num_scalar_prefetch=2,
            grid=(TOKENS // QUERY_BLOCK,),
            in_specs=[
                whole((3, heads, HD, TOKENS)),
                whole((2, heads, HD, slots)),
                whole((3, heads, HD, 1)),
                whole((4, 16, TOKENS)),
            ],
            out_specs=[
                lane_block(heads * HD, QUERY_BLOCK),
                pl.BlockSpec((heads, 8, QUERY_BLOCK), lambda t, *_: (0, 0, t)),
            ],
            scratch_shapes=[
                pltpu.VMEM((heads, HD, TOKENS), BF16),
                pltpu.VMEM((heads, HD, TOKENS), BF16),
                pltpu.VMEM((heads, HD, TOKENS), BF16),
                pltpu.VMEM((heads, HD, slots), BF16),
                pltpu.VMEM((heads, HD, slots), BF16),
            ],
        ),
        out_shape=[
            jax.ShapeDtypeStruct((heads * HD, TOKENS), BF16),
            jax.ShapeDtypeStruct((heads, 8, TOKENS), F32),
        ],
        compiler_params=params(),
        cost_estimate=LIGHT,
        name="attend",
    )(cap, gates, raw, text_raw, gains, table)


def attend_back_kernel(
    cap_ref, gate_ref, raw_ref, text_ref, gain_ref, table_ref, lse_ref, grad_ref,
    d_raw_ref, d_text_ref, d_gain_ref, dv_ref, dk_ref, dq_ref, dtv_ref, dtk_ref,
):
    table = table_ref[...]
    head = pl.program_id(0)
    gate = gate_ref[head]
    q = turn(normed(raw_ref[0], gain_ref[0]), table, 1.0).astype(BF16) * jnp.asarray(0.125, BF16)
    k = turn(normed(raw_ref[1], gain_ref[1]), table, 1.0).astype(BF16)
    v = raw_ref[2].astype(BF16)
    tk = normed(text_ref[0], gain_ref[2]).astype(BF16)
    tv = text_ref[1].astype(BF16)
    slots = tk.shape[1]
    mask = lax.broadcasted_iota(jnp.int32, (slots, QUERY_BLOCK), 0) < cap_ref[0]
    gate_sum = jnp.zeros((HD, QUERY_BLOCK), F32)
    for first in range(0, TOKENS, QUERY_BLOCK):
        here = slice(first, first + QUERY_BLOCK)
        qb = q[:, here]
        gb = grad_ref[:, here]
        p = jnp.exp(dot(k, qb, (0, 0)) - lse_ref[0:1, here])
        dv = dot(gb, p.astype(BF16), (1, 1))
        pd = p * dot(v, gb, (0, 0))
        ds = (pd - p * jnp.sum(pd, axis=0, keepdims=True)).astype(BF16)
        dq = dot(k, ds, (1, 0))
        dk = dot(qb, ds, (1, 1))
        tp = jnp.exp(jnp.where(mask, dot(tk, qb, (0, 0)), MASKED) - lse_ref[1:2, here])
        tpb = tp.astype(BF16)
        dtv = dot(gb, tpb, (1, 1))
        gate_sum = gate_sum + gb.astype(F32) * dot(tv, tpb, (1, 0))
        tpd = tp * dot(tv, gb, (0, 0)) * gate
        dts = (tpd - tp * jnp.sum(tpd, axis=0, keepdims=True)).astype(BF16)
        dq_ref[:, here] = dq + dot(tk, dts, (1, 0))
        dtk = dot(qb, dts, (1, 1))
        if first == 0:
            dv_ref[...] = dv
            dk_ref[...] = dk
            dtv_ref[...] = dtv
            dtk_ref[...] = dtk
        else:
            dv_ref[...] += dv
            dk_ref[...] += dk
            dtv_ref[...] += dtv
            dtk_ref[...] += dtk

    def raw_back(which, d_turned):
        spun = turn(d_turned.astype(BF16).astype(F32), table, -1.0)
        values = raw_ref[which]
        d_raw_ref[which] = column_rms_back(values, spun * gain_ref[which]).astype(BF16)
        d_gain_ref[which] = jnp.sum(values * column_rms(values) * spun, axis=1, keepdims=True)

    raw_back(0, dq_ref[...] * 0.125)
    raw_back(1, dk_ref[...])
    d_raw_ref[2] = dv_ref[...].astype(BF16)
    values = text_ref[0]
    d_tk = dtk_ref[...]
    d_text_ref[0] = column_rms_back(values, d_tk * gain_ref[2]).astype(BF16)
    d_gain_ref[2] = jnp.sum(values * column_rms(values) * d_tk, axis=1, keepdims=True)
    d_text_ref[1] = (dtv_ref[...] * gate).astype(BF16)
    d_gain_ref[3] = jnp.sum(gate_sum, axis=1, keepdims=True)


def attend_back(raw, text_raw, gains, table, lse, grads, cap, gates):
    heads = raw.shape[1]
    slots = text_raw.shape[3]
    return pl.pallas_call(
        attend_back_kernel,
        grid_spec=pltpu.PrefetchScalarGridSpec(
            num_scalar_prefetch=2,
            grid=(heads,),
            in_specs=[
                pl.BlockSpec((3, None, HD, TOKENS), lambda h, *_: (0, h, 0, 0)),
                pl.BlockSpec((2, None, HD, slots), lambda h, *_: (0, h, 0, 0)),
                pl.BlockSpec((3, None, HD, 1), lambda h, *_: (0, h, 0, 0)),
                pl.BlockSpec((4, 16, TOKENS), lambda h, *_: (0, 0, 0)),
                pl.BlockSpec((None, 8, TOKENS), lambda h, *_: (h, 0, 0)),
                pl.BlockSpec((None, HD, TOKENS), lambda h, *_: (h, 0, 0)),
            ],
            out_specs=[
                pl.BlockSpec((3, None, HD, TOKENS), lambda h, *_: (0, h, 0, 0)),
                pl.BlockSpec((2, None, HD, slots), lambda h, *_: (0, h, 0, 0)),
                pl.BlockSpec((4, None, HD, 1), lambda h, *_: (0, h, 0, 0)),
            ],
            scratch_shapes=[
                pltpu.VMEM((HD, TOKENS), F32),
                pltpu.VMEM((HD, TOKENS), F32),
                pltpu.VMEM((HD, TOKENS), F32),
                pltpu.VMEM((HD, slots), F32),
                pltpu.VMEM((HD, slots), F32),
            ],
        ),
        out_shape=[
            jax.ShapeDtypeStruct((3, heads, HD, TOKENS), BF16),
            jax.ShapeDtypeStruct((2, heads, HD, slots), BF16),
            jax.ShapeDtypeStruct((4, heads, HD, 1), F32),
        ],
        compiler_params=pltpu.CompilerParams(vmem_limit_bytes=48 * 2**20),
        cost_estimate=LIGHT,
    )(cap, gates, raw, text_raw, gains, table, lse, grads)


def tile_places(chunk_first):
    r, c, k = np.meshgrid(np.arange(ROWS), np.arange(COLS), np.arange(8), indexing="ij")
    token = r * BLOCK + (k // 2) * GRID + c * 2 + k % 2
    source = (k * ROWS + r) * COLS + c if chunk_first else (r * COLS + c) * 8 + k
    places = np.zeros((TOKENS, TOKENS), np.float32)
    places[source.ravel(), token.ravel()] = 1.0
    return jnp.asarray(places, BF16)


def grid_shift(field, di, dj):
    step = di * GRID + dj
    moved = pltpu.roll(field, (-step) % TOKENS, 1) if step else field
    place = lax.broadcasted_iota(jnp.int32, field.shape, 1)
    row = place // GRID + di
    col = place % GRID + dj
    inside = (row >= 0) & (row < GRID) & (col >= 0) & (col < GRID)
    return jnp.where(inside, moved, 0.0)


def image_kernel(packed_ref, place_ref, patch_ref, cot_ref):
    for which, sign, out_ref in ((0, 1, patch_ref), (1, -1, cot_ref)):
        lanes = slice(which * 128, (which + 1) * 128)
        tiles = jnp.concatenate([packed_ref[r, :, lanes] for r in range(ROWS)], 0)
        turned = tiles.astype(F32).T
        chunks = jnp.concatenate([turned[k * 16 : (k + 1) * 16] for k in range(8)], 1)
        image = dot(chunks.astype(BF16), place_ref[...], (1, 0))
        for a in range(3):
            for b in range(3):
                first = (a * 3 + b) * 16
                out_ref[first : first + 16] = grid_shift(
                    image, sign * (a - 1), sign * (b - 1)
                ).astype(BF16)


def image_taps(packed):
    out = jax.ShapeDtypeStruct((144, TOKENS), BF16)
    return pl.pallas_call(
        image_kernel,
        out_shape=[out, out],
        compiler_params=pltpu.CompilerParams(vmem_limit_bytes=VMEM),
        cost_estimate=LIGHT,
        name="image_taps",
    )(packed, tile_places(True))


def field_of(taps, place, sign):
    total = jnp.zeros((16, TOKENS), F32)
    for a in range(3):
        for b in range(3):
            first = (a * 3 + b) * 16
            total = total + grid_shift(taps[first : first + 16], sign * (a - 1), sign * (b - 1))
    tiles = dot(total.astype(BF16), place, (1, 1))
    return [tiles[:, r * BLOCK : (r + 1) * BLOCK] for r in range(ROWS)]


def row_rms(v):
    return lax.rsqrt(jnp.mean(v * v, axis=-1, keepdims=True) + EPSILON)


def row_rms_back(v, scale, u):
    return (u - v * (jnp.mean(u * v, axis=-1, keepdims=True) * scale * scale)) * scale


def qkv_kernel(patch_ref, embed_ref, vec_ref, weight_ref, raw_ref, joined_ref, out_ref, turn_ref):
    width = embed_ref.shape[1]
    local_width = joined_ref.shape[2]
    part = width // COLS

    @pl.when(pl.program_id(0) == 0)
    def _():
        for c in range(COLS):
            here = slice(c * part, (c + 1) * part)
            for s in range(4):
                first = s // 2 * part
                lanes = slice(s % 2 * local_width, (s % 2 + 1) * local_width)
                piece = weight_ref[c, first : first + part, lanes]
                if s < 3:
                    joined_ref[s, here] = piece
                else:
                    turn_ref[here] = piece
        out_ref[...] = turn_ref[...].T

    x = dot(patch_ref[...], embed_ref[...], (0, 0))
    h = (x * row_rms(x) * vec_ref[0:1]).astype(BF16)
    for s in range(3):
        raw_ref[s] = dot(h, joined_ref[s], (1, 0)).T


def qkv_project(patches, embed, vec, weight):
    width = embed.shape[1]
    part = weight.shape[2] // 2
    return pl.pallas_call(
        qkv_kernel,
        grid=(TOKENS // PAIR,),
        in_specs=[
            lane_block(144, PAIR),
            whole(embed.shape),
            whole(vec.shape),
            whole(weight.shape),
        ],
        out_specs=[
            pl.BlockSpec((3, part, PAIR), lambda t: (0, 0, t)),
            pl.BlockSpec((3, width, part), lambda t: (0, 0, 0)),
            pl.BlockSpec((part, width), lambda t: (0, 0)),
        ],
        out_shape=[
            jax.ShapeDtypeStruct((3, part, TOKENS), F32),
            jax.ShapeDtypeStruct((3, width, part), BF16),
            jax.ShapeDtypeStruct((part, width), BF16),
        ],
        scratch_shapes=[pltpu.VMEM((width, part), BF16)],
        compiler_params=params(),
        cost_estimate=LIGHT,
        name="qkv_project",
    )(patches, embed, vec, weight)


def halves(core, first, second):
    return jnp.where(core == 0, first, second)


def forward_kernel(
    at_ref, near_ref, far_ref, out_near_ref, out_far_ref, patch_ref, embed_ref, vec_ref, ffn_ref,
    attn_ref, second_ref, gate_up_ref, hidden_ref, own_ref, other_ref,
):
    core = at_ref[1]
    hidden_width = hidden_ref.shape[1]
    x = dot(patch_ref[...], embed_ref[...], (0, 0))
    attn = dot(near_ref[0], out_near_ref[0], (0, 0))
    for k in range(1, 4):
        attn = attn + dot(near_ref[k], out_near_ref[k], (0, 0))
    for k in range(4):
        attn = attn + dot(far_ref[k], out_far_ref[k], (0, 0))
    attn_ref[...] = attn
    mid = x + vec_ref[1:2] * (attn * row_rms(attn))
    second = (mid * row_rms(mid) * vec_ref[2:3]).astype(BF16)
    second_ref[...] = second
    gate_up = dot(second, ffn_ref[:, : 2 * hidden_width], (1, 0))
    gate_up_ref[...] = gate_up
    gate = gate_up[:, :hidden_width]
    hidden = (gate * jax.nn.sigmoid(gate) * gate_up[:, hidden_width:]).astype(BF16)
    hidden_ref[...] = hidden
    part = dot(hidden, ffn_ref[:, 2 * hidden_width :], (1, 1)).astype(BF16)
    own_ref[0] = halves(core, part[:BLOCK], part[BLOCK:])
    other_ref[0] = halves(core, part[BLOCK:], part[:BLOCK])


def forward(at, mixed, out_whole, patches, embed, vec, ffn):
    width = embed.shape[1]
    part = mixed[0].shape[1]
    hidden_width = ffn.shape[1] // 3
    by_chip = pl.BlockSpec((1, BLOCK, width), lambda t, at: ((t - at[0] + 4) % 4, 0, 0))
    return pl.pallas_call(
        forward_kernel,
        grid_spec=pltpu.PrefetchScalarGridSpec(
            num_scalar_prefetch=1,
            grid=(4,),
            in_specs=[
                pl.BlockSpec((4, part, PAIR), lambda t, at: (0, 0, t)),
                pl.BlockSpec((4, part, PAIR), lambda t, at: (0, 0, t)),
                whole((4, part, width)),
                whole((4, part, width)),
                lane_block(144, PAIR),
                whole(embed.shape),
                whole(vec.shape),
                whole(ffn.shape),
            ],
            out_specs=[
                row_block(PAIR, width),
                row_block(PAIR, width),
                row_block(PAIR, 2 * hidden_width),
                row_block(PAIR, hidden_width),
                by_chip,
                by_chip,
            ],
        ),
        out_shape=[
            jax.ShapeDtypeStruct((TOKENS, width), F32),
            jax.ShapeDtypeStruct((TOKENS, width), BF16),
            jax.ShapeDtypeStruct((TOKENS, 2 * hidden_width), F32),
            jax.ShapeDtypeStruct((TOKENS, hidden_width), BF16),
            jax.ShapeDtypeStruct((4, BLOCK, width), BF16),
            jax.ShapeDtypeStruct((4, BLOCK, width), BF16),
        ],
        compiler_params=params(),
        cost_estimate=LIGHT,
        name="forward",
    )(at, *mixed, *out_whole, patches, embed, vec, ffn)


def own_kernel(
    at_ref, p0_ref, p1_ref, p2_ref, p3_ref, attn_ref, patch_ref, cot_ref, embed_ref, unpatch_ref,
    vec_ref, d_ffn_ref, taps_ref, unpatch_sum_ref, sums_ref,
):
    ffn = sum(p[...].astype(F32) for p in (p0_ref, p1_ref, p2_ref, p3_ref))
    d_last = dot(cot_ref[...], unpatch_ref[...], (0, 0))
    scale = row_rms(ffn)
    gated = vec_ref[3:4]
    d_ffn_ref[...] = row_rms_back(ffn, scale, gated * d_last).astype(BF16)
    normed_ffn = ffn * scale
    sums_ref[...] = jnp.broadcast_to(
        jnp.sum(normed_ffn * d_last, axis=0, keepdims=True), sums_ref.shape
    )
    attn = attn_ref[...]
    x = dot(patch_ref[...], embed_ref[...], (0, 0))
    last = (x + vec_ref[1:2] * (attn * row_rms(attn)) + gated * normed_ffn).astype(BF16)
    taps_ref[...] = dot(unpatch_ref[...], last, (1, 1))
    unpatch_sum_ref[...] = dot(cot_ref[...], last, (1, 0))


def own_block(at, pieces, attn, patches, cot_taps, embed, unpatch, vec):
    width = embed.shape[1]
    piece = pl.BlockSpec((BLOCK, width), lambda t, at: (0, 0))
    lanes = pl.BlockSpec((144, BLOCK), lambda t, at: (0, 2 * at[0] + at[1]))
    return pl.pallas_call(
        own_kernel,
        grid_spec=pltpu.PrefetchScalarGridSpec(
            num_scalar_prefetch=1,
            grid=(1,),
            in_specs=[piece] * 4
            + [
                pl.BlockSpec((BLOCK, width), lambda t, at: (2 * at[0] + at[1], 0)),
                lanes,
                lanes,
                whole(embed.shape),
                whole(unpatch.shape),
                whole(vec.shape),
            ],
            out_specs=[
                piece,
                pl.BlockSpec((144, BLOCK), lambda t, at: (0, 0)),
                pl.BlockSpec((144, width), lambda t, at: (0, 0)),
                pl.BlockSpec((8, width), lambda t, at: (0, 0)),
            ],
        ),
        out_shape=[
            jax.ShapeDtypeStruct((BLOCK, width), BF16),
            jax.ShapeDtypeStruct((144, BLOCK), F32),
            jax.ShapeDtypeStruct((144, width), F32),
            jax.ShapeDtypeStruct((8, width), F32),
        ],
        compiler_params=params(),
        cost_estimate=LIGHT,
        name="own_block",
    )(at, *pieces, attn, patches, cot_taps, embed, unpatch, vec)


def backward_kernel(
    at_ref, own_ref, other_ref, ffn_ref, out_near_ref, out_far_ref, gate_up_ref, attn_ref,
    patch_ref, embed_ref, cot_ref, unpatch_ref, vec_ref,
    d_ffn_ref, d_gate_up_ref, d_attn_ref, d_mid_ref, mixed_own_ref, mixed_other_ref, sums_ref,
):
    step = pl.program_id(0)
    chip, core = at_ref[0], at_ref[1]
    hidden_width = d_gate_up_ref.shape[1] // 2
    own, other = own_ref[0], other_ref[0]
    d_ffn = jnp.concatenate([halves(core, own, other), halves(core, other, own)], 0)
    d_ffn_ref[...] = d_ffn
    d_hidden = dot(d_ffn, ffn_ref[:, 2 * hidden_width :], (1, 0))
    gate = gate_up_ref[:, :hidden_width]
    up = gate_up_ref[:, hidden_width:]
    sigma = jax.nn.sigmoid(gate)
    silu = gate * sigma
    d_gate = d_hidden * up * (sigma + silu * (1.0 - sigma))
    d_gate_up = jnp.concatenate([d_gate.astype(BF16), (d_hidden * silu).astype(BF16)], 1)
    d_gate_up_ref[...] = d_gate_up
    d_second = dot(d_gate_up, ffn_ref[:, : 2 * hidden_width], (1, 1))

    x = dot(patch_ref[...], embed_ref[...], (0, 0))
    attn = attn_ref[...]
    attn_scale = row_rms(attn)
    attn_normed = attn * attn_scale
    mid = x + vec_ref[1:2] * attn_normed
    mid_scale = row_rms(mid)
    mid_sum = jnp.sum(mid * mid_scale * d_second, axis=0, keepdims=True)
    d_last = dot(cot_ref[...], unpatch_ref[...], (0, 0))
    place = lax.broadcasted_iota(jnp.int32, (PAIR, 1), 0) // BLOCK
    mine = (place == core) & (step == chip)
    d_mid = row_rms_back(mid, mid_scale, vec_ref[2:3] * d_second) + jnp.where(mine, d_last, 0.0)
    d_mid_ref[...] = d_mid
    attn_sum = jnp.sum(attn_normed * d_mid, axis=0, keepdims=True)
    d_attn = row_rms_back(attn, attn_scale, vec_ref[1:2] * d_mid).astype(BF16)
    d_attn_ref[...] = d_attn
    for k in range(4):
        mixed_own_ref[k] = dot(out_near_ref[k], d_attn, (1, 1)).astype(BF16)
        mixed_other_ref[k] = dot(out_far_ref[k], d_attn, (1, 1)).astype(BF16)

    @pl.when(step == 0)
    def _():
        sums_ref[...] = jnp.zeros_like(sums_ref)

    sums_ref[0:1] += mid_sum
    sums_ref[1:2] += attn_sum


def backward(at, d_ffn, ffn, out_whole, gate_up, attn, patches, embed, cot_taps, unpatch, vec):
    width = embed.shape[1]
    part = out_whole[0].shape[1]
    hidden_width = ffn.shape[1] // 3
    by_chip = pl.BlockSpec((1, BLOCK, width), lambda t, at: ((t - at[0] + 4) % 4, 0, 0))
    parts = pl.BlockSpec((4, part, PAIR), lambda t, at: (0, 0, t))
    return pl.pallas_call(
        backward_kernel,
        grid_spec=pltpu.PrefetchScalarGridSpec(
            num_scalar_prefetch=1,
            grid=(4,),
            in_specs=[
                by_chip,
                by_chip,
                whole(ffn.shape),
                whole((4, part, width)),
                whole((4, part, width)),
                row_block(PAIR, 2 * hidden_width),
                row_block(PAIR, width),
                lane_block(144, PAIR),
                whole(embed.shape),
                lane_block(144, PAIR),
                whole(unpatch.shape),
                whole(vec.shape),
            ],
            out_specs=[
                row_block(PAIR, width),
                row_block(PAIR, 2 * hidden_width),
                row_block(PAIR, width),
                row_block(PAIR, width),
                parts,
                parts,
                pl.BlockSpec((8, width), lambda t, at: (0, 0)),
            ],
        ),
        out_shape=[
            jax.ShapeDtypeStruct((TOKENS, width), BF16),
            jax.ShapeDtypeStruct((TOKENS, 2 * hidden_width), BF16),
            jax.ShapeDtypeStruct((TOKENS, width), BF16),
            jax.ShapeDtypeStruct((TOKENS, width), F32),
            jax.ShapeDtypeStruct((4, part, TOKENS), BF16),
            jax.ShapeDtypeStruct((4, part, TOKENS), BF16),
            jax.ShapeDtypeStruct((8, width), F32),
        ],
        compiler_params=params(),
        cost_estimate=LIGHT,
        name="backward",
    )(at, *d_ffn, ffn, *out_whole, gate_up, attn, patches, embed, cot_taps, unpatch, vec)


def ffn_grad_kernel(second_ref, d_gate_up_ref, d_ffn_ref, hidden_ref, out_ref):
    split = d_gate_up_ref.shape[1]
    out_ref[:, :split] = dot(second_ref[...], d_gate_up_ref[...], (0, 0)).astype(BF16)
    out_ref[:, split:] = dot(d_ffn_ref[...], hidden_ref[...], (0, 0)).astype(BF16)


def ffn_grads(second, d_gate_up, d_ffn, hidden):
    width = second.shape[1]
    lanes = d_gate_up.shape[1] + hidden.shape[1]
    return pl.pallas_call(
        ffn_grad_kernel,
        grid=(4,),
        in_specs=[
            lane_block(TOKENS, width // 4),
            whole(d_gate_up.shape),
            lane_block(TOKENS, width // 4),
            whole(hidden.shape),
        ],
        out_specs=row_block(width // 4, lanes),
        out_shape=jax.ShapeDtypeStruct((width, lanes), BF16),
        compiler_params=params(),
        cost_estimate=LIGHT,
        name="ffn_grads",
    )(second, d_gate_up, d_ffn, hidden)


def out_grad_kernel(near_ref, far_ref, d_attn_ref, out_near_ref, out_far_ref):
    out_near_ref[0] = dot(near_ref[0], d_attn_ref[...], (1, 0)).astype(BF16)
    out_far_ref[0] = dot(far_ref[0], d_attn_ref[...], (1, 0)).astype(BF16)


def out_grads(mixed, d_attn):
    pieces, part, _ = mixed[0].shape
    width = d_attn.shape[1]
    piece = pl.BlockSpec((1, part, TOKENS), lambda t: (t, 0, 0))
    out_piece = pl.BlockSpec((1, part, width), lambda t: (t, 0, 0))
    return pl.pallas_call(
        out_grad_kernel,
        grid=(pieces,),
        in_specs=[piece, piece, whole(d_attn.shape)],
        out_specs=[out_piece] * 2,
        out_shape=[jax.ShapeDtypeStruct((pieces, part, width), BF16)] * 2,
        compiler_params=params(),
        cost_estimate=LIGHT,
        name="out_grads",
    )(*mixed, d_attn)


def first_kernel(
    at_ref, patch_ref, embed_ref, vec_ref, weight_ref, d_raw_ref, d_mid_ref, place_ref,
    caption_ref, d_text_ref, unpatch_sum_ref, back_sums_ref, own_sums_ref, head_rows_ref, coef_ref,
    activation_ref,
    p0_ref, p1_ref, p2_ref, p3_ref, pack_ref,
    qkv_acc, taps_acc, embed_acc, first_acc, shared_acc, turned_acc,
):
    step = pl.program_id(0)
    last = pl.num_programs(0) - 1
    parts = (p0_ref, p1_ref, p2_ref, p3_ref)
    places = [lax.rem(at_ref[3] + d, 4) for d in range(4)]
    part = weight_ref.shape[1] // COLS
    text_rows = caption_ref.shape[1] // COLS
    x = dot(patch_ref[...], embed_ref[...], (0, 0))
    scale = row_rms(x)
    x_normed = x * scale
    h = (x_normed * vec_ref[0:1]).astype(BF16)
    d_h = dot(d_raw_ref[0], weight_ref[0], (0, 1))
    for s in (1, 2):
        d_h = d_h + dot(d_raw_ref[s], weight_ref[s], (0, 1))

    @pl.when(step == 0)
    def _():
        qkv_acc[...] = jnp.zeros_like(qkv_acc)
        embed_acc[...] = jnp.zeros_like(embed_acc)
        first_acc[...] = jnp.zeros_like(first_acc)

    for s in range(3):
        qkv_acc[s] += dot(d_raw_ref[s], h, (1, 0))
    first_acc[0:1] += jnp.sum(x_normed * d_h, axis=0, keepdims=True)
    d_first = (d_mid_ref[...] + row_rms_back(x, scale, vec_ref[0:1] * d_h)).astype(BF16)
    embed_acc[...] += dot(patch_ref[...], d_first, (1, 0))
    ahead = lax.rem(step - at_ref[2] + 4, 4)
    for place, ref in zip(places, parts):
        first = pl.multiple_of((step * 4 + place) * text_rows, text_rows)
        ref[ahead, :text_rows] = dot(
            caption_ref[:, pl.ds(first, text_rows)], d_text_ref[...], (0, 1)
        ).astype(BF16)
    here = pl.ds(pl.multiple_of(step * PAIR, PAIR), PAIR)
    taps_acc[:, here] = dot(embed_ref[...], d_first, (1, 1))

    @pl.when(step == last)
    def _():
        for s in range(3):
            turned_acc[s] = qkv_acc[s].T.astype(BF16)
        middle = text_rows + part
        end = middle + part // 2
        for place, ref in zip(places, parts):
            for y in range(4):
                ahead_y = lax.rem(y - at_ref[2] + 4, 4)
                first = pl.multiple_of((y * 4 + place) * part, part)
                rows = [turned_acc[s, pl.ds(first, part), :] for s in range(3)]
                ref[ahead_y, text_rows:middle] = jnp.concatenate(rows[:2], 1)
                ref[ahead_y, middle:end] = jnp.concatenate(
                    [rows[2][: part // 2], rows[2][part // 2 :]], 1
                )
        terms = jnp.concatenate(
            [first_acc[0:1], back_sums_ref[1:2], back_sums_ref[0:1], own_sums_ref[0:1]], 0
        )
        d_gains = terms * coef_ref[0:4]
        d_modulation = terms * coef_ref[4:8]
        small = jnp.concatenate(
            [d_gains, head_rows_ref[0:4], jnp.zeros((24, d_gains.shape[1]), F32)], 0
        )
        for tile in range(12):
            lanes = slice(tile * 128, (tile + 1) * 128)
            first = tile * SHARED
            shared_acc[first : first + 144] = embed_acc[:, lanes].astype(BF16)
            shared_acc[first + 144 : first + 288] = unpatch_sum_ref[:, lanes].astype(BF16)
            shared_acc[first + 288 : first + SHARED] = small[:, lanes].astype(BF16)
        shared_acc[12 * SHARED :] = jnp.zeros((8 * CHUNK - 12 * SHARED, 128), BF16)
        latent = field_of(taps_acc[...], place_ref[...], -1)
        rows = [
            d_modulation[q : q + 1, tile * 128 : (tile + 1) * 128]
            for q in range(4)
            for tile in range(12)
        ]
        for r in range(ROWS):
            pack_ref[r, :CHUNK] = shared_acc[r * CHUNK : (r + 1) * CHUNK]
            pack_ref[r, CHUNK : CHUNK + 16] = activation_ref[r].astype(BF16)
            pack_ref[r, CHUNK + 16 : CHUNK + 32] = latent[r].astype(BF16)
            pack_ref[r, CHUNK + 32 : CHUNK + 48] = jnp.concatenate(
                rows[6 * r : 6 * r + 6] + [jnp.zeros((10, 128), F32)], 0
            ).astype(BF16)


def first_back(
    at, patches, embed, vec, weight, d_raw, d_mid, place, caption, d_text, unpatch_sum,
    back_sums, own_sums, head_rows, coef, activation,
):
    width = embed.shape[1]
    part = weight.shape[2]
    text_rows = caption.shape[1] // COLS
    grads = (4, text_rows + 3 * width // (2 * COLS), 2 * part)
    pack = (ROWS, CHUNK + 48, 128)
    rest = (place, caption, d_text, unpatch_sum, back_sums, own_sums, head_rows, coef, activation)
    return pl.pallas_call(
        first_kernel,
        grid_spec=pltpu.PrefetchScalarGridSpec(
            num_scalar_prefetch=1,
            grid=(TOKENS // PAIR,),
            in_specs=[
                lane_block(144, PAIR),
                whole(embed.shape),
                whole(vec.shape),
                whole(weight.shape),
                pl.BlockSpec((3, part, PAIR), lambda t, at: (0, 0, t)),
                row_block(PAIR, width),
            ]
            + [whole(value.shape) for value in rest],
            out_specs=[pl.BlockSpec(grads, lambda t, at: (0, 0, 0))] * 4
            + [pl.BlockSpec(pack, lambda t, at: (0, 0, 0))],
            scratch_shapes=[
                pltpu.VMEM((3, part, width), F32),
                pltpu.VMEM((144, TOKENS), F32),
                pltpu.VMEM((144, width), F32),
                pltpu.VMEM((8, width), F32),
                pltpu.VMEM((8 * CHUNK, 128), BF16),
                pltpu.VMEM((3, width, part), BF16),
            ],
        ),
        out_shape=[jax.ShapeDtypeStruct(grads, BF16)] * 4 + [jax.ShapeDtypeStruct(pack, BF16)],
        compiler_params=params(),
        cost_estimate=LIGHT,
        name="first_back",
    )(at, patches, embed, vec, weight, d_raw, d_mid, *rest)


def field_kernel(taps_ref, place_ref, field_ref):
    for r, tile in enumerate(field_of(taps_ref[...], place_ref[...], 1)):
        field_ref[r] = tile


def local(
    latent, condition, caption, cap_len, cotangent, embed_weight, modulate_weight, norm_gains,
    cross_gate, qkv_weight, text_kv_weight, out_weight, gate_up_weight, down_weight, unpatch_weight,
):
    images, _, _, channels = latent.shape
    width = embed_weight.shape[3]
    local_width = qkv_weight.shape[2]
    heads = local_width // HD
    hidden_width = down_weight.shape[0]
    taps = 9 * channels
    row_at = lax.axis_index("row")
    col_at = lax.axis_index("col")
    at = jnp.stack([row_at // 2, row_at % 2, col_at // 4, col_at % 4]).astype(jnp.int32)
    tile = latent.shape[1] * latent.shape[2] * channels

    cond_low = jax.nn.silu(condition.astype(F32)).astype(BF16)
    mod_piece = jnp.dot(cond_low, modulate_weight, preferred_element_type=F32)
    mod_columns = mod_piece.shape[1]
    mod_high = mod_piece.astype(BF16)
    mod_low = (mod_piece - mod_high.astype(F32)).astype(BF16)

    packed = jnp.concatenate(
        [latent.reshape(images, tile), cotangent.reshape(images, tile), mod_high, mod_low], axis=1
    )
    packed = jnp.pad(packed, ((0, 0), (0, 2 * local_width - packed.shape[1])))

    head_piece = jnp.concatenate(
        [
            jnp.concatenate([qkv_weight[0], qkv_weight[1]], axis=1),
            jnp.concatenate([qkv_weight[2], out_weight.T], axis=1),
        ]
    )
    piece_rows = head_piece.shape[0]
    head_pieces = jnp.concatenate(
        [
            jnp.broadcast_to(head_piece, (COLS,) + head_piece.shape),
            jnp.pad(packed[:, None], ((0, 0), (0, 15), (0, 0))),
        ],
        axis=1,
    )
    head_pieces = lax.all_to_all(head_pieces, "col", 0, 0)
    packed = send_all(head_pieces[:, piece_rows], "row")

    text_piece = jnp.concatenate([text_kv_weight[0], text_kv_weight[1]], axis=1)
    text_whole = lax.all_gather(text_piece, "col", axis=0, tiled=True)
    ffn_piece = jnp.concatenate([gate_up_weight[0], gate_up_weight[1], down_weight.T], axis=1)

    patches, cot_taps = image_taps(packed)
    ffn_whole = lax.all_gather(after(ffn_piece, text_whole, patches), "col", axis=0, tiled=True)
    mod_at = 2 * tile
    modulation = packed[:, :, mod_at : mod_at + mod_columns].astype(F32)
    modulation = modulation + packed[:, :, mod_at + mod_columns : mod_at + 2 * mod_columns].astype(F32)
    modulation = modulation.reshape(4, width)
    attn_gate = jnp.tanh(modulation[1])
    ffn_gate = jnp.tanh(modulation[3])
    vec = jnp.stack(
        [
            norm_gains[0] * (1.0 + modulation[0]),
            norm_gains[1] * attn_gate,
            norm_gains[2] * (1.0 + modulation[2]),
            norm_gains[3] * ffn_gate,
        ]
    )
    vec = jnp.pad(vec, ((0, 4), (0, 0)))
    embed = embed_weight.reshape(taps, width)
    unpatch = unpatch_weight.transpose(0, 1, 3, 2).reshape(taps, width)
    raw, qkv_whole, out_rows = qkv_project(patches, embed, vec, head_pieces)
    out_whole = gather_near(out_rows)
    raw = raw.reshape(3, heads, HD, TOKENS)
    caption_rows = caption[0]
    text_raw = dot(text_whole, caption_rows, (0, 1)).reshape(2, heads, HD, caption_rows.shape[0])
    head_gains = lax.dynamic_slice(norm_gains, (4, row_at * local_width), (3, local_width)).reshape(
        3, heads, HD, 1
    )
    head_gates = jnp.tanh(lax.dynamic_slice_in_dim(cross_gate, row_at * heads, heads))
    cap = lax.dynamic_slice_in_dim(cap_len, col_at, 1)
    table = jnp.asarray(rope_tables())
    mixed, lse = attend(raw, text_raw, head_gains, table, cap, head_gates)

    mixed_whole = gather_near(mixed)
    attn, second, gate_up, hidden, ffn_own, ffn_other = forward(
        at, mixed_whole, out_whole, patches, embed, vec, ffn_whole
    )
    d_ffn_own, last_taps, unpatch_sum, own_sums = own_block(
        at, to_chips(sum_cores(ffn_own, ffn_other)), attn, patches, cot_taps, embed, unpatch, vec
    )
    d_ffn, d_gate_up, d_attn, d_mid, mixed_own, mixed_other, back_sums = backward(
        at, gather_near(d_ffn_own), ffn_whole, out_whole, gate_up, attn, patches, embed, cot_taps,
        unpatch, vec,
    )
    mixed_near = sum_cores(mixed_own, mixed_other)
    mixed_terms = to_chips(mixed_near)
    ffn_sum = ffn_grads(after(second, *mixed_near), d_gate_up, d_ffn, hidden)
    *mixed_terms, ffn_sum = lax.optimization_barrier((*mixed_terms, ffn_sum))
    d_mixed = sum(term.astype(F32) for term in mixed_terms).astype(BF16)

    d_raw, d_text, d_head = attend_back(
        raw, text_raw, head_gains, table, lse, d_mixed.reshape(heads, HD, TOKENS), cap, head_gates
    )
    place = tile_places(False)
    activation_field = pl.pallas_call(
        field_kernel,
        out_shape=jax.ShapeDtypeStruct((ROWS, channels, BLOCK), F32),
        compiler_params=pltpu.CompilerParams(vmem_limit_bytes=VMEM),
        cost_estimate=LIGHT,
        name="activation_field",
    )(
        lax.dynamic_update_slice(jnp.zeros((taps, TOKENS), F32), last_taps, (0, row_at * BLOCK)),
        place,
    )
    one = jnp.ones_like(attn_gate)
    coef = jnp.stack(
        [
            one + modulation[0],
            attn_gate,
            one + modulation[2],
            ffn_gate,
            norm_gains[0],
            norm_gains[1] * (1.0 - attn_gate * attn_gate),
            norm_gains[2],
            norm_gains[3] * (1.0 - ffn_gate * ffn_gate),
        ]
    )
    head_sums = lax.dynamic_update_slice(
        jnp.zeros((8, width), F32), d_head[:3].reshape(3, local_width), (0, row_at * local_width)
    )
    gate_part = jnp.sum(d_head[3], axis=(1, 2)) * (1.0 - head_gates * head_gates)
    head_sums = lax.dynamic_update_slice(head_sums, gate_part[None], (3, row_at * heads))
    *grads, row_pack = first_back(
        at, patches, embed, vec, qkv_whole, d_raw.reshape(3, local_width, TOKENS), d_mid, place,
        caption_rows, d_text.reshape(2 * local_width, -1), unpatch_sum, back_sums, own_sums,
        head_sums, coef, activation_field,
    )
    d_attn = after(d_attn, row_pack)
    grads = scatter_col(grads)

    row_pack = jnp.sum(lax.all_to_all(row_pack, "row", 0, 0).astype(F32), axis=0)
    fields = row_pack[CHUNK : CHUNK + 2 * channels].T.reshape(COLS, 8, 2 * channels)
    mod_sums = row_pack[CHUNK + 2 * channels : CHUNK + 2 * channels + 6].reshape(COLS, 8, 6)
    fields = jnp.concatenate([fields, mod_sums], axis=2).astype(BF16)
    fields = jnp.pad(fields, ((0, 0), (0, 0), (0, 128 - fields.shape[2])))
    shared = row_pack[:CHUNK].astype(BF16).reshape(COLS, CHUNK // COLS, 128)
    col_pack = lax.all_to_all(jnp.concatenate([shared, fields], axis=1), "col", 0, 0)
    shared = jnp.sum(col_pack[:, : CHUNK // COLS].astype(F32), axis=0)
    shared = send_all(send_all(shared.astype(BF16), "col"), "row").reshape(-1, 128)
    shared = shared[: 12 * SHARED].reshape(12, SHARED, 128).astype(F32)
    fields = col_pack[:, CHUNK // COLS :]
    activation = fields[:, :, :channels].reshape(latent.shape)
    latent_grad = fields[:, :, channels : 2 * channels].reshape(latent.shape)
    modulate_grad = lax.dot_general(
        cond_low.astype(F32),
        fields[:, :, 2 * channels : 2 * channels + 6].reshape(images, mod_columns).astype(F32),
        (((0,), (0,)), ((), ())),
        precision=lax.Precision.HIGHEST,
        preferred_element_type=F32,
    )
    embed_grad = shared[:, :taps].transpose(1, 0, 2).reshape(embed_weight.shape)
    unpatch_grad = shared[:, taps : 2 * taps].reshape(12, 3, 3, channels, 128)
    unpatch_grad = unpatch_grad.transpose(1, 2, 0, 4, 3).reshape(unpatch_weight.shape)
    gains_grad = shared[:, 2 * taps : 2 * taps + 7].transpose(1, 0, 2).reshape(7, width)
    gate_grad = shared[0, 2 * taps + 7, :HEADS]

    ffn_total = lax.psum_scatter(ffn_sum, "col", scatter_dimension=0, tiled=True).astype(F32)
    gate_up_grad = jnp.stack(
        [ffn_total[:, :hidden_width], ffn_total[:, hidden_width : 2 * hidden_width]]
    )
    down_grad = ffn_total[:, 2 * hidden_width :].T
    text_rows = text_kv_weight.shape[1]
    part = width // COLS
    first, second_half = grads[:, :local_width], grads[:, local_width:]
    text_kv_grad = jnp.stack([first[:text_rows], second_half[:text_rows]])
    head_at = text_rows + part
    half = head_at + part // 2
    values = jnp.concatenate([first[head_at:half], second_half[head_at:half]])
    qkv_grad = jnp.stack([first[text_rows:head_at], second_half[text_rows:head_at], values])
    out_sum = sum(term.astype(F32) for term in to_chips(sum_cores(*out_grads(mixed_whole, d_attn))))
    out_sum = out_sum.astype(BF16).reshape(local_width, COLS, part).transpose(1, 0, 2)
    out_grad = jnp.sum(lax.all_to_all(out_sum, "col", 0, 0).astype(F32), axis=0)
    return (
        activation, latent_grad, embed_grad, modulate_grad, gains_grad, gate_grad,
        qkv_grad, text_kv_grad, out_grad, gate_up_grad, down_grad, unpatch_grad,
    )


def solution(mesh):
    placed = (
        P(None, "row", "col", None),
        P(),
        P("col", None, None),
        P(),
        P(None, "row", "col", None),
        P(),
        P(None, ("row", "col")),
        P(),
        P(),
        P(None, "col", "row"),
        P(None, "col", "row"),
        P("row", "col"),
        P(None, "col", "row"),
        P("row", "col"),
        P(),
    )
    return jax.shard_map(
        local,
        mesh=mesh,
        in_specs=placed,
        out_specs=(
            P(None, "row", "col", None),
            P(None, "row", "col", None),
            P(),
            P(None, ("row", "col")),
            P(),
            P(),
            P(None, "col", "row"),
            P(None, "col", "row"),
            P("row", "col"),
            P(None, "col", "row"),
            P("row", "col"),
            P(),
        ),
        check_vma=False,
    )
```

```python
import math
from functools import partial

import jax
import jax.numpy as jnp
import numpy as np
from jax import lax
from jax.experimental import pallas as pl
from jax.experimental.pallas import tpu as pltpu
from jax.sharding import PartitionSpec as P

HEADS = 24
HD = 64
GRID = 32
TOKENS = GRID * GRID
EPSILON = 1e-06
ROPE_BASE = 10000.0
MASKED = -1e30
F32 = jnp.float32
BF16 = jnp.bfloat16
ROWS = 8
COLS = 16
QUERY_BLOCK = 256
BLOCK = TOKENS // ROWS
PAIR = 2 * BLOCK
VMEM = 56 * 2**20
SHARED = 320
CHUNK = 512
LIGHT = pl.CostEstimate(flops=1, bytes_accessed=1, transcendentals=0)


def dot(left, right, contract):
    return lax.dot_general(
        left, right, ((contract[:1], contract[1:]), ((), ())), preferred_element_type=F32
    )


def row_pairs(dx, dc):
    return [
        (((x + dx) % 4) * 2 + (c + dc) % 2, x * 2 + c) for x in range(4) for c in range(2)
    ]


def row_pairs_to(dx, dc):
    return [(dst, src) for src, dst in row_pairs(dx, dc)]


def from_chips(piece):
    return [piece] + [lax.ppermute(piece, "row", row_pairs(d, 0)) for d in (1, 2, 3)]


def with_other_core(pieces):
    quad = jnp.stack(pieces)
    return quad, lax.ppermute(quad, "row", row_pairs(0, 1))


def gather_near(piece):
    return with_other_core(from_chips(piece))


def sum_cores(own, other):
    other = lax.ppermute(other, "row", row_pairs(0, 1))
    return [(own[d].astype(F32) + other[d].astype(F32)).astype(BF16) for d in range(4)]


def to_chips(near):
    return [near[0]] + [lax.ppermute(near[d], "row", row_pairs_to(d, 0)) for d in (1, 2, 3)]


def col_pairs_to(dy, dz):
    return [(y * 4 + z, (y + dy) % 4 * 4 + (z + dz) % 4) for y in range(4) for z in range(4)]


def scatter_col(parts):
    near = parts[0].astype(F32)
    for d in (1, 2, 3):
        near = near + lax.ppermute(parts[d], "col", col_pairs_to(0, d)).astype(F32)
    near = near.astype(BF16)
    total = near[0].astype(F32)
    for d in (1, 2, 3):
        total = total + lax.ppermute(near[d], "col", col_pairs_to(d, 0)).astype(F32)
    return total


def send_all(piece, axis):
    copies = jnp.broadcast_to(piece, (lax.axis_size(axis),) + piece.shape)
    return lax.all_to_all(copies, axis, 0, 0)


def after(value, *others):
    return lax.optimization_barrier((value,) + others)[0]


def rope_tables():
    quarter = HD // 4
    frequency = np.float32(ROPE_BASE) ** (-np.arange(quarter, dtype=np.float32) / np.float32(quarter))
    place = np.arange(TOKENS)
    row = frequency[:, None] * (place // GRID).astype(np.float32)[None, :]
    col = frequency[:, None] * (place % GRID).astype(np.float32)[None, :]
    return np.stack([np.cos(row), np.sin(row), np.cos(col), np.sin(col)]).astype(np.float32)


def turn(v, table, sign):
    a, b, c, d = (v[k * 16 : (k + 1) * 16] for k in range(4))
    cr, sr, cc, sc = table[0], table[1] * sign, table[2], table[3] * sign
    return jnp.concatenate([a * cr - b * sr, a * sr + b * cr, c * cc - d * sc, c * sc + d * cc], 0)


def column_rms(v):
    return lax.rsqrt(jnp.mean(v * v, axis=0, keepdims=True) + EPSILON)


def normed(v, gain):
    return v * column_rms(v) * gain


def column_rms_back(v, u):
    scale = column_rms(v)
    return (u - v * (jnp.mean(u * v, axis=0, keepdims=True) * scale * scale)) * scale


def whole(shape):
    zeros = (0,) * len(shape)
    return pl.BlockSpec(shape, lambda *_: zeros, pipeline_mode=pl.Buffered(1))


def lane_block(rows, lanes):
    return pl.BlockSpec((rows, lanes), lambda t, *_: (0, t))


def row_block(rows, lanes):
    return pl.BlockSpec((rows, lanes), lambda t, *_: (t, 0))


def params():
    return pltpu.CompilerParams(vmem_limit_bytes=VMEM, dimension_semantics=("arbitrary",))


def attend_kernel(
    cap_ref, gate_ref, raw_ref, text_ref, gain_ref, table_ref, mixed_ref, lse_ref,
    q_ref, k_ref, v_ref, tk_ref, tv_ref,
):
    step = pl.program_id(0)
    heads = raw_ref.shape[1]

    @pl.when(step == 0)
    def _():
        table = table_ref[...]
        for h in range(heads):
            q = turn(normed(raw_ref[0, h], gain_ref[0, h]), table, 1.0).astype(BF16)
            q_ref[h] = q * jnp.asarray(0.125, BF16)
            k_ref[h] = turn(normed(raw_ref[1, h], gain_ref[1, h]), table, 1.0).astype(BF16)
            v_ref[h] = raw_ref[2, h].astype(BF16)
            tk_ref[h] = normed(text_ref[0, h], gain_ref[2, h]).astype(BF16)
            tv_ref[h] = text_ref[1, h].astype(BF16)

    slots = tk_ref.shape[2]
    mask = lax.broadcasted_iota(jnp.int32, (slots, QUERY_BLOCK), 0) < cap_ref[0]
    here = pl.ds(pl.multiple_of(step * QUERY_BLOCK, QUERY_BLOCK), QUERY_BLOCK)
    outs = []
    for h in range(heads):
        qb = q_ref[h, :, here]
        e = jnp.exp(dot(k_ref[h], qb, (0, 0)))
        total = jnp.sum(e, axis=0, keepdims=True)
        own = dot(v_ref[h], e.astype(BF16), (1, 0)) / total
        te = jnp.exp(jnp.where(mask, dot(tk_ref[h], qb, (0, 0)), MASKED))
        text_total = jnp.sum(te, axis=0, keepdims=True)
        text = dot(tv_ref[h], te.astype(BF16), (1, 0)) / text_total
        outs.append(own + gate_ref[h] * text)
        lse_ref[h, 0:1] = jnp.log(total)
        lse_ref[h, 1:2] = jnp.log(text_total)
    mixed_ref[...] = jnp.concatenate(outs, 0).astype(BF16)


def attend(raw, text_raw, gains, table, cap, gates):
    heads = raw.shape[1]
    slots = text_raw.shape[3]
    return pl.pallas_call(
        attend_kernel,
        grid_spec=pltpu.PrefetchScalarGridSpec(
            num_scalar_prefetch=2,
            grid=(TOKENS // QUERY_BLOCK,),
            in_specs=[
                whole((3, heads, HD, TOKENS)),
                whole((2, heads, HD, slots)),
                whole((3, heads, HD, 1)),
                whole((4, 16, TOKENS)),
            ],
            out_specs=[
                lane_block(heads * HD, QUERY_BLOCK),
                pl.BlockSpec((heads, 8, QUERY_BLOCK), lambda t, *_: (0, 0, t)),
            ],
            scratch_shapes=[
                pltpu.VMEM((heads, HD, TOKENS), BF16),
                pltpu.VMEM((heads, HD, TOKENS), BF16),
                pltpu.VMEM((heads, HD, TOKENS), BF16),
                pltpu.VMEM((heads, HD, slots), BF16),
                pltpu.VMEM((heads, HD, slots), BF16),
            ],
        ),
        out_shape=[
            jax.ShapeDtypeStruct((heads * HD, TOKENS), BF16),
            jax.ShapeDtypeStruct((heads, 8, TOKENS), F32),
        ],
        compiler_params=params(),
        cost_estimate=LIGHT,
        name="attend",
    )(cap, gates, raw, text_raw, gains, table)


def text_back_kernel(
    cap_ref, gate_ref, q_raw_ref, text_ref, gain_ref, table_ref, lse_ref, grad_ref, caption_ref, held_ref,
    grads_ref, dq_ref, d_gain_ref, low_ref,
):
    del held_ref
    step = pl.program_id(0)
    heads, _, slots = low_ref.shape[1:]

    @pl.when(step == 0)
    def _():
        table = table_ref[...]
        mask = lax.broadcasted_iota(jnp.int32, (slots, TOKENS), 0) < cap_ref[0]
        for h in range(heads):
            gate = gate_ref[h]
            q = turn(normed(q_raw_ref[h], gain_ref[0, h]), table, 1.0).astype(BF16)
            q = q * jnp.asarray(0.125, BF16)
            tk = normed(text_ref[0, h], gain_ref[2, h]).astype(BF16)
            tv = text_ref[1, h].astype(BF16)
            g = grad_ref[h]
            tp = jnp.exp(jnp.where(mask, dot(tk, q, (0, 0)), MASKED) - lse_ref[h, 1:2])
            tpb = tp.astype(BF16)
            low_ref[1, h] = (dot(g, tpb, (1, 1)) * gate).astype(BF16)
            gate_terms = g.astype(F32) * dot(tv, tpb, (1, 0))
            tpd = tp * dot(tv, g, (0, 0)) * gate
            dts = (tpd - tp * jnp.sum(tpd, axis=0, keepdims=True)).astype(BF16)
            dq_ref[h] = dot(tk, dts, (1, 0))
            d_tk = dot(q, dts, (1, 1))
            values = text_ref[0, h]
            low_ref[0, h] = column_rms_back(values, d_tk * gain_ref[2, h]).astype(BF16)
            d_gain_ref[0, h] = jnp.sum(values * column_rms(values) * d_tk, axis=1, keepdims=True)
            d_gain_ref[1, h] = jnp.sum(gate_terms, axis=1, keepdims=True)

    d_text = low_ref[...].reshape(2 * heads * HD, slots)
    rows = grads_ref.shape[1]
    for k in range(grads_ref.shape[0]):
        grads_ref[k] = dot(caption_ref[:, k * rows : (k + 1) * rows], d_text, (0, 1)).astype(BF16)


def text_back(raw, text_raw, gains, table, lse, grads, cap, gates, caption, held):
    heads = raw.shape[1]
    slots = text_raw.shape[3]
    rows = caption.shape[1] // COLS
    lanes = 2 * heads * HD
    return pl.pallas_call(
        text_back_kernel,
        grid_spec=pltpu.PrefetchScalarGridSpec(
            num_scalar_prefetch=2,
            grid=(4,),
            in_specs=[
                pl.BlockSpec((None, heads, HD, TOKENS), lambda t, *_: (0, 0, 0, 0)),
                whole(text_raw.shape),
                whole(gains.shape),
                whole(table.shape),
                whole(lse.shape),
                whole(grads.shape),
                pl.BlockSpec((slots, 4 * rows), lambda t, *_: (0, t)),
                pl.BlockSpec(memory_space=pl.ANY),
            ],
            out_specs=[
                pl.BlockSpec((4, rows, lanes), lambda t, *_: (t, 0, 0)),
                pl.BlockSpec((heads, HD, TOKENS), lambda t, *_: (0, 0, 0)),
                pl.BlockSpec((2, heads, HD, 1), lambda t, *_: (0, 0, 0, 0)),
            ],
            scratch_shapes=[pltpu.VMEM((2, heads, HD, slots), BF16)],
        ),
        out_shape=[
            jax.ShapeDtypeStruct(held.shape, BF16),
            jax.ShapeDtypeStruct((heads, HD, TOKENS), F32),
            jax.ShapeDtypeStruct((2, heads, HD, 1), F32),
        ],
        input_output_aliases={9: 0},
        compiler_params=params(),
        cost_estimate=LIGHT,
        name="text_back",
    )(cap, gates, raw, text_raw, gains, table, lse, grads, caption, held)


def attend_back_kernel(
    raw_ref, gain_ref, table_ref, lse_ref, grad_ref, dq_text_ref,
    d_raw_ref, d_gain_ref, dv_ref, dk_ref, dq_ref,
):
    table = table_ref[...]
    q = turn(normed(raw_ref[0], gain_ref[0]), table, 1.0).astype(BF16) * jnp.asarray(0.125, BF16)
    k = turn(normed(raw_ref[1], gain_ref[1]), table, 1.0).astype(BF16)
    v = raw_ref[2].astype(BF16)
    for first in range(0, TOKENS, QUERY_BLOCK):
        here = slice(first, first + QUERY_BLOCK)
        qb = q[:, here]
        gb = grad_ref[:, here]
        p = jnp.exp(dot(k, qb, (0, 0)) - lse_ref[0:1, here])
        dv = dot(gb, p.astype(BF16), (1, 1))
        pd = p * dot(v, gb, (0, 0))
        ds = (pd - p * jnp.sum(pd, axis=0, keepdims=True)).astype(BF16)
        dq_ref[:, here] = dot(k, ds, (1, 0)) + dq_text_ref[:, here]
        dk = dot(qb, ds, (1, 1))
        if first == 0:
            dv_ref[...] = dv
            dk_ref[...] = dk
        else:
            dv_ref[...] += dv
            dk_ref[...] += dk

    def raw_back(which, d_turned):
        spun = turn(d_turned.astype(BF16).astype(F32), table, -1.0)
        values = raw_ref[which]
        d_raw_ref[which] = column_rms_back(values, spun * gain_ref[which]).astype(BF16)
        d_gain_ref[which] = jnp.sum(values * column_rms(values) * spun, axis=1, keepdims=True)

    raw_back(0, dq_ref[...] * 0.125)
    raw_back(1, dk_ref[...])
    d_raw_ref[2] = dv_ref[...].astype(BF16)


def attend_back(raw, gains, table, lse, grads, dq_text):
    heads = raw.shape[1]
    return pl.pallas_call(
        attend_back_kernel,
        grid=(heads,),
        in_specs=[
            pl.BlockSpec((3, None, HD, TOKENS), lambda h: (0, h, 0, 0)),
            pl.BlockSpec((3, None, HD, 1), lambda h: (0, h, 0, 0)),
            pl.BlockSpec((4, 16, TOKENS), lambda h: (0, 0, 0)),
            pl.BlockSpec((None, 8, TOKENS), lambda h: (h, 0, 0)),
            pl.BlockSpec((None, HD, TOKENS), lambda h: (h, 0, 0)),
            pl.BlockSpec((None, HD, TOKENS), lambda h: (h, 0, 0)),
        ],
        out_specs=[
            pl.BlockSpec((3, None, HD, TOKENS), lambda h: (0, h, 0, 0)),
            pl.BlockSpec((2, None, HD, 1), lambda h: (0, h, 0, 0)),
        ],
        scratch_shapes=[pltpu.VMEM((HD, TOKENS), F32) for _ in range(3)],
        out_shape=[
            jax.ShapeDtypeStruct((3, heads, HD, TOKENS), BF16),
            jax.ShapeDtypeStruct((2, heads, HD, 1), F32),
        ],
        compiler_params=params(),
        cost_estimate=LIGHT,
        name="attend_back",
    )(raw, gains, table, lse, grads, dq_text)


def tile_places(chunk_first):
    r, c, k = np.meshgrid(np.arange(ROWS), np.arange(COLS), np.arange(8), indexing="ij")
    token = r * BLOCK + (k // 2) * GRID + c * 2 + k % 2
    source = (k * ROWS + r) * COLS + c if chunk_first else (r * COLS + c) * 8 + k
    places = np.zeros((TOKENS, TOKENS), np.float32)
    places[source.ravel(), token.ravel()] = 1.0
    return jnp.asarray(places, BF16)


def grid_shift(field, di, dj):
    step = di * GRID + dj
    moved = pltpu.roll(field, (-step) % TOKENS, 1) if step else field
    place = lax.broadcasted_iota(jnp.int32, field.shape, 1)
    row = place // GRID + di
    col = place % GRID + dj
    inside = (row >= 0) & (row < GRID) & (col >= 0) & (col < GRID)
    return jnp.where(inside, moved, 0.0)


def image_kernel(packed_ref, place_ref, patch_ref, cot_ref):
    for which, sign, out_ref in ((0, 1, patch_ref), (1, -1, cot_ref)):
        lanes = slice(which * 128, (which + 1) * 128)
        tiles = jnp.concatenate([packed_ref[r, :, lanes] for r in range(ROWS)], 0)
        turned = tiles.astype(F32).T
        chunks = jnp.concatenate([turned[k * 16 : (k + 1) * 16] for k in range(8)], 1)
        image = dot(chunks.astype(BF16), place_ref[...], (1, 0))
        for a in range(3):
            for b in range(3):
                first = (a * 3 + b) * 16
                out_ref[first : first + 16] = grid_shift(
                    image, sign * (a - 1), sign * (b - 1)
                ).astype(BF16)


def image_taps(packed):
    out = jax.ShapeDtypeStruct((144, TOKENS), BF16)
    return pl.pallas_call(
        image_kernel,
        out_shape=[out, out],
        compiler_params=pltpu.CompilerParams(vmem_limit_bytes=VMEM),
        cost_estimate=LIGHT,
        name="image_taps",
    )(packed, tile_places(True))


def field_of(taps, place, sign):
    total = jnp.zeros((16, TOKENS), F32)
    for a in range(3):
        for b in range(3):
            first = (a * 3 + b) * 16
            total = total + grid_shift(taps[first : first + 16], sign * (a - 1), sign * (b - 1))
    tiles = dot(total.astype(BF16), place, (1, 1))
    return [tiles[:, r * BLOCK : (r + 1) * BLOCK] for r in range(ROWS)]


def row_rms(v):
    return lax.rsqrt(jnp.mean(v * v, axis=-1, keepdims=True) + EPSILON)


def row_rms_back(v, scale, u):
    return (u - v * (jnp.mean(u * v, axis=-1, keepdims=True) * scale * scale)) * scale


def out_rows_kernel(weight_ref, out_ref, turn_ref):
    part = turn_ref.shape[0] // COLS
    local_width = turn_ref.shape[1]
    for c in range(COLS):
        turn_ref[c * part : (c + 1) * part] = weight_ref[c, part : 2 * part, local_width:]
    out_ref[...] = turn_ref[...].T


def out_weight_rows(weight, width):
    part = weight.shape[2] // 2
    return pl.pallas_call(
        out_rows_kernel,
        out_shape=jax.ShapeDtypeStruct((part, width), BF16),
        scratch_shapes=[pltpu.VMEM((width, part), BF16)],
        compiler_params=pltpu.CompilerParams(vmem_limit_bytes=VMEM),
        cost_estimate=LIGHT,
        name="out_weight_rows",
    )(weight)


def qkv_kernel(patch_ref, embed_ref, vec_ref, weight_ref, raw_ref, joined_ref):
    width = embed_ref.shape[1]
    local_width = joined_ref.shape[2]
    part = width // COLS

    @pl.when(pl.program_id(0) == 0)
    def _():
        for c in range(COLS):
            here = slice(c * part, (c + 1) * part)
            for s in range(3):
                first = s // 2 * part
                lanes = slice(s % 2 * local_width, (s % 2 + 1) * local_width)
                joined_ref[s, here] = weight_ref[c, first : first + part, lanes]

    x = dot(patch_ref[...], embed_ref[...], (0, 0))
    h = (x * row_rms(x) * vec_ref[0:1]).astype(BF16)
    for s in range(3):
        raw_ref[s] = dot(h, joined_ref[s], (1, 0)).T


def qkv_project(patches, embed, vec, weight):
    width = embed.shape[1]
    part = weight.shape[2] // 2
    return pl.pallas_call(
        qkv_kernel,
        grid=(TOKENS // PAIR,),
        in_specs=[
            lane_block(144, PAIR),
            whole(embed.shape),
            whole(vec.shape),
            whole(weight.shape),
        ],
        out_specs=[
            pl.BlockSpec((3, part, PAIR), lambda t: (0, 0, t)),
            pl.BlockSpec((3, width, part), lambda t: (0, 0, 0)),
        ],
        out_shape=[
            jax.ShapeDtypeStruct((3, part, TOKENS), F32),
            jax.ShapeDtypeStruct((3, width, part), BF16),
        ],
        compiler_params=params(),
        cost_estimate=LIGHT,
        name="qkv_project",
    )(patches, embed, vec, weight)


def halves(core, first, second):
    return jnp.where(core == 0, first, second)


def forward_kernel(
    at_ref, near_ref, far_ref, out_near_ref, out_far_ref, patch_ref, embed_ref, vec_ref, ffn_ref,
    attn_ref, second_ref, gate_up_ref, hidden_ref, own_ref, other_ref,
):
    core = at_ref[1]
    hidden_width = hidden_ref.shape[1]
    x = dot(patch_ref[...], embed_ref[...], (0, 0))
    attn = dot(near_ref[0], out_near_ref[0], (0, 0))
    for k in range(1, 4):
        attn = attn + dot(near_ref[k], out_near_ref[k], (0, 0))
    for k in range(4):
        attn = attn + dot(far_ref[k], out_far_ref[k], (0, 0))
    attn_ref[...] = attn
    mid = x + vec_ref[1:2] * (attn * row_rms(attn))
    second = (mid * row_rms(mid) * vec_ref[2:3]).astype(BF16)
    second_ref[...] = second
    gate_up = dot(second, ffn_ref[:, : 2 * hidden_width], (1, 0))
    gate_up_ref[...] = gate_up
    gate = gate_up[:, :hidden_width]
    hidden = (gate * jax.nn.sigmoid(gate) * gate_up[:, hidden_width:]).astype(BF16)
    hidden_ref[...] = hidden
    part = dot(hidden, ffn_ref[:, 2 * hidden_width :], (1, 1)).astype(BF16)
    own_ref[0] = halves(core, part[:BLOCK], part[BLOCK:])
    other_ref[0] = halves(core, part[BLOCK:], part[:BLOCK])


def forward(at, mixed, out_whole, patches, embed, vec, ffn):
    width = embed.shape[1]
    part = mixed[0].shape[1]
    hidden_width = ffn.shape[1] // 3
    by_chip = pl.BlockSpec((1, BLOCK, width), lambda t, at: ((t - at[0] + 4) % 4, 0, 0))
    return pl.pallas_call(
        forward_kernel,
        grid_spec=pltpu.PrefetchScalarGridSpec(
            num_scalar_prefetch=1,
            grid=(4,),
            in_specs=[
                pl.BlockSpec((4, part, PAIR), lambda t, at: (0, 0, t)),
                pl.BlockSpec((4, part, PAIR), lambda t, at: (0, 0, t)),
                whole((4, part, width)),
                whole((4, part, width)),
                lane_block(144, PAIR),
                whole(embed.shape),
                whole(vec.shape),
                whole(ffn.shape),
            ],
            out_specs=[
                row_block(PAIR, width),
                row_block(PAIR, width),
                row_block(PAIR, 2 * hidden_width),
                row_block(PAIR, hidden_width),
                by_chip,
                by_chip,
            ],
        ),
        out_shape=[
            jax.ShapeDtypeStruct((TOKENS, width), F32),
            jax.ShapeDtypeStruct((TOKENS, width), BF16),
            jax.ShapeDtypeStruct((TOKENS, 2 * hidden_width), F32),
            jax.ShapeDtypeStruct((TOKENS, hidden_width), BF16),
            jax.ShapeDtypeStruct((4, BLOCK, width), BF16),
            jax.ShapeDtypeStruct((4, BLOCK, width), BF16),
        ],
        compiler_params=params(),
        cost_estimate=LIGHT,
        name="forward",
    )(at, *mixed, *out_whole, patches, embed, vec, ffn)


def own_kernel(
    at_ref, p0_ref, p1_ref, p2_ref, p3_ref, attn_ref, patch_ref, cot_ref, embed_ref, unpatch_ref,
    vec_ref, d_ffn_ref, taps_ref, unpatch_sum_ref, sums_ref,
):
    ffn = sum(p[...].astype(F32) for p in (p0_ref, p1_ref, p2_ref, p3_ref))
    d_last = dot(cot_ref[...], unpatch_ref[...], (0, 0))
    scale = row_rms(ffn)
    gated = vec_ref[3:4]
    d_ffn_ref[...] = row_rms_back(ffn, scale, gated * d_last).astype(BF16)
    normed_ffn = ffn * scale
    sums_ref[...] = jnp.broadcast_to(
        jnp.sum(normed_ffn * d_last, axis=0, keepdims=True), sums_ref.shape
    )
    attn = attn_ref[...]
    x = dot(patch_ref[...], embed_ref[...], (0, 0))
    last = (x + vec_ref[1:2] * (attn * row_rms(attn)) + gated * normed_ffn).astype(BF16)
    taps_ref[...] = dot(unpatch_ref[...], last, (1, 1))
    unpatch_sum_ref[...] = dot(cot_ref[...], last, (1, 0))


def own_block(at, pieces, attn, patches, cot_taps, embed, unpatch, vec):
    width = embed.shape[1]
    piece = pl.BlockSpec((BLOCK, width), lambda t, at: (0, 0))
    lanes = pl.BlockSpec((144, BLOCK), lambda t, at: (0, 2 * at[0] + at[1]))
    return pl.pallas_call(
        own_kernel,
        grid_spec=pltpu.PrefetchScalarGridSpec(
            num_scalar_prefetch=1,
            grid=(1,),
            in_specs=[piece] * 4
            + [
                pl.BlockSpec((BLOCK, width), lambda t, at: (2 * at[0] + at[1], 0)),
                lanes,
                lanes,
                whole(embed.shape),
                whole(unpatch.shape),
                whole(vec.shape),
            ],
            out_specs=[
                piece,
                pl.BlockSpec((144, BLOCK), lambda t, at: (0, 0)),
                pl.BlockSpec((144, width), lambda t, at: (0, 0)),
                pl.BlockSpec((8, width), lambda t, at: (0, 0)),
            ],
        ),
        out_shape=[
            jax.ShapeDtypeStruct((BLOCK, width), BF16),
            jax.ShapeDtypeStruct((144, BLOCK), F32),
            jax.ShapeDtypeStruct((144, width), F32),
            jax.ShapeDtypeStruct((8, width), F32),
        ],
        compiler_params=params(),
        cost_estimate=LIGHT,
        name="own_block",
    )(at, *pieces, attn, patches, cot_taps, embed, unpatch, vec)


def backward_kernel(
    at_ref, own_ref, other_ref, ffn_ref, out_near_ref, out_far_ref, gate_up_ref, attn_ref,
    patch_ref, embed_ref, cot_ref, unpatch_ref, vec_ref,
    d_ffn_ref, d_gate_up_ref, d_attn_ref, d_mid_ref, mixed_own_ref, mixed_other_ref, sums_ref,
):
    step = pl.program_id(0)
    chip, core = at_ref[0], at_ref[1]
    hidden_width = d_gate_up_ref.shape[1] // 2
    own, other = own_ref[0], other_ref[0]
    d_ffn = jnp.concatenate([halves(core, own, other), halves(core, other, own)], 0)
    d_ffn_ref[...] = d_ffn
    d_hidden = dot(d_ffn, ffn_ref[:, 2 * hidden_width :], (1, 0))
    gate = gate_up_ref[:, :hidden_width]
    up = gate_up_ref[:, hidden_width:]
    sigma = jax.nn.sigmoid(gate)
    silu = gate * sigma
    d_gate = d_hidden * up * (sigma + silu * (1.0 - sigma))
    d_gate_up = jnp.concatenate([d_gate.astype(BF16), (d_hidden * silu).astype(BF16)], 1)
    d_gate_up_ref[...] = d_gate_up
    d_second = dot(d_gate_up, ffn_ref[:, : 2 * hidden_width], (1, 1))

    x = dot(patch_ref[...], embed_ref[...], (0, 0))
    attn = attn_ref[...]
    attn_scale = row_rms(attn)
    attn_normed = attn * attn_scale
    mid = x + vec_ref[1:2] * attn_normed
    mid_scale = row_rms(mid)
    mid_sum = jnp.sum(mid * mid_scale * d_second, axis=0, keepdims=True)
    d_last = dot(cot_ref[...], unpatch_ref[...], (0, 0))
    place = lax.broadcasted_iota(jnp.int32, (PAIR, 1), 0) // BLOCK
    mine = (place == core) & (step == chip)
    d_mid = row_rms_back(mid, mid_scale, vec_ref[2:3] * d_second) + jnp.where(mine, d_last, 0.0)
    d_mid_ref[...] = d_mid
    attn_sum = jnp.sum(attn_normed * d_mid, axis=0, keepdims=True)
    d_attn = row_rms_back(attn, attn_scale, vec_ref[1:2] * d_mid).astype(BF16)
    d_attn_ref[...] = d_attn
    for k in range(4):
        mixed_own_ref[k] = dot(out_near_ref[k], d_attn, (1, 1)).astype(BF16)
        mixed_other_ref[k] = dot(out_far_ref[k], d_attn, (1, 1)).astype(BF16)

    @pl.when(step == 0)
    def _():
        sums_ref[...] = jnp.zeros_like(sums_ref)

    sums_ref[0:1] += mid_sum
    sums_ref[1:2] += attn_sum


def backward(at, d_ffn, ffn, out_whole, gate_up, attn, patches, embed, cot_taps, unpatch, vec):
    width = embed.shape[1]
    part = out_whole[0].shape[1]
    hidden_width = ffn.shape[1] // 3
    by_chip = pl.BlockSpec((1, BLOCK, width), lambda t, at: ((t - at[0] + 4) % 4, 0, 0))
    parts = pl.BlockSpec((4, part, PAIR), lambda t, at: (0, 0, t))
    return pl.pallas_call(
        backward_kernel,
        grid_spec=pltpu.PrefetchScalarGridSpec(
            num_scalar_prefetch=1,
            grid=(4,),
            in_specs=[
                by_chip,
                by_chip,
                whole(ffn.shape),
                whole((4, part, width)),
                whole((4, part, width)),
                row_block(PAIR, 2 * hidden_width),
                row_block(PAIR, width),
                lane_block(144, PAIR),
                whole(embed.shape),
                lane_block(144, PAIR),
                whole(unpatch.shape),
                whole(vec.shape),
            ],
            out_specs=[
                row_block(PAIR, width),
                row_block(PAIR, 2 * hidden_width),
                row_block(PAIR, width),
                row_block(PAIR, width),
                parts,
                parts,
                pl.BlockSpec((8, width), lambda t, at: (0, 0)),
            ],
        ),
        out_shape=[
            jax.ShapeDtypeStruct((TOKENS, width), BF16),
            jax.ShapeDtypeStruct((TOKENS, 2 * hidden_width), BF16),
            jax.ShapeDtypeStruct((TOKENS, width), BF16),
            jax.ShapeDtypeStruct((TOKENS, width), F32),
            jax.ShapeDtypeStruct((4, part, TOKENS), BF16),
            jax.ShapeDtypeStruct((4, part, TOKENS), BF16),
            jax.ShapeDtypeStruct((8, width), F32),
        ],
        compiler_params=params(),
        cost_estimate=LIGHT,
        name="backward",
    )(at, *d_ffn, ffn, *out_whole, gate_up, attn, patches, embed, cot_taps, unpatch, vec)


def weight_kernel(
    second_ref, d_gate_up_ref, d_ffn_ref, hidden_ref, near_ref, far_ref, d_attn_ref,
    grads_ref, out_near_ref, out_far_ref,
):
    step = pl.program_id(0)
    chunk, _, lanes = grads_ref.shape[0] // 4, *grads_ref.shape[1:]
    part = second_ref.shape[1] // chunk
    rows = jnp.concatenate(
        [
            dot(second_ref[...], d_gate_up_ref[...], (0, 0)).astype(BF16),
            dot(d_ffn_ref[...], hidden_ref[...], (0, 0)).astype(BF16),
        ],
        1,
    )
    groups = rows.shape[1] // lanes
    first = grads_ref.shape[1] - groups * part
    for c in range(chunk):
        for g in range(groups):
            grads_ref[step * chunk + c, first + g * part : first + (g + 1) * part] = rows[
                c * part : (c + 1) * part, g * lanes : (g + 1) * lanes
            ]
    out_near_ref[0] = dot(near_ref[0], d_attn_ref[...], (1, 0)).astype(BF16)
    out_far_ref[0] = dot(far_ref[0], d_attn_ref[...], (1, 0)).astype(BF16)


def weight_grads(second, d_gate_up, d_ffn, hidden, mixed, d_attn, text_rows):
    width = second.shape[1]
    heads_width = mixed[0].shape[1]
    lanes = 2 * heads_width
    grads = (COLS, text_rows + width // COLS * 3 * hidden.shape[1] // lanes, lanes)
    pieces = pl.BlockSpec((1, heads_width, TOKENS), lambda t: (t, 0, 0))
    out_piece = pl.BlockSpec((1, heads_width, width), lambda t: (t, 0, 0))
    out_shape = jax.ShapeDtypeStruct((4, heads_width, width), BF16)
    return pl.pallas_call(
        weight_kernel,
        grid=(4,),
        in_specs=[
            lane_block(TOKENS, width // 4),
            whole(d_gate_up.shape),
            lane_block(TOKENS, width // 4),
            whole(hidden.shape),
            pieces,
            pieces,
            whole(d_attn.shape),
        ],
        out_specs=[pl.BlockSpec(grads, lambda t: (0, 0, 0)), out_piece, out_piece],
        out_shape=[jax.ShapeDtypeStruct(grads, BF16), out_shape, out_shape],
        compiler_params=params(),
        cost_estimate=LIGHT,
        name="weight_grads",
    )(second, d_gate_up, d_ffn, hidden, *mixed, d_attn)


def first_kernel(
    at_ref, patch_ref, embed_ref, vec_ref, weight_ref, d_raw_ref, d_mid_ref, place_ref,
    unpatch_sum_ref, back_sums_ref, own_sums_ref, head_rows_ref, coef_ref,
    activation_ref,
    p0_ref, p1_ref, p2_ref, p3_ref, pack_ref,
    qkv_acc, taps_acc, embed_acc, first_acc, shared_acc, turned_acc,
):
    step = pl.program_id(0)
    last = pl.num_programs(0) - 1
    parts = (p0_ref, p1_ref, p2_ref, p3_ref)
    places = [lax.rem(at_ref[3] + d, 4) for d in range(4)]
    part = weight_ref.shape[1] // COLS
    x = dot(patch_ref[...], embed_ref[...], (0, 0))
    scale = row_rms(x)
    x_normed = x * scale
    h = (x_normed * vec_ref[0:1]).astype(BF16)
    d_h = dot(d_raw_ref[0], weight_ref[0], (0, 1))
    for s in (1, 2):
        d_h = d_h + dot(d_raw_ref[s], weight_ref[s], (0, 1))

    @pl.when(step == 0)
    def _():
        qkv_acc[...] = jnp.zeros_like(qkv_acc)
        embed_acc[...] = jnp.zeros_like(embed_acc)
        first_acc[...] = jnp.zeros_like(first_acc)

    for s in range(3):
        qkv_acc[s] += dot(d_raw_ref[s], h, (1, 0))
    first_acc[0:1] += jnp.sum(x_normed * d_h, axis=0, keepdims=True)
    d_first = (d_mid_ref[...] + row_rms_back(x, scale, vec_ref[0:1] * d_h)).astype(BF16)
    embed_acc[...] += dot(patch_ref[...], d_first, (1, 0))
    here = pl.ds(pl.multiple_of(step * PAIR, PAIR), PAIR)
    taps_acc[:, here] = dot(embed_ref[...], d_first, (1, 1))

    @pl.when(step == last)
    def _():
        for s in range(3):
            turned_acc[s] = qkv_acc[s].T.astype(BF16)
        end = part + part // 2
        for place, ref in zip(places, parts):
            for y in range(4):
                ahead_y = lax.rem(y - at_ref[2] + 4, 4)
                first = pl.multiple_of((y * 4 + place) * part, part)
                rows = [turned_acc[s, pl.ds(first, part), :] for s in range(3)]
                ref[ahead_y, :part] = jnp.concatenate(rows[:2], 1)
                ref[ahead_y, part:end] = jnp.concatenate(
                    [rows[2][: part // 2], rows[2][part // 2 :]], 1
                )
        terms = jnp.concatenate(
            [first_acc[0:1], back_sums_ref[1:2], back_sums_ref[0:1], own_sums_ref[0:1]], 0
        )
        d_gains = terms * coef_ref[0:4]
        d_modulation = terms * coef_ref[4:8]
        small = jnp.concatenate(
            [d_gains, head_rows_ref[0:4], jnp.zeros((24, d_gains.shape[1]), F32)], 0
        )
        for tile in range(12):
            lanes = slice(tile * 128, (tile + 1) * 128)
            first = tile * SHARED
            shared_acc[first : first + 144] = embed_acc[:, lanes].astype(BF16)
            shared_acc[first + 144 : first + 288] = unpatch_sum_ref[:, lanes].astype(BF16)
            shared_acc[first + 288 : first + SHARED] = small[:, lanes].astype(BF16)
        shared_acc[12 * SHARED :] = jnp.zeros((8 * CHUNK - 12 * SHARED, 128), BF16)
        latent = field_of(taps_acc[...], place_ref[...], -1)
        rows = [
            d_modulation[q : q + 1, tile * 128 : (tile + 1) * 128]
            for q in range(4)
            for tile in range(12)
        ]
        for r in range(ROWS):
            pack_ref[r, :CHUNK] = shared_acc[r * CHUNK : (r + 1) * CHUNK]
            pack_ref[r, CHUNK : CHUNK + 16] = activation_ref[r].astype(BF16)
            pack_ref[r, CHUNK + 16 : CHUNK + 32] = latent[r].astype(BF16)
            pack_ref[r, CHUNK + 32 : CHUNK + 48] = jnp.concatenate(
                rows[6 * r : 6 * r + 6] + [jnp.zeros((10, 128), F32)], 0
            ).astype(BF16)


def first_back(
    at, patches, embed, vec, weight, d_raw, d_mid, place, unpatch_sum,
    back_sums, own_sums, head_rows, coef, activation,
):
    width = embed.shape[1]
    part = weight.shape[2]
    grads = (4, 3 * width // (2 * COLS), 2 * part)
    pack = (ROWS, CHUNK + 48, 128)
    rest = (place, unpatch_sum, back_sums, own_sums, head_rows, coef, activation)
    return pl.pallas_call(
        first_kernel,
        grid_spec=pltpu.PrefetchScalarGridSpec(
            num_scalar_prefetch=1,
            grid=(TOKENS // PAIR,),
            in_specs=[
                lane_block(144, PAIR),
                whole(embed.shape),
                whole(vec.shape),
                whole(weight.shape),
                pl.BlockSpec((3, part, PAIR), lambda t, at: (0, 0, t)),
                row_block(PAIR, width),
            ]
            + [whole(value.shape) for value in rest],
            out_specs=[pl.BlockSpec(grads, lambda t, at: (0, 0, 0))] * 4
            + [pl.BlockSpec(pack, lambda t, at: (0, 0, 0))],
            scratch_shapes=[
                pltpu.VMEM((3, part, width), F32),
                pltpu.VMEM((144, TOKENS), F32),
                pltpu.VMEM((144, width), F32),
                pltpu.VMEM((8, width), F32),
                pltpu.VMEM((8 * CHUNK, 128), BF16),
                pltpu.VMEM((3, width, part), BF16),
            ],
        ),
        out_shape=[jax.ShapeDtypeStruct(grads, BF16)] * 4 + [jax.ShapeDtypeStruct(pack, BF16)],
        compiler_params=params(),
        cost_estimate=LIGHT,
        name="first_back",
    )(at, patches, embed, vec, weight, d_raw, d_mid, *rest)


def field_kernel(taps_ref, place_ref, field_ref):
    for r, tile in enumerate(field_of(taps_ref[...], place_ref[...], 1)):
        field_ref[r] = tile


def local(
    latent, condition, caption, cap_len, cotangent, embed_weight, modulate_weight, norm_gains,
    cross_gate, qkv_weight, text_kv_weight, out_weight, gate_up_weight, down_weight, unpatch_weight,
):
    images, _, _, channels = latent.shape
    width = embed_weight.shape[3]
    local_width = qkv_weight.shape[2]
    heads = local_width // HD
    hidden_width = down_weight.shape[0]
    taps = 9 * channels
    row_at = lax.axis_index("row")
    col_at = lax.axis_index("col")
    at = jnp.stack([row_at // 2, row_at % 2, col_at // 4, col_at % 4]).astype(jnp.int32)
    tile = latent.shape[1] * latent.shape[2] * channels

    cond_low = jax.nn.silu(condition.astype(F32)).astype(BF16)
    mod_piece = jnp.dot(cond_low, modulate_weight, preferred_element_type=F32)
    mod_columns = mod_piece.shape[1]
    mod_high = mod_piece.astype(BF16)
    mod_low = (mod_piece - mod_high.astype(F32)).astype(BF16)

    packed = jnp.concatenate(
        [latent.reshape(images, tile), cotangent.reshape(images, tile), mod_high, mod_low], axis=1
    )
    packed = jnp.pad(packed, ((0, 0), (0, 2 * local_width - packed.shape[1])))

    head_piece = jnp.concatenate(
        [
            jnp.concatenate([qkv_weight[0], qkv_weight[1]], axis=1),
            jnp.concatenate([qkv_weight[2], out_weight.T], axis=1),
        ]
    )
    piece_rows = head_piece.shape[0]
    head_pieces = jnp.concatenate(
        [
            jnp.broadcast_to(head_piece, (COLS,) + head_piece.shape),
            jnp.pad(packed[:, None], ((0, 0), (0, 15), (0, 0))),
        ],
        axis=1,
    )
    head_pieces = lax.all_to_all(head_pieces, "col", 0, 0)
    packed = send_all(head_pieces[:, piece_rows], "row")
    out_rows = out_weight_rows(head_pieces, width)
    packed = after(packed, out_rows)
    out_pieces = from_chips(out_rows)

    text_piece = jnp.concatenate([text_kv_weight[0], text_kv_weight[1]], axis=1)
    text_whole = lax.all_gather(text_piece, "col", axis=0, tiled=True)
    ffn_piece = jnp.concatenate([gate_up_weight[0], gate_up_weight[1], down_weight.T], axis=1)

    patches, cot_taps = image_taps(packed)
    mod_at = 2 * tile
    modulation = packed[:, :, mod_at : mod_at + mod_columns].astype(F32)
    modulation = modulation + packed[:, :, mod_at + mod_columns : mod_at + 2 * mod_columns].astype(F32)
    modulation = modulation.reshape(4, width)
    attn_gate = jnp.tanh(modulation[1])
    ffn_gate = jnp.tanh(modulation[3])
    vec = jnp.stack(
        [
            norm_gains[0] * (1.0 + modulation[0]),
            norm_gains[1] * attn_gate,
            norm_gains[2] * (1.0 + modulation[2]),
            norm_gains[3] * ffn_gate,
        ]
    )
    vec = jnp.pad(vec, ((0, 4), (0, 0)))
    embed = embed_weight.reshape(taps, width)
    unpatch = unpatch_weight.transpose(0, 1, 3, 2).reshape(taps, width)
    raw, qkv_whole = qkv_project(patches, embed, vec, head_pieces)
    ffn_whole = lax.all_gather(after(ffn_piece, text_whole, raw), "col", axis=0, tiled=True)
    raw = raw.reshape(3, heads, HD, TOKENS)
    caption_rows = caption[0]
    text_raw = dot(text_whole, caption_rows, (0, 1)).reshape(2, heads, HD, caption_rows.shape[0])
    head_gains = lax.dynamic_slice(norm_gains, (4, row_at * local_width), (3, local_width)).reshape(
        3, heads, HD, 1
    )
    head_gates = jnp.tanh(lax.dynamic_slice_in_dim(cross_gate, row_at * heads, heads))
    cap = lax.dynamic_slice_in_dim(cap_len, col_at, 1)
    table = jnp.asarray(rope_tables())
    mixed, lse = attend(raw, text_raw, head_gains, table, cap, head_gates)

    out_whole = with_other_core(lax.optimization_barrier((*out_pieces, mixed))[:4])
    mixed_whole = gather_near(mixed)
    attn, second, gate_up, hidden, ffn_own, ffn_other = forward(
        at, mixed_whole, out_whole, patches, embed, vec, ffn_whole
    )
    d_ffn_own, last_taps, unpatch_sum, own_sums = own_block(
        at, to_chips(sum_cores(ffn_own, ffn_other)), attn, patches, cot_taps, embed, unpatch, vec
    )
    d_ffn, d_gate_up, d_attn, d_mid, mixed_own, mixed_other, back_sums = backward(
        at, gather_near(d_ffn_own), ffn_whole, out_whole, gate_up, attn, patches, embed, cot_taps,
        unpatch, vec,
    )
    mixed_near = sum_cores(mixed_own, mixed_other)
    mixed_terms = to_chips(mixed_near)
    text_rows = text_kv_weight.shape[1]
    grads, out_near, out_far = weight_grads(
        after(second, *mixed_near), d_gate_up, d_ffn, hidden, mixed_whole, d_attn, text_rows
    )
    *mixed_terms, grads, out_near, out_far = lax.optimization_barrier(
        (*mixed_terms, grads, out_near, out_far)
    )
    d_mixed = sum(term.astype(F32) for term in mixed_terms).astype(BF16)
    d_mixed = d_mixed.reshape(heads, HD, TOKENS)
    out_near = sum_cores(out_near, out_far)

    grads, dq_text, d_text_head = text_back(
        raw, text_raw, head_gains, table, lse, d_mixed, cap, head_gates, caption_rows, grads
    )
    d_raw, d_head = attend_back(raw, head_gains, table, lse, d_mixed, after(dq_text, grads))
    d_raw = after(d_raw, *out_near)
    place = tile_places(False)
    activation_field = pl.pallas_call(
        field_kernel,
        out_shape=jax.ShapeDtypeStruct((ROWS, channels, BLOCK), F32),
        compiler_params=pltpu.CompilerParams(vmem_limit_bytes=VMEM),
        cost_estimate=LIGHT,
        name="activation_field",
    )(
        lax.dynamic_update_slice(jnp.zeros((taps, TOKENS), F32), last_taps, (0, row_at * BLOCK)),
        place,
    )
    one = jnp.ones_like(attn_gate)
    coef = jnp.stack(
        [
            one + modulation[0],
            attn_gate,
            one + modulation[2],
            ffn_gate,
            norm_gains[0],
            norm_gains[1] * (1.0 - attn_gate * attn_gate),
            norm_gains[2],
            norm_gains[3] * (1.0 - ffn_gate * ffn_gate),
        ]
    )
    head_part = jnp.concatenate([d_head, d_text_head[:1]]).reshape(3, local_width)
    head_sums = lax.dynamic_update_slice(
        jnp.zeros((8, width), F32), head_part, (0, row_at * local_width)
    )
    gate_part = jnp.sum(d_text_head[1], axis=(1, 2)) * (1.0 - head_gates * head_gates)
    head_sums = lax.dynamic_update_slice(head_sums, gate_part[None], (3, row_at * heads))
    *qkv_parts, row_pack = first_back(
        at, patches, embed, vec, qkv_whole, d_raw.reshape(3, local_width, TOKENS), d_mid, place,
        unpatch_sum, back_sums, own_sums,
        head_sums, coef, activation_field,
    )
    out_terms = to_chips(out_near)

    row_pack = jnp.sum(lax.all_to_all(row_pack, "row", 0, 0).astype(F32), axis=0)
    fields = row_pack[CHUNK : CHUNK + 2 * channels].T.reshape(COLS, 8, 2 * channels)
    mod_sums = row_pack[CHUNK + 2 * channels : CHUNK + 2 * channels + 6].reshape(COLS, 8, 6)
    fields = jnp.concatenate([fields, mod_sums], axis=2).astype(BF16)
    fields = jnp.pad(fields, ((0, 0), (0, 0), (0, 128 - fields.shape[2])))
    shared = row_pack[:CHUNK].astype(BF16).reshape(COLS, CHUNK // COLS, 128)
    col_pack = lax.all_to_all(jnp.concatenate([shared, fields], axis=1), "col", 0, 0)
    shared = jnp.sum(col_pack[:, : CHUNK // COLS].astype(F32), axis=0)
    shared = send_all(send_all(shared.astype(BF16), "col"), "row").reshape(-1, 128)
    shared = shared[: 12 * SHARED].reshape(12, SHARED, 128).astype(F32)
    fields = col_pack[:, CHUNK // COLS :]
    activation = fields[:, :, :channels].reshape(latent.shape)
    latent_grad = fields[:, :, channels : 2 * channels].reshape(latent.shape)
    modulate_grad = lax.dot_general(
        cond_low.astype(F32),
        fields[:, :, 2 * channels : 2 * channels + 6].reshape(images, mod_columns).astype(F32),
        (((0,), (0,)), ((), ())),
        precision=lax.Precision.HIGHEST,
        preferred_element_type=F32,
    )
    embed_grad = shared[:, :taps].transpose(1, 0, 2).reshape(embed_weight.shape)
    unpatch_grad = shared[:, taps : 2 * taps].reshape(12, 3, 3, channels, 128)
    unpatch_grad = unpatch_grad.transpose(1, 2, 0, 4, 3).reshape(unpatch_weight.shape)
    gains_grad = shared[:, 2 * taps : 2 * taps + 7].transpose(1, 0, 2).reshape(7, width)
    gate_grad = shared[0, 2 * taps + 7, :HEADS]

    part = width // COLS
    grads = lax.psum_scatter(
        grads.reshape(-1, 2 * local_width), "col", scatter_dimension=0, tiled=True
    ).astype(F32)
    text_kv_grad = jnp.stack([grads[:text_rows, :local_width], grads[:text_rows, local_width:]])
    ffn_total = jnp.concatenate(
        [grads[first : first + part] for first in range(text_rows, grads.shape[0], part)], axis=1
    )
    gate_up_grad = jnp.stack(
        [ffn_total[:, :hidden_width], ffn_total[:, hidden_width : 2 * hidden_width]]
    )
    down_grad = ffn_total[:, 2 * hidden_width :].T
    qkv_total = scatter_col(qkv_parts)
    first, second_half = qkv_total[:, :local_width], qkv_total[:, local_width:]
    values = jnp.concatenate([first[part:], second_half[part:]])
    qkv_grad = jnp.stack([first[:part], second_half[:part], values])
    out_sum = sum(term.astype(F32) for term in out_terms).astype(BF16)
    out_sum = out_sum.reshape(local_width, COLS, part).transpose(1, 0, 2)
    out_grad = jnp.sum(lax.all_to_all(out_sum, "col", 0, 0).astype(F32), axis=0)
    return (
        activation, latent_grad, embed_grad, modulate_grad, gains_grad, gate_grad,
        qkv_grad, text_kv_grad, out_grad, gate_up_grad, down_grad, unpatch_grad,
    )


def solution(mesh):
    placed = (
        P(None, "row", "col", None),
        P(),
        P("col", None, None),
        P(),
        P(None, "row", "col", None),
        P(),
        P(None, ("row", "col")),
        P(),
        P(),
        P(None, "col", "row"),
        P(None, "col", "row"),
        P("row", "col"),
        P(None, "col", "row"),
        P("row", "col"),
        P(),
    )
    return jax.shard_map(
        local,
        mesh=mesh,
        in_specs=placed,
        out_specs=(
            P(None, "row", "col", None),
            P(None, "row", "col", None),
            P(),
            P(None, ("row", "col")),
            P(),
            P(),
            P(None, "col", "row"),
            P(None, "col", "row"),
            P("row", "col"),
            P(None, "col", "row"),
            P("row", "col"),
            P(),
        ),
        check_vma=False,
    )
```

```python
import math
from functools import partial

import jax
import jax.numpy as jnp
import numpy as np
from jax import lax
from jax.experimental import pallas as pl
from jax.experimental.pallas import tpu as pltpu
from jax.sharding import PartitionSpec as P

HEADS = 24
HD = 64
GRID = 32
TOKENS = GRID * GRID
EPSILON = 1e-06
ROPE_BASE = 10000.0
MASKED = -1e30
F32 = jnp.float32
BF16 = jnp.bfloat16
ROWS = 8
COLS = 16
QUERY_BLOCK = 256
BLOCK = TOKENS // ROWS
PAIR = 2 * BLOCK
VMEM = 56 * 2**20
SHARED = 320
CHUNK = 512
LIGHT = pl.CostEstimate(flops=1, bytes_accessed=1, transcendentals=0)


def dot(left, right, contract):
    return lax.dot_general(
        left, right, ((contract[:1], contract[1:]), ((), ())), preferred_element_type=F32
    )


def row_pairs(dx, dc):
    return [
        (((x + dx) % 4) * 2 + (c + dc) % 2, x * 2 + c) for x in range(4) for c in range(2)
    ]


def row_pairs_to(dx, dc):
    return [(dst, src) for src, dst in row_pairs(dx, dc)]


def from_chips(piece):
    return [piece] + [lax.ppermute(piece, "row", row_pairs(d, 0)) for d in (1, 2, 3)]


def with_other_core(pieces):
    quad = jnp.stack(pieces)
    return quad, lax.ppermute(quad, "row", row_pairs(0, 1))


def gather_near(piece):
    return with_other_core(from_chips(piece))


def sum_cores(own, other):
    other = lax.ppermute(other, "row", row_pairs(0, 1))
    return [(own[d].astype(F32) + other[d].astype(F32)).astype(BF16) for d in range(4)]


def to_chips(near):
    return [near[0]] + [lax.ppermute(near[d], "row", row_pairs_to(d, 0)) for d in (1, 2, 3)]


def col_pairs_to(dy, dz):
    return [(y * 4 + z, (y + dy) % 4 * 4 + (z + dz) % 4) for y in range(4) for z in range(4)]


def along_col(parts, step):
    return [parts[0]] + [lax.ppermute(parts[d], "col", col_pairs_to(*step(d))) for d in (1, 2, 3)]


def send_all(piece, axis):
    copies = jnp.broadcast_to(piece, (lax.axis_size(axis),) + piece.shape)
    return lax.all_to_all(copies, axis, 0, 0)


def after(value, *others):
    return lax.optimization_barrier((value,) + others)[0]


def rope_tables():
    quarter = HD // 4
    frequency = np.float32(ROPE_BASE) ** (-np.arange(quarter, dtype=np.float32) / np.float32(quarter))
    place = np.arange(TOKENS)
    row = frequency[:, None] * (place // GRID).astype(np.float32)[None, :]
    col = frequency[:, None] * (place % GRID).astype(np.float32)[None, :]
    return np.stack([np.cos(row), np.sin(row), np.cos(col), np.sin(col)]).astype(np.float32)


def turn(v, table, sign):
    a, b, c, d = (v[k * 16 : (k + 1) * 16] for k in range(4))
    cr, sr, cc, sc = table[0], table[1] * sign, table[2], table[3] * sign
    return jnp.concatenate([a * cr - b * sr, a * sr + b * cr, c * cc - d * sc, c * sc + d * cc], 0)


def column_rms(v):
    return lax.rsqrt(jnp.mean(v * v, axis=0, keepdims=True) + EPSILON)


def normed(v, gain):
    return v * column_rms(v) * gain


def column_rms_back(v, u):
    scale = column_rms(v)
    return (u - v * (jnp.mean(u * v, axis=0, keepdims=True) * scale * scale)) * scale


def whole(shape):
    zeros = (0,) * len(shape)
    return pl.BlockSpec(shape, lambda *_: zeros, pipeline_mode=pl.Buffered(1))


def lane_block(rows, lanes):
    return pl.BlockSpec((rows, lanes), lambda t, *_: (0, t))


def row_block(rows, lanes):
    return pl.BlockSpec((rows, lanes), lambda t, *_: (t, 0))


def params():
    return pltpu.CompilerParams(vmem_limit_bytes=VMEM, dimension_semantics=("arbitrary",))


def attend_kernel(
    cap_ref, gate_ref, raw_ref, text_ref, gain_ref, table_ref, mixed_ref, lse_ref,
    q_ref, k_ref, v_ref, tk_ref, tv_ref,
):
    step = pl.program_id(0)
    heads = raw_ref.shape[1]

    @pl.when(step == 0)
    def _():
        table = table_ref[...]
        for h in range(heads):
            q = turn(normed(raw_ref[0, h], gain_ref[0, h]), table, 1.0).astype(BF16)
            q_ref[h] = q * jnp.asarray(0.125, BF16)
            k_ref[h] = turn(normed(raw_ref[1, h], gain_ref[1, h]), table, 1.0).T.astype(BF16)
            v_ref[h] = raw_ref[2, h].astype(BF16)
            tk_ref[h] = normed(text_ref[0, h], gain_ref[2, h]).T.astype(BF16)
            tv_ref[h] = text_ref[1, h].astype(BF16)

    slots = tk_ref.shape[1]
    mask = lax.broadcasted_iota(jnp.int32, (slots, QUERY_BLOCK), 0) < cap_ref[0]
    here = pl.ds(pl.multiple_of(step * QUERY_BLOCK, QUERY_BLOCK), QUERY_BLOCK)
    outs = []
    for h in range(heads):
        qb = q_ref[h, :, here]
        e = jnp.exp(dot(k_ref[h], qb, (1, 0)))
        total = jnp.sum(e, axis=0, keepdims=True)
        own = dot(v_ref[h], e.astype(BF16), (1, 0)) / total
        te = jnp.exp(jnp.where(mask, dot(tk_ref[h], qb, (1, 0)), MASKED))
        text_total = jnp.sum(te, axis=0, keepdims=True)
        text = dot(tv_ref[h], te.astype(BF16), (1, 0)) / text_total
        outs.append(own + gate_ref[h] * text)
        lse_ref[h, 0:1] = jnp.log(total)
        lse_ref[h, 1:2] = jnp.log(text_total)
    mixed_ref[...] = jnp.concatenate(outs, 0).astype(BF16)


def attend(raw, text_raw, gains, table, cap, gates):
    heads = raw.shape[1]
    slots = text_raw.shape[3]
    return pl.pallas_call(
        attend_kernel,
        grid_spec=pltpu.PrefetchScalarGridSpec(
            num_scalar_prefetch=2,
            grid=(TOKENS // QUERY_BLOCK,),
            in_specs=[
                whole((3, heads, HD, TOKENS)),
                whole((2, heads, HD, slots)),
                whole((3, heads, HD, 1)),
                whole((4, 16, TOKENS)),
            ],
            out_specs=[
                lane_block(heads * HD, QUERY_BLOCK),
                pl.BlockSpec((heads, 8, QUERY_BLOCK), lambda t, *_: (0, 0, t)),
            ],
            scratch_shapes=[
                pltpu.VMEM((heads, HD, TOKENS), BF16),
                pltpu.VMEM((heads, TOKENS, HD), BF16),
                pltpu.VMEM((heads, HD, TOKENS), BF16),
                pltpu.VMEM((heads, slots, HD), BF16),
                pltpu.VMEM((heads, HD, slots), BF16),
            ],
        ),
        out_shape=[
            jax.ShapeDtypeStruct((heads * HD, TOKENS), BF16),
            jax.ShapeDtypeStruct((heads, 8, TOKENS), F32),
        ],
        compiler_params=params(),
        cost_estimate=LIGHT,
        name="attend",
    )(cap, gates, raw, text_raw, gains, table)


def text_back_kernel(
    cap_ref, gate_ref, q_raw_ref, text_ref, gain_ref, table_ref, lse_ref, grad_ref, caption_ref, held_ref,
    grads_ref, dq_ref, d_gain_ref, low_ref,
):
    del held_ref
    step = pl.program_id(0)
    heads, _, slots = low_ref.shape[1:]

    @pl.when(step == 0)
    def _():
        table = table_ref[...]
        mask = lax.broadcasted_iota(jnp.int32, (slots, TOKENS), 0) < cap_ref[0]
        for h in range(heads):
            gate = gate_ref[h]
            q = turn(normed(q_raw_ref[h], gain_ref[0, h]), table, 1.0).astype(BF16)
            q = q * jnp.asarray(0.125, BF16)
            tk = normed(text_ref[0, h], gain_ref[2, h]).astype(BF16)
            tv = text_ref[1, h].astype(BF16)
            g = grad_ref[h]
            tp = jnp.exp(jnp.where(mask, dot(tk, q, (0, 0)), MASKED) - lse_ref[h, 1:2])
            tpb = tp.astype(BF16)
            low_ref[1, h] = (dot(g, tpb, (1, 1)) * gate).astype(BF16)
            gate_terms = g.astype(F32) * dot(tv, tpb, (1, 0))
            tpd = tp * dot(tv, g, (0, 0)) * gate
            dts = (tpd - tp * jnp.sum(tpd, axis=0, keepdims=True)).astype(BF16)
            dq_ref[h] = dot(tk, dts, (1, 0))
            d_tk = dot(q, dts, (1, 1))
            values = text_ref[0, h]
            low_ref[0, h] = column_rms_back(values, d_tk * gain_ref[2, h]).astype(BF16)
            d_gain_ref[0, h] = jnp.sum(values * column_rms(values) * d_tk, axis=1, keepdims=True)
            d_gain_ref[1, h] = jnp.sum(gate_terms, axis=1, keepdims=True)

    d_text = low_ref[...].reshape(2 * heads * HD, slots)
    rows = grads_ref.shape[1]
    for k in range(grads_ref.shape[0]):
        grads_ref[k] = dot(caption_ref[:, k * rows : (k + 1) * rows], d_text, (0, 1)).astype(BF16)


def text_back(raw, text_raw, gains, table, lse, grads, cap, gates, caption, held):
    heads = raw.shape[1]
    slots = text_raw.shape[3]
    rows = caption.shape[1] // COLS
    lanes = 2 * heads * HD
    return pl.pallas_call(
        text_back_kernel,
        grid_spec=pltpu.PrefetchScalarGridSpec(
            num_scalar_prefetch=2,
            grid=(4,),
            in_specs=[
                pl.BlockSpec((None, heads, HD, TOKENS), lambda t, *_: (0, 0, 0, 0)),
                whole(text_raw.shape),
                whole(gains.shape),
                whole(table.shape),
                whole(lse.shape),
                whole(grads.shape),
                pl.BlockSpec((slots, 4 * rows), lambda t, *_: (0, t)),
                pl.BlockSpec(memory_space=pl.ANY),
            ],
            out_specs=[
                pl.BlockSpec((4, rows, lanes), lambda t, *_: (t, 0, 0)),
                pl.BlockSpec((heads, HD, TOKENS), lambda t, *_: (0, 0, 0)),
                pl.BlockSpec((2, heads, HD, 1), lambda t, *_: (0, 0, 0, 0)),
            ],
            scratch_shapes=[pltpu.VMEM((2, heads, HD, slots), BF16)],
        ),
        out_shape=[
            jax.ShapeDtypeStruct(held.shape, BF16),
            jax.ShapeDtypeStruct((heads, HD, TOKENS), F32),
            jax.ShapeDtypeStruct((2, heads, HD, 1), F32),
        ],
        input_output_aliases={9: 0},
        compiler_params=params(),
        cost_estimate=LIGHT,
        name="text_back",
    )(cap, gates, raw, text_raw, gains, table, lse, grads, caption, held)


def attend_back_kernel(
    raw_ref, gain_ref, table_ref, lse_ref, grad_ref, dq_text_ref,
    d_raw_ref, d_gain_ref, dv_ref, dk_ref, dq_ref,
):
    table = table_ref[...]
    q = turn(normed(raw_ref[0], gain_ref[0]), table, 1.0).astype(BF16) * jnp.asarray(0.125, BF16)
    k = turn(normed(raw_ref[1], gain_ref[1]), table, 1.0)
    k, k_turned = k.astype(BF16), k.T.astype(BF16)
    v_turned = raw_ref[2].T.astype(BF16)
    for first in range(0, TOKENS, QUERY_BLOCK):
        here = slice(first, first + QUERY_BLOCK)
        qb = q[:, here]
        gb = grad_ref[:, here]
        p = jnp.exp(dot(k_turned, qb, (1, 0)) - lse_ref[0:1, here])
        dv = dot(gb, p.astype(BF16), (1, 1))
        pd = p * dot(v_turned, gb, (1, 0))
        ds = (pd - p * jnp.sum(pd, axis=0, keepdims=True)).astype(BF16)
        dq_ref[:, here] = dot(k, ds, (1, 0)) + dq_text_ref[:, here]
        dk = dot(qb, ds, (1, 1))
        if first == 0:
            dv_ref[...] = dv
            dk_ref[...] = dk
        else:
            dv_ref[...] += dv
            dk_ref[...] += dk

    def raw_back(which, d_turned):
        spun = turn(d_turned.astype(BF16).astype(F32), table, -1.0)
        values = raw_ref[which]
        d_raw_ref[which] = column_rms_back(values, spun * gain_ref[which]).astype(BF16)
        d_gain_ref[which] = jnp.sum(values * column_rms(values) * spun, axis=1, keepdims=True)

    raw_back(0, dq_ref[...] * 0.125)
    raw_back(1, dk_ref[...])
    d_raw_ref[2] = dv_ref[...].astype(BF16)


def attend_back(raw, gains, table, lse, grads, dq_text):
    heads = raw.shape[1]
    return pl.pallas_call(
        attend_back_kernel,
        grid=(heads,),
        in_specs=[
            pl.BlockSpec((3, None, HD, TOKENS), lambda h: (0, h, 0, 0)),
            pl.BlockSpec((3, None, HD, 1), lambda h: (0, h, 0, 0)),
            pl.BlockSpec((4, 16, TOKENS), lambda h: (0, 0, 0)),
            pl.BlockSpec((None, 8, TOKENS), lambda h: (h, 0, 0)),
            pl.BlockSpec((None, HD, TOKENS), lambda h: (h, 0, 0)),
            pl.BlockSpec((None, HD, TOKENS), lambda h: (h, 0, 0)),
        ],
        out_specs=[
            pl.BlockSpec((3, None, HD, TOKENS), lambda h: (0, h, 0, 0)),
            pl.BlockSpec((2, None, HD, 1), lambda h: (0, h, 0, 0)),
        ],
        scratch_shapes=[pltpu.VMEM((HD, TOKENS), F32) for _ in range(3)],
        out_shape=[
            jax.ShapeDtypeStruct((3, heads, HD, TOKENS), BF16),
            jax.ShapeDtypeStruct((2, heads, HD, 1), F32),
        ],
        compiler_params=params(),
        cost_estimate=LIGHT,
        name="attend_back",
    )(raw, gains, table, lse, grads, dq_text)


def tile_places(chunk_first):
    r, c, k = np.meshgrid(np.arange(ROWS), np.arange(COLS), np.arange(8), indexing="ij")
    token = r * BLOCK + (k // 2) * GRID + c * 2 + k % 2
    source = (k * ROWS + r) * COLS + c if chunk_first else (r * COLS + c) * 8 + k
    places = np.zeros((TOKENS, TOKENS), np.float32)
    places[source.ravel(), token.ravel()] = 1.0
    return jnp.asarray(places, BF16)


def grid_shift(field, di, dj):
    step = di * GRID + dj
    moved = pltpu.roll(field, (-step) % TOKENS, 1) if step else field
    place = lax.broadcasted_iota(jnp.int32, field.shape, 1)
    row = place // GRID + di
    col = place % GRID + dj
    inside = (row >= 0) & (row < GRID) & (col >= 0) & (col < GRID)
    return jnp.where(inside, moved, 0.0)


def image_kernel(packed_ref, place_ref, patch_ref, cot_ref):
    for which, sign, out_ref in ((0, 1, patch_ref), (1, -1, cot_ref)):
        lanes = slice(which * 128, (which + 1) * 128)
        tiles = jnp.concatenate([packed_ref[r, :, lanes] for r in range(ROWS)], 0)
        turned = tiles.astype(F32).T
        chunks = jnp.concatenate([turned[k * 16 : (k + 1) * 16] for k in range(8)], 1)
        image = dot(chunks.astype(BF16), place_ref[...], (1, 0))
        for a in range(3):
            for b in range(3):
                first = (a * 3 + b) * 16
                out_ref[first : first + 16] = grid_shift(
                    image, sign * (a - 1), sign * (b - 1)
                ).astype(BF16)


def image_taps(packed):
    out = jax.ShapeDtypeStruct((144, TOKENS), BF16)
    return pl.pallas_call(
        image_kernel,
        out_shape=[out, out],
        compiler_params=pltpu.CompilerParams(vmem_limit_bytes=VMEM),
        cost_estimate=LIGHT,
        name="image_taps",
    )(packed, tile_places(True))


def field_of(taps, place, sign):
    total = jnp.zeros((16, TOKENS), F32)
    for a in range(3):
        for b in range(3):
            first = (a * 3 + b) * 16
            total = total + grid_shift(taps[first : first + 16], sign * (a - 1), sign * (b - 1))
    tiles = dot(total.astype(BF16), place, (1, 1))
    return [tiles[:, r * BLOCK : (r + 1) * BLOCK] for r in range(ROWS)]


def row_rms(v):
    return lax.rsqrt(jnp.mean(v * v, axis=-1, keepdims=True) + EPSILON)


def row_rms_back(v, scale, u):
    return (u - v * (jnp.mean(u * v, axis=-1, keepdims=True) * scale * scale)) * scale


def out_rows_kernel(weight_ref, out_ref, turn_ref):
    part = turn_ref.shape[0] // COLS
    local_width = turn_ref.shape[1]
    for c in range(COLS):
        turn_ref[c * part : (c + 1) * part] = weight_ref[c, part : 2 * part, local_width:]
    out_ref[...] = turn_ref[...].T


def out_weight_rows(weight, width):
    part = weight.shape[2] // 2
    return pl.pallas_call(
        out_rows_kernel,
        out_shape=jax.ShapeDtypeStruct((part, width), BF16),
        scratch_shapes=[pltpu.VMEM((width, part), BF16)],
        compiler_params=pltpu.CompilerParams(vmem_limit_bytes=VMEM),
        cost_estimate=LIGHT,
        name="out_weight_rows",
    )(weight)


def qkv_kernel(patch_ref, embed_ref, vec_ref, weight_ref, raw_ref, joined_ref):
    width = embed_ref.shape[1]
    local_width = joined_ref.shape[2]
    part = width // COLS

    @pl.when(pl.program_id(0) == 0)
    def _():
        for c in range(COLS):
            here = slice(c * part, (c + 1) * part)
            for s in range(3):
                first = s // 2 * part
                lanes = slice(s % 2 * local_width, (s % 2 + 1) * local_width)
                joined_ref[s, here] = weight_ref[c, first : first + part, lanes]

    x = dot(patch_ref[...], embed_ref[...], (0, 0))
    h = (x * row_rms(x) * vec_ref[0:1]).astype(BF16)
    for s in range(3):
        raw_ref[s] = dot(h, joined_ref[s], (1, 0)).T


def qkv_project(patches, embed, vec, weight):
    width = embed.shape[1]
    part = weight.shape[2] // 2
    return pl.pallas_call(
        qkv_kernel,
        grid=(TOKENS // PAIR,),
        in_specs=[
            lane_block(144, PAIR),
            whole(embed.shape),
            whole(vec.shape),
            whole(weight.shape),
        ],
        out_specs=[
            pl.BlockSpec((3, part, PAIR), lambda t: (0, 0, t)),
            pl.BlockSpec((3, width, part), lambda t: (0, 0, 0)),
        ],
        out_shape=[
            jax.ShapeDtypeStruct((3, part, TOKENS), F32),
            jax.ShapeDtypeStruct((3, width, part), BF16),
        ],
        compiler_params=params(),
        cost_estimate=LIGHT,
        name="qkv_project",
    )(patches, embed, vec, weight)


def joined(ref):
    return ref[...].reshape(-1, ref.shape[2])


def halves(core, first, second):
    return jnp.where(core == 0, first, second)


def forward_kernel(
    at_ref, near_ref, far_ref, out_near_ref, out_far_ref, patch_ref, embed_ref, vec_ref, ffn_ref,
    attn_ref, second_ref, gate_up_ref, hidden_ref, own_ref, other_ref,
):
    core = at_ref[1]
    hidden_width = hidden_ref.shape[1]
    x = dot(patch_ref[...], embed_ref[...], (0, 0))
    attn = dot(joined(near_ref), joined(out_near_ref), (0, 0))
    attn = attn + dot(joined(far_ref), joined(out_far_ref), (0, 0))
    attn_ref[...] = attn
    mid = x + vec_ref[1:2] * (attn * row_rms(attn))
    second = (mid * row_rms(mid) * vec_ref[2:3]).astype(BF16)
    second_ref[...] = second
    gate_up = dot(second, ffn_ref[:, : 2 * hidden_width], (1, 0))
    gate_up_ref[...] = gate_up
    gate = gate_up[:, :hidden_width]
    hidden = (gate * jax.nn.sigmoid(gate) * gate_up[:, hidden_width:]).astype(BF16)
    hidden_ref[...] = hidden
    part = dot(hidden, ffn_ref[:, 2 * hidden_width :], (1, 1)).astype(BF16)
    own_ref[0] = halves(core, part[:BLOCK], part[BLOCK:])
    other_ref[0] = halves(core, part[BLOCK:], part[:BLOCK])


def forward(at, mixed, out_whole, patches, embed, vec, ffn):
    width = embed.shape[1]
    part = mixed[0].shape[1]
    hidden_width = ffn.shape[1] // 3
    by_chip = pl.BlockSpec((1, BLOCK, width), lambda t, at: ((t - at[0] + 4) % 4, 0, 0))
    return pl.pallas_call(
        forward_kernel,
        grid_spec=pltpu.PrefetchScalarGridSpec(
            num_scalar_prefetch=1,
            grid=(4,),
            in_specs=[
                pl.BlockSpec((4, part, PAIR), lambda t, at: (0, 0, t)),
                pl.BlockSpec((4, part, PAIR), lambda t, at: (0, 0, t)),
                whole((4, part, width)),
                whole((4, part, width)),
                lane_block(144, PAIR),
                whole(embed.shape),
                whole(vec.shape),
                whole(ffn.shape),
            ],
            out_specs=[
                row_block(PAIR, width),
                row_block(PAIR, width),
                row_block(PAIR, 2 * hidden_width),
                row_block(PAIR, hidden_width),
                by_chip,
                by_chip,
            ],
        ),
        out_shape=[
            jax.ShapeDtypeStruct((TOKENS, width), F32),
            jax.ShapeDtypeStruct((TOKENS, width), BF16),
            jax.ShapeDtypeStruct((TOKENS, 2 * hidden_width), F32),
            jax.ShapeDtypeStruct((TOKENS, hidden_width), BF16),
            jax.ShapeDtypeStruct((4, BLOCK, width), BF16),
            jax.ShapeDtypeStruct((4, BLOCK, width), BF16),
        ],
        compiler_params=params(),
        cost_estimate=LIGHT,
        name="forward",
    )(at, *mixed, *out_whole, patches, embed, vec, ffn)


def own_grad_kernel(p0_ref, p1_ref, p2_ref, p3_ref, cot_ref, unpatch_ref, vec_ref, d_ffn_ref, ffn_ref):
    ffn = sum(p[...].astype(F32) for p in (p0_ref, p1_ref, p2_ref, p3_ref))
    ffn_ref[...] = ffn
    d_last = dot(cot_ref[...], unpatch_ref[...], (0, 0))
    d_ffn_ref[...] = row_rms_back(ffn, row_rms(ffn), vec_ref[3:4] * d_last).astype(BF16)


def own_grad(pieces, cot_own, unpatch, vec):
    shape = (BLOCK, unpatch.shape[1])
    return pl.pallas_call(
        own_grad_kernel,
        out_shape=[jax.ShapeDtypeStruct(shape, BF16), jax.ShapeDtypeStruct(shape, F32)],
        compiler_params=pltpu.CompilerParams(vmem_limit_bytes=VMEM),
        cost_estimate=LIGHT,
        name="own_grad",
    )(*pieces, cot_own, unpatch, vec)


def own_kernel(
    at_ref, ffn_ref, attn_ref, patch_ref, cot_ref, embed_ref, unpatch_ref, vec_ref, place_ref,
    field_ref, unpatch_sum_ref, sums_ref, taps_ref,
):
    ffn = ffn_ref[...]
    d_last = dot(cot_ref[...], unpatch_ref[...], (0, 0))
    normed_ffn = ffn * row_rms(ffn)
    sums_ref[...] = jnp.broadcast_to(
        jnp.sum(normed_ffn * d_last, axis=0, keepdims=True), sums_ref.shape
    )
    attn = attn_ref[...]
    x = dot(patch_ref[...], embed_ref[...], (0, 0))
    last = (x + vec_ref[1:2] * (attn * row_rms(attn)) + vec_ref[3:4] * normed_ffn).astype(BF16)
    unpatch_sum_ref[...] = dot(cot_ref[...], last, (1, 0))
    taps_ref[...] = jnp.zeros_like(taps_ref)
    here = pl.multiple_of((2 * at_ref[0] + at_ref[1]) * BLOCK, BLOCK)
    taps_ref[:, pl.ds(here, BLOCK)] = dot(unpatch_ref[...], last, (1, 1))
    for r, tile in enumerate(field_of(taps_ref[...], place_ref[...], 1)):
        field_ref[r] = tile


def own_block(at, ffn, attn, patches, cot_taps, embed, unpatch, vec, place):
    width = embed.shape[1]
    lanes = pl.BlockSpec((144, BLOCK), lambda t, at: (0, 2 * at[0] + at[1]))
    return pl.pallas_call(
        own_kernel,
        grid_spec=pltpu.PrefetchScalarGridSpec(
            num_scalar_prefetch=1,
            grid=(1,),
            in_specs=[
                whole((BLOCK, width)),
                pl.BlockSpec((BLOCK, width), lambda t, at: (2 * at[0] + at[1], 0)),
                lanes,
                lanes,
                whole(embed.shape),
                whole(unpatch.shape),
                whole(vec.shape),
                whole(place.shape),
            ],
            out_specs=[
                pl.BlockSpec((ROWS, 16, BLOCK), lambda t, at: (0, 0, 0)),
                pl.BlockSpec((144, width), lambda t, at: (0, 0)),
                pl.BlockSpec((8, width), lambda t, at: (0, 0)),
            ],
            scratch_shapes=[pltpu.VMEM((144, TOKENS), F32)],
        ),
        out_shape=[
            jax.ShapeDtypeStruct((ROWS, 16, BLOCK), F32),
            jax.ShapeDtypeStruct((144, width), F32),
            jax.ShapeDtypeStruct((8, width), F32),
        ],
        compiler_params=params(),
        cost_estimate=LIGHT,
        name="own_block",
    )(at, ffn, attn, patches, cot_taps, embed, unpatch, vec, place)


def backward_kernel(
    at_ref, own_ref, other_ref, ffn_ref, out_near_ref, out_far_ref, gate_up_ref, attn_ref,
    patch_ref, embed_ref, cot_ref, unpatch_ref, vec_ref,
    d_ffn_ref, d_gate_up_ref, d_attn_ref, d_mid_ref, mixed_own_ref, mixed_other_ref, sums_ref,
):
    step = pl.program_id(0)
    chip, core = at_ref[0], at_ref[1]
    hidden_width = d_gate_up_ref.shape[1] // 2
    own, other = own_ref[0], other_ref[0]
    d_ffn = jnp.concatenate([halves(core, own, other), halves(core, other, own)], 0)
    d_ffn_ref[...] = d_ffn
    d_hidden = dot(d_ffn, ffn_ref[:, 2 * hidden_width :], (1, 0))
    gate = gate_up_ref[:, :hidden_width]
    up = gate_up_ref[:, hidden_width:]
    sigma = jax.nn.sigmoid(gate)
    silu = gate * sigma
    d_gate = d_hidden * up * (sigma + silu * (1.0 - sigma))
    d_gate_up = jnp.concatenate([d_gate.astype(BF16), (d_hidden * silu).astype(BF16)], 1)
    d_gate_up_ref[...] = d_gate_up
    d_second = dot(d_gate_up, ffn_ref[:, : 2 * hidden_width], (1, 1))

    x = dot(patch_ref[...], embed_ref[...], (0, 0))
    attn = attn_ref[...]
    attn_scale = row_rms(attn)
    attn_normed = attn * attn_scale
    mid = x + vec_ref[1:2] * attn_normed
    mid_scale = row_rms(mid)
    mid_sum = jnp.sum(mid * mid_scale * d_second, axis=0, keepdims=True)
    d_last = dot(cot_ref[...], unpatch_ref[...], (0, 0))
    place = lax.broadcasted_iota(jnp.int32, (PAIR, 1), 0) // BLOCK
    mine = (place == core) & (step == chip)
    d_mid = row_rms_back(mid, mid_scale, vec_ref[2:3] * d_second) + jnp.where(mine, d_last, 0.0)
    d_mid_ref[...] = d_mid
    attn_sum = jnp.sum(attn_normed * d_mid, axis=0, keepdims=True)
    d_attn = row_rms_back(attn, attn_scale, vec_ref[1:2] * d_mid).astype(BF16)
    d_attn_ref[...] = d_attn
    for weight_ref, part_ref in ((out_near_ref, mixed_own_ref), (out_far_ref, mixed_other_ref)):
        part_ref[...] = dot(joined(weight_ref), d_attn, (1, 1)).astype(BF16).reshape(part_ref.shape)

    @pl.when(step == 0)
    def _():
        sums_ref[...] = jnp.zeros_like(sums_ref)

    sums_ref[0:1] += mid_sum
    sums_ref[1:2] += attn_sum


def backward(at, d_ffn, ffn, out_whole, gate_up, attn, patches, embed, cot_taps, unpatch, vec):
    width = embed.shape[1]
    part = out_whole[0].shape[1]
    hidden_width = ffn.shape[1] // 3
    by_chip = pl.BlockSpec((1, BLOCK, width), lambda t, at: ((t - at[0] + 4) % 4, 0, 0))
    parts = pl.BlockSpec((4, part, PAIR), lambda t, at: (0, 0, t))
    return pl.pallas_call(
        backward_kernel,
        grid_spec=pltpu.PrefetchScalarGridSpec(
            num_scalar_prefetch=1,
            grid=(4,),
            in_specs=[
                by_chip,
                by_chip,
                whole(ffn.shape),
                whole((4, part, width)),
                whole((4, part, width)),
                row_block(PAIR, 2 * hidden_width),
                row_block(PAIR, width),
                lane_block(144, PAIR),
                whole(embed.shape),
                lane_block(144, PAIR),
                whole(unpatch.shape),
                whole(vec.shape),
            ],
            out_specs=[
                row_block(PAIR, width),
                row_block(PAIR, 2 * hidden_width),
                row_block(PAIR, width),
                row_block(PAIR, width),
                parts,
                parts,
                pl.BlockSpec((8, width), lambda t, at: (0, 0)),
            ],
        ),
        out_shape=[
            jax.ShapeDtypeStruct((TOKENS, width), BF16),
            jax.ShapeDtypeStruct((TOKENS, 2 * hidden_width), BF16),
            jax.ShapeDtypeStruct((TOKENS, width), BF16),
            jax.ShapeDtypeStruct((TOKENS, width), F32),
            jax.ShapeDtypeStruct((4, part, TOKENS), BF16),
            jax.ShapeDtypeStruct((4, part, TOKENS), BF16),
            jax.ShapeDtypeStruct((8, width), F32),
        ],
        compiler_params=params(),
        cost_estimate=LIGHT,
        name="backward",
    )(at, *d_ffn, ffn, *out_whole, gate_up, attn, patches, embed, cot_taps, unpatch, vec)


def weight_kernel(
    second_ref, d_gate_up_ref, d_ffn_ref, hidden_ref, near_ref, far_ref, d_attn_ref,
    grads_ref, out_near_ref, out_far_ref,
):
    step = pl.program_id(0)
    chunk, _, lanes = grads_ref.shape[0] // 4, *grads_ref.shape[1:]
    part = second_ref.shape[1] // chunk
    rows = jnp.concatenate(
        [
            dot(second_ref[...], d_gate_up_ref[...], (0, 0)).astype(BF16),
            dot(d_ffn_ref[...], hidden_ref[...], (0, 0)).astype(BF16),
        ],
        1,
    )
    groups = rows.shape[1] // lanes
    first = grads_ref.shape[1] - groups * part
    for c in range(chunk):
        for g in range(groups):
            grads_ref[step * chunk + c, first + g * part : first + (g + 1) * part] = rows[
                c * part : (c + 1) * part, g * lanes : (g + 1) * lanes
            ]
    out_near_ref[0] = dot(near_ref[0], d_attn_ref[...], (1, 0)).astype(BF16)
    out_far_ref[0] = dot(far_ref[0], d_attn_ref[...], (1, 0)).astype(BF16)


def weight_grads(second, d_gate_up, d_ffn, hidden, mixed, d_attn, text_rows):
    width = second.shape[1]
    heads_width = mixed[0].shape[1]
    lanes = 2 * heads_width
    grads = (COLS, text_rows + width // COLS * 3 * hidden.shape[1] // lanes, lanes)
    pieces = pl.BlockSpec((1, heads_width, TOKENS), lambda t: (t, 0, 0))
    out_piece = pl.BlockSpec((1, heads_width, width), lambda t: (t, 0, 0))
    out_shape = jax.ShapeDtypeStruct((4, heads_width, width), BF16)
    return pl.pallas_call(
        weight_kernel,
        grid=(4,),
        in_specs=[
            lane_block(TOKENS, width // 4),
            whole(d_gate_up.shape),
            lane_block(TOKENS, width // 4),
            whole(hidden.shape),
            pieces,
            pieces,
            whole(d_attn.shape),
        ],
        out_specs=[pl.BlockSpec(grads, lambda t: (0, 0, 0)), out_piece, out_piece],
        out_shape=[jax.ShapeDtypeStruct(grads, BF16), out_shape, out_shape],
        compiler_params=params(),
        cost_estimate=LIGHT,
        name="weight_grads",
    )(second, d_gate_up, d_ffn, hidden, *mixed, d_attn)


def first_kernel(
    at_ref, patch_ref, embed_ref, vec_ref, weight_ref, d_raw_ref, d_mid_ref, place_ref, out_sum_ref,
    unpatch_sum_ref, back_sums_ref, own_sums_ref, head_rows_ref, coef_ref, activation_ref,
    p0_ref, p1_ref, p2_ref, p3_ref, pack_ref,
    qkv_acc, taps_acc, embed_acc, first_acc, shared_acc, turned_acc,
):
    step = pl.program_id(0)
    last = pl.num_programs(0) - 1
    parts = (p0_ref, p1_ref, p2_ref, p3_ref)
    places = [lax.rem(at_ref[3] + d, 4) for d in range(4)]
    part = weight_ref.shape[1] // COLS
    x = dot(patch_ref[...], embed_ref[...], (0, 0))
    scale = row_rms(x)
    x_normed = x * scale
    h = (x_normed * vec_ref[0:1]).astype(BF16)
    d_h = dot(d_raw_ref[0], weight_ref[0], (0, 1))
    for s in (1, 2):
        d_h = d_h + dot(d_raw_ref[s], weight_ref[s], (0, 1))

    @pl.when(step == 0)
    def _():
        qkv_acc[...] = jnp.zeros_like(qkv_acc)
        embed_acc[...] = jnp.zeros_like(embed_acc)
        first_acc[...] = jnp.zeros_like(first_acc)

    qkv_acc[...] += dot(joined(d_raw_ref), h, (1, 0)).reshape(qkv_acc.shape)
    first_acc[0:1] += jnp.sum(x_normed * d_h, axis=0, keepdims=True)
    d_first = (d_mid_ref[...] + row_rms_back(x, scale, vec_ref[0:1] * d_h)).astype(BF16)
    embed_acc[...] += dot(patch_ref[...], d_first, (1, 0))
    here = pl.ds(pl.multiple_of(step * PAIR, PAIR), PAIR)
    taps_acc[:, here] = dot(embed_ref[...], d_first, (1, 1))

    @pl.when(step == last)
    def _():
        for s in range(4):
            turned_acc[s] = (qkv_acc[s] if s < 3 else out_sum_ref[...]).T.astype(BF16)
        for place, ref in zip(places, parts):
            for y in range(4):
                ahead_y = lax.rem(y - at_ref[2] + 4, 4)
                first = pl.multiple_of((y * 4 + place) * part, part)
                rows = [turned_acc[s, pl.ds(first, part), :] for s in range(4)]
                for k in range(2):
                    ref[ahead_y, k * part : (k + 1) * part] = jnp.concatenate(
                        rows[2 * k : 2 * k + 2], 1
                    )
        terms = jnp.concatenate(
            [first_acc[0:1], back_sums_ref[1:2], back_sums_ref[0:1], own_sums_ref[0:1]], 0
        )
        d_gains = terms * coef_ref[0:4]
        d_modulation = terms * coef_ref[4:8]
        small = jnp.concatenate(
            [d_gains, head_rows_ref[0:4], jnp.zeros((24, d_gains.shape[1]), F32)], 0
        )
        for tile in range(12):
            lanes = slice(tile * 128, (tile + 1) * 128)
            first = tile * SHARED
            shared_acc[first : first + 144] = embed_acc[:, lanes].astype(BF16)
            shared_acc[first + 144 : first + 288] = unpatch_sum_ref[:, lanes].astype(BF16)
            shared_acc[first + 288 : first + SHARED] = small[:, lanes].astype(BF16)
        shared_acc[12 * SHARED :] = jnp.zeros((8 * CHUNK - 12 * SHARED, 128), BF16)
        latent = field_of(taps_acc[...], place_ref[...], -1)
        rows = [
            d_modulation[q : q + 1, tile * 128 : (tile + 1) * 128]
            for q in range(4)
            for tile in range(12)
        ]
        for r in range(ROWS):
            pack_ref[r, :CHUNK] = shared_acc[r * CHUNK : (r + 1) * CHUNK]
            pack_ref[r, CHUNK : CHUNK + 16] = activation_ref[r].astype(BF16)
            pack_ref[r, CHUNK + 16 : CHUNK + 32] = latent[r].astype(BF16)
            pack_ref[r, CHUNK + 32 : CHUNK + 48] = jnp.concatenate(
                rows[6 * r : 6 * r + 6] + [jnp.zeros((10, 128), F32)], 0
            ).astype(BF16)


def first_back(
    at, patches, embed, vec, weight, d_raw, d_mid, place, out_sum, unpatch_sum,
    back_sums, own_sums, head_rows, coef, activation,
):
    width = embed.shape[1]
    part = weight.shape[2]
    grads = (4, 2 * width // COLS, 2 * part)
    pack = (ROWS, CHUNK + 48, 128)
    rest = (place, out_sum, unpatch_sum, back_sums, own_sums, head_rows, coef, activation)
    return pl.pallas_call(
        first_kernel,
        grid_spec=pltpu.PrefetchScalarGridSpec(
            num_scalar_prefetch=1,
            grid=(TOKENS // PAIR,),
            in_specs=[
                lane_block(144, PAIR),
                whole(embed.shape),
                whole(vec.shape),
                whole(weight.shape),
                pl.BlockSpec((3, part, PAIR), lambda t, at: (0, 0, t)),
                row_block(PAIR, width),
            ]
            + [whole(value.shape) for value in rest],
            out_specs=[pl.BlockSpec(grads, lambda t, at: (0, 0, 0))] * 4
            + [pl.BlockSpec(pack, lambda t, at: (0, 0, 0))],
            scratch_shapes=[
                pltpu.VMEM((3, part, width), F32),
                pltpu.VMEM((144, TOKENS), F32),
                pltpu.VMEM((144, width), F32),
                pltpu.VMEM((8, width), F32),
                pltpu.VMEM((8 * CHUNK, 128), BF16),
                pltpu.VMEM((4, width, part), BF16),
            ],
        ),
        out_shape=[jax.ShapeDtypeStruct(grads, BF16)] * 4 + [jax.ShapeDtypeStruct(pack, BF16)],
        compiler_params=params(),
        cost_estimate=LIGHT,
        name="first_back",
    )(at, patches, embed, vec, weight, d_raw, d_mid, *rest)


def local(
    latent, condition, caption, cap_len, cotangent, embed_weight, modulate_weight, norm_gains,
    cross_gate, qkv_weight, text_kv_weight, out_weight, gate_up_weight, down_weight, unpatch_weight,
):
    images, _, _, channels = latent.shape
    width = embed_weight.shape[3]
    local_width = qkv_weight.shape[2]
    heads = local_width // HD
    hidden_width = down_weight.shape[0]
    taps = 9 * channels
    row_at = lax.axis_index("row")
    col_at = lax.axis_index("col")
    at = jnp.stack([row_at // 2, row_at % 2, col_at // 4, col_at % 4]).astype(jnp.int32)
    tile = latent.shape[1] * latent.shape[2] * channels

    cond_low = jax.nn.silu(condition.astype(F32)).astype(BF16)
    mod_piece = jnp.dot(cond_low, modulate_weight, preferred_element_type=F32)
    mod_columns = mod_piece.shape[1]
    mod_high = mod_piece.astype(BF16)
    mod_low = (mod_piece - mod_high.astype(F32)).astype(BF16)

    packed = jnp.concatenate(
        [latent.reshape(images, tile), cotangent.reshape(images, tile), mod_high, mod_low], axis=1
    )
    packed = jnp.pad(packed, ((0, 0), (0, 2 * local_width - packed.shape[1])))

    head_piece = jnp.concatenate(
        [
            jnp.concatenate([qkv_weight[0], qkv_weight[1]], axis=1),
            jnp.concatenate([qkv_weight[2], out_weight.T], axis=1),
        ]
    )
    piece_rows = head_piece.shape[0]
    head_pieces = jnp.concatenate(
        [
            jnp.broadcast_to(head_piece, (COLS,) + head_piece.shape),
            jnp.pad(packed[:, None], ((0, 0), (0, 15), (0, 0))),
        ],
        axis=1,
    )
    head_pieces = lax.all_to_all(head_pieces, "col", 0, 0)
    packed = send_all(head_pieces[:, piece_rows], "row")
    out_rows = out_weight_rows(head_pieces, width)
    packed = after(packed, out_rows)
    out_pieces = from_chips(out_rows)

    text_piece = jnp.concatenate([text_kv_weight[0], text_kv_weight[1]], axis=1)
    text_whole = lax.all_gather(text_piece, "col", axis=0, tiled=True)
    ffn_piece = jnp.concatenate([gate_up_weight[0], gate_up_weight[1], down_weight.T], axis=1)

    patches, cot_taps = image_taps(packed)
    mod_at = 2 * tile
    modulation = packed[:, :, mod_at : mod_at + mod_columns].astype(F32)
    modulation = modulation + packed[:, :, mod_at + mod_columns : mod_at + 2 * mod_columns].astype(F32)
    modulation = modulation.reshape(4, width)
    attn_gate = jnp.tanh(modulation[1])
    ffn_gate = jnp.tanh(modulation[3])
    vec = jnp.stack(
        [
            norm_gains[0] * (1.0 + modulation[0]),
            norm_gains[1] * attn_gate,
            norm_gains[2] * (1.0 + modulation[2]),
            norm_gains[3] * ffn_gate,
        ]
    )
    vec = jnp.pad(vec, ((0, 4), (0, 0)))
    embed = embed_weight.reshape(taps, width)
    unpatch = unpatch_weight.transpose(0, 1, 3, 2).reshape(taps, width)
    raw, qkv_whole = qkv_project(patches, embed, vec, head_pieces)
    ffn_whole = lax.all_gather(after(ffn_piece, text_whole, raw), "col", axis=0, tiled=True)
    raw = raw.reshape(3, heads, HD, TOKENS)
    caption_rows = caption[0]
    text_raw = dot(text_whole, caption_rows, (0, 1)).reshape(2, heads, HD, caption_rows.shape[0])
    head_gains = lax.dynamic_slice(norm_gains, (4, row_at * local_width), (3, local_width)).reshape(
        3, heads, HD, 1
    )
    head_gates = jnp.tanh(lax.dynamic_slice_in_dim(cross_gate, row_at * heads, heads))
    cap = lax.dynamic_slice_in_dim(cap_len, col_at, 1)
    table = jnp.asarray(rope_tables())
    mixed, lse = attend(raw, text_raw, head_gains, table, cap, head_gates)

    out_whole = with_other_core(lax.optimization_barrier((*out_pieces, mixed))[:4])
    mixed_whole = gather_near(mixed)
    attn, second, gate_up, hidden, ffn_own, ffn_other = forward(
        at, mixed_whole, out_whole, patches, embed, vec, ffn_whole
    )
    place = tile_places(False)
    cot_own = lax.dynamic_slice_in_dim(cot_taps, row_at * BLOCK, BLOCK, 1)
    d_ffn_own, ffn_out = own_grad(
        to_chips(sum_cores(ffn_own, ffn_other)), cot_own, unpatch, vec
    )
    d_ffn_near = from_chips(d_ffn_own)
    activation_field, unpatch_sum, own_sums = own_block(
        at, ffn_out, attn, patches, cot_taps, embed, unpatch, vec, place
    )
    d_ffn_near = lax.optimization_barrier((*d_ffn_near, activation_field))[:4]
    d_ffn, d_gate_up, d_attn, d_mid, mixed_own, mixed_other, back_sums = backward(
        at, with_other_core(d_ffn_near), ffn_whole, out_whole, gate_up, attn, patches, embed, cot_taps,
        unpatch, vec,
    )
    mixed_near = sum_cores(mixed_own, mixed_other)
    mixed_terms = to_chips(mixed_near)
    text_rows = text_kv_weight.shape[1]
    grads, out_near, out_far = weight_grads(
        after(second, *mixed_near), d_gate_up, d_ffn, hidden, mixed_whole, d_attn, text_rows
    )
    *mixed_terms, grads, out_near, out_far = lax.optimization_barrier(
        (*mixed_terms, grads, out_near, out_far)
    )
    d_mixed = sum(term.astype(F32) for term in mixed_terms).astype(BF16)
    d_mixed = d_mixed.reshape(heads, HD, TOKENS)
    out_near = sum_cores(out_near, out_far)
    out_apart = lax.ppermute(out_near[2], "row", row_pairs_to(2, 0))

    grads, dq_text, d_text_head = text_back(
        raw, text_raw, head_gains, table, lse, d_mixed, cap, head_gates, caption_rows,
        after(grads, *out_near),
    )
    dq_text, grads, out_apart, *out_near = lax.optimization_barrier(
        (dq_text, grads, out_apart, *out_near)
    )
    d_raw, d_head = attend_back(raw, head_gains, table, lse, d_mixed, dq_text)
    out_beside = [lax.ppermute(out_near[d], "row", row_pairs_to(d, 0)) for d in (1, 3)]
    d_raw, *out_terms = lax.optimization_barrier((d_raw, out_near[0], out_apart, *out_beside))
    out_sum = sum(term.astype(F32) for term in out_terms)
    one = jnp.ones_like(attn_gate)
    coef = jnp.stack(
        [
            one + modulation[0],
            attn_gate,
            one + modulation[2],
            ffn_gate,
            norm_gains[0],
            norm_gains[1] * (1.0 - attn_gate * attn_gate),
            norm_gains[2],
            norm_gains[3] * (1.0 - ffn_gate * ffn_gate),
        ]
    )
    head_part = jnp.concatenate([d_head, d_text_head[:1]]).reshape(3, local_width)
    head_sums = lax.dynamic_update_slice(
        jnp.zeros((8, width), F32), head_part, (0, row_at * local_width)
    )
    gate_part = jnp.sum(d_text_head[1], axis=(1, 2)) * (1.0 - head_gates * head_gates)
    head_sums = lax.dynamic_update_slice(head_sums, gate_part[None], (3, row_at * heads))
    *head_parts, row_pack = first_back(
        at, patches, embed, vec, qkv_whole, d_raw.reshape(3, local_width, TOKENS), d_mid, place,
        out_sum, unpatch_sum, back_sums, own_sums, head_sums, coef, activation_field,
    )
    head_terms = along_col(head_parts, lambda d: (0, d))

    row_pack = jnp.sum(lax.all_to_all(row_pack, "row", 0, 0).astype(F32), axis=0)
    fields = row_pack[CHUNK : CHUNK + 2 * channels].T.reshape(COLS, 8, 2 * channels)
    mod_sums = row_pack[CHUNK + 2 * channels : CHUNK + 2 * channels + 6].reshape(COLS, 8, 6)
    fields = jnp.concatenate([fields, mod_sums], axis=2).astype(BF16)
    fields = jnp.pad(fields, ((0, 0), (0, 0), (0, 128 - fields.shape[2])))
    shared = row_pack[:CHUNK].astype(BF16).reshape(COLS, CHUNK // COLS, 128)
    col_pack = lax.all_to_all(jnp.concatenate([shared, fields], axis=1), "col", 0, 0)
    shared = jnp.sum(col_pack[:, : CHUNK // COLS].astype(F32), axis=0)
    shared = send_all(send_all(shared.astype(BF16), "col"), "row").reshape(-1, 128)
    shared = shared[: 12 * SHARED].reshape(12, SHARED, 128).astype(F32)
    fields = col_pack[:, CHUNK // COLS :]
    activation = fields[:, :, :channels].reshape(latent.shape)
    latent_grad = fields[:, :, channels : 2 * channels].reshape(latent.shape)
    modulate_grad = lax.dot_general(
        cond_low.astype(F32),
        fields[:, :, 2 * channels : 2 * channels + 6].reshape(images, mod_columns).astype(F32),
        (((0,), (0,)), ((), ())),
        precision=lax.Precision.HIGHEST,
        preferred_element_type=F32,
    )
    embed_grad = shared[:, :taps].transpose(1, 0, 2).reshape(embed_weight.shape)
    unpatch_grad = shared[:, taps : 2 * taps].reshape(12, 3, 3, channels, 128)
    unpatch_grad = unpatch_grad.transpose(1, 2, 0, 4, 3).reshape(unpatch_weight.shape)
    gains_grad = shared[:, 2 * taps : 2 * taps + 7].transpose(1, 0, 2).reshape(7, width)
    gate_grad = shared[0, 2 * taps + 7, :HEADS]

    part = width // COLS
    grads = lax.psum_scatter(
        grads.reshape(-1, 2 * local_width), "col", scatter_dimension=0, tiled=True
    ).astype(F32)
    text_kv_grad = jnp.stack([grads[:text_rows, :local_width], grads[:text_rows, local_width:]])
    ffn_total = jnp.concatenate(
        [grads[first : first + part] for first in range(text_rows, grads.shape[0], part)], axis=1
    )
    gate_up_grad = jnp.stack(
        [ffn_total[:, :hidden_width], ffn_total[:, hidden_width : 2 * hidden_width]]
    )
    down_grad = ffn_total[:, 2 * hidden_width :].T
    head_near = sum(term.astype(F32) for term in lax.optimization_barrier((*head_terms, col_pack))[:4])
    head_total = sum(
        term.astype(F32) for term in along_col(head_near.astype(BF16), lambda d: (d, 0))
    )
    first, second_half = head_total[:, :local_width], head_total[:, local_width:]
    qkv_grad = jnp.stack([first[:part], second_half[:part], first[part:]])
    out_grad = second_half[part:].T
    return (
        activation, latent_grad, embed_grad, modulate_grad, gains_grad, gate_grad,
        qkv_grad, text_kv_grad, out_grad, gate_up_grad, down_grad, unpatch_grad,
    )


def solution(mesh):
    placed = (
        P(None, "row", "col", None),
        P(),
        P("col", None, None),
        P(),
        P(None, "row", "col", None),
        P(),
        P(None, ("row", "col")),
        P(),
        P(),
        P(None, "col", "row"),
        P(None, "col", "row"),
        P("row", "col"),
        P(None, "col", "row"),
        P("row", "col"),
        P(),
    )
    return jax.shard_map(
        local,
        mesh=mesh,
        in_specs=placed,
        out_specs=(
            P(None, "row", "col", None),
            P(None, "row", "col", None),
            P(),
            P(None, ("row", "col")),
            P(),
            P(),
            P(None, "col", "row"),
            P(None, "col", "row"),
            P("row", "col"),
            P(None, "col", "row"),
            P("row", "col"),
            P(),
        ),
        check_vma=False,
    )
```

```python
import math
from functools import partial

import jax
import jax.numpy as jnp
import numpy as np
from jax import lax
from jax.experimental import pallas as pl
from jax.experimental.pallas import tpu as pltpu
from jax.sharding import PartitionSpec as P

HEADS = 24
HD = 64
GRID = 32
TOKENS = GRID * GRID
EPSILON = 1e-06
ROPE_BASE = 10000.0
MASKED = -1e30
F32 = jnp.float32
BF16 = jnp.bfloat16
ROWS = 8
COLS = 16
QUERY_BLOCK = 256
BLOCK = TOKENS // ROWS
PAIR = 2 * BLOCK
VMEM = 40 * 2**20
SHARED = 320
CHUNK = 512
LIGHT = pl.CostEstimate(flops=1, bytes_accessed=1, transcendentals=0)


def dot(left, right, contract):
    return lax.dot_general(
        left, right, ((contract[:1], contract[1:]), ((), ())), preferred_element_type=F32
    )


def row_pairs(dx, dc):
    return [
        (((x + dx) % 4) * 2 + (c + dc) % 2, x * 2 + c) for x in range(4) for c in range(2)
    ]


def row_pairs_to(dx, dc):
    return [(dst, src) for src, dst in row_pairs(dx, dc)]


def from_chips(piece):
    return [piece] + [lax.ppermute(piece, "row", row_pairs(d, 0)) for d in (1, 2, 3)]


def with_other_core(pieces):
    quad = jnp.stack(pieces)
    return quad, lax.ppermute(quad, "row", row_pairs(0, 1))


def gather_near(piece):
    return with_other_core(from_chips(piece))


def sum_cores(own, other):
    other = lax.ppermute(other, "row", row_pairs(0, 1))
    return [(own[d].astype(F32) + other[d].astype(F32)).astype(BF16) for d in range(4)]


def to_chips(near):
    return [near[0]] + [lax.ppermute(near[d], "row", row_pairs_to(d, 0)) for d in (1, 2, 3)]


def col_pairs_to(dy, dz):
    return [(y * 4 + z, (y + dy) % 4 * 4 + (z + dz) % 4) for y in range(4) for z in range(4)]


def col_pairs(dy, dz):
    return [(dst, src) for src, dst in col_pairs_to(dy, dz)]


def from_col(piece, step):
    return [piece] + [lax.ppermute(piece, "col", col_pairs(*step(d))) for d in (1, 2, 3)]


def along_y(d):
    return (d, 0)


def along_z(d):
    return (0, d)


def along_col(parts, step):
    return [parts[0]] + [lax.ppermute(parts[d], "col", col_pairs_to(*step(d))) for d in (1, 2, 3)]


def send_all(piece, axis):
    copies = jnp.broadcast_to(piece, (lax.axis_size(axis),) + piece.shape)
    return lax.all_to_all(copies, axis, 0, 0)


def after(value, *others):
    return lax.optimization_barrier((value,) + others)[0]


def rope_tables():
    quarter = HD // 4
    frequency = np.float32(ROPE_BASE) ** (-np.arange(quarter, dtype=np.float32) / np.float32(quarter))
    place = np.arange(TOKENS)
    row = frequency[:, None] * (place // GRID).astype(np.float32)[None, :]
    col = frequency[:, None] * (place % GRID).astype(np.float32)[None, :]
    return np.stack([np.cos(row), np.sin(row), np.cos(col), np.sin(col)]).astype(np.float32)


def turn(v, table, sign):
    a, b, c, d = (v[k * 16 : (k + 1) * 16] for k in range(4))
    cr, sr, cc, sc = table[0], table[1] * sign, table[2], table[3] * sign
    return jnp.concatenate([a * cr - b * sr, a * sr + b * cr, c * cc - d * sc, c * sc + d * cc], 0)


def column_rms(v):
    return lax.rsqrt(jnp.mean(v * v, axis=0, keepdims=True) + EPSILON)


def normed(v, gain):
    return v * column_rms(v) * gain


def column_rms_back(v, u):
    scale = column_rms(v)
    return (u - v * (jnp.mean(u * v, axis=0, keepdims=True) * scale * scale)) * scale


def whole(shape):
    zeros = (0,) * len(shape)
    return pl.BlockSpec(shape, lambda *_: zeros, pipeline_mode=pl.Buffered(1))


def held():
    return pl.BlockSpec(memory_space=pltpu.VMEM)


def lane_block(rows, lanes):
    return pl.BlockSpec((rows, lanes), lambda t, *_: (0, t))


def row_block(rows, lanes):
    return pl.BlockSpec((rows, lanes), lambda t, *_: (t, 0))


def params():
    return pltpu.CompilerParams(vmem_limit_bytes=VMEM, dimension_semantics=("arbitrary",))


def attend_kernel(
    cap_ref, gate_ref, raw_ref, text_ref, gain_ref, table_ref, mixed_ref, lse_ref,
    q_ref, k_ref, v_ref, tk_ref, tv_ref,
):
    step = pl.program_id(0)
    heads = raw_ref.shape[1]

    @pl.when(step == 0)
    def _():
        table = table_ref[...]
        for h in range(heads):
            q = turn(normed(raw_ref[0, h], gain_ref[0, h]), table, 1.0).astype(BF16)
            q_ref[h] = q * jnp.asarray(0.125, BF16)
            k_ref[h] = turn(normed(raw_ref[1, h], gain_ref[1, h]), table, 1.0).T.astype(BF16)
            v_ref[h] = raw_ref[2, h].astype(BF16)
            tk_ref[h] = normed(text_ref[0, h], gain_ref[2, h]).T.astype(BF16)
            tv_ref[h] = text_ref[1, h].astype(BF16)

    slots = tk_ref.shape[1]
    mask = lax.broadcasted_iota(jnp.int32, (slots, QUERY_BLOCK), 0) < cap_ref[0]
    here = pl.ds(pl.multiple_of(step * QUERY_BLOCK, QUERY_BLOCK), QUERY_BLOCK)
    outs = []
    for h in range(heads):
        qb = q_ref[h, :, here]
        e = jnp.exp(dot(k_ref[h], qb, (1, 0)))
        total = jnp.sum(e, axis=0, keepdims=True)
        own = dot(v_ref[h], e.astype(BF16), (1, 0)) / total
        te = jnp.exp(jnp.where(mask, dot(tk_ref[h], qb, (1, 0)), MASKED))
        text_total = jnp.sum(te, axis=0, keepdims=True)
        text = dot(tv_ref[h], te.astype(BF16), (1, 0)) / text_total
        outs.append(own + gate_ref[h] * text)
        lse_ref[h, 0:1] = jnp.log(total)
        lse_ref[h, 1:2] = jnp.log(text_total)
    mixed_ref[...] = jnp.concatenate(outs, 0).astype(BF16)


def attend(raw, text_raw, gains, table, cap, gates):
    heads = raw.shape[1]
    slots = text_raw.shape[3]
    return pl.pallas_call(
        attend_kernel,
        grid_spec=pltpu.PrefetchScalarGridSpec(
            num_scalar_prefetch=2,
            grid=(TOKENS // QUERY_BLOCK,),
            in_specs=[
                whole((3, heads, HD, TOKENS)),
                whole((2, heads, HD, slots)),
                whole((3, heads, HD, 1)),
                whole((4, 16, TOKENS)),
            ],
            out_specs=[
                lane_block(heads * HD, QUERY_BLOCK),
                pl.BlockSpec((heads, 8, QUERY_BLOCK), lambda t, *_: (0, 0, t)),
            ],
            scratch_shapes=[
                pltpu.VMEM((heads, HD, TOKENS), BF16),
                pltpu.VMEM((heads, TOKENS, HD), BF16),
                pltpu.VMEM((heads, HD, TOKENS), BF16),
                pltpu.VMEM((heads, slots, HD), BF16),
                pltpu.VMEM((heads, HD, slots), BF16),
            ],
        ),
        out_shape=[
            jax.ShapeDtypeStruct((heads * HD, TOKENS), BF16),
            jax.ShapeDtypeStruct((heads, 8, TOKENS), F32),
        ],
        compiler_params=params(),
        cost_estimate=LIGHT,
        name="attend",
    )(cap, gates, raw, text_raw, gains, table)


def text_back_kernel(
    cap_ref, gate_ref, q_raw_ref, text_ref, gain_ref, table_ref, lse_ref, grad_ref, caption_ref, held_ref,
    grads_ref, dq_ref, d_gain_ref, low_ref,
):
    del held_ref
    step = pl.program_id(0)
    heads, _, slots = low_ref.shape[1:]

    @pl.when(step == 0)
    def _():
        table = table_ref[...]
        mask = lax.broadcasted_iota(jnp.int32, (slots, TOKENS), 0) < cap_ref[0]
        for h in range(heads):
            gate = gate_ref[h]
            q = turn(normed(q_raw_ref[h], gain_ref[0, h]), table, 1.0).astype(BF16)
            q = q * jnp.asarray(0.125, BF16)
            tk = normed(text_ref[0, h], gain_ref[2, h]).astype(BF16)
            tv = text_ref[1, h].astype(BF16)
            g = grad_ref[h]
            tp = jnp.exp(jnp.where(mask, dot(tk, q, (0, 0)), MASKED) - lse_ref[h, 1:2])
            tpb = tp.astype(BF16)
            low_ref[1, h] = (dot(g, tpb, (1, 1)) * gate).astype(BF16)
            gate_terms = g.astype(F32) * dot(tv, tpb, (1, 0))
            tpd = tp * dot(tv, g, (0, 0)) * gate
            dts = (tpd - tp * jnp.sum(tpd, axis=0, keepdims=True)).astype(BF16)
            dq_ref[h] = dot(tk, dts, (1, 0))
            d_tk = dot(q, dts, (1, 1))
            values = text_ref[0, h]
            low_ref[0, h] = column_rms_back(values, d_tk * gain_ref[2, h]).astype(BF16)
            d_gain_ref[0, h] = jnp.sum(values * column_rms(values) * d_tk, axis=1, keepdims=True)
            d_gain_ref[1, h] = jnp.sum(gate_terms, axis=1, keepdims=True)

    d_text = low_ref[...].reshape(2 * heads * HD, slots)
    rows = grads_ref.shape[1]
    for k in range(grads_ref.shape[0]):
        grads_ref[k] = dot(caption_ref[:, k * rows : (k + 1) * rows], d_text, (0, 1)).astype(BF16)


def text_back(raw, text_raw, gains, table, lse, grads, cap, gates, caption, held):
    heads = raw.shape[1]
    slots = text_raw.shape[3]
    rows = caption.shape[1] // COLS
    lanes = 2 * heads * HD
    return pl.pallas_call(
        text_back_kernel,
        grid_spec=pltpu.PrefetchScalarGridSpec(
            num_scalar_prefetch=2,
            grid=(4,),
            in_specs=[
                pl.BlockSpec((None, heads, HD, TOKENS), lambda t, *_: (0, 0, 0, 0)),
                whole(text_raw.shape),
                whole(gains.shape),
                whole(table.shape),
                whole(lse.shape),
                whole(grads.shape),
                pl.BlockSpec((slots, 4 * rows), lambda t, *_: (0, t)),
                pl.BlockSpec(memory_space=pl.ANY),
            ],
            out_specs=[
                pl.BlockSpec((4, rows, lanes), lambda t, *_: (t, 0, 0)),
                pl.BlockSpec((heads, HD, TOKENS), lambda t, *_: (0, 0, 0)),
                pl.BlockSpec((2, heads, HD, 1), lambda t, *_: (0, 0, 0, 0)),
            ],
            scratch_shapes=[pltpu.VMEM((2, heads, HD, slots), BF16)],
        ),
        out_shape=[
            jax.ShapeDtypeStruct(held.shape, BF16),
            jax.ShapeDtypeStruct((heads, HD, TOKENS), F32),
            jax.ShapeDtypeStruct((2, heads, HD, 1), F32),
        ],
        input_output_aliases={9: 0},
        compiler_params=params(),
        cost_estimate=LIGHT,
        name="text_back",
    )(cap, gates, raw, text_raw, gains, table, lse, grads, caption, held)


def attend_back_kernel(
    raw_ref, gain_ref, table_ref, lse_ref, grad_ref, dq_text_ref,
    d_raw_ref, d_gain_ref, dv_ref, dk_ref, dq_ref,
):
    table = table_ref[...]
    q = turn(normed(raw_ref[0], gain_ref[0]), table, 1.0).astype(BF16) * jnp.asarray(0.125, BF16)
    k = turn(normed(raw_ref[1], gain_ref[1]), table, 1.0)
    k, k_turned = k.astype(BF16), k.T.astype(BF16)
    v_turned = raw_ref[2].T.astype(BF16)
    for first in range(0, TOKENS, QUERY_BLOCK):
        here = slice(first, first + QUERY_BLOCK)
        qb = q[:, here]
        gb = grad_ref[:, here]
        p = jnp.exp(dot(k_turned, qb, (1, 0)) - lse_ref[0:1, here])
        dv = dot(gb, p.astype(BF16), (1, 1))
        pd = p * dot(v_turned, gb, (1, 0))
        ds = (pd - p * jnp.sum(pd, axis=0, keepdims=True)).astype(BF16)
        dq_ref[:, here] = dot(k, ds, (1, 0)) + dq_text_ref[:, here]
        dk = dot(qb, ds, (1, 1))
        if first == 0:
            dv_ref[...] = dv
            dk_ref[...] = dk
        else:
            dv_ref[...] += dv
            dk_ref[...] += dk

    def raw_back(which, d_turned):
        spun = turn(d_turned.astype(BF16).astype(F32), table, -1.0)
        values = raw_ref[which]
        d_raw_ref[which] = column_rms_back(values, spun * gain_ref[which]).astype(BF16)
        d_gain_ref[which] = jnp.sum(values * column_rms(values) * spun, axis=1, keepdims=True)

    raw_back(0, dq_ref[...] * 0.125)
    raw_back(1, dk_ref[...])
    d_raw_ref[2] = dv_ref[...].astype(BF16)


def attend_back(raw, gains, table, lse, grads, dq_text):
    heads = raw.shape[1]
    return pl.pallas_call(
        attend_back_kernel,
        grid=(heads,),
        in_specs=[
            pl.BlockSpec((3, None, HD, TOKENS), lambda h: (0, h, 0, 0)),
            pl.BlockSpec((3, None, HD, 1), lambda h: (0, h, 0, 0)),
            pl.BlockSpec((4, 16, TOKENS), lambda h: (0, 0, 0)),
            pl.BlockSpec((None, 8, TOKENS), lambda h: (h, 0, 0)),
            pl.BlockSpec((None, HD, TOKENS), lambda h: (h, 0, 0)),
            pl.BlockSpec((None, HD, TOKENS), lambda h: (h, 0, 0)),
        ],
        out_specs=[
            pl.BlockSpec((3, None, HD, TOKENS), lambda h: (0, h, 0, 0)),
            pl.BlockSpec((2, None, HD, 1), lambda h: (0, h, 0, 0)),
        ],
        scratch_shapes=[pltpu.VMEM((HD, TOKENS), F32) for _ in range(3)],
        out_shape=[
            jax.ShapeDtypeStruct((3, heads, HD, TOKENS), BF16),
            jax.ShapeDtypeStruct((2, heads, HD, 1), F32),
        ],
        compiler_params=params(),
        cost_estimate=LIGHT,
        name="attend_back",
    )(raw, gains, table, lse, grads, dq_text)


def tile_places(chunk_first):
    r, c, k = np.meshgrid(np.arange(ROWS), np.arange(COLS), np.arange(8), indexing="ij")
    token = r * BLOCK + (k // 2) * GRID + c * 2 + k % 2
    source = (k * ROWS + r) * COLS + c if chunk_first else (r * COLS + c) * 8 + k
    places = np.zeros((TOKENS, TOKENS), np.float32)
    places[source.ravel(), token.ravel()] = 1.0
    return jnp.asarray(places, BF16)


def grid_shift(field, di, dj):
    step = di * GRID + dj
    moved = pltpu.roll(field, (-step) % TOKENS, 1) if step else field
    place = lax.broadcasted_iota(jnp.int32, field.shape, 1)
    row = place // GRID + di
    col = place % GRID + dj
    inside = (row >= 0) & (row < GRID) & (col >= 0) & (col < GRID)
    return jnp.where(inside, moved, 0.0)


def image_kernel(packed_ref, place_ref, patch_ref, cot_ref):
    for which, sign, out_ref in ((0, 1, patch_ref), (1, -1, cot_ref)):
        lanes = slice(which * 128, (which + 1) * 128)
        tiles = jnp.concatenate([packed_ref[r, :, lanes] for r in range(ROWS)], 0)
        turned = tiles.astype(F32).T
        chunks = jnp.concatenate([turned[k * 16 : (k + 1) * 16] for k in range(8)], 1)
        image = dot(chunks.astype(BF16), place_ref[...], (1, 0))
        for a in range(3):
            for b in range(3):
                first = (a * 3 + b) * 16
                out_ref[first : first + 16] = grid_shift(
                    image, sign * (a - 1), sign * (b - 1)
                ).astype(BF16)


def image_taps(packed):
    out = jax.ShapeDtypeStruct((144, TOKENS), BF16)
    return pl.pallas_call(
        image_kernel,
        out_shape=[out, out],
        compiler_params=pltpu.CompilerParams(vmem_limit_bytes=VMEM),
        cost_estimate=LIGHT,
        name="image_taps",
    )(packed, tile_places(True))


def field_of(taps, place, sign):
    total = jnp.zeros((16, TOKENS), F32)
    for a in range(3):
        for b in range(3):
            first = (a * 3 + b) * 16
            total = total + grid_shift(taps[first : first + 16], sign * (a - 1), sign * (b - 1))
    tiles = dot(total.astype(BF16), place, (1, 1))
    return [tiles[:, r * BLOCK : (r + 1) * BLOCK] for r in range(ROWS)]


def row_rms(v):
    return lax.rsqrt(jnp.mean(v * v, axis=-1, keepdims=True) + EPSILON)


def row_rms_back(v, scale, u):
    return (u - v * (jnp.mean(u * v, axis=-1, keepdims=True) * scale * scale)) * scale


def unpack_kernel(at_ref, *refs):
    first_refs, second_refs, (joined_ref, out_ref, turn_ref) = refs[:4], refs[4:8], refs[8:]
    part = first_refs[0].shape[1]
    local_width = first_refs[0].shape[2] // 2
    ys = [lax.rem(at_ref[2] + d, 4) for d in range(4)]
    zs = [lax.rem(at_ref[3] + d, 4) for d in range(4)]
    for dy in range(4):
        for dz in range(4):
            rows = pl.ds(pl.multiple_of((ys[dy] * 4 + zs[dz]) * part, part), part)
            piece = first_refs[dy][dz]
            joined_ref[0, rows, :] = piece[:, :local_width]
            joined_ref[1, rows, :] = piece[:, local_width:]
            piece = second_refs[dz][dy]
            joined_ref[2, rows, :] = piece[:, :local_width]
            turn_ref[rows, :] = piece[:, local_width:]
    out_ref[...] = turn_ref[...].T


def unpack_head(at, first, second):
    _, part, lanes = first[0].shape
    width, local_width = COLS * part, lanes // 2
    return pl.pallas_call(
        unpack_kernel,
        grid_spec=pltpu.PrefetchScalarGridSpec(
            num_scalar_prefetch=1,
            grid=(1,),
            in_specs=[whole(first[0].shape)] * 8,
            out_specs=[
                pl.BlockSpec((3, width, local_width), lambda t, at: (0, 0, 0)),
                pl.BlockSpec((local_width, width), lambda t, at: (0, 0)),
            ],
            scratch_shapes=[pltpu.VMEM((width, local_width), BF16)],
        ),
        out_shape=[
            jax.ShapeDtypeStruct((3, width, local_width), BF16),
            jax.ShapeDtypeStruct((local_width, width), BF16),
        ],
        compiler_params=params(),
        cost_estimate=LIGHT,
        name="unpack_head",
    )(at, *first, *second)


def qkv_kernel(patch_ref, embed_ref, vec_ref, weight_ref, raw_ref):
    x = dot(patch_ref[...], embed_ref[...], (0, 0))
    h = (x * row_rms(x) * vec_ref[0:1]).astype(BF16)
    for s in range(3):
        raw_ref[s] = dot(h, weight_ref[s], (1, 0)).T


def qkv_project(patches, embed, vec, weight):
    part = weight.shape[2]
    return pl.pallas_call(
        qkv_kernel,
        grid=(TOKENS // PAIR,),
        in_specs=[lane_block(144, PAIR), whole(embed.shape), whole(vec.shape), whole(weight.shape)],
        out_specs=pl.BlockSpec((3, part, PAIR), lambda t: (0, 0, t)),
        out_shape=jax.ShapeDtypeStruct((3, part, TOKENS), F32),
        compiler_params=params(),
        cost_estimate=LIGHT,
        name="qkv_project",
    )(patches, embed, vec, weight)


def joined(ref):
    return ref[...].reshape(-1, ref.shape[2])


def halves(core, first, second):
    return jnp.where(core == 0, first, second)


def forward_kernel(
    at_ref, near_ref, far_ref, out_near_ref, out_far_ref, patch_ref, embed_ref, vec_ref, ffn_ref,
    attn_ref, second_ref, gate_up_ref, hidden_ref, own_ref, other_ref,
):
    core = at_ref[1]
    hidden_width = hidden_ref.shape[1]
    x = dot(patch_ref[...], embed_ref[...], (0, 0))
    attn = dot(joined(near_ref), joined(out_near_ref), (0, 0))
    attn = attn + dot(joined(far_ref), joined(out_far_ref), (0, 0))
    attn_ref[...] = attn.astype(BF16)
    mid = x + vec_ref[1:2] * (attn * row_rms(attn))
    second = (mid * row_rms(mid) * vec_ref[2:3]).astype(BF16)
    second_ref[...] = second
    gate_up = dot(second, ffn_ref[:, : 2 * hidden_width], (1, 0))
    gate_up_ref[...] = gate_up.astype(BF16)
    gate = gate_up[:, :hidden_width]
    hidden = (gate * jax.nn.sigmoid(gate) * gate_up[:, hidden_width:]).astype(BF16)
    hidden_ref[...] = hidden
    part = dot(hidden, ffn_ref[:, 2 * hidden_width :], (1, 1)).astype(BF16)
    own_ref[0] = halves(core, part[:BLOCK], part[BLOCK:])
    other_ref[0] = halves(core, part[BLOCK:], part[:BLOCK])


def forward(at, mixed, out_whole, patches, embed, vec, ffn):
    width = embed.shape[1]
    part = mixed[0].shape[1]
    hidden_width = ffn.shape[1] // 3
    by_chip = pl.BlockSpec((1, BLOCK, width), lambda t, at: ((t - at[0] + 4) % 4, 0, 0))
    return pl.pallas_call(
        forward_kernel,
        grid_spec=pltpu.PrefetchScalarGridSpec(
            num_scalar_prefetch=1,
            grid=(4,),
            in_specs=[
                pl.BlockSpec((4, part, PAIR), lambda t, at: (0, 0, t)),
                pl.BlockSpec((4, part, PAIR), lambda t, at: (0, 0, t)),
                held(),
                held(),
                lane_block(144, PAIR),
                whole(embed.shape),
                whole(vec.shape),
                held(),
            ],
            out_specs=[
                row_block(PAIR, width),
                row_block(PAIR, width),
                row_block(PAIR, 2 * hidden_width),
                row_block(PAIR, hidden_width),
                by_chip,
                by_chip,
            ],
        ),
        out_shape=[
            jax.ShapeDtypeStruct((TOKENS, width), BF16),
            jax.ShapeDtypeStruct((TOKENS, width), BF16),
            jax.ShapeDtypeStruct((TOKENS, 2 * hidden_width), BF16),
            jax.ShapeDtypeStruct((TOKENS, hidden_width), BF16),
            jax.ShapeDtypeStruct((4, BLOCK, width), BF16),
            jax.ShapeDtypeStruct((4, BLOCK, width), BF16),
        ],
        compiler_params=params(),
        cost_estimate=LIGHT,
        name="forward",
    )(at, *mixed, *out_whole, patches, embed, vec, ffn)


def own_grad_kernel(p0_ref, p1_ref, p2_ref, p3_ref, cot_ref, unpatch_ref, vec_ref, d_ffn_ref, ffn_ref):
    ffn = sum(p[...].astype(F32) for p in (p0_ref, p1_ref, p2_ref, p3_ref))
    ffn_ref[...] = ffn
    d_last = dot(cot_ref[...], unpatch_ref[...], (0, 0))
    d_ffn_ref[...] = row_rms_back(ffn, row_rms(ffn), vec_ref[3:4] * d_last).astype(BF16)


def own_grad(pieces, cot_own, unpatch, vec):
    shape = (BLOCK, unpatch.shape[1])
    return pl.pallas_call(
        own_grad_kernel,
        out_shape=[jax.ShapeDtypeStruct(shape, BF16), jax.ShapeDtypeStruct(shape, F32)],
        compiler_params=pltpu.CompilerParams(vmem_limit_bytes=VMEM),
        cost_estimate=LIGHT,
        name="own_grad",
    )(*pieces, cot_own, unpatch, vec)


def own_kernel(
    at_ref, ffn_ref, attn_ref, patch_ref, cot_ref, embed_ref, unpatch_ref, vec_ref, place_ref,
    field_ref, unpatch_sum_ref, sums_ref, taps_ref,
):
    ffn = ffn_ref[...]
    d_last = dot(cot_ref[...], unpatch_ref[...], (0, 0))
    normed_ffn = ffn * row_rms(ffn)
    sums_ref[...] = jnp.broadcast_to(
        jnp.sum(normed_ffn * d_last, axis=0, keepdims=True), sums_ref.shape
    )
    attn = attn_ref[...].astype(F32)
    x = dot(patch_ref[...], embed_ref[...], (0, 0))
    last = (x + vec_ref[1:2] * (attn * row_rms(attn)) + vec_ref[3:4] * normed_ffn).astype(BF16)
    unpatch_sum_ref[...] = dot(cot_ref[...], last, (1, 0))
    taps_ref[...] = jnp.zeros_like(taps_ref)
    here = pl.multiple_of((2 * at_ref[0] + at_ref[1]) * BLOCK, BLOCK)
    taps_ref[:, pl.ds(here, BLOCK)] = dot(unpatch_ref[...], last, (1, 1))
    for r, tile in enumerate(field_of(taps_ref[...], place_ref[...], 1)):
        field_ref[r] = tile


def own_block(at, ffn, attn, patches, cot_taps, embed, unpatch, vec, place):
    width = embed.shape[1]
    lanes = pl.BlockSpec((144, BLOCK), lambda t, at: (0, 2 * at[0] + at[1]))
    return pl.pallas_call(
        own_kernel,
        grid_spec=pltpu.PrefetchScalarGridSpec(
            num_scalar_prefetch=1,
            grid=(1,),
            in_specs=[
                whole((BLOCK, width)),
                pl.BlockSpec((BLOCK, width), lambda t, at: (2 * at[0] + at[1], 0)),
                lanes,
                lanes,
                whole(embed.shape),
                whole(unpatch.shape),
                whole(vec.shape),
                whole(place.shape),
            ],
            out_specs=[
                pl.BlockSpec((ROWS, 16, BLOCK), lambda t, at: (0, 0, 0)),
                pl.BlockSpec((144, width), lambda t, at: (0, 0)),
                pl.BlockSpec((8, width), lambda t, at: (0, 0)),
            ],
            scratch_shapes=[pltpu.VMEM((144, TOKENS), F32)],
        ),
        out_shape=[
            jax.ShapeDtypeStruct((ROWS, 16, BLOCK), F32),
            jax.ShapeDtypeStruct((144, width), F32),
            jax.ShapeDtypeStruct((8, width), F32),
        ],
        compiler_params=params(),
        cost_estimate=LIGHT,
        name="own_block",
    )(at, ffn, attn, patches, cot_taps, embed, unpatch, vec, place)


def backward_kernel(
    at_ref, own_ref, other_ref, ffn_ref, out_near_ref, out_far_ref, gate_up_ref, attn_ref,
    patch_ref, embed_ref, cot_ref, unpatch_ref, vec_ref,
    d_ffn_ref, d_gate_up_ref, d_attn_ref, d_mid_ref, mixed_own_ref, mixed_other_ref, sums_ref,
):
    step = pl.program_id(0)
    chip, core = at_ref[0], at_ref[1]
    hidden_width = d_gate_up_ref.shape[1] // 2
    own, other = own_ref[0], other_ref[0]
    d_ffn = jnp.concatenate([halves(core, own, other), halves(core, other, own)], 0)
    d_ffn_ref[...] = d_ffn
    d_hidden = dot(d_ffn, ffn_ref[:, 2 * hidden_width :], (1, 0))
    gate = gate_up_ref[:, :hidden_width].astype(F32)
    up = gate_up_ref[:, hidden_width:].astype(F32)
    sigma = jax.nn.sigmoid(gate)
    silu = gate * sigma
    d_gate = d_hidden * up * (sigma + silu * (1.0 - sigma))
    d_gate_up = jnp.concatenate([d_gate.astype(BF16), (d_hidden * silu).astype(BF16)], 1)
    d_gate_up_ref[...] = d_gate_up
    d_second = dot(d_gate_up, ffn_ref[:, : 2 * hidden_width], (1, 1))

    x = dot(patch_ref[...], embed_ref[...], (0, 0))
    attn = attn_ref[...].astype(F32)
    attn_scale = row_rms(attn)
    attn_normed = attn * attn_scale
    mid = x + vec_ref[1:2] * attn_normed
    mid_scale = row_rms(mid)
    mid_sum = jnp.sum(mid * mid_scale * d_second, axis=0, keepdims=True)
    d_last = dot(cot_ref[...], unpatch_ref[...], (0, 0))
    place = lax.broadcasted_iota(jnp.int32, (PAIR, 1), 0) // BLOCK
    mine = (place == core) & (step == chip)
    d_mid = row_rms_back(mid, mid_scale, vec_ref[2:3] * d_second) + jnp.where(mine, d_last, 0.0)
    d_mid_ref[...] = d_mid.astype(BF16)
    attn_sum = jnp.sum(attn_normed * d_mid, axis=0, keepdims=True)
    d_attn = row_rms_back(attn, attn_scale, vec_ref[1:2] * d_mid).astype(BF16)
    d_attn_ref[...] = d_attn
    for weight_ref, part_ref in ((out_near_ref, mixed_own_ref), (out_far_ref, mixed_other_ref)):
        part_ref[...] = dot(joined(weight_ref), d_attn, (1, 1)).astype(BF16).reshape(part_ref.shape)

    @pl.when(step == 0)
    def _():
        sums_ref[...] = jnp.zeros_like(sums_ref)

    sums_ref[0:1] += mid_sum
    sums_ref[1:2] += attn_sum


def backward(at, d_ffn, ffn, out_whole, gate_up, attn, patches, embed, cot_taps, unpatch, vec):
    width = embed.shape[1]
    part = out_whole[0].shape[1]
    hidden_width = ffn.shape[1] // 3
    by_chip = pl.BlockSpec((1, BLOCK, width), lambda t, at: ((t - at[0] + 4) % 4, 0, 0))
    parts = pl.BlockSpec((4, part, PAIR), lambda t, at: (0, 0, t))
    return pl.pallas_call(
        backward_kernel,
        grid_spec=pltpu.PrefetchScalarGridSpec(
            num_scalar_prefetch=1,
            grid=(4,),
            in_specs=[
                by_chip,
                by_chip,
                held(),
                held(),
                held(),
                row_block(PAIR, 2 * hidden_width),
                row_block(PAIR, width),
                lane_block(144, PAIR),
                whole(embed.shape),
                lane_block(144, PAIR),
                whole(unpatch.shape),
                whole(vec.shape),
            ],
            out_specs=[
                row_block(PAIR, width),
                row_block(PAIR, 2 * hidden_width),
                row_block(PAIR, width),
                row_block(PAIR, width),
                parts,
                parts,
                pl.BlockSpec((8, width), lambda t, at: (0, 0)),
            ],
        ),
        out_shape=[
            jax.ShapeDtypeStruct((TOKENS, width), BF16),
            jax.ShapeDtypeStruct((TOKENS, 2 * hidden_width), BF16),
            jax.ShapeDtypeStruct((TOKENS, width), BF16),
            jax.ShapeDtypeStruct((TOKENS, width), BF16),
            jax.ShapeDtypeStruct((4, part, TOKENS), BF16),
            jax.ShapeDtypeStruct((4, part, TOKENS), BF16),
            jax.ShapeDtypeStruct((8, width), F32),
        ],
        compiler_params=params(),
        cost_estimate=LIGHT,
        name="backward",
    )(at, *d_ffn, ffn, *out_whole, gate_up, attn, patches, embed, cot_taps, unpatch, vec)


def weight_kernel(
    second_ref, d_gate_up_ref, d_ffn_ref, hidden_ref, near_ref, far_ref, d_attn_ref,
    grads_ref, out_near_ref, out_far_ref,
):
    step = pl.program_id(0)
    chunk, _, lanes = grads_ref.shape[0] // 4, *grads_ref.shape[1:]
    part = second_ref.shape[1] // chunk
    rows = jnp.concatenate(
        [
            dot(second_ref[...], d_gate_up_ref[...], (0, 0)).astype(BF16),
            dot(d_ffn_ref[...], hidden_ref[...], (0, 0)).astype(BF16),
        ],
        1,
    )
    groups = rows.shape[1] // lanes
    first = grads_ref.shape[1] - groups * part
    for c in range(chunk):
        for g in range(groups):
            grads_ref[step * chunk + c, first + g * part : first + (g + 1) * part] = rows[
                c * part : (c + 1) * part, g * lanes : (g + 1) * lanes
            ]
    out_near_ref[0] = dot(near_ref[0], d_attn_ref[...], (1, 0)).astype(BF16)
    out_far_ref[0] = dot(far_ref[0], d_attn_ref[...], (1, 0)).astype(BF16)


def weight_grads(second, d_gate_up, d_ffn, hidden, mixed, d_attn, text_rows):
    width = second.shape[1]
    heads_width = mixed[0].shape[1]
    lanes = 2 * heads_width
    grads = (COLS, text_rows + width // COLS * 3 * hidden.shape[1] // lanes, lanes)
    pieces = pl.BlockSpec((1, heads_width, TOKENS), lambda t: (t, 0, 0))
    out_piece = pl.BlockSpec((1, heads_width, width), lambda t: (t, 0, 0))
    out_shape = jax.ShapeDtypeStruct((4, heads_width, width), BF16)
    return pl.pallas_call(
        weight_kernel,
        grid=(4,),
        in_specs=[
            lane_block(TOKENS, width // 4),
            whole(d_gate_up.shape),
            lane_block(TOKENS, width // 4),
            whole(hidden.shape),
            pieces,
            pieces,
            whole(d_attn.shape),
        ],
        out_specs=[pl.BlockSpec(grads, lambda t: (0, 0, 0)), out_piece, out_piece],
        out_shape=[jax.ShapeDtypeStruct(grads, BF16), out_shape, out_shape],
        compiler_params=params(),
        cost_estimate=LIGHT,
        name="weight_grads",
    )(second, d_gate_up, d_ffn, hidden, *mixed, d_attn)


def first_kernel(
    patch_ref, embed_ref, vec_ref, weight_ref, d_raw_ref, d_mid_ref, place_ref,
    unpatch_sum_ref, back_sums_ref, own_sums_ref, head_rows_ref, coef_ref, activation_ref,
    pack_ref, taps_acc, embed_acc, first_acc, shared_acc,
):
    step = pl.program_id(0)
    last = pl.num_programs(0) - 1
    x = dot(patch_ref[...], embed_ref[...], (0, 0))
    scale = row_rms(x)
    x_normed = x * scale
    d_h = dot(d_raw_ref[0], weight_ref[0], (0, 1))
    for s in (1, 2):
        d_h = d_h + dot(d_raw_ref[s], weight_ref[s], (0, 1))

    @pl.when(step == 0)
    def _():
        embed_acc[...] = jnp.zeros_like(embed_acc)
        first_acc[...] = jnp.zeros_like(first_acc)

    first_acc[0:1] += jnp.sum(x_normed * d_h, axis=0, keepdims=True)
    d_first = (d_mid_ref[...].astype(F32) + row_rms_back(x, scale, vec_ref[0:1] * d_h)).astype(BF16)
    embed_acc[...] += dot(patch_ref[...], d_first, (1, 0))
    here = pl.ds(pl.multiple_of(step * PAIR, PAIR), PAIR)
    taps_acc[:, here] = dot(embed_ref[...], d_first, (1, 1))

    @pl.when(step == last)
    def _():
        terms = jnp.concatenate(
            [first_acc[0:1], back_sums_ref[1:2], back_sums_ref[0:1], own_sums_ref[0:1]], 0
        )
        d_gains = terms * coef_ref[0:4]
        d_modulation = terms * coef_ref[4:8]
        small = jnp.concatenate(
            [d_gains, head_rows_ref[0:4], jnp.zeros((24, d_gains.shape[1]), F32)], 0
        )
        for tile in range(12):
            lanes = slice(tile * 128, (tile + 1) * 128)
            first = tile * SHARED
            shared_acc[first : first + 144] = embed_acc[:, lanes].astype(BF16)
            shared_acc[first + 144 : first + 288] = unpatch_sum_ref[:, lanes].astype(BF16)
            shared_acc[first + 288 : first + SHARED] = small[:, lanes].astype(BF16)
        shared_acc[12 * SHARED :] = jnp.zeros((8 * CHUNK - 12 * SHARED, 128), BF16)
        latent = field_of(taps_acc[...], place_ref[...], -1)
        rows = [
            d_modulation[q : q + 1, tile * 128 : (tile + 1) * 128]
            for q in range(4)
            for tile in range(12)
        ]
        for r in range(ROWS):
            pack_ref[r, :CHUNK] = shared_acc[r * CHUNK : (r + 1) * CHUNK]
            pack_ref[r, CHUNK : CHUNK + 16] = activation_ref[r].astype(BF16)
            pack_ref[r, CHUNK + 16 : CHUNK + 32] = latent[r].astype(BF16)
            pack_ref[r, CHUNK + 32 : CHUNK + 48] = jnp.concatenate(
                rows[6 * r : 6 * r + 6] + [jnp.zeros((10, 128), F32)], 0
            ).astype(BF16)


def first_back(
    patches, embed, vec, weight, d_raw, d_mid, place, unpatch_sum, back_sums, own_sums, head_rows, coef,
    activation,
):
    width = embed.shape[1]
    part = weight.shape[2]
    pack = (ROWS, CHUNK + 48, 128)
    rest = (place, unpatch_sum, back_sums, own_sums, head_rows, coef, activation)
    return pl.pallas_call(
        first_kernel,
        grid=(TOKENS // PAIR,),
        in_specs=[
            lane_block(144, PAIR),
            whole(embed.shape),
            whole(vec.shape),
            whole(weight.shape),
            pl.BlockSpec((3, part, PAIR), lambda t: (0, 0, t)),
            row_block(PAIR, width),
        ]
        + [whole(value.shape) for value in rest],
        out_specs=pl.BlockSpec(pack, lambda t: (0, 0, 0)),
        out_shape=jax.ShapeDtypeStruct(pack, BF16),
        scratch_shapes=[
            pltpu.VMEM((144, TOKENS), F32),
            pltpu.VMEM((144, width), F32),
            pltpu.VMEM((8, width), F32),
            pltpu.VMEM((8 * CHUNK, 128), BF16),
        ],
        compiler_params=params(),
        cost_estimate=LIGHT,
        name="first_back",
    )(patches, embed, vec, weight, d_raw, d_mid, *rest)


def head_grad_kernel(
    at_ref, patch_ref, embed_ref, vec_ref, d_raw_ref, out_sum_ref,
    p0_ref, p1_ref, p2_ref, p3_ref, qkv_acc, turned_acc,
):
    step = pl.program_id(0)
    part = p0_ref.shape[1] // 2
    x = dot(patch_ref[...], embed_ref[...], (0, 0))
    h = (x * row_rms(x) * vec_ref[0:1]).astype(BF16)

    @pl.when(step == 0)
    def _():
        qkv_acc[...] = jnp.zeros_like(qkv_acc)

    qkv_acc[...] += dot(joined(d_raw_ref), h, (1, 0)).reshape(qkv_acc.shape)

    @pl.when(step == pl.num_programs(0) - 1)
    def _():
        for s in range(4):
            turned_acc[s] = (qkv_acc[s] if s < 3 else out_sum_ref[...]).T.astype(BF16)
        for dz, ref in enumerate((p0_ref, p1_ref, p2_ref, p3_ref)):
            z = lax.rem(at_ref[3] + dz, 4)
            for y in range(4):
                dy = lax.rem(y - at_ref[2] + 4, 4)
                first = pl.multiple_of((y * 4 + z) * part, part)
                rows = [turned_acc[s, pl.ds(first, part), :] for s in range(4)]
                for k in range(2):
                    ref[dy, k * part : (k + 1) * part] = jnp.concatenate(rows[2 * k : 2 * k + 2], 1)


def head_grads(at, patches, embed, vec, d_raw, out_sum):
    width = embed.shape[1]
    part = d_raw.shape[1]
    grads = (4, 2 * width // COLS, 2 * part)
    return pl.pallas_call(
        head_grad_kernel,
        grid_spec=pltpu.PrefetchScalarGridSpec(
            num_scalar_prefetch=1,
            grid=(TOKENS // PAIR,),
            in_specs=[
                lane_block(144, PAIR),
                whole(embed.shape),
                whole(vec.shape),
                pl.BlockSpec((3, part, PAIR), lambda t, at: (0, 0, t)),
                whole(out_sum.shape),
            ],
            out_specs=[pl.BlockSpec(grads, lambda t, at: (0, 0, 0))] * 4,
            scratch_shapes=[
                pltpu.VMEM((3, part, width), F32),
                pltpu.VMEM((4, width, part), BF16),
            ],
        ),
        out_shape=[jax.ShapeDtypeStruct(grads, BF16)] * 4,
        compiler_params=params(),
        cost_estimate=LIGHT,
        name="head_grads",
    )(at, patches, embed, vec, d_raw, out_sum)


def local(
    latent, condition, caption, cap_len, cotangent, embed_weight, modulate_weight, norm_gains,
    cross_gate, qkv_weight, text_kv_weight, out_weight, gate_up_weight, down_weight, unpatch_weight,
):
    images, _, _, channels = latent.shape
    width = embed_weight.shape[3]
    local_width = qkv_weight.shape[2]
    heads = local_width // HD
    hidden_width = down_weight.shape[0]
    taps = 9 * channels
    row_at = lax.axis_index("row")
    col_at = lax.axis_index("col")
    at = jnp.stack([row_at // 2, row_at % 2, col_at // 4, col_at % 4]).astype(jnp.int32)
    tile = latent.shape[1] * latent.shape[2] * channels

    cond_low = jax.nn.silu(condition.astype(F32)).astype(BF16)
    mod_piece = jnp.dot(cond_low, modulate_weight, preferred_element_type=F32)
    mod_columns = mod_piece.shape[1]
    mod_high = mod_piece.astype(BF16)
    mod_low = (mod_piece - mod_high.astype(F32)).astype(BF16)

    packed = jnp.concatenate(
        [latent.reshape(images, tile), cotangent.reshape(images, tile), mod_high, mod_low], axis=1
    )
    packed = jnp.pad(packed, ((0, 0), (0, 2 * local_width - packed.shape[1])))

    packed = lax.all_to_all(packed, "col", 0, 0, tiled=True)
    packed = send_all(packed, "row")

    head_pieces = (
        jnp.concatenate([qkv_weight[0], qkv_weight[1]], axis=1),
        jnp.concatenate([qkv_weight[2], out_weight.T], axis=1),
    )
    first_head = from_col(head_pieces[0], along_z)
    second_head = from_col(head_pieces[1], along_y)
    first_head = from_col(jnp.stack(first_head), along_y)
    second_head = from_col(jnp.stack(second_head), along_z)
    qkv_whole, out_rows = unpack_head(at, first_head, second_head)
    out_pieces = from_chips(out_rows)

    text_piece = jnp.concatenate([text_kv_weight[0], text_kv_weight[1]], axis=1)
    text_whole = lax.all_gather(text_piece, "col", axis=0, tiled=True)
    ffn_piece = jnp.concatenate([gate_up_weight[0], gate_up_weight[1], down_weight.T], axis=1)

    patches, cot_taps = image_taps(packed)
    mod_at = 2 * tile
    modulation = packed[:, :, mod_at : mod_at + mod_columns].astype(F32)
    modulation = modulation + packed[:, :, mod_at + mod_columns : mod_at + 2 * mod_columns].astype(F32)
    modulation = modulation.reshape(4, width)
    attn_gate = jnp.tanh(modulation[1])
    ffn_gate = jnp.tanh(modulation[3])
    vec = jnp.stack(
        [
            norm_gains[0] * (1.0 + modulation[0]),
            norm_gains[1] * attn_gate,
            norm_gains[2] * (1.0 + modulation[2]),
            norm_gains[3] * ffn_gate,
        ]
    )
    vec = jnp.pad(vec, ((0, 4), (0, 0)))
    embed = embed_weight.reshape(taps, width)
    unpatch = unpatch_weight.transpose(0, 1, 3, 2).reshape(taps, width)
    raw = qkv_project(patches, embed, vec, qkv_whole)
    ffn_whole = lax.all_gather(after(ffn_piece, text_whole, raw), "col", axis=0, tiled=True)
    raw = raw.reshape(3, heads, HD, TOKENS)
    caption_rows = caption[0]
    text_raw = dot(text_whole, caption_rows, (0, 1)).reshape(2, heads, HD, caption_rows.shape[0])
    head_gains = lax.dynamic_slice(norm_gains, (4, row_at * local_width), (3, local_width)).reshape(
        3, heads, HD, 1
    )
    head_gates = jnp.tanh(lax.dynamic_slice_in_dim(cross_gate, row_at * heads, heads))
    cap = lax.dynamic_slice_in_dim(cap_len, col_at, 1)
    table = jnp.asarray(rope_tables())
    mixed, lse = attend(raw, text_raw, head_gains, table, cap, head_gates)

    out_whole = with_other_core(lax.optimization_barrier((*out_pieces, mixed))[:4])
    mixed_whole = gather_near(mixed)
    attn, second, gate_up, hidden, ffn_own, ffn_other = forward(
        at, mixed_whole, out_whole, patches, embed, vec, ffn_whole
    )
    place = tile_places(False)
    cot_own = lax.dynamic_slice_in_dim(cot_taps, row_at * BLOCK, BLOCK, 1)
    d_ffn_own, ffn_out = own_grad(
        to_chips(sum_cores(ffn_own, ffn_other)), cot_own, unpatch, vec
    )
    d_ffn_near = from_chips(d_ffn_own)
    activation_field, unpatch_sum, own_sums = own_block(
        at, ffn_out, attn, patches, cot_taps, embed, unpatch, vec, place
    )
    d_ffn_near = lax.optimization_barrier((*d_ffn_near, activation_field))[:4]
    d_ffn, d_gate_up, d_attn, d_mid, mixed_own, mixed_other, back_sums = backward(
        at, with_other_core(d_ffn_near), ffn_whole, out_whole, gate_up, attn, patches, embed, cot_taps,
        unpatch, vec,
    )
    mixed_near = sum_cores(mixed_own, mixed_other)
    mixed_terms = to_chips(mixed_near)
    text_rows = text_kv_weight.shape[1]
    grads, out_near, out_far = weight_grads(
        after(second, *mixed_near), d_gate_up, d_ffn, hidden, mixed_whole, d_attn, text_rows
    )
    *mixed_terms, grads, out_near, out_far = lax.optimization_barrier(
        (*mixed_terms, grads, out_near, out_far)
    )
    d_mixed = sum(term.astype(F32) for term in mixed_terms).astype(BF16)
    d_mixed = d_mixed.reshape(heads, HD, TOKENS)
    out_near = sum_cores(out_near, out_far)
    out_apart = lax.ppermute(out_near[2], "row", row_pairs_to(2, 0))

    grads, dq_text, d_text_head = text_back(
        raw, text_raw, head_gains, table, lse, d_mixed, cap, head_gates, caption_rows,
        after(grads, *out_near),
    )
    dq_text, grads, out_apart, *out_near = lax.optimization_barrier(
        (dq_text, grads, out_apart, *out_near)
    )
    d_raw, d_head = attend_back(raw, head_gains, table, lse, d_mixed, dq_text)
    out_beside = [lax.ppermute(out_near[d], "row", row_pairs_to(d, 0)) for d in (1, 3)]
    d_raw, *out_terms = lax.optimization_barrier((d_raw, out_near[0], out_apart, *out_beside))
    out_sum = sum(term.astype(F32) for term in out_terms)
    one = jnp.ones_like(attn_gate)
    coef = jnp.stack(
        [
            one + modulation[0],
            attn_gate,
            one + modulation[2],
            ffn_gate,
            norm_gains[0],
            norm_gains[1] * (1.0 - attn_gate * attn_gate),
            norm_gains[2],
            norm_gains[3] * (1.0 - ffn_gate * ffn_gate),
        ]
    )
    head_part = jnp.concatenate([d_head, d_text_head[:1]]).reshape(3, local_width)
    head_sums = lax.dynamic_update_slice(
        jnp.zeros((8, width), F32), head_part, (0, row_at * local_width)
    )
    gate_part = jnp.sum(d_text_head[1], axis=(1, 2)) * (1.0 - head_gates * head_gates)
    head_sums = lax.dynamic_update_slice(head_sums, gate_part[None], (3, row_at * heads))
    d_raw = d_raw.reshape(3, local_width, TOKENS)
    row_pack = first_back(
        patches, embed, vec, qkv_whole, d_raw, d_mid, place, unpatch_sum, back_sums, own_sums,
        head_sums, coef, activation_field,
    )
    head_parts = head_grads(at, patches, embed, vec, after(d_raw, row_pack), out_sum)
    head_terms = along_col(head_parts, along_z)

    row_pack = jnp.sum(lax.all_to_all(row_pack, "row", 0, 0).astype(F32), axis=0)
    fields = row_pack[CHUNK : CHUNK + 2 * channels].T.reshape(COLS, 8, 2 * channels)
    mod_sums = row_pack[CHUNK + 2 * channels : CHUNK + 2 * channels + 6].reshape(COLS, 8, 6)
    fields = jnp.concatenate([fields, mod_sums], axis=2).astype(BF16)
    fields = jnp.pad(fields, ((0, 0), (0, 0), (0, 128 - fields.shape[2])))
    shared = row_pack[:CHUNK].astype(BF16).reshape(COLS, CHUNK // COLS, 128)
    col_pack = lax.all_to_all(jnp.concatenate([shared, fields], axis=1), "col", 0, 0)
    shared = jnp.sum(col_pack[:, : CHUNK // COLS].astype(F32), axis=0)
    shared = send_all(send_all(shared.astype(BF16), "col"), "row").reshape(-1, 128)
    shared = shared[: 12 * SHARED].reshape(12, SHARED, 128).astype(F32)
    fields = col_pack[:, CHUNK // COLS :]
    activation = fields[:, :, :channels].reshape(latent.shape)
    latent_grad = fields[:, :, channels : 2 * channels].reshape(latent.shape)
    modulate_grad = lax.dot_general(
        cond_low.astype(F32),
        fields[:, :, 2 * channels : 2 * channels + 6].reshape(images, mod_columns).astype(F32),
        (((0,), (0,)), ((), ())),
        precision=lax.Precision.HIGHEST,
        preferred_element_type=F32,
    )
    embed_grad = shared[:, :taps].transpose(1, 0, 2).reshape(embed_weight.shape)
    unpatch_grad = shared[:, taps : 2 * taps].reshape(12, 3, 3, channels, 128)
    unpatch_grad = unpatch_grad.transpose(1, 2, 0, 4, 3).reshape(unpatch_weight.shape)
    gains_grad = shared[:, 2 * taps : 2 * taps + 7].transpose(1, 0, 2).reshape(7, width)
    gate_grad = shared[0, 2 * taps + 7, :HEADS]

    part = width // COLS
    grads = lax.psum_scatter(
        grads.reshape(-1, 2 * local_width), "col", scatter_dimension=0, tiled=True
    ).astype(F32)
    text_kv_grad = jnp.stack([grads[:text_rows, :local_width], grads[:text_rows, local_width:]])
    ffn_total = jnp.concatenate(
        [grads[first : first + part] for first in range(text_rows, grads.shape[0], part)], axis=1
    )
    gate_up_grad = jnp.stack(
        [ffn_total[:, :hidden_width], ffn_total[:, hidden_width : 2 * hidden_width]]
    )
    down_grad = ffn_total[:, 2 * hidden_width :].T
    head_near = sum(term.astype(F32) for term in lax.optimization_barrier((*head_terms, col_pack))[:4])
    head_total = sum(
        term.astype(F32) for term in along_col(head_near.astype(BF16), along_y)
    )
    first, second_half = head_total[:, :local_width], head_total[:, local_width:]
    qkv_grad = jnp.stack([first[:part], second_half[:part], first[part:]])
    out_grad = second_half[part:].T
    return (
        activation, latent_grad, embed_grad, modulate_grad, gains_grad, gate_grad,
        qkv_grad, text_kv_grad, out_grad, gate_up_grad, down_grad, unpatch_grad,
    )


def solution(mesh):
    placed = (
        P(None, "row", "col", None),
        P(),
        P("col", None, None),
        P(),
        P(None, "row", "col", None),
        P(),
        P(None, ("row", "col")),
        P(),
        P(),
        P(None, "col", "row"),
        P(None, "col", "row"),
        P("row", "col"),
        P(None, "col", "row"),
        P("row", "col"),
        P(),
    )
    return jax.shard_map(
        local,
        mesh=mesh,
        in_specs=placed,
        out_specs=(
            P(None, "row", "col", None),
            P(None, "row", "col", None),
            P(),
            P(None, ("row", "col")),
            P(),
            P(),
            P(None, "col", "row"),
            P(None, "col", "row"),
            P("row", "col"),
            P(None, "col", "row"),
            P("row", "col"),
            P(),
        ),
        check_vma=False,
    )
```

```python
import math
from functools import partial

import jax
import jax.numpy as jnp
import numpy as np
from jax import lax
from jax.experimental import pallas as pl
from jax.experimental.pallas import tpu as pltpu
from jax.sharding import PartitionSpec as P

HEADS = 24
HD = 64
GRID = 32
TOKENS = GRID * GRID
EPSILON = 1e-06
ROPE_BASE = 10000.0
MASKED = -1e30
F32 = jnp.float32
BF16 = jnp.bfloat16
ROWS = 8
COLS = 16
QUERY_BLOCK = 256
BLOCK = TOKENS // ROWS
PAIR = 2 * BLOCK
MIB = 2**20
SHARED = 320
CHUNK = 512
LIGHT = pl.CostEstimate(flops=1, bytes_accessed=1, transcendentals=0)


def dot(left, right, contract):
    return lax.dot_general(
        left, right, ((contract[:1], contract[1:]), ((), ())), preferred_element_type=F32
    )


def row_pairs(dx, dc):
    return [
        (((x + dx) % 4) * 2 + (c + dc) % 2, x * 2 + c) for x in range(4) for c in range(2)
    ]


def row_pairs_to(dx, dc):
    return [(dst, src) for src, dst in row_pairs(dx, dc)]


def from_chips(piece):
    return [piece] + [lax.ppermute(piece, "row", row_pairs(d, 0)) for d in (1, 2, 3)]


def with_other_core(pieces):
    quad = jnp.stack(pieces)
    return quad, lax.ppermute(quad, "row", row_pairs(0, 1))


def gather_near(piece):
    return with_other_core(from_chips(piece))


def sum_cores(own, other):
    other = lax.ppermute(other, "row", row_pairs(0, 1))
    return [(own[d].astype(F32) + other[d].astype(F32)).astype(BF16) for d in range(4)]


def to_chips(near):
    return [near[0]] + [lax.ppermute(near[d], "row", row_pairs_to(d, 0)) for d in (1, 2, 3)]


def col_pairs_to(dy, dz):
    return [(y * 4 + z, (y + dy) % 4 * 4 + (z + dz) % 4) for y in range(4) for z in range(4)]


def col_pairs(dy, dz):
    return [(dst, src) for src, dst in col_pairs_to(dy, dz)]


def from_col(piece, step):
    return [piece] + [lax.ppermute(piece, "col", col_pairs(*step(d))) for d in (1, 2, 3)]


def along_y(d):
    return (d, 0)


def along_z(d):
    return (0, d)


def along_col(parts, step):
    return [parts[0]] + [lax.ppermute(parts[d], "col", col_pairs_to(*step(d))) for d in (1, 2, 3)]


def send_all(piece, axis):
    copies = jnp.broadcast_to(piece, (lax.axis_size(axis),) + piece.shape)
    return lax.all_to_all(copies, axis, 0, 0)


def after(value, *others):
    return lax.optimization_barrier((value,) + others)[0]


def rope_tables():
    quarter = HD // 4
    frequency = np.float32(ROPE_BASE) ** (-np.arange(quarter, dtype=np.float32) / np.float32(quarter))
    place = np.arange(TOKENS)
    row = frequency[:, None] * (place // GRID).astype(np.float32)[None, :]
    col = frequency[:, None] * (place % GRID).astype(np.float32)[None, :]
    return np.stack([np.cos(row), np.sin(row), np.cos(col), np.sin(col)]).astype(np.float32)


def turn(v, table, sign):
    a, b, c, d = (v[k * 16 : (k + 1) * 16] for k in range(4))
    cr, sr, cc, sc = table[0], table[1] * sign, table[2], table[3] * sign
    return jnp.concatenate([a * cr - b * sr, a * sr + b * cr, c * cc - d * sc, c * sc + d * cc], 0)


def column_rms(v):
    return lax.rsqrt(jnp.mean(v * v, axis=0, keepdims=True) + EPSILON)


def normed(v, gain):
    return v * column_rms(v) * gain


def column_rms_back(v, u):
    scale = column_rms(v)
    return (u - v * (jnp.mean(u * v, axis=0, keepdims=True) * scale * scale)) * scale


def whole(shape):
    zeros = (0,) * len(shape)
    return pl.BlockSpec(shape, lambda *_: zeros, pipeline_mode=pl.Buffered(1))


def held():
    return pl.BlockSpec(memory_space=pltpu.VMEM)


def lane_block(rows, lanes):
    return pl.BlockSpec((rows, lanes), lambda t, *_: (0, t))


def row_block(rows, lanes):
    return pl.BlockSpec((rows, lanes), lambda t, *_: (t, 0))


def params(mib):
    return pltpu.CompilerParams(vmem_limit_bytes=mib * MIB, dimension_semantics=("arbitrary",))


def row_of_sums(v):
    return jnp.sum(v.T, axis=0, keepdims=True)


def attend_kernel(
    cap_ref, gate_ref, raw_ref, text_ref, gain_ref, table_ref, mixed_ref, lse_ref,
    q_ref, k_ref, v_ref, tk_ref, tv_ref,
):
    step = pl.program_id(0)
    heads = raw_ref.shape[1]

    @pl.when(step == 0)
    def _():
        table = table_ref[...]
        for h in range(heads):
            q = turn(normed(raw_ref[0, h], gain_ref[0, h]), table, 1.0).astype(BF16)
            q_ref[h] = q * jnp.asarray(0.125, BF16)
            k_ref[h] = turn(normed(raw_ref[1, h], gain_ref[1, h]), table, 1.0).T.astype(BF16)
            v_ref[h] = raw_ref[2, h].astype(BF16)
            tk_ref[h] = normed(text_ref[0, h], gain_ref[2, h]).T.astype(BF16)
            tv_ref[h] = text_ref[1, h].astype(BF16)

    slots = tk_ref.shape[1]
    mask = lax.broadcasted_iota(jnp.int32, (slots, QUERY_BLOCK), 0) < cap_ref[0]
    here = pl.ds(pl.multiple_of(step * QUERY_BLOCK, QUERY_BLOCK), QUERY_BLOCK)
    outs = []
    for h in range(heads):
        qb = q_ref[h, :, here]
        e = jnp.exp(dot(k_ref[h], qb, (1, 0)))
        total = jnp.sum(e, axis=0, keepdims=True)
        own = dot(v_ref[h], e.astype(BF16), (1, 0)) / total
        te = jnp.exp(jnp.where(mask, dot(tk_ref[h], qb, (1, 0)), MASKED))
        text_total = jnp.sum(te, axis=0, keepdims=True)
        text = dot(tv_ref[h], te.astype(BF16), (1, 0)) / text_total
        outs.append(own + gate_ref[h] * text)
        lse_ref[h, 0:1] = jnp.log(total)
        lse_ref[h, 1:2] = jnp.log(text_total)
    mixed_ref[...] = jnp.concatenate(outs, 0).astype(BF16)


def attend(raw, text_raw, gains, table, cap, gates):
    heads = raw.shape[1]
    slots = text_raw.shape[3]
    return pl.pallas_call(
        attend_kernel,
        grid_spec=pltpu.PrefetchScalarGridSpec(
            num_scalar_prefetch=2,
            grid=(TOKENS // QUERY_BLOCK,),
            in_specs=[
                whole((3, heads, HD, TOKENS)),
                whole((2, heads, HD, slots)),
                whole((3, heads, HD, 1)),
                whole((4, 16, TOKENS)),
            ],
            out_specs=[
                lane_block(heads * HD, QUERY_BLOCK),
                pl.BlockSpec((heads, 8, QUERY_BLOCK), lambda t, *_: (0, 0, t)),
            ],
            scratch_shapes=[
                pltpu.VMEM((heads, HD, TOKENS), BF16),
                pltpu.VMEM((heads, TOKENS, HD), BF16),
                pltpu.VMEM((heads, HD, TOKENS), BF16),
                pltpu.VMEM((heads, slots, HD), BF16),
                pltpu.VMEM((heads, HD, slots), BF16),
            ],
        ),
        out_shape=[
            jax.ShapeDtypeStruct((heads * HD, TOKENS), BF16),
            jax.ShapeDtypeStruct((heads, 8, TOKENS), F32),
        ],
        compiler_params=params(20),
        cost_estimate=LIGHT,
        name="attend",
    )(cap, gates, raw, text_raw, gains, table)


def text_back_kernel(
    cap_ref, gate_ref, q_raw_ref, text_ref, gain_ref, table_ref, lse_ref, grad_ref, caption_ref, held_ref,
    grads_ref, dq_ref, d_gain_ref, low_ref,
):
    del held_ref
    step = pl.program_id(0)
    heads, _, slots = low_ref.shape[1:]

    @pl.when(step == 0)
    def _():
        table = table_ref[...]
        mask = lax.broadcasted_iota(jnp.int32, (slots, TOKENS), 0) < cap_ref[0]
        for h in range(heads):
            gate = gate_ref[h]
            q = turn(normed(q_raw_ref[h], gain_ref[0, h]), table, 1.0).astype(BF16)
            q = q * jnp.asarray(0.125, BF16)
            tk = normed(text_ref[0, h], gain_ref[2, h]).astype(BF16)
            tv = text_ref[1, h].astype(BF16)
            g = grad_ref[h]
            tp = jnp.exp(jnp.where(mask, dot(tk, q, (0, 0)), MASKED) - lse_ref[h, 1:2])
            tpb = tp.astype(BF16)
            low_ref[1, h] = (dot(g, tpb, (1, 1)) * gate).astype(BF16)
            gate_terms = g.astype(F32) * dot(tv, tpb, (1, 0))
            tpd = tp * dot(tv, g, (0, 0)) * gate
            dts = (tpd - tp * jnp.sum(tpd, axis=0, keepdims=True)).astype(BF16)
            dq_ref[h] = dot(tk, dts, (1, 0))
            d_tk = dot(q, dts, (1, 1))
            values = text_ref[0, h]
            low_ref[0, h] = column_rms_back(values, d_tk * gain_ref[2, h]).astype(BF16)
            d_gain_ref[h, 0:1] = row_of_sums(values * column_rms(values) * d_tk)
            d_gain_ref[h, 1:2] = row_of_sums(gate_terms)

    d_text = low_ref[...].reshape(2 * heads * HD, slots)
    rows = grads_ref.shape[1]
    for k in range(grads_ref.shape[0]):
        grads_ref[k] = dot(caption_ref[:, k * rows : (k + 1) * rows], d_text, (0, 1)).astype(BF16)


def text_back(raw, text_raw, gains, table, lse, grads, cap, gates, caption, held):
    heads = raw.shape[1]
    slots = text_raw.shape[3]
    rows = caption.shape[1] // COLS
    lanes = 2 * heads * HD
    return pl.pallas_call(
        text_back_kernel,
        grid_spec=pltpu.PrefetchScalarGridSpec(
            num_scalar_prefetch=2,
            grid=(4,),
            in_specs=[
                pl.BlockSpec((None, heads, HD, TOKENS), lambda t, *_: (0, 0, 0, 0)),
                whole(text_raw.shape),
                whole(gains.shape),
                whole(table.shape),
                whole(lse.shape),
                whole(grads.shape),
                pl.BlockSpec((slots, 4 * rows), lambda t, *_: (0, t)),
                pl.BlockSpec(memory_space=pl.ANY),
            ],
            out_specs=[
                pl.BlockSpec((4, rows, lanes), lambda t, *_: (t, 0, 0)),
                pl.BlockSpec((heads, HD, TOKENS), lambda t, *_: (0, 0, 0)),
                pl.BlockSpec((heads, 8, HD), lambda t, *_: (0, 0, 0)),
            ],
            scratch_shapes=[pltpu.VMEM((2, heads, HD, slots), BF16)],
        ),
        out_shape=[
            jax.ShapeDtypeStruct(held.shape, BF16),
            jax.ShapeDtypeStruct((heads, HD, TOKENS), F32),
            jax.ShapeDtypeStruct((heads, 8, HD), F32),
        ],
        input_output_aliases={9: 0},
        compiler_params=params(58),
        cost_estimate=LIGHT,
        name="text_back",
    )(cap, gates, raw, text_raw, gains, table, lse, grads, caption, held)


def attend_back_kernel(
    raw_ref, gain_ref, table_ref, lse_ref, grad_ref, dq_text_ref,
    d_raw_ref, d_gain_ref, dv_ref, dk_ref, dq_ref,
):
    table = table_ref[...]
    q = turn(normed(raw_ref[0], gain_ref[0]), table, 1.0).astype(BF16) * jnp.asarray(0.125, BF16)
    k = turn(normed(raw_ref[1], gain_ref[1]), table, 1.0)
    k, k_turned = k.astype(BF16), k.T.astype(BF16)
    v_turned = raw_ref[2].T.astype(BF16)
    for first in range(0, TOKENS, QUERY_BLOCK):
        here = slice(first, first + QUERY_BLOCK)
        qb = q[:, here]
        gb = grad_ref[:, here]
        p = jnp.exp(dot(k_turned, qb, (1, 0)) - lse_ref[0:1, here])
        dv = dot(gb, p.astype(BF16), (1, 1))
        pd = p * dot(v_turned, gb, (1, 0))
        ds = (pd - p * jnp.sum(pd, axis=0, keepdims=True)).astype(BF16)
        dq_ref[:, here] = dot(k, ds, (1, 0)) + dq_text_ref[:, here]
        dk = dot(qb, ds, (1, 1))
        if first == 0:
            dv_ref[...] = dv
            dk_ref[...] = dk
        else:
            dv_ref[...] += dv
            dk_ref[...] += dk

    def raw_back(which, d_turned):
        spun = turn(d_turned.astype(BF16).astype(F32), table, -1.0)
        values = raw_ref[which]
        d_raw_ref[which] = column_rms_back(values, spun * gain_ref[which]).astype(BF16)
        d_gain_ref[which : which + 1] = row_of_sums(values * column_rms(values) * spun)

    raw_back(0, dq_ref[...] * 0.125)
    raw_back(1, dk_ref[...])
    d_raw_ref[2] = dv_ref[...].astype(BF16)


def attend_back(raw, gains, table, lse, grads, dq_text):
    heads = raw.shape[1]
    return pl.pallas_call(
        attend_back_kernel,
        grid=(heads,),
        in_specs=[
            pl.BlockSpec((3, None, HD, TOKENS), lambda h: (0, h, 0, 0)),
            pl.BlockSpec((3, None, HD, 1), lambda h: (0, h, 0, 0)),
            pl.BlockSpec((4, 16, TOKENS), lambda h: (0, 0, 0)),
            pl.BlockSpec((None, 8, TOKENS), lambda h: (h, 0, 0)),
            pl.BlockSpec((None, HD, TOKENS), lambda h: (h, 0, 0)),
            pl.BlockSpec((None, HD, TOKENS), lambda h: (h, 0, 0)),
        ],
        out_specs=[
            pl.BlockSpec((3, None, HD, TOKENS), lambda h: (0, h, 0, 0)),
            pl.BlockSpec((None, 8, HD), lambda h: (h, 0, 0)),
        ],
        scratch_shapes=[pltpu.VMEM((HD, TOKENS), F32) for _ in range(3)],
        out_shape=[
            jax.ShapeDtypeStruct((3, heads, HD, TOKENS), BF16),
            jax.ShapeDtypeStruct((heads, 8, HD), F32),
        ],
        compiler_params=params(58),
        cost_estimate=LIGHT,
        name="attend_back",
    )(raw, gains, table, lse, grads, dq_text)


def tile_places(chunk_first):
    r, c, k = np.meshgrid(np.arange(ROWS), np.arange(COLS), np.arange(8), indexing="ij")
    token = r * BLOCK + (k // 2) * GRID + c * 2 + k % 2
    source = (k * ROWS + r) * COLS + c if chunk_first else (r * COLS + c) * 8 + k
    places = np.zeros((TOKENS, TOKENS), np.float32)
    places[source.ravel(), token.ravel()] = 1.0
    return jnp.asarray(places, BF16)


def grid_shift(field, di, dj):
    step = di * GRID + dj
    moved = pltpu.roll(field, (-step) % TOKENS, 1) if step else field
    place = lax.broadcasted_iota(jnp.int32, field.shape, 1)
    row = place // GRID + di
    col = place % GRID + dj
    inside = (row >= 0) & (row < GRID) & (col >= 0) & (col < GRID)
    return jnp.where(inside, moved, 0.0)


def image_kernel(packed_ref, place_ref, patch_ref, cot_ref):
    for which, sign, out_ref in ((0, 1, patch_ref), (1, -1, cot_ref)):
        lanes = slice(which * 128, (which + 1) * 128)
        tiles = jnp.concatenate([packed_ref[r, :, lanes] for r in range(ROWS)], 0)
        turned = tiles.astype(F32).T
        chunks = jnp.concatenate([turned[k * 16 : (k + 1) * 16] for k in range(8)], 1)
        image = dot(chunks.astype(BF16), place_ref[...], (1, 0))
        for a in range(3):
            for b in range(3):
                first = (a * 3 + b) * 16
                out_ref[first : first + 16] = grid_shift(
                    image, sign * (a - 1), sign * (b - 1)
                ).astype(BF16)


def image_taps(packed):
    out = jax.ShapeDtypeStruct((144, TOKENS), BF16)
    return pl.pallas_call(
        image_kernel,
        out_shape=[out, out],
        compiler_params=pltpu.CompilerParams(vmem_limit_bytes=12 * MIB),
        cost_estimate=LIGHT,
        name="image_taps",
    )(packed, tile_places(True))


def field_of(taps, place, sign):
    total = jnp.zeros((16, TOKENS), F32)
    for a in range(3):
        for b in range(3):
            first = (a * 3 + b) * 16
            total = total + grid_shift(taps[first : first + 16], sign * (a - 1), sign * (b - 1))
    tiles = dot(total.astype(BF16), place, (1, 1))
    return [tiles[:, r * BLOCK : (r + 1) * BLOCK] for r in range(ROWS)]


def row_rms(v):
    return lax.rsqrt(jnp.mean(v * v, axis=-1, keepdims=True) + EPSILON)


def row_rms_back(v, scale, u):
    return (u - v * (jnp.mean(u * v, axis=-1, keepdims=True) * scale * scale)) * scale


def unpack_kernel(at_ref, *refs):
    first_refs, second_refs, (joined_ref, out_ref, turn_ref) = refs[:4], refs[4:8], refs[8:]
    part = first_refs[0].shape[1]
    local_width = first_refs[0].shape[2] // 2
    ys = [lax.rem(at_ref[2] + d, 4) for d in range(4)]
    zs = [lax.rem(at_ref[3] + d, 4) for d in range(4)]
    for dy in range(4):
        for dz in range(4):
            rows = pl.ds(pl.multiple_of((ys[dy] * 4 + zs[dz]) * part, part), part)
            piece = first_refs[dy][dz]
            joined_ref[0, rows, :] = piece[:, :local_width]
            joined_ref[1, rows, :] = piece[:, local_width:]
            piece = second_refs[dz][dy]
            joined_ref[2, rows, :] = piece[:, :local_width]
            turn_ref[rows, :] = piece[:, local_width:]
    out_ref[...] = turn_ref[...].T


def unpack_head(at, first, second):
    _, part, lanes = first[0].shape
    width, local_width = COLS * part, lanes // 2
    return pl.pallas_call(
        unpack_kernel,
        grid_spec=pltpu.PrefetchScalarGridSpec(
            num_scalar_prefetch=1,
            grid=(1,),
            in_specs=[whole(first[0].shape)] * 8,
            out_specs=[
                pl.BlockSpec((3, width, local_width), lambda t, at: (0, 0, 0)),
                pl.BlockSpec((local_width, width), lambda t, at: (0, 0)),
            ],
            scratch_shapes=[pltpu.VMEM((width, local_width), BF16)],
        ),
        out_shape=[
            jax.ShapeDtypeStruct((3, width, local_width), BF16),
            jax.ShapeDtypeStruct((local_width, width), BF16),
        ],
        compiler_params=params(14),
        cost_estimate=LIGHT,
        name="unpack_head",
    )(at, *first, *second)


def qkv_kernel(patch_ref, embed_ref, vec_ref, weight_ref, raw_ref):
    x = dot(patch_ref[...], embed_ref[...], (0, 0))
    h = (x * row_rms(x) * vec_ref[0:1]).astype(BF16)
    for s in range(3):
        raw_ref[s] = dot(h, weight_ref[s], (1, 0)).T


def qkv_project(patches, embed, vec, weight):
    part = weight.shape[2]
    return pl.pallas_call(
        qkv_kernel,
        grid=(TOKENS // PAIR,),
        in_specs=[lane_block(144, PAIR), whole(embed.shape), whole(vec.shape), whole(weight.shape)],
        out_specs=pl.BlockSpec((3, part, PAIR), lambda t: (0, 0, t)),
        out_shape=jax.ShapeDtypeStruct((3, part, TOKENS), F32),
        compiler_params=params(16),
        cost_estimate=LIGHT,
        name="qkv_project",
    )(patches, embed, vec, weight)


def joined(ref):
    return ref[...].reshape(-1, ref.shape[2])


def halves(core, first, second):
    return jnp.where(core == 0, first, second)


def forward_kernel(
    at_ref, near_ref, far_ref, out_near_ref, out_far_ref, patch_ref, embed_ref, vec_ref, ffn_ref,
    attn_ref, second_ref, gate_up_ref, hidden_ref, own_ref, other_ref,
):
    core = at_ref[1]
    hidden_width = hidden_ref.shape[1]
    x = dot(patch_ref[...], embed_ref[...], (0, 0))
    attn = dot(joined(near_ref), joined(out_near_ref), (0, 0))
    attn = attn + dot(joined(far_ref), joined(out_far_ref), (0, 0))
    attn_ref[...] = attn.astype(BF16)
    mid = x + vec_ref[1:2] * (attn * row_rms(attn))
    second = (mid * row_rms(mid) * vec_ref[2:3]).astype(BF16)
    second_ref[...] = second
    gate_up = dot(second, ffn_ref[:, : 2 * hidden_width], (1, 0))
    gate_up_ref[...] = gate_up.astype(BF16)
    gate = gate_up[:, :hidden_width]
    hidden = (gate * jax.nn.sigmoid(gate) * gate_up[:, hidden_width:]).astype(BF16)
    hidden_ref[...] = hidden
    part = dot(hidden, ffn_ref[:, 2 * hidden_width :], (1, 1)).astype(BF16)
    own_ref[0] = halves(core, part[:BLOCK], part[BLOCK:])
    other_ref[0] = halves(core, part[BLOCK:], part[:BLOCK])


def forward(at, mixed, out_whole, patches, embed, vec, ffn):
    width = embed.shape[1]
    part = mixed[0].shape[1]
    hidden_width = ffn.shape[1] // 3
    by_chip = pl.BlockSpec((1, BLOCK, width), lambda t, at: ((t - at[0] + 4) % 4, 0, 0))
    return pl.pallas_call(
        forward_kernel,
        grid_spec=pltpu.PrefetchScalarGridSpec(
            num_scalar_prefetch=1,
            grid=(4,),
            in_specs=[
                pl.BlockSpec((4, part, PAIR), lambda t, at: (0, 0, t)),
                pl.BlockSpec((4, part, PAIR), lambda t, at: (0, 0, t)),
                held(),
                held(),
                lane_block(144, PAIR),
                whole(embed.shape),
                whole(vec.shape),
                held(),
            ],
            out_specs=[
                row_block(PAIR, width),
                row_block(PAIR, width),
                row_block(PAIR, 2 * hidden_width),
                row_block(PAIR, hidden_width),
                by_chip,
                by_chip,
            ],
        ),
        out_shape=[
            jax.ShapeDtypeStruct((TOKENS, width), BF16),
            jax.ShapeDtypeStruct((TOKENS, width), BF16),
            jax.ShapeDtypeStruct((TOKENS, 2 * hidden_width), BF16),
            jax.ShapeDtypeStruct((TOKENS, hidden_width), BF16),
            jax.ShapeDtypeStruct((4, BLOCK, width), BF16),
            jax.ShapeDtypeStruct((4, BLOCK, width), BF16),
        ],
        compiler_params=params(24),
        cost_estimate=LIGHT,
        name="forward",
    )(at, *mixed, *out_whole, patches, embed, vec, ffn)


def own_grad_kernel(p0_ref, p1_ref, p2_ref, p3_ref, cot_ref, unpatch_ref, vec_ref, d_ffn_ref, ffn_ref):
    ffn = sum(p[...].astype(F32) for p in (p0_ref, p1_ref, p2_ref, p3_ref))
    ffn_ref[...] = ffn
    d_last = dot(cot_ref[...], unpatch_ref[...], (0, 0))
    d_ffn_ref[...] = row_rms_back(ffn, row_rms(ffn), vec_ref[3:4] * d_last).astype(BF16)


def own_grad(pieces, cot_own, unpatch, vec):
    shape = (BLOCK, unpatch.shape[1])
    return pl.pallas_call(
        own_grad_kernel,
        out_shape=[jax.ShapeDtypeStruct(shape, BF16), jax.ShapeDtypeStruct(shape, F32)],
        compiler_params=pltpu.CompilerParams(vmem_limit_bytes=12 * MIB),
        cost_estimate=LIGHT,
        name="own_grad",
    )(*pieces, cot_own, unpatch, vec)


def own_kernel(
    at_ref, ffn_ref, attn_ref, patch_ref, cot_ref, embed_ref, unpatch_ref, vec_ref, place_ref,
    field_ref, unpatch_sum_ref, sums_ref, taps_ref,
):
    ffn = ffn_ref[...]
    d_last = dot(cot_ref[...], unpatch_ref[...], (0, 0))
    normed_ffn = ffn * row_rms(ffn)
    sums_ref[...] = jnp.broadcast_to(
        jnp.sum(normed_ffn * d_last, axis=0, keepdims=True), sums_ref.shape
    )
    attn = attn_ref[...].astype(F32)
    x = dot(patch_ref[...], embed_ref[...], (0, 0))
    last = (x + vec_ref[1:2] * (attn * row_rms(attn)) + vec_ref[3:4] * normed_ffn).astype(BF16)
    unpatch_sum_ref[...] = dot(cot_ref[...], last, (1, 0))
    taps_ref[...] = jnp.zeros_like(taps_ref)
    here = pl.multiple_of((2 * at_ref[0] + at_ref[1]) * BLOCK, BLOCK)
    taps_ref[:, pl.ds(here, BLOCK)] = dot(unpatch_ref[...], last, (1, 1))
    for r, tile in enumerate(field_of(taps_ref[...], place_ref[...], 1)):
        field_ref[r] = tile


def own_block(at, ffn, attn, patches, cot_taps, embed, unpatch, vec, place):
    width = embed.shape[1]
    lanes = pl.BlockSpec((144, BLOCK), lambda t, at: (0, 2 * at[0] + at[1]))
    return pl.pallas_call(
        own_kernel,
        grid_spec=pltpu.PrefetchScalarGridSpec(
            num_scalar_prefetch=1,
            grid=(1,),
            in_specs=[
                whole((BLOCK, width)),
                pl.BlockSpec((BLOCK, width), lambda t, at: (2 * at[0] + at[1], 0)),
                lanes,
                lanes,
                whole(embed.shape),
                whole(unpatch.shape),
                whole(vec.shape),
                whole(place.shape),
            ],
            out_specs=[
                pl.BlockSpec((ROWS, 16, BLOCK), lambda t, at: (0, 0, 0)),
                pl.BlockSpec((144, width), lambda t, at: (0, 0)),
                pl.BlockSpec((8, width), lambda t, at: (0, 0)),
            ],
            scratch_shapes=[pltpu.VMEM((144, TOKENS), F32)],
        ),
        out_shape=[
            jax.ShapeDtypeStruct((ROWS, 16, BLOCK), F32),
            jax.ShapeDtypeStruct((144, width), F32),
            jax.ShapeDtypeStruct((8, width), F32),
        ],
        compiler_params=params(14),
        cost_estimate=LIGHT,
        name="own_block",
    )(at, ffn, attn, patches, cot_taps, embed, unpatch, vec, place)


def backward_kernel(
    at_ref, own_ref, other_ref, ffn_ref, out_near_ref, out_far_ref, gate_up_ref, attn_ref,
    patch_ref, embed_ref, cot_ref, unpatch_ref, vec_ref,
    d_ffn_ref, d_gate_up_ref, d_attn_ref, d_mid_ref, mixed_own_ref, mixed_other_ref, sums_ref,
):
    step = pl.program_id(0)
    chip, core = at_ref[0], at_ref[1]
    hidden_width = d_gate_up_ref.shape[1] // 2
    own, other = own_ref[0], other_ref[0]
    d_ffn = jnp.concatenate([halves(core, own, other), halves(core, other, own)], 0)
    d_ffn_ref[...] = d_ffn
    d_hidden = dot(d_ffn, ffn_ref[:, 2 * hidden_width :], (1, 0))
    gate = gate_up_ref[:, :hidden_width].astype(F32)
    up = gate_up_ref[:, hidden_width:].astype(F32)
    sigma = jax.nn.sigmoid(gate)
    silu = gate * sigma
    d_gate = d_hidden * up * (sigma + silu * (1.0 - sigma))
    d_gate_up = jnp.concatenate([d_gate.astype(BF16), (d_hidden * silu).astype(BF16)], 1)
    d_gate_up_ref[...] = d_gate_up
    d_second = dot(d_gate_up, ffn_ref[:, : 2 * hidden_width], (1, 1))

    x = dot(patch_ref[...], embed_ref[...], (0, 0))
    attn = attn_ref[...].astype(F32)
    attn_scale = row_rms(attn)
    attn_normed = attn * attn_scale
    mid = x + vec_ref[1:2] * attn_normed
    mid_scale = row_rms(mid)
    mid_sum = jnp.sum(mid * mid_scale * d_second, axis=0, keepdims=True)
    d_last = dot(cot_ref[...], unpatch_ref[...], (0, 0))
    place = lax.broadcasted_iota(jnp.int32, (PAIR, 1), 0) // BLOCK
    mine = (place == core) & (step == chip)
    d_mid = row_rms_back(mid, mid_scale, vec_ref[2:3] * d_second) + jnp.where(mine, d_last, 0.0)
    d_mid_ref[...] = d_mid.astype(BF16)
    attn_sum = jnp.sum(attn_normed * d_mid, axis=0, keepdims=True)
    d_attn = row_rms_back(attn, attn_scale, vec_ref[1:2] * d_mid).astype(BF16)
    d_attn_ref[...] = d_attn
    for weight_ref, part_ref in ((out_near_ref, mixed_own_ref), (out_far_ref, mixed_other_ref)):
        part_ref[...] = dot(joined(weight_ref), d_attn, (1, 1)).astype(BF16).reshape(part_ref.shape)

    @pl.when(step == 0)
    def _():
        sums_ref[...] = jnp.zeros_like(sums_ref)

    sums_ref[0:1] += mid_sum
    sums_ref[1:2] += attn_sum


def backward(at, d_ffn, ffn, out_whole, gate_up, attn, patches, embed, cot_taps, unpatch, vec):
    width = embed.shape[1]
    part = out_whole[0].shape[1]
    hidden_width = ffn.shape[1] // 3
    by_chip = pl.BlockSpec((1, BLOCK, width), lambda t, at: ((t - at[0] + 4) % 4, 0, 0))
    parts = pl.BlockSpec((4, part, PAIR), lambda t, at: (0, 0, t))
    return pl.pallas_call(
        backward_kernel,
        grid_spec=pltpu.PrefetchScalarGridSpec(
            num_scalar_prefetch=1,
            grid=(4,),
            in_specs=[
                by_chip,
                by_chip,
                held(),
                held(),
                held(),
                row_block(PAIR, 2 * hidden_width),
                row_block(PAIR, width),
                lane_block(144, PAIR),
                whole(embed.shape),
                lane_block(144, PAIR),
                whole(unpatch.shape),
                whole(vec.shape),
            ],
            out_specs=[
                row_block(PAIR, width),
                row_block(PAIR, 2 * hidden_width),
                row_block(PAIR, width),
                row_block(PAIR, width),
                parts,
                parts,
                pl.BlockSpec((8, width), lambda t, at: (0, 0)),
            ],
        ),
        out_shape=[
            jax.ShapeDtypeStruct((TOKENS, width), BF16),
            jax.ShapeDtypeStruct((TOKENS, 2 * hidden_width), BF16),
            jax.ShapeDtypeStruct((TOKENS, width), BF16),
            jax.ShapeDtypeStruct((TOKENS, width), BF16),
            jax.ShapeDtypeStruct((4, part, TOKENS), BF16),
            jax.ShapeDtypeStruct((4, part, TOKENS), BF16),
            jax.ShapeDtypeStruct((8, width), F32),
        ],
        compiler_params=params(32),
        cost_estimate=LIGHT,
        name="backward",
    )(at, *d_ffn, ffn, *out_whole, gate_up, attn, patches, embed, cot_taps, unpatch, vec)


def weight_kernel(
    second_ref, d_gate_up_ref, d_ffn_ref, hidden_ref, near_ref, far_ref, d_attn_ref,
    grads_ref, out_near_ref, out_far_ref,
):
    step = pl.program_id(0)
    chunk, _, lanes = grads_ref.shape[0] // 4, *grads_ref.shape[1:]
    part = second_ref.shape[1] // chunk
    rows = jnp.concatenate(
        [
            dot(second_ref[...], d_gate_up_ref[...], (0, 0)).astype(BF16),
            dot(d_ffn_ref[...], hidden_ref[...], (0, 0)).astype(BF16),
        ],
        1,
    )
    groups = rows.shape[1] // lanes
    first = grads_ref.shape[1] - groups * part
    for c in range(chunk):
        for g in range(groups):
            grads_ref[step * chunk + c, first + g * part : first + (g + 1) * part] = rows[
                c * part : (c + 1) * part, g * lanes : (g + 1) * lanes
            ]
    out_near_ref[0] = dot(near_ref[0], d_attn_ref[...], (1, 0)).astype(BF16)
    out_far_ref[0] = dot(far_ref[0], d_attn_ref[...], (1, 0)).astype(BF16)


def weight_grads(second, d_gate_up, d_ffn, hidden, mixed, d_attn, text_rows):
    width = second.shape[1]
    heads_width = mixed[0].shape[1]
    lanes = 2 * heads_width
    grads = (COLS, text_rows + width // COLS * 3 * hidden.shape[1] // lanes, lanes)
    pieces = pl.BlockSpec((1, heads_width, TOKENS), lambda t: (t, 0, 0))
    out_piece = pl.BlockSpec((1, heads_width, width), lambda t: (t, 0, 0))
    out_shape = jax.ShapeDtypeStruct((4, heads_width, width), BF16)
    return pl.pallas_call(
        weight_kernel,
        grid=(4,),
        in_specs=[
            lane_block(TOKENS, width // 4),
            whole(d_gate_up.shape),
            lane_block(TOKENS, width // 4),
            whole(hidden.shape),
            pieces,
            pieces,
            whole(d_attn.shape),
        ],
        out_specs=[pl.BlockSpec(grads, lambda t: (0, 0, 0)), out_piece, out_piece],
        out_shape=[jax.ShapeDtypeStruct(grads, BF16), out_shape, out_shape],
        compiler_params=params(40),
        cost_estimate=LIGHT,
        name="weight_grads",
    )(second, d_gate_up, d_ffn, hidden, *mixed, d_attn)


def first_kernel(
    at_ref, gate_ref, patch_ref, embed_ref, vec_ref, weight_ref, d_raw_ref, d_mid_ref, place_ref,
    unpatch_sum_ref, back_sums_ref, own_sums_ref, head_ref, text_head_ref, gains_ref, mod_ref, activation_ref,
    pack_ref, taps_acc, embed_acc, first_acc, shared_acc,
):
    step = pl.program_id(0)
    last = pl.num_programs(0) - 1
    x = dot(patch_ref[...], embed_ref[...], (0, 0))
    scale = row_rms(x)
    x_normed = x * scale
    d_h = dot(d_raw_ref[0], weight_ref[0], (0, 1))
    for s in (1, 2):
        d_h = d_h + dot(d_raw_ref[s], weight_ref[s], (0, 1))

    @pl.when(step == 0)
    def _():
        embed_acc[...] = jnp.zeros_like(embed_acc)
        first_acc[...] = jnp.zeros_like(first_acc)

    first_acc[0:1] += jnp.sum(x_normed * d_h, axis=0, keepdims=True)
    d_first = (d_mid_ref[...].astype(F32) + row_rms_back(x, scale, vec_ref[0:1] * d_h)).astype(BF16)
    embed_acc[...] += dot(patch_ref[...], d_first, (1, 0))
    here = pl.ds(pl.multiple_of(step * PAIR, PAIR), PAIR)
    taps_acc[:, here] = dot(embed_ref[...], d_first, (1, 1))

    @pl.when(step == last)
    def _():
        terms = jnp.concatenate(
            [first_acc[0:1], back_sums_ref[1:2], back_sums_ref[0:1], own_sums_ref[0:1]], 0
        )
        gates = [jnp.tanh(mod_ref[k : k + 1]) for k in (1, 3)]
        into = jnp.concatenate(
            [1.0 + mod_ref[0:1], gates[0], 1.0 + mod_ref[2:3], gates[1]], 0
        )
        d_gains = terms * into
        slope = jnp.concatenate(
            [jnp.ones_like(gates[0]), 1.0 - gates[0] * gates[0]] * 1
            + [jnp.ones_like(gates[0]), 1.0 - gates[1] * gates[1]],
            0,
        )
        d_modulation = terms * gains_ref[0:4] * slope
        heads = head_ref.shape[0]
        width = d_gains.shape[1]
        rows = [head_ref[h] for h in range(heads)], [text_head_ref[h] for h in range(heads)]
        own = jnp.concatenate(
            [
                jnp.concatenate([r[0:2] for r in rows[0]], 1),
                jnp.concatenate([r[0:1] for r in rows[1]], 1),
                jnp.zeros((5, heads * HD), F32),
            ],
            0,
        )
        own = jnp.concatenate([own, jnp.zeros((8, width - heads * HD), F32)], 1)
        row_at = 2 * at_ref[0] + at_ref[1]
        own = pltpu.roll(own, row_at * (heads * HD), 1)
        lane = lax.broadcasted_iota(jnp.int32, (1, width), 1)
        gate_row = jnp.zeros((1, width), F32)
        for h in range(heads):
            total = jnp.sum(rows[1][h][1:2], axis=1, keepdims=True)
            total = total * (1.0 - gate_ref[h] * gate_ref[h])
            gate_row = gate_row + jnp.where(lane == row_at * heads + h, total, 0.0)
        small = jnp.concatenate(
            [d_gains, own[0:3], gate_row, jnp.zeros((24, width), F32)], 0
        )
        for tile in range(12):
            lanes = slice(tile * 128, (tile + 1) * 128)
            first = tile * SHARED
            shared_acc[first : first + 144] = embed_acc[:, lanes].astype(BF16)
            shared_acc[first + 144 : first + 288] = unpatch_sum_ref[:, lanes].astype(BF16)
            shared_acc[first + 288 : first + SHARED] = small[:, lanes].astype(BF16)
        shared_acc[12 * SHARED :] = jnp.zeros((8 * CHUNK - 12 * SHARED, 128), BF16)
        latent = field_of(taps_acc[...], place_ref[...], -1)
        rows = [
            d_modulation[q : q + 1, tile * 128 : (tile + 1) * 128]
            for q in range(4)
            for tile in range(12)
        ]
        for r in range(ROWS):
            pack_ref[r, :CHUNK] = shared_acc[r * CHUNK : (r + 1) * CHUNK]
            pack_ref[r, CHUNK : CHUNK + 16] = activation_ref[r].astype(BF16)
            pack_ref[r, CHUNK + 16 : CHUNK + 32] = latent[r].astype(BF16)
            pack_ref[r, CHUNK + 32 : CHUNK + 48] = jnp.concatenate(
                rows[6 * r : 6 * r + 6] + [jnp.zeros((10, 128), F32)], 0
            ).astype(BF16)


def first_back(
    at, gates, patches, embed, vec, weight, d_raw, d_mid, place, unpatch_sum, back_sums, own_sums, head,
    text_head, gains, modulation, activation,
):
    width = embed.shape[1]
    part = weight.shape[2]
    pack = (ROWS, CHUNK + 48, 128)
    rest = (place, unpatch_sum, back_sums, own_sums, head, text_head, gains, modulation, activation)
    return pl.pallas_call(
        first_kernel,
        grid_spec=pltpu.PrefetchScalarGridSpec(
            num_scalar_prefetch=2,
            grid=(TOKENS // PAIR,),
            in_specs=[
                lane_block(144, PAIR),
                whole(embed.shape),
                whole(vec.shape),
                whole(weight.shape),
                pl.BlockSpec((3, part, PAIR), lambda t, *_: (0, 0, t)),
                row_block(PAIR, width),
            ]
            + [whole(value.shape) for value in rest],
            out_specs=pl.BlockSpec(pack, lambda t, *_: (0, 0, 0)),
            scratch_shapes=[
                pltpu.VMEM((144, TOKENS), F32),
                pltpu.VMEM((144, width), F32),
                pltpu.VMEM((8, width), F32),
                pltpu.VMEM((8 * CHUNK, 128), BF16),
            ],
        ),
        out_shape=jax.ShapeDtypeStruct(pack, BF16),
        compiler_params=params(58),
        cost_estimate=LIGHT,
        name="first_back",
    )(at, gates, patches, embed, vec, weight, d_raw, d_mid, *rest)


def head_grad_kernel(
    at_ref, patch_ref, embed_ref, vec_ref, d_raw_ref, out_sum_ref,
    p0_ref, p1_ref, p2_ref, p3_ref, qkv_acc, turned_acc,
):
    step = pl.program_id(0)
    part = p0_ref.shape[1] // 2
    x = dot(patch_ref[...], embed_ref[...], (0, 0))
    h = (x * row_rms(x) * vec_ref[0:1]).astype(BF16)

    @pl.when(step == 0)
    def _():
        qkv_acc[...] = jnp.zeros_like(qkv_acc)

    qkv_acc[...] += dot(joined(d_raw_ref), h, (1, 0)).reshape(qkv_acc.shape)

    @pl.when(step == pl.num_programs(0) - 1)
    def _():
        for s in range(4):
            turned_acc[s] = (qkv_acc[s] if s < 3 else out_sum_ref[...]).T.astype(BF16)
        for dz, ref in enumerate((p0_ref, p1_ref, p2_ref, p3_ref)):
            z = lax.rem(at_ref[3] + dz, 4)
            for y in range(4):
                dy = lax.rem(y - at_ref[2] + 4, 4)
                first = pl.multiple_of((y * 4 + z) * part, part)
                rows = [turned_acc[s, pl.ds(first, part), :] for s in range(4)]
                for k in range(2):
                    ref[dy, k * part : (k + 1) * part] = jnp.concatenate(rows[2 * k : 2 * k + 2], 1)


def head_grads(at, patches, embed, vec, d_raw, out_sum):
    width = embed.shape[1]
    part = d_raw.shape[1]
    grads = (4, 2 * width // COLS, 2 * part)
    return pl.pallas_call(
        head_grad_kernel,
        grid_spec=pltpu.PrefetchScalarGridSpec(
            num_scalar_prefetch=1,
            grid=(TOKENS // PAIR,),
            in_specs=[
                lane_block(144, PAIR),
                whole(embed.shape),
                whole(vec.shape),
                pl.BlockSpec((3, part, PAIR), lambda t, at: (0, 0, t)),
                whole(out_sum.shape),
            ],
            out_specs=[pl.BlockSpec(grads, lambda t, at: (0, 0, 0))] * 4,
            scratch_shapes=[
                pltpu.VMEM((3, part, width), F32),
                pltpu.VMEM((4, width, part), BF16),
            ],
        ),
        out_shape=[jax.ShapeDtypeStruct(grads, BF16)] * 4,
        compiler_params=params(58),
        cost_estimate=LIGHT,
        name="head_grads",
    )(at, patches, embed, vec, d_raw, out_sum)


def local(
    latent, condition, caption, cap_len, cotangent, embed_weight, modulate_weight, norm_gains,
    cross_gate, qkv_weight, text_kv_weight, out_weight, gate_up_weight, down_weight, unpatch_weight,
):
    images, _, _, channels = latent.shape
    width = embed_weight.shape[3]
    local_width = qkv_weight.shape[2]
    heads = local_width // HD
    hidden_width = down_weight.shape[0]
    taps = 9 * channels
    row_at = lax.axis_index("row")
    col_at = lax.axis_index("col")
    at = jnp.stack([row_at // 2, row_at % 2, col_at // 4, col_at % 4]).astype(jnp.int32)
    tile = latent.shape[1] * latent.shape[2] * channels

    cond_low = jax.nn.silu(condition.astype(F32)).astype(BF16)
    mod_piece = jnp.dot(cond_low, modulate_weight, preferred_element_type=F32)
    mod_columns = mod_piece.shape[1]
    mod_high = mod_piece.astype(BF16)
    mod_low = (mod_piece - mod_high.astype(F32)).astype(BF16)

    packed = jnp.concatenate(
        [latent.reshape(images, tile), cotangent.reshape(images, tile), mod_high, mod_low], axis=1
    )
    packed = jnp.pad(packed, ((0, 0), (0, 2 * local_width - packed.shape[1])))

    packed = lax.all_to_all(packed, "col", 0, 0, tiled=True)
    packed = send_all(packed, "row")

    head_pieces = (
        jnp.concatenate([qkv_weight[0], qkv_weight[1]], axis=1),
        jnp.concatenate([qkv_weight[2], out_weight.T], axis=1),
    )
    first_head = from_col(head_pieces[0], along_z)
    second_head = from_col(head_pieces[1], along_y)
    first_head = from_col(jnp.stack(first_head), along_y)
    second_head = from_col(jnp.stack(second_head), along_z)
    qkv_whole, out_rows = unpack_head(at, first_head, second_head)
    out_far = lax.ppermute(out_rows, "row", row_pairs(2, 0))

    text_piece = jnp.concatenate([text_kv_weight[0], text_kv_weight[1]], axis=1)
    text_whole = lax.all_gather(text_piece, "col", axis=0, tiled=True)
    ffn_piece = jnp.concatenate([gate_up_weight[0], gate_up_weight[1], down_weight.T], axis=1)

    patches, cot_taps = image_taps(packed)
    mod_at = 2 * tile
    modulation = packed[:, :, mod_at : mod_at + mod_columns].astype(F32)
    modulation = modulation + packed[:, :, mod_at + mod_columns : mod_at + 2 * mod_columns].astype(F32)
    modulation = modulation.reshape(4, width)
    attn_gate = jnp.tanh(modulation[1])
    ffn_gate = jnp.tanh(modulation[3])
    vec = jnp.stack(
        [
            norm_gains[0] * (1.0 + modulation[0]),
            norm_gains[1] * attn_gate,
            norm_gains[2] * (1.0 + modulation[2]),
            norm_gains[3] * ffn_gate,
        ]
    )
    vec = jnp.pad(vec, ((0, 4), (0, 0)))
    embed = embed_weight.reshape(taps, width)
    unpatch = unpatch_weight.transpose(0, 1, 3, 2).reshape(taps, width)
    raw = qkv_project(patches, embed, vec, qkv_whole)
    raw = raw.reshape(3, heads, HD, TOKENS)
    text_whole, out_far = lax.optimization_barrier((text_whole, out_far, raw))[:2]
    ffn_whole = lax.all_gather(after(ffn_piece, text_whole), "col", axis=0, tiled=True)
    out_rows = after(out_rows, out_far)
    out_beside = [lax.ppermute(out_rows, "row", row_pairs(d, 0)) for d in (1, 3)]
    caption_rows = caption[0]
    text_raw = dot(text_whole, caption_rows, (0, 1)).reshape(2, heads, HD, caption_rows.shape[0])
    head_gains = lax.dynamic_slice(norm_gains, (4, row_at * local_width), (3, local_width)).reshape(
        3, heads, HD, 1
    )
    head_gates = jnp.tanh(lax.dynamic_slice_in_dim(cross_gate, row_at * heads, heads))
    cap = lax.dynamic_slice_in_dim(cap_len, col_at, 1)
    table = jnp.asarray(rope_tables())
    mixed, lse = attend(raw, text_raw, head_gains, table, cap, head_gates)

    mixed_pieces = from_chips(mixed)
    *mixed_pieces, next_out, last_out = lax.optimization_barrier((*mixed_pieces, *out_beside))
    mixed_whole = with_other_core(mixed_pieces)
    out_whole = with_other_core([out_rows, next_out, out_far, last_out])
    attn, second, gate_up, hidden, ffn_own, ffn_other = forward(
        at, mixed_whole, out_whole, patches, embed, vec, ffn_whole
    )
    place = tile_places(False)
    cot_own = lax.dynamic_slice_in_dim(cot_taps, row_at * BLOCK, BLOCK, 1)
    d_ffn_own, ffn_out = own_grad(
        to_chips(sum_cores(ffn_own, ffn_other)), cot_own, unpatch, vec
    )
    d_ffn_near = from_chips(d_ffn_own)
    activation_field, unpatch_sum, own_sums = own_block(
        at, ffn_out, attn, patches, cot_taps, embed, unpatch, vec, place
    )
    d_ffn_near = lax.optimization_barrier((*d_ffn_near, activation_field))[:4]
    d_ffn, d_gate_up, d_attn, d_mid, mixed_own, mixed_other, back_sums = backward(
        at, with_other_core(d_ffn_near), ffn_whole, out_whole, gate_up, attn, patches, embed, cot_taps,
        unpatch, vec,
    )
    mixed_near = sum_cores(mixed_own, mixed_other)
    mixed_terms = to_chips(mixed_near)
    text_rows = text_kv_weight.shape[1]
    grads, out_near, out_far = weight_grads(
        after(second, *mixed_near), d_gate_up, d_ffn, hidden, mixed_whole, d_attn, text_rows
    )
    *mixed_terms, grads, out_near, out_far = lax.optimization_barrier(
        (*mixed_terms, grads, out_near, out_far)
    )
    d_mixed = sum(term.astype(F32) for term in mixed_terms).astype(BF16)
    d_mixed = d_mixed.reshape(heads, HD, TOKENS)
    out_near = sum_cores(out_near, out_far)
    out_apart = lax.ppermute(out_near[2], "row", row_pairs_to(2, 0))

    grads, dq_text, d_text_head = text_back(
        raw, text_raw, head_gains, table, lse, d_mixed, cap, head_gates, caption_rows,
        after(grads, *out_near),
    )
    dq_text, grads, out_apart, *out_near = lax.optimization_barrier(
        (dq_text, grads, out_apart, *out_near)
    )
    d_raw, d_head = attend_back(raw, head_gains, table, lse, d_mixed, dq_text)
    out_beside = [lax.ppermute(out_near[d], "row", row_pairs_to(d, 0)) for d in (1, 3)]
    d_raw, *out_terms = lax.optimization_barrier((d_raw, out_near[0], out_apart, *out_beside))
    out_sum = sum(term.astype(F32) for term in out_terms)
    d_raw = d_raw.reshape(3, local_width, TOKENS)
    row_pack = first_back(
        at, head_gates, patches, embed, vec, qkv_whole, d_raw, d_mid, place, unpatch_sum, back_sums,
        own_sums, d_head, d_text_head, norm_gains, modulation, activation_field,
    )
    head_parts = head_grads(at, patches, embed, vec, after(d_raw, row_pack), out_sum)
    row_pack = jnp.sum(lax.all_to_all(row_pack, "row", 0, 0).astype(F32), axis=0)
    fields = row_pack[CHUNK : CHUNK + 2 * channels].T.reshape(COLS, 8, 2 * channels)
    mod_sums = row_pack[CHUNK + 2 * channels : CHUNK + 2 * channels + 6].reshape(COLS, 8, 6)
    fields = jnp.concatenate([fields, mod_sums], axis=2).astype(BF16)
    fields = jnp.pad(fields, ((0, 0), (0, 0), (0, 128 - fields.shape[2])))
    shared = row_pack[:CHUNK].astype(BF16).reshape(COLS, CHUNK // COLS, 128)
    col_pack = lax.all_to_all(jnp.concatenate([shared, fields], axis=1), "col", 0, 0)
    shared = jnp.sum(col_pack[:, : CHUNK // COLS].astype(F32), axis=0)
    shared = send_all(send_all(shared.astype(BF16), "col"), "row").reshape(-1, 128)
    shared = shared[: 12 * SHARED].reshape(12, SHARED, 128).astype(F32)
    fields = col_pack[:, CHUNK // COLS :]
    activation = fields[:, :, :channels].reshape(latent.shape)
    latent_grad = fields[:, :, channels : 2 * channels].reshape(latent.shape)
    modulate_grad = lax.dot_general(
        cond_low.astype(F32),
        fields[:, :, 2 * channels : 2 * channels + 6].reshape(images, mod_columns).astype(F32),
        (((0,), (0,)), ((), ())),
        precision=lax.Precision.HIGHEST,
        preferred_element_type=F32,
    )
    embed_grad = shared[:, :taps].transpose(1, 0, 2).reshape(embed_weight.shape)
    unpatch_grad = shared[:, taps : 2 * taps].reshape(12, 3, 3, channels, 128)
    unpatch_grad = unpatch_grad.transpose(1, 2, 0, 4, 3).reshape(unpatch_weight.shape)
    gains_grad = shared[:, 2 * taps : 2 * taps + 7].transpose(1, 0, 2).reshape(7, width)
    gate_grad = shared[0, 2 * taps + 7, :HEADS]

    part = width // COLS
    grads = lax.psum_scatter(
        grads.reshape(-1, 2 * local_width), "col", scatter_dimension=0, tiled=True
    ).astype(F32)
    text_kv_grad = jnp.stack([grads[:text_rows, :local_width], grads[:text_rows, local_width:]])
    ffn_total = jnp.concatenate(
        [grads[first : first + part] for first in range(text_rows, grads.shape[0], part)], axis=1
    )
    gate_up_grad = jnp.stack(
        [ffn_total[:, :hidden_width], ffn_total[:, hidden_width : 2 * hidden_width]]
    )
    down_grad = ffn_total[:, 2 * hidden_width :].T
    head_parts = lax.optimization_barrier((*head_parts, col_pack))[:4]
    head_near = sum(term.astype(F32) for term in along_col(head_parts, along_z))
    head_total = sum(
        term.astype(F32) for term in along_col(head_near.astype(BF16), along_y)
    )
    first, second_half = head_total[:, :local_width], head_total[:, local_width:]
    qkv_grad = jnp.stack([first[:part], second_half[:part], first[part:]])
    out_grad = second_half[part:].T
    return (
        activation, latent_grad, embed_grad, modulate_grad, gains_grad, gate_grad,
        qkv_grad, text_kv_grad, out_grad, gate_up_grad, down_grad, unpatch_grad,
    )


def solution(mesh):
    placed = (
        P(None, "row", "col", None),
        P(),
        P("col", None, None),
        P(),
        P(None, "row", "col", None),
        P(),
        P(None, ("row", "col")),
        P(),
        P(),
        P(None, "col", "row"),
        P(None, "col", "row"),
        P("row", "col"),
        P(None, "col", "row"),
        P("row", "col"),
        P(),
    )
    return jax.shard_map(
        local,
        mesh=mesh,
        in_specs=placed,
        out_specs=(
            P(None, "row", "col", None),
            P(None, "row", "col", None),
            P(),
            P(None, ("row", "col")),
            P(),
            P(),
            P(None, "col", "row"),
            P(None, "col", "row"),
            P("row", "col"),
            P(None, "col", "row"),
            P("row", "col"),
            P(),
        ),
        check_vma=False,
    )
```

```python
import math
from functools import partial

import jax
import jax.numpy as jnp
import numpy as np
from jax import lax
from jax.experimental import pallas as pl
from jax.experimental.pallas import tpu as pltpu
from jax.sharding import PartitionSpec as P

HEADS = 24
HD = 64
GRID = 32
TOKENS = GRID * GRID
EPSILON = 1e-06
ROPE_BASE = 10000.0
MASKED = -1e30
F32 = jnp.float32
BF16 = jnp.bfloat16
ROWS = 8
COLS = 16
QUERY_BLOCK = 256
BLOCK = TOKENS // ROWS
PAIR = 2 * BLOCK
MIB = 2**20
SHARED = 320
CHUNK = 512
LIGHT = pl.CostEstimate(flops=1, bytes_accessed=1, transcendentals=0)


def dot(left, right, contract):
    return lax.dot_general(
        left, right, ((contract[:1], contract[1:]), ((), ())), preferred_element_type=F32
    )


def row_pairs(dx, dc):
    return [
        (((x + dx) % 4) * 2 + (c + dc) % 2, x * 2 + c) for x in range(4) for c in range(2)
    ]


def row_pairs_to(dx, dc):
    return [(dst, src) for src, dst in row_pairs(dx, dc)]


def from_chips(piece):
    return [piece] + [lax.ppermute(piece, "row", row_pairs(d, 0)) for d in (1, 2, 3)]


def with_other_core(pieces):
    quad = jnp.stack(pieces)
    return quad, lax.ppermute(quad, "row", row_pairs(0, 1))


def gather_near(piece):
    return with_other_core(from_chips(piece))


def sum_cores(own, other):
    other = lax.ppermute(other, "row", row_pairs(0, 1))
    return [(own[d].astype(F32) + other[d].astype(F32)).astype(BF16) for d in range(4)]


def to_chips(near):
    return [near[0]] + [lax.ppermute(near[d], "row", row_pairs_to(d, 0)) for d in (1, 2, 3)]


def col_pairs_to(dy, dz):
    return [(y * 4 + z, (y + dy) % 4 * 4 + (z + dz) % 4) for y in range(4) for z in range(4)]


def col_pairs(dy, dz):
    return [(dst, src) for src, dst in col_pairs_to(dy, dz)]


def from_col(piece, step):
    return [piece] + [lax.ppermute(piece, "col", col_pairs(*step(d))) for d in (1, 2, 3)]


def along_y(d):
    return (d, 0)


def along_z(d):
    return (0, d)


def along_col(parts, step):
    return [parts[0]] + [lax.ppermute(parts[d], "col", col_pairs_to(*step(d))) for d in (1, 2, 3)]


def send_all(piece, axis):
    copies = jnp.broadcast_to(piece, (lax.axis_size(axis),) + piece.shape)
    return lax.all_to_all(copies, axis, 0, 0)


def after(value, *others):
    return lax.optimization_barrier((value,) + others)[0]


def rope_tables():
    quarter = HD // 4
    frequency = np.float32(ROPE_BASE) ** (-np.arange(quarter, dtype=np.float32) / np.float32(quarter))
    place = np.arange(TOKENS)
    row = frequency[:, None] * (place // GRID).astype(np.float32)[None, :]
    col = frequency[:, None] * (place % GRID).astype(np.float32)[None, :]
    return np.stack([np.cos(row), np.sin(row), np.cos(col), np.sin(col)]).astype(np.float32)


def turn(v, table, sign):
    a, b, c, d = (v[k * 16 : (k + 1) * 16] for k in range(4))
    cr, sr, cc, sc = table[0], table[1] * sign, table[2], table[3] * sign
    return jnp.concatenate([a * cr - b * sr, a * sr + b * cr, c * cc - d * sc, c * sc + d * cc], 0)


def column_rms(v):
    return lax.rsqrt(jnp.mean(v * v, axis=0, keepdims=True) + EPSILON)


def normed(v, gain):
    return v * column_rms(v) * gain


def column_rms_back(v, u):
    scale = column_rms(v)
    return (u - v * (jnp.mean(u * v, axis=0, keepdims=True) * scale * scale)) * scale


def whole(shape):
    zeros = (0,) * len(shape)
    return pl.BlockSpec(shape, lambda *_: zeros, pipeline_mode=pl.Buffered(1))


def held():
    return pl.BlockSpec(memory_space=pltpu.VMEM)


def lane_block(rows, lanes):
    return pl.BlockSpec((rows, lanes), lambda t, *_: (0, t))


def row_block(rows, lanes):
    return pl.BlockSpec((rows, lanes), lambda t, *_: (t, 0))


def params(mib):
    return pltpu.CompilerParams(vmem_limit_bytes=mib * MIB, dimension_semantics=("arbitrary",))


def row_of_sums(v):
    return jnp.sum(v.T, axis=0, keepdims=True)


def attend_kernel(
    cap_ref, gate_ref, raw_ref, text_ref, gain_ref, table_ref, mixed_ref, lse_ref,
    q_ref, k_ref, v_ref, tk_ref, tv_ref,
):
    step = pl.program_id(0)
    heads = raw_ref.shape[1]

    @pl.when(step == 0)
    def _():
        table = table_ref[...]
        for h in range(heads):
            q = turn(normed(raw_ref[0, h], gain_ref[0, h]), table, 1.0).astype(BF16)
            q_ref[h] = q * jnp.asarray(0.125, BF16)
            k_ref[h] = turn(normed(raw_ref[1, h], gain_ref[1, h]), table, 1.0).T.astype(BF16)
            v_ref[h] = raw_ref[2, h].astype(BF16)
            tk_ref[h] = normed(text_ref[0, h], gain_ref[2, h]).T.astype(BF16)
            tv_ref[h] = text_ref[1, h].astype(BF16)

    slots = tk_ref.shape[1]
    mask = lax.broadcasted_iota(jnp.int32, (slots, QUERY_BLOCK), 0) < cap_ref[0]
    here = pl.ds(pl.multiple_of(step * QUERY_BLOCK, QUERY_BLOCK), QUERY_BLOCK)
    outs = []
    for h in range(heads):
        qb = q_ref[h, :, here]
        e = jnp.exp(dot(k_ref[h], qb, (1, 0)))
        total = jnp.sum(e, axis=0, keepdims=True)
        own = dot(v_ref[h], e.astype(BF16), (1, 0)) / total
        te = jnp.exp(jnp.where(mask, dot(tk_ref[h], qb, (1, 0)), MASKED))
        text_total = jnp.sum(te, axis=0, keepdims=True)
        text = dot(tv_ref[h], te.astype(BF16), (1, 0)) / text_total
        outs.append(own + gate_ref[h] * text)
        lse_ref[h, 0:1] = jnp.log(total)
        lse_ref[h, 1:2] = jnp.log(text_total)
    mixed_ref[...] = jnp.concatenate(outs, 0).astype(BF16)


def attend(raw, text_raw, gains, table, cap, gates):
    heads = raw.shape[1]
    slots = text_raw.shape[3]
    return pl.pallas_call(
        attend_kernel,
        grid_spec=pltpu.PrefetchScalarGridSpec(
            num_scalar_prefetch=2,
            grid=(TOKENS // QUERY_BLOCK,),
            in_specs=[
                whole((3, heads, HD, TOKENS)),
                whole((2, heads, HD, slots)),
                whole((3, heads, HD, 1)),
                whole((4, 16, TOKENS)),
            ],
            out_specs=[
                lane_block(heads * HD, QUERY_BLOCK),
                pl.BlockSpec((heads, 8, QUERY_BLOCK), lambda t, *_: (0, 0, t)),
            ],
            scratch_shapes=[
                pltpu.VMEM((heads, HD, TOKENS), BF16),
                pltpu.VMEM((heads, TOKENS, HD), BF16),
                pltpu.VMEM((heads, HD, TOKENS), BF16),
                pltpu.VMEM((heads, slots, HD), BF16),
                pltpu.VMEM((heads, HD, slots), BF16),
            ],
        ),
        out_shape=[
            jax.ShapeDtypeStruct((heads * HD, TOKENS), BF16),
            jax.ShapeDtypeStruct((heads, 8, TOKENS), F32),
        ],
        compiler_params=params(20),
        cost_estimate=LIGHT,
        name="attend",
    )(cap, gates, raw, text_raw, gains, table)


def text_back_kernel(
    cap_ref, gate_ref, q_raw_ref, text_ref, gain_ref, table_ref, lse_ref, grad_ref, caption_ref, held_ref,
    grads_ref, dq_ref, d_gain_ref, low_ref,
):
    del held_ref
    step = pl.program_id(0)
    heads, _, slots = low_ref.shape[1:]

    @pl.when(step == 0)
    def _():
        table = table_ref[...]
        mask = lax.broadcasted_iota(jnp.int32, (slots, TOKENS), 0) < cap_ref[0]
        for h in range(heads):
            gate = gate_ref[h]
            q = turn(normed(q_raw_ref[h], gain_ref[0, h]), table, 1.0).astype(BF16)
            q = q * jnp.asarray(0.125, BF16)
            tk = normed(text_ref[0, h], gain_ref[2, h]).astype(BF16)
            tv = text_ref[1, h].astype(BF16)
            g = grad_ref[h]
            tp = jnp.exp(jnp.where(mask, dot(tk, q, (0, 0)), MASKED) - lse_ref[h, 1:2])
            tpb = tp.astype(BF16)
            low_ref[1, h] = (dot(g, tpb, (1, 1)) * gate).astype(BF16)
            gate_terms = g.astype(F32) * dot(tv, tpb, (1, 0))
            tpd = tp * dot(tv, g, (0, 0)) * gate
            dts = (tpd - tp * jnp.sum(tpd, axis=0, keepdims=True)).astype(BF16)
            dq_ref[h] = dot(tk, dts, (1, 0))
            d_tk = dot(q, dts, (1, 1))
            values = text_ref[0, h]
            low_ref[0, h] = column_rms_back(values, d_tk * gain_ref[2, h]).astype(BF16)
            d_gain_ref[h, 0:1] = row_of_sums(values * column_rms(values) * d_tk)
            d_gain_ref[h, 1:2] = row_of_sums(gate_terms)

    d_text = low_ref[...].reshape(2 * heads * HD, slots)
    rows = grads_ref.shape[1]
    for k in range(grads_ref.shape[0]):
        grads_ref[k] = dot(caption_ref[:, k * rows : (k + 1) * rows], d_text, (0, 1)).astype(BF16)


def text_back(raw, text_raw, gains, table, lse, grads, cap, gates, caption, held):
    heads = raw.shape[1]
    slots = text_raw.shape[3]
    rows = caption.shape[1] // COLS
    lanes = 2 * heads * HD
    return pl.pallas_call(
        text_back_kernel,
        grid_spec=pltpu.PrefetchScalarGridSpec(
            num_scalar_prefetch=2,
            grid=(4,),
            in_specs=[
                pl.BlockSpec((None, heads, HD, TOKENS), lambda t, *_: (0, 0, 0, 0)),
                whole(text_raw.shape),
                whole(gains.shape),
                whole(table.shape),
                whole(lse.shape),
                whole(grads.shape),
                pl.BlockSpec((slots, 4 * rows), lambda t, *_: (0, t)),
                pl.BlockSpec(memory_space=pl.ANY),
            ],
            out_specs=[
                pl.BlockSpec((4, rows, lanes), lambda t, *_: (t, 0, 0)),
                pl.BlockSpec((heads, HD, TOKENS), lambda t, *_: (0, 0, 0)),
                pl.BlockSpec((heads, 8, HD), lambda t, *_: (0, 0, 0)),
            ],
            scratch_shapes=[pltpu.VMEM((2, heads, HD, slots), BF16)],
        ),
        out_shape=[
            jax.ShapeDtypeStruct(held.shape, BF16),
            jax.ShapeDtypeStruct((heads, HD, TOKENS), F32),
            jax.ShapeDtypeStruct((heads, 8, HD), F32),
        ],
        input_output_aliases={9: 0},
        compiler_params=params(58),
        cost_estimate=LIGHT,
        name="text_back",
    )(cap, gates, raw, text_raw, gains, table, lse, grads, caption, held)


def attend_back_kernel(
    raw_ref, gain_ref, table_ref, lse_ref, grad_ref, dq_text_ref,
    d_raw_ref, d_gain_ref, dv_ref, dk_ref, dq_ref,
):
    table = table_ref[...]
    q = turn(normed(raw_ref[0], gain_ref[0]), table, 1.0).astype(BF16) * jnp.asarray(0.125, BF16)
    k = turn(normed(raw_ref[1], gain_ref[1]), table, 1.0)
    k, k_turned = k.astype(BF16), k.T.astype(BF16)
    v_turned = raw_ref[2].T.astype(BF16)
    for first in range(0, TOKENS, QUERY_BLOCK):
        here = slice(first, first + QUERY_BLOCK)
        qb = q[:, here]
        gb = grad_ref[:, here]
        p = jnp.exp(dot(k_turned, qb, (1, 0)) - lse_ref[0:1, here])
        dv = dot(gb, p.astype(BF16), (1, 1))
        pd = p * dot(v_turned, gb, (1, 0))
        ds = (pd - p * jnp.sum(pd, axis=0, keepdims=True)).astype(BF16)
        dq_ref[:, here] = dot(k, ds, (1, 0)) + dq_text_ref[:, here]
        dk = dot(qb, ds, (1, 1))
        if first == 0:
            dv_ref[...] = dv
            dk_ref[...] = dk
        else:
            dv_ref[...] += dv
            dk_ref[...] += dk

    def raw_back(which, d_turned):
        spun = turn(d_turned.astype(BF16).astype(F32), table, -1.0)
        values = raw_ref[which]
        d_raw_ref[which] = column_rms_back(values, spun * gain_ref[which]).astype(BF16)
        d_gain_ref[which : which + 1] = row_of_sums(values * column_rms(values) * spun)

    raw_back(0, dq_ref[...] * 0.125)
    raw_back(1, dk_ref[...])
    d_raw_ref[2] = dv_ref[...].astype(BF16)


def attend_back(raw, gains, table, lse, grads, dq_text):
    heads = raw.shape[1]
    return pl.pallas_call(
        attend_back_kernel,
        grid=(heads,),
        in_specs=[
            pl.BlockSpec((3, None, HD, TOKENS), lambda h: (0, h, 0, 0)),
            pl.BlockSpec((3, None, HD, 1), lambda h: (0, h, 0, 0)),
            pl.BlockSpec((4, 16, TOKENS), lambda h: (0, 0, 0)),
            pl.BlockSpec((None, 8, TOKENS), lambda h: (h, 0, 0)),
            pl.BlockSpec((None, HD, TOKENS), lambda h: (h, 0, 0)),
            pl.BlockSpec((None, HD, TOKENS), lambda h: (h, 0, 0)),
        ],
        out_specs=[
            pl.BlockSpec((3, None, HD, TOKENS), lambda h: (0, h, 0, 0)),
            pl.BlockSpec((None, 8, HD), lambda h: (h, 0, 0)),
        ],
        scratch_shapes=[pltpu.VMEM((HD, TOKENS), F32) for _ in range(3)],
        out_shape=[
            jax.ShapeDtypeStruct((3, heads, HD, TOKENS), BF16),
            jax.ShapeDtypeStruct((heads, 8, HD), F32),
        ],
        compiler_params=params(58),
        cost_estimate=LIGHT,
        name="attend_back",
    )(raw, gains, table, lse, grads, dq_text)


def tile_places(chunk_first):
    r, c, k = np.meshgrid(np.arange(ROWS), np.arange(COLS), np.arange(8), indexing="ij")
    token = r * BLOCK + (k // 2) * GRID + c * 2 + k % 2
    source = (k * ROWS + r) * COLS + c if chunk_first else (r * COLS + c) * 8 + k
    places = np.zeros((TOKENS, TOKENS), np.float32)
    places[source.ravel(), token.ravel()] = 1.0
    return jnp.asarray(places, BF16)


def grid_shift(field, di, dj):
    step = di * GRID + dj
    moved = pltpu.roll(field, (-step) % TOKENS, 1) if step else field
    place = lax.broadcasted_iota(jnp.int32, field.shape, 1)
    row = place // GRID + di
    col = place % GRID + dj
    inside = (row >= 0) & (row < GRID) & (col >= 0) & (col < GRID)
    return jnp.where(inside, moved, 0.0)


def image_kernel(packed_ref, place_ref, patch_ref, cot_ref):
    for which, sign, out_ref in ((0, 1, patch_ref), (1, -1, cot_ref)):
        lanes = slice(which * 128, (which + 1) * 128)
        tiles = jnp.concatenate([packed_ref[r, :, lanes] for r in range(ROWS)], 0)
        turned = tiles.astype(F32).T
        chunks = jnp.concatenate([turned[k * 16 : (k + 1) * 16] for k in range(8)], 1)
        image = dot(chunks.astype(BF16), place_ref[...], (1, 0))
        for a in range(3):
            for b in range(3):
                first = (a * 3 + b) * 16
                out_ref[first : first + 16] = grid_shift(
                    image, sign * (a - 1), sign * (b - 1)
                ).astype(BF16)


def image_taps(packed):
    out = jax.ShapeDtypeStruct((144, TOKENS), BF16)
    return pl.pallas_call(
        image_kernel,
        out_shape=[out, out],
        compiler_params=pltpu.CompilerParams(vmem_limit_bytes=12 * MIB),
        cost_estimate=LIGHT,
        name="image_taps",
    )(packed, tile_places(True))


def field_of(taps, place, sign):
    total = jnp.zeros((16, TOKENS), F32)
    for a in range(3):
        for b in range(3):
            first = (a * 3 + b) * 16
            total = total + grid_shift(taps[first : first + 16], sign * (a - 1), sign * (b - 1))
    tiles = dot(total.astype(BF16), place, (1, 1))
    return [tiles[:, r * BLOCK : (r + 1) * BLOCK] for r in range(ROWS)]


def row_rms(v):
    return lax.rsqrt(jnp.mean(v * v, axis=-1, keepdims=True) + EPSILON)


def row_rms_back(v, scale, u):
    return (u - v * (jnp.mean(u * v, axis=-1, keepdims=True) * scale * scale)) * scale


def unpack_kernel(at_ref, *refs):
    first_refs, second_refs, (joined_ref, out_ref, turn_ref) = refs[:4], refs[4:8], refs[8:]
    part = first_refs[0].shape[1]
    local_width = first_refs[0].shape[2] // 2
    ys = [lax.rem(at_ref[2] + d, 4) for d in range(4)]
    zs = [lax.rem(at_ref[3] + d, 4) for d in range(4)]
    for dy in range(4):
        for dz in range(4):
            rows = pl.ds(pl.multiple_of((ys[dy] * 4 + zs[dz]) * part, part), part)
            piece = first_refs[dy][dz]
            joined_ref[0, rows, :] = piece[:, :local_width]
            joined_ref[1, rows, :] = piece[:, local_width:]
            piece = second_refs[dz][dy]
            joined_ref[2, rows, :] = piece[:, :local_width]
            turn_ref[rows, :] = piece[:, local_width:]
    out_ref[...] = turn_ref[...].T


def unpack_head(at, first, second):
    _, part, lanes = first[0].shape
    width, local_width = COLS * part, lanes // 2
    return pl.pallas_call(
        unpack_kernel,
        grid_spec=pltpu.PrefetchScalarGridSpec(
            num_scalar_prefetch=1,
            grid=(1,),
            in_specs=[whole(first[0].shape)] * 8,
            out_specs=[
                pl.BlockSpec((3, width, local_width), lambda t, at: (0, 0, 0)),
                pl.BlockSpec((local_width, width), lambda t, at: (0, 0)),
            ],
            scratch_shapes=[pltpu.VMEM((width, local_width), BF16)],
        ),
        out_shape=[
            jax.ShapeDtypeStruct((3, width, local_width), BF16),
            jax.ShapeDtypeStruct((local_width, width), BF16),
        ],
        compiler_params=params(14),
        cost_estimate=LIGHT,
        name="unpack_head",
    )(at, *first, *second)


def qkv_kernel(patch_ref, embed_ref, vec_ref, weight_ref, raw_ref):
    x = dot(patch_ref[...], embed_ref[...], (0, 0))
    h = (x * row_rms(x) * vec_ref[0:1]).astype(BF16)
    for s in range(3):
        raw_ref[s] = dot(h, weight_ref[s], (1, 0)).T


def qkv_project(patches, embed, vec, weight):
    part = weight.shape[2]
    return pl.pallas_call(
        qkv_kernel,
        grid=(TOKENS // PAIR,),
        in_specs=[lane_block(144, PAIR), whole(embed.shape), whole(vec.shape), whole(weight.shape)],
        out_specs=pl.BlockSpec((3, part, PAIR), lambda t: (0, 0, t)),
        out_shape=jax.ShapeDtypeStruct((3, part, TOKENS), F32),
        compiler_params=params(16),
        cost_estimate=LIGHT,
        name="qkv_project",
    )(patches, embed, vec, weight)


def joined(ref):
    return ref[...].reshape(-1, ref.shape[2])


def halves(core, first, second):
    return jnp.where(core == 0, first, second)


def forward_kernel(
    at_ref, near_ref, far_ref, out_near_ref, out_far_ref, patch_ref, embed_ref, vec_ref, ffn_ref,
    attn_ref, second_ref, gate_up_ref, hidden_ref, own_ref, other_ref,
):
    core = at_ref[1]
    hidden_width = hidden_ref.shape[1]
    x = dot(patch_ref[...], embed_ref[...], (0, 0))
    attn = dot(joined(near_ref), joined(out_near_ref), (0, 0))
    attn = attn + dot(joined(far_ref), joined(out_far_ref), (0, 0))
    attn_ref[...] = attn.astype(BF16)
    mid = x + vec_ref[1:2] * (attn * row_rms(attn))
    second = (mid * row_rms(mid) * vec_ref[2:3]).astype(BF16)
    second_ref[...] = second
    gate_up = dot(second, ffn_ref[:, : 2 * hidden_width], (1, 0))
    gate_up_ref[...] = gate_up.astype(BF16)
    gate = gate_up[:, :hidden_width]
    hidden = (gate * jax.nn.sigmoid(gate) * gate_up[:, hidden_width:]).astype(BF16)
    hidden_ref[...] = hidden
    part = dot(hidden, ffn_ref[:, 2 * hidden_width :], (1, 1)).astype(BF16)
    own_ref[0] = halves(core, part[:BLOCK], part[BLOCK:])
    other_ref[0] = halves(core, part[BLOCK:], part[:BLOCK])


def forward(at, mixed, out_whole, patches, embed, vec, ffn):
    width = embed.shape[1]
    part = mixed[0].shape[1]
    hidden_width = ffn.shape[1] // 3
    by_chip = pl.BlockSpec((1, BLOCK, width), lambda t, at: ((t - at[0] + 4) % 4, 0, 0))
    return pl.pallas_call(
        forward_kernel,
        grid_spec=pltpu.PrefetchScalarGridSpec(
            num_scalar_prefetch=1,
            grid=(4,),
            in_specs=[
                pl.BlockSpec((4, part, PAIR), lambda t, at: (0, 0, t)),
                pl.BlockSpec((4, part, PAIR), lambda t, at: (0, 0, t)),
                held(),
                held(),
                lane_block(144, PAIR),
                whole(embed.shape),
                whole(vec.shape),
                held(),
            ],
            out_specs=[
                row_block(PAIR, width),
                row_block(PAIR, width),
                row_block(PAIR, 2 * hidden_width),
                row_block(PAIR, hidden_width),
                by_chip,
                by_chip,
            ],
        ),
        out_shape=[
            jax.ShapeDtypeStruct((TOKENS, width), BF16),
            jax.ShapeDtypeStruct((TOKENS, width), BF16),
            jax.ShapeDtypeStruct((TOKENS, 2 * hidden_width), BF16),
            jax.ShapeDtypeStruct((TOKENS, hidden_width), BF16),
            jax.ShapeDtypeStruct((4, BLOCK, width), BF16),
            jax.ShapeDtypeStruct((4, BLOCK, width), BF16),
        ],
        compiler_params=params(24),
        cost_estimate=LIGHT,
        name="forward",
    )(at, *mixed, *out_whole, patches, embed, vec, ffn)


def own_grad_kernel(p0_ref, p1_ref, p2_ref, p3_ref, cot_ref, unpatch_ref, vec_ref, d_ffn_ref, ffn_ref):
    ffn = sum(p[...].astype(F32) for p in (p0_ref, p1_ref, p2_ref, p3_ref))
    ffn_ref[...] = ffn
    d_last = dot(cot_ref[...], unpatch_ref[...], (0, 0))
    d_ffn_ref[...] = row_rms_back(ffn, row_rms(ffn), vec_ref[3:4] * d_last).astype(BF16)


def own_grad(pieces, cot_own, unpatch, vec):
    shape = (BLOCK, unpatch.shape[1])
    return pl.pallas_call(
        own_grad_kernel,
        out_shape=[jax.ShapeDtypeStruct(shape, BF16), jax.ShapeDtypeStruct(shape, F32)],
        compiler_params=pltpu.CompilerParams(vmem_limit_bytes=12 * MIB),
        cost_estimate=LIGHT,
        name="own_grad",
    )(*pieces, cot_own, unpatch, vec)


def own_kernel(
    at_ref, ffn_ref, attn_ref, patch_ref, cot_ref, embed_ref, unpatch_ref, vec_ref, place_ref,
    field_ref, unpatch_sum_ref, sums_ref, taps_ref,
):
    ffn = ffn_ref[...]
    d_last = dot(cot_ref[...], unpatch_ref[...], (0, 0))
    normed_ffn = ffn * row_rms(ffn)
    sums_ref[...] = jnp.broadcast_to(
        jnp.sum(normed_ffn * d_last, axis=0, keepdims=True), sums_ref.shape
    )
    attn = attn_ref[...].astype(F32)
    x = dot(patch_ref[...], embed_ref[...], (0, 0))
    last = (x + vec_ref[1:2] * (attn * row_rms(attn)) + vec_ref[3:4] * normed_ffn).astype(BF16)
    unpatch_sum_ref[...] = dot(cot_ref[...], last, (1, 0))
    taps_ref[...] = jnp.zeros_like(taps_ref)
    here = pl.multiple_of((2 * at_ref[0] + at_ref[1]) * BLOCK, BLOCK)
    taps_ref[:, pl.ds(here, BLOCK)] = dot(unpatch_ref[...], last, (1, 1))
    for r, tile in enumerate(field_of(taps_ref[...], place_ref[...], 1)):
        field_ref[r] = tile


def own_block(at, ffn, attn, patches, cot_taps, embed, unpatch, vec, place):
    width = embed.shape[1]
    lanes = pl.BlockSpec((144, BLOCK), lambda t, at: (0, 2 * at[0] + at[1]))
    return pl.pallas_call(
        own_kernel,
        grid_spec=pltpu.PrefetchScalarGridSpec(
            num_scalar_prefetch=1,
            grid=(1,),
            in_specs=[
                whole((BLOCK, width)),
                pl.BlockSpec((BLOCK, width), lambda t, at: (2 * at[0] + at[1], 0)),
                lanes,
                lanes,
                whole(embed.shape),
                whole(unpatch.shape),
                whole(vec.shape),
                whole(place.shape),
            ],
            out_specs=[
                pl.BlockSpec((ROWS, 16, BLOCK), lambda t, at: (0, 0, 0)),
                pl.BlockSpec((144, width), lambda t, at: (0, 0)),
                pl.BlockSpec((8, width), lambda t, at: (0, 0)),
            ],
            scratch_shapes=[pltpu.VMEM((144, TOKENS), F32)],
        ),
        out_shape=[
            jax.ShapeDtypeStruct((ROWS, 16, BLOCK), F32),
            jax.ShapeDtypeStruct((144, width), F32),
            jax.ShapeDtypeStruct((8, width), F32),
        ],
        compiler_params=params(14),
        cost_estimate=LIGHT,
        name="own_block",
    )(at, ffn, attn, patches, cot_taps, embed, unpatch, vec, place)


def backward_kernel(
    at_ref, own_ref, other_ref, ffn_ref, out_near_ref, out_far_ref, gate_up_ref, attn_ref,
    patch_ref, embed_ref, cot_ref, unpatch_ref, vec_ref,
    d_ffn_ref, d_gate_up_ref, d_attn_ref, d_mid_ref, mixed_own_ref, mixed_other_ref, sums_ref,
):
    step = pl.program_id(0)
    chip, core = at_ref[0], at_ref[1]
    hidden_width = d_gate_up_ref.shape[1] // 2
    own, other = own_ref[0], other_ref[0]
    d_ffn = jnp.concatenate([halves(core, own, other), halves(core, other, own)], 0)
    d_ffn_ref[...] = d_ffn
    d_hidden = dot(d_ffn, ffn_ref[:, 2 * hidden_width :], (1, 0))
    gate = gate_up_ref[:, :hidden_width].astype(F32)
    up = gate_up_ref[:, hidden_width:].astype(F32)
    sigma = jax.nn.sigmoid(gate)
    silu = gate * sigma
    d_gate = d_hidden * up * (sigma + silu * (1.0 - sigma))
    d_gate_up = jnp.concatenate([d_gate.astype(BF16), (d_hidden * silu).astype(BF16)], 1)
    d_gate_up_ref[...] = d_gate_up
    d_second = dot(d_gate_up, ffn_ref[:, : 2 * hidden_width], (1, 1))

    x = dot(patch_ref[...], embed_ref[...], (0, 0))
    attn = attn_ref[...].astype(F32)
    attn_scale = row_rms(attn)
    attn_normed = attn * attn_scale
    mid = x + vec_ref[1:2] * attn_normed
    mid_scale = row_rms(mid)
    mid_sum = jnp.sum(mid * mid_scale * d_second, axis=0, keepdims=True)
    d_last = dot(cot_ref[...], unpatch_ref[...], (0, 0))
    place = lax.broadcasted_iota(jnp.int32, (PAIR, 1), 0) // BLOCK
    mine = (place == core) & (step == chip)
    d_mid = row_rms_back(mid, mid_scale, vec_ref[2:3] * d_second) + jnp.where(mine, d_last, 0.0)
    d_mid_ref[...] = d_mid.astype(BF16)
    attn_sum = jnp.sum(attn_normed * d_mid, axis=0, keepdims=True)
    d_attn = row_rms_back(attn, attn_scale, vec_ref[1:2] * d_mid).astype(BF16)
    d_attn_ref[...] = d_attn
    for weight_ref, part_ref in ((out_near_ref, mixed_own_ref), (out_far_ref, mixed_other_ref)):
        part_ref[...] = dot(joined(weight_ref), d_attn, (1, 1)).astype(BF16).reshape(part_ref.shape)

    @pl.when(step == 0)
    def _():
        sums_ref[...] = jnp.zeros_like(sums_ref)

    sums_ref[0:1] += mid_sum
    sums_ref[1:2] += attn_sum


def backward(at, d_ffn, ffn, out_whole, gate_up, attn, patches, embed, cot_taps, unpatch, vec):
    width = embed.shape[1]
    part = out_whole[0].shape[1]
    hidden_width = ffn.shape[1] // 3
    by_chip = pl.BlockSpec((1, BLOCK, width), lambda t, at: ((t - at[0] + 4) % 4, 0, 0))
    parts = pl.BlockSpec((4, part, PAIR), lambda t, at: (0, 0, t))
    return pl.pallas_call(
        backward_kernel,
        grid_spec=pltpu.PrefetchScalarGridSpec(
            num_scalar_prefetch=1,
            grid=(4,),
            in_specs=[
                by_chip,
                by_chip,
                held(),
                held(),
                held(),
                row_block(PAIR, 2 * hidden_width),
                row_block(PAIR, width),
                lane_block(144, PAIR),
                whole(embed.shape),
                lane_block(144, PAIR),
                whole(unpatch.shape),
                whole(vec.shape),
            ],
            out_specs=[
                row_block(PAIR, width),
                row_block(PAIR, 2 * hidden_width),
                row_block(PAIR, width),
                row_block(PAIR, width),
                parts,
                parts,
                pl.BlockSpec((8, width), lambda t, at: (0, 0)),
            ],
        ),
        out_shape=[
            jax.ShapeDtypeStruct((TOKENS, width), BF16),
            jax.ShapeDtypeStruct((TOKENS, 2 * hidden_width), BF16),
            jax.ShapeDtypeStruct((TOKENS, width), BF16),
            jax.ShapeDtypeStruct((TOKENS, width), BF16),
            jax.ShapeDtypeStruct((4, part, TOKENS), BF16),
            jax.ShapeDtypeStruct((4, part, TOKENS), BF16),
            jax.ShapeDtypeStruct((8, width), F32),
        ],
        compiler_params=params(32),
        cost_estimate=LIGHT,
        name="backward",
    )(at, *d_ffn, ffn, *out_whole, gate_up, attn, patches, embed, cot_taps, unpatch, vec)


def weight_kernel(
    second_ref, d_gate_up_ref, d_ffn_ref, hidden_ref, near_ref, far_ref, d_attn_ref,
    grads_ref, out_near_ref, out_far_ref,
):
    step = pl.program_id(0)
    chunk, _, lanes = grads_ref.shape[0] // 4, *grads_ref.shape[1:]
    part = second_ref.shape[1] // chunk
    rows = jnp.concatenate(
        [
            dot(second_ref[...], d_gate_up_ref[...], (0, 0)).astype(BF16),
            dot(d_ffn_ref[...], hidden_ref[...], (0, 0)).astype(BF16),
        ],
        1,
    )
    groups = rows.shape[1] // lanes
    first = grads_ref.shape[1] - groups * part
    for c in range(chunk):
        for g in range(groups):
            grads_ref[step * chunk + c, first + g * part : first + (g + 1) * part] = rows[
                c * part : (c + 1) * part, g * lanes : (g + 1) * lanes
            ]
    out_near_ref[0] = dot(near_ref[0], d_attn_ref[...], (1, 0)).astype(BF16)
    out_far_ref[0] = dot(far_ref[0], d_attn_ref[...], (1, 0)).astype(BF16)


def weight_grads(second, d_gate_up, d_ffn, hidden, mixed, d_attn, text_rows):
    width = second.shape[1]
    heads_width = mixed[0].shape[1]
    lanes = 2 * heads_width
    grads = (COLS, text_rows + width // COLS * 3 * hidden.shape[1] // lanes, lanes)
    pieces = pl.BlockSpec((1, heads_width, TOKENS), lambda t: (t, 0, 0))
    out_piece = pl.BlockSpec((1, heads_width, width), lambda t: (t, 0, 0))
    out_shape = jax.ShapeDtypeStruct((4, heads_width, width), BF16)
    return pl.pallas_call(
        weight_kernel,
        grid=(4,),
        in_specs=[
            lane_block(TOKENS, width // 4),
            whole(d_gate_up.shape),
            lane_block(TOKENS, width // 4),
            whole(hidden.shape),
            pieces,
            pieces,
            whole(d_attn.shape),
        ],
        out_specs=[pl.BlockSpec(grads, lambda t: (0, 0, 0)), out_piece, out_piece],
        out_shape=[jax.ShapeDtypeStruct(grads, BF16), out_shape, out_shape],
        compiler_params=params(40),
        cost_estimate=LIGHT,
        name="weight_grads",
    )(second, d_gate_up, d_ffn, hidden, *mixed, d_attn)


def first_kernel(
    at_ref, gate_ref, patch_ref, embed_ref, vec_ref, weight_ref, d_raw_ref, d_mid_ref, place_ref,
    unpatch_sum_ref, back_sums_ref, own_sums_ref, head_ref, text_head_ref, gains_ref, mod_ref, activation_ref,
    own_pack_ref, other_pack_ref, taps_acc, embed_acc, first_acc, shared_acc,
):
    step = pl.program_id(0)
    last = pl.num_programs(0) - 1
    x = dot(patch_ref[...], embed_ref[...], (0, 0))
    scale = row_rms(x)
    x_normed = x * scale
    d_h = dot(d_raw_ref[0], weight_ref[0], (0, 1))
    for s in (1, 2):
        d_h = d_h + dot(d_raw_ref[s], weight_ref[s], (0, 1))

    @pl.when(step == 0)
    def _():
        embed_acc[...] = jnp.zeros_like(embed_acc)
        first_acc[...] = jnp.zeros_like(first_acc)

    first_acc[0:1] += jnp.sum(x_normed * d_h, axis=0, keepdims=True)
    d_first = (d_mid_ref[...].astype(F32) + row_rms_back(x, scale, vec_ref[0:1] * d_h)).astype(BF16)
    embed_acc[...] += dot(patch_ref[...], d_first, (1, 0))
    here = pl.ds(pl.multiple_of(step * PAIR, PAIR), PAIR)
    taps_acc[:, here] = dot(embed_ref[...], d_first, (1, 1))

    @pl.when(step == last)
    def _():
        terms = jnp.concatenate(
            [first_acc[0:1], back_sums_ref[1:2], back_sums_ref[0:1], own_sums_ref[0:1]], 0
        )
        gates = [jnp.tanh(mod_ref[k : k + 1]) for k in (1, 3)]
        into = jnp.concatenate(
            [1.0 + mod_ref[0:1], gates[0], 1.0 + mod_ref[2:3], gates[1]], 0
        )
        d_gains = terms * into
        slope = jnp.concatenate(
            [jnp.ones_like(gates[0]), 1.0 - gates[0] * gates[0]] * 1
            + [jnp.ones_like(gates[0]), 1.0 - gates[1] * gates[1]],
            0,
        )
        d_modulation = terms * gains_ref[0:4] * slope
        heads = head_ref.shape[0]
        width = d_gains.shape[1]
        rows = [head_ref[h] for h in range(heads)], [text_head_ref[h] for h in range(heads)]
        own = jnp.concatenate(
            [
                jnp.concatenate([r[0:2] for r in rows[0]], 1),
                jnp.concatenate([r[0:1] for r in rows[1]], 1),
                jnp.zeros((5, heads * HD), F32),
            ],
            0,
        )
        own = jnp.concatenate([own, jnp.zeros((8, width - heads * HD), F32)], 1)
        row_at = 2 * at_ref[0] + at_ref[1]
        own = pltpu.roll(own, row_at * (heads * HD), 1)
        lane = lax.broadcasted_iota(jnp.int32, (1, width), 1)
        gate_row = jnp.zeros((1, width), F32)
        for h in range(heads):
            total = jnp.sum(rows[1][h][1:2], axis=1, keepdims=True)
            total = total * (1.0 - gate_ref[h] * gate_ref[h])
            gate_row = gate_row + jnp.where(lane == row_at * heads + h, total, 0.0)
        small = jnp.concatenate(
            [d_gains, own[0:3], gate_row, jnp.zeros((24, width), F32)], 0
        )
        for tile in range(12):
            lanes = slice(tile * 128, (tile + 1) * 128)
            first = tile * SHARED
            shared_acc[first : first + 144] = embed_acc[:, lanes].astype(BF16)
            shared_acc[first + 144 : first + 288] = unpatch_sum_ref[:, lanes].astype(BF16)
            shared_acc[first + 288 : first + SHARED] = small[:, lanes].astype(BF16)
        shared_acc[12 * SHARED :] = jnp.zeros((8 * CHUNK - 12 * SHARED, 128), BF16)
        latent = field_of(taps_acc[...], place_ref[...], -1)
        rows = [
            d_modulation[q : q + 1, tile * 128 : (tile + 1) * 128]
            for q in range(4)
            for tile in range(12)
        ]
        for r in range(ROWS):
            ahead = lax.rem(r // 2 - at_ref[0] + 4, 4)
            mods = jnp.concatenate(rows[6 * r : 6 * r + 6] + [jnp.zeros((10, 128), F32)], 0)
            piece = jnp.concatenate(
                [
                    shared_acc[r * CHUNK : (r + 1) * CHUNK],
                    activation_ref[r].astype(BF16),
                    latent[r].astype(BF16),
                    mods.astype(BF16),
                ],
                0,
            )

            @pl.when(at_ref[1] == r % 2)
            def _():
                own_pack_ref[ahead] = piece

            @pl.when(at_ref[1] != r % 2)
            def _():
                other_pack_ref[ahead] = piece


def first_back(
    at, gates, patches, embed, vec, weight, d_raw, d_mid, place, unpatch_sum, back_sums, own_sums, head,
    text_head, gains, modulation, activation,
):
    width = embed.shape[1]
    part = weight.shape[2]
    pack = (4, CHUNK + 48, 128)
    rest = (place, unpatch_sum, back_sums, own_sums, head, text_head, gains, modulation, activation)
    return pl.pallas_call(
        first_kernel,
        grid_spec=pltpu.PrefetchScalarGridSpec(
            num_scalar_prefetch=2,
            grid=(TOKENS // PAIR,),
            in_specs=[
                lane_block(144, PAIR),
                whole(embed.shape),
                whole(vec.shape),
                whole(weight.shape),
                pl.BlockSpec((3, part, PAIR), lambda t, *_: (0, 0, t)),
                row_block(PAIR, width),
            ]
            + [whole(value.shape) for value in rest],
            out_specs=[pl.BlockSpec(pack, lambda t, *_: (0, 0, 0))] * 2,
            scratch_shapes=[
                pltpu.VMEM((144, TOKENS), F32),
                pltpu.VMEM((144, width), F32),
                pltpu.VMEM((8, width), F32),
                pltpu.VMEM((8 * CHUNK, 128), BF16),
            ],
        ),
        out_shape=[jax.ShapeDtypeStruct(pack, BF16)] * 2,
        compiler_params=params(58),
        cost_estimate=LIGHT,
        name="first_back",
    )(at, gates, patches, embed, vec, weight, d_raw, d_mid, *rest)


def head_grad_kernel(
    at_ref, patch_ref, embed_ref, vec_ref, d_raw_ref, out_sum_ref,
    p0_ref, p1_ref, p2_ref, p3_ref, qkv_acc, turned_acc,
):
    step = pl.program_id(0)
    part = p0_ref.shape[1] // 2
    x = dot(patch_ref[...], embed_ref[...], (0, 0))
    h = (x * row_rms(x) * vec_ref[0:1]).astype(BF16)

    @pl.when(step == 0)
    def _():
        qkv_acc[...] = jnp.zeros_like(qkv_acc)

    qkv_acc[...] += dot(joined(d_raw_ref), h, (1, 0)).reshape(qkv_acc.shape)

    @pl.when(step == pl.num_programs(0) - 1)
    def _():
        for s in range(4):
            turned_acc[s] = (qkv_acc[s] if s < 3 else out_sum_ref[...]).T.astype(BF16)
        for dz, ref in enumerate((p0_ref, p1_ref, p2_ref, p3_ref)):
            z = lax.rem(at_ref[3] + dz, 4)
            for y in range(4):
                dy = lax.rem(y - at_ref[2] + 4, 4)
                first = pl.multiple_of((y * 4 + z) * part, part)
                rows = [turned_acc[s, pl.ds(first, part), :] for s in range(4)]
                for k in range(2):
                    ref[dy, k * part : (k + 1) * part] = jnp.concatenate(rows[2 * k : 2 * k + 2], 1)


def head_grads(at, patches, embed, vec, d_raw, out_sum):
    width = embed.shape[1]
    part = d_raw.shape[1]
    grads = (4, 2 * width // COLS, 2 * part)
    return pl.pallas_call(
        head_grad_kernel,
        grid_spec=pltpu.PrefetchScalarGridSpec(
            num_scalar_prefetch=1,
            grid=(TOKENS // PAIR,),
            in_specs=[
                lane_block(144, PAIR),
                whole(embed.shape),
                whole(vec.shape),
                pl.BlockSpec((3, part, PAIR), lambda t, at: (0, 0, t)),
                whole(out_sum.shape),
            ],
            out_specs=[pl.BlockSpec(grads, lambda t, at: (0, 0, 0))] * 4,
            scratch_shapes=[
                pltpu.VMEM((3, part, width), F32),
                pltpu.VMEM((4, width, part), BF16),
            ],
        ),
        out_shape=[jax.ShapeDtypeStruct(grads, BF16)] * 4,
        compiler_params=params(58),
        cost_estimate=LIGHT,
        name="head_grads",
    )(at, patches, embed, vec, d_raw, out_sum)


def local(
    latent, condition, caption, cap_len, cotangent, embed_weight, modulate_weight, norm_gains,
    cross_gate, qkv_weight, text_kv_weight, out_weight, gate_up_weight, down_weight, unpatch_weight,
):
    images, _, _, channels = latent.shape
    width = embed_weight.shape[3]
    local_width = qkv_weight.shape[2]
    heads = local_width // HD
    hidden_width = down_weight.shape[0]
    taps = 9 * channels
    row_at = lax.axis_index("row")
    col_at = lax.axis_index("col")
    at = jnp.stack([row_at // 2, row_at % 2, col_at // 4, col_at % 4]).astype(jnp.int32)
    tile = latent.shape[1] * latent.shape[2] * channels

    cond_low = jax.nn.silu(condition.astype(F32)).astype(BF16)
    mod_piece = jnp.dot(cond_low, modulate_weight, preferred_element_type=F32)
    mod_columns = mod_piece.shape[1]
    mod_high = mod_piece.astype(BF16)
    mod_low = (mod_piece - mod_high.astype(F32)).astype(BF16)

    packed = jnp.concatenate(
        [latent.reshape(images, tile), cotangent.reshape(images, tile), mod_high, mod_low], axis=1
    )
    packed = jnp.pad(packed, ((0, 0), (0, 2 * local_width - packed.shape[1])))

    packed = lax.all_to_all(packed, "col", 0, 0, tiled=True)
    packed = send_all(packed, "row")

    head_pieces = (
        jnp.concatenate([qkv_weight[0], qkv_weight[1]], axis=1),
        jnp.concatenate([qkv_weight[2], out_weight.T], axis=1),
    )
    first_head = from_col(head_pieces[0], along_z)
    second_head = from_col(head_pieces[1], along_y)
    first_head = from_col(jnp.stack(first_head), along_y)
    second_head = from_col(jnp.stack(second_head), along_z)
    qkv_whole, out_rows = unpack_head(at, first_head, second_head)
    out_pieces = from_chips(out_rows)

    text_piece = jnp.concatenate([text_kv_weight[0], text_kv_weight[1]], axis=1)
    text_whole = lax.all_gather(text_piece, "col", axis=0, tiled=True)
    ffn_piece = jnp.concatenate([gate_up_weight[0], gate_up_weight[1], down_weight.T], axis=1)

    patches, cot_taps = image_taps(packed)
    mod_at = 2 * tile
    modulation = packed[:, :, mod_at : mod_at + mod_columns].astype(F32)
    modulation = modulation + packed[:, :, mod_at + mod_columns : mod_at + 2 * mod_columns].astype(F32)
    modulation = modulation.reshape(4, width)
    attn_gate = jnp.tanh(modulation[1])
    ffn_gate = jnp.tanh(modulation[3])
    vec = jnp.stack(
        [
            norm_gains[0] * (1.0 + modulation[0]),
            norm_gains[1] * attn_gate,
            norm_gains[2] * (1.0 + modulation[2]),
            norm_gains[3] * ffn_gate,
        ]
    )
    vec = jnp.pad(vec, ((0, 4), (0, 0)))
    embed = embed_weight.reshape(taps, width)
    unpatch = unpatch_weight.transpose(0, 1, 3, 2).reshape(taps, width)
    raw = qkv_project(patches, embed, vec, qkv_whole)
    raw = raw.reshape(3, heads, HD, TOKENS)
    ffn_whole = lax.all_gather(after(ffn_piece, text_whole, raw), "col", axis=0, tiled=True)
    caption_rows = caption[0]
    text_raw = dot(text_whole, caption_rows, (0, 1)).reshape(2, heads, HD, caption_rows.shape[0])
    head_gains = lax.dynamic_slice(norm_gains, (4, row_at * local_width), (3, local_width)).reshape(
        3, heads, HD, 1
    )
    head_gates = jnp.tanh(lax.dynamic_slice_in_dim(cross_gate, row_at * heads, heads))
    cap = lax.dynamic_slice_in_dim(cap_len, col_at, 1)
    table = jnp.asarray(rope_tables())
    mixed, lse = attend(raw, text_raw, head_gains, table, cap, head_gates)

    mixed_pieces = from_chips(mixed)
    reached = lax.optimization_barrier((*mixed_pieces, *out_pieces))
    mixed_whole = with_other_core(reached[:4])
    out_whole = with_other_core(reached[4:])
    attn, second, gate_up, hidden, ffn_own, ffn_other = forward(
        at, mixed_whole, out_whole, patches, embed, vec, ffn_whole
    )
    place = tile_places(False)
    cot_own = lax.dynamic_slice_in_dim(cot_taps, row_at * BLOCK, BLOCK, 1)
    d_ffn_own, ffn_out = own_grad(
        to_chips(sum_cores(ffn_own, ffn_other)), cot_own, unpatch, vec
    )
    d_ffn_near = from_chips(d_ffn_own)
    activation_field, unpatch_sum, own_sums = own_block(
        at, ffn_out, attn, patches, cot_taps, embed, unpatch, vec, place
    )
    d_ffn_near = lax.optimization_barrier((*d_ffn_near, activation_field))[:4]
    d_ffn, d_gate_up, d_attn, d_mid, mixed_own, mixed_other, back_sums = backward(
        at, with_other_core(d_ffn_near), ffn_whole, out_whole, gate_up, attn, patches, embed, cot_taps,
        unpatch, vec,
    )
    mixed_near = sum_cores(mixed_own, mixed_other)
    mixed_terms = to_chips(mixed_near)
    text_rows = text_kv_weight.shape[1]
    grads, out_near, out_far = weight_grads(
        after(second, *mixed_near), d_gate_up, d_ffn, hidden, mixed_whole, d_attn, text_rows
    )
    *mixed_terms, grads, out_near, out_far = lax.optimization_barrier(
        (*mixed_terms, grads, out_near, out_far)
    )
    d_mixed = sum(term.astype(F32) for term in mixed_terms).astype(BF16)
    d_mixed = d_mixed.reshape(heads, HD, TOKENS)
    out_near = sum_cores(out_near, out_far)
    out_apart = lax.ppermute(out_near[2], "row", row_pairs_to(2, 0))

    grads, dq_text, d_text_head = text_back(
        raw, text_raw, head_gains, table, lse, d_mixed, cap, head_gates, caption_rows,
        after(grads, *out_near),
    )
    dq_text, grads, out_apart, *out_near = lax.optimization_barrier(
        (dq_text, grads, out_apart, *out_near)
    )
    d_raw, d_head = attend_back(raw, head_gains, table, lse, d_mixed, dq_text)
    out_beside = [lax.ppermute(out_near[d], "row", row_pairs_to(d, 0)) for d in (1, 3)]
    d_raw, *out_terms = lax.optimization_barrier((d_raw, out_near[0], out_apart, *out_beside))
    out_sum = sum(term.astype(F32) for term in out_terms)
    d_raw = d_raw.reshape(3, local_width, TOKENS)
    head_parts = head_grads(at, patches, embed, vec, d_raw, out_sum)
    beside = [lax.ppermute(head_parts[d], "col", col_pairs_to(0, d)) for d in (1, 3)]
    own_pack, other_pack = first_back(
        at, head_gates, patches, embed, vec, qkv_whole, after(d_raw, *head_parts), d_mid, place,
        unpatch_sum, back_sums, own_sums, d_head, d_text_head, norm_gains, modulation, activation_field,
    )
    own_pack, other_pack, apart, *beside = lax.optimization_barrier(
        (own_pack, other_pack, head_parts[2], *beside)
    )
    apart = lax.ppermute(apart, "col", col_pairs_to(0, 2))

    *row_terms, apart = lax.optimization_barrier((*to_chips(sum_cores(own_pack, other_pack)), apart))
    row_pack = sum(term.astype(F32) for term in row_terms)
    head_near = sum(term.astype(F32) for term in (head_parts[0], apart, *beside)).astype(BF16)
    fields = row_pack[CHUNK : CHUNK + 2 * channels].T.reshape(COLS, 8, 2 * channels)
    mod_sums = row_pack[CHUNK + 2 * channels : CHUNK + 2 * channels + 6].reshape(COLS, 8, 6)
    fields = jnp.concatenate([fields, mod_sums], axis=2).astype(BF16)
    fields = jnp.pad(fields, ((0, 0), (0, 0), (0, 128 - fields.shape[2])))
    shared = row_pack[:CHUNK].astype(BF16).reshape(COLS, CHUNK // COLS, 128)
    col_pack = lax.all_to_all(jnp.concatenate([shared, fields], axis=1), "col", 0, 0)
    shared = jnp.sum(col_pack[:, : CHUNK // COLS].astype(F32), axis=0)
    shared = send_all(send_all(shared.astype(BF16), "col"), "row").reshape(-1, 128)
    shared = shared[: 12 * SHARED].reshape(12, SHARED, 128).astype(F32)
    fields = col_pack[:, CHUNK // COLS :]
    activation = fields[:, :, :channels].reshape(latent.shape)
    latent_grad = fields[:, :, channels : 2 * channels].reshape(latent.shape)
    modulate_grad = lax.dot_general(
        cond_low.astype(F32),
        fields[:, :, 2 * channels : 2 * channels + 6].reshape(images, mod_columns).astype(F32),
        (((0,), (0,)), ((), ())),
        precision=lax.Precision.HIGHEST,
        preferred_element_type=F32,
    )
    embed_grad = shared[:, :taps].transpose(1, 0, 2).reshape(embed_weight.shape)
    unpatch_grad = shared[:, taps : 2 * taps].reshape(12, 3, 3, channels, 128)
    unpatch_grad = unpatch_grad.transpose(1, 2, 0, 4, 3).reshape(unpatch_weight.shape)
    gains_grad = shared[:, 2 * taps : 2 * taps + 7].transpose(1, 0, 2).reshape(7, width)
    gate_grad = shared[0, 2 * taps + 7, :HEADS]

    part = width // COLS
    grads = lax.psum_scatter(
        grads.reshape(-1, 2 * local_width), "col", scatter_dimension=0, tiled=True
    ).astype(F32)
    text_kv_grad = jnp.stack([grads[:text_rows, :local_width], grads[:text_rows, local_width:]])
    ffn_total = jnp.concatenate(
        [grads[first : first + part] for first in range(text_rows, grads.shape[0], part)], axis=1
    )
    gate_up_grad = jnp.stack(
        [ffn_total[:, :hidden_width], ffn_total[:, hidden_width : 2 * hidden_width]]
    )
    down_grad = ffn_total[:, 2 * hidden_width :].T
    head_total = sum(term.astype(F32) for term in along_col(head_near, along_y))
    first, second_half = head_total[:, :local_width], head_total[:, local_width:]
    qkv_grad = jnp.stack([first[:part], second_half[:part], first[part:]])
    out_grad = second_half[part:].T
    return (
        activation, latent_grad, embed_grad, modulate_grad, gains_grad, gate_grad,
        qkv_grad, text_kv_grad, out_grad, gate_up_grad, down_grad, unpatch_grad,
    )


def solution(mesh):
    placed = (
        P(None, "row", "col", None),
        P(),
        P("col", None, None),
        P(),
        P(None, "row", "col", None),
        P(),
        P(None, ("row", "col")),
        P(),
        P(),
        P(None, "col", "row"),
        P(None, "col", "row"),
        P("row", "col"),
        P(None, "col", "row"),
        P("row", "col"),
        P(),
    )
    return jax.shard_map(
        local,
        mesh=mesh,
        in_specs=placed,
        out_specs=(
            P(None, "row", "col", None),
            P(None, "row", "col", None),
            P(),
            P(None, ("row", "col")),
            P(),
            P(),
            P(None, "col", "row"),
            P(None, "col", "row"),
            P("row", "col"),
            P(None, "col", "row"),
            P("row", "col"),
            P(),
        ),
        check_vma=False,
    )
```

```python
import math
from functools import partial

import jax
import jax.numpy as jnp
import numpy as np
from jax import lax
from jax.experimental import pallas as pl
from jax.experimental.pallas import tpu as pltpu
from jax.sharding import PartitionSpec as P

HEADS = 24
HD = 64
GRID = 32
TOKENS = GRID * GRID
EPSILON = 1e-06
ROPE_BASE = 10000.0
MASKED = -1e30
F32 = jnp.float32
BF16 = jnp.bfloat16
ROWS = 8
COLS = 16
QUERY_BLOCK = 256
BLOCK = TOKENS // ROWS
PAIR = 2 * BLOCK
MIB = 2**20
SHARED = 320
CHUNK = 512
LIGHT = pl.CostEstimate(flops=1, bytes_accessed=1, transcendentals=0)


def dot(left, right, contract):
    return lax.dot_general(
        left, right, ((contract[:1], contract[1:]), ((), ())), preferred_element_type=F32
    )


def row_pairs(dx, dc):
    return [
        (((x + dx) % 4) * 2 + (c + dc) % 2, x * 2 + c) for x in range(4) for c in range(2)
    ]


def row_pairs_to(dx, dc):
    return [(dst, src) for src, dst in row_pairs(dx, dc)]


def from_chips(piece):
    return [piece] + [lax.ppermute(piece, "row", row_pairs(d, 0)) for d in (1, 2, 3)]


def with_other_core(pieces):
    quad = jnp.stack(pieces)
    return quad, lax.ppermute(quad, "row", row_pairs(0, 1))


def gather_near(piece):
    return with_other_core(from_chips(piece))


def sum_cores(own, other):
    other = lax.ppermute(other, "row", row_pairs(0, 1))
    return [(own[d].astype(F32) + other[d].astype(F32)).astype(BF16) for d in range(4)]


def to_chips(near):
    return [near[0]] + [lax.ppermute(near[d], "row", row_pairs_to(d, 0)) for d in (1, 2, 3)]


def col_pairs_to(dy, dz):
    return [(y * 4 + z, (y + dy) % 4 * 4 + (z + dz) % 4) for y in range(4) for z in range(4)]


def col_pairs(dy, dz):
    return [(dst, src) for src, dst in col_pairs_to(dy, dz)]


def from_col(piece, step):
    return [piece] + [lax.ppermute(piece, "col", col_pairs(*step(d))) for d in (1, 2, 3)]


def along_y(d):
    return (d, 0)


def along_z(d):
    return (0, d)


def along_col(parts, step):
    return [parts[0]] + [lax.ppermute(parts[d], "col", col_pairs_to(*step(d))) for d in (1, 2, 3)]


def send_all(piece, axis):
    copies = jnp.broadcast_to(piece, (lax.axis_size(axis),) + piece.shape)
    return lax.all_to_all(copies, axis, 0, 0)


def after(value, *others):
    return lax.optimization_barrier((value,) + others)[0]


def rope_tables():
    quarter = HD // 4
    frequency = np.float32(ROPE_BASE) ** (-np.arange(quarter, dtype=np.float32) / np.float32(quarter))
    place = np.arange(TOKENS)
    row = frequency[:, None] * (place // GRID).astype(np.float32)[None, :]
    col = frequency[:, None] * (place % GRID).astype(np.float32)[None, :]
    return np.stack([np.cos(row), np.sin(row), np.cos(col), np.sin(col)]).astype(np.float32)


def turn(v, table, sign):
    a, b, c, d = (v[k * 16 : (k + 1) * 16] for k in range(4))
    cr, sr, cc, sc = table[0], table[1] * sign, table[2], table[3] * sign
    return jnp.concatenate([a * cr - b * sr, a * sr + b * cr, c * cc - d * sc, c * sc + d * cc], 0)


def column_rms(v):
    return lax.rsqrt(jnp.mean(v * v, axis=0, keepdims=True) + EPSILON)


def normed(v, gain):
    return v * column_rms(v) * gain


def column_rms_back(v, u):
    scale = column_rms(v)
    return (u - v * (jnp.mean(u * v, axis=0, keepdims=True) * scale * scale)) * scale


def whole(shape):
    zeros = (0,) * len(shape)
    return pl.BlockSpec(shape, lambda *_: zeros, pipeline_mode=pl.Buffered(1))


def held():
    return pl.BlockSpec(memory_space=pltpu.VMEM)


def lane_block(rows, lanes):
    return pl.BlockSpec((rows, lanes), lambda t, *_: (0, t))


def row_block(rows, lanes):
    return pl.BlockSpec((rows, lanes), lambda t, *_: (t, 0))


def params(mib):
    return pltpu.CompilerParams(vmem_limit_bytes=mib * MIB, dimension_semantics=("arbitrary",))


def row_of_sums(v):
    return jnp.sum(v.T, axis=0, keepdims=True)


def attend_kernel(
    cap_ref, gate_ref, raw_ref, text_ref, gain_ref, table_ref, mixed_ref, lse_ref,
    q_ref, k_ref, v_ref, tk_ref, tv_ref,
):
    step = pl.program_id(0)
    heads = raw_ref.shape[1]

    @pl.when(step == 0)
    def _():
        table = table_ref[...]
        for h in range(heads):
            q = turn(normed(raw_ref[0, h], gain_ref[0, h]), table, 1.0).astype(BF16)
            q_ref[h] = q * jnp.asarray(0.125, BF16)
            k_ref[h] = turn(normed(raw_ref[1, h], gain_ref[1, h]), table, 1.0).T.astype(BF16)
            v_ref[h] = raw_ref[2, h].astype(BF16)
            tk_ref[h] = normed(text_ref[0, h], gain_ref[2, h]).T.astype(BF16)
            tv_ref[h] = text_ref[1, h].astype(BF16)

    slots = tk_ref.shape[1]
    mask = lax.broadcasted_iota(jnp.int32, (slots, QUERY_BLOCK), 0) < cap_ref[0]
    here = pl.ds(pl.multiple_of(step * QUERY_BLOCK, QUERY_BLOCK), QUERY_BLOCK)
    outs = []
    for h in range(heads):
        qb = q_ref[h, :, here]
        e = jnp.exp(dot(k_ref[h], qb, (1, 0)))
        total = jnp.sum(e, axis=0, keepdims=True)
        own = dot(v_ref[h], e.astype(BF16), (1, 0)) / total
        te = jnp.exp(jnp.where(mask, dot(tk_ref[h], qb, (1, 0)), MASKED))
        text_total = jnp.sum(te, axis=0, keepdims=True)
        text = dot(tv_ref[h], te.astype(BF16), (1, 0)) / text_total
        outs.append(own + gate_ref[h] * text)
        lse_ref[h, 0:1] = jnp.log(total)
        lse_ref[h, 1:2] = jnp.log(text_total)
    mixed_ref[...] = jnp.concatenate(outs, 0).astype(BF16)


def attend(raw, text_raw, gains, table, cap, gates):
    heads = raw.shape[1]
    slots = text_raw.shape[3]
    return pl.pallas_call(
        attend_kernel,
        grid_spec=pltpu.PrefetchScalarGridSpec(
            num_scalar_prefetch=2,
            grid=(TOKENS // QUERY_BLOCK,),
            in_specs=[
                whole((3, heads, HD, TOKENS)),
                whole((2, heads, HD, slots)),
                whole((3, heads, HD, 1)),
                whole((4, 16, TOKENS)),
            ],
            out_specs=[
                lane_block(heads * HD, QUERY_BLOCK),
                pl.BlockSpec((heads, 8, QUERY_BLOCK), lambda t, *_: (0, 0, t)),
            ],
            scratch_shapes=[
                pltpu.VMEM((heads, HD, TOKENS), BF16),
                pltpu.VMEM((heads, TOKENS, HD), BF16),
                pltpu.VMEM((heads, HD, TOKENS), BF16),
                pltpu.VMEM((heads, slots, HD), BF16),
                pltpu.VMEM((heads, HD, slots), BF16),
            ],
        ),
        out_shape=[
            jax.ShapeDtypeStruct((heads * HD, TOKENS), BF16),
            jax.ShapeDtypeStruct((heads, 8, TOKENS), F32),
        ],
        compiler_params=params(20),
        cost_estimate=LIGHT,
        name="attend",
    )(cap, gates, raw, text_raw, gains, table)


def text_back_kernel(
    cap_ref, gate_ref, q_raw_ref, text_ref, gain_ref, table_ref, lse_ref, grad_ref, caption_ref, held_ref,
    grads_ref, dq_ref, d_gain_ref, low_ref,
):
    del held_ref
    step = pl.program_id(0)
    heads, _, slots = low_ref.shape[1:]

    @pl.when(step == 0)
    def _():
        table = table_ref[...]
        mask = lax.broadcasted_iota(jnp.int32, (slots, TOKENS), 0) < cap_ref[0]
        for h in range(heads):
            gate = gate_ref[h]
            q = turn(normed(q_raw_ref[h], gain_ref[0, h]), table, 1.0).astype(BF16)
            q = q * jnp.asarray(0.125, BF16)
            tk = normed(text_ref[0, h], gain_ref[2, h]).astype(BF16)
            tv = text_ref[1, h].astype(BF16)
            g = grad_ref[h]
            tp = jnp.exp(jnp.where(mask, dot(tk, q, (0, 0)), MASKED) - lse_ref[h, 1:2])
            tpb = tp.astype(BF16)
            low_ref[1, h] = (dot(g, tpb, (1, 1)) * gate).astype(BF16)
            gate_terms = g.astype(F32) * dot(tv, tpb, (1, 0))
            tpd = tp * dot(tv, g, (0, 0)) * gate
            dts = (tpd - tp * jnp.sum(tpd, axis=0, keepdims=True)).astype(BF16)
            dq_ref[h] = dot(tk, dts, (1, 0))
            d_tk = dot(q, dts, (1, 1))
            values = text_ref[0, h]
            low_ref[0, h] = column_rms_back(values, d_tk * gain_ref[2, h]).astype(BF16)
            d_gain_ref[h, 0:1] = row_of_sums(values * column_rms(values) * d_tk)
            d_gain_ref[h, 1:2] = row_of_sums(gate_terms)

    d_text = low_ref[...].reshape(2 * heads * HD, slots)
    rows = grads_ref.shape[1]
    for k in range(grads_ref.shape[0]):
        grads_ref[k] = dot(caption_ref[:, k * rows : (k + 1) * rows], d_text, (0, 1)).astype(BF16)


def text_back(raw, text_raw, gains, table, lse, grads, cap, gates, caption, held):
    heads = raw.shape[1]
    slots = text_raw.shape[3]
    rows = caption.shape[1] // COLS
    lanes = 2 * heads * HD
    return pl.pallas_call(
        text_back_kernel,
        grid_spec=pltpu.PrefetchScalarGridSpec(
            num_scalar_prefetch=2,
            grid=(4,),
            in_specs=[
                pl.BlockSpec((None, heads, HD, TOKENS), lambda t, *_: (0, 0, 0, 0)),
                whole(text_raw.shape),
                whole(gains.shape),
                whole(table.shape),
                whole(lse.shape),
                whole(grads.shape),
                pl.BlockSpec((slots, 4 * rows), lambda t, *_: (0, t)),
                pl.BlockSpec(memory_space=pl.ANY),
            ],
            out_specs=[
                pl.BlockSpec((4, rows, lanes), lambda t, *_: (t, 0, 0)),
                pl.BlockSpec((heads, HD, TOKENS), lambda t, *_: (0, 0, 0)),
                pl.BlockSpec((heads, 8, HD), lambda t, *_: (0, 0, 0)),
            ],
            scratch_shapes=[pltpu.VMEM((2, heads, HD, slots), BF16)],
        ),
        out_shape=[
            jax.ShapeDtypeStruct(held.shape, BF16),
            jax.ShapeDtypeStruct((heads, HD, TOKENS), F32),
            jax.ShapeDtypeStruct((heads, 8, HD), F32),
        ],
        input_output_aliases={9: 0},
        compiler_params=params(58),
        cost_estimate=LIGHT,
        name="text_back",
    )(cap, gates, raw, text_raw, gains, table, lse, grads, caption, held)


def attend_back_kernel(
    raw_ref, gain_ref, table_ref, lse_ref, grad_ref, dq_text_ref,
    d_raw_ref, d_gain_ref, dv_ref, dk_ref, dq_ref,
):
    table = table_ref[...]
    q = turn(normed(raw_ref[0], gain_ref[0]), table, 1.0).astype(BF16) * jnp.asarray(0.125, BF16)
    k = turn(normed(raw_ref[1], gain_ref[1]), table, 1.0)
    k, k_turned = k.astype(BF16), k.T.astype(BF16)
    v_turned = raw_ref[2].T.astype(BF16)
    for first in range(0, TOKENS, QUERY_BLOCK):
        here = slice(first, first + QUERY_BLOCK)
        qb = q[:, here]
        gb = grad_ref[:, here]
        p = jnp.exp(dot(k_turned, qb, (1, 0)) - lse_ref[0:1, here])
        dv = dot(gb, p.astype(BF16), (1, 1))
        pd = p * dot(v_turned, gb, (1, 0))
        ds = (pd - p * jnp.sum(pd, axis=0, keepdims=True)).astype(BF16)
        dq_ref[:, here] = dot(k, ds, (1, 0)) + dq_text_ref[:, here]
        dk = dot(qb, ds, (1, 1))
        if first == 0:
            dv_ref[...] = dv
            dk_ref[...] = dk
        else:
            dv_ref[...] += dv
            dk_ref[...] += dk

    def raw_back(which, d_turned):
        spun = turn(d_turned.astype(BF16).astype(F32), table, -1.0)
        values = raw_ref[which]
        d_raw_ref[which] = column_rms_back(values, spun * gain_ref[which]).astype(BF16)
        d_gain_ref[which : which + 1] = row_of_sums(values * column_rms(values) * spun)

    raw_back(0, dq_ref[...] * 0.125)
    raw_back(1, dk_ref[...])
    d_raw_ref[2] = dv_ref[...].astype(BF16)


def attend_back(raw, gains, table, lse, grads, dq_text):
    heads = raw.shape[1]
    return pl.pallas_call(
        attend_back_kernel,
        grid=(heads,),
        in_specs=[
            pl.BlockSpec((3, None, HD, TOKENS), lambda h: (0, h, 0, 0)),
            pl.BlockSpec((3, None, HD, 1), lambda h: (0, h, 0, 0)),
            pl.BlockSpec((4, 16, TOKENS), lambda h: (0, 0, 0)),
            pl.BlockSpec((None, 8, TOKENS), lambda h: (h, 0, 0)),
            pl.BlockSpec((None, HD, TOKENS), lambda h: (h, 0, 0)),
            pl.BlockSpec((None, HD, TOKENS), lambda h: (h, 0, 0)),
        ],
        out_specs=[
            pl.BlockSpec((3, None, HD, TOKENS), lambda h: (0, h, 0, 0)),
            pl.BlockSpec((None, 8, HD), lambda h: (h, 0, 0)),
        ],
        scratch_shapes=[pltpu.VMEM((HD, TOKENS), F32) for _ in range(3)],
        out_shape=[
            jax.ShapeDtypeStruct((3, heads, HD, TOKENS), BF16),
            jax.ShapeDtypeStruct((heads, 8, HD), F32),
        ],
        compiler_params=params(58),
        cost_estimate=LIGHT,
        name="attend_back",
    )(raw, gains, table, lse, grads, dq_text)


def tile_places(chunk_first):
    r, c, k = np.meshgrid(np.arange(ROWS), np.arange(COLS), np.arange(8), indexing="ij")
    token = r * BLOCK + (k // 2) * GRID + c * 2 + k % 2
    source = (k * ROWS + r) * COLS + c if chunk_first else (r * COLS + c) * 8 + k
    places = np.zeros((TOKENS, TOKENS), np.float32)
    places[source.ravel(), token.ravel()] = 1.0
    return jnp.asarray(places, BF16)


def grid_shift(field, di, dj):
    step = di * GRID + dj
    moved = pltpu.roll(field, (-step) % TOKENS, 1) if step else field
    place = lax.broadcasted_iota(jnp.int32, field.shape, 1)
    row = place // GRID + di
    col = place % GRID + dj
    inside = (row >= 0) & (row < GRID) & (col >= 0) & (col < GRID)
    return jnp.where(inside, moved, 0.0)


def image_kernel(packed_ref, place_ref, patch_ref, cot_ref):
    for which, sign, out_ref in ((0, 1, patch_ref), (1, -1, cot_ref)):
        lanes = slice(which * 128, (which + 1) * 128)
        tiles = jnp.concatenate([packed_ref[r, :, lanes] for r in range(ROWS)], 0)
        turned = tiles.astype(F32).T
        chunks = jnp.concatenate([turned[k * 16 : (k + 1) * 16] for k in range(8)], 1)
        image = dot(chunks.astype(BF16), place_ref[...], (1, 0))
        for a in range(3):
            for b in range(3):
                first = (a * 3 + b) * 16
                out_ref[first : first + 16] = grid_shift(
                    image, sign * (a - 1), sign * (b - 1)
                ).astype(BF16)


def image_taps(packed):
    out = jax.ShapeDtypeStruct((144, TOKENS), BF16)
    return pl.pallas_call(
        image_kernel,
        out_shape=[out, out],
        compiler_params=pltpu.CompilerParams(vmem_limit_bytes=12 * MIB),
        cost_estimate=LIGHT,
        name="image_taps",
    )(packed, tile_places(True))


def field_of(taps, place, sign):
    total = jnp.zeros((16, TOKENS), F32)
    for a in range(3):
        for b in range(3):
            first = (a * 3 + b) * 16
            total = total + grid_shift(taps[first : first + 16], sign * (a - 1), sign * (b - 1))
    tiles = dot(total.astype(BF16), place, (1, 1))
    return [tiles[:, r * BLOCK : (r + 1) * BLOCK] for r in range(ROWS)]


def row_rms(v):
    return lax.rsqrt(jnp.mean(v * v, axis=-1, keepdims=True) + EPSILON)


def row_rms_back(v, scale, u):
    return (u - v * (jnp.mean(u * v, axis=-1, keepdims=True) * scale * scale)) * scale


def unpack_kernel(at_ref, *refs):
    first_refs, second_refs, (joined_ref, out_ref, turn_ref) = refs[:4], refs[4:8], refs[8:]
    part = first_refs[0].shape[1]
    local_width = first_refs[0].shape[2] // 2
    ys = [lax.rem(at_ref[2] + d, 4) for d in range(4)]
    zs = [lax.rem(at_ref[3] + d, 4) for d in range(4)]
    for dy in range(4):
        for dz in range(4):
            rows = pl.ds(pl.multiple_of((ys[dy] * 4 + zs[dz]) * part, part), part)
            piece = first_refs[dy][dz]
            joined_ref[0, rows, :] = piece[:, :local_width]
            joined_ref[1, rows, :] = piece[:, local_width:]
            piece = second_refs[dz][dy]
            joined_ref[2, rows, :] = piece[:, :local_width]
            turn_ref[rows, :] = piece[:, local_width:]
    out_ref[...] = turn_ref[...].T


def unpack_head(at, first, second):
    _, part, lanes = first[0].shape
    width, local_width = COLS * part, lanes // 2
    return pl.pallas_call(
        unpack_kernel,
        grid_spec=pltpu.PrefetchScalarGridSpec(
            num_scalar_prefetch=1,
            grid=(1,),
            in_specs=[whole(first[0].shape)] * 8,
            out_specs=[
                pl.BlockSpec((3, width, local_width), lambda t, at: (0, 0, 0)),
                pl.BlockSpec((local_width, width), lambda t, at: (0, 0)),
            ],
            scratch_shapes=[pltpu.VMEM((width, local_width), BF16)],
        ),
        out_shape=[
            jax.ShapeDtypeStruct((3, width, local_width), BF16),
            jax.ShapeDtypeStruct((local_width, width), BF16),
        ],
        compiler_params=params(14),
        cost_estimate=LIGHT,
        name="unpack_head",
    )(at, *first, *second)


def qkv_kernel(patch_ref, embed_ref, vec_ref, weight_ref, raw_ref):
    x = dot(patch_ref[...], embed_ref[...], (0, 0))
    h = (x * row_rms(x) * vec_ref[0:1]).astype(BF16)
    for s in range(3):
        raw_ref[s] = dot(h, weight_ref[s], (1, 0)).T


def qkv_project(patches, embed, vec, weight):
    part = weight.shape[2]
    return pl.pallas_call(
        qkv_kernel,
        grid=(TOKENS // PAIR,),
        in_specs=[lane_block(144, PAIR), whole(embed.shape), whole(vec.shape), whole(weight.shape)],
        out_specs=pl.BlockSpec((3, part, PAIR), lambda t: (0, 0, t)),
        out_shape=jax.ShapeDtypeStruct((3, part, TOKENS), F32),
        compiler_params=params(16),
        cost_estimate=LIGHT,
        name="qkv_project",
    )(patches, embed, vec, weight)


def joined(ref):
    return ref[...].reshape(-1, ref.shape[2])


def halves(core, first, second):
    return jnp.where(core == 0, first, second)


def forward_kernel(
    at_ref, near_ref, far_ref, out_near_ref, out_far_ref, patch_ref, embed_ref, vec_ref, ffn_ref,
    attn_ref, second_ref, gate_up_ref, hidden_ref, own_ref, other_ref,
):
    core = at_ref[1]
    hidden_width = hidden_ref.shape[1]
    x = dot(patch_ref[...], embed_ref[...], (0, 0))
    attn = dot(joined(near_ref), joined(out_near_ref), (0, 0))
    attn = attn + dot(joined(far_ref), joined(out_far_ref), (0, 0))
    attn_ref[...] = attn.astype(BF16)
    mid = x + vec_ref[1:2] * (attn * row_rms(attn))
    second = (mid * row_rms(mid) * vec_ref[2:3]).astype(BF16)
    second_ref[...] = second
    gate_up = dot(second, ffn_ref[:, : 2 * hidden_width], (1, 0))
    gate_up_ref[...] = gate_up.astype(BF16)
    gate = gate_up[:, :hidden_width]
    hidden = (gate * jax.nn.sigmoid(gate) * gate_up[:, hidden_width:]).astype(BF16)
    hidden_ref[...] = hidden
    part = dot(hidden, ffn_ref[:, 2 * hidden_width :], (1, 1)).astype(BF16)
    own_ref[0] = halves(core, part[:BLOCK], part[BLOCK:])
    other_ref[0] = halves(core, part[BLOCK:], part[:BLOCK])


def forward(at, mixed, out_whole, patches, embed, vec, ffn):
    width = embed.shape[1]
    part = mixed[0].shape[1]
    hidden_width = ffn.shape[1] // 3
    by_chip = pl.BlockSpec((1, BLOCK, width), lambda t, at: ((t - at[0] + 4) % 4, 0, 0))
    return pl.pallas_call(
        forward_kernel,
        grid_spec=pltpu.PrefetchScalarGridSpec(
            num_scalar_prefetch=1,
            grid=(4,),
            in_specs=[
                pl.BlockSpec((4, part, PAIR), lambda t, at: (0, 0, t)),
                pl.BlockSpec((4, part, PAIR), lambda t, at: (0, 0, t)),
                whole((4, part, width)),
                whole((4, part, width)),
                lane_block(144, PAIR),
                whole(embed.shape),
                whole(vec.shape),
                whole(ffn.shape),
            ],
            out_specs=[
                row_block(PAIR, width),
                row_block(PAIR, width),
                row_block(PAIR, 2 * hidden_width),
                row_block(PAIR, hidden_width),
                by_chip,
                by_chip,
            ],
        ),
        out_shape=[
            jax.ShapeDtypeStruct((TOKENS, width), BF16),
            jax.ShapeDtypeStruct((TOKENS, width), BF16),
            jax.ShapeDtypeStruct((TOKENS, 2 * hidden_width), BF16),
            jax.ShapeDtypeStruct((TOKENS, hidden_width), BF16),
            jax.ShapeDtypeStruct((4, BLOCK, width), BF16),
            jax.ShapeDtypeStruct((4, BLOCK, width), BF16),
        ],
        compiler_params=params(56),
        cost_estimate=LIGHT,
        name="forward",
    )(at, *mixed, *out_whole, patches, embed, vec, ffn)


def own_grad_kernel(p0_ref, p1_ref, p2_ref, p3_ref, cot_ref, unpatch_ref, vec_ref, d_ffn_ref, ffn_ref):
    ffn = sum(p[...].astype(F32) for p in (p0_ref, p1_ref, p2_ref, p3_ref))
    ffn_ref[...] = ffn
    d_last = dot(cot_ref[...], unpatch_ref[...], (0, 0))
    d_ffn_ref[...] = row_rms_back(ffn, row_rms(ffn), vec_ref[3:4] * d_last).astype(BF16)


def own_grad(pieces, cot_own, unpatch, vec):
    shape = (BLOCK, unpatch.shape[1])
    return pl.pallas_call(
        own_grad_kernel,
        out_shape=[jax.ShapeDtypeStruct(shape, BF16), jax.ShapeDtypeStruct(shape, F32)],
        compiler_params=pltpu.CompilerParams(vmem_limit_bytes=12 * MIB),
        cost_estimate=LIGHT,
        name="own_grad",
    )(*pieces, cot_own, unpatch, vec)


def own_kernel(
    at_ref, ffn_ref, attn_ref, patch_ref, cot_ref, embed_ref, unpatch_ref, vec_ref, place_ref,
    field_ref, unpatch_sum_ref, sums_ref, taps_ref,
):
    ffn = ffn_ref[...]
    d_last = dot(cot_ref[...], unpatch_ref[...], (0, 0))
    normed_ffn = ffn * row_rms(ffn)
    sums_ref[...] = jnp.broadcast_to(
        jnp.sum(normed_ffn * d_last, axis=0, keepdims=True), sums_ref.shape
    )
    attn = attn_ref[...].astype(F32)
    x = dot(patch_ref[...], embed_ref[...], (0, 0))
    last = (x + vec_ref[1:2] * (attn * row_rms(attn)) + vec_ref[3:4] * normed_ffn).astype(BF16)
    unpatch_sum_ref[...] = dot(cot_ref[...], last, (1, 0))
    taps_ref[...] = jnp.zeros_like(taps_ref)
    here = pl.multiple_of((2 * at_ref[0] + at_ref[1]) * BLOCK, BLOCK)
    taps_ref[:, pl.ds(here, BLOCK)] = dot(unpatch_ref[...], last, (1, 1))
    for r, tile in enumerate(field_of(taps_ref[...], place_ref[...], 1)):
        field_ref[r] = tile


def own_block(at, ffn, attn, patches, cot_taps, embed, unpatch, vec, place):
    width = embed.shape[1]
    lanes = pl.BlockSpec((144, BLOCK), lambda t, at: (0, 2 * at[0] + at[1]))
    return pl.pallas_call(
        own_kernel,
        grid_spec=pltpu.PrefetchScalarGridSpec(
            num_scalar_prefetch=1,
            grid=(1,),
            in_specs=[
                whole((BLOCK, width)),
                pl.BlockSpec((BLOCK, width), lambda t, at: (2 * at[0] + at[1], 0)),
                lanes,
                lanes,
                whole(embed.shape),
                whole(unpatch.shape),
                whole(vec.shape),
                whole(place.shape),
            ],
            out_specs=[
                pl.BlockSpec((ROWS, 16, BLOCK), lambda t, at: (0, 0, 0)),
                pl.BlockSpec((144, width), lambda t, at: (0, 0)),
                pl.BlockSpec((8, width), lambda t, at: (0, 0)),
            ],
            scratch_shapes=[pltpu.VMEM((144, TOKENS), F32)],
        ),
        out_shape=[
            jax.ShapeDtypeStruct((ROWS, 16, BLOCK), F32),
            jax.ShapeDtypeStruct((144, width), F32),
            jax.ShapeDtypeStruct((8, width), F32),
        ],
        compiler_params=params(14),
        cost_estimate=LIGHT,
        name="own_block",
    )(at, ffn, attn, patches, cot_taps, embed, unpatch, vec, place)


def backward_kernel(
    at_ref, own_ref, other_ref, ffn_ref, out_near_ref, out_far_ref, gate_up_ref, attn_ref,
    patch_ref, embed_ref, cot_ref, unpatch_ref, vec_ref,
    d_ffn_ref, d_gate_up_ref, d_attn_ref, d_mid_ref, mixed_own_ref, mixed_other_ref, sums_ref,
):
    step = pl.program_id(0)
    chip, core = at_ref[0], at_ref[1]
    hidden_width = d_gate_up_ref.shape[1] // 2
    own, other = own_ref[0], other_ref[0]
    d_ffn = jnp.concatenate([halves(core, own, other), halves(core, other, own)], 0)
    d_ffn_ref[...] = d_ffn
    d_hidden = dot(d_ffn, ffn_ref[:, 2 * hidden_width :], (1, 0))
    gate = gate_up_ref[:, :hidden_width].astype(F32)
    up = gate_up_ref[:, hidden_width:].astype(F32)
    sigma = jax.nn.sigmoid(gate)
    silu = gate * sigma
    d_gate = d_hidden * up * (sigma + silu * (1.0 - sigma))
    d_gate_up = jnp.concatenate([d_gate.astype(BF16), (d_hidden * silu).astype(BF16)], 1)
    d_gate_up_ref[...] = d_gate_up
    d_second = dot(d_gate_up, ffn_ref[:, : 2 * hidden_width], (1, 1))

    x = dot(patch_ref[...], embed_ref[...], (0, 0))
    attn = attn_ref[...].astype(F32)
    attn_scale = row_rms(attn)
    attn_normed = attn * attn_scale
    mid = x + vec_ref[1:2] * attn_normed
    mid_scale = row_rms(mid)
    mid_sum = jnp.sum(mid * mid_scale * d_second, axis=0, keepdims=True)
    d_last = dot(cot_ref[...], unpatch_ref[...], (0, 0))
    place = lax.broadcasted_iota(jnp.int32, (PAIR, 1), 0) // BLOCK
    mine = (place == core) & (step == chip)
    d_mid = row_rms_back(mid, mid_scale, vec_ref[2:3] * d_second) + jnp.where(mine, d_last, 0.0)
    d_mid_ref[...] = d_mid.astype(BF16)
    attn_sum = jnp.sum(attn_normed * d_mid, axis=0, keepdims=True)
    d_attn = row_rms_back(attn, attn_scale, vec_ref[1:2] * d_mid).astype(BF16)
    d_attn_ref[...] = d_attn
    for weight_ref, part_ref in ((out_near_ref, mixed_own_ref), (out_far_ref, mixed_other_ref)):
        part_ref[...] = dot(joined(weight_ref), d_attn, (1, 1)).astype(BF16).reshape(part_ref.shape)

    @pl.when(step == 0)
    def _():
        sums_ref[...] = jnp.zeros_like(sums_ref)

    sums_ref[0:1] += mid_sum
    sums_ref[1:2] += attn_sum


def backward(at, d_ffn, ffn, out_whole, gate_up, attn, patches, embed, cot_taps, unpatch, vec):
    width = embed.shape[1]
    part = out_whole[0].shape[1]
    hidden_width = ffn.shape[1] // 3
    by_chip = pl.BlockSpec((1, BLOCK, width), lambda t, at: ((t - at[0] + 4) % 4, 0, 0))
    parts = pl.BlockSpec((4, part, PAIR), lambda t, at: (0, 0, t))
    return pl.pallas_call(
        backward_kernel,
        grid_spec=pltpu.PrefetchScalarGridSpec(
            num_scalar_prefetch=1,
            grid=(4,),
            in_specs=[
                by_chip,
                by_chip,
                held(),
                held(),
                held(),
                row_block(PAIR, 2 * hidden_width),
                row_block(PAIR, width),
                lane_block(144, PAIR),
                whole(embed.shape),
                lane_block(144, PAIR),
                whole(unpatch.shape),
                whole(vec.shape),
            ],
            out_specs=[
                row_block(PAIR, width),
                row_block(PAIR, 2 * hidden_width),
                row_block(PAIR, width),
                row_block(PAIR, width),
                parts,
                parts,
                pl.BlockSpec((8, width), lambda t, at: (0, 0)),
            ],
        ),
        out_shape=[
            jax.ShapeDtypeStruct((TOKENS, width), BF16),
            jax.ShapeDtypeStruct((TOKENS, 2 * hidden_width), BF16),
            jax.ShapeDtypeStruct((TOKENS, width), BF16),
            jax.ShapeDtypeStruct((TOKENS, width), BF16),
            jax.ShapeDtypeStruct((4, part, TOKENS), BF16),
            jax.ShapeDtypeStruct((4, part, TOKENS), BF16),
            jax.ShapeDtypeStruct((8, width), F32),
        ],
        compiler_params=params(32),
        cost_estimate=LIGHT,
        name="backward",
    )(at, *d_ffn, ffn, *out_whole, gate_up, attn, patches, embed, cot_taps, unpatch, vec)


def weight_kernel(
    second_ref, d_gate_up_ref, d_ffn_ref, hidden_ref, near_ref, far_ref, d_attn_ref,
    grads_ref, out_near_ref, out_far_ref,
):
    step = pl.program_id(0)
    chunk, _, lanes = grads_ref.shape[0] // 4, *grads_ref.shape[1:]
    part = second_ref.shape[1] // chunk
    rows = jnp.concatenate(
        [
            dot(second_ref[...], d_gate_up_ref[...], (0, 0)).astype(BF16),
            dot(d_ffn_ref[...], hidden_ref[...], (0, 0)).astype(BF16),
        ],
        1,
    )
    groups = rows.shape[1] // lanes
    first = grads_ref.shape[1] - groups * part
    for c in range(chunk):
        for g in range(groups):
            grads_ref[step * chunk + c, first + g * part : first + (g + 1) * part] = rows[
                c * part : (c + 1) * part, g * lanes : (g + 1) * lanes
            ]
    out_near_ref[0] = dot(near_ref[0], d_attn_ref[...], (1, 0)).astype(BF16)
    out_far_ref[0] = dot(far_ref[0], d_attn_ref[...], (1, 0)).astype(BF16)


def weight_grads(second, d_gate_up, d_ffn, hidden, mixed, d_attn, text_rows):
    width = second.shape[1]
    heads_width = mixed[0].shape[1]
    lanes = 2 * heads_width
    grads = (COLS, text_rows + width // COLS * 3 * hidden.shape[1] // lanes, lanes)
    pieces = pl.BlockSpec((1, heads_width, TOKENS), lambda t: (t, 0, 0))
    out_piece = pl.BlockSpec((1, heads_width, width), lambda t: (t, 0, 0))
    out_shape = jax.ShapeDtypeStruct((4, heads_width, width), BF16)
    return pl.pallas_call(
        weight_kernel,
        grid=(4,),
        in_specs=[
            lane_block(TOKENS, width // 4),
            whole(d_gate_up.shape),
            lane_block(TOKENS, width // 4),
            whole(hidden.shape),
            pieces,
            pieces,
            whole(d_attn.shape),
        ],
        out_specs=[pl.BlockSpec(grads, lambda t: (0, 0, 0)), out_piece, out_piece],
        out_shape=[jax.ShapeDtypeStruct(grads, BF16), out_shape, out_shape],
        compiler_params=params(40),
        cost_estimate=LIGHT,
        name="weight_grads",
    )(second, d_gate_up, d_ffn, hidden, *mixed, d_attn)


def first_kernel(
    at_ref, gate_ref, patch_ref, embed_ref, vec_ref, weight_ref, d_raw_ref, d_mid_ref, place_ref, out_sum_ref,
    unpatch_sum_ref, back_sums_ref, own_sums_ref, head_ref, text_head_ref, gains_ref, mod_ref, activation_ref,
    own_pack_ref, other_pack_ref, p0_ref, p1_ref, p2_ref, p3_ref,
    taps_acc, embed_acc, first_acc, shared_acc, qkv_acc, turned_acc,
):
    step = pl.program_id(0)
    last = pl.num_programs(0) - 1
    x = dot(patch_ref[...], embed_ref[...], (0, 0))
    scale = row_rms(x)
    x_normed = x * scale
    h = (x_normed * vec_ref[0:1]).astype(BF16)
    d_h = dot(d_raw_ref[0], weight_ref[0], (0, 1))
    for s in (1, 2):
        d_h = d_h + dot(d_raw_ref[s], weight_ref[s], (0, 1))

    @pl.when(step == 0)
    def _():
        qkv_acc[...] = jnp.zeros_like(qkv_acc)
        embed_acc[...] = jnp.zeros_like(embed_acc)
        first_acc[...] = jnp.zeros_like(first_acc)

    qkv_acc[...] += dot(joined(d_raw_ref), h, (1, 0)).reshape(qkv_acc.shape)
    first_acc[0:1] += jnp.sum(x_normed * d_h, axis=0, keepdims=True)
    d_first = (d_mid_ref[...].astype(F32) + row_rms_back(x, scale, vec_ref[0:1] * d_h)).astype(BF16)
    embed_acc[...] += dot(patch_ref[...], d_first, (1, 0))
    here = pl.ds(pl.multiple_of(step * PAIR, PAIR), PAIR)
    taps_acc[:, here] = dot(embed_ref[...], d_first, (1, 1))

    @pl.when(step == last)
    def _():
        part = p0_ref.shape[1] // 2
        for s in range(4):
            turned_acc[s] = (qkv_acc[s] if s < 3 else out_sum_ref[...]).T.astype(BF16)
        for dz, ref in enumerate((p0_ref, p1_ref, p2_ref, p3_ref)):
            z = lax.rem(at_ref[3] + dz, 4)
            for y in range(4):
                dy = lax.rem(y - at_ref[2] + 4, 4)
                first = pl.multiple_of((y * 4 + z) * part, part)
                pieces = [turned_acc[s, pl.ds(first, part), :] for s in range(4)]
                for k in range(2):
                    ref[dy, k * part : (k + 1) * part] = jnp.concatenate(
                        pieces[2 * k : 2 * k + 2], 1
                    )
        terms = jnp.concatenate(
            [first_acc[0:1], back_sums_ref[1:2], back_sums_ref[0:1], own_sums_ref[0:1]], 0
        )
        gates = [jnp.tanh(mod_ref[k : k + 1]) for k in (1, 3)]
        into = jnp.concatenate(
            [1.0 + mod_ref[0:1], gates[0], 1.0 + mod_ref[2:3], gates[1]], 0
        )
        d_gains = terms * into
        slope = jnp.concatenate(
            [jnp.ones_like(gates[0]), 1.0 - gates[0] * gates[0]] * 1
            + [jnp.ones_like(gates[0]), 1.0 - gates[1] * gates[1]],
            0,
        )
        d_modulation = terms * gains_ref[0:4] * slope
        heads = head_ref.shape[0]
        width = d_gains.shape[1]
        rows = [head_ref[h] for h in range(heads)], [text_head_ref[h] for h in range(heads)]
        own = jnp.concatenate(
            [
                jnp.concatenate([r[0:2] for r in rows[0]], 1),
                jnp.concatenate([r[0:1] for r in rows[1]], 1),
                jnp.zeros((5, heads * HD), F32),
            ],
            0,
        )
        own = jnp.concatenate([own, jnp.zeros((8, width - heads * HD), F32)], 1)
        row_at = 2 * at_ref[0] + at_ref[1]
        own = pltpu.roll(own, row_at * (heads * HD), 1)
        lane = lax.broadcasted_iota(jnp.int32, (1, width), 1)
        gate_row = jnp.zeros((1, width), F32)
        for h in range(heads):
            total = jnp.sum(rows[1][h][1:2], axis=1, keepdims=True)
            total = total * (1.0 - gate_ref[h] * gate_ref[h])
            gate_row = gate_row + jnp.where(lane == row_at * heads + h, total, 0.0)
        small = jnp.concatenate(
            [d_gains, own[0:3], gate_row, jnp.zeros((24, width), F32)], 0
        )
        for tile in range(12):
            lanes = slice(tile * 128, (tile + 1) * 128)
            first = tile * SHARED
            shared_acc[first : first + 144] = embed_acc[:, lanes].astype(BF16)
            shared_acc[first + 144 : first + 288] = unpatch_sum_ref[:, lanes].astype(BF16)
            shared_acc[first + 288 : first + SHARED] = small[:, lanes].astype(BF16)
        shared_acc[12 * SHARED :] = jnp.zeros((8 * CHUNK - 12 * SHARED, 128), BF16)
        latent = field_of(taps_acc[...], place_ref[...], -1)
        rows = [
            d_modulation[q : q + 1, tile * 128 : (tile + 1) * 128]
            for q in range(4)
            for tile in range(12)
        ]
        for r in range(ROWS):
            ahead = lax.rem(r // 2 - at_ref[0] + 4, 4)
            mods = jnp.concatenate(rows[6 * r : 6 * r + 6] + [jnp.zeros((10, 128), F32)], 0)
            piece = jnp.concatenate(
                [
                    shared_acc[r * CHUNK : (r + 1) * CHUNK],
                    activation_ref[r].astype(BF16),
                    latent[r].astype(BF16),
                    mods.astype(BF16),
                ],
                0,
            )

            @pl.when(at_ref[1] == r % 2)
            def _():
                own_pack_ref[ahead] = piece

            @pl.when(at_ref[1] != r % 2)
            def _():
                other_pack_ref[ahead] = piece


def first_back(
    at, gates, patches, embed, vec, weight, d_raw, d_mid, place, out_sum, unpatch_sum, back_sums, own_sums,
    head, text_head, gains, modulation, activation,
):
    width = embed.shape[1]
    part = weight.shape[2]
    pack = (4, CHUNK + 48, 128)
    grads = (4, 2 * width // COLS, 2 * part)
    rest = (place, out_sum, unpatch_sum, back_sums, own_sums, head, text_head, gains, modulation, activation)
    return pl.pallas_call(
        first_kernel,
        grid_spec=pltpu.PrefetchScalarGridSpec(
            num_scalar_prefetch=2,
            grid=(TOKENS // PAIR,),
            in_specs=[
                lane_block(144, PAIR),
                whole(embed.shape),
                whole(vec.shape),
                whole(weight.shape),
                pl.BlockSpec((3, part, PAIR), lambda t, *_: (0, 0, t)),
                row_block(PAIR, width),
            ]
            + [whole(value.shape) for value in rest],
            out_specs=[pl.BlockSpec(pack, lambda t, *_: (0, 0, 0))] * 2
            + [pl.BlockSpec(grads, lambda t, *_: (0, 0, 0))] * 4,
            scratch_shapes=[
                pltpu.VMEM((144, TOKENS), F32),
                pltpu.VMEM((144, width), F32),
                pltpu.VMEM((8, width), F32),
                pltpu.VMEM((8 * CHUNK, 128), BF16),
                pltpu.VMEM((3, part, width), F32),
                pltpu.VMEM((4, width, part), BF16),
            ],
        ),
        out_shape=[jax.ShapeDtypeStruct(pack, BF16)] * 2 + [jax.ShapeDtypeStruct(grads, BF16)] * 4,
        compiler_params=params(58),
        cost_estimate=LIGHT,
        name="first_back",
    )(at, gates, patches, embed, vec, weight, d_raw, d_mid, *rest)


def local(
    latent, condition, caption, cap_len, cotangent, embed_weight, modulate_weight, norm_gains,
    cross_gate, qkv_weight, text_kv_weight, out_weight, gate_up_weight, down_weight, unpatch_weight,
):
    images, _, _, channels = latent.shape
    width = embed_weight.shape[3]
    local_width = qkv_weight.shape[2]
    heads = local_width // HD
    hidden_width = down_weight.shape[0]
    taps = 9 * channels
    row_at = lax.axis_index("row")
    col_at = lax.axis_index("col")
    at = jnp.stack([row_at // 2, row_at % 2, col_at // 4, col_at % 4]).astype(jnp.int32)
    tile = latent.shape[1] * latent.shape[2] * channels

    cond_low = jax.nn.silu(condition.astype(F32)).astype(BF16)
    mod_piece = jnp.dot(cond_low, modulate_weight, preferred_element_type=F32)
    mod_columns = mod_piece.shape[1]
    mod_high = mod_piece.astype(BF16)
    mod_low = (mod_piece - mod_high.astype(F32)).astype(BF16)

    packed = jnp.concatenate(
        [latent.reshape(images, tile), cotangent.reshape(images, tile), mod_high, mod_low], axis=1
    )
    packed = jnp.pad(packed, ((0, 0), (0, 2 * local_width - packed.shape[1])))

    head_pieces = (
        jnp.concatenate([qkv_weight[0], qkv_weight[1]], axis=1),
        jnp.concatenate([qkv_weight[2], out_weight.T], axis=1),
    )
    first_head = from_col(head_pieces[0], along_z)
    second_head = from_col(head_pieces[1], along_y)
    packed = after(packed, *first_head, *second_head)
    packed = lax.all_to_all(packed, "col", 0, 0, tiled=True)
    first_head = from_col(jnp.stack(first_head), along_y)
    second_head = from_col(jnp.stack(second_head), along_z)
    packed, *reached = lax.optimization_barrier((packed, *first_head, *second_head))
    first_head, second_head = reached[:4], reached[4:]
    packed = send_all(packed, "row")
    qkv_whole, out_rows = unpack_head(at, first_head, second_head)
    out_pieces = from_chips(out_rows)

    text_piece = jnp.concatenate([text_kv_weight[0], text_kv_weight[1]], axis=1)
    text_whole = lax.all_gather(text_piece, "col", axis=0, tiled=True)
    ffn_piece = jnp.concatenate([gate_up_weight[0], gate_up_weight[1], down_weight.T], axis=1)

    patches, cot_taps = image_taps(packed)
    mod_at = 2 * tile
    modulation = packed[:, :, mod_at : mod_at + mod_columns].astype(F32)
    modulation = modulation + packed[:, :, mod_at + mod_columns : mod_at + 2 * mod_columns].astype(F32)
    modulation = modulation.reshape(4, width)
    attn_gate = jnp.tanh(modulation[1])
    ffn_gate = jnp.tanh(modulation[3])
    vec = jnp.stack(
        [
            norm_gains[0] * (1.0 + modulation[0]),
            norm_gains[1] * attn_gate,
            norm_gains[2] * (1.0 + modulation[2]),
            norm_gains[3] * ffn_gate,
        ]
    )
    vec = jnp.pad(vec, ((0, 4), (0, 0)))
    embed = embed_weight.reshape(taps, width)
    unpatch = unpatch_weight.transpose(0, 1, 3, 2).reshape(taps, width)
    raw = qkv_project(patches, embed, vec, qkv_whole)
    raw = raw.reshape(3, heads, HD, TOKENS)
    ffn_whole = lax.all_gather(after(ffn_piece, text_whole, raw), "col", axis=0, tiled=True)
    caption_rows = caption[0]
    text_raw = dot(text_whole, caption_rows, (0, 1)).reshape(2, heads, HD, caption_rows.shape[0])
    head_gains = lax.dynamic_slice(norm_gains, (4, row_at * local_width), (3, local_width)).reshape(
        3, heads, HD, 1
    )
    head_gates = jnp.tanh(lax.dynamic_slice_in_dim(cross_gate, row_at * heads, heads))
    cap = lax.dynamic_slice_in_dim(cap_len, col_at, 1)
    table = jnp.asarray(rope_tables())
    mixed, lse = attend(raw, text_raw, head_gains, table, cap, head_gates)

    mixed_pieces = from_chips(mixed)
    reached = lax.optimization_barrier((*mixed_pieces, *out_pieces))
    mixed_whole = with_other_core(reached[:4])
    out_whole = with_other_core(reached[4:])
    attn, second, gate_up, hidden, ffn_own, ffn_other = forward(
        at, mixed_whole, out_whole, patches, embed, vec, ffn_whole
    )
    place = tile_places(False)
    cot_own = lax.dynamic_slice_in_dim(cot_taps, row_at * BLOCK, BLOCK, 1)
    d_ffn_own, ffn_out = own_grad(
        to_chips(sum_cores(ffn_own, ffn_other)), cot_own, unpatch, vec
    )
    d_ffn_near = from_chips(d_ffn_own)
    activation_field, unpatch_sum, own_sums = own_block(
        at, ffn_out, attn, patches, cot_taps, embed, unpatch, vec, place
    )
    d_ffn_near = lax.optimization_barrier((*d_ffn_near, activation_field))[:4]
    d_ffn, d_gate_up, d_attn, d_mid, mixed_own, mixed_other, back_sums = backward(
        at, with_other_core(d_ffn_near), ffn_whole, out_whole, gate_up, attn, patches, embed, cot_taps,
        unpatch, vec,
    )
    mixed_near = sum_cores(mixed_own, mixed_other)
    mixed_terms = to_chips(mixed_near)
    text_rows = text_kv_weight.shape[1]
    grads, out_near, out_far = weight_grads(
        after(second, *mixed_near), d_gate_up, d_ffn, hidden, mixed_whole, d_attn, text_rows
    )
    *mixed_terms, grads, out_near, out_far = lax.optimization_barrier(
        (*mixed_terms, grads, out_near, out_far)
    )
    d_mixed = sum(term.astype(F32) for term in mixed_terms).astype(BF16)
    d_mixed = d_mixed.reshape(heads, HD, TOKENS)
    out_near = sum_cores(out_near, out_far)
    out_apart = lax.ppermute(out_near[2], "row", row_pairs_to(2, 0))

    grads, dq_text, d_text_head = text_back(
        raw, text_raw, head_gains, table, lse, d_mixed, cap, head_gates, caption_rows,
        after(grads, *out_near),
    )
    dq_text, grads, out_apart, *out_near = lax.optimization_barrier(
        (dq_text, grads, out_apart, *out_near)
    )
    d_raw, d_head = attend_back(raw, head_gains, table, lse, d_mixed, dq_text)
    out_beside = [lax.ppermute(out_near[d], "row", row_pairs_to(d, 0)) for d in (1, 3)]
    d_raw, *out_terms = lax.optimization_barrier((d_raw, out_near[0], out_apart, *out_beside))
    out_sum = sum(term.astype(F32) for term in out_terms)
    d_raw = d_raw.reshape(3, local_width, TOKENS)
    own_pack, other_pack, *head_parts = first_back(
        at, head_gates, patches, embed, vec, qkv_whole, d_raw, d_mid, place, out_sum, unpatch_sum,
        back_sums, own_sums, d_head, d_text_head, norm_gains, modulation, activation_field,
    )
    beside = [lax.ppermute(head_parts[d], "col", col_pairs_to(0, d)) for d in (1, 3)]

    *row_terms, apart, left, right = lax.optimization_barrier(
        (*to_chips(sum_cores(own_pack, other_pack)), head_parts[2], *beside)
    )
    apart = lax.ppermute(apart, "col", col_pairs_to(0, 2))
    row_pack = sum(term.astype(F32) for term in row_terms)
    fields = row_pack[CHUNK : CHUNK + 2 * channels].T.reshape(COLS, 8, 2 * channels)
    mod_sums = row_pack[CHUNK + 2 * channels : CHUNK + 2 * channels + 6].reshape(COLS, 8, 6)
    fields = jnp.concatenate([fields, mod_sums], axis=2).astype(BF16)
    fields = jnp.pad(fields, ((0, 0), (0, 0), (0, 128 - fields.shape[2])))
    shared = row_pack[:CHUNK].astype(BF16).reshape(COLS, CHUNK // COLS, 128)
    col_pack = lax.all_to_all(jnp.concatenate([shared, fields], axis=1), "col", 0, 0)
    col_pack, apart = lax.optimization_barrier((col_pack, apart))
    head_near = sum(term.astype(F32) for term in (head_parts[0], left, apart, right)).astype(BF16)
    shared = jnp.sum(col_pack[:, : CHUNK // COLS].astype(F32), axis=0)
    shared = send_all(send_all(shared.astype(BF16), "col"), "row").reshape(-1, 128)
    shared = shared[: 12 * SHARED].reshape(12, SHARED, 128).astype(F32)
    fields = col_pack[:, CHUNK // COLS :]
    activation = fields[:, :, :channels].reshape(latent.shape)
    latent_grad = fields[:, :, channels : 2 * channels].reshape(latent.shape)
    modulate_grad = lax.dot_general(
        cond_low.astype(F32),
        fields[:, :, 2 * channels : 2 * channels + 6].reshape(images, mod_columns).astype(F32),
        (((0,), (0,)), ((), ())),
        precision=lax.Precision.HIGHEST,
        preferred_element_type=F32,
    )
    embed_grad = shared[:, :taps].transpose(1, 0, 2).reshape(embed_weight.shape)
    unpatch_grad = shared[:, taps : 2 * taps].reshape(12, 3, 3, channels, 128)
    unpatch_grad = unpatch_grad.transpose(1, 2, 0, 4, 3).reshape(unpatch_weight.shape)
    gains_grad = shared[:, 2 * taps : 2 * taps + 7].transpose(1, 0, 2).reshape(7, width)
    gate_grad = shared[0, 2 * taps + 7, :HEADS]

    part = width // COLS
    grads = lax.psum_scatter(
        grads.reshape(-1, 2 * local_width), "col", scatter_dimension=0, tiled=True
    ).astype(F32)
    text_kv_grad = jnp.stack([grads[:text_rows, :local_width], grads[:text_rows, local_width:]])
    ffn_total = jnp.concatenate(
        [grads[first : first + part] for first in range(text_rows, grads.shape[0], part)], axis=1
    )
    gate_up_grad = jnp.stack(
        [ffn_total[:, :hidden_width], ffn_total[:, hidden_width : 2 * hidden_width]]
    )
    down_grad = ffn_total[:, 2 * hidden_width :].T
    head_total = sum(term.astype(F32) for term in along_col(head_near, along_y))
    first, second_half = head_total[:, :local_width], head_total[:, local_width:]
    qkv_grad = jnp.stack([first[:part], second_half[:part], first[part:]])
    out_grad = second_half[part:].T
    return (
        activation, latent_grad, embed_grad, modulate_grad, gains_grad, gate_grad,
        qkv_grad, text_kv_grad, out_grad, gate_up_grad, down_grad, unpatch_grad,
    )


def solution(mesh):
    placed = (
        P(None, "row", "col", None),
        P(),
        P("col", None, None),
        P(),
        P(None, "row", "col", None),
        P(),
        P(None, ("row", "col")),
        P(),
        P(),
        P(None, "col", "row"),
        P(None, "col", "row"),
        P("row", "col"),
        P(None, "col", "row"),
        P("row", "col"),
        P(),
    )
    return jax.shard_map(
        local,
        mesh=mesh,
        in_specs=placed,
        out_specs=(
            P(None, "row", "col", None),
            P(None, "row", "col", None),
            P(),
            P(None, ("row", "col")),
            P(),
            P(),
            P(None, "col", "row"),
            P(None, "col", "row"),
            P("row", "col"),
            P(None, "col", "row"),
            P("row", "col"),
            P(),
        ),
        check_vma=False,
    )
```

```python
import math
from functools import partial

import jax
import jax.numpy as jnp
import numpy as np
from jax import lax
from jax.experimental import pallas as pl
from jax.experimental.pallas import tpu as pltpu
from jax.sharding import PartitionSpec as P

HEADS = 24
HD = 64
GRID = 32
TOKENS = GRID * GRID
EPSILON = 1e-06
ROPE_BASE = 10000.0
MASKED = -1e30
F32 = jnp.float32
BF16 = jnp.bfloat16
ROWS = 8
COLS = 16
QUERY_BLOCK = 256
BLOCK = TOKENS // ROWS
PAIR = 2 * BLOCK
MIB = 2**20
SHARED = 320
CHUNK = 512
LIGHT = pl.CostEstimate(flops=1, bytes_accessed=1, transcendentals=0)


def dot(left, right, contract):
    return lax.dot_general(
        left, right, ((contract[:1], contract[1:]), ((), ())), preferred_element_type=F32
    )


def row_pairs(dx, dc):
    return [
        (((x + dx) % 4) * 2 + (c + dc) % 2, x * 2 + c) for x in range(4) for c in range(2)
    ]


def row_pairs_to(dx, dc):
    return [(dst, src) for src, dst in row_pairs(dx, dc)]


def from_chips(piece):
    return [piece] + [lax.ppermute(piece, "row", row_pairs(d, 0)) for d in (1, 2, 3)]


def with_other_core(pieces):
    quad = jnp.stack(pieces)
    return quad, lax.ppermute(quad, "row", row_pairs(0, 1))


def gather_near(piece):
    return with_other_core(from_chips(piece))


def sum_cores(own, other):
    other = lax.ppermute(other, "row", row_pairs(0, 1))
    return [(own[d].astype(F32) + other[d].astype(F32)).astype(BF16) for d in range(4)]


def to_chips(near):
    return [near[0]] + [lax.ppermute(near[d], "row", row_pairs_to(d, 0)) for d in (1, 2, 3)]


def col_pairs_to(dy, dz):
    return [(y * 4 + z, (y + dy) % 4 * 4 + (z + dz) % 4) for y in range(4) for z in range(4)]


def col_pairs(dy, dz):
    return [(dst, src) for src, dst in col_pairs_to(dy, dz)]


def from_col(piece, step):
    return [piece] + [lax.ppermute(piece, "col", col_pairs(*step(d))) for d in (1, 2, 3)]


def along_y(d):
    return (d, 0)


def along_z(d):
    return (0, d)


def along_col(parts, step):
    return [parts[0]] + [lax.ppermute(parts[d], "col", col_pairs_to(*step(d))) for d in (1, 2, 3)]


def send_all(piece, axis):
    copies = jnp.broadcast_to(piece, (lax.axis_size(axis),) + piece.shape)
    return lax.all_to_all(copies, axis, 0, 0)


def after(value, *others):
    return lax.optimization_barrier((value,) + others)[0]


def rope_tables():
    quarter = HD // 4
    frequency = np.float32(ROPE_BASE) ** (-np.arange(quarter, dtype=np.float32) / np.float32(quarter))
    place = np.arange(TOKENS)
    row = frequency[:, None] * (place // GRID).astype(np.float32)[None, :]
    col = frequency[:, None] * (place % GRID).astype(np.float32)[None, :]
    return np.stack([np.cos(row), np.sin(row), np.cos(col), np.sin(col)]).astype(np.float32)


def turn(v, table, sign):
    a, b, c, d = (v[k * 16 : (k + 1) * 16] for k in range(4))
    cr, sr, cc, sc = table[0], table[1] * sign, table[2], table[3] * sign
    return jnp.concatenate([a * cr - b * sr, a * sr + b * cr, c * cc - d * sc, c * sc + d * cc], 0)


def column_rms(v):
    return lax.rsqrt(jnp.mean(v * v, axis=0, keepdims=True) + EPSILON)


def normed(v, gain):
    return v * column_rms(v) * gain


def column_rms_back(v, u):
    scale = column_rms(v)
    return (u - v * (jnp.mean(u * v, axis=0, keepdims=True) * scale * scale)) * scale


def whole(shape):
    zeros = (0,) * len(shape)
    return pl.BlockSpec(shape, lambda *_: zeros, pipeline_mode=pl.Buffered(1))


def held():
    return pl.BlockSpec(memory_space=pltpu.VMEM)


def lane_block(rows, lanes):
    return pl.BlockSpec((rows, lanes), lambda t, *_: (0, t))


def row_block(rows, lanes):
    return pl.BlockSpec((rows, lanes), lambda t, *_: (t, 0))


def params(mib):
    return pltpu.CompilerParams(vmem_limit_bytes=mib * MIB, dimension_semantics=("arbitrary",))


def row_of_sums(v):
    return jnp.sum(v.T, axis=0, keepdims=True)


def attend_kernel(
    cap_ref, gate_ref, raw_ref, text_ref, gain_ref, table_ref, mixed_ref, lse_ref,
    q_ref, k_ref, v_ref, tk_ref, tv_ref,
):
    step = pl.program_id(0)
    heads = raw_ref.shape[1]

    @pl.when(step == 0)
    def _():
        table = table_ref[...]
        for h in range(heads):
            q = turn(normed(raw_ref[0, h], gain_ref[0, h]), table, 1.0).astype(BF16)
            q_ref[h] = q * jnp.asarray(0.125, BF16)
            k_ref[h] = turn(normed(raw_ref[1, h], gain_ref[1, h]), table, 1.0).T.astype(BF16)
            v_ref[h] = raw_ref[2, h].astype(BF16)
            tk_ref[h] = normed(text_ref[0, h], gain_ref[2, h]).T.astype(BF16)
            tv_ref[h] = text_ref[1, h].astype(BF16)

    slots = tk_ref.shape[1]
    mask = lax.broadcasted_iota(jnp.int32, (slots, QUERY_BLOCK), 0) < cap_ref[0]
    here = pl.ds(pl.multiple_of(step * QUERY_BLOCK, QUERY_BLOCK), QUERY_BLOCK)
    outs = []
    for h in range(heads):
        qb = q_ref[h, :, here]
        e = jnp.exp(dot(k_ref[h], qb, (1, 0)))
        total = jnp.sum(e, axis=0, keepdims=True)
        own = dot(v_ref[h], e.astype(BF16), (1, 0)) / total
        te = jnp.exp(jnp.where(mask, dot(tk_ref[h], qb, (1, 0)), MASKED))
        text_total = jnp.sum(te, axis=0, keepdims=True)
        text = dot(tv_ref[h], te.astype(BF16), (1, 0)) / text_total
        outs.append(own + gate_ref[h] * text)
        lse_ref[h, 0:1] = jnp.log(total)
        lse_ref[h, 1:2] = jnp.log(text_total)
    mixed_ref[...] = jnp.concatenate(outs, 0).astype(BF16)


def attend(raw, text_raw, gains, table, cap, gates):
    heads = raw.shape[1]
    slots = text_raw.shape[3]
    return pl.pallas_call(
        attend_kernel,
        grid_spec=pltpu.PrefetchScalarGridSpec(
            num_scalar_prefetch=2,
            grid=(TOKENS // QUERY_BLOCK,),
            in_specs=[
                whole((3, heads, HD, TOKENS)),
                whole((2, heads, HD, slots)),
                whole((3, heads, HD, 1)),
                whole((4, 16, TOKENS)),
            ],
            out_specs=[
                lane_block(heads * HD, QUERY_BLOCK),
                pl.BlockSpec((heads, 8, QUERY_BLOCK), lambda t, *_: (0, 0, t)),
            ],
            scratch_shapes=[
                pltpu.VMEM((heads, HD, TOKENS), BF16),
                pltpu.VMEM((heads, TOKENS, HD), BF16),
                pltpu.VMEM((heads, HD, TOKENS), BF16),
                pltpu.VMEM((heads, slots, HD), BF16),
                pltpu.VMEM((heads, HD, slots), BF16),
            ],
        ),
        out_shape=[
            jax.ShapeDtypeStruct((heads * HD, TOKENS), BF16),
            jax.ShapeDtypeStruct((heads, 8, TOKENS), F32),
        ],
        compiler_params=params(20),
        cost_estimate=LIGHT,
        name="attend",
    )(cap, gates, raw, text_raw, gains, table)


def text_back_kernel(
    cap_ref, gate_ref, q_raw_ref, text_ref, gain_ref, table_ref, lse_ref, grad_ref, caption_ref, held_ref,
    grads_ref, dq_ref, d_gain_ref, low_ref,
):
    del held_ref
    step = pl.program_id(0)
    heads, _, slots = low_ref.shape[1:]

    @pl.when(step == 0)
    def _():
        table = table_ref[...]
        mask = lax.broadcasted_iota(jnp.int32, (slots, TOKENS), 0) < cap_ref[0]
        for h in range(heads):
            gate = gate_ref[h]
            q = turn(normed(q_raw_ref[h], gain_ref[0, h]), table, 1.0).astype(BF16)
            q = q * jnp.asarray(0.125, BF16)
            tk = normed(text_ref[0, h], gain_ref[2, h]).astype(BF16)
            tv = text_ref[1, h].astype(BF16)
            g = grad_ref[h]
            tp = jnp.exp(jnp.where(mask, dot(tk, q, (0, 0)), MASKED) - lse_ref[h, 1:2])
            tpb = tp.astype(BF16)
            low_ref[1, h] = (dot(g, tpb, (1, 1)) * gate).astype(BF16)
            gate_terms = g.astype(F32) * dot(tv, tpb, (1, 0))
            tpd = tp * dot(tv, g, (0, 0)) * gate
            dts = (tpd - tp * jnp.sum(tpd, axis=0, keepdims=True)).astype(BF16)
            dq_ref[h] = dot(tk, dts, (1, 0))
            d_tk = dot(q, dts, (1, 1))
            values = text_ref[0, h]
            low_ref[0, h] = column_rms_back(values, d_tk * gain_ref[2, h]).astype(BF16)
            d_gain_ref[h, 0:1] = row_of_sums(values * column_rms(values) * d_tk)
            d_gain_ref[h, 1:2] = row_of_sums(gate_terms)

    d_text = low_ref[...].reshape(2 * heads * HD, slots)
    rows = grads_ref.shape[1]
    for k in range(grads_ref.shape[0]):
        grads_ref[k] = dot(caption_ref[:, k * rows : (k + 1) * rows], d_text, (0, 1)).astype(BF16)


def text_back(raw, text_raw, gains, table, lse, grads, cap, gates, caption, held):
    heads = raw.shape[1]
    slots = text_raw.shape[3]
    rows = caption.shape[1] // COLS
    lanes = 2 * heads * HD
    return pl.pallas_call(
        text_back_kernel,
        grid_spec=pltpu.PrefetchScalarGridSpec(
            num_scalar_prefetch=2,
            grid=(4,),
            in_specs=[
                pl.BlockSpec((None, heads, HD, TOKENS), lambda t, *_: (0, 0, 0, 0)),
                whole(text_raw.shape),
                whole(gains.shape),
                whole(table.shape),
                whole(lse.shape),
                whole(grads.shape),
                pl.BlockSpec((slots, 4 * rows), lambda t, *_: (0, t)),
                pl.BlockSpec(memory_space=pl.ANY),
            ],
            out_specs=[
                pl.BlockSpec((4, rows, lanes), lambda t, *_: (t, 0, 0)),
                pl.BlockSpec((heads, HD, TOKENS), lambda t, *_: (0, 0, 0)),
                pl.BlockSpec((heads, 8, HD), lambda t, *_: (0, 0, 0)),
            ],
            scratch_shapes=[pltpu.VMEM((2, heads, HD, slots), BF16)],
        ),
        out_shape=[
            jax.ShapeDtypeStruct(held.shape, BF16),
            jax.ShapeDtypeStruct((heads, HD, TOKENS), F32),
            jax.ShapeDtypeStruct((heads, 8, HD), F32),
        ],
        input_output_aliases={9: 0},
        compiler_params=params(58),
        cost_estimate=LIGHT,
        name="text_back",
    )(cap, gates, raw, text_raw, gains, table, lse, grads, caption, held)


def attend_back_kernel(
    raw_ref, gain_ref, table_ref, lse_ref, grad_ref, dq_text_ref,
    d_raw_ref, d_gain_ref, dv_ref, dk_ref, dq_ref,
):
    table = table_ref[...]
    q = turn(normed(raw_ref[0], gain_ref[0]), table, 1.0).astype(BF16) * jnp.asarray(0.125, BF16)
    k = turn(normed(raw_ref[1], gain_ref[1]), table, 1.0)
    k, k_turned = k.astype(BF16), k.T.astype(BF16)
    v_turned = raw_ref[2].T.astype(BF16)
    for first in range(0, TOKENS, QUERY_BLOCK):
        here = slice(first, first + QUERY_BLOCK)
        qb = q[:, here]
        gb = grad_ref[:, here]
        p = jnp.exp(dot(k_turned, qb, (1, 0)) - lse_ref[0:1, here])
        dv = dot(gb, p.astype(BF16), (1, 1))
        pd = p * dot(v_turned, gb, (1, 0))
        ds = (pd - p * jnp.sum(pd, axis=0, keepdims=True)).astype(BF16)
        dq_ref[:, here] = dot(k, ds, (1, 0)) + dq_text_ref[:, here]
        dk = dot(qb, ds, (1, 1))
        if first == 0:
            dv_ref[...] = dv
            dk_ref[...] = dk
        else:
            dv_ref[...] += dv
            dk_ref[...] += dk

    def raw_back(which, d_turned):
        spun = turn(d_turned.astype(BF16).astype(F32), table, -1.0)
        values = raw_ref[which]
        d_raw_ref[which] = column_rms_back(values, spun * gain_ref[which]).astype(BF16)
        d_gain_ref[which : which + 1] = row_of_sums(values * column_rms(values) * spun)

    raw_back(0, dq_ref[...] * 0.125)
    raw_back(1, dk_ref[...])
    d_raw_ref[2] = dv_ref[...].astype(BF16)


def attend_back(raw, gains, table, lse, grads, dq_text):
    heads = raw.shape[1]
    return pl.pallas_call(
        attend_back_kernel,
        grid=(heads,),
        in_specs=[
            pl.BlockSpec((3, None, HD, TOKENS), lambda h: (0, h, 0, 0)),
            pl.BlockSpec((3, None, HD, 1), lambda h: (0, h, 0, 0)),
            pl.BlockSpec((4, 16, TOKENS), lambda h: (0, 0, 0)),
            pl.BlockSpec((None, 8, TOKENS), lambda h: (h, 0, 0)),
            pl.BlockSpec((None, HD, TOKENS), lambda h: (h, 0, 0)),
            pl.BlockSpec((None, HD, TOKENS), lambda h: (h, 0, 0)),
        ],
        out_specs=[
            pl.BlockSpec((3, None, HD, TOKENS), lambda h: (0, h, 0, 0)),
            pl.BlockSpec((None, 8, HD), lambda h: (h, 0, 0)),
        ],
        scratch_shapes=[pltpu.VMEM((HD, TOKENS), F32) for _ in range(3)],
        out_shape=[
            jax.ShapeDtypeStruct((3, heads, HD, TOKENS), BF16),
            jax.ShapeDtypeStruct((heads, 8, HD), F32),
        ],
        compiler_params=params(58),
        cost_estimate=LIGHT,
        name="attend_back",
    )(raw, gains, table, lse, grads, dq_text)


def tile_places(chunk_first):
    r, c, k = np.meshgrid(np.arange(ROWS), np.arange(COLS), np.arange(8), indexing="ij")
    token = r * BLOCK + (k // 2) * GRID + c * 2 + k % 2
    source = (k * ROWS + r) * COLS + c if chunk_first else (r * COLS + c) * 8 + k
    places = np.zeros((TOKENS, TOKENS), np.float32)
    places[source.ravel(), token.ravel()] = 1.0
    return jnp.asarray(places, BF16)


def grid_shift(field, di, dj):
    step = di * GRID + dj
    moved = pltpu.roll(field, (-step) % TOKENS, 1) if step else field
    place = lax.broadcasted_iota(jnp.int32, field.shape, 1)
    row = place // GRID + di
    col = place % GRID + dj
    inside = (row >= 0) & (row < GRID) & (col >= 0) & (col < GRID)
    return jnp.where(inside, moved, 0.0)


def image_kernel(packed_ref, place_ref, patch_ref, cot_ref):
    for which, sign, out_ref in ((0, 1, patch_ref), (1, -1, cot_ref)):
        lanes = slice(which * 128, (which + 1) * 128)
        tiles = jnp.concatenate([packed_ref[r, :, lanes] for r in range(ROWS)], 0)
        turned = tiles.astype(F32).T
        chunks = jnp.concatenate([turned[k * 16 : (k + 1) * 16] for k in range(8)], 1)
        image = dot(chunks.astype(BF16), place_ref[...], (1, 0))
        for a in range(3):
            for b in range(3):
                first = (a * 3 + b) * 16
                out_ref[first : first + 16] = grid_shift(
                    image, sign * (a - 1), sign * (b - 1)
                ).astype(BF16)


def image_taps(packed):
    out = jax.ShapeDtypeStruct((144, TOKENS), BF16)
    return pl.pallas_call(
        image_kernel,
        out_shape=[out, out],
        compiler_params=pltpu.CompilerParams(vmem_limit_bytes=12 * MIB),
        cost_estimate=LIGHT,
        name="image_taps",
    )(packed, tile_places(True))


def field_of(taps, place, sign):
    total = jnp.zeros((16, TOKENS), F32)
    for a in range(3):
        for b in range(3):
            first = (a * 3 + b) * 16
            total = total + grid_shift(taps[first : first + 16], sign * (a - 1), sign * (b - 1))
    tiles = dot(total.astype(BF16), place, (1, 1))
    return [tiles[:, r * BLOCK : (r + 1) * BLOCK] for r in range(ROWS)]


def row_rms(v):
    return lax.rsqrt(jnp.mean(v * v, axis=-1, keepdims=True) + EPSILON)


def row_rms_back(v, scale, u):
    return (u - v * (jnp.mean(u * v, axis=-1, keepdims=True) * scale * scale)) * scale


def unpack_kernel(at_ref, *refs):
    piece_refs, (joined_ref, out_ref, turn_ref) = refs[:4], refs[4:]
    part = piece_refs[0].shape[1] // 2
    local_width = piece_refs[0].shape[2] // 2
    for dz in range(4):
        for dy in range(4):
            c = lax.rem(at_ref[2] + dy, 4) * 4 + lax.rem(at_ref[3] + dz, 4)
            rows = pl.ds(pl.multiple_of(c * part, part), part)
            piece = piece_refs[dz][dy]
            joined_ref[0, rows, :] = piece[:part, :local_width]
            joined_ref[1, rows, :] = piece[:part, local_width:]
            joined_ref[2, rows, :] = piece[part:, :local_width]
            turn_ref[rows, :] = piece[part:, local_width:]
    out_ref[...] = turn_ref[...].T


def unpack_head(at, pieces):
    _, rows, lanes = pieces[0].shape
    width, local_width = COLS * rows // 2, lanes // 2
    return pl.pallas_call(
        unpack_kernel,
        grid_spec=pltpu.PrefetchScalarGridSpec(
            num_scalar_prefetch=1,
            grid=(1,),
            in_specs=[whole(pieces[0].shape)] * 4,
            out_specs=[
                pl.BlockSpec((3, width, local_width), lambda t, at: (0, 0, 0)),
                pl.BlockSpec((local_width, width), lambda t, at: (0, 0)),
            ],
            scratch_shapes=[pltpu.VMEM((width, local_width), BF16)],
        ),
        out_shape=[
            jax.ShapeDtypeStruct((3, width, local_width), BF16),
            jax.ShapeDtypeStruct((local_width, width), BF16),
        ],
        compiler_params=params(14),
        cost_estimate=LIGHT,
        name="unpack_head",
    )(at, *pieces)


def text_kernel(at_ref, p0_ref, p1_ref, p2_ref, p3_ref, caption_ref, raw_ref):
    rows = p0_ref.shape[1]
    total = 0.0
    for dy, ref in enumerate((p0_ref, p1_ref, p2_ref, p3_ref)):
        for dz in range(4):
            c = lax.rem(at_ref[2] + dy, 4) * 4 + lax.rem(at_ref[3] + dz, 4)
            lanes = pl.ds(pl.multiple_of(c * rows, rows), rows)
            total = total + dot(ref[dz], caption_ref[:, lanes], (0, 1))
    raw_ref[...] = total


def text_project(at, pieces, caption):
    lanes = pieces[0].shape[2]
    slots = caption.shape[0]
    return pl.pallas_call(
        text_kernel,
        grid_spec=pltpu.PrefetchScalarGridSpec(
            num_scalar_prefetch=1,
            grid=(1,),
            in_specs=[whole(pieces[0].shape)] * 4 + [whole(caption.shape)],
            out_specs=pl.BlockSpec((lanes, slots), lambda t, at: (0, 0)),
        ),
        out_shape=jax.ShapeDtypeStruct((lanes, slots), F32),
        compiler_params=params(16),
        cost_estimate=LIGHT,
        name="text_project",
    )(at, *pieces, caption)


def qkv_kernel(patch_ref, embed_ref, vec_ref, weight_ref, raw_ref):
    x = dot(patch_ref[...], embed_ref[...], (0, 0))
    h = (x * row_rms(x) * vec_ref[0:1]).astype(BF16)
    for s in range(3):
        raw_ref[s] = dot(h, weight_ref[s], (1, 0)).T


def qkv_project(patches, embed, vec, weight):
    part = weight.shape[2]
    return pl.pallas_call(
        qkv_kernel,
        grid=(TOKENS // PAIR,),
        in_specs=[lane_block(144, PAIR), whole(embed.shape), whole(vec.shape), whole(weight.shape)],
        out_specs=pl.BlockSpec((3, part, PAIR), lambda t: (0, 0, t)),
        out_shape=jax.ShapeDtypeStruct((3, part, TOKENS), F32),
        compiler_params=params(16),
        cost_estimate=LIGHT,
        name="qkv_project",
    )(patches, embed, vec, weight)


def joined(ref):
    return ref[...].reshape(-1, ref.shape[2])


def halves(core, first, second):
    return jnp.where(core == 0, first, second)


def forward_kernel(
    at_ref, near_ref, far_ref, out_near_ref, out_far_ref, patch_ref, embed_ref, vec_ref, ffn_ref,
    attn_ref, second_ref, gate_up_ref, hidden_ref, own_ref, other_ref,
):
    core = at_ref[1]
    hidden_width = hidden_ref.shape[1]
    x = dot(patch_ref[...], embed_ref[...], (0, 0))
    attn = dot(joined(near_ref), joined(out_near_ref), (0, 0))
    attn = attn + dot(joined(far_ref), joined(out_far_ref), (0, 0))
    attn_ref[...] = attn.astype(BF16)
    mid = x + vec_ref[1:2] * (attn * row_rms(attn))
    second = (mid * row_rms(mid) * vec_ref[2:3]).astype(BF16)
    second_ref[...] = second
    gate_up = dot(second, ffn_ref[:, : 2 * hidden_width], (1, 0))
    gate_up_ref[...] = gate_up.astype(BF16)
    gate = gate_up[:, :hidden_width]
    hidden = (gate * jax.nn.sigmoid(gate) * gate_up[:, hidden_width:]).astype(BF16)
    hidden_ref[...] = hidden
    part = dot(hidden, ffn_ref[:, 2 * hidden_width :], (1, 1)).astype(BF16)
    own_ref[0] = halves(core, part[:BLOCK], part[BLOCK:])
    other_ref[0] = halves(core, part[BLOCK:], part[:BLOCK])


def forward(at, mixed, out_whole, patches, embed, vec, ffn):
    width = embed.shape[1]
    part = mixed[0].shape[1]
    hidden_width = ffn.shape[1] // 3
    by_chip = pl.BlockSpec((1, BLOCK, width), lambda t, at: ((t - at[0] + 4) % 4, 0, 0))
    return pl.pallas_call(
        forward_kernel,
        grid_spec=pltpu.PrefetchScalarGridSpec(
            num_scalar_prefetch=1,
            grid=(4,),
            in_specs=[
                pl.BlockSpec((4, part, PAIR), lambda t, at: (0, 0, t)),
                pl.BlockSpec((4, part, PAIR), lambda t, at: (0, 0, t)),
                whole((4, part, width)),
                whole((4, part, width)),
                lane_block(144, PAIR),
                whole(embed.shape),
                whole(vec.shape),
                whole(ffn.shape),
            ],
            out_specs=[
                row_block(PAIR, width),
                row_block(PAIR, width),
                row_block(PAIR, 2 * hidden_width),
                row_block(PAIR, hidden_width),
                by_chip,
                by_chip,
            ],
        ),
        out_shape=[
            jax.ShapeDtypeStruct((TOKENS, width), BF16),
            jax.ShapeDtypeStruct((TOKENS, width), BF16),
            jax.ShapeDtypeStruct((TOKENS, 2 * hidden_width), BF16),
            jax.ShapeDtypeStruct((TOKENS, hidden_width), BF16),
            jax.ShapeDtypeStruct((4, BLOCK, width), BF16),
            jax.ShapeDtypeStruct((4, BLOCK, width), BF16),
        ],
        compiler_params=params(56),
        cost_estimate=LIGHT,
        name="forward",
    )(at, *mixed, *out_whole, patches, embed, vec, ffn)


def own_grad_kernel(p0_ref, p1_ref, p2_ref, p3_ref, cot_ref, unpatch_ref, vec_ref, d_ffn_ref, ffn_ref):
    ffn = sum(p[...].astype(F32) for p in (p0_ref, p1_ref, p2_ref, p3_ref))
    ffn_ref[...] = ffn
    d_last = dot(cot_ref[...], unpatch_ref[...], (0, 0))
    d_ffn_ref[...] = row_rms_back(ffn, row_rms(ffn), vec_ref[3:4] * d_last).astype(BF16)


def own_grad(pieces, cot_own, unpatch, vec):
    shape = (BLOCK, unpatch.shape[1])
    return pl.pallas_call(
        own_grad_kernel,
        out_shape=[jax.ShapeDtypeStruct(shape, BF16), jax.ShapeDtypeStruct(shape, F32)],
        compiler_params=pltpu.CompilerParams(vmem_limit_bytes=12 * MIB),
        cost_estimate=LIGHT,
        name="own_grad",
    )(*pieces, cot_own, unpatch, vec)


def own_kernel(
    at_ref, ffn_ref, attn_ref, patch_ref, cot_ref, embed_ref, unpatch_ref, vec_ref, place_ref,
    field_ref, unpatch_sum_ref, sums_ref, taps_ref,
):
    ffn = ffn_ref[...]
    d_last = dot(cot_ref[...], unpatch_ref[...], (0, 0))
    normed_ffn = ffn * row_rms(ffn)
    sums_ref[...] = jnp.broadcast_to(
        jnp.sum(normed_ffn * d_last, axis=0, keepdims=True), sums_ref.shape
    )
    attn = attn_ref[...].astype(F32)
    x = dot(patch_ref[...], embed_ref[...], (0, 0))
    last = (x + vec_ref[1:2] * (attn * row_rms(attn)) + vec_ref[3:4] * normed_ffn).astype(BF16)
    unpatch_sum_ref[...] = dot(cot_ref[...], last, (1, 0))
    taps_ref[...] = jnp.zeros_like(taps_ref)
    here = pl.multiple_of((2 * at_ref[0] + at_ref[1]) * BLOCK, BLOCK)
    taps_ref[:, pl.ds(here, BLOCK)] = dot(unpatch_ref[...], last, (1, 1))
    for r, tile in enumerate(field_of(taps_ref[...], place_ref[...], 1)):
        field_ref[r] = tile


def own_block(at, ffn, attn, patches, cot_taps, embed, unpatch, vec, place):
    width = embed.shape[1]
    lanes = pl.BlockSpec((144, BLOCK), lambda t, at: (0, 2 * at[0] + at[1]))
    return pl.pallas_call(
        own_kernel,
        grid_spec=pltpu.PrefetchScalarGridSpec(
            num_scalar_prefetch=1,
            grid=(1,),
            in_specs=[
                whole((BLOCK, width)),
                pl.BlockSpec((BLOCK, width), lambda t, at: (2 * at[0] + at[1], 0)),
                lanes,
                lanes,
                whole(embed.shape),
                whole(unpatch.shape),
                whole(vec.shape),
                whole(place.shape),
            ],
            out_specs=[
                pl.BlockSpec((ROWS, 16, BLOCK), lambda t, at: (0, 0, 0)),
                pl.BlockSpec((144, width), lambda t, at: (0, 0)),
                pl.BlockSpec((8, width), lambda t, at: (0, 0)),
            ],
            scratch_shapes=[pltpu.VMEM((144, TOKENS), F32)],
        ),
        out_shape=[
            jax.ShapeDtypeStruct((ROWS, 16, BLOCK), F32),
            jax.ShapeDtypeStruct((144, width), F32),
            jax.ShapeDtypeStruct((8, width), F32),
        ],
        compiler_params=params(14),
        cost_estimate=LIGHT,
        name="own_block",
    )(at, ffn, attn, patches, cot_taps, embed, unpatch, vec, place)


def backward_kernel(
    at_ref, own_ref, other_ref, ffn_ref, out_near_ref, out_far_ref, gate_up_ref, attn_ref,
    patch_ref, embed_ref, cot_ref, unpatch_ref, vec_ref,
    d_ffn_ref, d_gate_up_ref, d_attn_ref, d_mid_ref, mixed_own_ref, mixed_other_ref, sums_ref,
):
    step = pl.program_id(0)
    chip, core = at_ref[0], at_ref[1]
    hidden_width = d_gate_up_ref.shape[1] // 2
    own, other = own_ref[0], other_ref[0]
    d_ffn = jnp.concatenate([halves(core, own, other), halves(core, other, own)], 0)
    d_ffn_ref[...] = d_ffn
    d_hidden = dot(d_ffn, ffn_ref[:, 2 * hidden_width :], (1, 0))
    gate = gate_up_ref[:, :hidden_width].astype(F32)
    up = gate_up_ref[:, hidden_width:].astype(F32)
    sigma = jax.nn.sigmoid(gate)
    silu = gate * sigma
    d_gate = d_hidden * up * (sigma + silu * (1.0 - sigma))
    d_gate_up = jnp.concatenate([d_gate.astype(BF16), (d_hidden * silu).astype(BF16)], 1)
    d_gate_up_ref[...] = d_gate_up
    d_second = dot(d_gate_up, ffn_ref[:, : 2 * hidden_width], (1, 1))

    x = dot(patch_ref[...], embed_ref[...], (0, 0))
    attn = attn_ref[...].astype(F32)
    attn_scale = row_rms(attn)
    attn_normed = attn * attn_scale
    mid = x + vec_ref[1:2] * attn_normed
    mid_scale = row_rms(mid)
    mid_sum = jnp.sum(mid * mid_scale * d_second, axis=0, keepdims=True)
    d_last = dot(cot_ref[...], unpatch_ref[...], (0, 0))
    place = lax.broadcasted_iota(jnp.int32, (PAIR, 1), 0) // BLOCK
    mine = (place == core) & (step == chip)
    d_mid = row_rms_back(mid, mid_scale, vec_ref[2:3] * d_second) + jnp.where(mine, d_last, 0.0)
    d_mid_ref[...] = d_mid.astype(BF16)
    attn_sum = jnp.sum(attn_normed * d_mid, axis=0, keepdims=True)
    d_attn = row_rms_back(attn, attn_scale, vec_ref[1:2] * d_mid).astype(BF16)
    d_attn_ref[...] = d_attn
    for weight_ref, part_ref in ((out_near_ref, mixed_own_ref), (out_far_ref, mixed_other_ref)):
        part_ref[...] = dot(joined(weight_ref), d_attn, (1, 1)).astype(BF16).reshape(part_ref.shape)

    @pl.when(step == 0)
    def _():
        sums_ref[...] = jnp.zeros_like(sums_ref)

    sums_ref[0:1] += mid_sum
    sums_ref[1:2] += attn_sum


def backward(at, d_ffn, ffn, out_whole, gate_up, attn, patches, embed, cot_taps, unpatch, vec):
    width = embed.shape[1]
    part = out_whole[0].shape[1]
    hidden_width = ffn.shape[1] // 3
    by_chip = pl.BlockSpec((1, BLOCK, width), lambda t, at: ((t - at[0] + 4) % 4, 0, 0))
    parts = pl.BlockSpec((4, part, PAIR), lambda t, at: (0, 0, t))
    return pl.pallas_call(
        backward_kernel,
        grid_spec=pltpu.PrefetchScalarGridSpec(
            num_scalar_prefetch=1,
            grid=(4,),
            in_specs=[
                by_chip,
                by_chip,
                held(),
                held(),
                held(),
                row_block(PAIR, 2 * hidden_width),
                row_block(PAIR, width),
                lane_block(144, PAIR),
                whole(embed.shape),
                lane_block(144, PAIR),
                whole(unpatch.shape),
                whole(vec.shape),
            ],
            out_specs=[
                row_block(PAIR, width),
                row_block(PAIR, 2 * hidden_width),
                row_block(PAIR, width),
                row_block(PAIR, width),
                parts,
                parts,
                pl.BlockSpec((8, width), lambda t, at: (0, 0)),
            ],
        ),
        out_shape=[
            jax.ShapeDtypeStruct((TOKENS, width), BF16),
            jax.ShapeDtypeStruct((TOKENS, 2 * hidden_width), BF16),
            jax.ShapeDtypeStruct((TOKENS, width), BF16),
            jax.ShapeDtypeStruct((TOKENS, width), BF16),
            jax.ShapeDtypeStruct((4, part, TOKENS), BF16),
            jax.ShapeDtypeStruct((4, part, TOKENS), BF16),
            jax.ShapeDtypeStruct((8, width), F32),
        ],
        compiler_params=params(32),
        cost_estimate=LIGHT,
        name="backward",
    )(at, *d_ffn, ffn, *out_whole, gate_up, attn, patches, embed, cot_taps, unpatch, vec)


def weight_kernel(
    second_ref, d_gate_up_ref, d_ffn_ref, hidden_ref, near_ref, far_ref, d_attn_ref,
    grads_ref, out_near_ref, out_far_ref,
):
    step = pl.program_id(0)
    chunk, _, lanes = grads_ref.shape[0] // 4, *grads_ref.shape[1:]
    part = second_ref.shape[1] // chunk
    rows = jnp.concatenate(
        [
            dot(second_ref[...], d_gate_up_ref[...], (0, 0)).astype(BF16),
            dot(d_ffn_ref[...], hidden_ref[...], (0, 0)).astype(BF16),
        ],
        1,
    )
    groups = rows.shape[1] // lanes
    first = grads_ref.shape[1] - groups * part
    for c in range(chunk):
        for g in range(groups):
            grads_ref[step * chunk + c, first + g * part : first + (g + 1) * part] = rows[
                c * part : (c + 1) * part, g * lanes : (g + 1) * lanes
            ]
    out_near_ref[0] = dot(near_ref[0], d_attn_ref[...], (1, 0)).astype(BF16)
    out_far_ref[0] = dot(far_ref[0], d_attn_ref[...], (1, 0)).astype(BF16)


def weight_grads(second, d_gate_up, d_ffn, hidden, mixed, d_attn, text_rows):
    width = second.shape[1]
    heads_width = mixed[0].shape[1]
    lanes = 2 * heads_width
    grads = (COLS, text_rows + width // COLS * 3 * hidden.shape[1] // lanes, lanes)
    pieces = pl.BlockSpec((1, heads_width, TOKENS), lambda t: (t, 0, 0))
    out_piece = pl.BlockSpec((1, heads_width, width), lambda t: (t, 0, 0))
    out_shape = jax.ShapeDtypeStruct((4, heads_width, width), BF16)
    return pl.pallas_call(
        weight_kernel,
        grid=(4,),
        in_specs=[
            lane_block(TOKENS, width // 4),
            whole(d_gate_up.shape),
            lane_block(TOKENS, width // 4),
            whole(hidden.shape),
            pieces,
            pieces,
            whole(d_attn.shape),
        ],
        out_specs=[pl.BlockSpec(grads, lambda t: (0, 0, 0)), out_piece, out_piece],
        out_shape=[jax.ShapeDtypeStruct(grads, BF16), out_shape, out_shape],
        compiler_params=params(40),
        cost_estimate=LIGHT,
        name="weight_grads",
    )(second, d_gate_up, d_ffn, hidden, *mixed, d_attn)


def first_kernel(
    at_ref, gate_ref, patch_ref, embed_ref, vec_ref, weight_ref, d_raw_ref, d_mid_ref, place_ref, out_sum_ref,
    unpatch_sum_ref, back_sums_ref, own_sums_ref, head_ref, text_head_ref, gains_ref, mod_ref, activation_ref,
    own_pack_ref, other_pack_ref, p0_ref, p1_ref, p2_ref, p3_ref,
    taps_acc, embed_acc, first_acc, shared_acc, qkv_acc, turned_acc,
):
    step = pl.program_id(0)
    last = pl.num_programs(0) - 1
    x = dot(patch_ref[...], embed_ref[...], (0, 0))
    scale = row_rms(x)
    x_normed = x * scale
    h = (x_normed * vec_ref[0:1]).astype(BF16)
    d_h = dot(d_raw_ref[0], weight_ref[0], (0, 1))
    for s in (1, 2):
        d_h = d_h + dot(d_raw_ref[s], weight_ref[s], (0, 1))

    @pl.when(step == 0)
    def _():
        qkv_acc[...] = jnp.zeros_like(qkv_acc)
        embed_acc[...] = jnp.zeros_like(embed_acc)
        first_acc[...] = jnp.zeros_like(first_acc)

    qkv_acc[...] += dot(joined(d_raw_ref), h, (1, 0)).reshape(qkv_acc.shape)
    first_acc[0:1] += jnp.sum(x_normed * d_h, axis=0, keepdims=True)
    d_first = (d_mid_ref[...].astype(F32) + row_rms_back(x, scale, vec_ref[0:1] * d_h)).astype(BF16)
    embed_acc[...] += dot(patch_ref[...], d_first, (1, 0))
    here = pl.ds(pl.multiple_of(step * PAIR, PAIR), PAIR)
    taps_acc[:, here] = dot(embed_ref[...], d_first, (1, 1))

    @pl.when(step == last)
    def _():
        part = p0_ref.shape[1] // 2
        for s in range(4):
            turned_acc[s] = (qkv_acc[s] if s < 3 else out_sum_ref[...]).T.astype(BF16)
        for dz, ref in enumerate((p0_ref, p1_ref, p2_ref, p3_ref)):
            z = lax.rem(at_ref[3] + dz, 4)
            for y in range(4):
                dy = lax.rem(y - at_ref[2] + 4, 4)
                first = pl.multiple_of((y * 4 + z) * part, part)
                pieces = [turned_acc[s, pl.ds(first, part), :] for s in range(4)]
                for k in range(2):
                    ref[dy, k * part : (k + 1) * part] = jnp.concatenate(
                        pieces[2 * k : 2 * k + 2], 1
                    )
        terms = jnp.concatenate(
            [first_acc[0:1], back_sums_ref[1:2], back_sums_ref[0:1], own_sums_ref[0:1]], 0
        )
        gates = [jnp.tanh(mod_ref[k : k + 1]) for k in (1, 3)]
        into = jnp.concatenate(
            [1.0 + mod_ref[0:1], gates[0], 1.0 + mod_ref[2:3], gates[1]], 0
        )
        d_gains = terms * into
        slope = jnp.concatenate(
            [jnp.ones_like(gates[0]), 1.0 - gates[0] * gates[0]] * 1
            + [jnp.ones_like(gates[0]), 1.0 - gates[1] * gates[1]],
            0,
        )
        d_modulation = terms * gains_ref[0:4] * slope
        heads = head_ref.shape[0]
        width = d_gains.shape[1]
        rows = [head_ref[h] for h in range(heads)], [text_head_ref[h] for h in range(heads)]
        own = jnp.concatenate(
            [
                jnp.concatenate([r[0:2] for r in rows[0]], 1),
                jnp.concatenate([r[0:1] for r in rows[1]], 1),
                jnp.zeros((5, heads * HD), F32),
            ],
            0,
        )
        own = jnp.concatenate([own, jnp.zeros((8, width - heads * HD), F32)], 1)
        row_at = 2 * at_ref[0] + at_ref[1]
        own = pltpu.roll(own, row_at * (heads * HD), 1)
        lane = lax.broadcasted_iota(jnp.int32, (1, width), 1)
        gate_row = jnp.zeros((1, width), F32)
        for h in range(heads):
            total = jnp.sum(rows[1][h][1:2], axis=1, keepdims=True)
            total = total * (1.0 - gate_ref[h] * gate_ref[h])
            gate_row = gate_row + jnp.where(lane == row_at * heads + h, total, 0.0)
        small = jnp.concatenate(
            [d_gains, own[0:3], gate_row, jnp.zeros((24, width), F32)], 0
        )
        for tile in range(12):
            lanes = slice(tile * 128, (tile + 1) * 128)
            first = tile * SHARED
            shared_acc[first : first + 144] = embed_acc[:, lanes].astype(BF16)
            shared_acc[first + 144 : first + 288] = unpatch_sum_ref[:, lanes].astype(BF16)
            shared_acc[first + 288 : first + SHARED] = small[:, lanes].astype(BF16)
        shared_acc[12 * SHARED :] = jnp.zeros((8 * CHUNK - 12 * SHARED, 128), BF16)
        latent = field_of(taps_acc[...], place_ref[...], -1)
        rows = [
            d_modulation[q : q + 1, tile * 128 : (tile + 1) * 128]
            for q in range(4)
            for tile in range(12)
        ]
        for r in range(ROWS):
            ahead = lax.rem(r // 2 - at_ref[0] + 4, 4)
            mods = jnp.concatenate(rows[6 * r : 6 * r + 6] + [jnp.zeros((10, 128), F32)], 0)
            piece = jnp.concatenate(
                [
                    shared_acc[r * CHUNK : (r + 1) * CHUNK],
                    activation_ref[r].astype(BF16),
                    latent[r].astype(BF16),
                    mods.astype(BF16),
                ],
                0,
            )

            @pl.when(at_ref[1] == r % 2)
            def _():
                own_pack_ref[ahead] = piece

            @pl.when(at_ref[1] != r % 2)
            def _():
                other_pack_ref[ahead] = piece


def first_back(
    at, gates, patches, embed, vec, weight, d_raw, d_mid, place, out_sum, unpatch_sum, back_sums, own_sums,
    head, text_head, gains, modulation, activation,
):
    width = embed.shape[1]
    part = weight.shape[2]
    pack = (4, CHUNK + 48, 128)
    grads = (4, 2 * width // COLS, 2 * part)
    rest = (place, out_sum, unpatch_sum, back_sums, own_sums, head, text_head, gains, modulation, activation)
    return pl.pallas_call(
        first_kernel,
        grid_spec=pltpu.PrefetchScalarGridSpec(
            num_scalar_prefetch=2,
            grid=(TOKENS // PAIR,),
            in_specs=[
                lane_block(144, PAIR),
                whole(embed.shape),
                whole(vec.shape),
                whole(weight.shape),
                pl.BlockSpec((3, part, PAIR), lambda t, *_: (0, 0, t)),
                row_block(PAIR, width),
            ]
            + [whole(value.shape) for value in rest],
            out_specs=[pl.BlockSpec(pack, lambda t, *_: (0, 0, 0))] * 2
            + [pl.BlockSpec(grads, lambda t, *_: (0, 0, 0))] * 4,
            scratch_shapes=[
                pltpu.VMEM((144, TOKENS), F32),
                pltpu.VMEM((144, width), F32),
                pltpu.VMEM((8, width), F32),
                pltpu.VMEM((8 * CHUNK, 128), BF16),
                pltpu.VMEM((3, part, width), F32),
                pltpu.VMEM((4, width, part), BF16),
            ],
        ),
        out_shape=[jax.ShapeDtypeStruct(pack, BF16)] * 2 + [jax.ShapeDtypeStruct(grads, BF16)] * 4,
        compiler_params=params(58),
        cost_estimate=LIGHT,
        name="first_back",
    )(at, gates, patches, embed, vec, weight, d_raw, d_mid, *rest)


def local(
    latent, condition, caption, cap_len, cotangent, embed_weight, modulate_weight, norm_gains,
    cross_gate, qkv_weight, text_kv_weight, out_weight, gate_up_weight, down_weight, unpatch_weight,
):
    images, _, _, channels = latent.shape
    width = embed_weight.shape[3]
    local_width = qkv_weight.shape[2]
    heads = local_width // HD
    hidden_width = down_weight.shape[0]
    taps = 9 * channels
    row_at = lax.axis_index("row")
    col_at = lax.axis_index("col")
    at = jnp.stack([row_at // 2, row_at % 2, col_at // 4, col_at % 4]).astype(jnp.int32)
    tile = latent.shape[1] * latent.shape[2] * channels

    cond_low = jax.nn.silu(condition.astype(F32)).astype(BF16)
    mod_piece = jnp.dot(cond_low, modulate_weight, preferred_element_type=F32)
    mod_columns = mod_piece.shape[1]
    mod_high = mod_piece.astype(BF16)
    mod_low = (mod_piece - mod_high.astype(F32)).astype(BF16)

    packed = jnp.concatenate(
        [latent.reshape(images, tile), cotangent.reshape(images, tile), mod_high, mod_low], axis=1
    )
    packed = jnp.pad(packed, ((0, 0), (0, 2 * local_width - packed.shape[1])))

    ffn_piece = jnp.concatenate([gate_up_weight[0], gate_up_weight[1], down_weight.T], axis=1)
    ffn_whole = lax.all_gather(ffn_piece, "col", axis=0, tiled=True)
    head_piece = jnp.concatenate(
        [
            jnp.concatenate([qkv_weight[0], qkv_weight[1]], axis=1),
            jnp.concatenate([qkv_weight[2], out_weight.T], axis=1),
        ]
    )
    text_piece = jnp.concatenate([text_kv_weight[0], text_kv_weight[1]], axis=1)
    head_pieces = from_col(head_piece, along_y)
    text_pieces = from_col(text_piece, along_z)
    packed = after(packed, *head_pieces, *text_pieces)
    packed = lax.all_to_all(packed, "col", 0, 0, tiled=True)
    head_pieces = from_col(jnp.stack(head_pieces), along_z)
    text_own = jnp.stack(text_pieces)
    text_beside = [lax.ppermute(text_own, "col", col_pairs(d, 0)) for d in (1, 3)]
    packed, text_own, next_text, last_text, *head_pieces = lax.optimization_barrier(
        (packed, text_own, *text_beside, *head_pieces)
    )
    text_apart = lax.ppermute(text_own, "col", col_pairs(2, 0))
    text_pieces = [text_own, next_text, text_apart, last_text]
    packed = send_all(packed, "row")
    qkv_whole, out_rows = unpack_head(at, head_pieces)
    out_pieces = from_chips(out_rows)

    patches, cot_taps = image_taps(packed)
    mod_at = 2 * tile
    modulation = packed[:, :, mod_at : mod_at + mod_columns].astype(F32)
    modulation = modulation + packed[:, :, mod_at + mod_columns : mod_at + 2 * mod_columns].astype(F32)
    modulation = modulation.reshape(4, width)
    attn_gate = jnp.tanh(modulation[1])
    ffn_gate = jnp.tanh(modulation[3])
    vec = jnp.stack(
        [
            norm_gains[0] * (1.0 + modulation[0]),
            norm_gains[1] * attn_gate,
            norm_gains[2] * (1.0 + modulation[2]),
            norm_gains[3] * ffn_gate,
        ]
    )
    vec = jnp.pad(vec, ((0, 4), (0, 0)))
    embed = embed_weight.reshape(taps, width)
    unpatch = unpatch_weight.transpose(0, 1, 3, 2).reshape(taps, width)
    raw = qkv_project(patches, embed, vec, qkv_whole)
    raw = raw.reshape(3, heads, HD, TOKENS)
    caption_rows = caption[0]
    text_raw = text_project(at, text_pieces, caption_rows)
    text_raw = text_raw.reshape(2, heads, HD, caption_rows.shape[0])
    head_gains = lax.dynamic_slice(norm_gains, (4, row_at * local_width), (3, local_width)).reshape(
        3, heads, HD, 1
    )
    head_gates = jnp.tanh(lax.dynamic_slice_in_dim(cross_gate, row_at * heads, heads))
    cap = lax.dynamic_slice_in_dim(cap_len, col_at, 1)
    table = jnp.asarray(rope_tables())
    mixed, lse = attend(raw, text_raw, head_gains, table, cap, head_gates)

    mixed_pieces = from_chips(mixed)
    reached = lax.optimization_barrier((*mixed_pieces, *out_pieces))
    mixed_whole = with_other_core(reached[:4])
    out_whole = with_other_core(reached[4:])
    attn, second, gate_up, hidden, ffn_own, ffn_other = forward(
        at, mixed_whole, out_whole, patches, embed, vec, ffn_whole
    )
    place = tile_places(False)
    cot_own = lax.dynamic_slice_in_dim(cot_taps, row_at * BLOCK, BLOCK, 1)
    d_ffn_own, ffn_out = own_grad(
        to_chips(sum_cores(ffn_own, ffn_other)), cot_own, unpatch, vec
    )
    d_ffn_near = from_chips(d_ffn_own)
    activation_field, unpatch_sum, own_sums = own_block(
        at, ffn_out, attn, patches, cot_taps, embed, unpatch, vec, place
    )
    d_ffn_near = lax.optimization_barrier((*d_ffn_near, activation_field))[:4]
    d_ffn, d_gate_up, d_attn, d_mid, mixed_own, mixed_other, back_sums = backward(
        at, with_other_core(d_ffn_near), ffn_whole, out_whole, gate_up, attn, patches, embed, cot_taps,
        unpatch, vec,
    )
    mixed_near = sum_cores(mixed_own, mixed_other)
    mixed_terms = to_chips(mixed_near)
    text_rows = text_kv_weight.shape[1]
    grads, out_near, out_far = weight_grads(
        after(second, *mixed_near), d_gate_up, d_ffn, hidden, mixed_whole, d_attn, text_rows
    )
    *mixed_terms, grads, out_near, out_far = lax.optimization_barrier(
        (*mixed_terms, grads, out_near, out_far)
    )
    d_mixed = sum(term.astype(F32) for term in mixed_terms).astype(BF16)
    d_mixed = d_mixed.reshape(heads, HD, TOKENS)
    out_near = sum_cores(out_near, out_far)
    out_apart = lax.ppermute(out_near[2], "row", row_pairs_to(2, 0))

    grads, dq_text, d_text_head = text_back(
        raw, text_raw, head_gains, table, lse, d_mixed, cap, head_gates, caption_rows,
        after(grads, *out_near),
    )
    dq_text, grads, out_apart, *out_near = lax.optimization_barrier(
        (dq_text, grads, out_apart, *out_near)
    )
    d_raw, d_head = attend_back(raw, head_gains, table, lse, d_mixed, dq_text)
    out_beside = [lax.ppermute(out_near[d], "row", row_pairs_to(d, 0)) for d in (1, 3)]
    d_raw, *out_terms = lax.optimization_barrier((d_raw, out_near[0], out_apart, *out_beside))
    out_sum = sum(term.astype(F32) for term in out_terms)
    d_raw = d_raw.reshape(3, local_width, TOKENS)
    own_pack, other_pack, *head_parts = first_back(
        at, head_gates, patches, embed, vec, qkv_whole, d_raw, d_mid, place, out_sum, unpatch_sum,
        back_sums, own_sums, d_head, d_text_head, norm_gains, modulation, activation_field,
    )
    beside = [lax.ppermute(head_parts[d], "col", col_pairs_to(0, d)) for d in (1, 3)]

    row_terms = to_chips(sum_cores(own_pack, other_pack))
    row_pack = sum(term.astype(F32) for term in row_terms)
    fields = row_pack[CHUNK : CHUNK + 2 * channels].T.reshape(COLS, 8, 2 * channels)
    mod_sums = row_pack[CHUNK + 2 * channels : CHUNK + 2 * channels + 6].reshape(COLS, 8, 6)
    fields = jnp.concatenate([fields, mod_sums], axis=2).astype(BF16)
    fields = jnp.pad(fields, ((0, 0), (0, 0), (0, 128 - fields.shape[2])))
    shared = row_pack[:CHUNK].astype(BF16).reshape(COLS, CHUNK // COLS, 128)
    col_pack = lax.all_to_all(jnp.concatenate([shared, fields], axis=1), "col", 0, 0)
    col_pack, left, right = lax.optimization_barrier((col_pack, *beside))
    shared = jnp.sum(col_pack[:, : CHUNK // COLS].astype(F32), axis=0)
    shared, apart = lax.optimization_barrier(
        (send_all(shared.astype(BF16), "col"), head_parts[2])
    )
    shared = send_all(shared, "row").reshape(-1, 128)
    apart = lax.ppermute(apart, "col", col_pairs_to(0, 2))
    head_near = sum(term.astype(F32) for term in (head_parts[0], left, apart, right)).astype(BF16)
    shared = shared[: 12 * SHARED].reshape(12, SHARED, 128).astype(F32)
    fields = col_pack[:, CHUNK // COLS :]
    activation = fields[:, :, :channels].reshape(latent.shape)
    latent_grad = fields[:, :, channels : 2 * channels].reshape(latent.shape)
    modulate_grad = lax.dot_general(
        cond_low.astype(F32),
        fields[:, :, 2 * channels : 2 * channels + 6].reshape(images, mod_columns).astype(F32),
        (((0,), (0,)), ((), ())),
        precision=lax.Precision.HIGHEST,
        preferred_element_type=F32,
    )
    embed_grad = shared[:, :taps].transpose(1, 0, 2).reshape(embed_weight.shape)
    unpatch_grad = shared[:, taps : 2 * taps].reshape(12, 3, 3, channels, 128)
    unpatch_grad = unpatch_grad.transpose(1, 2, 0, 4, 3).reshape(unpatch_weight.shape)
    gains_grad = shared[:, 2 * taps : 2 * taps + 7].transpose(1, 0, 2).reshape(7, width)
    gate_grad = shared[0, 2 * taps + 7, :HEADS]

    part = width // COLS
    grads = lax.psum_scatter(
        grads.reshape(-1, 2 * local_width), "col", scatter_dimension=0, tiled=True
    ).astype(F32)
    text_kv_grad = jnp.stack([grads[:text_rows, :local_width], grads[:text_rows, local_width:]])
    ffn_total = jnp.concatenate(
        [grads[first : first + part] for first in range(text_rows, grads.shape[0], part)], axis=1
    )
    gate_up_grad = jnp.stack(
        [ffn_total[:, :hidden_width], ffn_total[:, hidden_width : 2 * hidden_width]]
    )
    down_grad = ffn_total[:, 2 * hidden_width :].T
    head_total = sum(term.astype(F32) for term in along_col(head_near, along_y))
    first, second_half = head_total[:, :local_width], head_total[:, local_width:]
    qkv_grad = jnp.stack([first[:part], second_half[:part], first[part:]])
    out_grad = second_half[part:].T
    return (
        activation, latent_grad, embed_grad, modulate_grad, gains_grad, gate_grad,
        qkv_grad, text_kv_grad, out_grad, gate_up_grad, down_grad, unpatch_grad,
    )


def solution(mesh):
    placed = (
        P(None, "row", "col", None),
        P(),
        P("col", None, None),
        P(),
        P(None, "row", "col", None),
        P(),
        P(None, ("row", "col")),
        P(),
        P(),
        P(None, "col", "row"),
        P(None, "col", "row"),
        P("row", "col"),
        P(None, "col", "row"),
        P("row", "col"),
        P(),
    )
    return jax.shard_map(
        local,
        mesh=mesh,
        in_specs=placed,
        out_specs=(
            P(None, "row", "col", None),
            P(None, "row", "col", None),
            P(),
            P(None, ("row", "col")),
            P(),
            P(),
            P(None, "col", "row"),
            P(None, "col", "row"),
            P("row", "col"),
            P(None, "col", "row"),
            P("row", "col"),
            P(),
        ),
        check_vma=False,
    )
```

```python
import math
from functools import partial

import jax
import jax.numpy as jnp
import numpy as np
from jax import lax
from jax.experimental import pallas as pl
from jax.experimental.pallas import tpu as pltpu
from jax.sharding import PartitionSpec as P

HEADS = 24
HD = 64
GRID = 32
TOKENS = GRID * GRID
EPSILON = 1e-06
ROPE_BASE = 10000.0
MASKED = -1e30
F32 = jnp.float32
BF16 = jnp.bfloat16
ROWS = 8
COLS = 16
QUERY_BLOCK = 256
BLOCK = TOKENS // ROWS
PAIR = 2 * BLOCK
MIB = 2**20
SHARED = 320
CHUNK = 512
LIGHT = pl.CostEstimate(flops=1, bytes_accessed=1, transcendentals=0)


def dot(left, right, contract):
    return lax.dot_general(
        left, right, ((contract[:1], contract[1:]), ((), ())), preferred_element_type=F32
    )


def row_pairs(dx, dc):
    return [
        (((x + dx) % 4) * 2 + (c + dc) % 2, x * 2 + c) for x in range(4) for c in range(2)
    ]


def row_pairs_to(dx, dc):
    return [(dst, src) for src, dst in row_pairs(dx, dc)]


def from_chips(piece):
    return [piece] + [lax.ppermute(piece, "row", row_pairs(d, 0)) for d in (1, 2, 3)]


def with_other_core(pieces):
    quad = jnp.stack(pieces)
    return quad, lax.ppermute(quad, "row", row_pairs(0, 1))


def gather_near(piece):
    return with_other_core(from_chips(piece))


def sum_cores(own, other):
    other = lax.ppermute(other, "row", row_pairs(0, 1))
    return [(own[d].astype(F32) + other[d].astype(F32)).astype(BF16) for d in range(4)]


def to_chips(near):
    return [near[0]] + [lax.ppermute(near[d], "row", row_pairs_to(d, 0)) for d in (1, 2, 3)]


def col_pairs_to(dy, dz):
    return [(y * 4 + z, (y + dy) % 4 * 4 + (z + dz) % 4) for y in range(4) for z in range(4)]


def col_pairs(dy, dz):
    return [(dst, src) for src, dst in col_pairs_to(dy, dz)]


def from_col(piece, step):
    return [piece] + [lax.ppermute(piece, "col", col_pairs(*step(d))) for d in (1, 2, 3)]


def along_y(d):
    return (d, 0)


def along_z(d):
    return (0, d)


def along_col(parts, step):
    return [parts[0]] + [lax.ppermute(parts[d], "col", col_pairs_to(*step(d))) for d in (1, 2, 3)]


def send_all(piece, axis):
    copies = jnp.broadcast_to(piece, (lax.axis_size(axis),) + piece.shape)
    return lax.all_to_all(copies, axis, 0, 0)


def after(value, *others):
    return lax.optimization_barrier((value,) + others)[0]


def rope_tables():
    quarter = HD // 4
    frequency = np.float32(ROPE_BASE) ** (-np.arange(quarter, dtype=np.float32) / np.float32(quarter))
    place = np.arange(TOKENS)
    row = frequency[:, None] * (place // GRID).astype(np.float32)[None, :]
    col = frequency[:, None] * (place % GRID).astype(np.float32)[None, :]
    return np.stack([np.cos(row), np.sin(row), np.cos(col), np.sin(col)]).astype(np.float32)


def turn(v, table, sign):
    a, b, c, d = (v[k * 16 : (k + 1) * 16] for k in range(4))
    cr, sr, cc, sc = table[0], table[1] * sign, table[2], table[3] * sign
    return jnp.concatenate([a * cr - b * sr, a * sr + b * cr, c * cc - d * sc, c * sc + d * cc], 0)


def column_rms(v):
    return lax.rsqrt(jnp.mean(v * v, axis=0, keepdims=True) + EPSILON)


def normed(v, gain):
    return v * column_rms(v) * gain


def column_rms_back(v, u):
    scale = column_rms(v)
    return (u - v * (jnp.mean(u * v, axis=0, keepdims=True) * scale * scale)) * scale


def whole(shape):
    zeros = (0,) * len(shape)
    return pl.BlockSpec(shape, lambda *_: zeros, pipeline_mode=pl.Buffered(1))


def held():
    return pl.BlockSpec(memory_space=pltpu.VMEM)


def lane_block(rows, lanes):
    return pl.BlockSpec((rows, lanes), lambda t, *_: (0, t))


def row_block(rows, lanes):
    return pl.BlockSpec((rows, lanes), lambda t, *_: (t, 0))


def params(mib):
    return pltpu.CompilerParams(vmem_limit_bytes=mib * MIB, dimension_semantics=("arbitrary",))


def row_of_sums(v):
    return jnp.sum(v.T, axis=0, keepdims=True)


def attend_kernel(
    cap_ref, gate_ref, raw_ref, text_ref, gain_ref, table_ref, mixed_ref, lse_ref,
    q_ref, k_ref, v_ref, tk_ref, tv_ref,
):
    step = pl.program_id(0)
    heads = raw_ref.shape[1]

    @pl.when(step == 0)
    def _():
        table = table_ref[...]
        for h in range(heads):
            q = turn(normed(raw_ref[0, h], gain_ref[0, h]), table, 1.0).astype(BF16)
            q_ref[h] = q * jnp.asarray(0.125, BF16)
            k_ref[h] = turn(normed(raw_ref[1, h], gain_ref[1, h]), table, 1.0).T.astype(BF16)
            v_ref[h] = raw_ref[2, h].astype(BF16)
            tk_ref[h] = normed(text_ref[0, h], gain_ref[2, h]).T.astype(BF16)
            tv_ref[h] = text_ref[1, h].astype(BF16)

    slots = tk_ref.shape[1]
    mask = lax.broadcasted_iota(jnp.int32, (slots, QUERY_BLOCK), 0) < cap_ref[0]
    here = pl.ds(pl.multiple_of(step * QUERY_BLOCK, QUERY_BLOCK), QUERY_BLOCK)
    outs = []
    for h in range(heads):
        qb = q_ref[h, :, here]
        e = jnp.exp(dot(k_ref[h], qb, (1, 0)))
        total = jnp.sum(e, axis=0, keepdims=True)
        own = dot(v_ref[h], e.astype(BF16), (1, 0)) / total
        te = jnp.exp(jnp.where(mask, dot(tk_ref[h], qb, (1, 0)), MASKED))
        text_total = jnp.sum(te, axis=0, keepdims=True)
        text = dot(tv_ref[h], te.astype(BF16), (1, 0)) / text_total
        outs.append(own + gate_ref[h] * text)
        lse_ref[h, 0:1] = jnp.log(total)
        lse_ref[h, 1:2] = jnp.log(text_total)
    mixed_ref[...] = jnp.concatenate(outs, 0).astype(BF16)


def attend(raw, text_raw, gains, table, cap, gates):
    heads = raw.shape[1]
    slots = text_raw.shape[3]
    return pl.pallas_call(
        attend_kernel,
        grid_spec=pltpu.PrefetchScalarGridSpec(
            num_scalar_prefetch=2,
            grid=(TOKENS // QUERY_BLOCK,),
            in_specs=[
                whole((3, heads, HD, TOKENS)),
                whole((2, heads, HD, slots)),
                whole((3, heads, HD, 1)),
                whole((4, 16, TOKENS)),
            ],
            out_specs=[
                lane_block(heads * HD, QUERY_BLOCK),
                pl.BlockSpec((heads, 8, QUERY_BLOCK), lambda t, *_: (0, 0, t)),
            ],
            scratch_shapes=[
                pltpu.VMEM((heads, HD, TOKENS), BF16),
                pltpu.VMEM((heads, TOKENS, HD), BF16),
                pltpu.VMEM((heads, HD, TOKENS), BF16),
                pltpu.VMEM((heads, slots, HD), BF16),
                pltpu.VMEM((heads, HD, slots), BF16),
            ],
        ),
        out_shape=[
            jax.ShapeDtypeStruct((heads * HD, TOKENS), BF16),
            jax.ShapeDtypeStruct((heads, 8, TOKENS), F32),
        ],
        compiler_params=params(20),
        cost_estimate=LIGHT,
        name="attend",
    )(cap, gates, raw, text_raw, gains, table)


def text_back_kernel(
    cap_ref, gate_ref, q_raw_ref, text_ref, gain_ref, table_ref, lse_ref, grad_ref, caption_ref, held_ref,
    grads_ref, dq_ref, d_gain_ref, low_ref,
):
    del held_ref
    step = pl.program_id(0)
    heads, _, slots = low_ref.shape[1:]

    @pl.when(step == 0)
    def _():
        table = table_ref[...]
        mask = lax.broadcasted_iota(jnp.int32, (slots, TOKENS), 0) < cap_ref[0]
        for h in range(heads):
            gate = gate_ref[h]
            q = turn(normed(q_raw_ref[h], gain_ref[0, h]), table, 1.0).astype(BF16)
            q = q * jnp.asarray(0.125, BF16)
            tk = normed(text_ref[0, h], gain_ref[2, h]).astype(BF16)
            tv = text_ref[1, h].astype(BF16)
            g = grad_ref[h]
            tp = jnp.exp(jnp.where(mask, dot(tk, q, (0, 0)), MASKED) - lse_ref[h, 1:2])
            tpb = tp.astype(BF16)
            low_ref[1, h] = (dot(g, tpb, (1, 1)) * gate).astype(BF16)
            gate_terms = g.astype(F32) * dot(tv, tpb, (1, 0))
            tpd = tp * dot(tv, g, (0, 0)) * gate
            dts = (tpd - tp * jnp.sum(tpd, axis=0, keepdims=True)).astype(BF16)
            dq_ref[h] = dot(tk, dts, (1, 0))
            d_tk = dot(q, dts, (1, 1))
            values = text_ref[0, h]
            low_ref[0, h] = column_rms_back(values, d_tk * gain_ref[2, h]).astype(BF16)
            d_gain_ref[h, 0:1] = row_of_sums(values * column_rms(values) * d_tk)
            d_gain_ref[h, 1:2] = row_of_sums(gate_terms)

    d_text = low_ref[...].reshape(2 * heads * HD, slots)
    rows = grads_ref.shape[1]
    for k in range(grads_ref.shape[0]):
        grads_ref[k] = dot(caption_ref[:, k * rows : (k + 1) * rows], d_text, (0, 1)).astype(BF16)


def text_back(raw, text_raw, gains, table, lse, grads, cap, gates, caption, held):
    heads = raw.shape[1]
    slots = text_raw.shape[3]
    rows = caption.shape[1] // COLS
    lanes = 2 * heads * HD
    return pl.pallas_call(
        text_back_kernel,
        grid_spec=pltpu.PrefetchScalarGridSpec(
            num_scalar_prefetch=2,
            grid=(4,),
            in_specs=[
                pl.BlockSpec((None, heads, HD, TOKENS), lambda t, *_: (0, 0, 0, 0)),
                whole(text_raw.shape),
                whole(gains.shape),
                whole(table.shape),
                whole(lse.shape),
                whole(grads.shape),
                pl.BlockSpec((slots, 4 * rows), lambda t, *_: (0, t)),
                pl.BlockSpec(memory_space=pl.ANY),
            ],
            out_specs=[
                pl.BlockSpec((4, rows, lanes), lambda t, *_: (t, 0, 0)),
                pl.BlockSpec((heads, HD, TOKENS), lambda t, *_: (0, 0, 0)),
                pl.BlockSpec((heads, 8, HD), lambda t, *_: (0, 0, 0)),
            ],
            scratch_shapes=[pltpu.VMEM((2, heads, HD, slots), BF16)],
        ),
        out_shape=[
            jax.ShapeDtypeStruct(held.shape, BF16),
            jax.ShapeDtypeStruct((heads, HD, TOKENS), F32),
            jax.ShapeDtypeStruct((heads, 8, HD), F32),
        ],
        input_output_aliases={9: 0},
        compiler_params=params(58),
        cost_estimate=LIGHT,
        name="text_back",
    )(cap, gates, raw, text_raw, gains, table, lse, grads, caption, held)


def attend_back_kernel(
    raw_ref, gain_ref, table_ref, lse_ref, grad_ref, dq_text_ref,
    d_raw_ref, d_gain_ref, dv_ref, dk_ref, dq_ref,
):
    table = table_ref[...]
    q = turn(normed(raw_ref[0], gain_ref[0]), table, 1.0).astype(BF16) * jnp.asarray(0.125, BF16)
    k = turn(normed(raw_ref[1], gain_ref[1]), table, 1.0)
    k, k_turned = k.astype(BF16), k.T.astype(BF16)
    v_turned = raw_ref[2].T.astype(BF16)
    for first in range(0, TOKENS, QUERY_BLOCK):
        here = slice(first, first + QUERY_BLOCK)
        qb = q[:, here]
        gb = grad_ref[:, here]
        p = jnp.exp(dot(k_turned, qb, (1, 0)) - lse_ref[0:1, here])
        dv = dot(gb, p.astype(BF16), (1, 1))
        pd = p * dot(v_turned, gb, (1, 0))
        ds = (pd - p * jnp.sum(pd, axis=0, keepdims=True)).astype(BF16)
        dq_ref[:, here] = dot(k, ds, (1, 0)) + dq_text_ref[:, here]
        dk = dot(qb, ds, (1, 1))
        if first == 0:
            dv_ref[...] = dv
            dk_ref[...] = dk
        else:
            dv_ref[...] += dv
            dk_ref[...] += dk

    def raw_back(which, d_turned):
        spun = turn(d_turned.astype(BF16).astype(F32), table, -1.0)
        values = raw_ref[which]
        d_raw_ref[which] = column_rms_back(values, spun * gain_ref[which]).astype(BF16)
        d_gain_ref[which : which + 1] = row_of_sums(values * column_rms(values) * spun)

    raw_back(0, dq_ref[...] * 0.125)
    raw_back(1, dk_ref[...])
    d_raw_ref[2] = dv_ref[...].astype(BF16)


def attend_back(raw, gains, table, lse, grads, dq_text):
    heads = raw.shape[1]
    return pl.pallas_call(
        attend_back_kernel,
        grid=(heads,),
        in_specs=[
            pl.BlockSpec((3, None, HD, TOKENS), lambda h: (0, h, 0, 0)),
            pl.BlockSpec((3, None, HD, 1), lambda h: (0, h, 0, 0)),
            pl.BlockSpec((4, 16, TOKENS), lambda h: (0, 0, 0)),
            pl.BlockSpec((None, 8, TOKENS), lambda h: (h, 0, 0)),
            pl.BlockSpec((None, HD, TOKENS), lambda h: (h, 0, 0)),
            pl.BlockSpec((None, HD, TOKENS), lambda h: (h, 0, 0)),
        ],
        out_specs=[
            pl.BlockSpec((3, None, HD, TOKENS), lambda h: (0, h, 0, 0)),
            pl.BlockSpec((None, 8, HD), lambda h: (h, 0, 0)),
        ],
        scratch_shapes=[pltpu.VMEM((HD, TOKENS), F32) for _ in range(3)],
        out_shape=[
            jax.ShapeDtypeStruct((3, heads, HD, TOKENS), BF16),
            jax.ShapeDtypeStruct((heads, 8, HD), F32),
        ],
        compiler_params=params(58),
        cost_estimate=LIGHT,
        name="attend_back",
    )(raw, gains, table, lse, grads, dq_text)


def tile_places(chunk_first):
    r, c, k = np.meshgrid(np.arange(ROWS), np.arange(COLS), np.arange(8), indexing="ij")
    token = r * BLOCK + (k // 2) * GRID + c * 2 + k % 2
    source = (k * ROWS + r) * COLS + c if chunk_first else (r * COLS + c) * 8 + k
    places = np.zeros((TOKENS, TOKENS), np.float32)
    places[source.ravel(), token.ravel()] = 1.0
    return jnp.asarray(places, BF16)


def grid_shift(field, di, dj):
    step = di * GRID + dj
    moved = pltpu.roll(field, (-step) % TOKENS, 1) if step else field
    place = lax.broadcasted_iota(jnp.int32, field.shape, 1)
    row = place // GRID + di
    col = place % GRID + dj
    inside = (row >= 0) & (row < GRID) & (col >= 0) & (col < GRID)
    return jnp.where(inside, moved, 0.0)


def image_kernel(packed_ref, place_ref, patch_ref, cot_ref):
    for which, sign, out_ref in ((0, 1, patch_ref), (1, -1, cot_ref)):
        lanes = slice(which * 128, (which + 1) * 128)
        tiles = jnp.concatenate([packed_ref[r, :, lanes] for r in range(ROWS)], 0)
        turned = tiles.astype(F32).T
        chunks = jnp.concatenate([turned[k * 16 : (k + 1) * 16] for k in range(8)], 1)
        image = dot(chunks.astype(BF16), place_ref[...], (1, 0))
        for a in range(3):
            for b in range(3):
                first = (a * 3 + b) * 16
                out_ref[first : first + 16] = grid_shift(
                    image, sign * (a - 1), sign * (b - 1)
                ).astype(BF16)


def image_taps(packed):
    out = jax.ShapeDtypeStruct((144, TOKENS), BF16)
    return pl.pallas_call(
        image_kernel,
        out_shape=[out, out],
        compiler_params=pltpu.CompilerParams(vmem_limit_bytes=12 * MIB),
        cost_estimate=LIGHT,
        name="image_taps",
    )(packed, tile_places(True))


def field_of(taps, place, sign):
    total = jnp.zeros((16, TOKENS), F32)
    for a in range(3):
        for b in range(3):
            first = (a * 3 + b) * 16
            total = total + grid_shift(taps[first : first + 16], sign * (a - 1), sign * (b - 1))
    tiles = dot(total.astype(BF16), place, (1, 1))
    return [tiles[:, r * BLOCK : (r + 1) * BLOCK] for r in range(ROWS)]


def row_rms(v):
    return lax.rsqrt(jnp.mean(v * v, axis=-1, keepdims=True) + EPSILON)


def row_rms_back(v, scale, u):
    return (u - v * (jnp.mean(u * v, axis=-1, keepdims=True) * scale * scale)) * scale


def unpack_kernel(at_ref, *refs):
    piece_refs, (joined_ref, out_ref, turn_ref) = refs[:4], refs[4:]
    part = piece_refs[0].shape[1] // 2
    local_width = piece_refs[0].shape[2] // 2
    for dz in range(4):
        for dy in range(4):
            c = lax.rem(at_ref[2] + dy, 4) * 4 + lax.rem(at_ref[3] + dz, 4)
            rows = pl.ds(pl.multiple_of(c * part, part), part)
            piece = piece_refs[dz][dy]
            joined_ref[0, rows, :] = piece[:part, :local_width]
            joined_ref[1, rows, :] = piece[:part, local_width:]
            joined_ref[2, rows, :] = piece[part:, :local_width]
            turn_ref[rows, :] = piece[part:, local_width:]
    out_ref[...] = turn_ref[...].T


def unpack_head(at, pieces):
    _, rows, lanes = pieces[0].shape
    width, local_width = COLS * rows // 2, lanes // 2
    return pl.pallas_call(
        unpack_kernel,
        grid_spec=pltpu.PrefetchScalarGridSpec(
            num_scalar_prefetch=1,
            grid=(1,),
            in_specs=[whole(pieces[0].shape)] * 4,
            out_specs=[
                pl.BlockSpec((3, width, local_width), lambda t, at: (0, 0, 0)),
                pl.BlockSpec((local_width, width), lambda t, at: (0, 0)),
            ],
            scratch_shapes=[pltpu.VMEM((width, local_width), BF16)],
        ),
        out_shape=[
            jax.ShapeDtypeStruct((3, width, local_width), BF16),
            jax.ShapeDtypeStruct((local_width, width), BF16),
        ],
        compiler_params=params(14),
        cost_estimate=LIGHT,
        name="unpack_head",
    )(at, *pieces)


def text_kernel(at_ref, p0_ref, p1_ref, p2_ref, p3_ref, caption_ref, raw_ref):
    rows = p0_ref.shape[1]
    total = 0.0
    for dy, ref in enumerate((p0_ref, p1_ref, p2_ref, p3_ref)):
        for dz in range(4):
            c = lax.rem(at_ref[2] + dy, 4) * 4 + lax.rem(at_ref[3] + dz, 4)
            lanes = pl.ds(pl.multiple_of(c * rows, rows), rows)
            total = total + dot(ref[dz], caption_ref[:, lanes], (0, 1))
    raw_ref[...] = total


def text_project(at, pieces, caption):
    lanes = pieces[0].shape[2]
    slots = caption.shape[0]
    return pl.pallas_call(
        text_kernel,
        grid_spec=pltpu.PrefetchScalarGridSpec(
            num_scalar_prefetch=1,
            grid=(1,),
            in_specs=[whole(pieces[0].shape)] * 4 + [whole(caption.shape)],
            out_specs=pl.BlockSpec((lanes, slots), lambda t, at: (0, 0)),
        ),
        out_shape=jax.ShapeDtypeStruct((lanes, slots), F32),
        compiler_params=params(16),
        cost_estimate=LIGHT,
        name="text_project",
    )(at, *pieces, caption)


def qkv_kernel(patch_ref, embed_ref, vec_ref, weight_ref, raw_ref):
    x = dot(patch_ref[...], embed_ref[...], (0, 0))
    h = (x * row_rms(x) * vec_ref[0:1]).astype(BF16)
    for s in range(3):
        raw_ref[s] = dot(h, weight_ref[s], (1, 0)).T


def qkv_project(patches, embed, vec, weight):
    part = weight.shape[2]
    return pl.pallas_call(
        qkv_kernel,
        grid=(TOKENS // PAIR,),
        in_specs=[lane_block(144, PAIR), whole(embed.shape), whole(vec.shape), whole(weight.shape)],
        out_specs=pl.BlockSpec((3, part, PAIR), lambda t: (0, 0, t)),
        out_shape=jax.ShapeDtypeStruct((3, part, TOKENS), F32),
        compiler_params=params(16),
        cost_estimate=LIGHT,
        name="qkv_project",
    )(patches, embed, vec, weight)


def joined(ref):
    return ref[...].reshape(-1, ref.shape[2])


def halves(core, first, second):
    return jnp.where(core == 0, first, second)


def forward_kernel(
    at_ref, near_ref, far_ref, out_near_ref, out_far_ref, patch_ref, embed_ref, vec_ref, ffn_ref,
    attn_ref, second_ref, gate_up_ref, hidden_ref, own_ref, other_ref,
):
    core = at_ref[1]
    hidden_width = hidden_ref.shape[1]
    x = dot(patch_ref[...], embed_ref[...], (0, 0))
    attn = dot(joined(near_ref), joined(out_near_ref), (0, 0))
    attn = attn + dot(joined(far_ref), joined(out_far_ref), (0, 0))
    attn_ref[...] = attn.astype(BF16)
    mid = x + vec_ref[1:2] * (attn * row_rms(attn))
    second = (mid * row_rms(mid) * vec_ref[2:3]).astype(BF16)
    second_ref[...] = second
    gate_up = dot(second, ffn_ref[:, : 2 * hidden_width], (1, 0))
    gate_up_ref[...] = gate_up.astype(BF16)
    gate = gate_up[:, :hidden_width]
    hidden = (gate * jax.nn.sigmoid(gate) * gate_up[:, hidden_width:]).astype(BF16)
    hidden_ref[...] = hidden
    part = dot(hidden, ffn_ref[:, 2 * hidden_width :], (1, 1)).astype(BF16)
    own_ref[0] = halves(core, part[:BLOCK], part[BLOCK:])
    other_ref[0] = halves(core, part[BLOCK:], part[:BLOCK])


def forward(at, mixed, out_whole, patches, embed, vec, ffn):
    width = embed.shape[1]
    part = mixed[0].shape[1]
    hidden_width = ffn.shape[1] // 3
    by_chip = pl.BlockSpec((1, BLOCK, width), lambda t, at: ((t - at[0] + 4) % 4, 0, 0))
    return pl.pallas_call(
        forward_kernel,
        grid_spec=pltpu.PrefetchScalarGridSpec(
            num_scalar_prefetch=1,
            grid=(4,),
            in_specs=[
                pl.BlockSpec((4, part, PAIR), lambda t, at: (0, 0, t)),
                pl.BlockSpec((4, part, PAIR), lambda t, at: (0, 0, t)),
                whole((4, part, width)),
                whole((4, part, width)),
                lane_block(144, PAIR),
                whole(embed.shape),
                whole(vec.shape),
                whole(ffn.shape),
            ],
            out_specs=[
                row_block(PAIR, width),
                row_block(PAIR, width),
                row_block(PAIR, 2 * hidden_width),
                row_block(PAIR, hidden_width),
                by_chip,
                by_chip,
            ],
        ),
        out_shape=[
            jax.ShapeDtypeStruct((TOKENS, width), BF16),
            jax.ShapeDtypeStruct((TOKENS, width), BF16),
            jax.ShapeDtypeStruct((TOKENS, 2 * hidden_width), BF16),
            jax.ShapeDtypeStruct((TOKENS, hidden_width), BF16),
            jax.ShapeDtypeStruct((4, BLOCK, width), BF16),
            jax.ShapeDtypeStruct((4, BLOCK, width), BF16),
        ],
        compiler_params=params(56),
        cost_estimate=LIGHT,
        name="forward",
    )(at, *mixed, *out_whole, patches, embed, vec, ffn)


def own_grad_kernel(p0_ref, p1_ref, p2_ref, p3_ref, cot_ref, unpatch_ref, vec_ref, d_ffn_ref, ffn_ref):
    ffn = sum(p[...].astype(F32) for p in (p0_ref, p1_ref, p2_ref, p3_ref))
    ffn_ref[...] = ffn
    d_last = dot(cot_ref[...], unpatch_ref[...], (0, 0))
    d_ffn_ref[...] = row_rms_back(ffn, row_rms(ffn), vec_ref[3:4] * d_last).astype(BF16)


def own_grad(pieces, cot_own, unpatch, vec):
    shape = (BLOCK, unpatch.shape[1])
    return pl.pallas_call(
        own_grad_kernel,
        out_shape=[jax.ShapeDtypeStruct(shape, BF16), jax.ShapeDtypeStruct(shape, F32)],
        compiler_params=pltpu.CompilerParams(vmem_limit_bytes=12 * MIB),
        cost_estimate=LIGHT,
        name="own_grad",
    )(*pieces, cot_own, unpatch, vec)


def own_kernel(
    at_ref, ffn_ref, attn_ref, patch_ref, cot_ref, embed_ref, unpatch_ref, vec_ref, place_ref,
    field_ref, unpatch_sum_ref, sums_ref, taps_ref,
):
    ffn = ffn_ref[...]
    d_last = dot(cot_ref[...], unpatch_ref[...], (0, 0))
    normed_ffn = ffn * row_rms(ffn)
    sums_ref[...] = jnp.broadcast_to(
        jnp.sum(normed_ffn * d_last, axis=0, keepdims=True), sums_ref.shape
    )
    attn = attn_ref[...].astype(F32)
    x = dot(patch_ref[...], embed_ref[...], (0, 0))
    last = (x + vec_ref[1:2] * (attn * row_rms(attn)) + vec_ref[3:4] * normed_ffn).astype(BF16)
    unpatch_sum_ref[...] = dot(cot_ref[...], last, (1, 0))
    taps_ref[...] = jnp.zeros_like(taps_ref)
    here = pl.multiple_of((2 * at_ref[0] + at_ref[1]) * BLOCK, BLOCK)
    taps_ref[:, pl.ds(here, BLOCK)] = dot(unpatch_ref[...], last, (1, 1))
    for r, tile in enumerate(field_of(taps_ref[...], place_ref[...], 1)):
        field_ref[r] = tile


def own_block(at, ffn, attn, patches, cot_taps, embed, unpatch, vec, place):
    width = embed.shape[1]
    lanes = pl.BlockSpec((144, BLOCK), lambda t, at: (0, 2 * at[0] + at[1]))
    return pl.pallas_call(
        own_kernel,
        grid_spec=pltpu.PrefetchScalarGridSpec(
            num_scalar_prefetch=1,
            grid=(1,),
            in_specs=[
                whole((BLOCK, width)),
                pl.BlockSpec((BLOCK, width), lambda t, at: (2 * at[0] + at[1], 0)),
                lanes,
                lanes,
                whole(embed.shape),
                whole(unpatch.shape),
                whole(vec.shape),
                whole(place.shape),
            ],
            out_specs=[
                pl.BlockSpec((ROWS, 16, BLOCK), lambda t, at: (0, 0, 0)),
                pl.BlockSpec((144, width), lambda t, at: (0, 0)),
                pl.BlockSpec((8, width), lambda t, at: (0, 0)),
            ],
            scratch_shapes=[pltpu.VMEM((144, TOKENS), F32)],
        ),
        out_shape=[
            jax.ShapeDtypeStruct((ROWS, 16, BLOCK), F32),
            jax.ShapeDtypeStruct((144, width), F32),
            jax.ShapeDtypeStruct((8, width), F32),
        ],
        compiler_params=params(14),
        cost_estimate=LIGHT,
        name="own_block",
    )(at, ffn, attn, patches, cot_taps, embed, unpatch, vec, place)


def backward_kernel(
    at_ref, own_ref, other_ref, ffn_ref, out_near_ref, out_far_ref, gate_up_ref, attn_ref,
    patch_ref, embed_ref, cot_ref, unpatch_ref, vec_ref,
    d_ffn_ref, d_gate_up_ref, d_attn_ref, d_mid_ref, mixed_own_ref, mixed_other_ref, sums_ref,
):
    step = pl.program_id(0)
    chip, core = at_ref[0], at_ref[1]
    hidden_width = d_gate_up_ref.shape[1] // 2
    own, other = own_ref[0], other_ref[0]
    d_ffn = jnp.concatenate([halves(core, own, other), halves(core, other, own)], 0)
    d_ffn_ref[...] = d_ffn
    d_hidden = dot(d_ffn, ffn_ref[:, 2 * hidden_width :], (1, 0))
    gate = gate_up_ref[:, :hidden_width].astype(F32)
    up = gate_up_ref[:, hidden_width:].astype(F32)
    sigma = jax.nn.sigmoid(gate)
    silu = gate * sigma
    d_gate = d_hidden * up * (sigma + silu * (1.0 - sigma))
    d_gate_up = jnp.concatenate([d_gate.astype(BF16), (d_hidden * silu).astype(BF16)], 1)
    d_gate_up_ref[...] = d_gate_up
    d_second = dot(d_gate_up, ffn_ref[:, : 2 * hidden_width], (1, 1))

    x = dot(patch_ref[...], embed_ref[...], (0, 0))
    attn = attn_ref[...].astype(F32)
    attn_scale = row_rms(attn)
    attn_normed = attn * attn_scale
    mid = x + vec_ref[1:2] * attn_normed
    mid_scale = row_rms(mid)
    mid_sum = jnp.sum(mid * mid_scale * d_second, axis=0, keepdims=True)
    d_last = dot(cot_ref[...], unpatch_ref[...], (0, 0))
    place = lax.broadcasted_iota(jnp.int32, (PAIR, 1), 0) // BLOCK
    mine = (place == core) & (step == chip)
    d_mid = row_rms_back(mid, mid_scale, vec_ref[2:3] * d_second) + jnp.where(mine, d_last, 0.0)
    d_mid_ref[...] = d_mid.astype(BF16)
    attn_sum = jnp.sum(attn_normed * d_mid, axis=0, keepdims=True)
    d_attn = row_rms_back(attn, attn_scale, vec_ref[1:2] * d_mid).astype(BF16)
    d_attn_ref[...] = d_attn
    for weight_ref, part_ref in ((out_near_ref, mixed_own_ref), (out_far_ref, mixed_other_ref)):
        part_ref[...] = dot(joined(weight_ref), d_attn, (1, 1)).astype(BF16).reshape(part_ref.shape)

    @pl.when(step == 0)
    def _():
        sums_ref[...] = jnp.zeros_like(sums_ref)

    sums_ref[0:1] += mid_sum
    sums_ref[1:2] += attn_sum


def backward(at, d_ffn, ffn, out_whole, gate_up, attn, patches, embed, cot_taps, unpatch, vec):
    width = embed.shape[1]
    part = out_whole[0].shape[1]
    hidden_width = ffn.shape[1] // 3
    by_chip = pl.BlockSpec((1, BLOCK, width), lambda t, at: ((t - at[0] + 4) % 4, 0, 0))
    parts = pl.BlockSpec((4, part, PAIR), lambda t, at: (0, 0, t))
    return pl.pallas_call(
        backward_kernel,
        grid_spec=pltpu.PrefetchScalarGridSpec(
            num_scalar_prefetch=1,
            grid=(4,),
            in_specs=[
                by_chip,
                by_chip,
                held(),
                held(),
                held(),
                row_block(PAIR, 2 * hidden_width),
                row_block(PAIR, width),
                lane_block(144, PAIR),
                whole(embed.shape),
                lane_block(144, PAIR),
                whole(unpatch.shape),
                whole(vec.shape),
            ],
            out_specs=[
                row_block(PAIR, width),
                row_block(PAIR, 2 * hidden_width),
                row_block(PAIR, width),
                row_block(PAIR, width),
                parts,
                parts,
                pl.BlockSpec((8, width), lambda t, at: (0, 0)),
            ],
        ),
        out_shape=[
            jax.ShapeDtypeStruct((TOKENS, width), BF16),
            jax.ShapeDtypeStruct((TOKENS, 2 * hidden_width), BF16),
            jax.ShapeDtypeStruct((TOKENS, width), BF16),
            jax.ShapeDtypeStruct((TOKENS, width), BF16),
            jax.ShapeDtypeStruct((4, part, TOKENS), BF16),
            jax.ShapeDtypeStruct((4, part, TOKENS), BF16),
            jax.ShapeDtypeStruct((8, width), F32),
        ],
        compiler_params=params(32),
        cost_estimate=LIGHT,
        name="backward",
    )(at, *d_ffn, ffn, *out_whole, gate_up, attn, patches, embed, cot_taps, unpatch, vec)


def weight_kernel(
    second_ref, d_gate_up_ref, d_ffn_ref, hidden_ref, near_ref, far_ref, d_attn_ref,
    grads_ref, out_near_ref, out_far_ref,
):
    step = pl.program_id(0)
    chunk, _, lanes = grads_ref.shape[0] // 4, *grads_ref.shape[1:]
    part = second_ref.shape[1] // chunk
    rows = jnp.concatenate(
        [
            dot(second_ref[...], d_gate_up_ref[...], (0, 0)).astype(BF16),
            dot(d_ffn_ref[...], hidden_ref[...], (0, 0)).astype(BF16),
        ],
        1,
    )
    groups = rows.shape[1] // lanes
    first = grads_ref.shape[1] - groups * part
    for c in range(chunk):
        for g in range(groups):
            grads_ref[step * chunk + c, first + g * part : first + (g + 1) * part] = rows[
                c * part : (c + 1) * part, g * lanes : (g + 1) * lanes
            ]
    out_near_ref[0] = dot(near_ref[0], d_attn_ref[...], (1, 0)).astype(BF16)
    out_far_ref[0] = dot(far_ref[0], d_attn_ref[...], (1, 0)).astype(BF16)


def weight_grads(second, d_gate_up, d_ffn, hidden, mixed, d_attn, text_rows):
    width = second.shape[1]
    heads_width = mixed[0].shape[1]
    lanes = 2 * heads_width
    grads = (COLS, text_rows + width // COLS * 3 * hidden.shape[1] // lanes, lanes)
    pieces = pl.BlockSpec((1, heads_width, TOKENS), lambda t: (t, 0, 0))
    out_piece = pl.BlockSpec((1, heads_width, width), lambda t: (t, 0, 0))
    out_shape = jax.ShapeDtypeStruct((4, heads_width, width), BF16)
    return pl.pallas_call(
        weight_kernel,
        grid=(4,),
        in_specs=[
            lane_block(TOKENS, width // 4),
            whole(d_gate_up.shape),
            lane_block(TOKENS, width // 4),
            whole(hidden.shape),
            pieces,
            pieces,
            whole(d_attn.shape),
        ],
        out_specs=[pl.BlockSpec(grads, lambda t: (0, 0, 0)), out_piece, out_piece],
        out_shape=[jax.ShapeDtypeStruct(grads, BF16), out_shape, out_shape],
        compiler_params=params(40),
        cost_estimate=LIGHT,
        name="weight_grads",
    )(second, d_gate_up, d_ffn, hidden, *mixed, d_attn)


def first_kernel(
    at_ref, gate_ref, patch_ref, embed_ref, vec_ref, weight_ref, d_raw_ref, d_mid_ref, place_ref, out_sum_ref,
    unpatch_sum_ref, back_sums_ref, own_sums_ref, head_ref, text_head_ref, gains_ref, mod_ref, activation_ref,
    own_pack_ref, other_pack_ref, p0_ref, p1_ref, p2_ref, p3_ref,
    taps_acc, embed_acc, first_acc, shared_acc, qkv_acc, turned_acc,
):
    step = pl.program_id(0)
    last = pl.num_programs(0) - 1
    x = dot(patch_ref[...], embed_ref[...], (0, 0))
    scale = row_rms(x)
    x_normed = x * scale
    h = (x_normed * vec_ref[0:1]).astype(BF16)
    d_h = dot(d_raw_ref[0], weight_ref[0], (0, 1))
    for s in (1, 2):
        d_h = d_h + dot(d_raw_ref[s], weight_ref[s], (0, 1))

    @pl.when(step == 0)
    def _():
        qkv_acc[...] = jnp.zeros_like(qkv_acc)
        embed_acc[...] = jnp.zeros_like(embed_acc)
        first_acc[...] = jnp.zeros_like(first_acc)

    qkv_acc[...] += dot(joined(d_raw_ref), h, (1, 0)).reshape(qkv_acc.shape)
    first_acc[0:1] += jnp.sum(x_normed * d_h, axis=0, keepdims=True)
    d_first = (d_mid_ref[...].astype(F32) + row_rms_back(x, scale, vec_ref[0:1] * d_h)).astype(BF16)
    embed_acc[...] += dot(patch_ref[...], d_first, (1, 0))
    here = pl.ds(pl.multiple_of(step * PAIR, PAIR), PAIR)
    taps_acc[:, here] = dot(embed_ref[...], d_first, (1, 1))

    @pl.when(step == last)
    def _():
        part = p0_ref.shape[1] // 2
        for s in range(4):
            turned_acc[s] = (qkv_acc[s] if s < 3 else out_sum_ref[...]).T.astype(BF16)
        for dz, ref in enumerate((p0_ref, p1_ref, p2_ref, p3_ref)):
            z = lax.rem(at_ref[3] + dz, 4)
            for y in range(4):
                dy = lax.rem(y - at_ref[2] + 4, 4)
                first = pl.multiple_of((y * 4 + z) * part, part)
                pieces = [turned_acc[s, pl.ds(first, part), :] for s in range(4)]
                for k in range(2):
                    ref[dy, k * part : (k + 1) * part] = jnp.concatenate(
                        pieces[2 * k : 2 * k + 2], 1
                    )
        terms = jnp.concatenate(
            [first_acc[0:1], back_sums_ref[1:2], back_sums_ref[0:1], own_sums_ref[0:1]], 0
        )
        gates = [jnp.tanh(mod_ref[k : k + 1]) for k in (1, 3)]
        into = jnp.concatenate(
            [1.0 + mod_ref[0:1], gates[0], 1.0 + mod_ref[2:3], gates[1]], 0
        )
        d_gains = terms * into
        slope = jnp.concatenate(
            [jnp.ones_like(gates[0]), 1.0 - gates[0] * gates[0]] * 1
            + [jnp.ones_like(gates[0]), 1.0 - gates[1] * gates[1]],
            0,
        )
        d_modulation = terms * gains_ref[0:4] * slope
        heads = head_ref.shape[0]
        width = d_gains.shape[1]
        rows = [head_ref[h] for h in range(heads)], [text_head_ref[h] for h in range(heads)]
        own = jnp.concatenate(
            [
                jnp.concatenate([r[0:2] for r in rows[0]], 1),
                jnp.concatenate([r[0:1] for r in rows[1]], 1),
                jnp.zeros((5, heads * HD), F32),
            ],
            0,
        )
        own = jnp.concatenate([own, jnp.zeros((8, width - heads * HD), F32)], 1)
        row_at = 2 * at_ref[0] + at_ref[1]
        own = pltpu.roll(own, row_at * (heads * HD), 1)
        lane = lax.broadcasted_iota(jnp.int32, (1, width), 1)
        gate_row = jnp.zeros((1, width), F32)
        for h in range(heads):
            total = jnp.sum(rows[1][h][1:2], axis=1, keepdims=True)
            total = total * (1.0 - gate_ref[h] * gate_ref[h])
            gate_row = gate_row + jnp.where(lane == row_at * heads + h, total, 0.0)
        small = jnp.concatenate(
            [d_gains, own[0:3], gate_row, jnp.zeros((24, width), F32)], 0
        )
        for tile in range(12):
            lanes = slice(tile * 128, (tile + 1) * 128)
            first = tile * SHARED
            shared_acc[first : first + 144] = embed_acc[:, lanes].astype(BF16)
            shared_acc[first + 144 : first + 288] = unpatch_sum_ref[:, lanes].astype(BF16)
            shared_acc[first + 288 : first + SHARED] = small[:, lanes].astype(BF16)
        shared_acc[12 * SHARED :] = jnp.zeros((8 * CHUNK - 12 * SHARED, 128), BF16)
        latent = field_of(taps_acc[...], place_ref[...], -1)
        rows = [
            d_modulation[q : q + 1, tile * 128 : (tile + 1) * 128]
            for q in range(4)
            for tile in range(12)
        ]
        for r in range(ROWS):
            ahead = lax.rem(r // 2 - at_ref[0] + 4, 4)
            mods = jnp.concatenate(rows[6 * r : 6 * r + 6] + [jnp.zeros((10, 128), F32)], 0)
            piece = jnp.concatenate(
                [
                    shared_acc[r * CHUNK : (r + 1) * CHUNK],
                    activation_ref[r].astype(BF16),
                    latent[r].astype(BF16),
                    mods.astype(BF16),
                ],
                0,
            )

            @pl.when(at_ref[1] == r % 2)
            def _():
                own_pack_ref[ahead] = piece

            @pl.when(at_ref[1] != r % 2)
            def _():
                other_pack_ref[ahead] = piece


def first_back(
    at, gates, patches, embed, vec, weight, d_raw, d_mid, place, out_sum, unpatch_sum, back_sums, own_sums,
    head, text_head, gains, modulation, activation,
):
    width = embed.shape[1]
    part = weight.shape[2]
    pack = (4, CHUNK + 48, 128)
    grads = (4, 2 * width // COLS, 2 * part)
    rest = (place, out_sum, unpatch_sum, back_sums, own_sums, head, text_head, gains, modulation, activation)
    return pl.pallas_call(
        first_kernel,
        grid_spec=pltpu.PrefetchScalarGridSpec(
            num_scalar_prefetch=2,
            grid=(TOKENS // PAIR,),
            in_specs=[
                lane_block(144, PAIR),
                whole(embed.shape),
                whole(vec.shape),
                whole(weight.shape),
                pl.BlockSpec((3, part, PAIR), lambda t, *_: (0, 0, t)),
                row_block(PAIR, width),
            ]
            + [whole(value.shape) for value in rest],
            out_specs=[pl.BlockSpec(pack, lambda t, *_: (0, 0, 0))] * 2
            + [pl.BlockSpec(grads, lambda t, *_: (0, 0, 0))] * 4,
            scratch_shapes=[
                pltpu.VMEM((144, TOKENS), F32),
                pltpu.VMEM((144, width), F32),
                pltpu.VMEM((8, width), F32),
                pltpu.VMEM((8 * CHUNK, 128), BF16),
                pltpu.VMEM((3, part, width), F32),
                pltpu.VMEM((4, width, part), BF16),
            ],
        ),
        out_shape=[jax.ShapeDtypeStruct(pack, BF16)] * 2 + [jax.ShapeDtypeStruct(grads, BF16)] * 4,
        compiler_params=params(58),
        cost_estimate=LIGHT,
        name="first_back",
    )(at, gates, patches, embed, vec, weight, d_raw, d_mid, *rest)


def local(
    latent, condition, caption, cap_len, cotangent, embed_weight, modulate_weight, norm_gains,
    cross_gate, qkv_weight, text_kv_weight, out_weight, gate_up_weight, down_weight, unpatch_weight,
):
    images, _, _, channels = latent.shape
    width = embed_weight.shape[3]
    local_width = qkv_weight.shape[2]
    heads = local_width // HD
    hidden_width = down_weight.shape[0]
    taps = 9 * channels
    row_at = lax.axis_index("row")
    col_at = lax.axis_index("col")
    at = jnp.stack([row_at // 2, row_at % 2, col_at // 4, col_at % 4]).astype(jnp.int32)
    tile = latent.shape[1] * latent.shape[2] * channels

    cond_low = jax.nn.silu(condition.astype(F32)).astype(BF16)
    mod_piece = jnp.dot(cond_low, modulate_weight, preferred_element_type=F32)
    mod_columns = mod_piece.shape[1]
    mod_high = mod_piece.astype(BF16)
    mod_low = (mod_piece - mod_high.astype(F32)).astype(BF16)

    packed = jnp.concatenate(
        [latent.reshape(images, tile), cotangent.reshape(images, tile), mod_high, mod_low], axis=1
    )
    packed = jnp.pad(packed, ((0, 0), (0, 2 * local_width - packed.shape[1])))

    head_piece = jnp.concatenate(
        [
            jnp.concatenate([qkv_weight[0], qkv_weight[1]], axis=1),
            jnp.concatenate([qkv_weight[2], out_weight.T], axis=1),
        ]
    )
    text_piece = jnp.concatenate([text_kv_weight[0], text_kv_weight[1]], axis=1)
    head_pieces = from_col(head_piece, along_y)
    text_pieces = from_col(text_piece, along_z)
    packed = lax.all_to_all(packed, "col", 0, 0, tiled=True)
    packed, *reached = lax.optimization_barrier((packed, *head_pieces, *text_pieces))
    head_pieces, text_pieces = reached[:4], reached[4:]
    packed = send_all(packed, "row")
    patches, cot_taps = image_taps(packed)
    head_pieces = from_col(jnp.stack(head_pieces), along_z)
    text_own = jnp.stack(text_pieces)
    text_beside = [lax.ppermute(text_own, "col", col_pairs(d, 0)) for d in (1, 3)]
    ffn_piece = jnp.concatenate([gate_up_weight[0], gate_up_weight[1], down_weight.T], axis=1)
    ffn_piece, patches, text_own, next_text, last_text, *head_pieces = lax.optimization_barrier(
        (ffn_piece, patches, text_own, *text_beside, *head_pieces)
    )
    ffn_whole = lax.all_gather(ffn_piece, "col", axis=0, tiled=True)
    text_apart = lax.ppermute(text_own, "col", col_pairs(2, 0))
    text_pieces = [text_own, next_text, text_apart, last_text]
    qkv_whole, out_rows = unpack_head(at, head_pieces)
    out_pieces = from_chips(out_rows)

    mod_at = 2 * tile
    modulation = packed[:, :, mod_at : mod_at + mod_columns].astype(F32)
    modulation = modulation + packed[:, :, mod_at + mod_columns : mod_at + 2 * mod_columns].astype(F32)
    modulation = modulation.reshape(4, width)
    attn_gate = jnp.tanh(modulation[1])
    ffn_gate = jnp.tanh(modulation[3])
    vec = jnp.stack(
        [
            norm_gains[0] * (1.0 + modulation[0]),
            norm_gains[1] * attn_gate,
            norm_gains[2] * (1.0 + modulation[2]),
            norm_gains[3] * ffn_gate,
        ]
    )
    vec = jnp.pad(vec, ((0, 4), (0, 0)))
    embed = embed_weight.reshape(taps, width)
    unpatch = unpatch_weight.transpose(0, 1, 3, 2).reshape(taps, width)
    raw = qkv_project(patches, embed, vec, qkv_whole)
    raw = raw.reshape(3, heads, HD, TOKENS)
    caption_rows = caption[0]
    text_raw = text_project(at, text_pieces, caption_rows)
    text_raw = text_raw.reshape(2, heads, HD, caption_rows.shape[0])
    head_gains = lax.dynamic_slice(norm_gains, (4, row_at * local_width), (3, local_width)).reshape(
        3, heads, HD, 1
    )
    head_gates = jnp.tanh(lax.dynamic_slice_in_dim(cross_gate, row_at * heads, heads))
    cap = lax.dynamic_slice_in_dim(cap_len, col_at, 1)
    table = jnp.asarray(rope_tables())
    mixed, lse = attend(raw, text_raw, head_gains, table, cap, head_gates)

    mixed_pieces = from_chips(mixed)
    reached = lax.optimization_barrier((*mixed_pieces, *out_pieces))
    mixed_whole = with_other_core(reached[:4])
    out_whole = with_other_core(reached[4:])
    attn, second, gate_up, hidden, ffn_own, ffn_other = forward(
        at, mixed_whole, out_whole, patches, embed, vec, ffn_whole
    )
    place = tile_places(False)
    cot_own = lax.dynamic_slice_in_dim(cot_taps, row_at * BLOCK, BLOCK, 1)
    d_ffn_own, ffn_out = own_grad(
        to_chips(sum_cores(ffn_own, ffn_other)), cot_own, unpatch, vec
    )
    d_ffn_near = from_chips(d_ffn_own)
    activation_field, unpatch_sum, own_sums = own_block(
        at, ffn_out, attn, patches, cot_taps, embed, unpatch, vec, place
    )
    d_ffn_near = lax.optimization_barrier((*d_ffn_near, activation_field))[:4]
    d_ffn, d_gate_up, d_attn, d_mid, mixed_own, mixed_other, back_sums = backward(
        at, with_other_core(d_ffn_near), ffn_whole, out_whole, gate_up, attn, patches, embed, cot_taps,
        unpatch, vec,
    )
    mixed_near = sum_cores(mixed_own, mixed_other)
    mixed_terms = to_chips(mixed_near)
    text_rows = text_kv_weight.shape[1]
    grads, out_near, out_far = weight_grads(
        after(second, *mixed_near), d_gate_up, d_ffn, hidden, mixed_whole, d_attn, text_rows
    )
    *mixed_terms, grads, out_near, out_far = lax.optimization_barrier(
        (*mixed_terms, grads, out_near, out_far)
    )
    d_mixed = sum(term.astype(F32) for term in mixed_terms).astype(BF16)
    d_mixed = d_mixed.reshape(heads, HD, TOKENS)
    out_near = sum_cores(out_near, out_far)
    out_apart = lax.ppermute(out_near[2], "row", row_pairs_to(2, 0))

    grads, dq_text, d_text_head = text_back(
        raw, text_raw, head_gains, table, lse, d_mixed, cap, head_gates, caption_rows,
        after(grads, *out_near),
    )
    dq_text, grads, out_apart, *out_near = lax.optimization_barrier(
        (dq_text, grads, out_apart, *out_near)
    )
    d_raw, d_head = attend_back(raw, head_gains, table, lse, d_mixed, dq_text)
    out_beside = [lax.ppermute(out_near[d], "row", row_pairs_to(d, 0)) for d in (1, 3)]
    d_raw, *out_terms = lax.optimization_barrier((d_raw, out_near[0], out_apart, *out_beside))
    out_sum = sum(term.astype(F32) for term in out_terms)
    d_raw = d_raw.reshape(3, local_width, TOKENS)
    own_pack, other_pack, *head_parts = first_back(
        at, head_gates, patches, embed, vec, qkv_whole, d_raw, d_mid, place, out_sum, unpatch_sum,
        back_sums, own_sums, d_head, d_text_head, norm_gains, modulation, activation_field,
    )
    beside = [lax.ppermute(head_parts[d], "col", col_pairs_to(0, d)) for d in (1, 3)]

    row_terms = to_chips(sum_cores(own_pack, other_pack))
    row_pack = sum(term.astype(F32) for term in row_terms)
    fields = row_pack[CHUNK : CHUNK + 2 * channels].T.reshape(COLS, 8, 2 * channels)
    mod_sums = row_pack[CHUNK + 2 * channels : CHUNK + 2 * channels + 6].reshape(COLS, 8, 6)
    fields = jnp.concatenate([fields, mod_sums], axis=2).astype(BF16)
    fields = jnp.pad(fields, ((0, 0), (0, 0), (0, 128 - fields.shape[2])))
    shared = row_pack[:CHUNK].astype(BF16).reshape(COLS, CHUNK // COLS, 128)
    col_pack = lax.all_to_all(jnp.concatenate([shared, fields], axis=1), "col", 0, 0)
    col_pack, left, right = lax.optimization_barrier((col_pack, *beside))
    shared = jnp.sum(col_pack[:, : CHUNK // COLS].astype(F32), axis=0)
    shared, apart = lax.optimization_barrier(
        (send_all(shared.astype(BF16), "col"), head_parts[2])
    )
    shared = send_all(shared, "row").reshape(-1, 128)
    apart = lax.ppermute(apart, "col", col_pairs_to(0, 2))
    head_near = sum(term.astype(F32) for term in (head_parts[0], left, apart, right)).astype(BF16)
    shared = shared[: 12 * SHARED].reshape(12, SHARED, 128).astype(F32)
    fields = col_pack[:, CHUNK // COLS :]
    activation = fields[:, :, :channels].reshape(latent.shape)
    latent_grad = fields[:, :, channels : 2 * channels].reshape(latent.shape)
    modulate_grad = lax.dot_general(
        cond_low.astype(F32),
        fields[:, :, 2 * channels : 2 * channels + 6].reshape(images, mod_columns).astype(F32),
        (((0,), (0,)), ((), ())),
        precision=lax.Precision.HIGHEST,
        preferred_element_type=F32,
    )
    embed_grad = shared[:, :taps].transpose(1, 0, 2).reshape(embed_weight.shape)
    unpatch_grad = shared[:, taps : 2 * taps].reshape(12, 3, 3, channels, 128)
    unpatch_grad = unpatch_grad.transpose(1, 2, 0, 4, 3).reshape(unpatch_weight.shape)
    gains_grad = shared[:, 2 * taps : 2 * taps + 7].transpose(1, 0, 2).reshape(7, width)
    gate_grad = shared[0, 2 * taps + 7, :HEADS]

    part = width // COLS
    grads = lax.psum_scatter(
        grads.reshape(-1, 2 * local_width), "col", scatter_dimension=0, tiled=True
    ).astype(F32)
    text_kv_grad = jnp.stack([grads[:text_rows, :local_width], grads[:text_rows, local_width:]])
    ffn_total = jnp.concatenate(
        [grads[first : first + part] for first in range(text_rows, grads.shape[0], part)], axis=1
    )
    gate_up_grad = jnp.stack(
        [ffn_total[:, :hidden_width], ffn_total[:, hidden_width : 2 * hidden_width]]
    )
    down_grad = ffn_total[:, 2 * hidden_width :].T
    head_total = sum(term.astype(F32) for term in along_col(head_near, along_y))
    first, second_half = head_total[:, :local_width], head_total[:, local_width:]
    qkv_grad = jnp.stack([first[:part], second_half[:part], first[part:]])
    out_grad = second_half[part:].T
    return (
        activation, latent_grad, embed_grad, modulate_grad, gains_grad, gate_grad,
        qkv_grad, text_kv_grad, out_grad, gate_up_grad, down_grad, unpatch_grad,
    )


def solution(mesh):
    placed = (
        P(None, "row", "col", None),
        P(),
        P("col", None, None),
        P(),
        P(None, "row", "col", None),
        P(),
        P(None, ("row", "col")),
        P(),
        P(),
        P(None, "col", "row"),
        P(None, "col", "row"),
        P("row", "col"),
        P(None, "col", "row"),
        P("row", "col"),
        P(),
    )
    return jax.shard_map(
        local,
        mesh=mesh,
        in_specs=placed,
        out_specs=(
            P(None, "row", "col", None),
            P(None, "row", "col", None),
            P(),
            P(None, ("row", "col")),
            P(),
            P(),
            P(None, "col", "row"),
            P(None, "col", "row"),
            P("row", "col"),
            P(None, "col", "row"),
            P("row", "col"),
            P(),
        ),
        check_vma=False,
    )
```

```python
import math
from functools import partial

import jax
import jax.numpy as jnp
import numpy as np
from jax import lax
from jax.experimental import pallas as pl
from jax.experimental.pallas import tpu as pltpu
from jax.sharding import PartitionSpec as P

HEADS = 24
HD = 64
GRID = 32
TOKENS = GRID * GRID
EPSILON = 1e-06
ROPE_BASE = 10000.0
MASKED = -1e30
F32 = jnp.float32
BF16 = jnp.bfloat16
ROWS = 8
COLS = 16
QUERY_BLOCK = 256
BLOCK = TOKENS // ROWS
PAIR = 2 * BLOCK
MIB = 2**20
SHARED = 320
CHUNK = 512
LIGHT = pl.CostEstimate(flops=1, bytes_accessed=1, transcendentals=0)


def dot(left, right, contract):
    return lax.dot_general(
        left, right, ((contract[:1], contract[1:]), ((), ())), preferred_element_type=F32
    )


def row_pairs(dx, dc):
    return [
        (((x + dx) % 4) * 2 + (c + dc) % 2, x * 2 + c) for x in range(4) for c in range(2)
    ]


def row_pairs_to(dx, dc):
    return [(dst, src) for src, dst in row_pairs(dx, dc)]


def from_chips(piece):
    return [piece] + [lax.ppermute(piece, "row", row_pairs(d, 0)) for d in (1, 2, 3)]


def with_other_core(pieces):
    quad = jnp.stack(pieces)
    return quad, lax.ppermute(quad, "row", row_pairs(0, 1))


def gather_near(piece):
    return with_other_core(from_chips(piece))


def sum_cores(own, other):
    other = lax.ppermute(other, "row", row_pairs(0, 1))
    return [(own[d].astype(F32) + other[d].astype(F32)).astype(BF16) for d in range(4)]


def to_chips(near):
    return [near[0]] + [lax.ppermute(near[d], "row", row_pairs_to(d, 0)) for d in (1, 2, 3)]


def col_pairs_to(dy, dz):
    return [(y * 4 + z, (y + dy) % 4 * 4 + (z + dz) % 4) for y in range(4) for z in range(4)]


def col_pairs(dy, dz):
    return [(dst, src) for src, dst in col_pairs_to(dy, dz)]


def from_col(piece, step):
    return [piece] + [lax.ppermute(piece, "col", col_pairs(*step(d))) for d in (1, 2, 3)]


def along_y(d):
    return (d, 0)


def along_z(d):
    return (0, d)


def along_col(parts, step):
    return [parts[0]] + [lax.ppermute(parts[d], "col", col_pairs_to(*step(d))) for d in (1, 2, 3)]


def send_all(piece, axis):
    copies = jnp.broadcast_to(piece, (lax.axis_size(axis),) + piece.shape)
    return lax.all_to_all(copies, axis, 0, 0)


def after(value, *others):
    return lax.optimization_barrier((value,) + others)[0]


def rope_tables():
    quarter = HD // 4
    frequency = np.float32(ROPE_BASE) ** (-np.arange(quarter, dtype=np.float32) / np.float32(quarter))
    place = np.arange(TOKENS)
    row = frequency[:, None] * (place // GRID).astype(np.float32)[None, :]
    col = frequency[:, None] * (place % GRID).astype(np.float32)[None, :]
    return np.stack([np.cos(row), np.sin(row), np.cos(col), np.sin(col)]).astype(np.float32)


def turn(v, table, sign):
    a, b, c, d = (v[k * 16 : (k + 1) * 16] for k in range(4))
    cr, sr, cc, sc = table[0], table[1] * sign, table[2], table[3] * sign
    return jnp.concatenate([a * cr - b * sr, a * sr + b * cr, c * cc - d * sc, c * sc + d * cc], 0)


def column_rms(v):
    return lax.rsqrt(jnp.mean(v * v, axis=0, keepdims=True) + EPSILON)


def normed(v, gain):
    return v * column_rms(v) * gain


def column_rms_back(v, u):
    scale = column_rms(v)
    return (u - v * (jnp.mean(u * v, axis=0, keepdims=True) * scale * scale)) * scale


def whole(shape):
    zeros = (0,) * len(shape)
    return pl.BlockSpec(shape, lambda *_: zeros, pipeline_mode=pl.Buffered(1))


def held():
    return pl.BlockSpec(memory_space=pltpu.VMEM)


def lane_block(rows, lanes):
    return pl.BlockSpec((rows, lanes), lambda t, *_: (0, t))


def row_block(rows, lanes):
    return pl.BlockSpec((rows, lanes), lambda t, *_: (t, 0))


def params(mib):
    return pltpu.CompilerParams(vmem_limit_bytes=mib * MIB, dimension_semantics=("arbitrary",))


def row_of_sums(v):
    return jnp.sum(v.T, axis=0, keepdims=True)


def attend_kernel(
    cap_ref, gate_ref, raw_ref, text_ref, gain_ref, table_ref, mixed_ref, lse_ref,
    q_ref, k_ref, v_ref, tk_ref, tv_ref,
):
    step = pl.program_id(0)
    heads = raw_ref.shape[1]

    @pl.when(step == 0)
    def _():
        table = table_ref[...]
        for h in range(heads):
            q = turn(normed(raw_ref[0, h], gain_ref[0, h]), table, 1.0).astype(BF16)
            q_ref[h] = q * jnp.asarray(0.125, BF16)
            k_ref[h] = turn(normed(raw_ref[1, h], gain_ref[1, h]), table, 1.0).T.astype(BF16)
            v_ref[h] = raw_ref[2, h].astype(BF16)
            tk_ref[h] = normed(text_ref[0, h], gain_ref[2, h]).T.astype(BF16)
            tv_ref[h] = text_ref[1, h].astype(BF16)

    slots = tk_ref.shape[1]
    mask = lax.broadcasted_iota(jnp.int32, (slots, QUERY_BLOCK), 0) < cap_ref[0]
    here = pl.ds(pl.multiple_of(step * QUERY_BLOCK, QUERY_BLOCK), QUERY_BLOCK)
    outs = []
    for h in range(heads):
        qb = q_ref[h, :, here]
        e = jnp.exp(dot(k_ref[h], qb, (1, 0)))
        total = jnp.sum(e, axis=0, keepdims=True)
        own = dot(v_ref[h], e.astype(BF16), (1, 0)) / total
        te = jnp.exp(jnp.where(mask, dot(tk_ref[h], qb, (1, 0)), MASKED))
        text_total = jnp.sum(te, axis=0, keepdims=True)
        text = dot(tv_ref[h], te.astype(BF16), (1, 0)) / text_total
        outs.append(own + gate_ref[h] * text)
        lse_ref[h, 0:1] = jnp.log(total)
        lse_ref[h, 1:2] = jnp.log(text_total)
    mixed_ref[...] = jnp.concatenate(outs, 0).astype(BF16)


def attend(raw, text_raw, gains, table, cap, gates):
    heads = raw.shape[1]
    slots = text_raw.shape[3]
    return pl.pallas_call(
        attend_kernel,
        grid_spec=pltpu.PrefetchScalarGridSpec(
            num_scalar_prefetch=2,
            grid=(TOKENS // QUERY_BLOCK,),
            in_specs=[
                whole((3, heads, HD, TOKENS)),
                whole((2, heads, HD, slots)),
                whole((3, heads, HD, 1)),
                whole((4, 16, TOKENS)),
            ],
            out_specs=[
                lane_block(heads * HD, QUERY_BLOCK),
                pl.BlockSpec((heads, 8, QUERY_BLOCK), lambda t, *_: (0, 0, t)),
            ],
            scratch_shapes=[
                pltpu.VMEM((heads, HD, TOKENS), BF16),
                pltpu.VMEM((heads, TOKENS, HD), BF16),
                pltpu.VMEM((heads, HD, TOKENS), BF16),
                pltpu.VMEM((heads, slots, HD), BF16),
                pltpu.VMEM((heads, HD, slots), BF16),
            ],
        ),
        out_shape=[
            jax.ShapeDtypeStruct((heads * HD, TOKENS), BF16),
            jax.ShapeDtypeStruct((heads, 8, TOKENS), F32),
        ],
        compiler_params=params(20),
        cost_estimate=LIGHT,
        name="attend",
    )(cap, gates, raw, text_raw, gains, table)


def text_back_kernel(
    cap_ref, gate_ref, q_raw_ref, text_ref, gain_ref, table_ref, lse_ref, grad_ref, caption_ref, held_ref,
    grads_ref, dq_ref, d_gain_ref, low_ref,
):
    del held_ref
    step = pl.program_id(0)
    heads, _, slots = low_ref.shape[1:]

    @pl.when(step == 0)
    def _():
        table = table_ref[...]
        mask = lax.broadcasted_iota(jnp.int32, (slots, TOKENS), 0) < cap_ref[0]
        for h in range(heads):
            gate = gate_ref[h]
            q = turn(normed(q_raw_ref[h], gain_ref[0, h]), table, 1.0).astype(BF16)
            q = q * jnp.asarray(0.125, BF16)
            tk = normed(text_ref[0, h], gain_ref[2, h]).astype(BF16)
            tv = text_ref[1, h].astype(BF16)
            g = grad_ref[h]
            tp = jnp.exp(jnp.where(mask, dot(tk, q, (0, 0)), MASKED) - lse_ref[h, 1:2])
            tpb = tp.astype(BF16)
            low_ref[1, h] = (dot(g, tpb, (1, 1)) * gate).astype(BF16)
            gate_terms = g.astype(F32) * dot(tv, tpb, (1, 0))
            tpd = tp * dot(tv, g, (0, 0)) * gate
            dts = (tpd - tp * jnp.sum(tpd, axis=0, keepdims=True)).astype(BF16)
            dq_ref[h] = dot(tk, dts, (1, 0))
            d_tk = dot(q, dts, (1, 1))
            values = text_ref[0, h]
            low_ref[0, h] = column_rms_back(values, d_tk * gain_ref[2, h]).astype(BF16)
            d_gain_ref[h, 0:1] = row_of_sums(values * column_rms(values) * d_tk)
            d_gain_ref[h, 1:2] = row_of_sums(gate_terms)

    d_text = low_ref[...].reshape(2 * heads * HD, slots)
    rows = grads_ref.shape[1]
    for k in range(grads_ref.shape[0]):
        grads_ref[k] = dot(caption_ref[:, k * rows : (k + 1) * rows], d_text, (0, 1)).astype(BF16)


def text_back(raw, text_raw, gains, table, lse, grads, cap, gates, caption, held):
    heads = raw.shape[1]
    slots = text_raw.shape[3]
    rows = caption.shape[1] // COLS
    lanes = 2 * heads * HD
    return pl.pallas_call(
        text_back_kernel,
        grid_spec=pltpu.PrefetchScalarGridSpec(
            num_scalar_prefetch=2,
            grid=(4,),
            in_specs=[
                pl.BlockSpec((None, heads, HD, TOKENS), lambda t, *_: (0, 0, 0, 0)),
                whole(text_raw.shape),
                whole(gains.shape),
                whole(table.shape),
                whole(lse.shape),
                whole(grads.shape),
                pl.BlockSpec((slots, 4 * rows), lambda t, *_: (0, t)),
                pl.BlockSpec(memory_space=pl.ANY),
            ],
            out_specs=[
                pl.BlockSpec((4, rows, lanes), lambda t, *_: (t, 0, 0)),
                pl.BlockSpec((heads, HD, TOKENS), lambda t, *_: (0, 0, 0)),
                pl.BlockSpec((heads, 8, HD), lambda t, *_: (0, 0, 0)),
            ],
            scratch_shapes=[pltpu.VMEM((2, heads, HD, slots), BF16)],
        ),
        out_shape=[
            jax.ShapeDtypeStruct(held.shape, BF16),
            jax.ShapeDtypeStruct((heads, HD, TOKENS), F32),
            jax.ShapeDtypeStruct((heads, 8, HD), F32),
        ],
        input_output_aliases={9: 0},
        compiler_params=params(58),
        cost_estimate=LIGHT,
        name="text_back",
    )(cap, gates, raw, text_raw, gains, table, lse, grads, caption, held)


def attend_back_kernel(
    raw_ref, gain_ref, table_ref, lse_ref, grad_ref, dq_text_ref,
    d_raw_ref, d_gain_ref, dv_ref, dk_ref, dq_ref,
):
    table = table_ref[...]
    q = turn(normed(raw_ref[0], gain_ref[0]), table, 1.0).astype(BF16) * jnp.asarray(0.125, BF16)
    k = turn(normed(raw_ref[1], gain_ref[1]), table, 1.0)
    k, k_turned = k.astype(BF16), k.T.astype(BF16)
    v_turned = raw_ref[2].T.astype(BF16)
    for first in range(0, TOKENS, QUERY_BLOCK):
        here = slice(first, first + QUERY_BLOCK)
        qb = q[:, here]
        gb = grad_ref[:, here]
        p = jnp.exp(dot(k_turned, qb, (1, 0)) - lse_ref[0:1, here])
        dv = dot(gb, p.astype(BF16), (1, 1))
        pd = p * dot(v_turned, gb, (1, 0))
        ds = (pd - p * jnp.sum(pd, axis=0, keepdims=True)).astype(BF16)
        dq_ref[:, here] = dot(k, ds, (1, 0)) + dq_text_ref[:, here]
        dk = dot(qb, ds, (1, 1))
        if first == 0:
            dv_ref[...] = dv
            dk_ref[...] = dk
        else:
            dv_ref[...] += dv
            dk_ref[...] += dk

    def raw_back(which, d_turned):
        spun = turn(d_turned.astype(BF16).astype(F32), table, -1.0)
        values = raw_ref[which]
        d_raw_ref[which] = column_rms_back(values, spun * gain_ref[which]).astype(BF16)
        d_gain_ref[which : which + 1] = row_of_sums(values * column_rms(values) * spun)

    raw_back(0, dq_ref[...] * 0.125)
    raw_back(1, dk_ref[...])
    d_raw_ref[2] = dv_ref[...].astype(BF16)


def attend_back(raw, gains, table, lse, grads, dq_text):
    heads = raw.shape[1]
    return pl.pallas_call(
        attend_back_kernel,
        grid=(heads,),
        in_specs=[
            pl.BlockSpec((3, None, HD, TOKENS), lambda h: (0, h, 0, 0)),
            pl.BlockSpec((3, None, HD, 1), lambda h: (0, h, 0, 0)),
            pl.BlockSpec((4, 16, TOKENS), lambda h: (0, 0, 0)),
            pl.BlockSpec((None, 8, TOKENS), lambda h: (h, 0, 0)),
            pl.BlockSpec((None, HD, TOKENS), lambda h: (h, 0, 0)),
            pl.BlockSpec((None, HD, TOKENS), lambda h: (h, 0, 0)),
        ],
        out_specs=[
            pl.BlockSpec((3, None, HD, TOKENS), lambda h: (0, h, 0, 0)),
            pl.BlockSpec((None, 8, HD), lambda h: (h, 0, 0)),
        ],
        scratch_shapes=[pltpu.VMEM((HD, TOKENS), F32) for _ in range(3)],
        out_shape=[
            jax.ShapeDtypeStruct((3, heads, HD, TOKENS), BF16),
            jax.ShapeDtypeStruct((heads, 8, HD), F32),
        ],
        compiler_params=params(58),
        cost_estimate=LIGHT,
        name="attend_back",
    )(raw, gains, table, lse, grads, dq_text)


def tile_places(chunk_first):
    r, c, k = np.meshgrid(np.arange(ROWS), np.arange(COLS), np.arange(8), indexing="ij")
    token = r * BLOCK + (k // 2) * GRID + c * 2 + k % 2
    source = (k * ROWS + r) * COLS + c if chunk_first else (r * COLS + c) * 8 + k
    places = np.zeros((TOKENS, TOKENS), np.float32)
    places[source.ravel(), token.ravel()] = 1.0
    return jnp.asarray(places, BF16)


def grid_shift(field, di, dj):
    step = di * GRID + dj
    moved = pltpu.roll(field, (-step) % TOKENS, 1) if step else field
    place = lax.broadcasted_iota(jnp.int32, field.shape, 1)
    row = place // GRID + di
    col = place % GRID + dj
    inside = (row >= 0) & (row < GRID) & (col >= 0) & (col < GRID)
    return jnp.where(inside, moved, 0.0)


def image_kernel(packed_ref, place_ref, patch_ref, cot_ref):
    for which, sign, out_ref in ((0, 1, patch_ref), (1, -1, cot_ref)):
        lanes = slice(which * 128, (which + 1) * 128)
        tiles = jnp.concatenate([packed_ref[r, :, lanes] for r in range(ROWS)], 0)
        turned = tiles.astype(F32).T
        chunks = jnp.concatenate([turned[k * 16 : (k + 1) * 16] for k in range(8)], 1)
        image = dot(chunks.astype(BF16), place_ref[...], (1, 0))
        for a in range(3):
            for b in range(3):
                first = (a * 3 + b) * 16
                out_ref[first : first + 16] = grid_shift(
                    image, sign * (a - 1), sign * (b - 1)
                ).astype(BF16)


def image_taps(packed):
    out = jax.ShapeDtypeStruct((144, TOKENS), BF16)
    return pl.pallas_call(
        image_kernel,
        out_shape=[out, out],
        compiler_params=pltpu.CompilerParams(vmem_limit_bytes=12 * MIB),
        cost_estimate=LIGHT,
        name="image_taps",
    )(packed, tile_places(True))


def field_of(taps, place, sign):
    total = jnp.zeros((16, TOKENS), F32)
    for a in range(3):
        for b in range(3):
            first = (a * 3 + b) * 16
            total = total + grid_shift(taps[first : first + 16], sign * (a - 1), sign * (b - 1))
    tiles = dot(total.astype(BF16), place, (1, 1))
    return [tiles[:, r * BLOCK : (r + 1) * BLOCK] for r in range(ROWS)]


def row_rms(v):
    return lax.rsqrt(jnp.mean(v * v, axis=-1, keepdims=True) + EPSILON)


def row_rms_back(v, scale, u):
    return (u - v * (jnp.mean(u * v, axis=-1, keepdims=True) * scale * scale)) * scale


def unpack_kernel(at_ref, *refs):
    piece_refs, (joined_ref, out_ref, turn_ref) = refs[:4], refs[4:]
    part = piece_refs[0].shape[1] // 2
    local_width = piece_refs[0].shape[2] // 2
    for dz in range(4):
        for dy in range(4):
            c = lax.rem(at_ref[2] + dy, 4) * 4 + lax.rem(at_ref[3] + dz, 4)
            rows = pl.ds(pl.multiple_of(c * part, part), part)
            piece = piece_refs[dz][dy]
            joined_ref[0, rows, :] = piece[:part, :local_width]
            joined_ref[1, rows, :] = piece[:part, local_width:]
            joined_ref[2, rows, :] = piece[part:, :local_width]
            turn_ref[rows, :] = piece[part:, local_width:]
    out_ref[...] = turn_ref[...].T


def unpack_head(at, pieces):
    _, rows, lanes = pieces[0].shape
    width, local_width = COLS * rows // 2, lanes // 2
    return pl.pallas_call(
        unpack_kernel,
        grid_spec=pltpu.PrefetchScalarGridSpec(
            num_scalar_prefetch=1,
            grid=(1,),
            in_specs=[whole(pieces[0].shape)] * 4,
            out_specs=[
                pl.BlockSpec((3, width, local_width), lambda t, at: (0, 0, 0)),
                pl.BlockSpec((local_width, width), lambda t, at: (0, 0)),
            ],
            scratch_shapes=[pltpu.VMEM((width, local_width), BF16)],
        ),
        out_shape=[
            jax.ShapeDtypeStruct((3, width, local_width), BF16),
            jax.ShapeDtypeStruct((local_width, width), BF16),
        ],
        compiler_params=params(14),
        cost_estimate=LIGHT,
        name="unpack_head",
    )(at, *pieces)


def text_kernel(at_ref, p0_ref, p1_ref, p2_ref, p3_ref, caption_ref, raw_ref):
    rows = p0_ref.shape[1]
    total = 0.0
    for dy, ref in enumerate((p0_ref, p1_ref, p2_ref, p3_ref)):
        for dz in range(4):
            c = lax.rem(at_ref[2] + dy, 4) * 4 + lax.rem(at_ref[3] + dz, 4)
            lanes = pl.ds(pl.multiple_of(c * rows, rows), rows)
            total = total + dot(ref[dz], caption_ref[:, lanes], (0, 1))
    raw_ref[...] = total


def text_project(at, pieces, caption):
    lanes = pieces[0].shape[2]
    slots = caption.shape[0]
    return pl.pallas_call(
        text_kernel,
        grid_spec=pltpu.PrefetchScalarGridSpec(
            num_scalar_prefetch=1,
            grid=(1,),
            in_specs=[whole(pieces[0].shape)] * 4 + [whole(caption.shape)],
            out_specs=pl.BlockSpec((lanes, slots), lambda t, at: (0, 0)),
        ),
        out_shape=jax.ShapeDtypeStruct((lanes, slots), F32),
        compiler_params=params(16),
        cost_estimate=LIGHT,
        name="text_project",
    )(at, *pieces, caption)


def qkv_kernel(patch_ref, embed_ref, vec_ref, weight_ref, raw_ref):
    x = dot(patch_ref[...], embed_ref[...], (0, 0))
    h = (x * row_rms(x) * vec_ref[0:1]).astype(BF16)
    for s in range(3):
        raw_ref[s] = dot(h, weight_ref[s], (1, 0)).T


def qkv_project(patches, embed, vec, weight):
    part = weight.shape[2]
    return pl.pallas_call(
        qkv_kernel,
        grid=(TOKENS // PAIR,),
        in_specs=[lane_block(144, PAIR), whole(embed.shape), whole(vec.shape), whole(weight.shape)],
        out_specs=pl.BlockSpec((3, part, PAIR), lambda t: (0, 0, t)),
        out_shape=jax.ShapeDtypeStruct((3, part, TOKENS), F32),
        compiler_params=params(16),
        cost_estimate=LIGHT,
        name="qkv_project",
    )(patches, embed, vec, weight)


def joined(ref):
    return ref[...].reshape(-1, ref.shape[2])


def halves(core, first, second):
    return jnp.where(core == 0, first, second)


def forward_kernel(
    at_ref, near_ref, far_ref, out_near_ref, out_far_ref, patch_ref, embed_ref, vec_ref, ffn_ref,
    attn_ref, second_ref, gate_up_ref, hidden_ref, own_ref, other_ref,
):
    core = at_ref[1]
    hidden_width = hidden_ref.shape[1]
    x = dot(patch_ref[...], embed_ref[...], (0, 0))
    attn = dot(joined(near_ref), joined(out_near_ref), (0, 0))
    attn = attn + dot(joined(far_ref), joined(out_far_ref), (0, 0))
    attn_ref[...] = attn.astype(BF16)
    mid = x + vec_ref[1:2] * (attn * row_rms(attn))
    second = (mid * row_rms(mid) * vec_ref[2:3]).astype(BF16)
    second_ref[...] = second
    gate_up = dot(second, ffn_ref[:, : 2 * hidden_width], (1, 0))
    gate_up_ref[...] = gate_up.astype(BF16)
    gate = gate_up[:, :hidden_width]
    hidden = (gate * jax.nn.sigmoid(gate) * gate_up[:, hidden_width:]).astype(BF16)
    hidden_ref[...] = hidden
    part = dot(hidden, ffn_ref[:, 2 * hidden_width :], (1, 1)).astype(BF16)
    own_ref[0] = halves(core, part[:BLOCK], part[BLOCK:])
    other_ref[0] = halves(core, part[BLOCK:], part[:BLOCK])


def forward(at, mixed, out_whole, patches, embed, vec, ffn):
    width = embed.shape[1]
    part = mixed[0].shape[1]
    hidden_width = ffn.shape[1] // 3
    by_chip = pl.BlockSpec((1, BLOCK, width), lambda t, at: ((t - at[0] + 4) % 4, 0, 0))
    return pl.pallas_call(
        forward_kernel,
        grid_spec=pltpu.PrefetchScalarGridSpec(
            num_scalar_prefetch=1,
            grid=(4,),
            in_specs=[
                pl.BlockSpec((4, part, PAIR), lambda t, at: (0, 0, t)),
                pl.BlockSpec((4, part, PAIR), lambda t, at: (0, 0, t)),
                whole((4, part, width)),
                whole((4, part, width)),
                lane_block(144, PAIR),
                whole(embed.shape),
                whole(vec.shape),
                whole(ffn.shape),
            ],
            out_specs=[
                row_block(PAIR, width),
                row_block(PAIR, width),
                row_block(PAIR, 2 * hidden_width),
                row_block(PAIR, hidden_width),
                by_chip,
                by_chip,
            ],
        ),
        out_shape=[
            jax.ShapeDtypeStruct((TOKENS, width), BF16),
            jax.ShapeDtypeStruct((TOKENS, width), BF16),
            jax.ShapeDtypeStruct((TOKENS, 2 * hidden_width), BF16),
            jax.ShapeDtypeStruct((TOKENS, hidden_width), BF16),
            jax.ShapeDtypeStruct((4, BLOCK, width), BF16),
            jax.ShapeDtypeStruct((4, BLOCK, width), BF16),
        ],
        compiler_params=params(56),
        cost_estimate=LIGHT,
        name="forward",
    )(at, *mixed, *out_whole, patches, embed, vec, ffn)


def own_grad_kernel(p0_ref, p1_ref, p2_ref, p3_ref, cot_ref, unpatch_ref, vec_ref, d_ffn_ref, ffn_ref):
    ffn = sum(p[...].astype(F32) for p in (p0_ref, p1_ref, p2_ref, p3_ref))
    ffn_ref[...] = ffn
    d_last = dot(cot_ref[...], unpatch_ref[...], (0, 0))
    d_ffn_ref[...] = row_rms_back(ffn, row_rms(ffn), vec_ref[3:4] * d_last).astype(BF16)


def own_grad(pieces, cot_own, unpatch, vec):
    shape = (BLOCK, unpatch.shape[1])
    return pl.pallas_call(
        own_grad_kernel,
        out_shape=[jax.ShapeDtypeStruct(shape, BF16), jax.ShapeDtypeStruct(shape, F32)],
        compiler_params=pltpu.CompilerParams(vmem_limit_bytes=12 * MIB),
        cost_estimate=LIGHT,
        name="own_grad",
    )(*pieces, cot_own, unpatch, vec)


def own_kernel(
    at_ref, ffn_ref, attn_ref, patch_ref, cot_ref, embed_ref, unpatch_ref, vec_ref, place_ref,
    field_ref, unpatch_sum_ref, sums_ref, taps_ref,
):
    ffn = ffn_ref[...]
    d_last = dot(cot_ref[...], unpatch_ref[...], (0, 0))
    normed_ffn = ffn * row_rms(ffn)
    sums_ref[...] = jnp.broadcast_to(
        jnp.sum(normed_ffn * d_last, axis=0, keepdims=True), sums_ref.shape
    )
    attn = attn_ref[...].astype(F32)
    x = dot(patch_ref[...], embed_ref[...], (0, 0))
    last = (x + vec_ref[1:2] * (attn * row_rms(attn)) + vec_ref[3:4] * normed_ffn).astype(BF16)
    unpatch_sum_ref[...] = dot(cot_ref[...], last, (1, 0))
    taps_ref[...] = jnp.zeros_like(taps_ref)
    here = pl.multiple_of((2 * at_ref[0] + at_ref[1]) * BLOCK, BLOCK)
    taps_ref[:, pl.ds(here, BLOCK)] = dot(unpatch_ref[...], last, (1, 1))
    for r, tile in enumerate(field_of(taps_ref[...], place_ref[...], 1)):
        field_ref[r] = tile


def own_block(at, ffn, attn, patches, cot_taps, embed, unpatch, vec, place):
    width = embed.shape[1]
    lanes = pl.BlockSpec((144, BLOCK), lambda t, at: (0, 2 * at[0] + at[1]))
    return pl.pallas_call(
        own_kernel,
        grid_spec=pltpu.PrefetchScalarGridSpec(
            num_scalar_prefetch=1,
            grid=(1,),
            in_specs=[
                whole((BLOCK, width)),
                pl.BlockSpec((BLOCK, width), lambda t, at: (2 * at[0] + at[1], 0)),
                lanes,
                lanes,
                whole(embed.shape),
                whole(unpatch.shape),
                whole(vec.shape),
                whole(place.shape),
            ],
            out_specs=[
                pl.BlockSpec((ROWS, 16, BLOCK), lambda t, at: (0, 0, 0)),
                pl.BlockSpec((144, width), lambda t, at: (0, 0)),
                pl.BlockSpec((8, width), lambda t, at: (0, 0)),
            ],
            scratch_shapes=[pltpu.VMEM((144, TOKENS), F32)],
        ),
        out_shape=[
            jax.ShapeDtypeStruct((ROWS, 16, BLOCK), F32),
            jax.ShapeDtypeStruct((144, width), F32),
            jax.ShapeDtypeStruct((8, width), F32),
        ],
        compiler_params=params(14),
        cost_estimate=LIGHT,
        name="own_block",
    )(at, ffn, attn, patches, cot_taps, embed, unpatch, vec, place)


def backward_kernel(
    at_ref, own_ref, other_ref, ffn_ref, out_near_ref, out_far_ref, gate_up_ref, attn_ref,
    patch_ref, embed_ref, cot_ref, unpatch_ref, vec_ref,
    d_ffn_ref, d_gate_up_ref, d_attn_ref, d_mid_ref, mixed_own_ref, mixed_other_ref, sums_ref,
):
    step = pl.program_id(0)
    chip, core = at_ref[0], at_ref[1]
    hidden_width = d_gate_up_ref.shape[1] // 2
    own, other = own_ref[0], other_ref[0]
    d_ffn = jnp.concatenate([halves(core, own, other), halves(core, other, own)], 0)
    d_ffn_ref[...] = d_ffn
    d_hidden = dot(d_ffn, ffn_ref[:, 2 * hidden_width :], (1, 0))
    gate = gate_up_ref[:, :hidden_width].astype(F32)
    up = gate_up_ref[:, hidden_width:].astype(F32)
    sigma = jax.nn.sigmoid(gate)
    silu = gate * sigma
    d_gate = d_hidden * up * (sigma + silu * (1.0 - sigma))
    d_gate_up = jnp.concatenate([d_gate.astype(BF16), (d_hidden * silu).astype(BF16)], 1)
    d_gate_up_ref[...] = d_gate_up
    d_second = dot(d_gate_up, ffn_ref[:, : 2 * hidden_width], (1, 1))

    x = dot(patch_ref[...], embed_ref[...], (0, 0))
    attn = attn_ref[...].astype(F32)
    attn_scale = row_rms(attn)
    attn_normed = attn * attn_scale
    mid = x + vec_ref[1:2] * attn_normed
    mid_scale = row_rms(mid)
    mid_sum = jnp.sum(mid * mid_scale * d_second, axis=0, keepdims=True)
    d_last = dot(cot_ref[...], unpatch_ref[...], (0, 0))
    place = lax.broadcasted_iota(jnp.int32, (PAIR, 1), 0) // BLOCK
    mine = (place == core) & (step == chip)
    d_mid = row_rms_back(mid, mid_scale, vec_ref[2:3] * d_second) + jnp.where(mine, d_last, 0.0)
    d_mid_ref[...] = d_mid.astype(BF16)
    attn_sum = jnp.sum(attn_normed * d_mid, axis=0, keepdims=True)
    d_attn = row_rms_back(attn, attn_scale, vec_ref[1:2] * d_mid).astype(BF16)
    d_attn_ref[...] = d_attn
    for weight_ref, part_ref in ((out_near_ref, mixed_own_ref), (out_far_ref, mixed_other_ref)):
        part_ref[...] = dot(joined(weight_ref), d_attn, (1, 1)).astype(BF16).reshape(part_ref.shape)

    @pl.when(step == 0)
    def _():
        sums_ref[...] = jnp.zeros_like(sums_ref)

    sums_ref[0:1] += mid_sum
    sums_ref[1:2] += attn_sum


def backward(at, d_ffn, ffn, out_whole, gate_up, attn, patches, embed, cot_taps, unpatch, vec):
    width = embed.shape[1]
    part = out_whole[0].shape[1]
    hidden_width = ffn.shape[1] // 3
    by_chip = pl.BlockSpec((1, BLOCK, width), lambda t, at: ((t - at[0] + 4) % 4, 0, 0))
    parts = pl.BlockSpec((4, part, PAIR), lambda t, at: (0, 0, t))
    return pl.pallas_call(
        backward_kernel,
        grid_spec=pltpu.PrefetchScalarGridSpec(
            num_scalar_prefetch=1,
            grid=(4,),
            in_specs=[
                by_chip,
                by_chip,
                held(),
                held(),
                held(),
                row_block(PAIR, 2 * hidden_width),
                row_block(PAIR, width),
                lane_block(144, PAIR),
                whole(embed.shape),
                lane_block(144, PAIR),
                whole(unpatch.shape),
                whole(vec.shape),
            ],
            out_specs=[
                row_block(PAIR, width),
                row_block(PAIR, 2 * hidden_width),
                row_block(PAIR, width),
                row_block(PAIR, width),
                parts,
                parts,
                pl.BlockSpec((8, width), lambda t, at: (0, 0)),
            ],
        ),
        out_shape=[
            jax.ShapeDtypeStruct((TOKENS, width), BF16),
            jax.ShapeDtypeStruct((TOKENS, 2 * hidden_width), BF16),
            jax.ShapeDtypeStruct((TOKENS, width), BF16),
            jax.ShapeDtypeStruct((TOKENS, width), BF16),
            jax.ShapeDtypeStruct((4, part, TOKENS), BF16),
            jax.ShapeDtypeStruct((4, part, TOKENS), BF16),
            jax.ShapeDtypeStruct((8, width), F32),
        ],
        compiler_params=params(32),
        cost_estimate=LIGHT,
        name="backward",
    )(at, *d_ffn, ffn, *out_whole, gate_up, attn, patches, embed, cot_taps, unpatch, vec)


def weight_kernel(
    second_ref, d_gate_up_ref, d_ffn_ref, hidden_ref, near_ref, far_ref, d_attn_ref,
    grads_ref, out_near_ref, out_far_ref,
):
    step = pl.program_id(0)
    chunk, _, lanes = grads_ref.shape[0] // 4, *grads_ref.shape[1:]
    part = second_ref.shape[1] // chunk
    rows = jnp.concatenate(
        [
            dot(second_ref[...], d_gate_up_ref[...], (0, 0)).astype(BF16),
            dot(d_ffn_ref[...], hidden_ref[...], (0, 0)).astype(BF16),
        ],
        1,
    )
    groups = rows.shape[1] // lanes
    first = grads_ref.shape[1] - groups * part
    for c in range(chunk):
        for g in range(groups):
            grads_ref[step * chunk + c, first + g * part : first + (g + 1) * part] = rows[
                c * part : (c + 1) * part, g * lanes : (g + 1) * lanes
            ]
    out_near_ref[0] = dot(near_ref[0], d_attn_ref[...], (1, 0)).astype(BF16)
    out_far_ref[0] = dot(far_ref[0], d_attn_ref[...], (1, 0)).astype(BF16)


def weight_grads(second, d_gate_up, d_ffn, hidden, mixed, d_attn, text_rows):
    width = second.shape[1]
    heads_width = mixed[0].shape[1]
    lanes = 2 * heads_width
    grads = (COLS, text_rows + width // COLS * 3 * hidden.shape[1] // lanes, lanes)
    pieces = pl.BlockSpec((1, heads_width, TOKENS), lambda t: (t, 0, 0))
    out_piece = pl.BlockSpec((1, heads_width, width), lambda t: (t, 0, 0))
    out_shape = jax.ShapeDtypeStruct((4, heads_width, width), BF16)
    return pl.pallas_call(
        weight_kernel,
        grid=(4,),
        in_specs=[
            lane_block(TOKENS, width // 4),
            whole(d_gate_up.shape),
            lane_block(TOKENS, width // 4),
            whole(hidden.shape),
            pieces,
            pieces,
            whole(d_attn.shape),
        ],
        out_specs=[pl.BlockSpec(grads, lambda t: (0, 0, 0)), out_piece, out_piece],
        out_shape=[jax.ShapeDtypeStruct(grads, BF16), out_shape, out_shape],
        compiler_params=params(40),
        cost_estimate=LIGHT,
        name="weight_grads",
    )(second, d_gate_up, d_ffn, hidden, *mixed, d_attn)


def first_kernel(
    at_ref, gate_ref, patch_ref, embed_ref, vec_ref, weight_ref, d_raw_ref, d_mid_ref, place_ref, out_sum_ref,
    unpatch_sum_ref, back_sums_ref, own_sums_ref, head_ref, text_head_ref, gains_ref, mod_ref, activation_ref,
    own_pack_ref, other_pack_ref, p0_ref, p1_ref, p2_ref, p3_ref,
    taps_acc, embed_acc, first_acc, shared_acc, qkv_acc, turned_acc,
):
    step = pl.program_id(0)
    last = pl.num_programs(0) - 1
    x = dot(patch_ref[...], embed_ref[...], (0, 0))
    scale = row_rms(x)
    x_normed = x * scale
    h = (x_normed * vec_ref[0:1]).astype(BF16)
    d_h = dot(d_raw_ref[0], weight_ref[0], (0, 1))
    for s in (1, 2):
        d_h = d_h + dot(d_raw_ref[s], weight_ref[s], (0, 1))

    @pl.when(step == 0)
    def _():
        qkv_acc[...] = jnp.zeros_like(qkv_acc)
        embed_acc[...] = jnp.zeros_like(embed_acc)
        first_acc[...] = jnp.zeros_like(first_acc)

    qkv_acc[...] += dot(joined(d_raw_ref), h, (1, 0)).reshape(qkv_acc.shape)
    first_acc[0:1] += jnp.sum(x_normed * d_h, axis=0, keepdims=True)
    d_first = (d_mid_ref[...].astype(F32) + row_rms_back(x, scale, vec_ref[0:1] * d_h)).astype(BF16)
    embed_acc[...] += dot(patch_ref[...], d_first, (1, 0))
    here = pl.ds(pl.multiple_of(step * PAIR, PAIR), PAIR)
    taps_acc[:, here] = dot(embed_ref[...], d_first, (1, 1))

    @pl.when(step == last)
    def _():
        part = p0_ref.shape[1] // 2
        for s in range(4):
            turned_acc[s] = (qkv_acc[s] if s < 3 else out_sum_ref[...]).T.astype(BF16)
        for dz, ref in enumerate((p0_ref, p1_ref, p2_ref, p3_ref)):
            z = lax.rem(at_ref[3] + dz, 4)
            for y in range(4):
                dy = lax.rem(y - at_ref[2] + 4, 4)
                first = pl.multiple_of((y * 4 + z) * part, part)
                pieces = [turned_acc[s, pl.ds(first, part), :] for s in range(4)]
                for k in range(2):
                    ref[dy, k * part : (k + 1) * part] = jnp.concatenate(
                        pieces[2 * k : 2 * k + 2], 1
                    )
        terms = jnp.concatenate(
            [first_acc[0:1], back_sums_ref[1:2], back_sums_ref[0:1], own_sums_ref[0:1]], 0
        )
        gates = [jnp.tanh(mod_ref[k : k + 1]) for k in (1, 3)]
        into = jnp.concatenate(
            [1.0 + mod_ref[0:1], gates[0], 1.0 + mod_ref[2:3], gates[1]], 0
        )
        d_gains = terms * into
        slope = jnp.concatenate(
            [jnp.ones_like(gates[0]), 1.0 - gates[0] * gates[0]] * 1
            + [jnp.ones_like(gates[0]), 1.0 - gates[1] * gates[1]],
            0,
        )
        d_modulation = terms * gains_ref[0:4] * slope
        heads = head_ref.shape[0]
        width = d_gains.shape[1]
        rows = [head_ref[h] for h in range(heads)], [text_head_ref[h] for h in range(heads)]
        own = jnp.concatenate(
            [
                jnp.concatenate([r[0:2] for r in rows[0]], 1),
                jnp.concatenate([r[0:1] for r in rows[1]], 1),
                jnp.zeros((5, heads * HD), F32),
            ],
            0,
        )
        own = jnp.concatenate([own, jnp.zeros((8, width - heads * HD), F32)], 1)
        row_at = 2 * at_ref[0] + at_ref[1]
        own = pltpu.roll(own, row_at * (heads * HD), 1)
        lane = lax.broadcasted_iota(jnp.int32, (1, width), 1)
        gate_row = jnp.zeros((1, width), F32)
        for h in range(heads):
            total = jnp.sum(rows[1][h][1:2], axis=1, keepdims=True)
            total = total * (1.0 - gate_ref[h] * gate_ref[h])
            gate_row = gate_row + jnp.where(lane == row_at * heads + h, total, 0.0)
        small = jnp.concatenate(
            [d_gains, own[0:3], gate_row, jnp.zeros((24, width), F32)], 0
        )
        for tile in range(12):
            lanes = slice(tile * 128, (tile + 1) * 128)
            first = tile * SHARED
            shared_acc[first : first + 144] = embed_acc[:, lanes].astype(BF16)
            shared_acc[first + 144 : first + 288] = unpatch_sum_ref[:, lanes].astype(BF16)
            shared_acc[first + 288 : first + SHARED] = small[:, lanes].astype(BF16)
        shared_acc[12 * SHARED :] = jnp.zeros((8 * CHUNK - 12 * SHARED, 128), BF16)
        latent = field_of(taps_acc[...], place_ref[...], -1)
        rows = [
            d_modulation[q : q + 1, tile * 128 : (tile + 1) * 128]
            for q in range(4)
            for tile in range(12)
        ]
        for r in range(ROWS):
            ahead = lax.rem(r // 2 - at_ref[0] + 4, 4)
            mods = jnp.concatenate(rows[6 * r : 6 * r + 6] + [jnp.zeros((10, 128), F32)], 0)
            piece = jnp.concatenate(
                [
                    shared_acc[r * CHUNK : (r + 1) * CHUNK],
                    activation_ref[r].astype(BF16),
                    latent[r].astype(BF16),
                    mods.astype(BF16),
                ],
                0,
            )

            @pl.when(at_ref[1] == r % 2)
            def _():
                own_pack_ref[ahead] = piece

            @pl.when(at_ref[1] != r % 2)
            def _():
                other_pack_ref[ahead] = piece


def first_back(
    at, gates, patches, embed, vec, weight, d_raw, d_mid, place, out_sum, unpatch_sum, back_sums, own_sums,
    head, text_head, gains, modulation, activation,
):
    width = embed.shape[1]
    part = weight.shape[2]
    pack = (4, CHUNK + 48, 128)
    grads = (4, 2 * width // COLS, 2 * part)
    rest = (place, out_sum, unpatch_sum, back_sums, own_sums, head, text_head, gains, modulation, activation)
    return pl.pallas_call(
        first_kernel,
        grid_spec=pltpu.PrefetchScalarGridSpec(
            num_scalar_prefetch=2,
            grid=(TOKENS // PAIR,),
            in_specs=[
                lane_block(144, PAIR),
                whole(embed.shape),
                whole(vec.shape),
                whole(weight.shape),
                pl.BlockSpec((3, part, PAIR), lambda t, *_: (0, 0, t)),
                row_block(PAIR, width),
            ]
            + [whole(value.shape) for value in rest],
            out_specs=[pl.BlockSpec(pack, lambda t, *_: (0, 0, 0))] * 2
            + [pl.BlockSpec(grads, lambda t, *_: (0, 0, 0))] * 4,
            scratch_shapes=[
                pltpu.VMEM((144, TOKENS), F32),
                pltpu.VMEM((144, width), F32),
                pltpu.VMEM((8, width), F32),
                pltpu.VMEM((8 * CHUNK, 128), BF16),
                pltpu.VMEM((3, part, width), F32),
                pltpu.VMEM((4, width, part), BF16),
            ],
        ),
        out_shape=[jax.ShapeDtypeStruct(pack, BF16)] * 2 + [jax.ShapeDtypeStruct(grads, BF16)] * 4,
        compiler_params=params(58),
        cost_estimate=LIGHT,
        name="first_back",
    )(at, gates, patches, embed, vec, weight, d_raw, d_mid, *rest)


def local(
    latent, condition, caption, cap_len, cotangent, embed_weight, modulate_weight, norm_gains,
    cross_gate, qkv_weight, text_kv_weight, out_weight, gate_up_weight, down_weight, unpatch_weight,
):
    images, _, _, channels = latent.shape
    width = embed_weight.shape[3]
    local_width = qkv_weight.shape[2]
    heads = local_width // HD
    hidden_width = down_weight.shape[0]
    taps = 9 * channels
    row_at = lax.axis_index("row")
    col_at = lax.axis_index("col")
    at = jnp.stack([row_at // 2, row_at % 2, col_at // 4, col_at % 4]).astype(jnp.int32)
    tile = latent.shape[1] * latent.shape[2] * channels

    cond_low = jax.nn.silu(condition.astype(F32)).astype(BF16)
    mod_piece = jnp.dot(cond_low, modulate_weight, preferred_element_type=F32)
    mod_columns = mod_piece.shape[1]
    mod_high = mod_piece.astype(BF16)
    mod_low = (mod_piece - mod_high.astype(F32)).astype(BF16)

    packed = jnp.concatenate(
        [latent.reshape(images, tile), cotangent.reshape(images, tile), mod_high, mod_low], axis=1
    )
    packed = jnp.pad(packed, ((0, 0), (0, 2 * local_width - packed.shape[1])))

    head_piece = jnp.concatenate(
        [
            jnp.concatenate([qkv_weight[0], qkv_weight[1]], axis=1),
            jnp.concatenate([qkv_weight[2], out_weight.T], axis=1),
        ]
    )
    text_piece = jnp.concatenate([text_kv_weight[0], text_kv_weight[1]], axis=1)
    head_pieces = from_col(head_piece, along_y)
    text_pieces = from_col(text_piece, along_z)
    packed = lax.all_to_all(packed, "col", 0, 0, tiled=True)
    packed, *text_pieces = lax.optimization_barrier((packed, *text_pieces))
    packed = send_all(packed, "row")
    patches, cot_taps = image_taps(packed)
    head_own = jnp.stack(head_pieces)
    head_beside = [lax.ppermute(head_own, "col", col_pairs(0, d)) for d in (1, 3)]
    text_own = jnp.stack(text_pieces)
    text_beside = [lax.ppermute(text_own, "col", col_pairs(d, 0)) for d in (1, 3)]
    ffn_piece = jnp.concatenate([gate_up_weight[0], gate_up_weight[1], down_weight.T], axis=1)
    ffn_piece, patches, text_own, next_text, last_text, head_own, next_head, last_head = (
        lax.optimization_barrier((ffn_piece, patches, text_own, *text_beside, head_own, *head_beside))
    )
    head_apart = lax.ppermute(head_own, "col", col_pairs(0, 2))
    text_apart = lax.ppermute(text_own, "col", col_pairs(2, 0))
    ffn_whole = lax.all_gather(ffn_piece, "col", axis=0, tiled=True)
    head_pieces = [head_own, next_head, head_apart, last_head]
    text_pieces = [text_own, next_text, text_apart, last_text]
    qkv_whole, out_rows = unpack_head(at, head_pieces)
    out_beside = [lax.ppermute(out_rows, "row", row_pairs(d, 0)) for d in (1, 3)]

    mod_at = 2 * tile
    modulation = packed[:, :, mod_at : mod_at + mod_columns].astype(F32)
    modulation = modulation + packed[:, :, mod_at + mod_columns : mod_at + 2 * mod_columns].astype(F32)
    modulation = modulation.reshape(4, width)
    attn_gate = jnp.tanh(modulation[1])
    ffn_gate = jnp.tanh(modulation[3])
    vec = jnp.stack(
        [
            norm_gains[0] * (1.0 + modulation[0]),
            norm_gains[1] * attn_gate,
            norm_gains[2] * (1.0 + modulation[2]),
            norm_gains[3] * ffn_gate,
        ]
    )
    vec = jnp.pad(vec, ((0, 4), (0, 0)))
    embed = embed_weight.reshape(taps, width)
    unpatch = unpatch_weight.transpose(0, 1, 3, 2).reshape(taps, width)
    raw = qkv_project(patches, embed, vec, qkv_whole)
    raw, out_rows, next_out, last_out, *text_pieces = lax.optimization_barrier(
        (raw, out_rows, *out_beside, *text_pieces)
    )
    out_apart = lax.ppermute(out_rows, "row", row_pairs(2, 0))
    raw = raw.reshape(3, heads, HD, TOKENS)
    caption_rows = caption[0]
    text_raw = text_project(at, text_pieces, caption_rows)
    text_raw = text_raw.reshape(2, heads, HD, caption_rows.shape[0])
    head_gains = lax.dynamic_slice(norm_gains, (4, row_at * local_width), (3, local_width)).reshape(
        3, heads, HD, 1
    )
    head_gates = jnp.tanh(lax.dynamic_slice_in_dim(cross_gate, row_at * heads, heads))
    cap = lax.dynamic_slice_in_dim(cap_len, col_at, 1)
    table = jnp.asarray(rope_tables())
    mixed, lse = attend(raw, text_raw, head_gains, table, cap, head_gates)

    mixed, out_apart = lax.optimization_barrier((mixed, out_apart))
    mixed_pieces = from_chips(mixed)
    out_whole = with_other_core([out_rows, next_out, out_apart, last_out])
    mixed_whole = with_other_core(mixed_pieces)
    attn, second, gate_up, hidden, ffn_own, ffn_other = forward(
        at, mixed_whole, out_whole, patches, embed, vec, ffn_whole
    )
    place = tile_places(False)
    cot_own = lax.dynamic_slice_in_dim(cot_taps, row_at * BLOCK, BLOCK, 1)
    d_ffn_own, ffn_out = own_grad(
        to_chips(sum_cores(ffn_own, ffn_other)), cot_own, unpatch, vec
    )
    d_ffn_near = from_chips(d_ffn_own)
    activation_field, unpatch_sum, own_sums = own_block(
        at, ffn_out, attn, patches, cot_taps, embed, unpatch, vec, place
    )
    d_ffn_near = lax.optimization_barrier((*d_ffn_near, activation_field))[:4]
    d_ffn, d_gate_up, d_attn, d_mid, mixed_own, mixed_other, back_sums = backward(
        at, with_other_core(d_ffn_near), ffn_whole, out_whole, gate_up, attn, patches, embed, cot_taps,
        unpatch, vec,
    )
    mixed_near = sum_cores(mixed_own, mixed_other)
    mixed_terms = to_chips(mixed_near)
    text_rows = text_kv_weight.shape[1]
    grads, out_near, out_far = weight_grads(
        after(second, *mixed_near), d_gate_up, d_ffn, hidden, mixed_whole, d_attn, text_rows
    )
    *mixed_terms, grads, out_near, out_far = lax.optimization_barrier(
        (*mixed_terms, grads, out_near, out_far)
    )
    d_mixed = sum(term.astype(F32) for term in mixed_terms).astype(BF16)
    d_mixed = d_mixed.reshape(heads, HD, TOKENS)
    out_near = sum_cores(out_near, out_far)
    out_apart = lax.ppermute(out_near[2], "row", row_pairs_to(2, 0))

    grads, dq_text, d_text_head = text_back(
        raw, text_raw, head_gains, table, lse, d_mixed, cap, head_gates, caption_rows,
        after(grads, *out_near),
    )
    dq_text, grads, out_apart, *out_near = lax.optimization_barrier(
        (dq_text, grads, out_apart, *out_near)
    )
    d_raw, d_head = attend_back(raw, head_gains, table, lse, d_mixed, dq_text)
    out_beside = [lax.ppermute(out_near[d], "row", row_pairs_to(d, 0)) for d in (1, 3)]
    d_raw, *out_terms = lax.optimization_barrier((d_raw, out_near[0], out_apart, *out_beside))
    out_sum = sum(term.astype(F32) for term in out_terms)
    d_raw = d_raw.reshape(3, local_width, TOKENS)
    own_pack, other_pack, *head_parts = first_back(
        at, head_gates, patches, embed, vec, qkv_whole, d_raw, d_mid, place, out_sum, unpatch_sum,
        back_sums, own_sums, d_head, d_text_head, norm_gains, modulation, activation_field,
    )
    beside = [lax.ppermute(head_parts[d], "col", col_pairs_to(0, d)) for d in (1, 3)]

    row_terms = to_chips(sum_cores(own_pack, other_pack))
    row_pack = sum(term.astype(F32) for term in row_terms)
    fields = row_pack[CHUNK : CHUNK + 2 * channels].T.reshape(COLS, 8, 2 * channels)
    mod_sums = row_pack[CHUNK + 2 * channels : CHUNK + 2 * channels + 6].reshape(COLS, 8, 6)
    fields = jnp.concatenate([fields, mod_sums], axis=2).astype(BF16)
    fields = jnp.pad(fields, ((0, 0), (0, 0), (0, 128 - fields.shape[2])))
    shared = row_pack[:CHUNK].astype(BF16).reshape(COLS, CHUNK // COLS, 128)
    col_pack = lax.all_to_all(jnp.concatenate([shared, fields], axis=1), "col", 0, 0)
    col_pack, left, right = lax.optimization_barrier((col_pack, *beside))
    shared = jnp.sum(col_pack[:, : CHUNK // COLS].astype(F32), axis=0)
    shared, apart = lax.optimization_barrier(
        (send_all(shared.astype(BF16), "col"), head_parts[2])
    )
    shared = send_all(shared, "row").reshape(-1, 128)
    apart = lax.ppermute(apart, "col", col_pairs_to(0, 2))
    head_near = sum(term.astype(F32) for term in (head_parts[0], left, apart, right)).astype(BF16)
    shared = shared[: 12 * SHARED].reshape(12, SHARED, 128).astype(F32)
    fields = col_pack[:, CHUNK // COLS :]
    activation = fields[:, :, :channels].reshape(latent.shape)
    latent_grad = fields[:, :, channels : 2 * channels].reshape(latent.shape)
    modulate_grad = lax.dot_general(
        cond_low.astype(F32),
        fields[:, :, 2 * channels : 2 * channels + 6].reshape(images, mod_columns).astype(F32),
        (((0,), (0,)), ((), ())),
        precision=lax.Precision.HIGHEST,
        preferred_element_type=F32,
    )
    embed_grad = shared[:, :taps].transpose(1, 0, 2).reshape(embed_weight.shape)
    unpatch_grad = shared[:, taps : 2 * taps].reshape(12, 3, 3, channels, 128)
    unpatch_grad = unpatch_grad.transpose(1, 2, 0, 4, 3).reshape(unpatch_weight.shape)
    gains_grad = shared[:, 2 * taps : 2 * taps + 7].transpose(1, 0, 2).reshape(7, width)
    gate_grad = shared[0, 2 * taps + 7, :HEADS]

    part = width // COLS
    grads = lax.psum_scatter(
        grads.reshape(-1, 2 * local_width), "col", scatter_dimension=0, tiled=True
    ).astype(F32)
    text_kv_grad = jnp.stack([grads[:text_rows, :local_width], grads[:text_rows, local_width:]])
    ffn_total = jnp.concatenate(
        [grads[first : first + part] for first in range(text_rows, grads.shape[0], part)], axis=1
    )
    gate_up_grad = jnp.stack(
        [ffn_total[:, :hidden_width], ffn_total[:, hidden_width : 2 * hidden_width]]
    )
    down_grad = ffn_total[:, 2 * hidden_width :].T
    head_total = sum(term.astype(F32) for term in along_col(head_near, along_y))
    first, second_half = head_total[:, :local_width], head_total[:, local_width:]
    qkv_grad = jnp.stack([first[:part], second_half[:part], first[part:]])
    out_grad = second_half[part:].T
    return (
        activation, latent_grad, embed_grad, modulate_grad, gains_grad, gate_grad,
        qkv_grad, text_kv_grad, out_grad, gate_up_grad, down_grad, unpatch_grad,
    )


def solution(mesh):
    placed = (
        P(None, "row", "col", None),
        P(),
        P("col", None, None),
        P(),
        P(None, "row", "col", None),
        P(),
        P(None, ("row", "col")),
        P(),
        P(),
        P(None, "col", "row"),
        P(None, "col", "row"),
        P("row", "col"),
        P(None, "col", "row"),
        P("row", "col"),
        P(),
    )
    return jax.shard_map(
        local,
        mesh=mesh,
        in_specs=placed,
        out_specs=(
            P(None, "row", "col", None),
            P(None, "row", "col", None),
            P(),
            P(None, ("row", "col")),
            P(),
            P(),
            P(None, "col", "row"),
            P(None, "col", "row"),
            P("row", "col"),
            P(None, "col", "row"),
            P("row", "col"),
            P(),
        ),
        check_vma=False,
    )
```

```python
import math
from functools import partial

import jax
import jax.numpy as jnp
import numpy as np
from jax import lax
from jax.experimental import pallas as pl
from jax.experimental.pallas import tpu as pltpu
from jax.sharding import PartitionSpec as P

HEADS = 24
HD = 64
GRID = 32
TOKENS = GRID * GRID
EPSILON = 1e-06
ROPE_BASE = 10000.0
MASKED = -1e30
F32 = jnp.float32
BF16 = jnp.bfloat16
ROWS = 8
COLS = 16
QUERY_BLOCK = 256
BLOCK = TOKENS // ROWS
PAIR = 2 * BLOCK
MIB = 2**20
SHARED = 320
CHUNK = 512
LIGHT = pl.CostEstimate(flops=1, bytes_accessed=1, transcendentals=0)


def dot(left, right, contract):
    return lax.dot_general(
        left, right, ((contract[:1], contract[1:]), ((), ())), preferred_element_type=F32
    )


def row_pairs(dx, dc):
    return [
        (((x + dx) % 4) * 2 + (c + dc) % 2, x * 2 + c) for x in range(4) for c in range(2)
    ]


def row_pairs_to(dx, dc):
    return [(dst, src) for src, dst in row_pairs(dx, dc)]


def from_chips(piece):
    return [piece] + [lax.ppermute(piece, "row", row_pairs(d, 0)) for d in (1, 2, 3)]


def with_other_core(pieces):
    quad = jnp.stack(pieces)
    return quad, lax.ppermute(quad, "row", row_pairs(0, 1))


def gather_near(piece):
    return with_other_core(from_chips(piece))


def sum_cores(own, other):
    other = lax.ppermute(other, "row", row_pairs(0, 1))
    return [(own[d].astype(F32) + other[d].astype(F32)).astype(BF16) for d in range(4)]


def to_chips(near):
    return [near[0]] + [lax.ppermute(near[d], "row", row_pairs_to(d, 0)) for d in (1, 2, 3)]


def col_pairs_to(dy, dz):
    return [(y * 4 + z, (y + dy) % 4 * 4 + (z + dz) % 4) for y in range(4) for z in range(4)]


def col_pairs(dy, dz):
    return [(dst, src) for src, dst in col_pairs_to(dy, dz)]


def from_col(piece, step):
    return [piece] + [lax.ppermute(piece, "col", col_pairs(*step(d))) for d in (1, 2, 3)]


def along_y(d):
    return (d, 0)


def along_z(d):
    return (0, d)


def along_col(parts, step):
    return [parts[0]] + [lax.ppermute(parts[d], "col", col_pairs_to(*step(d))) for d in (1, 2, 3)]


def send_all(piece, axis):
    copies = jnp.broadcast_to(piece, (lax.axis_size(axis),) + piece.shape)
    return lax.all_to_all(copies, axis, 0, 0)


def after(value, *others):
    return lax.optimization_barrier((value,) + others)[0]


def rope_tables():
    quarter = HD // 4
    frequency = np.float32(ROPE_BASE) ** (-np.arange(quarter, dtype=np.float32) / np.float32(quarter))
    place = np.arange(TOKENS)
    row = frequency[:, None] * (place // GRID).astype(np.float32)[None, :]
    col = frequency[:, None] * (place % GRID).astype(np.float32)[None, :]
    return np.stack([np.cos(row), np.sin(row), np.cos(col), np.sin(col)]).astype(np.float32)


def turn(v, table, sign):
    a, b, c, d = (v[k * 16 : (k + 1) * 16] for k in range(4))
    cr, sr, cc, sc = table[0], table[1] * sign, table[2], table[3] * sign
    return jnp.concatenate([a * cr - b * sr, a * sr + b * cr, c * cc - d * sc, c * sc + d * cc], 0)


def column_rms(v):
    return lax.rsqrt(jnp.mean(v * v, axis=0, keepdims=True) + EPSILON)


def normed(v, gain):
    return v * column_rms(v) * gain


def column_rms_back(v, u):
    scale = column_rms(v)
    return (u - v * (jnp.mean(u * v, axis=0, keepdims=True) * scale * scale)) * scale


def whole(shape):
    zeros = (0,) * len(shape)
    return pl.BlockSpec(shape, lambda *_: zeros, pipeline_mode=pl.Buffered(1))


def held():
    return pl.BlockSpec(memory_space=pltpu.VMEM)


def lane_block(rows, lanes):
    return pl.BlockSpec((rows, lanes), lambda t, *_: (0, t))


def row_block(rows, lanes):
    return pl.BlockSpec((rows, lanes), lambda t, *_: (t, 0))


def params(mib):
    return pltpu.CompilerParams(vmem_limit_bytes=mib * MIB, dimension_semantics=("arbitrary",))


def row_of_sums(v):
    return jnp.sum(v.T, axis=0, keepdims=True)


def attend_kernel(
    cap_ref, gate_ref, raw_ref, text_ref, gain_ref, table_ref, mixed_ref, lse_ref,
    q_ref, k_ref, v_ref, tk_ref, tv_ref,
):
    step = pl.program_id(0)
    heads = raw_ref.shape[1]

    @pl.when(step == 0)
    def _():
        table = table_ref[...]
        for h in range(heads):
            q = turn(normed(raw_ref[0, h], gain_ref[0, h]), table, 1.0).astype(BF16)
            q_ref[h] = q * jnp.asarray(0.125, BF16)
            k_ref[h] = turn(normed(raw_ref[1, h], gain_ref[1, h]), table, 1.0).T.astype(BF16)
            v_ref[h] = raw_ref[2, h].astype(BF16)
            tk_ref[h] = normed(text_ref[0, h], gain_ref[2, h]).T.astype(BF16)
            tv_ref[h] = text_ref[1, h].astype(BF16)

    slots = tk_ref.shape[1]
    mask = lax.broadcasted_iota(jnp.int32, (slots, QUERY_BLOCK), 0) < cap_ref[0]
    here = pl.ds(pl.multiple_of(step * QUERY_BLOCK, QUERY_BLOCK), QUERY_BLOCK)
    outs = []
    for h in range(heads):
        qb = q_ref[h, :, here]
        e = jnp.exp(dot(k_ref[h], qb, (1, 0)))
        total = jnp.sum(e, axis=0, keepdims=True)
        own = dot(v_ref[h], e.astype(BF16), (1, 0)) / total
        te = jnp.exp(jnp.where(mask, dot(tk_ref[h], qb, (1, 0)), MASKED))
        text_total = jnp.sum(te, axis=0, keepdims=True)
        text = dot(tv_ref[h], te.astype(BF16), (1, 0)) / text_total
        outs.append(own + gate_ref[h] * text)
        lse_ref[h, 0:1] = jnp.log(total)
        lse_ref[h, 1:2] = jnp.log(text_total)
    mixed_ref[...] = jnp.concatenate(outs, 0).astype(BF16)


def attend(raw, text_raw, gains, table, cap, gates):
    heads = raw.shape[1]
    slots = text_raw.shape[3]
    return pl.pallas_call(
        attend_kernel,
        grid_spec=pltpu.PrefetchScalarGridSpec(
            num_scalar_prefetch=2,
            grid=(TOKENS // QUERY_BLOCK,),
            in_specs=[
                whole((3, heads, HD, TOKENS)),
                whole((2, heads, HD, slots)),
                whole((3, heads, HD, 1)),
                whole((4, 16, TOKENS)),
            ],
            out_specs=[
                lane_block(heads * HD, QUERY_BLOCK),
                pl.BlockSpec((heads, 8, QUERY_BLOCK), lambda t, *_: (0, 0, t)),
            ],
            scratch_shapes=[
                pltpu.VMEM((heads, HD, TOKENS), BF16),
                pltpu.VMEM((heads, TOKENS, HD), BF16),
                pltpu.VMEM((heads, HD, TOKENS), BF16),
                pltpu.VMEM((heads, slots, HD), BF16),
                pltpu.VMEM((heads, HD, slots), BF16),
            ],
        ),
        out_shape=[
            jax.ShapeDtypeStruct((heads * HD, TOKENS), BF16),
            jax.ShapeDtypeStruct((heads, 8, TOKENS), F32),
        ],
        compiler_params=params(20),
        cost_estimate=LIGHT,
        name="attend",
    )(cap, gates, raw, text_raw, gains, table)


def text_back_kernel(
    cap_ref, gate_ref, q_raw_ref, text_ref, gain_ref, table_ref, lse_ref, grad_ref, caption_ref, held_ref,
    grads_ref, dq_ref, d_gain_ref, low_ref,
):
    del held_ref
    step = pl.program_id(0)
    heads, _, slots = low_ref.shape[1:]

    @pl.when(step == 0)
    def _():
        table = table_ref[...]
        mask = lax.broadcasted_iota(jnp.int32, (slots, TOKENS), 0) < cap_ref[0]
        for h in range(heads):
            gate = gate_ref[h]
            q = turn(normed(q_raw_ref[h], gain_ref[0, h]), table, 1.0).astype(BF16)
            q = q * jnp.asarray(0.125, BF16)
            tk = normed(text_ref[0, h], gain_ref[2, h]).astype(BF16)
            tv = text_ref[1, h].astype(BF16)
            g = grad_ref[h]
            tp = jnp.exp(jnp.where(mask, dot(tk, q, (0, 0)), MASKED) - lse_ref[h, 1:2])
            tpb = tp.astype(BF16)
            low_ref[1, h] = (dot(g, tpb, (1, 1)) * gate).astype(BF16)
            gate_terms = g.astype(F32) * dot(tv, tpb, (1, 0))
            tpd = tp * dot(tv, g, (0, 0)) * gate
            dts = (tpd - tp * jnp.sum(tpd, axis=0, keepdims=True)).astype(BF16)
            dq_ref[h] = dot(tk, dts, (1, 0))
            d_tk = dot(q, dts, (1, 1))
            values = text_ref[0, h]
            low_ref[0, h] = column_rms_back(values, d_tk * gain_ref[2, h]).astype(BF16)
            d_gain_ref[h, 0:1] = row_of_sums(values * column_rms(values) * d_tk)
            d_gain_ref[h, 1:2] = row_of_sums(gate_terms)

    d_text = low_ref[...].reshape(2 * heads * HD, slots)
    rows = grads_ref.shape[1]
    for k in range(grads_ref.shape[0]):
        grads_ref[k] = dot(caption_ref[:, k * rows : (k + 1) * rows], d_text, (0, 1)).astype(BF16)


def text_back(raw, text_raw, gains, table, lse, grads, cap, gates, caption, held):
    heads = raw.shape[1]
    slots = text_raw.shape[3]
    rows = caption.shape[1] // COLS
    lanes = 2 * heads * HD
    return pl.pallas_call(
        text_back_kernel,
        grid_spec=pltpu.PrefetchScalarGridSpec(
            num_scalar_prefetch=2,
            grid=(4,),
            in_specs=[
                pl.BlockSpec((None, heads, HD, TOKENS), lambda t, *_: (0, 0, 0, 0)),
                whole(text_raw.shape),
                whole(gains.shape),
                whole(table.shape),
                whole(lse.shape),
                whole(grads.shape),
                pl.BlockSpec((slots, 4 * rows), lambda t, *_: (0, t)),
                pl.BlockSpec(memory_space=pl.ANY),
            ],
            out_specs=[
                pl.BlockSpec((4, rows, lanes), lambda t, *_: (t, 0, 0)),
                pl.BlockSpec((heads, HD, TOKENS), lambda t, *_: (0, 0, 0)),
                pl.BlockSpec((heads, 8, HD), lambda t, *_: (0, 0, 0)),
            ],
            scratch_shapes=[pltpu.VMEM((2, heads, HD, slots), BF16)],
        ),
        out_shape=[
            jax.ShapeDtypeStruct(held.shape, BF16),
            jax.ShapeDtypeStruct((heads, HD, TOKENS), F32),
            jax.ShapeDtypeStruct((heads, 8, HD), F32),
        ],
        input_output_aliases={9: 0},
        compiler_params=params(58),
        cost_estimate=LIGHT,
        name="text_back",
    )(cap, gates, raw, text_raw, gains, table, lse, grads, caption, held)


def attend_back_kernel(
    raw_ref, gain_ref, table_ref, lse_ref, grad_ref, dq_text_ref,
    d_raw_ref, d_gain_ref, dv_ref, dk_ref, dq_ref,
):
    table = table_ref[...]
    q = turn(normed(raw_ref[0], gain_ref[0]), table, 1.0).astype(BF16) * jnp.asarray(0.125, BF16)
    k = turn(normed(raw_ref[1], gain_ref[1]), table, 1.0)
    k, k_turned = k.astype(BF16), k.T.astype(BF16)
    v_turned = raw_ref[2].T.astype(BF16)
    for first in range(0, TOKENS, QUERY_BLOCK):
        here = slice(first, first + QUERY_BLOCK)
        qb = q[:, here]
        gb = grad_ref[:, here]
        p = jnp.exp(dot(k_turned, qb, (1, 0)) - lse_ref[0:1, here])
        dv = dot(gb, p.astype(BF16), (1, 1))
        pd = p * dot(v_turned, gb, (1, 0))
        ds = (pd - p * jnp.sum(pd, axis=0, keepdims=True)).astype(BF16)
        dq_ref[:, here] = dot(k, ds, (1, 0)) + dq_text_ref[:, here]
        dk = dot(qb, ds, (1, 1))
        if first == 0:
            dv_ref[...] = dv
            dk_ref[...] = dk
        else:
            dv_ref[...] += dv
            dk_ref[...] += dk

    def raw_back(which, d_turned):
        spun = turn(d_turned.astype(BF16).astype(F32), table, -1.0)
        values = raw_ref[which]
        d_raw_ref[which] = column_rms_back(values, spun * gain_ref[which]).astype(BF16)
        d_gain_ref[which : which + 1] = row_of_sums(values * column_rms(values) * spun)

    raw_back(0, dq_ref[...] * 0.125)
    raw_back(1, dk_ref[...])
    d_raw_ref[2] = dv_ref[...].astype(BF16)


def attend_back(raw, gains, table, lse, grads, dq_text):
    heads = raw.shape[1]
    return pl.pallas_call(
        attend_back_kernel,
        grid=(heads,),
        in_specs=[
            pl.BlockSpec((3, None, HD, TOKENS), lambda h: (0, h, 0, 0)),
            pl.BlockSpec((3, None, HD, 1), lambda h: (0, h, 0, 0)),
            pl.BlockSpec((4, 16, TOKENS), lambda h: (0, 0, 0)),
            pl.BlockSpec((None, 8, TOKENS), lambda h: (h, 0, 0)),
            pl.BlockSpec((None, HD, TOKENS), lambda h: (h, 0, 0)),
            pl.BlockSpec((None, HD, TOKENS), lambda h: (h, 0, 0)),
        ],
        out_specs=[
            pl.BlockSpec((3, None, HD, TOKENS), lambda h: (0, h, 0, 0)),
            pl.BlockSpec((None, 8, HD), lambda h: (h, 0, 0)),
        ],
        scratch_shapes=[pltpu.VMEM((HD, TOKENS), F32) for _ in range(3)],
        out_shape=[
            jax.ShapeDtypeStruct((3, heads, HD, TOKENS), BF16),
            jax.ShapeDtypeStruct((heads, 8, HD), F32),
        ],
        compiler_params=params(58),
        cost_estimate=LIGHT,
        name="attend_back",
    )(raw, gains, table, lse, grads, dq_text)


def tile_places(chunk_first):
    r, c, k = np.meshgrid(np.arange(ROWS), np.arange(COLS), np.arange(8), indexing="ij")
    token = r * BLOCK + (k // 2) * GRID + c * 2 + k % 2
    source = (k * ROWS + r) * COLS + c if chunk_first else (r * COLS + c) * 8 + k
    places = np.zeros((TOKENS, TOKENS), np.float32)
    places[source.ravel(), token.ravel()] = 1.0
    return jnp.asarray(places, BF16)


def grid_shift(field, di, dj):
    step = di * GRID + dj
    moved = pltpu.roll(field, (-step) % TOKENS, 1) if step else field
    place = lax.broadcasted_iota(jnp.int32, field.shape, 1)
    row = place // GRID + di
    col = place % GRID + dj
    inside = (row >= 0) & (row < GRID) & (col >= 0) & (col < GRID)
    return jnp.where(inside, moved, 0.0)


def image_kernel(packed_ref, place_ref, patch_ref, cot_ref):
    for which, sign, out_ref in ((0, 1, patch_ref), (1, -1, cot_ref)):
        lanes = slice(which * 128, (which + 1) * 128)
        tiles = jnp.concatenate([packed_ref[r, :, lanes] for r in range(ROWS)], 0)
        turned = tiles.astype(F32).T
        chunks = jnp.concatenate([turned[k * 16 : (k + 1) * 16] for k in range(8)], 1)
        image = dot(chunks.astype(BF16), place_ref[...], (1, 0))
        for a in range(3):
            for b in range(3):
                first = (a * 3 + b) * 16
                out_ref[first : first + 16] = grid_shift(
                    image, sign * (a - 1), sign * (b - 1)
                ).astype(BF16)


def image_taps(packed):
    out = jax.ShapeDtypeStruct((144, TOKENS), BF16)
    return pl.pallas_call(
        image_kernel,
        out_shape=[out, out],
        compiler_params=pltpu.CompilerParams(vmem_limit_bytes=12 * MIB),
        cost_estimate=LIGHT,
        name="image_taps",
    )(packed, tile_places(True))


def field_of(taps, place, sign):
    total = jnp.zeros((16, TOKENS), F32)
    for a in range(3):
        for b in range(3):
            first = (a * 3 + b) * 16
            total = total + grid_shift(taps[first : first + 16], sign * (a - 1), sign * (b - 1))
    tiles = dot(total.astype(BF16), place, (1, 1))
    return [tiles[:, r * BLOCK : (r + 1) * BLOCK] for r in range(ROWS)]


def row_rms(v):
    return lax.rsqrt(jnp.mean(v * v, axis=-1, keepdims=True) + EPSILON)


def row_rms_back(v, scale, u):
    return (u - v * (jnp.mean(u * v, axis=-1, keepdims=True) * scale * scale)) * scale


def unpack_kernel(at_ref, *refs):
    piece_refs, (joined_ref, out_ref, turn_ref) = refs[:4], refs[4:]
    part = piece_refs[0].shape[1] // 2
    local_width = piece_refs[0].shape[2] // 2
    for dz in range(4):
        for dy in range(4):
            c = lax.rem(at_ref[2] + dy, 4) * 4 + lax.rem(at_ref[3] + dz, 4)
            rows = pl.ds(pl.multiple_of(c * part, part), part)
            piece = piece_refs[dz][dy]
            joined_ref[0, rows, :] = piece[:part, :local_width]
            joined_ref[1, rows, :] = piece[:part, local_width:]
            joined_ref[2, rows, :] = piece[part:, :local_width]
            turn_ref[rows, :] = piece[part:, local_width:]
    out_ref[...] = turn_ref[...].T


def unpack_head(at, pieces):
    _, rows, lanes = pieces[0].shape
    width, local_width = COLS * rows // 2, lanes // 2
    return pl.pallas_call(
        unpack_kernel,
        grid_spec=pltpu.PrefetchScalarGridSpec(
            num_scalar_prefetch=1,
            grid=(1,),
            in_specs=[whole(pieces[0].shape)] * 4,
            out_specs=[
                pl.BlockSpec((3, width, local_width), lambda t, at: (0, 0, 0)),
                pl.BlockSpec((local_width, width), lambda t, at: (0, 0)),
            ],
            scratch_shapes=[pltpu.VMEM((width, local_width), BF16)],
        ),
        out_shape=[
            jax.ShapeDtypeStruct((3, width, local_width), BF16),
            jax.ShapeDtypeStruct((local_width, width), BF16),
        ],
        compiler_params=params(14),
        cost_estimate=LIGHT,
        name="unpack_head",
    )(at, *pieces)


def text_kernel(at_ref, p0_ref, p1_ref, p2_ref, p3_ref, caption_ref, raw_ref):
    rows = p0_ref.shape[1]
    total = 0.0
    for dy, ref in enumerate((p0_ref, p1_ref, p2_ref, p3_ref)):
        for dz in range(4):
            c = lax.rem(at_ref[2] + dy, 4) * 4 + lax.rem(at_ref[3] + dz, 4)
            lanes = pl.ds(pl.multiple_of(c * rows, rows), rows)
            total = total + dot(ref[dz], caption_ref[:, lanes], (0, 1))
    raw_ref[...] = total


def text_project(at, pieces, caption):
    lanes = pieces[0].shape[2]
    slots = caption.shape[0]
    return pl.pallas_call(
        text_kernel,
        grid_spec=pltpu.PrefetchScalarGridSpec(
            num_scalar_prefetch=1,
            grid=(1,),
            in_specs=[whole(pieces[0].shape)] * 4 + [whole(caption.shape)],
            out_specs=pl.BlockSpec((lanes, slots), lambda t, at: (0, 0)),
        ),
        out_shape=jax.ShapeDtypeStruct((lanes, slots), F32),
        compiler_params=params(16),
        cost_estimate=LIGHT,
        name="text_project",
    )(at, *pieces, caption)


def qkv_kernel(patch_ref, embed_ref, vec_ref, weight_ref, raw_ref):
    x = dot(patch_ref[...], embed_ref[...], (0, 0))
    h = (x * row_rms(x) * vec_ref[0:1]).astype(BF16)
    for s in range(3):
        raw_ref[s] = dot(h, weight_ref[s], (1, 0)).T


def qkv_project(patches, embed, vec, weight):
    part = weight.shape[2]
    return pl.pallas_call(
        qkv_kernel,
        grid=(TOKENS // PAIR,),
        in_specs=[lane_block(144, PAIR), whole(embed.shape), whole(vec.shape), whole(weight.shape)],
        out_specs=pl.BlockSpec((3, part, PAIR), lambda t: (0, 0, t)),
        out_shape=jax.ShapeDtypeStruct((3, part, TOKENS), F32),
        compiler_params=params(16),
        cost_estimate=LIGHT,
        name="qkv_project",
    )(patches, embed, vec, weight)


def joined(ref):
    return ref[...].reshape(-1, ref.shape[2])


def halves(core, first, second):
    return jnp.where(core == 0, first, second)


def forward_kernel(
    at_ref, near_ref, far_ref, out_near_ref, out_far_ref, patch_ref, embed_ref, vec_ref, ffn_ref,
    attn_ref, second_ref, gate_up_ref, hidden_ref, own_ref, other_ref,
):
    core = at_ref[1]
    hidden_width = hidden_ref.shape[1]
    x = dot(patch_ref[...], embed_ref[...], (0, 0))
    attn = dot(joined(near_ref), joined(out_near_ref), (0, 0))
    attn = attn + dot(joined(far_ref), joined(out_far_ref), (0, 0))
    attn_ref[...] = attn.astype(BF16)
    mid = x + vec_ref[1:2] * (attn * row_rms(attn))
    second = (mid * row_rms(mid) * vec_ref[2:3]).astype(BF16)
    second_ref[...] = second
    gate_up = dot(second, ffn_ref[:, : 2 * hidden_width], (1, 0))
    gate_up_ref[...] = gate_up.astype(BF16)
    gate = gate_up[:, :hidden_width]
    hidden = (gate * jax.nn.sigmoid(gate) * gate_up[:, hidden_width:]).astype(BF16)
    hidden_ref[...] = hidden
    part = dot(hidden, ffn_ref[:, 2 * hidden_width :], (1, 1)).astype(BF16)
    own_ref[0] = halves(core, part[:BLOCK], part[BLOCK:])
    other_ref[0] = halves(core, part[BLOCK:], part[:BLOCK])


def forward(at, mixed, out_whole, patches, embed, vec, ffn):
    width = embed.shape[1]
    part = mixed[0].shape[1]
    hidden_width = ffn.shape[1] // 3
    by_chip = pl.BlockSpec((1, BLOCK, width), lambda t, at: ((t - at[0] + 4) % 4, 0, 0))
    return pl.pallas_call(
        forward_kernel,
        grid_spec=pltpu.PrefetchScalarGridSpec(
            num_scalar_prefetch=1,
            grid=(4,),
            in_specs=[
                pl.BlockSpec((4, part, PAIR), lambda t, at: (0, 0, t)),
                pl.BlockSpec((4, part, PAIR), lambda t, at: (0, 0, t)),
                whole((4, part, width)),
                whole((4, part, width)),
                lane_block(144, PAIR),
                whole(embed.shape),
                whole(vec.shape),
                whole(ffn.shape),
            ],
            out_specs=[
                row_block(PAIR, width),
                row_block(PAIR, width),
                row_block(PAIR, 2 * hidden_width),
                row_block(PAIR, hidden_width),
                by_chip,
                by_chip,
            ],
        ),
        out_shape=[
            jax.ShapeDtypeStruct((TOKENS, width), BF16),
            jax.ShapeDtypeStruct((TOKENS, width), BF16),
            jax.ShapeDtypeStruct((TOKENS, 2 * hidden_width), BF16),
            jax.ShapeDtypeStruct((TOKENS, hidden_width), BF16),
            jax.ShapeDtypeStruct((4, BLOCK, width), BF16),
            jax.ShapeDtypeStruct((4, BLOCK, width), BF16),
        ],
        compiler_params=params(56),
        cost_estimate=LIGHT,
        name="forward",
    )(at, *mixed, *out_whole, patches, embed, vec, ffn)


def own_grad_kernel(p0_ref, p1_ref, p2_ref, p3_ref, cot_ref, unpatch_ref, vec_ref, d_ffn_ref, ffn_ref):
    ffn = sum(p[...].astype(F32) for p in (p0_ref, p1_ref, p2_ref, p3_ref))
    ffn_ref[...] = ffn
    d_last = dot(cot_ref[...], unpatch_ref[...], (0, 0))
    d_ffn_ref[...] = row_rms_back(ffn, row_rms(ffn), vec_ref[3:4] * d_last).astype(BF16)


def own_grad(pieces, cot_own, unpatch, vec):
    shape = (BLOCK, unpatch.shape[1])
    return pl.pallas_call(
        own_grad_kernel,
        out_shape=[jax.ShapeDtypeStruct(shape, BF16), jax.ShapeDtypeStruct(shape, F32)],
        compiler_params=pltpu.CompilerParams(vmem_limit_bytes=12 * MIB),
        cost_estimate=LIGHT,
        name="own_grad",
    )(*pieces, cot_own, unpatch, vec)


def own_kernel(
    at_ref, ffn_ref, attn_ref, patch_ref, cot_ref, embed_ref, unpatch_ref, vec_ref, place_ref,
    field_ref, unpatch_sum_ref, sums_ref, taps_ref,
):
    ffn = ffn_ref[...]
    d_last = dot(cot_ref[...], unpatch_ref[...], (0, 0))
    normed_ffn = ffn * row_rms(ffn)
    sums_ref[...] = jnp.broadcast_to(
        jnp.sum(normed_ffn * d_last, axis=0, keepdims=True), sums_ref.shape
    )
    attn = attn_ref[...].astype(F32)
    x = dot(patch_ref[...], embed_ref[...], (0, 0))
    last = (x + vec_ref[1:2] * (attn * row_rms(attn)) + vec_ref[3:4] * normed_ffn).astype(BF16)
    unpatch_sum_ref[...] = dot(cot_ref[...], last, (1, 0))
    taps_ref[...] = jnp.zeros_like(taps_ref)
    here = pl.multiple_of((2 * at_ref[0] + at_ref[1]) * BLOCK, BLOCK)
    taps_ref[:, pl.ds(here, BLOCK)] = dot(unpatch_ref[...], last, (1, 1))
    for r, tile in enumerate(field_of(taps_ref[...], place_ref[...], 1)):
        field_ref[r] = tile


def own_block(at, ffn, attn, patches, cot_taps, embed, unpatch, vec, place):
    width = embed.shape[1]
    lanes = pl.BlockSpec((144, BLOCK), lambda t, at: (0, 2 * at[0] + at[1]))
    return pl.pallas_call(
        own_kernel,
        grid_spec=pltpu.PrefetchScalarGridSpec(
            num_scalar_prefetch=1,
            grid=(1,),
            in_specs=[
                whole((BLOCK, width)),
                pl.BlockSpec((BLOCK, width), lambda t, at: (2 * at[0] + at[1], 0)),
                lanes,
                lanes,
                whole(embed.shape),
                whole(unpatch.shape),
                whole(vec.shape),
                whole(place.shape),
            ],
            out_specs=[
                pl.BlockSpec((ROWS, 16, BLOCK), lambda t, at: (0, 0, 0)),
                pl.BlockSpec((144, width), lambda t, at: (0, 0)),
                pl.BlockSpec((8, width), lambda t, at: (0, 0)),
            ],
            scratch_shapes=[pltpu.VMEM((144, TOKENS), F32)],
        ),
        out_shape=[
            jax.ShapeDtypeStruct((ROWS, 16, BLOCK), F32),
            jax.ShapeDtypeStruct((144, width), F32),
            jax.ShapeDtypeStruct((8, width), F32),
        ],
        compiler_params=params(14),
        cost_estimate=LIGHT,
        name="own_block",
    )(at, ffn, attn, patches, cot_taps, embed, unpatch, vec, place)


def backward_kernel(
    at_ref, own_ref, other_ref, ffn_ref, out_near_ref, out_far_ref, gate_up_ref, attn_ref,
    patch_ref, embed_ref, cot_ref, unpatch_ref, vec_ref,
    d_ffn_ref, d_gate_up_ref, d_attn_ref, d_mid_ref, mixed_own_ref, mixed_other_ref, sums_ref,
):
    step = pl.program_id(0)
    chip, core = at_ref[0], at_ref[1]
    hidden_width = d_gate_up_ref.shape[1] // 2
    own, other = own_ref[0], other_ref[0]
    d_ffn = jnp.concatenate([halves(core, own, other), halves(core, other, own)], 0)
    d_ffn_ref[...] = d_ffn
    d_hidden = dot(d_ffn, ffn_ref[:, 2 * hidden_width :], (1, 0))
    gate = gate_up_ref[:, :hidden_width].astype(F32)
    up = gate_up_ref[:, hidden_width:].astype(F32)
    sigma = jax.nn.sigmoid(gate)
    silu = gate * sigma
    d_gate = d_hidden * up * (sigma + silu * (1.0 - sigma))
    d_gate_up = jnp.concatenate([d_gate.astype(BF16), (d_hidden * silu).astype(BF16)], 1)
    d_gate_up_ref[...] = d_gate_up
    d_second = dot(d_gate_up, ffn_ref[:, : 2 * hidden_width], (1, 1))

    x = dot(patch_ref[...], embed_ref[...], (0, 0))
    attn = attn_ref[...].astype(F32)
    attn_scale = row_rms(attn)
    attn_normed = attn * attn_scale
    mid = x + vec_ref[1:2] * attn_normed
    mid_scale = row_rms(mid)
    mid_sum = jnp.sum(mid * mid_scale * d_second, axis=0, keepdims=True)
    d_last = dot(cot_ref[...], unpatch_ref[...], (0, 0))
    place = lax.broadcasted_iota(jnp.int32, (PAIR, 1), 0) // BLOCK
    mine = (place == core) & (step == chip)
    d_mid = row_rms_back(mid, mid_scale, vec_ref[2:3] * d_second) + jnp.where(mine, d_last, 0.0)
    d_mid_ref[...] = d_mid.astype(BF16)
    attn_sum = jnp.sum(attn_normed * d_mid, axis=0, keepdims=True)
    d_attn = row_rms_back(attn, attn_scale, vec_ref[1:2] * d_mid).astype(BF16)
    d_attn_ref[...] = d_attn
    for weight_ref, part_ref in ((out_near_ref, mixed_own_ref), (out_far_ref, mixed_other_ref)):
        part_ref[...] = dot(joined(weight_ref), d_attn, (1, 1)).astype(BF16).reshape(part_ref.shape)

    @pl.when(step == 0)
    def _():
        sums_ref[...] = jnp.zeros_like(sums_ref)

    sums_ref[0:1] += mid_sum
    sums_ref[1:2] += attn_sum


def backward(at, d_ffn, ffn, out_whole, gate_up, attn, patches, embed, cot_taps, unpatch, vec):
    width = embed.shape[1]
    part = out_whole[0].shape[1]
    hidden_width = ffn.shape[1] // 3
    by_chip = pl.BlockSpec((1, BLOCK, width), lambda t, at: ((t - at[0] + 4) % 4, 0, 0))
    parts = pl.BlockSpec((4, part, PAIR), lambda t, at: (0, 0, t))
    return pl.pallas_call(
        backward_kernel,
        grid_spec=pltpu.PrefetchScalarGridSpec(
            num_scalar_prefetch=1,
            grid=(4,),
            in_specs=[
                by_chip,
                by_chip,
                held(),
                held(),
                held(),
                row_block(PAIR, 2 * hidden_width),
                row_block(PAIR, width),
                lane_block(144, PAIR),
                whole(embed.shape),
                lane_block(144, PAIR),
                whole(unpatch.shape),
                whole(vec.shape),
            ],
            out_specs=[
                row_block(PAIR, width),
                row_block(PAIR, 2 * hidden_width),
                row_block(PAIR, width),
                row_block(PAIR, width),
                parts,
                parts,
                pl.BlockSpec((8, width), lambda t, at: (0, 0)),
            ],
        ),
        out_shape=[
            jax.ShapeDtypeStruct((TOKENS, width), BF16),
            jax.ShapeDtypeStruct((TOKENS, 2 * hidden_width), BF16),
            jax.ShapeDtypeStruct((TOKENS, width), BF16),
            jax.ShapeDtypeStruct((TOKENS, width), BF16),
            jax.ShapeDtypeStruct((4, part, TOKENS), BF16),
            jax.ShapeDtypeStruct((4, part, TOKENS), BF16),
            jax.ShapeDtypeStruct((8, width), F32),
        ],
        compiler_params=params(32),
        cost_estimate=LIGHT,
        name="backward",
    )(at, *d_ffn, ffn, *out_whole, gate_up, attn, patches, embed, cot_taps, unpatch, vec)


def weight_kernel(
    second_ref, d_gate_up_ref, d_ffn_ref, hidden_ref, near_ref, far_ref, d_attn_ref,
    grads_ref, out_near_ref, out_far_ref,
):
    step = pl.program_id(0)
    chunk, _, lanes = grads_ref.shape[0] // 4, *grads_ref.shape[1:]
    part = second_ref.shape[1] // chunk
    rows = jnp.concatenate(
        [
            dot(second_ref[...], d_gate_up_ref[...], (0, 0)).astype(BF16),
            dot(d_ffn_ref[...], hidden_ref[...], (0, 0)).astype(BF16),
        ],
        1,
    )
    groups = rows.shape[1] // lanes
    first = grads_ref.shape[1] - groups * part
    for c in range(chunk):
        for g in range(groups):
            grads_ref[step * chunk + c, first + g * part : first + (g + 1) * part] = rows[
                c * part : (c + 1) * part, g * lanes : (g + 1) * lanes
            ]
    out_near_ref[0] = dot(near_ref[0], d_attn_ref[...], (1, 0)).astype(BF16)
    out_far_ref[0] = dot(far_ref[0], d_attn_ref[...], (1, 0)).astype(BF16)


def weight_grads(second, d_gate_up, d_ffn, hidden, mixed, d_attn, text_rows):
    width = second.shape[1]
    heads_width = mixed[0].shape[1]
    lanes = 2 * heads_width
    grads = (COLS, text_rows + width // COLS * 3 * hidden.shape[1] // lanes, lanes)
    pieces = pl.BlockSpec((1, heads_width, TOKENS), lambda t: (t, 0, 0))
    out_piece = pl.BlockSpec((1, heads_width, width), lambda t: (t, 0, 0))
    out_shape = jax.ShapeDtypeStruct((4, heads_width, width), BF16)
    return pl.pallas_call(
        weight_kernel,
        grid=(4,),
        in_specs=[
            lane_block(TOKENS, width // 4),
            whole(d_gate_up.shape),
            lane_block(TOKENS, width // 4),
            whole(hidden.shape),
            pieces,
            pieces,
            whole(d_attn.shape),
        ],
        out_specs=[pl.BlockSpec(grads, lambda t: (0, 0, 0)), out_piece, out_piece],
        out_shape=[jax.ShapeDtypeStruct(grads, BF16), out_shape, out_shape],
        compiler_params=params(40),
        cost_estimate=LIGHT,
        name="weight_grads",
    )(second, d_gate_up, d_ffn, hidden, *mixed, d_attn)


def first_kernel(
    at_ref, gate_ref, patch_ref, embed_ref, vec_ref, weight_ref, d_raw_ref, d_mid_ref, place_ref, out_sum_ref,
    unpatch_sum_ref, back_sums_ref, own_sums_ref, head_ref, text_head_ref, gains_ref, mod_ref, activation_ref,
    own_pack_ref, other_pack_ref, p0_ref, p1_ref, p2_ref, p3_ref,
    taps_acc, embed_acc, first_acc, shared_acc, qkv_acc, turned_acc,
):
    step = pl.program_id(0)
    last = pl.num_programs(0) - 1
    x = dot(patch_ref[...], embed_ref[...], (0, 0))
    scale = row_rms(x)
    x_normed = x * scale
    h = (x_normed * vec_ref[0:1]).astype(BF16)
    d_h = dot(d_raw_ref[0], weight_ref[0], (0, 1))
    for s in (1, 2):
        d_h = d_h + dot(d_raw_ref[s], weight_ref[s], (0, 1))

    @pl.when(step == 0)
    def _():
        qkv_acc[...] = jnp.zeros_like(qkv_acc)
        embed_acc[...] = jnp.zeros_like(embed_acc)
        first_acc[...] = jnp.zeros_like(first_acc)

    qkv_acc[...] += dot(joined(d_raw_ref), h, (1, 0)).reshape(qkv_acc.shape)
    first_acc[0:1] += jnp.sum(x_normed * d_h, axis=0, keepdims=True)
    d_first = (d_mid_ref[...].astype(F32) + row_rms_back(x, scale, vec_ref[0:1] * d_h)).astype(BF16)
    embed_acc[...] += dot(patch_ref[...], d_first, (1, 0))
    here = pl.ds(pl.multiple_of(step * PAIR, PAIR), PAIR)
    taps_acc[:, here] = dot(embed_ref[...], d_first, (1, 1))

    @pl.when(step == last)
    def _():
        part = p0_ref.shape[1] // 2
        for s in range(4):
            turned_acc[s] = (qkv_acc[s] if s < 3 else out_sum_ref[...]).T.astype(BF16)
        for dz, ref in enumerate((p0_ref, p1_ref, p2_ref, p3_ref)):
            z = lax.rem(at_ref[3] + dz, 4)
            for y in range(4):
                dy = lax.rem(y - at_ref[2] + 4, 4)
                first = pl.multiple_of((y * 4 + z) * part, part)
                pieces = [turned_acc[s, pl.ds(first, part), :] for s in range(4)]
                for k in range(2):
                    ref[dy, k * part : (k + 1) * part] = jnp.concatenate(
                        pieces[2 * k : 2 * k + 2], 1
                    )
        terms = jnp.concatenate(
            [first_acc[0:1], back_sums_ref[1:2], back_sums_ref[0:1], own_sums_ref[0:1]], 0
        )
        gates = [jnp.tanh(mod_ref[k : k + 1]) for k in (1, 3)]
        into = jnp.concatenate(
            [1.0 + mod_ref[0:1], gates[0], 1.0 + mod_ref[2:3], gates[1]], 0
        )
        d_gains = terms * into
        slope = jnp.concatenate(
            [jnp.ones_like(gates[0]), 1.0 - gates[0] * gates[0]] * 1
            + [jnp.ones_like(gates[0]), 1.0 - gates[1] * gates[1]],
            0,
        )
        d_modulation = terms * gains_ref[0:4] * slope
        heads = head_ref.shape[0]
        width = d_gains.shape[1]
        rows = [head_ref[h] for h in range(heads)], [text_head_ref[h] for h in range(heads)]
        own = jnp.concatenate(
            [
                jnp.concatenate([r[0:2] for r in rows[0]], 1),
                jnp.concatenate([r[0:1] for r in rows[1]], 1),
                jnp.zeros((5, heads * HD), F32),
            ],
            0,
        )
        own = jnp.concatenate([own, jnp.zeros((8, width - heads * HD), F32)], 1)
        row_at = 2 * at_ref[0] + at_ref[1]
        own = pltpu.roll(own, row_at * (heads * HD), 1)
        lane = lax.broadcasted_iota(jnp.int32, (1, width), 1)
        gate_row = jnp.zeros((1, width), F32)
        for h in range(heads):
            total = jnp.sum(rows[1][h][1:2], axis=1, keepdims=True)
            total = total * (1.0 - gate_ref[h] * gate_ref[h])
            gate_row = gate_row + jnp.where(lane == row_at * heads + h, total, 0.0)
        small = jnp.concatenate(
            [d_gains, own[0:3], gate_row, jnp.zeros((24, width), F32)], 0
        )
        for tile in range(12):
            lanes = slice(tile * 128, (tile + 1) * 128)
            first = tile * SHARED
            shared_acc[first : first + 144] = embed_acc[:, lanes].astype(BF16)
            shared_acc[first + 144 : first + 288] = unpatch_sum_ref[:, lanes].astype(BF16)
            shared_acc[first + 288 : first + SHARED] = small[:, lanes].astype(BF16)
        shared_acc[12 * SHARED :] = jnp.zeros((8 * CHUNK - 12 * SHARED, 128), BF16)
        latent = field_of(taps_acc[...], place_ref[...], -1)
        rows = [
            d_modulation[q : q + 1, tile * 128 : (tile + 1) * 128]
            for q in range(4)
            for tile in range(12)
        ]
        for r in range(ROWS):
            ahead = lax.rem(r // 2 - at_ref[0] + 4, 4)
            mods = jnp.concatenate(rows[6 * r : 6 * r + 6] + [jnp.zeros((10, 128), F32)], 0)
            piece = jnp.concatenate(
                [
                    shared_acc[r * CHUNK : (r + 1) * CHUNK],
                    activation_ref[r].astype(BF16),
                    latent[r].astype(BF16),
                    mods.astype(BF16),
                ],
                0,
            )

            @pl.when(at_ref[1] == r % 2)
            def _():
                own_pack_ref[ahead] = piece

            @pl.when(at_ref[1] != r % 2)
            def _():
                other_pack_ref[ahead] = piece


def first_back(
    at, gates, patches, embed, vec, weight, d_raw, d_mid, place, out_sum, unpatch_sum, back_sums, own_sums,
    head, text_head, gains, modulation, activation,
):
    width = embed.shape[1]
    part = weight.shape[2]
    pack = (4, CHUNK + 48, 128)
    grads = (4, 2 * width // COLS, 2 * part)
    rest = (place, out_sum, unpatch_sum, back_sums, own_sums, head, text_head, gains, modulation, activation)
    return pl.pallas_call(
        first_kernel,
        grid_spec=pltpu.PrefetchScalarGridSpec(
            num_scalar_prefetch=2,
            grid=(TOKENS // PAIR,),
            in_specs=[
                lane_block(144, PAIR),
                whole(embed.shape),
                whole(vec.shape),
                whole(weight.shape),
                pl.BlockSpec((3, part, PAIR), lambda t, *_: (0, 0, t)),
                row_block(PAIR, width),
            ]
            + [whole(value.shape) for value in rest],
            out_specs=[pl.BlockSpec(pack, lambda t, *_: (0, 0, 0))] * 2
            + [pl.BlockSpec(grads, lambda t, *_: (0, 0, 0))] * 4,
            scratch_shapes=[
                pltpu.VMEM((144, TOKENS), F32),
                pltpu.VMEM((144, width), F32),
                pltpu.VMEM((8, width), F32),
                pltpu.VMEM((8 * CHUNK, 128), BF16),
                pltpu.VMEM((3, part, width), F32),
                pltpu.VMEM((4, width, part), BF16),
            ],
        ),
        out_shape=[jax.ShapeDtypeStruct(pack, BF16)] * 2 + [jax.ShapeDtypeStruct(grads, BF16)] * 4,
        compiler_params=params(58),
        cost_estimate=LIGHT,
        name="first_back",
    )(at, gates, patches, embed, vec, weight, d_raw, d_mid, *rest)


def local(
    latent, condition, caption, cap_len, cotangent, embed_weight, modulate_weight, norm_gains,
    cross_gate, qkv_weight, text_kv_weight, out_weight, gate_up_weight, down_weight, unpatch_weight,
):
    images, _, _, channels = latent.shape
    width = embed_weight.shape[3]
    local_width = qkv_weight.shape[2]
    heads = local_width // HD
    hidden_width = down_weight.shape[0]
    taps = 9 * channels
    row_at = lax.axis_index("row")
    col_at = lax.axis_index("col")
    at = jnp.stack([row_at // 2, row_at % 2, col_at // 4, col_at % 4]).astype(jnp.int32)
    tile = latent.shape[1] * latent.shape[2] * channels

    cond_low = jax.nn.silu(condition.astype(F32)).astype(BF16)
    mod_piece = jnp.dot(cond_low, modulate_weight, preferred_element_type=F32)
    mod_columns = mod_piece.shape[1]
    mod_high = mod_piece.astype(BF16)
    mod_low = (mod_piece - mod_high.astype(F32)).astype(BF16)

    packed = jnp.concatenate(
        [latent.reshape(images, tile), cotangent.reshape(images, tile), mod_high, mod_low], axis=1
    )
    packed = jnp.pad(packed, ((0, 0), (0, 2 * local_width - packed.shape[1])))

    head_piece = jnp.concatenate(
        [
            jnp.concatenate([qkv_weight[0], qkv_weight[1]], axis=1),
            jnp.concatenate([qkv_weight[2], out_weight.T], axis=1),
        ]
    )
    text_piece = jnp.concatenate([text_kv_weight[0], text_kv_weight[1]], axis=1)
    head_pieces = from_col(head_piece, along_y)
    text_pieces = from_col(text_piece, along_z)
    packed = lax.all_to_all(packed, "col", 0, 0, tiled=True)
    packed, *text_pieces = lax.optimization_barrier((packed, *text_pieces))
    packed = send_all(packed, "row")
    patches, cot_taps = image_taps(packed)
    head_own = jnp.stack(head_pieces)
    head_beside = [lax.ppermute(head_own, "col", col_pairs(0, d)) for d in (1, 3)]
    text_own = jnp.stack(text_pieces)
    text_beside = [lax.ppermute(text_own, "col", col_pairs(d, 0)) for d in (1, 3)]
    ffn_piece = jnp.concatenate([gate_up_weight[0], gate_up_weight[1], down_weight.T], axis=1)
    ffn_piece, patches, text_own, next_text, last_text, head_own, next_head, last_head = (
        lax.optimization_barrier((ffn_piece, patches, text_own, *text_beside, head_own, *head_beside))
    )
    head_apart = lax.ppermute(head_own, "col", col_pairs(0, 2))
    text_apart = lax.ppermute(text_own, "col", col_pairs(2, 0))
    head_apart, text_apart = lax.optimization_barrier((head_apart, text_apart))
    head_pieces = [head_own, next_head, head_apart, last_head]
    text_pieces = [text_own, next_text, text_apart, last_text]
    qkv_whole, out_rows = unpack_head(at, head_pieces)
    ffn_whole = lax.all_gather(after(ffn_piece, out_rows), "col", axis=0, tiled=True)
    out_beside = [lax.ppermute(out_rows, "row", row_pairs(d, 0)) for d in (1, 3)]

    mod_at = 2 * tile
    modulation = packed[:, :, mod_at : mod_at + mod_columns].astype(F32)
    modulation = modulation + packed[:, :, mod_at + mod_columns : mod_at + 2 * mod_columns].astype(F32)
    modulation = modulation.reshape(4, width)
    attn_gate = jnp.tanh(modulation[1])
    ffn_gate = jnp.tanh(modulation[3])
    vec = jnp.stack(
        [
            norm_gains[0] * (1.0 + modulation[0]),
            norm_gains[1] * attn_gate,
            norm_gains[2] * (1.0 + modulation[2]),
            norm_gains[3] * ffn_gate,
        ]
    )
    vec = jnp.pad(vec, ((0, 4), (0, 0)))
    embed = embed_weight.reshape(taps, width)
    unpatch = unpatch_weight.transpose(0, 1, 3, 2).reshape(taps, width)
    raw = qkv_project(patches, embed, vec, qkv_whole)
    caption_rows = caption[0]
    text_raw = text_project(at, text_pieces, caption_rows)
    raw, text_raw, out_rows, next_out, last_out = lax.optimization_barrier(
        (raw, text_raw, out_rows, *out_beside)
    )
    out_apart = lax.ppermute(out_rows, "row", row_pairs(2, 0))
    raw = raw.reshape(3, heads, HD, TOKENS)
    text_raw = text_raw.reshape(2, heads, HD, caption_rows.shape[0])
    head_gains = lax.dynamic_slice(norm_gains, (4, row_at * local_width), (3, local_width)).reshape(
        3, heads, HD, 1
    )
    head_gates = jnp.tanh(lax.dynamic_slice_in_dim(cross_gate, row_at * heads, heads))
    cap = lax.dynamic_slice_in_dim(cap_len, col_at, 1)
    table = jnp.asarray(rope_tables())
    mixed, lse = attend(raw, text_raw, head_gains, table, cap, head_gates)

    mixed, out_apart = lax.optimization_barrier((mixed, out_apart))
    mixed_pieces = from_chips(mixed)
    out_whole = with_other_core([out_rows, next_out, out_apart, last_out])
    mixed_whole = with_other_core(mixed_pieces)
    attn, second, gate_up, hidden, ffn_own, ffn_other = forward(
        at, mixed_whole, out_whole, patches, embed, vec, ffn_whole
    )
    place = tile_places(False)
    cot_own = lax.dynamic_slice_in_dim(cot_taps, row_at * BLOCK, BLOCK, 1)
    d_ffn_own, ffn_out = own_grad(
        to_chips(sum_cores(ffn_own, ffn_other)), cot_own, unpatch, vec
    )
    d_ffn_near = from_chips(d_ffn_own)
    activation_field, unpatch_sum, own_sums = own_block(
        at, ffn_out, attn, patches, cot_taps, embed, unpatch, vec, place
    )
    d_ffn_near = lax.optimization_barrier((*d_ffn_near, activation_field))[:4]
    d_ffn, d_gate_up, d_attn, d_mid, mixed_own, mixed_other, back_sums = backward(
        at, with_other_core(d_ffn_near), ffn_whole, out_whole, gate_up, attn, patches, embed, cot_taps,
        unpatch, vec,
    )
    mixed_near = sum_cores(mixed_own, mixed_other)
    mixed_terms = to_chips(mixed_near)
    text_rows = text_kv_weight.shape[1]
    grads, out_near, out_far = weight_grads(
        after(second, *mixed_near), d_gate_up, d_ffn, hidden, mixed_whole, d_attn, text_rows
    )
    *mixed_terms, grads, out_near, out_far = lax.optimization_barrier(
        (*mixed_terms, grads, out_near, out_far)
    )
    d_mixed = sum(term.astype(F32) for term in mixed_terms).astype(BF16)
    d_mixed = d_mixed.reshape(heads, HD, TOKENS)
    out_near = sum_cores(out_near, out_far)
    out_apart = lax.ppermute(out_near[2], "row", row_pairs_to(2, 0))

    grads, dq_text, d_text_head = text_back(
        raw, text_raw, head_gains, table, lse, d_mixed, cap, head_gates, caption_rows,
        after(grads, *out_near),
    )
    dq_text, grads, out_apart, *out_near = lax.optimization_barrier(
        (dq_text, grads, out_apart, *out_near)
    )
    d_raw, d_head = attend_back(raw, head_gains, table, lse, d_mixed, dq_text)
    out_beside = [lax.ppermute(out_near[d], "row", row_pairs_to(d, 0)) for d in (1, 3)]
    d_raw, *out_terms = lax.optimization_barrier((d_raw, out_near[0], out_apart, *out_beside))
    out_sum = sum(term.astype(F32) for term in out_terms)
    d_raw = d_raw.reshape(3, local_width, TOKENS)
    own_pack, other_pack, *head_parts = first_back(
        at, head_gates, patches, embed, vec, qkv_whole, d_raw, d_mid, place, out_sum, unpatch_sum,
        back_sums, own_sums, d_head, d_text_head, norm_gains, modulation, activation_field,
    )
    beside = [lax.ppermute(head_parts[d], "col", col_pairs_to(0, d)) for d in (1, 3)]

    *row_terms, apart = lax.optimization_barrier(
        (*to_chips(sum_cores(own_pack, other_pack)), head_parts[2])
    )
    apart = lax.ppermute(apart, "col", col_pairs_to(0, 2))
    row_pack = sum(term.astype(F32) for term in row_terms)
    fields = row_pack[CHUNK : CHUNK + 2 * channels].T.reshape(COLS, 8, 2 * channels)
    mod_sums = row_pack[CHUNK + 2 * channels : CHUNK + 2 * channels + 6].reshape(COLS, 8, 6)
    fields = jnp.concatenate([fields, mod_sums], axis=2).astype(BF16)
    fields = jnp.pad(fields, ((0, 0), (0, 0), (0, 128 - fields.shape[2])))
    shared = row_pack[:CHUNK].astype(BF16).reshape(COLS, CHUNK // COLS, 128)
    col_pack = lax.all_to_all(jnp.concatenate([shared, fields], axis=1), "col", 0, 0)
    col_pack, left, right = lax.optimization_barrier((col_pack, *beside))
    shared = jnp.sum(col_pack[:, : CHUNK // COLS].astype(F32), axis=0)
    shared, apart = lax.optimization_barrier((send_all(shared.astype(BF16), "col"), apart))
    shared = send_all(shared, "row").reshape(-1, 128)
    head_near = sum(term.astype(F32) for term in (head_parts[0], left, apart, right)).astype(BF16)
    shared = shared[: 12 * SHARED].reshape(12, SHARED, 128).astype(F32)
    fields = col_pack[:, CHUNK // COLS :]
    activation = fields[:, :, :channels].reshape(latent.shape)
    latent_grad = fields[:, :, channels : 2 * channels].reshape(latent.shape)
    modulate_grad = lax.dot_general(
        cond_low.astype(F32),
        fields[:, :, 2 * channels : 2 * channels + 6].reshape(images, mod_columns).astype(F32),
        (((0,), (0,)), ((), ())),
        precision=lax.Precision.HIGHEST,
        preferred_element_type=F32,
    )
    embed_grad = shared[:, :taps].transpose(1, 0, 2).reshape(embed_weight.shape)
    unpatch_grad = shared[:, taps : 2 * taps].reshape(12, 3, 3, channels, 128)
    unpatch_grad = unpatch_grad.transpose(1, 2, 0, 4, 3).reshape(unpatch_weight.shape)
    gains_grad = shared[:, 2 * taps : 2 * taps + 7].transpose(1, 0, 2).reshape(7, width)
    gate_grad = shared[0, 2 * taps + 7, :HEADS]

    part = width // COLS
    grads = lax.psum_scatter(
        grads.reshape(-1, 2 * local_width), "col", scatter_dimension=0, tiled=True
    ).astype(F32)
    text_kv_grad = jnp.stack([grads[:text_rows, :local_width], grads[:text_rows, local_width:]])
    ffn_total = jnp.concatenate(
        [grads[first : first + part] for first in range(text_rows, grads.shape[0], part)], axis=1
    )
    gate_up_grad = jnp.stack(
        [ffn_total[:, :hidden_width], ffn_total[:, hidden_width : 2 * hidden_width]]
    )
    down_grad = ffn_total[:, 2 * hidden_width :].T
    head_total = sum(term.astype(F32) for term in along_col(head_near, along_y))
    first, second_half = head_total[:, :local_width], head_total[:, local_width:]
    qkv_grad = jnp.stack([first[:part], second_half[:part], first[part:]])
    out_grad = second_half[part:].T
    return (
        activation, latent_grad, embed_grad, modulate_grad, gains_grad, gate_grad,
        qkv_grad, text_kv_grad, out_grad, gate_up_grad, down_grad, unpatch_grad,
    )


def solution(mesh):
    placed = (
        P(None, "row", "col", None),
        P(),
        P("col", None, None),
        P(),
        P(None, "row", "col", None),
        P(),
        P(None, ("row", "col")),
        P(),
        P(),
        P(None, "col", "row"),
        P(None, "col", "row"),
        P("row", "col"),
        P(None, "col", "row"),
        P("row", "col"),
        P(),
    )
    return jax.shard_map(
        local,
        mesh=mesh,
        in_specs=placed,
        out_specs=(
            P(None, "row", "col", None),
            P(None, "row", "col", None),
            P(),
            P(None, ("row", "col")),
            P(),
            P(),
            P(None, "col", "row"),
            P(None, "col", "row"),
            P("row", "col"),
            P(None, "col", "row"),
            P("row", "col"),
            P(),
        ),
        check_vma=False,
    )
```

```python
import math
from functools import partial

import jax
import jax.numpy as jnp
import numpy as np
from jax import lax
from jax.experimental import pallas as pl
from jax.experimental.pallas import tpu as pltpu
from jax.sharding import PartitionSpec as P

HEADS = 24
HD = 64
GRID = 32
TOKENS = GRID * GRID
EPSILON = 1e-06
ROPE_BASE = 10000.0
MASKED = -1e30
F32 = jnp.float32
BF16 = jnp.bfloat16
ROWS = 8
COLS = 16
QUERY_BLOCK = 256
BLOCK = TOKENS // ROWS
PAIR = 2 * BLOCK
MIB = 2**20
SHARED = 320
CHUNK = 512
LIGHT = pl.CostEstimate(flops=1, bytes_accessed=1, transcendentals=0)


def dot(left, right, contract):
    return lax.dot_general(
        left, right, ((contract[:1], contract[1:]), ((), ())), preferred_element_type=F32
    )


def row_pairs(dx, dc):
    return [
        (((x + dx) % 4) * 2 + (c + dc) % 2, x * 2 + c) for x in range(4) for c in range(2)
    ]


def row_pairs_to(dx, dc):
    return [(dst, src) for src, dst in row_pairs(dx, dc)]


def from_chips(piece):
    return [piece] + [lax.ppermute(piece, "row", row_pairs(d, 0)) for d in (1, 2, 3)]


def with_other_core(pieces):
    quad = jnp.stack(pieces)
    return quad, lax.ppermute(quad, "row", row_pairs(0, 1))


def gather_near(piece):
    return with_other_core(from_chips(piece))


def sum_cores(own, other):
    other = lax.ppermute(other, "row", row_pairs(0, 1))
    return [(own[d].astype(F32) + other[d].astype(F32)).astype(BF16) for d in range(4)]


def to_chips(near):
    return [near[0]] + [lax.ppermute(near[d], "row", row_pairs_to(d, 0)) for d in (1, 2, 3)]


def col_pairs_to(dy, dz):
    return [(y * 4 + z, (y + dy) % 4 * 4 + (z + dz) % 4) for y in range(4) for z in range(4)]


def col_pairs(dy, dz):
    return [(dst, src) for src, dst in col_pairs_to(dy, dz)]


def from_col(piece, step):
    return [piece] + [lax.ppermute(piece, "col", col_pairs(*step(d))) for d in (1, 2, 3)]


def along_y(d):
    return (d, 0)


def along_z(d):
    return (0, d)


def along_col(parts, step):
    return [parts[0]] + [lax.ppermute(parts[d], "col", col_pairs_to(*step(d))) for d in (1, 2, 3)]


def send_all(piece, axis):
    copies = jnp.broadcast_to(piece, (lax.axis_size(axis),) + piece.shape)
    return lax.all_to_all(copies, axis, 0, 0)


def after(value, *others):
    return lax.optimization_barrier((value,) + others)[0]


def rope_tables():
    quarter = HD // 4
    frequency = np.float32(ROPE_BASE) ** (-np.arange(quarter, dtype=np.float32) / np.float32(quarter))
    place = np.arange(TOKENS)
    row = frequency[:, None] * (place // GRID).astype(np.float32)[None, :]
    col = frequency[:, None] * (place % GRID).astype(np.float32)[None, :]
    return np.stack([np.cos(row), np.sin(row), np.cos(col), np.sin(col)]).astype(np.float32)


def turn(v, table, sign):
    a, b, c, d = (v[k * 16 : (k + 1) * 16] for k in range(4))
    cr, sr, cc, sc = table[0], table[1] * sign, table[2], table[3] * sign
    return jnp.concatenate([a * cr - b * sr, a * sr + b * cr, c * cc - d * sc, c * sc + d * cc], 0)


def column_rms(v):
    return lax.rsqrt(jnp.mean(v * v, axis=0, keepdims=True) + EPSILON)


def normed(v, gain):
    return v * column_rms(v) * gain


def column_rms_back(v, u):
    scale = column_rms(v)
    return (u - v * (jnp.mean(u * v, axis=0, keepdims=True) * scale * scale)) * scale


def whole(shape):
    zeros = (0,) * len(shape)
    return pl.BlockSpec(shape, lambda *_: zeros, pipeline_mode=pl.Buffered(1))


def held():
    return pl.BlockSpec(memory_space=pltpu.VMEM)


def lane_block(rows, lanes):
    return pl.BlockSpec((rows, lanes), lambda t, *_: (0, t))


def row_block(rows, lanes):
    return pl.BlockSpec((rows, lanes), lambda t, *_: (t, 0))


def params(mib):
    return pltpu.CompilerParams(vmem_limit_bytes=mib * MIB, dimension_semantics=("arbitrary",))


def row_of_sums(v):
    return jnp.sum(v.T, axis=0, keepdims=True)


def attend_kernel(
    cap_ref, gate_ref, raw_ref, text_ref, gain_ref, table_ref, mixed_ref, lse_ref,
    q_ref, k_ref, v_ref, tk_ref, tv_ref,
):
    step = pl.program_id(0)
    heads = raw_ref.shape[1]

    @pl.when(step == 0)
    def _():
        table = table_ref[...]
        for h in range(heads):
            q = turn(normed(raw_ref[0, h], gain_ref[0, h]), table, 1.0).astype(BF16)
            q_ref[h] = q * jnp.asarray(0.125, BF16)
            k_ref[h] = turn(normed(raw_ref[1, h], gain_ref[1, h]), table, 1.0).T.astype(BF16)
            v_ref[h] = raw_ref[2, h].astype(BF16)
            tk_ref[h] = normed(text_ref[0, h], gain_ref[2, h]).T.astype(BF16)
            tv_ref[h] = text_ref[1, h].astype(BF16)

    slots = tk_ref.shape[1]
    mask = lax.broadcasted_iota(jnp.int32, (slots, QUERY_BLOCK), 0) < cap_ref[0]
    here = pl.ds(pl.multiple_of(step * QUERY_BLOCK, QUERY_BLOCK), QUERY_BLOCK)
    outs = []
    for h in range(heads):
        qb = q_ref[h, :, here]
        e = jnp.exp(dot(k_ref[h], qb, (1, 0)))
        total = jnp.sum(e, axis=0, keepdims=True)
        own = dot(v_ref[h], e.astype(BF16), (1, 0)) / total
        te = jnp.exp(jnp.where(mask, dot(tk_ref[h], qb, (1, 0)), MASKED))
        text_total = jnp.sum(te, axis=0, keepdims=True)
        text = dot(tv_ref[h], te.astype(BF16), (1, 0)) / text_total
        outs.append(own + gate_ref[h] * text)
        lse_ref[h, 0:1] = jnp.log(total)
        lse_ref[h, 1:2] = jnp.log(text_total)
    mixed_ref[...] = jnp.concatenate(outs, 0).astype(BF16)


def attend(raw, text_raw, gains, table, cap, gates):
    heads = raw.shape[1]
    slots = text_raw.shape[3]
    return pl.pallas_call(
        attend_kernel,
        grid_spec=pltpu.PrefetchScalarGridSpec(
            num_scalar_prefetch=2,
            grid=(TOKENS // QUERY_BLOCK,),
            in_specs=[
                whole((3, heads, HD, TOKENS)),
                whole((2, heads, HD, slots)),
                whole((3, heads, HD, 1)),
                whole((4, 16, TOKENS)),
            ],
            out_specs=[
                lane_block(heads * HD, QUERY_BLOCK),
                pl.BlockSpec((heads, 8, QUERY_BLOCK), lambda t, *_: (0, 0, t)),
            ],
            scratch_shapes=[
                pltpu.VMEM((heads, HD, TOKENS), BF16),
                pltpu.VMEM((heads, TOKENS, HD), BF16),
                pltpu.VMEM((heads, HD, TOKENS), BF16),
                pltpu.VMEM((heads, slots, HD), BF16),
                pltpu.VMEM((heads, HD, slots), BF16),
            ],
        ),
        out_shape=[
            jax.ShapeDtypeStruct((heads * HD, TOKENS), BF16),
            jax.ShapeDtypeStruct((heads, 8, TOKENS), F32),
        ],
        compiler_params=params(20),
        cost_estimate=LIGHT,
        name="attend",
    )(cap, gates, raw, text_raw, gains, table)


def text_back_kernel(
    cap_ref, gate_ref, q_raw_ref, text_ref, gain_ref, table_ref, lse_ref, grad_ref, caption_ref, held_ref,
    grads_ref, dq_ref, d_gain_ref, low_ref,
):
    del held_ref
    step = pl.program_id(0)
    heads, _, slots = low_ref.shape[1:]

    @pl.when(step == 0)
    def _():
        table = table_ref[...]
        mask = lax.broadcasted_iota(jnp.int32, (slots, TOKENS), 0) < cap_ref[0]
        for h in range(heads):
            gate = gate_ref[h]
            q = turn(normed(q_raw_ref[h], gain_ref[0, h]), table, 1.0).astype(BF16)
            q = q * jnp.asarray(0.125, BF16)
            tk = normed(text_ref[0, h], gain_ref[2, h]).astype(BF16)
            tv = text_ref[1, h].astype(BF16)
            g = grad_ref[h]
            tp = jnp.exp(jnp.where(mask, dot(tk, q, (0, 0)), MASKED) - lse_ref[h, 1:2])
            tpb = tp.astype(BF16)
            low_ref[1, h] = (dot(g, tpb, (1, 1)) * gate).astype(BF16)
            gate_terms = g.astype(F32) * dot(tv, tpb, (1, 0))
            tpd = tp * dot(tv, g, (0, 0)) * gate
            dts = (tpd - tp * jnp.sum(tpd, axis=0, keepdims=True)).astype(BF16)
            dq_ref[h] = dot(tk, dts, (1, 0))
            d_tk = dot(q, dts, (1, 1))
            values = text_ref[0, h]
            low_ref[0, h] = column_rms_back(values, d_tk * gain_ref[2, h]).astype(BF16)
            d_gain_ref[h, 0:1] = row_of_sums(values * column_rms(values) * d_tk)
            d_gain_ref[h, 1:2] = row_of_sums(gate_terms)

    d_text = low_ref[...].reshape(2 * heads * HD, slots)
    rows = grads_ref.shape[1]
    for k in range(grads_ref.shape[0]):
        grads_ref[k] = dot(caption_ref[:, k * rows : (k + 1) * rows], d_text, (0, 1)).astype(BF16)


def text_back(raw, text_raw, gains, table, lse, grads, cap, gates, caption, held):
    heads = raw.shape[1]
    slots = text_raw.shape[3]
    rows = caption.shape[1] // COLS
    lanes = 2 * heads * HD
    return pl.pallas_call(
        text_back_kernel,
        grid_spec=pltpu.PrefetchScalarGridSpec(
            num_scalar_prefetch=2,
            grid=(4,),
            in_specs=[
                pl.BlockSpec((None, heads, HD, TOKENS), lambda t, *_: (0, 0, 0, 0)),
                whole(text_raw.shape),
                whole(gains.shape),
                whole(table.shape),
                whole(lse.shape),
                whole(grads.shape),
                pl.BlockSpec((slots, 4 * rows), lambda t, *_: (0, t)),
                pl.BlockSpec(memory_space=pl.ANY),
            ],
            out_specs=[
                pl.BlockSpec((4, rows, lanes), lambda t, *_: (t, 0, 0)),
                pl.BlockSpec((heads, HD, TOKENS), lambda t, *_: (0, 0, 0)),
                pl.BlockSpec((heads, 8, HD), lambda t, *_: (0, 0, 0)),
            ],
            scratch_shapes=[pltpu.VMEM((2, heads, HD, slots), BF16)],
        ),
        out_shape=[
            jax.ShapeDtypeStruct(held.shape, BF16),
            jax.ShapeDtypeStruct((heads, HD, TOKENS), F32),
            jax.ShapeDtypeStruct((heads, 8, HD), F32),
        ],
        input_output_aliases={9: 0},
        compiler_params=params(58),
        cost_estimate=LIGHT,
        name="text_back",
    )(cap, gates, raw, text_raw, gains, table, lse, grads, caption, held)


def attend_back_kernel(
    raw_ref, gain_ref, table_ref, lse_ref, grad_ref, dq_text_ref,
    d_raw_ref, d_gain_ref, dv_ref, dk_ref, dq_ref,
):
    table = table_ref[...]
    q = turn(normed(raw_ref[0], gain_ref[0]), table, 1.0).astype(BF16) * jnp.asarray(0.125, BF16)
    k = turn(normed(raw_ref[1], gain_ref[1]), table, 1.0)
    k, k_turned = k.astype(BF16), k.T.astype(BF16)
    v_turned = raw_ref[2].T.astype(BF16)
    for first in range(0, TOKENS, QUERY_BLOCK):
        here = slice(first, first + QUERY_BLOCK)
        qb = q[:, here]
        gb = grad_ref[:, here]
        p = jnp.exp(dot(k_turned, qb, (1, 0)) - lse_ref[0:1, here])
        dv = dot(gb, p.astype(BF16), (1, 1))
        pd = p * dot(v_turned, gb, (1, 0))
        ds = (pd - p * jnp.sum(pd, axis=0, keepdims=True)).astype(BF16)
        dq_ref[:, here] = dot(k, ds, (1, 0)) + dq_text_ref[:, here]
        dk = dot(qb, ds, (1, 1))
        if first == 0:
            dv_ref[...] = dv
            dk_ref[...] = dk
        else:
            dv_ref[...] += dv
            dk_ref[...] += dk

    def raw_back(which, d_turned):
        spun = turn(d_turned.astype(BF16).astype(F32), table, -1.0)
        values = raw_ref[which]
        d_raw_ref[which] = column_rms_back(values, spun * gain_ref[which]).astype(BF16)
        d_gain_ref[which : which + 1] = row_of_sums(values * column_rms(values) * spun)

    raw_back(0, dq_ref[...] * 0.125)
    raw_back(1, dk_ref[...])
    d_raw_ref[2] = dv_ref[...].astype(BF16)


def attend_back(raw, gains, table, lse, grads, dq_text):
    heads = raw.shape[1]
    return pl.pallas_call(
        attend_back_kernel,
        grid=(heads,),
        in_specs=[
            pl.BlockSpec((3, None, HD, TOKENS), lambda h: (0, h, 0, 0)),
            pl.BlockSpec((3, None, HD, 1), lambda h: (0, h, 0, 0)),
            pl.BlockSpec((4, 16, TOKENS), lambda h: (0, 0, 0)),
            pl.BlockSpec((None, 8, TOKENS), lambda h: (h, 0, 0)),
            pl.BlockSpec((None, HD, TOKENS), lambda h: (h, 0, 0)),
            pl.BlockSpec((None, HD, TOKENS), lambda h: (h, 0, 0)),
        ],
        out_specs=[
            pl.BlockSpec((3, None, HD, TOKENS), lambda h: (0, h, 0, 0)),
            pl.BlockSpec((None, 8, HD), lambda h: (h, 0, 0)),
        ],
        scratch_shapes=[pltpu.VMEM((HD, TOKENS), F32) for _ in range(3)],
        out_shape=[
            jax.ShapeDtypeStruct((3, heads, HD, TOKENS), BF16),
            jax.ShapeDtypeStruct((heads, 8, HD), F32),
        ],
        compiler_params=params(58),
        cost_estimate=LIGHT,
        name="attend_back",
    )(raw, gains, table, lse, grads, dq_text)


def tile_places(chunk_first):
    r, c, k = np.meshgrid(np.arange(ROWS), np.arange(COLS), np.arange(8), indexing="ij")
    token = r * BLOCK + (k // 2) * GRID + c * 2 + k % 2
    source = (k * ROWS + r) * COLS + c if chunk_first else (r * COLS + c) * 8 + k
    places = np.zeros((TOKENS, TOKENS), np.float32)
    places[source.ravel(), token.ravel()] = 1.0
    return jnp.asarray(places, BF16)


def grid_shift(field, di, dj):
    step = di * GRID + dj
    moved = pltpu.roll(field, (-step) % TOKENS, 1) if step else field
    place = lax.broadcasted_iota(jnp.int32, field.shape, 1)
    row = place // GRID + di
    col = place % GRID + dj
    inside = (row >= 0) & (row < GRID) & (col >= 0) & (col < GRID)
    return jnp.where(inside, moved, 0.0)


def image_kernel(packed_ref, place_ref, patch_ref, cot_ref):
    for which, sign, out_ref in ((0, 1, patch_ref), (1, -1, cot_ref)):
        lanes = slice(which * 128, (which + 1) * 128)
        tiles = jnp.concatenate([packed_ref[r, :, lanes] for r in range(ROWS)], 0)
        turned = tiles.astype(F32).T
        chunks = jnp.concatenate([turned[k * 16 : (k + 1) * 16] for k in range(8)], 1)
        image = dot(chunks.astype(BF16), place_ref[...], (1, 0))
        for a in range(3):
            for b in range(3):
                first = (a * 3 + b) * 16
                out_ref[first : first + 16] = grid_shift(
                    image, sign * (a - 1), sign * (b - 1)
                ).astype(BF16)


def image_taps(packed):
    out = jax.ShapeDtypeStruct((144, TOKENS), BF16)
    return pl.pallas_call(
        image_kernel,
        out_shape=[out, out],
        compiler_params=pltpu.CompilerParams(vmem_limit_bytes=12 * MIB),
        cost_estimate=LIGHT,
        name="image_taps",
    )(packed, tile_places(True))


def field_of(taps, place, sign):
    total = jnp.zeros((16, TOKENS), F32)
    for a in range(3):
        for b in range(3):
            first = (a * 3 + b) * 16
            total = total + grid_shift(taps[first : first + 16], sign * (a - 1), sign * (b - 1))
    tiles = dot(total.astype(BF16), place, (1, 1))
    return [tiles[:, r * BLOCK : (r + 1) * BLOCK] for r in range(ROWS)]


def row_rms(v):
    return lax.rsqrt(jnp.mean(v * v, axis=-1, keepdims=True) + EPSILON)


def row_rms_back(v, scale, u):
    return (u - v * (jnp.mean(u * v, axis=-1, keepdims=True) * scale * scale)) * scale


def unpack_kernel(at_ref, *refs):
    piece_refs, (joined_ref, out_ref, turn_ref) = refs[:4], refs[4:]
    part = piece_refs[0].shape[1] // 2
    local_width = piece_refs[0].shape[2] // 2
    for dz in range(4):
        for dy in range(4):
            c = lax.rem(at_ref[2] + dy, 4) * 4 + lax.rem(at_ref[3] + dz, 4)
            rows = pl.ds(pl.multiple_of(c * part, part), part)
            piece = piece_refs[dz][dy]
            joined_ref[0, rows, :] = piece[:part, :local_width]
            joined_ref[1, rows, :] = piece[:part, local_width:]
            joined_ref[2, rows, :] = piece[part:, :local_width]
            turn_ref[rows, :] = piece[part:, local_width:]
    out_ref[...] = turn_ref[...].T


def unpack_head(at, pieces):
    _, rows, lanes = pieces[0].shape
    width, local_width = COLS * rows // 2, lanes // 2
    return pl.pallas_call(
        unpack_kernel,
        grid_spec=pltpu.PrefetchScalarGridSpec(
            num_scalar_prefetch=1,
            grid=(1,),
            in_specs=[whole(pieces[0].shape)] * 4,
            out_specs=[
                pl.BlockSpec((3, width, local_width), lambda t, at: (0, 0, 0)),
                pl.BlockSpec((local_width, width), lambda t, at: (0, 0)),
            ],
            scratch_shapes=[pltpu.VMEM((width, local_width), BF16)],
        ),
        out_shape=[
            jax.ShapeDtypeStruct((3, width, local_width), BF16),
            jax.ShapeDtypeStruct((local_width, width), BF16),
        ],
        compiler_params=params(14),
        cost_estimate=LIGHT,
        name="unpack_head",
    )(at, *pieces)


def text_kernel(at_ref, p0_ref, p1_ref, p2_ref, p3_ref, caption_ref, raw_ref):
    rows = p0_ref.shape[1]
    total = 0.0
    for dy, ref in enumerate((p0_ref, p1_ref, p2_ref, p3_ref)):
        for dz in range(4):
            c = lax.rem(at_ref[2] + dy, 4) * 4 + lax.rem(at_ref[3] + dz, 4)
            lanes = pl.ds(pl.multiple_of(c * rows, rows), rows)
            total = total + dot(ref[dz], caption_ref[:, lanes], (0, 1))
    raw_ref[...] = total


def text_project(at, pieces, caption):
    lanes = pieces[0].shape[2]
    slots = caption.shape[0]
    return pl.pallas_call(
        text_kernel,
        grid_spec=pltpu.PrefetchScalarGridSpec(
            num_scalar_prefetch=1,
            grid=(1,),
            in_specs=[whole(pieces[0].shape)] * 4 + [whole(caption.shape)],
            out_specs=pl.BlockSpec((lanes, slots), lambda t, at: (0, 0)),
        ),
        out_shape=jax.ShapeDtypeStruct((lanes, slots), F32),
        compiler_params=params(16),
        cost_estimate=LIGHT,
        name="text_project",
    )(at, *pieces, caption)


def qkv_kernel(patch_ref, embed_ref, vec_ref, weight_ref, raw_ref):
    x = dot(patch_ref[...], embed_ref[...], (0, 0))
    h = (x * row_rms(x) * vec_ref[0:1]).astype(BF16)
    for s in range(3):
        raw_ref[s] = dot(h, weight_ref[s], (1, 0)).T


def qkv_project(patches, embed, vec, weight):
    part = weight.shape[2]
    return pl.pallas_call(
        qkv_kernel,
        grid=(TOKENS // PAIR,),
        in_specs=[lane_block(144, PAIR), whole(embed.shape), whole(vec.shape), whole(weight.shape)],
        out_specs=pl.BlockSpec((3, part, PAIR), lambda t: (0, 0, t)),
        out_shape=jax.ShapeDtypeStruct((3, part, TOKENS), F32),
        compiler_params=params(16),
        cost_estimate=LIGHT,
        name="qkv_project",
    )(patches, embed, vec, weight)


def joined(ref):
    return ref[...].reshape(-1, ref.shape[2])


def halves(core, first, second):
    return jnp.where(core == 0, first, second)


def forward_kernel(
    at_ref, near_ref, far_ref, out_near_ref, out_far_ref, patch_ref, embed_ref, vec_ref, ffn_ref,
    attn_ref, second_ref, gate_up_ref, hidden_ref, own_ref, other_ref,
):
    core = at_ref[1]
    hidden_width = hidden_ref.shape[1]
    x = dot(patch_ref[...], embed_ref[...], (0, 0))
    attn = dot(joined(near_ref), joined(out_near_ref), (0, 0))
    attn = attn + dot(joined(far_ref), joined(out_far_ref), (0, 0))
    attn_ref[...] = attn.astype(BF16)
    mid = x + vec_ref[1:2] * (attn * row_rms(attn))
    second = (mid * row_rms(mid) * vec_ref[2:3]).astype(BF16)
    second_ref[...] = second
    gate_up = dot(second, ffn_ref[:, : 2 * hidden_width], (1, 0))
    gate_up_ref[...] = gate_up.astype(BF16)
    gate = gate_up[:, :hidden_width]
    hidden = (gate * jax.nn.sigmoid(gate) * gate_up[:, hidden_width:]).astype(BF16)
    hidden_ref[...] = hidden
    part = dot(hidden, ffn_ref[:, 2 * hidden_width :], (1, 1)).astype(BF16)
    own_ref[0] = halves(core, part[:BLOCK], part[BLOCK:])
    other_ref[0] = halves(core, part[BLOCK:], part[:BLOCK])


def forward(at, mixed, out_whole, patches, embed, vec, ffn):
    width = embed.shape[1]
    part = mixed[0].shape[1]
    hidden_width = ffn.shape[1] // 3
    by_chip = pl.BlockSpec((1, BLOCK, width), lambda t, at: ((t - at[0] + 4) % 4, 0, 0))
    return pl.pallas_call(
        forward_kernel,
        grid_spec=pltpu.PrefetchScalarGridSpec(
            num_scalar_prefetch=1,
            grid=(4,),
            in_specs=[
                pl.BlockSpec((4, part, PAIR), lambda t, at: (0, 0, t)),
                pl.BlockSpec((4, part, PAIR), lambda t, at: (0, 0, t)),
                whole((4, part, width)),
                whole((4, part, width)),
                lane_block(144, PAIR),
                whole(embed.shape),
                whole(vec.shape),
                whole(ffn.shape),
            ],
            out_specs=[
                row_block(PAIR, width),
                row_block(PAIR, width),
                row_block(PAIR, 2 * hidden_width),
                row_block(PAIR, hidden_width),
                by_chip,
                by_chip,
            ],
        ),
        out_shape=[
            jax.ShapeDtypeStruct((TOKENS, width), BF16),
            jax.ShapeDtypeStruct((TOKENS, width), BF16),
            jax.ShapeDtypeStruct((TOKENS, 2 * hidden_width), BF16),
            jax.ShapeDtypeStruct((TOKENS, hidden_width), BF16),
            jax.ShapeDtypeStruct((4, BLOCK, width), BF16),
            jax.ShapeDtypeStruct((4, BLOCK, width), BF16),
        ],
        compiler_params=params(56),
        cost_estimate=LIGHT,
        name="forward",
    )(at, *mixed, *out_whole, patches, embed, vec, ffn)


def own_grad_kernel(p0_ref, p1_ref, p2_ref, p3_ref, cot_ref, unpatch_ref, vec_ref, d_ffn_ref, ffn_ref):
    ffn = sum(p[...].astype(F32) for p in (p0_ref, p1_ref, p2_ref, p3_ref))
    ffn_ref[...] = ffn
    d_last = dot(cot_ref[...], unpatch_ref[...], (0, 0))
    d_ffn_ref[...] = row_rms_back(ffn, row_rms(ffn), vec_ref[3:4] * d_last).astype(BF16)


def own_grad(pieces, cot_own, unpatch, vec):
    shape = (BLOCK, unpatch.shape[1])
    return pl.pallas_call(
        own_grad_kernel,
        out_shape=[jax.ShapeDtypeStruct(shape, BF16), jax.ShapeDtypeStruct(shape, F32)],
        compiler_params=pltpu.CompilerParams(vmem_limit_bytes=58 * MIB),
        cost_estimate=LIGHT,
        name="own_grad",
    )(*pieces, cot_own, unpatch, vec)


def own_kernel(
    at_ref, ffn_ref, attn_ref, patch_ref, cot_ref, embed_ref, unpatch_ref, vec_ref, place_ref,
    field_ref, unpatch_sum_ref, sums_ref, taps_ref,
):
    ffn = ffn_ref[...]
    d_last = dot(cot_ref[...], unpatch_ref[...], (0, 0))
    normed_ffn = ffn * row_rms(ffn)
    sums_ref[...] = jnp.broadcast_to(
        jnp.sum(normed_ffn * d_last, axis=0, keepdims=True), sums_ref.shape
    )
    attn = attn_ref[...].astype(F32)
    x = dot(patch_ref[...], embed_ref[...], (0, 0))
    last = (x + vec_ref[1:2] * (attn * row_rms(attn)) + vec_ref[3:4] * normed_ffn).astype(BF16)
    unpatch_sum_ref[...] = dot(cot_ref[...], last, (1, 0))
    taps_ref[...] = jnp.zeros_like(taps_ref)
    here = pl.multiple_of((2 * at_ref[0] + at_ref[1]) * BLOCK, BLOCK)
    taps_ref[:, pl.ds(here, BLOCK)] = dot(unpatch_ref[...], last, (1, 1))
    for r, tile in enumerate(field_of(taps_ref[...], place_ref[...], 1)):
        field_ref[r] = tile


def own_block(at, ffn, attn, patches, cot_taps, embed, unpatch, vec, place):
    width = embed.shape[1]
    lanes = pl.BlockSpec((144, BLOCK), lambda t, at: (0, 2 * at[0] + at[1]))
    return pl.pallas_call(
        own_kernel,
        grid_spec=pltpu.PrefetchScalarGridSpec(
            num_scalar_prefetch=1,
            grid=(1,),
            in_specs=[
                whole((BLOCK, width)),
                pl.BlockSpec((BLOCK, width), lambda t, at: (2 * at[0] + at[1], 0)),
                lanes,
                lanes,
                whole(embed.shape),
                whole(unpatch.shape),
                whole(vec.shape),
                whole(place.shape),
            ],
            out_specs=[
                pl.BlockSpec((ROWS, 16, BLOCK), lambda t, at: (0, 0, 0)),
                pl.BlockSpec((144, width), lambda t, at: (0, 0)),
                pl.BlockSpec((8, width), lambda t, at: (0, 0)),
            ],
            scratch_shapes=[pltpu.VMEM((144, TOKENS), F32)],
        ),
        out_shape=[
            jax.ShapeDtypeStruct((ROWS, 16, BLOCK), F32),
            jax.ShapeDtypeStruct((144, width), F32),
            jax.ShapeDtypeStruct((8, width), F32),
        ],
        compiler_params=params(14),
        cost_estimate=LIGHT,
        name="own_block",
    )(at, ffn, attn, patches, cot_taps, embed, unpatch, vec, place)


def backward_kernel(
    at_ref, own_ref, other_ref, ffn_ref, out_near_ref, out_far_ref, gate_up_ref, attn_ref,
    patch_ref, embed_ref, cot_ref, unpatch_ref, vec_ref,
    d_ffn_ref, d_gate_up_ref, d_attn_ref, d_mid_ref, mixed_own_ref, mixed_other_ref, sums_ref,
):
    step = pl.program_id(0)
    chip, core = at_ref[0], at_ref[1]
    hidden_width = d_gate_up_ref.shape[1] // 2
    own, other = own_ref[0], other_ref[0]
    d_ffn = jnp.concatenate([halves(core, own, other), halves(core, other, own)], 0)
    d_ffn_ref[...] = d_ffn
    d_hidden = dot(d_ffn, ffn_ref[:, 2 * hidden_width :], (1, 0))
    gate = gate_up_ref[:, :hidden_width].astype(F32)
    up = gate_up_ref[:, hidden_width:].astype(F32)
    sigma = jax.nn.sigmoid(gate)
    silu = gate * sigma
    d_gate = d_hidden * up * (sigma + silu * (1.0 - sigma))
    d_gate_up = jnp.concatenate([d_gate.astype(BF16), (d_hidden * silu).astype(BF16)], 1)
    d_gate_up_ref[...] = d_gate_up
    d_second = dot(d_gate_up, ffn_ref[:, : 2 * hidden_width], (1, 1))

    x = dot(patch_ref[...], embed_ref[...], (0, 0))
    attn = attn_ref[...].astype(F32)
    attn_scale = row_rms(attn)
    attn_normed = attn * attn_scale
    mid = x + vec_ref[1:2] * attn_normed
    mid_scale = row_rms(mid)
    mid_sum = jnp.sum(mid * mid_scale * d_second, axis=0, keepdims=True)
    d_last = dot(cot_ref[...], unpatch_ref[...], (0, 0))
    place = lax.broadcasted_iota(jnp.int32, (PAIR, 1), 0) // BLOCK
    mine = (place == core) & (step == chip)
    d_mid = row_rms_back(mid, mid_scale, vec_ref[2:3] * d_second) + jnp.where(mine, d_last, 0.0)
    d_mid_ref[...] = d_mid.astype(BF16)
    attn_sum = jnp.sum(attn_normed * d_mid, axis=0, keepdims=True)
    d_attn = row_rms_back(attn, attn_scale, vec_ref[1:2] * d_mid).astype(BF16)
    d_attn_ref[...] = d_attn
    for weight_ref, part_ref in ((out_near_ref, mixed_own_ref), (out_far_ref, mixed_other_ref)):
        part_ref[...] = dot(joined(weight_ref), d_attn, (1, 1)).astype(BF16).reshape(part_ref.shape)

    @pl.when(step == 0)
    def _():
        sums_ref[...] = jnp.zeros_like(sums_ref)

    sums_ref[0:1] += mid_sum
    sums_ref[1:2] += attn_sum


def backward(at, d_ffn, ffn, out_whole, gate_up, attn, patches, embed, cot_taps, unpatch, vec):
    width = embed.shape[1]
    part = out_whole[0].shape[1]
    hidden_width = ffn.shape[1] // 3
    by_chip = pl.BlockSpec((1, BLOCK, width), lambda t, at: ((t - at[0] + 4) % 4, 0, 0))
    parts = pl.BlockSpec((4, part, PAIR), lambda t, at: (0, 0, t))
    return pl.pallas_call(
        backward_kernel,
        grid_spec=pltpu.PrefetchScalarGridSpec(
            num_scalar_prefetch=1,
            grid=(4,),
            in_specs=[
                by_chip,
                by_chip,
                held(),
                held(),
                held(),
                row_block(PAIR, 2 * hidden_width),
                row_block(PAIR, width),
                lane_block(144, PAIR),
                whole(embed.shape),
                lane_block(144, PAIR),
                whole(unpatch.shape),
                whole(vec.shape),
            ],
            out_specs=[
                row_block(PAIR, width),
                row_block(PAIR, 2 * hidden_width),
                row_block(PAIR, width),
                row_block(PAIR, width),
                parts,
                parts,
                pl.BlockSpec((8, width), lambda t, at: (0, 0)),
            ],
        ),
        out_shape=[
            jax.ShapeDtypeStruct((TOKENS, width), BF16),
            jax.ShapeDtypeStruct((TOKENS, 2 * hidden_width), BF16),
            jax.ShapeDtypeStruct((TOKENS, width), BF16),
            jax.ShapeDtypeStruct((TOKENS, width), BF16),
            jax.ShapeDtypeStruct((4, part, TOKENS), BF16),
            jax.ShapeDtypeStruct((4, part, TOKENS), BF16),
            jax.ShapeDtypeStruct((8, width), F32),
        ],
        compiler_params=params(32),
        cost_estimate=LIGHT,
        name="backward",
    )(at, *d_ffn, ffn, *out_whole, gate_up, attn, patches, embed, cot_taps, unpatch, vec)


def weight_kernel(
    second_ref, d_gate_up_ref, d_ffn_ref, hidden_ref, near_ref, far_ref, d_attn_ref,
    grads_ref, out_near_ref, out_far_ref,
):
    step = pl.program_id(0)
    chunk, _, lanes = grads_ref.shape[0] // 4, *grads_ref.shape[1:]
    part = second_ref.shape[1] // chunk
    rows = jnp.concatenate(
        [
            dot(second_ref[...], d_gate_up_ref[...], (0, 0)).astype(BF16),
            dot(d_ffn_ref[...], hidden_ref[...], (0, 0)).astype(BF16),
        ],
        1,
    )
    groups = rows.shape[1] // lanes
    first = grads_ref.shape[1] - groups * part
    for c in range(chunk):
        for g in range(groups):
            grads_ref[step * chunk + c, first + g * part : first + (g + 1) * part] = rows[
                c * part : (c + 1) * part, g * lanes : (g + 1) * lanes
            ]
    out_near_ref[0] = dot(near_ref[0], d_attn_ref[...], (1, 0)).astype(BF16)
    out_far_ref[0] = dot(far_ref[0], d_attn_ref[...], (1, 0)).astype(BF16)


def weight_grads(second, d_gate_up, d_ffn, hidden, mixed, d_attn, text_rows):
    width = second.shape[1]
    heads_width = mixed[0].shape[1]
    lanes = 2 * heads_width
    grads = (COLS, text_rows + width // COLS * 3 * hidden.shape[1] // lanes, lanes)
    pieces = pl.BlockSpec((1, heads_width, TOKENS), lambda t: (t, 0, 0))
    out_piece = pl.BlockSpec((1, heads_width, width), lambda t: (t, 0, 0))
    out_shape = jax.ShapeDtypeStruct((4, heads_width, width), BF16)
    return pl.pallas_call(
        weight_kernel,
        grid=(4,),
        in_specs=[
            lane_block(TOKENS, width // 4),
            whole(d_gate_up.shape),
            lane_block(TOKENS, width // 4),
            whole(hidden.shape),
            pieces,
            pieces,
            whole(d_attn.shape),
        ],
        out_specs=[pl.BlockSpec(grads, lambda t: (0, 0, 0)), out_piece, out_piece],
        out_shape=[jax.ShapeDtypeStruct(grads, BF16), out_shape, out_shape],
        compiler_params=params(40),
        cost_estimate=LIGHT,
        name="weight_grads",
    )(second, d_gate_up, d_ffn, hidden, *mixed, d_attn)


def first_kernel(
    at_ref, gate_ref, patch_ref, embed_ref, vec_ref, weight_ref, d_raw_ref, d_mid_ref, place_ref, out_sum_ref,
    unpatch_sum_ref, back_sums_ref, own_sums_ref, head_ref, text_head_ref, gains_ref, mod_ref, activation_ref,
    own_pack_ref, other_pack_ref, p0_ref, p1_ref, p2_ref, p3_ref,
    taps_acc, embed_acc, first_acc, shared_acc, qkv_acc, turned_acc,
):
    step = pl.program_id(0)
    last = pl.num_programs(0) - 1
    x = dot(patch_ref[...], embed_ref[...], (0, 0))
    scale = row_rms(x)
    x_normed = x * scale
    h = (x_normed * vec_ref[0:1]).astype(BF16)
    d_h = dot(d_raw_ref[0], weight_ref[0], (0, 1))
    for s in (1, 2):
        d_h = d_h + dot(d_raw_ref[s], weight_ref[s], (0, 1))

    @pl.when(step == 0)
    def _():
        qkv_acc[...] = jnp.zeros_like(qkv_acc)
        embed_acc[...] = jnp.zeros_like(embed_acc)
        first_acc[...] = jnp.zeros_like(first_acc)

    qkv_acc[...] += dot(joined(d_raw_ref), h, (1, 0)).reshape(qkv_acc.shape)
    first_acc[0:1] += jnp.sum(x_normed * d_h, axis=0, keepdims=True)
    d_first = (d_mid_ref[...].astype(F32) + row_rms_back(x, scale, vec_ref[0:1] * d_h)).astype(BF16)
    embed_acc[...] += dot(patch_ref[...], d_first, (1, 0))
    here = pl.ds(pl.multiple_of(step * PAIR, PAIR), PAIR)
    taps_acc[:, here] = dot(embed_ref[...], d_first, (1, 1))

    @pl.when(step == last)
    def _():
        part = p0_ref.shape[1] // 2
        for s in range(4):
            turned_acc[s] = (qkv_acc[s] if s < 3 else out_sum_ref[...]).T.astype(BF16)
        for dz, ref in enumerate((p0_ref, p1_ref, p2_ref, p3_ref)):
            z = lax.rem(at_ref[3] + dz, 4)
            for y in range(4):
                dy = lax.rem(y - at_ref[2] + 4, 4)
                first = pl.multiple_of((y * 4 + z) * part, part)
                pieces = [turned_acc[s, pl.ds(first, part), :] for s in range(4)]
                for k in range(2):
                    ref[dy, k * part : (k + 1) * part] = jnp.concatenate(
                        pieces[2 * k : 2 * k + 2], 1
                    )
        terms = jnp.concatenate(
            [first_acc[0:1], back_sums_ref[1:2], back_sums_ref[0:1], own_sums_ref[0:1]], 0
        )
        gates = [jnp.tanh(mod_ref[k : k + 1]) for k in (1, 3)]
        into = jnp.concatenate(
            [1.0 + mod_ref[0:1], gates[0], 1.0 + mod_ref[2:3], gates[1]], 0
        )
        d_gains = terms * into
        slope = jnp.concatenate(
            [jnp.ones_like(gates[0]), 1.0 - gates[0] * gates[0]] * 1
            + [jnp.ones_like(gates[0]), 1.0 - gates[1] * gates[1]],
            0,
        )
        d_modulation = terms * gains_ref[0:4] * slope
        heads = head_ref.shape[0]
        width = d_gains.shape[1]
        rows = [head_ref[h] for h in range(heads)], [text_head_ref[h] for h in range(heads)]
        own = jnp.concatenate(
            [
                jnp.concatenate([r[0:2] for r in rows[0]], 1),
                jnp.concatenate([r[0:1] for r in rows[1]], 1),
                jnp.zeros((5, heads * HD), F32),
            ],
            0,
        )
        own = jnp.concatenate([own, jnp.zeros((8, width - heads * HD), F32)], 1)
        row_at = 2 * at_ref[0] + at_ref[1]
        own = pltpu.roll(own, row_at * (heads * HD), 1)
        lane = lax.broadcasted_iota(jnp.int32, (1, width), 1)
        gate_row = jnp.zeros((1, width), F32)
        for h in range(heads):
            total = jnp.sum(rows[1][h][1:2], axis=1, keepdims=True)
            total = total * (1.0 - gate_ref[h] * gate_ref[h])
            gate_row = gate_row + jnp.where(lane == row_at * heads + h, total, 0.0)
        small = jnp.concatenate(
            [d_gains, own[0:3], gate_row, jnp.zeros((24, width), F32)], 0
        )
        for tile in range(12):
            lanes = slice(tile * 128, (tile + 1) * 128)
            first = tile * SHARED
            shared_acc[first : first + 144] = embed_acc[:, lanes].astype(BF16)
            shared_acc[first + 144 : first + 288] = unpatch_sum_ref[:, lanes].astype(BF16)
            shared_acc[first + 288 : first + SHARED] = small[:, lanes].astype(BF16)
        shared_acc[12 * SHARED :] = jnp.zeros((8 * CHUNK - 12 * SHARED, 128), BF16)
        latent = field_of(taps_acc[...], place_ref[...], -1)
        rows = [
            d_modulation[q : q + 1, tile * 128 : (tile + 1) * 128]
            for q in range(4)
            for tile in range(12)
        ]
        for r in range(ROWS):
            ahead = lax.rem(r // 2 - at_ref[0] + 4, 4)
            mods = jnp.concatenate(rows[6 * r : 6 * r + 6] + [jnp.zeros((10, 128), F32)], 0)
            piece = jnp.concatenate(
                [
                    shared_acc[r * CHUNK : (r + 1) * CHUNK],
                    activation_ref[r].astype(BF16),
                    latent[r].astype(BF16),
                    mods.astype(BF16),
                ],
                0,
            )

            @pl.when(at_ref[1] == r % 2)
            def _():
                own_pack_ref[ahead] = piece

            @pl.when(at_ref[1] != r % 2)
            def _():
                other_pack_ref[ahead] = piece


def first_back(
    at, gates, patches, embed, vec, weight, d_raw, d_mid, place, out_sum, unpatch_sum, back_sums, own_sums,
    head, text_head, gains, modulation, activation,
):
    width = embed.shape[1]
    part = weight.shape[2]
    pack = (4, CHUNK + 48, 128)
    grads = (4, 2 * width // COLS, 2 * part)
    rest = (place, out_sum, unpatch_sum, back_sums, own_sums, head, text_head, gains, modulation, activation)
    return pl.pallas_call(
        first_kernel,
        grid_spec=pltpu.PrefetchScalarGridSpec(
            num_scalar_prefetch=2,
            grid=(TOKENS // PAIR,),
            in_specs=[
                lane_block(144, PAIR),
                whole(embed.shape),
                whole(vec.shape),
                held(),
                pl.BlockSpec((3, part, PAIR), lambda t, *_: (0, 0, t)),
                row_block(PAIR, width),
            ]
            + [held()]
            + [whole(value.shape) for value in rest[1:]],
            out_specs=[pl.BlockSpec(pack, lambda t, *_: (0, 0, 0))] * 2
            + [pl.BlockSpec(grads, lambda t, *_: (0, 0, 0))] * 4,
            scratch_shapes=[
                pltpu.VMEM((144, TOKENS), F32),
                pltpu.VMEM((144, width), F32),
                pltpu.VMEM((8, width), F32),
                pltpu.VMEM((8 * CHUNK, 128), BF16),
                pltpu.VMEM((3, part, width), F32),
                pltpu.VMEM((4, width, part), BF16),
            ],
        ),
        out_shape=[jax.ShapeDtypeStruct(pack, BF16)] * 2 + [jax.ShapeDtypeStruct(grads, BF16)] * 4,
        compiler_params=params(58),
        cost_estimate=LIGHT,
        name="first_back",
    )(at, gates, patches, embed, vec, weight, d_raw, d_mid, *rest)


def local(
    latent, condition, caption, cap_len, cotangent, embed_weight, modulate_weight, norm_gains,
    cross_gate, qkv_weight, text_kv_weight, out_weight, gate_up_weight, down_weight, unpatch_weight,
):
    images, _, _, channels = latent.shape
    width = embed_weight.shape[3]
    local_width = qkv_weight.shape[2]
    heads = local_width // HD
    hidden_width = down_weight.shape[0]
    taps = 9 * channels
    row_at = lax.axis_index("row")
    col_at = lax.axis_index("col")
    at = jnp.stack([row_at // 2, row_at % 2, col_at // 4, col_at % 4]).astype(jnp.int32)
    tile = latent.shape[1] * latent.shape[2] * channels

    cond_low = jax.nn.silu(condition.astype(F32)).astype(BF16)
    mod_piece = jnp.dot(cond_low, modulate_weight, preferred_element_type=F32)
    mod_columns = mod_piece.shape[1]
    mod_high = mod_piece.astype(BF16)
    mod_low = (mod_piece - mod_high.astype(F32)).astype(BF16)

    packed = jnp.concatenate(
        [latent.reshape(images, tile), cotangent.reshape(images, tile), mod_high, mod_low], axis=1
    )
    packed = jnp.pad(packed, ((0, 0), (0, 2 * local_width - packed.shape[1])))

    head_piece = jnp.concatenate(
        [
            jnp.concatenate([qkv_weight[0], qkv_weight[1]], axis=1),
            jnp.concatenate([qkv_weight[2], out_weight.T], axis=1),
        ]
    )
    text_piece = jnp.concatenate([text_kv_weight[0], text_kv_weight[1]], axis=1)
    head_pieces = from_col(head_piece, along_y)
    text_pieces = from_col(text_piece, along_z)
    packed = lax.all_to_all(packed, "col", 0, 0, tiled=True)
    packed, *reached = lax.optimization_barrier((packed, *head_pieces, *text_pieces))
    head_pieces, text_pieces = reached[:4], reached[4:]
    packed = send_all(packed, "row")
    patches, cot_taps = image_taps(packed)
    head_pieces = from_col(jnp.stack(head_pieces), along_z)
    text_own = jnp.stack(text_pieces)
    text_beside = [lax.ppermute(text_own, "col", col_pairs(d, 0)) for d in (1, 3)]
    ffn_piece = jnp.concatenate([gate_up_weight[0], gate_up_weight[1], down_weight.T], axis=1)
    ffn_piece, patches, text_own, next_text, last_text, *head_pieces = lax.optimization_barrier(
        (ffn_piece, patches, text_own, *text_beside, *head_pieces)
    )
    ffn_whole = lax.all_gather(ffn_piece, "col", axis=0, tiled=True)
    text_apart = lax.ppermute(text_own, "col", col_pairs(2, 0))
    text_pieces = [text_own, next_text, text_apart, last_text]
    qkv_whole, out_rows = unpack_head(at, head_pieces)
    out_pieces = from_chips(out_rows)

    mod_at = 2 * tile
    modulation = packed[:, :, mod_at : mod_at + mod_columns].astype(F32)
    modulation = modulation + packed[:, :, mod_at + mod_columns : mod_at + 2 * mod_columns].astype(F32)
    modulation = modulation.reshape(4, width)
    attn_gate = jnp.tanh(modulation[1])
    ffn_gate = jnp.tanh(modulation[3])
    vec = jnp.stack(
        [
            norm_gains[0] * (1.0 + modulation[0]),
            norm_gains[1] * attn_gate,
            norm_gains[2] * (1.0 + modulation[2]),
            norm_gains[3] * ffn_gate,
        ]
    )
    vec = jnp.pad(vec, ((0, 4), (0, 0)))
    embed = embed_weight.reshape(taps, width)
    unpatch = unpatch_weight.transpose(0, 1, 3, 2).reshape(taps, width)
    raw = qkv_project(patches, embed, vec, qkv_whole)
    raw = raw.reshape(3, heads, HD, TOKENS)
    caption_rows = caption[0]
    text_raw = text_project(at, text_pieces, caption_rows)
    text_raw = text_raw.reshape(2, heads, HD, caption_rows.shape[0])
    head_gains = lax.dynamic_slice(norm_gains, (4, row_at * local_width), (3, local_width)).reshape(
        3, heads, HD, 1
    )
    head_gates = jnp.tanh(lax.dynamic_slice_in_dim(cross_gate, row_at * heads, heads))
    cap = lax.dynamic_slice_in_dim(cap_len, col_at, 1)
    table = jnp.asarray(rope_tables())
    mixed, lse = attend(raw, text_raw, head_gains, table, cap, head_gates)

    mixed_pieces = from_chips(mixed)
    reached = lax.optimization_barrier((*mixed_pieces, *out_pieces))
    mixed_whole = with_other_core(reached[:4])
    out_whole = with_other_core(reached[4:])
    attn, second, gate_up, hidden, ffn_own, ffn_other = forward(
        at, mixed_whole, out_whole, patches, embed, vec, ffn_whole
    )
    place = tile_places(False)
    cot_own = lax.dynamic_slice_in_dim(cot_taps, row_at * BLOCK, BLOCK, 1)
    d_ffn_own, ffn_out = own_grad(
        to_chips(sum_cores(ffn_own, ffn_other)), cot_own, unpatch, vec
    )
    d_ffn_near = from_chips(d_ffn_own)
    activation_field, unpatch_sum, own_sums = own_block(
        at, ffn_out, attn, patches, cot_taps, embed, unpatch, vec, place
    )
    d_ffn_near = lax.optimization_barrier((*d_ffn_near, activation_field))[:4]
    d_ffn, d_gate_up, d_attn, d_mid, mixed_own, mixed_other, back_sums = backward(
        at, with_other_core(d_ffn_near), ffn_whole, out_whole, gate_up, attn, patches, embed, cot_taps,
        unpatch, vec,
    )
    mixed_near = sum_cores(mixed_own, mixed_other)
    mixed_terms = to_chips(mixed_near)
    text_rows = text_kv_weight.shape[1]
    grads, out_near, out_far = weight_grads(
        after(second, *mixed_near), d_gate_up, d_ffn, hidden, mixed_whole, d_attn, text_rows
    )
    *mixed_terms, grads, out_near, out_far = lax.optimization_barrier(
        (*mixed_terms, grads, out_near, out_far)
    )
    d_mixed = sum(term.astype(F32) for term in mixed_terms).astype(BF16)
    d_mixed = d_mixed.reshape(heads, HD, TOKENS)
    out_near = sum_cores(out_near, out_far)
    out_apart = lax.ppermute(out_near[2], "row", row_pairs_to(2, 0))

    grads, dq_text, d_text_head = text_back(
        raw, text_raw, head_gains, table, lse, d_mixed, cap, head_gates, caption_rows,
        after(grads, *out_near),
    )
    dq_text, grads, out_apart, *out_near = lax.optimization_barrier(
        (dq_text, grads, out_apart, *out_near)
    )
    d_raw, d_head = attend_back(raw, head_gains, table, lse, d_mixed, dq_text)
    out_beside = [lax.ppermute(out_near[d], "row", row_pairs_to(d, 0)) for d in (1, 3)]
    d_raw, *out_terms = lax.optimization_barrier((d_raw, out_near[0], out_apart, *out_beside))
    out_sum = sum(term.astype(F32) for term in out_terms)
    d_raw = d_raw.reshape(3, local_width, TOKENS)
    own_pack, other_pack, *head_parts = first_back(
        at, head_gates, patches, embed, vec, qkv_whole, d_raw, d_mid, place, out_sum, unpatch_sum,
        back_sums, own_sums, d_head, d_text_head, norm_gains, modulation, activation_field,
    )
    beside = [lax.ppermute(head_parts[d], "col", col_pairs_to(0, d)) for d in (1, 3)]

    row_terms = to_chips(sum_cores(own_pack, other_pack))
    row_pack = sum(term.astype(F32) for term in row_terms)
    fields = row_pack[CHUNK : CHUNK + 2 * channels].T.reshape(COLS, 8, 2 * channels)
    mod_sums = row_pack[CHUNK + 2 * channels : CHUNK + 2 * channels + 6].reshape(COLS, 8, 6)
    fields = jnp.concatenate([fields, mod_sums], axis=2).astype(BF16)
    fields = jnp.pad(fields, ((0, 0), (0, 0), (0, 128 - fields.shape[2])))
    shared = row_pack[:CHUNK].astype(BF16).reshape(COLS, CHUNK // COLS, 128)
    col_pack = lax.all_to_all(jnp.concatenate([shared, fields], axis=1), "col", 0, 0)
    col_pack, left, right = lax.optimization_barrier((col_pack, *beside))
    shared = jnp.sum(col_pack[:, : CHUNK // COLS].astype(F32), axis=0)
    shared, apart = lax.optimization_barrier(
        (send_all(shared.astype(BF16), "col"), head_parts[2])
    )
    shared = send_all(shared, "row").reshape(-1, 128)
    apart = lax.ppermute(apart, "col", col_pairs_to(0, 2))
    head_near = sum(term.astype(F32) for term in (head_parts[0], left, apart, right)).astype(BF16)
    shared = shared[: 12 * SHARED].reshape(12, SHARED, 128).astype(F32)
    fields = col_pack[:, CHUNK // COLS :]
    activation = fields[:, :, :channels].reshape(latent.shape)
    latent_grad = fields[:, :, channels : 2 * channels].reshape(latent.shape)
    modulate_grad = lax.dot_general(
        cond_low.astype(F32),
        fields[:, :, 2 * channels : 2 * channels + 6].reshape(images, mod_columns).astype(F32),
        (((0,), (0,)), ((), ())),
        precision=lax.Precision.HIGHEST,
        preferred_element_type=F32,
    )
    embed_grad = shared[:, :taps].transpose(1, 0, 2).reshape(embed_weight.shape)
    unpatch_grad = shared[:, taps : 2 * taps].reshape(12, 3, 3, channels, 128)
    unpatch_grad = unpatch_grad.transpose(1, 2, 0, 4, 3).reshape(unpatch_weight.shape)
    gains_grad = shared[:, 2 * taps : 2 * taps + 7].transpose(1, 0, 2).reshape(7, width)
    gate_grad = shared[0, 2 * taps + 7, :HEADS]

    part = width // COLS
    grads = lax.psum_scatter(
        grads.reshape(-1, 2 * local_width), "col", scatter_dimension=0, tiled=True
    ).astype(F32)
    text_kv_grad = jnp.stack([grads[:text_rows, :local_width], grads[:text_rows, local_width:]])
    ffn_total = jnp.concatenate(
        [grads[first : first + part] for first in range(text_rows, grads.shape[0], part)], axis=1
    )
    gate_up_grad = jnp.stack(
        [ffn_total[:, :hidden_width], ffn_total[:, hidden_width : 2 * hidden_width]]
    )
    down_grad = ffn_total[:, 2 * hidden_width :].T
    head_total = sum(term.astype(F32) for term in along_col(head_near, along_y))
    first, second_half = head_total[:, :local_width], head_total[:, local_width:]
    qkv_grad = jnp.stack([first[:part], second_half[:part], first[part:]])
    out_grad = second_half[part:].T
    return (
        activation, latent_grad, embed_grad, modulate_grad, gains_grad, gate_grad,
        qkv_grad, text_kv_grad, out_grad, gate_up_grad, down_grad, unpatch_grad,
    )


def solution(mesh):
    placed = (
        P(None, "row", "col", None),
        P(),
        P("col", None, None),
        P(),
        P(None, "row", "col", None),
        P(),
        P(None, ("row", "col")),
        P(),
        P(),
        P(None, "col", "row"),
        P(None, "col", "row"),
        P("row", "col"),
        P(None, "col", "row"),
        P("row", "col"),
        P(),
    )
    return jax.shard_map(
        local,
        mesh=mesh,
        in_specs=placed,
        out_specs=(
            P(None, "row", "col", None),
            P(None, "row", "col", None),
            P(),
            P(None, ("row", "col")),
            P(),
            P(),
            P(None, "col", "row"),
            P(None, "col", "row"),
            P("row", "col"),
            P(None, "col", "row"),
            P("row", "col"),
            P(),
        ),
        check_vma=False,
    )
```

```python
import math
from functools import partial

import jax
import jax.numpy as jnp
import numpy as np
from jax import lax
from jax.experimental import pallas as pl
from jax.experimental.pallas import tpu as pltpu
from jax.sharding import PartitionSpec as P

HEADS = 24
HD = 64
GRID = 32
TOKENS = GRID * GRID
EPSILON = 1e-06
ROPE_BASE = 10000.0
MASKED = -1e30
F32 = jnp.float32
BF16 = jnp.bfloat16
ROWS = 8
COLS = 16
QUERY_BLOCK = 256
BLOCK = TOKENS // ROWS
PAIR = 2 * BLOCK
MIB = 2**20
SHARED = 320
CHUNK = 512
LIGHT = pl.CostEstimate(flops=1, bytes_accessed=1, transcendentals=0)


def dot(left, right, contract):
    return lax.dot_general(
        left, right, ((contract[:1], contract[1:]), ((), ())), preferred_element_type=F32
    )


def row_pairs(dx, dc):
    return [
        (((x + dx) % 4) * 2 + (c + dc) % 2, x * 2 + c) for x in range(4) for c in range(2)
    ]


def row_pairs_to(dx, dc):
    return [(dst, src) for src, dst in row_pairs(dx, dc)]


def from_chips(piece):
    return [piece] + [lax.ppermute(piece, "row", row_pairs(d, 0)) for d in (1, 2, 3)]


def with_other_core(pieces):
    quad = jnp.stack(pieces)
    return quad, lax.ppermute(quad, "row", row_pairs(0, 1))


def gather_near(piece):
    return with_other_core(from_chips(piece))


def sum_cores(own, other):
    other = lax.ppermute(other, "row", row_pairs(0, 1))
    return [(own[d].astype(F32) + other[d].astype(F32)).astype(BF16) for d in range(4)]


def to_chips(near):
    return [near[0]] + [lax.ppermute(near[d], "row", row_pairs_to(d, 0)) for d in (1, 2, 3)]


def col_pairs_to(dy, dz):
    return [(y * 4 + z, (y + dy) % 4 * 4 + (z + dz) % 4) for y in range(4) for z in range(4)]


def col_pairs(dy, dz):
    return [(dst, src) for src, dst in col_pairs_to(dy, dz)]


def from_col(piece, step):
    return [piece] + [lax.ppermute(piece, "col", col_pairs(*step(d))) for d in (1, 2, 3)]


def along_y(d):
    return (d, 0)


def along_z(d):
    return (0, d)


def along_col(parts, step):
    return [parts[0]] + [lax.ppermute(parts[d], "col", col_pairs_to(*step(d))) for d in (1, 2, 3)]


def send_all(piece, axis):
    copies = jnp.broadcast_to(piece, (lax.axis_size(axis),) + piece.shape)
    return lax.all_to_all(copies, axis, 0, 0)


def after(value, *others):
    return lax.optimization_barrier((value,) + others)[0]


def rope_tables():
    quarter = HD // 4
    frequency = np.float32(ROPE_BASE) ** (-np.arange(quarter, dtype=np.float32) / np.float32(quarter))
    place = np.arange(TOKENS)
    row = frequency[:, None] * (place // GRID).astype(np.float32)[None, :]
    col = frequency[:, None] * (place % GRID).astype(np.float32)[None, :]
    return np.stack([np.cos(row), np.sin(row), np.cos(col), np.sin(col)]).astype(np.float32)


def turn(v, table, sign):
    a, b, c, d = (v[k * 16 : (k + 1) * 16] for k in range(4))
    cr, sr, cc, sc = table[0], table[1] * sign, table[2], table[3] * sign
    return jnp.concatenate([a * cr - b * sr, a * sr + b * cr, c * cc - d * sc, c * sc + d * cc], 0)


def column_rms(v):
    return lax.rsqrt(jnp.mean(v * v, axis=0, keepdims=True) + EPSILON)


def normed(v, gain):
    return v * column_rms(v) * gain


def column_rms_back(v, u):
    scale = column_rms(v)
    return (u - v * (jnp.mean(u * v, axis=0, keepdims=True) * scale * scale)) * scale


def whole(shape):
    zeros = (0,) * len(shape)
    return pl.BlockSpec(shape, lambda *_: zeros, pipeline_mode=pl.Buffered(1))


def held():
    return pl.BlockSpec(memory_space=pltpu.VMEM)


def lane_block(rows, lanes):
    return pl.BlockSpec((rows, lanes), lambda t, *_: (0, t))


def row_block(rows, lanes):
    return pl.BlockSpec((rows, lanes), lambda t, *_: (t, 0))


def params(mib):
    return pltpu.CompilerParams(vmem_limit_bytes=mib * MIB, dimension_semantics=("arbitrary",))


def row_of_sums(v):
    return jnp.sum(v.T, axis=0, keepdims=True)


def attend_kernel(
    cap_ref, gate_ref, raw_ref, text_ref, gain_ref, table_ref, mixed_ref, lse_ref,
    q_ref, k_ref, v_ref, tk_ref, tv_ref,
):
    step = pl.program_id(0)
    heads = raw_ref.shape[1]

    @pl.when(step == 0)
    def _():
        table = table_ref[...]
        for h in range(heads):
            q = turn(normed(raw_ref[0, h], gain_ref[0, h]), table, 1.0).astype(BF16)
            q_ref[h] = q * jnp.asarray(0.125, BF16)
            k_ref[h] = turn(normed(raw_ref[1, h], gain_ref[1, h]), table, 1.0).T.astype(BF16)
            v_ref[h] = raw_ref[2, h].astype(BF16)
            tk_ref[h] = normed(text_ref[0, h], gain_ref[2, h]).T.astype(BF16)
            tv_ref[h] = text_ref[1, h].astype(BF16)

    slots = tk_ref.shape[1]
    mask = lax.broadcasted_iota(jnp.int32, (slots, QUERY_BLOCK), 0) < cap_ref[0]
    here = pl.ds(pl.multiple_of(step * QUERY_BLOCK, QUERY_BLOCK), QUERY_BLOCK)
    outs = []
    for h in range(heads):
        qb = q_ref[h, :, here]
        e = jnp.exp(dot(k_ref[h], qb, (1, 0)))
        total = jnp.sum(e, axis=0, keepdims=True)
        own = dot(v_ref[h], e.astype(BF16), (1, 0)) / total
        te = jnp.exp(jnp.where(mask, dot(tk_ref[h], qb, (1, 0)), MASKED))
        text_total = jnp.sum(te, axis=0, keepdims=True)
        text = dot(tv_ref[h], te.astype(BF16), (1, 0)) / text_total
        outs.append(own + gate_ref[h] * text)
        lse_ref[h, 0:1] = jnp.log(total)
        lse_ref[h, 1:2] = jnp.log(text_total)
    mixed_ref[...] = jnp.concatenate(outs, 0).astype(BF16)


def attend(raw, text_raw, gains, table, cap, gates):
    heads = raw.shape[1]
    slots = text_raw.shape[3]
    return pl.pallas_call(
        attend_kernel,
        grid_spec=pltpu.PrefetchScalarGridSpec(
            num_scalar_prefetch=2,
            grid=(TOKENS // QUERY_BLOCK,),
            in_specs=[
                whole((3, heads, HD, TOKENS)),
                whole((2, heads, HD, slots)),
                whole((3, heads, HD, 1)),
                whole((4, 16, TOKENS)),
            ],
            out_specs=[
                lane_block(heads * HD, QUERY_BLOCK),
                pl.BlockSpec((heads, 8, QUERY_BLOCK), lambda t, *_: (0, 0, t)),
            ],
            scratch_shapes=[
                pltpu.VMEM((heads, HD, TOKENS), BF16),
                pltpu.VMEM((heads, TOKENS, HD), BF16),
                pltpu.VMEM((heads, HD, TOKENS), BF16),
                pltpu.VMEM((heads, slots, HD), BF16),
                pltpu.VMEM((heads, HD, slots), BF16),
            ],
        ),
        out_shape=[
            jax.ShapeDtypeStruct((heads * HD, TOKENS), BF16),
            jax.ShapeDtypeStruct((heads, 8, TOKENS), F32),
        ],
        compiler_params=params(20),
        cost_estimate=LIGHT,
        name="attend",
    )(cap, gates, raw, text_raw, gains, table)


def text_back_kernel(
    cap_ref, gate_ref, q_raw_ref, text_ref, gain_ref, table_ref, lse_ref, grad_ref, caption_ref, held_ref,
    grads_ref, dq_ref, d_gain_ref, low_ref,
):
    del held_ref
    step = pl.program_id(0)
    heads, _, slots = low_ref.shape[1:]

    @pl.when(step == 0)
    def _():
        table = table_ref[...]
        mask = lax.broadcasted_iota(jnp.int32, (slots, TOKENS), 0) < cap_ref[0]
        for h in range(heads):
            gate = gate_ref[h]
            q = turn(normed(q_raw_ref[h], gain_ref[0, h]), table, 1.0).astype(BF16)
            q = q * jnp.asarray(0.125, BF16)
            tk = normed(text_ref[0, h], gain_ref[2, h]).astype(BF16)
            tv = text_ref[1, h].astype(BF16)
            g = grad_ref[h]
            tp = jnp.exp(jnp.where(mask, dot(tk, q, (0, 0)), MASKED) - lse_ref[h, 1:2])
            tpb = tp.astype(BF16)
            low_ref[1, h] = (dot(g, tpb, (1, 1)) * gate).astype(BF16)
            gate_terms = g.astype(F32) * dot(tv, tpb, (1, 0))
            tpd = tp * dot(tv, g, (0, 0)) * gate
            dts = (tpd - tp * jnp.sum(tpd, axis=0, keepdims=True)).astype(BF16)
            dq_ref[h] = dot(tk, dts, (1, 0))
            d_tk = dot(q, dts, (1, 1))
            values = text_ref[0, h]
            low_ref[0, h] = column_rms_back(values, d_tk * gain_ref[2, h]).astype(BF16)
            d_gain_ref[h, 0:1] = row_of_sums(values * column_rms(values) * d_tk)
            d_gain_ref[h, 1:2] = row_of_sums(gate_terms)

    d_text = low_ref[...].reshape(2 * heads * HD, slots)
    rows = grads_ref.shape[1]
    for k in range(grads_ref.shape[0]):
        grads_ref[k] = dot(caption_ref[:, k * rows : (k + 1) * rows], d_text, (0, 1)).astype(BF16)


def text_back(raw, text_raw, gains, table, lse, grads, cap, gates, caption, held):
    heads = raw.shape[1]
    slots = text_raw.shape[3]
    rows = caption.shape[1] // COLS
    lanes = 2 * heads * HD
    return pl.pallas_call(
        text_back_kernel,
        grid_spec=pltpu.PrefetchScalarGridSpec(
            num_scalar_prefetch=2,
            grid=(4,),
            in_specs=[
                pl.BlockSpec((None, heads, HD, TOKENS), lambda t, *_: (0, 0, 0, 0)),
                whole(text_raw.shape),
                whole(gains.shape),
                whole(table.shape),
                whole(lse.shape),
                whole(grads.shape),
                pl.BlockSpec((slots, 4 * rows), lambda t, *_: (0, t)),
                pl.BlockSpec(memory_space=pl.ANY),
            ],
            out_specs=[
                pl.BlockSpec((4, rows, lanes), lambda t, *_: (t, 0, 0)),
                pl.BlockSpec((heads, HD, TOKENS), lambda t, *_: (0, 0, 0)),
                pl.BlockSpec((heads, 8, HD), lambda t, *_: (0, 0, 0)),
            ],
            scratch_shapes=[pltpu.VMEM((2, heads, HD, slots), BF16)],
        ),
        out_shape=[
            jax.ShapeDtypeStruct(held.shape, BF16),
            jax.ShapeDtypeStruct((heads, HD, TOKENS), F32),
            jax.ShapeDtypeStruct((heads, 8, HD), F32),
        ],
        input_output_aliases={9: 0},
        compiler_params=params(58),
        cost_estimate=LIGHT,
        name="text_back",
    )(cap, gates, raw, text_raw, gains, table, lse, grads, caption, held)


def attend_back_kernel(
    raw_ref, gain_ref, table_ref, lse_ref, grad_ref, dq_text_ref,
    d_raw_ref, d_gain_ref, dv_ref, dk_ref, dq_ref,
):
    table = table_ref[...]
    q = turn(normed(raw_ref[0], gain_ref[0]), table, 1.0).astype(BF16) * jnp.asarray(0.125, BF16)
    k = turn(normed(raw_ref[1], gain_ref[1]), table, 1.0)
    k, k_turned = k.astype(BF16), k.T.astype(BF16)
    v_turned = raw_ref[2].T.astype(BF16)
    for first in range(0, TOKENS, QUERY_BLOCK):
        here = slice(first, first + QUERY_BLOCK)
        qb = q[:, here]
        gb = grad_ref[:, here]
        p = jnp.exp(dot(k_turned, qb, (1, 0)) - lse_ref[0:1, here])
        dv = dot(gb, p.astype(BF16), (1, 1))
        pd = p * dot(v_turned, gb, (1, 0))
        ds = (pd - p * jnp.sum(pd, axis=0, keepdims=True)).astype(BF16)
        dq_ref[:, here] = dot(k, ds, (1, 0)) + dq_text_ref[:, here]
        dk = dot(qb, ds, (1, 1))
        if first == 0:
            dv_ref[...] = dv
            dk_ref[...] = dk
        else:
            dv_ref[...] += dv
            dk_ref[...] += dk

    def raw_back(which, d_turned):
        spun = turn(d_turned.astype(BF16).astype(F32), table, -1.0)
        values = raw_ref[which]
        d_raw_ref[which] = column_rms_back(values, spun * gain_ref[which]).astype(BF16)
        d_gain_ref[which : which + 1] = row_of_sums(values * column_rms(values) * spun)

    raw_back(0, dq_ref[...] * 0.125)
    raw_back(1, dk_ref[...])
    d_raw_ref[2] = dv_ref[...].astype(BF16)


def attend_back(raw, gains, table, lse, grads, dq_text):
    heads = raw.shape[1]
    return pl.pallas_call(
        attend_back_kernel,
        grid=(heads,),
        in_specs=[
            pl.BlockSpec((3, None, HD, TOKENS), lambda h: (0, h, 0, 0)),
            pl.BlockSpec((3, None, HD, 1), lambda h: (0, h, 0, 0)),
            pl.BlockSpec((4, 16, TOKENS), lambda h: (0, 0, 0)),
            pl.BlockSpec((None, 8, TOKENS), lambda h: (h, 0, 0)),
            pl.BlockSpec((None, HD, TOKENS), lambda h: (h, 0, 0)),
            pl.BlockSpec((None, HD, TOKENS), lambda h: (h, 0, 0)),
        ],
        out_specs=[
            pl.BlockSpec((3, None, HD, TOKENS), lambda h: (0, h, 0, 0)),
            pl.BlockSpec((None, 8, HD), lambda h: (h, 0, 0)),
        ],
        scratch_shapes=[pltpu.VMEM((HD, TOKENS), F32) for _ in range(3)],
        out_shape=[
            jax.ShapeDtypeStruct((3, heads, HD, TOKENS), BF16),
            jax.ShapeDtypeStruct((heads, 8, HD), F32),
        ],
        compiler_params=params(58),
        cost_estimate=LIGHT,
        name="attend_back",
    )(raw, gains, table, lse, grads, dq_text)


def tile_places(chunk_first):
    r, c, k = np.meshgrid(np.arange(ROWS), np.arange(COLS), np.arange(8), indexing="ij")
    token = r * BLOCK + (k // 2) * GRID + c * 2 + k % 2
    source = (k * ROWS + r) * COLS + c if chunk_first else (r * COLS + c) * 8 + k
    places = np.zeros((TOKENS, TOKENS), np.float32)
    places[source.ravel(), token.ravel()] = 1.0
    return jnp.asarray(places, BF16)


def grid_shift(field, di, dj):
    step = di * GRID + dj
    moved = pltpu.roll(field, (-step) % TOKENS, 1) if step else field
    place = lax.broadcasted_iota(jnp.int32, field.shape, 1)
    row = place // GRID + di
    col = place % GRID + dj
    inside = (row >= 0) & (row < GRID) & (col >= 0) & (col < GRID)
    return jnp.where(inside, moved, 0.0)


def image_kernel(packed_ref, place_ref, patch_ref, cot_ref):
    for which, sign, out_ref in ((0, 1, patch_ref), (1, -1, cot_ref)):
        lanes = slice(which * 128, (which + 1) * 128)
        tiles = jnp.concatenate([packed_ref[r, :, lanes] for r in range(ROWS)], 0)
        turned = tiles.astype(F32).T
        chunks = jnp.concatenate([turned[k * 16 : (k + 1) * 16] for k in range(8)], 1)
        image = dot(chunks.astype(BF16), place_ref[...], (1, 0))
        for a in range(3):
            for b in range(3):
                first = (a * 3 + b) * 16
                out_ref[first : first + 16] = grid_shift(
                    image, sign * (a - 1), sign * (b - 1)
                ).astype(BF16)


def image_taps(packed):
    out = jax.ShapeDtypeStruct((144, TOKENS), BF16)
    return pl.pallas_call(
        image_kernel,
        out_shape=[out, out],
        compiler_params=pltpu.CompilerParams(vmem_limit_bytes=12 * MIB),
        cost_estimate=LIGHT,
        name="image_taps",
    )(packed, tile_places(True))


def field_of(taps, place, sign):
    total = jnp.zeros((16, TOKENS), F32)
    for a in range(3):
        for b in range(3):
            first = (a * 3 + b) * 16
            total = total + grid_shift(taps[first : first + 16], sign * (a - 1), sign * (b - 1))
    tiles = dot(total.astype(BF16), place, (1, 1))
    return [tiles[:, r * BLOCK : (r + 1) * BLOCK] for r in range(ROWS)]


def row_rms(v):
    return lax.rsqrt(jnp.mean(v * v, axis=-1, keepdims=True) + EPSILON)


def row_rms_back(v, scale, u):
    return (u - v * (jnp.mean(u * v, axis=-1, keepdims=True) * scale * scale)) * scale


def unpack_kernel(at_ref, *refs):
    piece_refs, (joined_ref, out_ref, turn_ref) = refs[:4], refs[4:]
    part = piece_refs[0].shape[1] // 2
    local_width = piece_refs[0].shape[2] // 2
    for dz in range(4):
        for dy in range(4):
            c = lax.rem(at_ref[2] + dy, 4) * 4 + lax.rem(at_ref[3] + dz, 4)
            rows = pl.ds(pl.multiple_of(c * part, part), part)
            piece = piece_refs[dz][dy]
            joined_ref[0, rows, :] = piece[:part, :local_width]
            joined_ref[1, rows, :] = piece[:part, local_width:]
            joined_ref[2, rows, :] = piece[part:, :local_width]
            turn_ref[rows, :] = piece[part:, local_width:]
    out_ref[...] = turn_ref[...].T


def unpack_head(at, pieces):
    _, rows, lanes = pieces[0].shape
    width, local_width = COLS * rows // 2, lanes // 2
    return pl.pallas_call(
        unpack_kernel,
        grid_spec=pltpu.PrefetchScalarGridSpec(
            num_scalar_prefetch=1,
            grid=(1,),
            in_specs=[whole(pieces[0].shape)] * 4,
            out_specs=[
                pl.BlockSpec((3, width, local_width), lambda t, at: (0, 0, 0)),
                pl.BlockSpec((local_width, width), lambda t, at: (0, 0)),
            ],
            scratch_shapes=[pltpu.VMEM((width, local_width), BF16)],
        ),
        out_shape=[
            jax.ShapeDtypeStruct((3, width, local_width), BF16),
            jax.ShapeDtypeStruct((local_width, width), BF16),
        ],
        compiler_params=params(14),
        cost_estimate=LIGHT,
        name="unpack_head",
    )(at, *pieces)


def text_kernel(at_ref, p0_ref, p1_ref, p2_ref, p3_ref, caption_ref, raw_ref):
    rows = p0_ref.shape[1]
    total = 0.0
    for dy, ref in enumerate((p0_ref, p1_ref, p2_ref, p3_ref)):
        for dz in range(4):
            c = lax.rem(at_ref[2] + dy, 4) * 4 + lax.rem(at_ref[3] + dz, 4)
            lanes = pl.ds(pl.multiple_of(c * rows, rows), rows)
            total = total + dot(ref[dz], caption_ref[:, lanes], (0, 1))
    raw_ref[...] = total


def text_project(at, pieces, caption):
    lanes = pieces[0].shape[2]
    slots = caption.shape[0]
    return pl.pallas_call(
        text_kernel,
        grid_spec=pltpu.PrefetchScalarGridSpec(
            num_scalar_prefetch=1,
            grid=(1,),
            in_specs=[whole(pieces[0].shape)] * 4 + [whole(caption.shape)],
            out_specs=pl.BlockSpec((lanes, slots), lambda t, at: (0, 0)),
        ),
        out_shape=jax.ShapeDtypeStruct((lanes, slots), F32),
        compiler_params=params(16),
        cost_estimate=LIGHT,
        name="text_project",
    )(at, *pieces, caption)


def qkv_kernel(patch_ref, embed_ref, vec_ref, weight_ref, raw_ref):
    x = dot(patch_ref[...], embed_ref[...], (0, 0))
    h = (x * row_rms(x) * vec_ref[0:1]).astype(BF16)
    for s in range(3):
        raw_ref[s] = dot(h, weight_ref[s], (1, 0)).T


def qkv_project(patches, embed, vec, weight):
    part = weight.shape[2]
    return pl.pallas_call(
        qkv_kernel,
        grid=(TOKENS // PAIR,),
        in_specs=[lane_block(144, PAIR), whole(embed.shape), whole(vec.shape), whole(weight.shape)],
        out_specs=pl.BlockSpec((3, part, PAIR), lambda t: (0, 0, t)),
        out_shape=jax.ShapeDtypeStruct((3, part, TOKENS), F32),
        compiler_params=params(16),
        cost_estimate=LIGHT,
        name="qkv_project",
    )(patches, embed, vec, weight)


def joined(ref):
    return ref[...].reshape(-1, ref.shape[2])


def halves(core, first, second):
    return jnp.where(core == 0, first, second)


def forward_kernel(
    at_ref, near_ref, far_ref, out_near_ref, out_far_ref, patch_ref, embed_ref, vec_ref, ffn_ref,
    attn_ref, second_ref, gate_up_ref, hidden_ref, own_ref, other_ref,
):
    core = at_ref[1]
    hidden_width = hidden_ref.shape[1]
    x = dot(patch_ref[...], embed_ref[...], (0, 0))
    attn = dot(joined(near_ref), joined(out_near_ref), (0, 0))
    attn = attn + dot(joined(far_ref), joined(out_far_ref), (0, 0))
    attn_ref[...] = attn.astype(BF16)
    mid = x + vec_ref[1:2] * (attn * row_rms(attn))
    second = (mid * row_rms(mid) * vec_ref[2:3]).astype(BF16)
    second_ref[...] = second
    gate_up = dot(second, ffn_ref[:, : 2 * hidden_width], (1, 0))
    gate_up_ref[...] = gate_up.astype(BF16)
    gate = gate_up[:, :hidden_width]
    hidden = (gate * jax.nn.sigmoid(gate) * gate_up[:, hidden_width:]).astype(BF16)
    hidden_ref[...] = hidden
    part = dot(hidden, ffn_ref[:, 2 * hidden_width :], (1, 1)).astype(BF16)
    own_ref[0] = halves(core, part[:BLOCK], part[BLOCK:])
    other_ref[0] = halves(core, part[BLOCK:], part[:BLOCK])


def forward(at, mixed, out_whole, patches, embed, vec, ffn):
    width = embed.shape[1]
    part = mixed[0].shape[1]
    hidden_width = ffn.shape[1] // 3
    by_chip = pl.BlockSpec((1, BLOCK, width), lambda t, at: ((t - at[0] + 4) % 4, 0, 0))
    return pl.pallas_call(
        forward_kernel,
        grid_spec=pltpu.PrefetchScalarGridSpec(
            num_scalar_prefetch=1,
            grid=(4,),
            in_specs=[
                pl.BlockSpec((4, part, PAIR), lambda t, at: (0, 0, t)),
                pl.BlockSpec((4, part, PAIR), lambda t, at: (0, 0, t)),
                whole((4, part, width)),
                whole((4, part, width)),
                lane_block(144, PAIR),
                whole(embed.shape),
                whole(vec.shape),
                whole(ffn.shape),
            ],
            out_specs=[
                row_block(PAIR, width),
                row_block(PAIR, width),
                row_block(PAIR, 2 * hidden_width),
                row_block(PAIR, hidden_width),
                by_chip,
                by_chip,
            ],
        ),
        out_shape=[
            jax.ShapeDtypeStruct((TOKENS, width), BF16),
            jax.ShapeDtypeStruct((TOKENS, width), BF16),
            jax.ShapeDtypeStruct((TOKENS, 2 * hidden_width), BF16),
            jax.ShapeDtypeStruct((TOKENS, hidden_width), BF16),
            jax.ShapeDtypeStruct((4, BLOCK, width), BF16),
            jax.ShapeDtypeStruct((4, BLOCK, width), BF16),
        ],
        compiler_params=params(56),
        cost_estimate=LIGHT,
        name="forward",
    )(at, *mixed, *out_whole, patches, embed, vec, ffn)


def own_grad_kernel(p0_ref, p1_ref, p2_ref, p3_ref, cot_ref, unpatch_ref, vec_ref, d_ffn_ref, ffn_ref):
    ffn = sum(p[...].astype(F32) for p in (p0_ref, p1_ref, p2_ref, p3_ref))
    ffn_ref[...] = ffn
    d_last = dot(cot_ref[...], unpatch_ref[...], (0, 0))
    d_ffn_ref[...] = row_rms_back(ffn, row_rms(ffn), vec_ref[3:4] * d_last).astype(BF16)


def own_grad(pieces, cot_own, unpatch, vec):
    shape = (BLOCK, unpatch.shape[1])
    return pl.pallas_call(
        own_grad_kernel,
        out_shape=[jax.ShapeDtypeStruct(shape, BF16), jax.ShapeDtypeStruct(shape, F32)],
        compiler_params=pltpu.CompilerParams(vmem_limit_bytes=58 * MIB),
        cost_estimate=LIGHT,
        name="own_grad",
    )(*pieces, cot_own, unpatch, vec)


def own_kernel(
    at_ref, ffn_ref, attn_ref, patch_ref, cot_ref, embed_ref, unpatch_ref, vec_ref, place_ref,
    field_ref, unpatch_sum_ref, sums_ref, taps_ref,
):
    ffn = ffn_ref[...]
    d_last = dot(cot_ref[...], unpatch_ref[...], (0, 0))
    normed_ffn = ffn * row_rms(ffn)
    sums_ref[...] = jnp.broadcast_to(
        jnp.sum(normed_ffn * d_last, axis=0, keepdims=True), sums_ref.shape
    )
    attn = attn_ref[...].astype(F32)
    x = dot(patch_ref[...], embed_ref[...], (0, 0))
    last = (x + vec_ref[1:2] * (attn * row_rms(attn)) + vec_ref[3:4] * normed_ffn).astype(BF16)
    unpatch_sum_ref[...] = dot(cot_ref[...], last, (1, 0))
    taps_ref[...] = jnp.zeros_like(taps_ref)
    here = pl.multiple_of((2 * at_ref[0] + at_ref[1]) * BLOCK, BLOCK)
    taps_ref[:, pl.ds(here, BLOCK)] = dot(unpatch_ref[...], last, (1, 1))
    for r, tile in enumerate(field_of(taps_ref[...], place_ref[...], 1)):
        field_ref[r] = tile


def own_block(at, ffn, attn, patches, cot_taps, embed, unpatch, vec, place):
    width = embed.shape[1]
    lanes = pl.BlockSpec((144, BLOCK), lambda t, at: (0, 2 * at[0] + at[1]))
    return pl.pallas_call(
        own_kernel,
        grid_spec=pltpu.PrefetchScalarGridSpec(
            num_scalar_prefetch=1,
            grid=(1,),
            in_specs=[
                whole((BLOCK, width)),
                pl.BlockSpec((BLOCK, width), lambda t, at: (2 * at[0] + at[1], 0)),
                lanes,
                lanes,
                whole(embed.shape),
                whole(unpatch.shape),
                whole(vec.shape),
                whole(place.shape),
            ],
            out_specs=[
                pl.BlockSpec((ROWS, 16, BLOCK), lambda t, at: (0, 0, 0)),
                pl.BlockSpec((144, width), lambda t, at: (0, 0)),
                pl.BlockSpec((8, width), lambda t, at: (0, 0)),
            ],
            scratch_shapes=[pltpu.VMEM((144, TOKENS), F32)],
        ),
        out_shape=[
            jax.ShapeDtypeStruct((ROWS, 16, BLOCK), F32),
            jax.ShapeDtypeStruct((144, width), F32),
            jax.ShapeDtypeStruct((8, width), F32),
        ],
        compiler_params=params(14),
        cost_estimate=LIGHT,
        name="own_block",
    )(at, ffn, attn, patches, cot_taps, embed, unpatch, vec, place)


def backward_kernel(
    at_ref, own_ref, other_ref, ffn_ref, out_near_ref, out_far_ref, gate_up_ref, attn_ref,
    patch_ref, embed_ref, cot_ref, unpatch_ref, vec_ref,
    d_ffn_ref, d_gate_up_ref, d_attn_ref, d_mid_ref, mixed_own_ref, mixed_other_ref, sums_ref,
):
    step = pl.program_id(0)
    chip, core = at_ref[0], at_ref[1]
    hidden_width = d_gate_up_ref.shape[1] // 2
    own, other = own_ref[0], other_ref[0]
    d_ffn = jnp.concatenate([halves(core, own, other), halves(core, other, own)], 0)
    d_ffn_ref[...] = d_ffn
    d_hidden = dot(d_ffn, ffn_ref[:, 2 * hidden_width :], (1, 0))
    gate = gate_up_ref[:, :hidden_width].astype(F32)
    up = gate_up_ref[:, hidden_width:].astype(F32)
    sigma = jax.nn.sigmoid(gate)
    silu = gate * sigma
    d_gate = d_hidden * up * (sigma + silu * (1.0 - sigma))
    d_gate_up = jnp.concatenate([d_gate.astype(BF16), (d_hidden * silu).astype(BF16)], 1)
    d_gate_up_ref[...] = d_gate_up
    d_second = dot(d_gate_up, ffn_ref[:, : 2 * hidden_width], (1, 1))

    x = dot(patch_ref[...], embed_ref[...], (0, 0))
    attn = attn_ref[...].astype(F32)
    attn_scale = row_rms(attn)
    attn_normed = attn * attn_scale
    mid = x + vec_ref[1:2] * attn_normed
    mid_scale = row_rms(mid)
    mid_sum = jnp.sum(mid * mid_scale * d_second, axis=0, keepdims=True)
    d_last = dot(cot_ref[...], unpatch_ref[...], (0, 0))
    place = lax.broadcasted_iota(jnp.int32, (PAIR, 1), 0) // BLOCK
    mine = (place == core) & (step == chip)
    d_mid = row_rms_back(mid, mid_scale, vec_ref[2:3] * d_second) + jnp.where(mine, d_last, 0.0)
    d_mid_ref[...] = d_mid.astype(BF16)
    attn_sum = jnp.sum(attn_normed * d_mid, axis=0, keepdims=True)
    d_attn = row_rms_back(attn, attn_scale, vec_ref[1:2] * d_mid).astype(BF16)
    d_attn_ref[...] = d_attn
    for weight_ref, part_ref in ((out_near_ref, mixed_own_ref), (out_far_ref, mixed_other_ref)):
        part_ref[...] = dot(joined(weight_ref), d_attn, (1, 1)).astype(BF16).reshape(part_ref.shape)

    @pl.when(step == 0)
    def _():
        sums_ref[...] = jnp.zeros_like(sums_ref)

    sums_ref[0:1] += mid_sum
    sums_ref[1:2] += attn_sum


def backward(at, d_ffn, ffn, out_whole, gate_up, attn, patches, embed, cot_taps, unpatch, vec):
    width = embed.shape[1]
    part = out_whole[0].shape[1]
    hidden_width = ffn.shape[1] // 3
    by_chip = pl.BlockSpec((1, BLOCK, width), lambda t, at: ((t - at[0] + 4) % 4, 0, 0))
    parts = pl.BlockSpec((4, part, PAIR), lambda t, at: (0, 0, t))
    return pl.pallas_call(
        backward_kernel,
        grid_spec=pltpu.PrefetchScalarGridSpec(
            num_scalar_prefetch=1,
            grid=(4,),
            in_specs=[
                by_chip,
                by_chip,
                held(),
                held(),
                held(),
                row_block(PAIR, 2 * hidden_width),
                row_block(PAIR, width),
                lane_block(144, PAIR),
                whole(embed.shape),
                lane_block(144, PAIR),
                whole(unpatch.shape),
                whole(vec.shape),
            ],
            out_specs=[
                row_block(PAIR, width),
                row_block(PAIR, 2 * hidden_width),
                row_block(PAIR, width),
                row_block(PAIR, width),
                parts,
                parts,
                pl.BlockSpec((8, width), lambda t, at: (0, 0)),
            ],
        ),
        out_shape=[
            jax.ShapeDtypeStruct((TOKENS, width), BF16),
            jax.ShapeDtypeStruct((TOKENS, 2 * hidden_width), BF16),
            jax.ShapeDtypeStruct((TOKENS, width), BF16),
            jax.ShapeDtypeStruct((TOKENS, width), BF16),
            jax.ShapeDtypeStruct((4, part, TOKENS), BF16),
            jax.ShapeDtypeStruct((4, part, TOKENS), BF16),
            jax.ShapeDtypeStruct((8, width), F32),
        ],
        compiler_params=params(32),
        cost_estimate=LIGHT,
        name="backward",
    )(at, *d_ffn, ffn, *out_whole, gate_up, attn, patches, embed, cot_taps, unpatch, vec)


def weight_kernel(
    second_ref, d_gate_up_ref, d_ffn_ref, hidden_ref, near_ref, far_ref, d_attn_ref,
    grads_ref, out_near_ref, out_far_ref,
):
    step = pl.program_id(0)
    chunk, _, lanes = grads_ref.shape[0] // 4, *grads_ref.shape[1:]
    part = second_ref.shape[1] // chunk
    rows = jnp.concatenate(
        [
            dot(second_ref[...], d_gate_up_ref[...], (0, 0)).astype(BF16),
            dot(d_ffn_ref[...], hidden_ref[...], (0, 0)).astype(BF16),
        ],
        1,
    )
    groups = rows.shape[1] // lanes
    first = grads_ref.shape[1] - groups * part
    for c in range(chunk):
        for g in range(groups):
            grads_ref[step * chunk + c, first + g * part : first + (g + 1) * part] = rows[
                c * part : (c + 1) * part, g * lanes : (g + 1) * lanes
            ]
    out_near_ref[0] = dot(near_ref[0], d_attn_ref[...], (1, 0)).astype(BF16)
    out_far_ref[0] = dot(far_ref[0], d_attn_ref[...], (1, 0)).astype(BF16)


def weight_grads(second, d_gate_up, d_ffn, hidden, mixed, d_attn, text_rows):
    width = second.shape[1]
    heads_width = mixed[0].shape[1]
    lanes = 2 * heads_width
    grads = (COLS, text_rows + width // COLS * 3 * hidden.shape[1] // lanes, lanes)
    pieces = pl.BlockSpec((1, heads_width, TOKENS), lambda t: (t, 0, 0))
    out_piece = pl.BlockSpec((1, heads_width, width), lambda t: (t, 0, 0))
    out_shape = jax.ShapeDtypeStruct((4, heads_width, width), BF16)
    return pl.pallas_call(
        weight_kernel,
        grid=(4,),
        in_specs=[
            lane_block(TOKENS, width // 4),
            whole(d_gate_up.shape),
            lane_block(TOKENS, width // 4),
            whole(hidden.shape),
            pieces,
            pieces,
            whole(d_attn.shape),
        ],
        out_specs=[pl.BlockSpec(grads, lambda t: (0, 0, 0)), out_piece, out_piece],
        out_shape=[jax.ShapeDtypeStruct(grads, BF16), out_shape, out_shape],
        compiler_params=params(40),
        cost_estimate=LIGHT,
        name="weight_grads",
    )(second, d_gate_up, d_ffn, hidden, *mixed, d_attn)


def first_kernel(
    at_ref, gate_ref, patch_ref, embed_ref, vec_ref, weight_ref, d_raw_ref, d_mid_ref, place_ref, out_sum_ref,
    unpatch_sum_ref, back_sums_ref, own_sums_ref, head_ref, text_head_ref, gains_ref, mod_ref, activation_ref,
    own_pack_ref, other_pack_ref, p0_ref, p1_ref, p2_ref, p3_ref,
    taps_acc, embed_acc, first_acc, shared_acc, qkv_acc, turned_acc,
):
    step = pl.program_id(0)
    last = pl.num_programs(0) - 1
    x = dot(patch_ref[...], embed_ref[...], (0, 0))
    scale = row_rms(x)
    x_normed = x * scale
    h = (x_normed * vec_ref[0:1]).astype(BF16)
    d_h = dot(d_raw_ref[0], weight_ref[0], (0, 1))
    for s in (1, 2):
        d_h = d_h + dot(d_raw_ref[s], weight_ref[s], (0, 1))

    @pl.when(step == 0)
    def _():
        qkv_acc[...] = jnp.zeros_like(qkv_acc)
        embed_acc[...] = jnp.zeros_like(embed_acc)
        first_acc[...] = jnp.zeros_like(first_acc)

    qkv_acc[...] += dot(joined(d_raw_ref), h, (1, 0)).reshape(qkv_acc.shape)
    first_acc[0:1] += jnp.sum(x_normed * d_h, axis=0, keepdims=True)
    d_first = (d_mid_ref[...].astype(F32) + row_rms_back(x, scale, vec_ref[0:1] * d_h)).astype(BF16)
    embed_acc[...] += dot(patch_ref[...], d_first, (1, 0))
    here = pl.ds(pl.multiple_of(step * PAIR, PAIR), PAIR)
    taps_acc[:, here] = dot(embed_ref[...], d_first, (1, 1))

    @pl.when(step == last)
    def _():
        part = p0_ref.shape[1] // 2
        for s in range(4):
            turned_acc[s] = (qkv_acc[s] if s < 3 else out_sum_ref[...]).T.astype(BF16)
        for dz, ref in enumerate((p0_ref, p1_ref, p2_ref, p3_ref)):
            z = lax.rem(at_ref[3] + dz, 4)
            for y in range(4):
                dy = lax.rem(y - at_ref[2] + 4, 4)
                first = pl.multiple_of((y * 4 + z) * part, part)
                pieces = [turned_acc[s, pl.ds(first, part), :] for s in range(4)]
                for k in range(2):
                    ref[dy, k * part : (k + 1) * part] = jnp.concatenate(
                        pieces[2 * k : 2 * k + 2], 1
                    )
        terms = jnp.concatenate(
            [first_acc[0:1], back_sums_ref[1:2], back_sums_ref[0:1], own_sums_ref[0:1]], 0
        )
        gates = [jnp.tanh(mod_ref[k : k + 1]) for k in (1, 3)]
        into = jnp.concatenate(
            [1.0 + mod_ref[0:1], gates[0], 1.0 + mod_ref[2:3], gates[1]], 0
        )
        d_gains = terms * into
        slope = jnp.concatenate(
            [jnp.ones_like(gates[0]), 1.0 - gates[0] * gates[0]] * 1
            + [jnp.ones_like(gates[0]), 1.0 - gates[1] * gates[1]],
            0,
        )
        d_modulation = terms * gains_ref[0:4] * slope
        heads = head_ref.shape[0]
        width = d_gains.shape[1]
        rows = [head_ref[h] for h in range(heads)], [text_head_ref[h] for h in range(heads)]
        own = jnp.concatenate(
            [
                jnp.concatenate([r[0:2] for r in rows[0]], 1),
                jnp.concatenate([r[0:1] for r in rows[1]], 1),
                jnp.zeros((5, heads * HD), F32),
            ],
            0,
        )
        own = jnp.concatenate([own, jnp.zeros((8, width - heads * HD), F32)], 1)
        row_at = 2 * at_ref[0] + at_ref[1]
        own = pltpu.roll(own, row_at * (heads * HD), 1)
        lane = lax.broadcasted_iota(jnp.int32, (1, width), 1)
        gate_row = jnp.zeros((1, width), F32)
        for h in range(heads):
            total = jnp.sum(rows[1][h][1:2], axis=1, keepdims=True)
            total = total * (1.0 - gate_ref[h] * gate_ref[h])
            gate_row = gate_row + jnp.where(lane == row_at * heads + h, total, 0.0)
        small = jnp.concatenate(
            [d_gains, own[0:3], gate_row, jnp.zeros((24, width), F32)], 0
        )
        for tile in range(12):
            lanes = slice(tile * 128, (tile + 1) * 128)
            first = tile * SHARED
            shared_acc[first : first + 144] = embed_acc[:, lanes].astype(BF16)
            shared_acc[first + 144 : first + 288] = unpatch_sum_ref[:, lanes].astype(BF16)
            shared_acc[first + 288 : first + SHARED] = small[:, lanes].astype(BF16)
        shared_acc[12 * SHARED :] = jnp.zeros((8 * CHUNK - 12 * SHARED, 128), BF16)
        latent = field_of(taps_acc[...], place_ref[...], -1)
        rows = [
            d_modulation[q : q + 1, tile * 128 : (tile + 1) * 128]
            for q in range(4)
            for tile in range(12)
        ]
        for r in range(ROWS):
            ahead = lax.rem(r // 2 - at_ref[0] + 4, 4)
            mods = jnp.concatenate(rows[6 * r : 6 * r + 6] + [jnp.zeros((10, 128), F32)], 0)
            piece = jnp.concatenate(
                [
                    shared_acc[r * CHUNK : (r + 1) * CHUNK],
                    activation_ref[r].astype(BF16),
                    latent[r].astype(BF16),
                    mods.astype(BF16),
                ],
                0,
            )

            @pl.when(at_ref[1] == r % 2)
            def _():
                own_pack_ref[ahead] = piece

            @pl.when(at_ref[1] != r % 2)
            def _():
                other_pack_ref[ahead] = piece


def first_back(
    at, gates, patches, embed, vec, weight, d_raw, d_mid, place, out_sum, unpatch_sum, back_sums, own_sums,
    head, text_head, gains, modulation, activation,
):
    width = embed.shape[1]
    part = weight.shape[2]
    pack = (4, CHUNK + 48, 128)
    grads = (4, 2 * width // COLS, 2 * part)
    rest = (place, out_sum, unpatch_sum, back_sums, own_sums, head, text_head, gains, modulation, activation)
    return pl.pallas_call(
        first_kernel,
        grid_spec=pltpu.PrefetchScalarGridSpec(
            num_scalar_prefetch=2,
            grid=(TOKENS // PAIR,),
            in_specs=[
                lane_block(144, PAIR),
                whole(embed.shape),
                whole(vec.shape),
                held(),
                pl.BlockSpec((3, part, PAIR), lambda t, *_: (0, 0, t)),
                row_block(PAIR, width),
            ]
            + [held()]
            + [whole(value.shape) for value in rest[1:]],
            out_specs=[pl.BlockSpec(pack, lambda t, *_: (0, 0, 0))] * 2
            + [pl.BlockSpec(grads, lambda t, *_: (0, 0, 0))] * 4,
            scratch_shapes=[
                pltpu.VMEM((144, TOKENS), F32),
                pltpu.VMEM((144, width), F32),
                pltpu.VMEM((8, width), F32),
                pltpu.VMEM((8 * CHUNK, 128), BF16),
                pltpu.VMEM((3, part, width), F32),
                pltpu.VMEM((4, width, part), BF16),
            ],
        ),
        out_shape=[jax.ShapeDtypeStruct(pack, BF16)] * 2 + [jax.ShapeDtypeStruct(grads, BF16)] * 4,
        compiler_params=params(58),
        cost_estimate=LIGHT,
        name="first_back",
    )(at, gates, patches, embed, vec, weight, d_raw, d_mid, *rest)


def local(
    latent, condition, caption, cap_len, cotangent, embed_weight, modulate_weight, norm_gains,
    cross_gate, qkv_weight, text_kv_weight, out_weight, gate_up_weight, down_weight, unpatch_weight,
):
    images, _, _, channels = latent.shape
    width = embed_weight.shape[3]
    local_width = qkv_weight.shape[2]
    heads = local_width // HD
    hidden_width = down_weight.shape[0]
    taps = 9 * channels
    row_at = lax.axis_index("row")
    col_at = lax.axis_index("col")
    at = jnp.stack([row_at // 2, row_at % 2, col_at // 4, col_at % 4]).astype(jnp.int32)
    tile = latent.shape[1] * latent.shape[2] * channels

    cond_low = jax.nn.silu(condition.astype(F32)).astype(BF16)
    mod_piece = jnp.dot(cond_low, modulate_weight, preferred_element_type=F32)
    mod_columns = mod_piece.shape[1]
    mod_high = mod_piece.astype(BF16)
    mod_low = (mod_piece - mod_high.astype(F32)).astype(BF16)

    packed = jnp.concatenate(
        [latent.reshape(images, tile), cotangent.reshape(images, tile), mod_high, mod_low], axis=1
    )
    packed = jnp.pad(packed, ((0, 0), (0, 2 * local_width - packed.shape[1])))

    head_piece = jnp.concatenate(
        [
            jnp.concatenate([qkv_weight[0], qkv_weight[1]], axis=1),
            jnp.concatenate([qkv_weight[2], out_weight.T], axis=1),
        ]
    )
    text_piece = jnp.concatenate([text_kv_weight[0], text_kv_weight[1]], axis=1)
    head_pieces = from_col(head_piece, along_y)
    text_pieces = from_col(text_piece, along_z)
    packed = lax.all_to_all(packed, "col", 0, 0, tiled=True)
    packed, *reached = lax.optimization_barrier((packed, *head_pieces, *text_pieces))
    head_pieces, text_pieces = reached[:4], reached[4:]
    packed = send_all(packed, "row")
    patches, cot_taps = image_taps(packed)
    head_pieces = from_col(jnp.stack(head_pieces), along_z)
    text_own = jnp.stack(text_pieces)
    text_beside = [lax.ppermute(text_own, "col", col_pairs(d, 0)) for d in (1, 3)]
    ffn_piece = jnp.concatenate([gate_up_weight[0], gate_up_weight[1], down_weight.T], axis=1)
    ffn_piece, patches, text_own, next_text, last_text, *head_pieces = lax.optimization_barrier(
        (ffn_piece, patches, text_own, *text_beside, *head_pieces)
    )
    ffn_whole = lax.all_gather(ffn_piece, "col", axis=0, tiled=True)
    text_apart = lax.ppermute(text_own, "col", col_pairs(2, 0))
    text_pieces = [text_own, next_text, text_apart, last_text]
    qkv_whole, out_rows = unpack_head(at, head_pieces)
    out_pieces = from_chips(out_rows)

    mod_at = 2 * tile
    modulation = packed[:, :, mod_at : mod_at + mod_columns].astype(F32)
    modulation = modulation + packed[:, :, mod_at + mod_columns : mod_at + 2 * mod_columns].astype(F32)
    modulation = modulation.reshape(4, width)
    attn_gate = jnp.tanh(modulation[1])
    ffn_gate = jnp.tanh(modulation[3])
    vec = jnp.stack(
        [
            norm_gains[0] * (1.0 + modulation[0]),
            norm_gains[1] * attn_gate,
            norm_gains[2] * (1.0 + modulation[2]),
            norm_gains[3] * ffn_gate,
        ]
    )
    vec = jnp.pad(vec, ((0, 4), (0, 0)))
    embed = embed_weight.reshape(taps, width)
    unpatch = unpatch_weight.transpose(0, 1, 3, 2).reshape(taps, width)
    raw = qkv_project(patches, embed, vec, qkv_whole)
    raw = raw.reshape(3, heads, HD, TOKENS)
    caption_rows = caption[0]
    text_raw = text_project(at, text_pieces, caption_rows)
    text_raw = text_raw.reshape(2, heads, HD, caption_rows.shape[0])
    head_gains = lax.dynamic_slice(norm_gains, (4, row_at * local_width), (3, local_width)).reshape(
        3, heads, HD, 1
    )
    head_gates = jnp.tanh(lax.dynamic_slice_in_dim(cross_gate, row_at * heads, heads))
    cap = lax.dynamic_slice_in_dim(cap_len, col_at, 1)
    table = jnp.asarray(rope_tables())
    mixed, lse = attend(raw, text_raw, head_gains, table, cap, head_gates)

    mixed_pieces = from_chips(mixed)
    reached = lax.optimization_barrier((*mixed_pieces, *out_pieces))
    mixed_whole = with_other_core(reached[:4])
    out_whole = with_other_core(reached[4:])
    attn, second, gate_up, hidden, ffn_own, ffn_other = forward(
        at, mixed_whole, out_whole, patches, embed, vec, ffn_whole
    )
    place = tile_places(False)
    cot_own = lax.dynamic_slice_in_dim(cot_taps, row_at * BLOCK, BLOCK, 1)
    d_ffn_own, ffn_out = own_grad(
        to_chips(sum_cores(ffn_own, ffn_other)), cot_own, unpatch, vec
    )
    d_ffn_near = from_chips(d_ffn_own)
    activation_field, unpatch_sum, own_sums = own_block(
        at, ffn_out, attn, patches, cot_taps, embed, unpatch, vec, place
    )
    d_ffn_near = lax.optimization_barrier((*d_ffn_near, activation_field))[:4]
    d_ffn, d_gate_up, d_attn, d_mid, mixed_own, mixed_other, back_sums = backward(
        at, with_other_core(d_ffn_near), ffn_whole, out_whole, gate_up, attn, patches, embed, cot_taps,
        unpatch, vec,
    )
    mixed_near = sum_cores(mixed_own, mixed_other)
    mixed_terms = to_chips(mixed_near)
    text_rows = text_kv_weight.shape[1]
    grads, out_near, out_far = weight_grads(
        after(second, *mixed_near), d_gate_up, d_ffn, hidden, mixed_whole, d_attn, text_rows
    )
    *mixed_terms, grads, out_near, out_far = lax.optimization_barrier(
        (*mixed_terms, grads, out_near, out_far)
    )
    d_mixed = sum(term.astype(F32) for term in mixed_terms).astype(BF16)
    d_mixed = d_mixed.reshape(heads, HD, TOKENS)
    out_near = sum_cores(out_near, out_far)
    out_apart = lax.ppermute(out_near[2], "row", row_pairs_to(2, 0))

    grads, dq_text, d_text_head = text_back(
        raw, text_raw, head_gains, table, lse, d_mixed, cap, head_gates, caption_rows,
        after(grads, *out_near),
    )
    dq_text, grads, out_apart, *out_near = lax.optimization_barrier(
        (dq_text, grads, out_apart, *out_near)
    )
    d_raw, d_head = attend_back(raw, head_gains, table, lse, d_mixed, dq_text)
    out_beside = [lax.ppermute(out_near[d], "row", row_pairs_to(d, 0)) for d in (1, 3)]
    d_raw, *out_terms = lax.optimization_barrier((d_raw, out_near[0], out_apart, *out_beside))
    out_sum = sum(term.astype(F32) for term in out_terms)
    d_raw = d_raw.reshape(3, local_width, TOKENS)
    own_pack, other_pack, *head_parts = first_back(
        at, head_gates, patches, embed, vec, qkv_whole, d_raw, d_mid, place, out_sum, unpatch_sum,
        back_sums, own_sums, d_head, d_text_head, norm_gains, modulation, activation_field,
    )
    beside = [lax.ppermute(head_parts[d], "col", col_pairs_to(0, d)) for d in (1, 3)]

    row_terms = to_chips(sum_cores(own_pack, other_pack))
    row_pack = sum(term.astype(F32) for term in row_terms)
    fields = row_pack[CHUNK : CHUNK + 2 * channels].T.reshape(COLS, 8, 2 * channels)
    mod_sums = row_pack[CHUNK + 2 * channels : CHUNK + 2 * channels + 6].reshape(COLS, 8, 6)
    fields = jnp.concatenate([fields, mod_sums], axis=2).astype(BF16)
    fields = jnp.pad(fields, ((0, 0), (0, 0), (0, 128 - fields.shape[2])))
    shared = row_pack[:CHUNK].astype(BF16).reshape(COLS, CHUNK // COLS, 128)
    col_pack = lax.all_to_all(jnp.concatenate([shared, fields], axis=1), "col", 0, 0)
    col_pack, left, right = lax.optimization_barrier((col_pack, *beside))
    shared = jnp.sum(col_pack[:, : CHUNK // COLS].astype(F32), axis=0)
    shared, apart = lax.optimization_barrier(
        (send_all(shared.astype(BF16), "col"), head_parts[2])
    )
    shared = send_all(shared, "row").reshape(-1, 128)
    apart = lax.ppermute(apart, "col", col_pairs_to(0, 2))
    head_near = sum(term.astype(F32) for term in (head_parts[0], left, apart, right)).astype(BF16)
    shared = shared[: 12 * SHARED].reshape(12, SHARED, 128).astype(F32)
    fields = col_pack[:, CHUNK // COLS :]
    activation = fields[:, :, :channels].reshape(latent.shape)
    latent_grad = fields[:, :, channels : 2 * channels].reshape(latent.shape)
    modulate_grad = lax.dot_general(
        cond_low.astype(F32),
        fields[:, :, 2 * channels : 2 * channels + 6].reshape(images, mod_columns).astype(F32),
        (((0,), (0,)), ((), ())),
        precision=lax.Precision.HIGHEST,
        preferred_element_type=F32,
    )
    embed_grad = shared[:, :taps].transpose(1, 0, 2).reshape(embed_weight.shape)
    unpatch_grad = shared[:, taps : 2 * taps].reshape(12, 3, 3, channels, 128)
    unpatch_grad = unpatch_grad.transpose(1, 2, 0, 4, 3).reshape(unpatch_weight.shape)
    gains_grad = shared[:, 2 * taps : 2 * taps + 7].transpose(1, 0, 2).reshape(7, width)
    gate_grad = shared[0, 2 * taps + 7, :HEADS]

    part = width // COLS
    grads = lax.psum_scatter(
        grads.reshape(-1, 2 * local_width), "col", scatter_dimension=0, tiled=True
    ).astype(F32)
    text_kv_grad = jnp.stack([grads[:text_rows, :local_width], grads[:text_rows, local_width:]])
    ffn_total = jnp.concatenate(
        [grads[first : first + part] for first in range(text_rows, grads.shape[0], part)], axis=1
    )
    gate_up_grad = jnp.stack(
        [ffn_total[:, :hidden_width], ffn_total[:, hidden_width : 2 * hidden_width]]
    )
    down_grad = ffn_total[:, 2 * hidden_width :].T
    head_terms, others = lax.optimization_barrier(
        (
            along_col(head_near, along_y),
            (
                activation, latent_grad, embed_grad, modulate_grad, gains_grad, gate_grad,
                text_kv_grad, gate_up_grad, down_grad, unpatch_grad,
            ),
        )
    )
    (
        activation, latent_grad, embed_grad, modulate_grad, gains_grad, gate_grad,
        text_kv_grad, gate_up_grad, down_grad, unpatch_grad,
    ) = others
    head_total = sum(term.astype(F32) for term in head_terms)
    first, second_half = head_total[:, :local_width], head_total[:, local_width:]
    qkv_grad = jnp.stack([first[:part], second_half[:part], first[part:]])
    out_grad = second_half[part:].T
    return (
        activation, latent_grad, embed_grad, modulate_grad, gains_grad, gate_grad,
        qkv_grad, text_kv_grad, out_grad, gate_up_grad, down_grad, unpatch_grad,
    )


def solution(mesh):
    placed = (
        P(None, "row", "col", None),
        P(),
        P("col", None, None),
        P(),
        P(None, "row", "col", None),
        P(),
        P(None, ("row", "col")),
        P(),
        P(),
        P(None, "col", "row"),
        P(None, "col", "row"),
        P("row", "col"),
        P(None, "col", "row"),
        P("row", "col"),
        P(),
    )
    return jax.shard_map(
        local,
        mesh=mesh,
        in_specs=placed,
        out_specs=(
            P(None, "row", "col", None),
            P(None, "row", "col", None),
            P(),
            P(None, ("row", "col")),
            P(),
            P(),
            P(None, "col", "row"),
            P(None, "col", "row"),
            P("row", "col"),
            P(None, "col", "row"),
            P("row", "col"),
            P(),
        ),
        check_vma=False,
    )
```

```python
import math
from functools import partial

import jax
import jax.numpy as jnp
import numpy as np
from jax import lax
from jax.experimental import pallas as pl
from jax.experimental.pallas import tpu as pltpu
from jax.sharding import PartitionSpec as P

HEADS = 24
HD = 64
GRID = 32
TOKENS = GRID * GRID
EPSILON = 1e-06
ROPE_BASE = 10000.0
MASKED = -1e30
F32 = jnp.float32
BF16 = jnp.bfloat16
ROWS = 8
COLS = 16
QUERY_BLOCK = 256
BLOCK = TOKENS // ROWS
PAIR = 2 * BLOCK
MIB = 2**20
SHARED = 320
CHUNK = 512
LIGHT = pl.CostEstimate(flops=1, bytes_accessed=1, transcendentals=0)


def dot(left, right, contract):
    return lax.dot_general(
        left, right, ((contract[:1], contract[1:]), ((), ())), preferred_element_type=F32
    )


def row_pairs(dx, dc):
    return [
        (((x + dx) % 4) * 2 + (c + dc) % 2, x * 2 + c) for x in range(4) for c in range(2)
    ]


def row_pairs_to(dx, dc):
    return [(dst, src) for src, dst in row_pairs(dx, dc)]


def from_chips(piece):
    return [piece] + [lax.ppermute(piece, "row", row_pairs(d, 0)) for d in (1, 2, 3)]


def with_other_core(pieces):
    quad = jnp.stack(pieces)
    return quad, lax.ppermute(quad, "row", row_pairs(0, 1))


def gather_near(piece):
    return with_other_core(from_chips(piece))


def sum_cores(own, other):
    other = lax.ppermute(other, "row", row_pairs(0, 1))
    return [(own[d].astype(F32) + other[d].astype(F32)).astype(BF16) for d in range(4)]


def to_chips(near):
    return [near[0]] + [lax.ppermute(near[d], "row", row_pairs_to(d, 0)) for d in (1, 3, 2)]


def col_pairs_to(dy, dz):
    return [(y * 4 + z, (y + dy) % 4 * 4 + (z + dz) % 4) for y in range(4) for z in range(4)]


def col_pairs(dy, dz):
    return [(dst, src) for src, dst in col_pairs_to(dy, dz)]


def from_col(piece, step):
    return [piece] + [lax.ppermute(piece, "col", col_pairs(*step(d))) for d in (1, 2, 3)]


def along_y(d):
    return (d, 0)


def along_z(d):
    return (0, d)


def along_col(parts, step):
    return [parts[0]] + [lax.ppermute(parts[d], "col", col_pairs_to(*step(d))) for d in (1, 3, 2)]


def send_all(piece, axis):
    copies = jnp.broadcast_to(piece, (lax.axis_size(axis),) + piece.shape)
    return lax.all_to_all(copies, axis, 0, 0)


def after(value, *others):
    return lax.optimization_barrier((value,) + others)[0]


def rope_tables():
    quarter = HD // 4
    frequency = np.float32(ROPE_BASE) ** (-np.arange(quarter, dtype=np.float32) / np.float32(quarter))
    place = np.arange(TOKENS)
    row = frequency[:, None] * (place // GRID).astype(np.float32)[None, :]
    col = frequency[:, None] * (place % GRID).astype(np.float32)[None, :]
    return np.stack([np.cos(row), np.sin(row), np.cos(col), np.sin(col)]).astype(np.float32)


def turn(v, table, sign):
    a, b, c, d = (v[k * 16 : (k + 1) * 16] for k in range(4))
    cr, sr, cc, sc = table[0], table[1] * sign, table[2], table[3] * sign
    return jnp.concatenate([a * cr - b * sr, a * sr + b * cr, c * cc - d * sc, c * sc + d * cc], 0)


def column_rms(v):
    return lax.rsqrt(jnp.mean(v * v, axis=0, keepdims=True) + EPSILON)


def normed(v, gain):
    return v * column_rms(v) * gain


def column_rms_back(v, u):
    scale = column_rms(v)
    return (u - v * (jnp.mean(u * v, axis=0, keepdims=True) * scale * scale)) * scale


def whole(shape):
    zeros = (0,) * len(shape)
    return pl.BlockSpec(shape, lambda *_: zeros, pipeline_mode=pl.Buffered(1))


def held():
    return pl.BlockSpec(memory_space=pltpu.VMEM)


def lane_block(rows, lanes):
    return pl.BlockSpec((rows, lanes), lambda t, *_: (0, t))


def row_block(rows, lanes):
    return pl.BlockSpec((rows, lanes), lambda t, *_: (t, 0))


def params(mib):
    return pltpu.CompilerParams(vmem_limit_bytes=mib * MIB, dimension_semantics=("arbitrary",))


def row_of_sums(v):
    return jnp.sum(v.T, axis=0, keepdims=True)


def attend_kernel(
    cap_ref, gate_ref, raw_ref, text_ref, gain_ref, table_ref, mixed_ref, lse_ref,
    q_ref, k_ref, v_ref, tk_ref, tv_ref,
):
    step = pl.program_id(0)
    heads = raw_ref.shape[1]

    @pl.when(step == 0)
    def _():
        table = table_ref[...]
        for h in range(heads):
            q = turn(normed(raw_ref[0, h], gain_ref[0, h]), table, 1.0).astype(BF16)
            q_ref[h] = q * jnp.asarray(0.125, BF16)
            k_ref[h] = turn(normed(raw_ref[1, h], gain_ref[1, h]), table, 1.0).T.astype(BF16)
            v_ref[h] = raw_ref[2, h].astype(BF16)
            tk_ref[h] = normed(text_ref[0, h], gain_ref[2, h]).T.astype(BF16)
            tv_ref[h] = text_ref[1, h].astype(BF16)

    slots = tk_ref.shape[1]
    mask = lax.broadcasted_iota(jnp.int32, (slots, QUERY_BLOCK), 0) < cap_ref[0]
    here = pl.ds(pl.multiple_of(step * QUERY_BLOCK, QUERY_BLOCK), QUERY_BLOCK)
    outs = []
    for h in range(heads):
        qb = q_ref[h, :, here]
        e = jnp.exp(dot(k_ref[h], qb, (1, 0)))
        total = jnp.sum(e, axis=0, keepdims=True)
        own = dot(v_ref[h], e.astype(BF16), (1, 0)) / total
        te = jnp.exp(jnp.where(mask, dot(tk_ref[h], qb, (1, 0)), MASKED))
        text_total = jnp.sum(te, axis=0, keepdims=True)
        text = dot(tv_ref[h], te.astype(BF16), (1, 0)) / text_total
        outs.append(own + gate_ref[h] * text)
        lse_ref[h, 0:1] = jnp.log(total)
        lse_ref[h, 1:2] = jnp.log(text_total)
    mixed_ref[...] = jnp.concatenate(outs, 0).astype(BF16)


def attend(raw, text_raw, gains, table, cap, gates):
    heads = raw.shape[1]
    slots = text_raw.shape[3]
    return pl.pallas_call(
        attend_kernel,
        grid_spec=pltpu.PrefetchScalarGridSpec(
            num_scalar_prefetch=2,
            grid=(TOKENS // QUERY_BLOCK,),
            in_specs=[
                whole((3, heads, HD, TOKENS)),
                whole((2, heads, HD, slots)),
                whole((3, heads, HD, 1)),
                whole((4, 16, TOKENS)),
            ],
            out_specs=[
                lane_block(heads * HD, QUERY_BLOCK),
                pl.BlockSpec((heads, 8, QUERY_BLOCK), lambda t, *_: (0, 0, t)),
            ],
            scratch_shapes=[
                pltpu.VMEM((heads, HD, TOKENS), BF16),
                pltpu.VMEM((heads, TOKENS, HD), BF16),
                pltpu.VMEM((heads, HD, TOKENS), BF16),
                pltpu.VMEM((heads, slots, HD), BF16),
                pltpu.VMEM((heads, HD, slots), BF16),
            ],
        ),
        out_shape=[
            jax.ShapeDtypeStruct((heads * HD, TOKENS), BF16),
            jax.ShapeDtypeStruct((heads, 8, TOKENS), F32),
        ],
        compiler_params=params(20),
        cost_estimate=LIGHT,
        name="attend",
    )(cap, gates, raw, text_raw, gains, table)


def text_back_kernel(
    cap_ref, gate_ref, q_raw_ref, text_ref, gain_ref, table_ref, lse_ref, grad_ref, caption_ref, held_ref,
    grads_ref, dq_ref, d_gain_ref, low_ref,
):
    del held_ref
    step = pl.program_id(0)
    heads, _, slots = low_ref.shape[1:]

    @pl.when(step == 0)
    def _():
        table = table_ref[...]
        mask = lax.broadcasted_iota(jnp.int32, (slots, TOKENS), 0) < cap_ref[0]
        for h in range(heads):
            gate = gate_ref[h]
            q = turn(normed(q_raw_ref[h], gain_ref[0, h]), table, 1.0).astype(BF16)
            q = q * jnp.asarray(0.125, BF16)
            tk = normed(text_ref[0, h], gain_ref[2, h]).astype(BF16)
            tv = text_ref[1, h].astype(BF16)
            g = grad_ref[h]
            tp = jnp.exp(jnp.where(mask, dot(tk, q, (0, 0)), MASKED) - lse_ref[h, 1:2])
            tpb = tp.astype(BF16)
            low_ref[1, h] = (dot(g, tpb, (1, 1)) * gate).astype(BF16)
            gate_terms = g.astype(F32) * dot(tv, tpb, (1, 0))
            tpd = tp * dot(tv, g, (0, 0)) * gate
            dts = (tpd - tp * jnp.sum(tpd, axis=0, keepdims=True)).astype(BF16)
            dq_ref[h] = dot(tk, dts, (1, 0))
            d_tk = dot(q, dts, (1, 1))
            values = text_ref[0, h]
            low_ref[0, h] = column_rms_back(values, d_tk * gain_ref[2, h]).astype(BF16)
            d_gain_ref[h, 0:1] = row_of_sums(values * column_rms(values) * d_tk)
            d_gain_ref[h, 1:2] = row_of_sums(gate_terms)

    d_text = low_ref[...].reshape(2 * heads * HD, slots)
    rows = grads_ref.shape[1]
    for k in range(grads_ref.shape[0]):
        grads_ref[k] = dot(caption_ref[:, k * rows : (k + 1) * rows], d_text, (0, 1)).astype(BF16)


def text_back(raw, text_raw, gains, table, lse, grads, cap, gates, caption, held):
    heads = raw.shape[1]
    slots = text_raw.shape[3]
    rows = caption.shape[1] // COLS
    lanes = 2 * heads * HD
    return pl.pallas_call(
        text_back_kernel,
        grid_spec=pltpu.PrefetchScalarGridSpec(
            num_scalar_prefetch=2,
            grid=(4,),
            in_specs=[
                pl.BlockSpec((None, heads, HD, TOKENS), lambda t, *_: (0, 0, 0, 0)),
                whole(text_raw.shape),
                whole(gains.shape),
                whole(table.shape),
                whole(lse.shape),
                whole(grads.shape),
                pl.BlockSpec((slots, 4 * rows), lambda t, *_: (0, t)),
                pl.BlockSpec(memory_space=pl.ANY),
            ],
            out_specs=[
                pl.BlockSpec((4, rows, lanes), lambda t, *_: (t, 0, 0)),
                pl.BlockSpec((heads, HD, TOKENS), lambda t, *_: (0, 0, 0)),
                pl.BlockSpec((heads, 8, HD), lambda t, *_: (0, 0, 0)),
            ],
            scratch_shapes=[pltpu.VMEM((2, heads, HD, slots), BF16)],
        ),
        out_shape=[
            jax.ShapeDtypeStruct(held.shape, BF16),
            jax.ShapeDtypeStruct((heads, HD, TOKENS), F32),
            jax.ShapeDtypeStruct((heads, 8, HD), F32),
        ],
        input_output_aliases={9: 0},
        compiler_params=params(58),
        cost_estimate=LIGHT,
        name="text_back",
    )(cap, gates, raw, text_raw, gains, table, lse, grads, caption, held)


def attend_back_kernel(
    raw_ref, gain_ref, table_ref, lse_ref, grad_ref, dq_text_ref,
    d_raw_ref, d_gain_ref, dv_ref, dk_ref, dq_ref,
):
    table = table_ref[...]
    q = turn(normed(raw_ref[0], gain_ref[0]), table, 1.0).astype(BF16) * jnp.asarray(0.125, BF16)
    k = turn(normed(raw_ref[1], gain_ref[1]), table, 1.0)
    k, k_turned = k.astype(BF16), k.T.astype(BF16)
    v_turned = raw_ref[2].T.astype(BF16)
    for first in range(0, TOKENS, QUERY_BLOCK):
        here = slice(first, first + QUERY_BLOCK)
        qb = q[:, here]
        gb = grad_ref[:, here]
        p = jnp.exp(dot(k_turned, qb, (1, 0)) - lse_ref[0:1, here])
        dv = dot(gb, p.astype(BF16), (1, 1))
        pd = p * dot(v_turned, gb, (1, 0))
        ds = (pd - p * jnp.sum(pd, axis=0, keepdims=True)).astype(BF16)
        dq_ref[:, here] = dot(k, ds, (1, 0)) + dq_text_ref[:, here]
        dk = dot(qb, ds, (1, 1))
        if first == 0:
            dv_ref[...] = dv
            dk_ref[...] = dk
        else:
            dv_ref[...] += dv
            dk_ref[...] += dk

    def raw_back(which, d_turned):
        spun = turn(d_turned.astype(BF16).astype(F32), table, -1.0)
        values = raw_ref[which]
        d_raw_ref[which] = column_rms_back(values, spun * gain_ref[which]).astype(BF16)
        d_gain_ref[which : which + 1] = row_of_sums(values * column_rms(values) * spun)

    raw_back(0, dq_ref[...] * 0.125)
    raw_back(1, dk_ref[...])
    d_raw_ref[2] = dv_ref[...].astype(BF16)


def attend_back(raw, gains, table, lse, grads, dq_text):
    heads = raw.shape[1]
    return pl.pallas_call(
        attend_back_kernel,
        grid=(heads,),
        in_specs=[
            pl.BlockSpec((3, None, HD, TOKENS), lambda h: (0, h, 0, 0)),
            pl.BlockSpec((3, None, HD, 1), lambda h: (0, h, 0, 0)),
            pl.BlockSpec((4, 16, TOKENS), lambda h: (0, 0, 0)),
            pl.BlockSpec((None, 8, TOKENS), lambda h: (h, 0, 0)),
            pl.BlockSpec((None, HD, TOKENS), lambda h: (h, 0, 0)),
            pl.BlockSpec((None, HD, TOKENS), lambda h: (h, 0, 0)),
        ],
        out_specs=[
            pl.BlockSpec((3, None, HD, TOKENS), lambda h: (0, h, 0, 0)),
            pl.BlockSpec((None, 8, HD), lambda h: (h, 0, 0)),
        ],
        scratch_shapes=[pltpu.VMEM((HD, TOKENS), F32) for _ in range(3)],
        out_shape=[
            jax.ShapeDtypeStruct((3, heads, HD, TOKENS), BF16),
            jax.ShapeDtypeStruct((heads, 8, HD), F32),
        ],
        compiler_params=params(58),
        cost_estimate=LIGHT,
        name="attend_back",
    )(raw, gains, table, lse, grads, dq_text)


def tile_places(chunk_first):
    r, c, k = np.meshgrid(np.arange(ROWS), np.arange(COLS), np.arange(8), indexing="ij")
    token = r * BLOCK + (k // 2) * GRID + c * 2 + k % 2
    source = (k * ROWS + r) * COLS + c if chunk_first else (r * COLS + c) * 8 + k
    places = np.zeros((TOKENS, TOKENS), np.float32)
    places[source.ravel(), token.ravel()] = 1.0
    return jnp.asarray(places, BF16)


def grid_shift(field, di, dj):
    step = di * GRID + dj
    moved = pltpu.roll(field, (-step) % TOKENS, 1) if step else field
    place = lax.broadcasted_iota(jnp.int32, field.shape, 1)
    row = place // GRID + di
    col = place % GRID + dj
    inside = (row >= 0) & (row < GRID) & (col >= 0) & (col < GRID)
    return jnp.where(inside, moved, 0.0)


def image_kernel(packed_ref, place_ref, patch_ref, cot_ref):
    for which, sign, out_ref in ((0, 1, patch_ref), (1, -1, cot_ref)):
        lanes = slice(which * 128, (which + 1) * 128)
        tiles = jnp.concatenate([packed_ref[r, :, lanes] for r in range(ROWS)], 0)
        turned = tiles.astype(F32).T
        chunks = jnp.concatenate([turned[k * 16 : (k + 1) * 16] for k in range(8)], 1)
        image = dot(chunks.astype(BF16), place_ref[...], (1, 0))
        for a in range(3):
            for b in range(3):
                first = (a * 3 + b) * 16
                out_ref[first : first + 16] = grid_shift(
                    image, sign * (a - 1), sign * (b - 1)
                ).astype(BF16)


def image_taps(packed):
    out = jax.ShapeDtypeStruct((144, TOKENS), BF16)
    return pl.pallas_call(
        image_kernel,
        out_shape=[out, out],
        compiler_params=pltpu.CompilerParams(vmem_limit_bytes=12 * MIB),
        cost_estimate=LIGHT,
        name="image_taps",
    )(packed, tile_places(True))


def field_of(taps, place, sign):
    total = jnp.zeros((16, TOKENS), F32)
    for a in range(3):
        for b in range(3):
            first = (a * 3 + b) * 16
            total = total + grid_shift(taps[first : first + 16], sign * (a - 1), sign * (b - 1))
    tiles = dot(total.astype(BF16), place, (1, 1))
    return [tiles[:, r * BLOCK : (r + 1) * BLOCK] for r in range(ROWS)]


def row_rms(v):
    return lax.rsqrt(jnp.mean(v * v, axis=-1, keepdims=True) + EPSILON)


def row_rms_back(v, scale, u):
    return (u - v * (jnp.mean(u * v, axis=-1, keepdims=True) * scale * scale)) * scale


def unpack_kernel(at_ref, *refs):
    piece_refs, (joined_ref, out_ref, turn_ref) = refs[:4], refs[4:]
    part = piece_refs[0].shape[1] // 2
    local_width = piece_refs[0].shape[2] // 2
    for dz in range(4):
        for dy in range(4):
            c = lax.rem(at_ref[2] + dy, 4) * 4 + lax.rem(at_ref[3] + dz, 4)
            rows = pl.ds(pl.multiple_of(c * part, part), part)
            piece = piece_refs[dz][dy]
            joined_ref[0, rows, :] = piece[:part, :local_width]
            joined_ref[1, rows, :] = piece[:part, local_width:]
            joined_ref[2, rows, :] = piece[part:, :local_width]
            turn_ref[rows, :] = piece[part:, local_width:]
    out_ref[...] = turn_ref[...].T


def unpack_head(at, pieces):
    _, rows, lanes = pieces[0].shape
    width, local_width = COLS * rows // 2, lanes // 2
    return pl.pallas_call(
        unpack_kernel,
        grid_spec=pltpu.PrefetchScalarGridSpec(
            num_scalar_prefetch=1,
            grid=(1,),
            in_specs=[whole(pieces[0].shape)] * 4,
            out_specs=[
                pl.BlockSpec((3, width, local_width), lambda t, at: (0, 0, 0)),
                pl.BlockSpec((local_width, width), lambda t, at: (0, 0)),
            ],
            scratch_shapes=[pltpu.VMEM((width, local_width), BF16)],
        ),
        out_shape=[
            jax.ShapeDtypeStruct((3, width, local_width), BF16),
            jax.ShapeDtypeStruct((local_width, width), BF16),
        ],
        compiler_params=params(14),
        cost_estimate=LIGHT,
        name="unpack_head",
    )(at, *pieces)


def text_kernel(at_ref, p0_ref, p1_ref, p2_ref, p3_ref, caption_ref, raw_ref):
    rows = p0_ref.shape[1]
    total = 0.0
    for dy, ref in enumerate((p0_ref, p1_ref, p2_ref, p3_ref)):
        for dz in range(4):
            c = lax.rem(at_ref[2] + dy, 4) * 4 + lax.rem(at_ref[3] + dz, 4)
            lanes = pl.ds(pl.multiple_of(c * rows, rows), rows)
            total = total + dot(ref[dz], caption_ref[:, lanes], (0, 1))
    raw_ref[...] = total


def text_project(at, pieces, caption):
    lanes = pieces[0].shape[2]
    slots = caption.shape[0]
    return pl.pallas_call(
        text_kernel,
        grid_spec=pltpu.PrefetchScalarGridSpec(
            num_scalar_prefetch=1,
            grid=(1,),
            in_specs=[whole(pieces[0].shape)] * 4 + [whole(caption.shape)],
            out_specs=pl.BlockSpec((lanes, slots), lambda t, at: (0, 0)),
        ),
        out_shape=jax.ShapeDtypeStruct((lanes, slots), F32),
        compiler_params=params(16),
        cost_estimate=LIGHT,
        name="text_project",
    )(at, *pieces, caption)


def qkv_kernel(patch_ref, embed_ref, vec_ref, weight_ref, raw_ref):
    x = dot(patch_ref[...], embed_ref[...], (0, 0))
    h = (x * row_rms(x) * vec_ref[0:1]).astype(BF16)
    for s in range(3):
        raw_ref[s] = dot(h, weight_ref[s], (1, 0)).T


def qkv_project(patches, embed, vec, weight):
    part = weight.shape[2]
    return pl.pallas_call(
        qkv_kernel,
        grid=(TOKENS // PAIR,),
        in_specs=[lane_block(144, PAIR), whole(embed.shape), whole(vec.shape), whole(weight.shape)],
        out_specs=pl.BlockSpec((3, part, PAIR), lambda t: (0, 0, t)),
        out_shape=jax.ShapeDtypeStruct((3, part, TOKENS), F32),
        compiler_params=params(16),
        cost_estimate=LIGHT,
        name="qkv_project",
    )(patches, embed, vec, weight)


def joined(ref):
    return ref[...].reshape(-1, ref.shape[2])


def halves(core, first, second):
    return jnp.where(core == 0, first, second)


def forward_kernel(
    at_ref, near_ref, far_ref, out_near_ref, out_far_ref, patch_ref, embed_ref, vec_ref, ffn_ref,
    attn_ref, second_ref, gate_up_ref, hidden_ref, own_ref, other_ref,
):
    core = at_ref[1]
    hidden_width = hidden_ref.shape[1]
    x = dot(patch_ref[...], embed_ref[...], (0, 0))
    attn = dot(joined(near_ref), joined(out_near_ref), (0, 0))
    attn = attn + dot(joined(far_ref), joined(out_far_ref), (0, 0))
    attn_ref[...] = attn.astype(BF16)
    mid = x + vec_ref[1:2] * (attn * row_rms(attn))
    second = (mid * row_rms(mid) * vec_ref[2:3]).astype(BF16)
    second_ref[...] = second
    gate_up = dot(second, ffn_ref[:, : 2 * hidden_width], (1, 0))
    gate_up_ref[...] = gate_up.astype(BF16)
    gate = gate_up[:, :hidden_width]
    hidden = (gate * jax.nn.sigmoid(gate) * gate_up[:, hidden_width:]).astype(BF16)
    hidden_ref[...] = hidden
    part = dot(hidden, ffn_ref[:, 2 * hidden_width :], (1, 1)).astype(BF16)
    own_ref[0] = halves(core, part[:BLOCK], part[BLOCK:])
    other_ref[0] = halves(core, part[BLOCK:], part[:BLOCK])


def forward(at, mixed, out_whole, patches, embed, vec, ffn):
    width = embed.shape[1]
    part = mixed[0].shape[1]
    hidden_width = ffn.shape[1] // 3
    by_chip = pl.BlockSpec((1, BLOCK, width), lambda t, at: ((t - at[0] + 4) % 4, 0, 0))
    return pl.pallas_call(
        forward_kernel,
        grid_spec=pltpu.PrefetchScalarGridSpec(
            num_scalar_prefetch=1,
            grid=(4,),
            in_specs=[
                pl.BlockSpec((4, part, PAIR), lambda t, at: (0, 0, t)),
                pl.BlockSpec((4, part, PAIR), lambda t, at: (0, 0, t)),
                whole((4, part, width)),
                whole((4, part, width)),
                lane_block(144, PAIR),
                whole(embed.shape),
                whole(vec.shape),
                whole(ffn.shape),
            ],
            out_specs=[
                row_block(PAIR, width),
                row_block(PAIR, width),
                row_block(PAIR, 2 * hidden_width),
                row_block(PAIR, hidden_width),
                by_chip,
                by_chip,
            ],
        ),
        out_shape=[
            jax.ShapeDtypeStruct((TOKENS, width), BF16),
            jax.ShapeDtypeStruct((TOKENS, width), BF16),
            jax.ShapeDtypeStruct((TOKENS, 2 * hidden_width), BF16),
            jax.ShapeDtypeStruct((TOKENS, hidden_width), BF16),
            jax.ShapeDtypeStruct((4, BLOCK, width), BF16),
            jax.ShapeDtypeStruct((4, BLOCK, width), BF16),
        ],
        compiler_params=params(56),
        cost_estimate=LIGHT,
        name="forward",
    )(at, *mixed, *out_whole, patches, embed, vec, ffn)


def own_grad_kernel(p0_ref, p1_ref, p2_ref, p3_ref, cot_ref, unpatch_ref, vec_ref, d_ffn_ref, ffn_ref):
    ffn = sum(p[...].astype(F32) for p in (p0_ref, p1_ref, p2_ref, p3_ref))
    ffn_ref[...] = ffn
    d_last = dot(cot_ref[...], unpatch_ref[...], (0, 0))
    d_ffn_ref[...] = row_rms_back(ffn, row_rms(ffn), vec_ref[3:4] * d_last).astype(BF16)


def own_grad(pieces, cot_own, unpatch, vec):
    shape = (BLOCK, unpatch.shape[1])
    return pl.pallas_call(
        own_grad_kernel,
        out_shape=[jax.ShapeDtypeStruct(shape, BF16), jax.ShapeDtypeStruct(shape, F32)],
        compiler_params=pltpu.CompilerParams(vmem_limit_bytes=58 * MIB),
        cost_estimate=LIGHT,
        name="own_grad",
    )(*pieces, cot_own, unpatch, vec)


def own_kernel(
    at_ref, ffn_ref, attn_ref, patch_ref, cot_ref, embed_ref, unpatch_ref, vec_ref, place_ref,
    field_ref, unpatch_sum_ref, sums_ref, taps_ref,
):
    ffn = ffn_ref[...]
    d_last = dot(cot_ref[...], unpatch_ref[...], (0, 0))
    normed_ffn = ffn * row_rms(ffn)
    sums_ref[...] = jnp.broadcast_to(
        jnp.sum(normed_ffn * d_last, axis=0, keepdims=True), sums_ref.shape
    )
    attn = attn_ref[...].astype(F32)
    x = dot(patch_ref[...], embed_ref[...], (0, 0))
    last = (x + vec_ref[1:2] * (attn * row_rms(attn)) + vec_ref[3:4] * normed_ffn).astype(BF16)
    unpatch_sum_ref[...] = dot(cot_ref[...], last, (1, 0))
    taps_ref[...] = jnp.zeros_like(taps_ref)
    here = pl.multiple_of((2 * at_ref[0] + at_ref[1]) * BLOCK, BLOCK)
    taps_ref[:, pl.ds(here, BLOCK)] = dot(unpatch_ref[...], last, (1, 1))
    for r, tile in enumerate(field_of(taps_ref[...], place_ref[...], 1)):
        field_ref[r] = tile


def own_block(at, ffn, attn, patches, cot_taps, embed, unpatch, vec, place):
    width = embed.shape[1]
    lanes = pl.BlockSpec((144, BLOCK), lambda t, at: (0, 2 * at[0] + at[1]))
    return pl.pallas_call(
        own_kernel,
        grid_spec=pltpu.PrefetchScalarGridSpec(
            num_scalar_prefetch=1,
            grid=(1,),
            in_specs=[
                whole((BLOCK, width)),
                pl.BlockSpec((BLOCK, width), lambda t, at: (2 * at[0] + at[1], 0)),
                lanes,
                lanes,
                whole(embed.shape),
                whole(unpatch.shape),
                whole(vec.shape),
                whole(place.shape),
            ],
            out_specs=[
                pl.BlockSpec((ROWS, 16, BLOCK), lambda t, at: (0, 0, 0)),
                pl.BlockSpec((144, width), lambda t, at: (0, 0)),
                pl.BlockSpec((8, width), lambda t, at: (0, 0)),
            ],
            scratch_shapes=[pltpu.VMEM((144, TOKENS), F32)],
        ),
        out_shape=[
            jax.ShapeDtypeStruct((ROWS, 16, BLOCK), F32),
            jax.ShapeDtypeStruct((144, width), F32),
            jax.ShapeDtypeStruct((8, width), F32),
        ],
        compiler_params=params(14),
        cost_estimate=LIGHT,
        name="own_block",
    )(at, ffn, attn, patches, cot_taps, embed, unpatch, vec, place)


def backward_kernel(
    at_ref, own_ref, other_ref, ffn_ref, out_near_ref, out_far_ref, gate_up_ref, attn_ref,
    patch_ref, embed_ref, cot_ref, unpatch_ref, vec_ref,
    d_ffn_ref, d_gate_up_ref, d_attn_ref, d_mid_ref, mixed_own_ref, mixed_other_ref, sums_ref,
):
    step = pl.program_id(0)
    chip, core = at_ref[0], at_ref[1]
    hidden_width = d_gate_up_ref.shape[1] // 2
    own, other = own_ref[0], other_ref[0]
    d_ffn = jnp.concatenate([halves(core, own, other), halves(core, other, own)], 0)
    d_ffn_ref[...] = d_ffn
    d_hidden = dot(d_ffn, ffn_ref[:, 2 * hidden_width :], (1, 0))
    gate = gate_up_ref[:, :hidden_width].astype(F32)
    up = gate_up_ref[:, hidden_width:].astype(F32)
    sigma = jax.nn.sigmoid(gate)
    silu = gate * sigma
    d_gate = d_hidden * up * (sigma + silu * (1.0 - sigma))
    d_gate_up = jnp.concatenate([d_gate.astype(BF16), (d_hidden * silu).astype(BF16)], 1)
    d_gate_up_ref[...] = d_gate_up
    d_second = dot(d_gate_up, ffn_ref[:, : 2 * hidden_width], (1, 1))

    x = dot(patch_ref[...], embed_ref[...], (0, 0))
    attn = attn_ref[...].astype(F32)
    attn_scale = row_rms(attn)
    attn_normed = attn * attn_scale
    mid = x + vec_ref[1:2] * attn_normed
    mid_scale = row_rms(mid)
    mid_sum = jnp.sum(mid * mid_scale * d_second, axis=0, keepdims=True)
    d_last = dot(cot_ref[...], unpatch_ref[...], (0, 0))
    place = lax.broadcasted_iota(jnp.int32, (PAIR, 1), 0) // BLOCK
    mine = (place == core) & (step == chip)
    d_mid = row_rms_back(mid, mid_scale, vec_ref[2:3] * d_second) + jnp.where(mine, d_last, 0.0)
    d_mid_ref[...] = d_mid.astype(BF16)
    attn_sum = jnp.sum(attn_normed * d_mid, axis=0, keepdims=True)
    d_attn = row_rms_back(attn, attn_scale, vec_ref[1:2] * d_mid).astype(BF16)
    d_attn_ref[...] = d_attn
    for weight_ref, part_ref in ((out_near_ref, mixed_own_ref), (out_far_ref, mixed_other_ref)):
        part_ref[...] = dot(joined(weight_ref), d_attn, (1, 1)).astype(BF16).reshape(part_ref.shape)

    @pl.when(step == 0)
    def _():
        sums_ref[...] = jnp.zeros_like(sums_ref)

    sums_ref[0:1] += mid_sum
    sums_ref[1:2] += attn_sum


def backward(at, d_ffn, ffn, out_whole, gate_up, attn, patches, embed, cot_taps, unpatch, vec):
    width = embed.shape[1]
    part = out_whole[0].shape[1]
    hidden_width = ffn.shape[1] // 3
    by_chip = pl.BlockSpec((1, BLOCK, width), lambda t, at: ((t - at[0] + 4) % 4, 0, 0))
    parts = pl.BlockSpec((4, part, PAIR), lambda t, at: (0, 0, t))
    return pl.pallas_call(
        backward_kernel,
        grid_spec=pltpu.PrefetchScalarGridSpec(
            num_scalar_prefetch=1,
            grid=(4,),
            in_specs=[
                by_chip,
                by_chip,
                held(),
                held(),
                held(),
                row_block(PAIR, 2 * hidden_width),
                row_block(PAIR, width),
                lane_block(144, PAIR),
                whole(embed.shape),
                lane_block(144, PAIR),
                whole(unpatch.shape),
                whole(vec.shape),
            ],
            out_specs=[
                row_block(PAIR, width),
                row_block(PAIR, 2 * hidden_width),
                row_block(PAIR, width),
                row_block(PAIR, width),
                parts,
                parts,
                pl.BlockSpec((8, width), lambda t, at: (0, 0)),
            ],
        ),
        out_shape=[
            jax.ShapeDtypeStruct((TOKENS, width), BF16),
            jax.ShapeDtypeStruct((TOKENS, 2 * hidden_width), BF16),
            jax.ShapeDtypeStruct((TOKENS, width), BF16),
            jax.ShapeDtypeStruct((TOKENS, width), BF16),
            jax.ShapeDtypeStruct((4, part, TOKENS), BF16),
            jax.ShapeDtypeStruct((4, part, TOKENS), BF16),
            jax.ShapeDtypeStruct((8, width), F32),
        ],
        compiler_params=params(32),
        cost_estimate=LIGHT,
        name="backward",
    )(at, *d_ffn, ffn, *out_whole, gate_up, attn, patches, embed, cot_taps, unpatch, vec)


def weight_kernel(
    second_ref, d_gate_up_ref, d_ffn_ref, hidden_ref, near_ref, far_ref, d_attn_ref,
    grads_ref, out_near_ref, out_far_ref,
):
    step = pl.program_id(0)
    chunk, _, lanes = grads_ref.shape[0] // 4, *grads_ref.shape[1:]
    part = second_ref.shape[1] // chunk
    rows = jnp.concatenate(
        [
            dot(second_ref[...], d_gate_up_ref[...], (0, 0)).astype(BF16),
            dot(d_ffn_ref[...], hidden_ref[...], (0, 0)).astype(BF16),
        ],
        1,
    )
    groups = rows.shape[1] // lanes
    first = grads_ref.shape[1] - groups * part
    for c in range(chunk):
        for g in range(groups):
            grads_ref[step * chunk + c, first + g * part : first + (g + 1) * part] = rows[
                c * part : (c + 1) * part, g * lanes : (g + 1) * lanes
            ]
    out_near_ref[0] = dot(near_ref[0], d_attn_ref[...], (1, 0)).astype(BF16)
    out_far_ref[0] = dot(far_ref[0], d_attn_ref[...], (1, 0)).astype(BF16)


def weight_grads(second, d_gate_up, d_ffn, hidden, mixed, d_attn, text_rows):
    width = second.shape[1]
    heads_width = mixed[0].shape[1]
    lanes = 2 * heads_width
    grads = (COLS, text_rows + width // COLS * 3 * hidden.shape[1] // lanes, lanes)
    pieces = pl.BlockSpec((1, heads_width, TOKENS), lambda t: (t, 0, 0))
    out_piece = pl.BlockSpec((1, heads_width, width), lambda t: (t, 0, 0))
    out_shape = jax.ShapeDtypeStruct((4, heads_width, width), BF16)
    return pl.pallas_call(
        weight_kernel,
        grid=(4,),
        in_specs=[
            lane_block(TOKENS, width // 4),
            whole(d_gate_up.shape),
            lane_block(TOKENS, width // 4),
            whole(hidden.shape),
            pieces,
            pieces,
            whole(d_attn.shape),
        ],
        out_specs=[pl.BlockSpec(grads, lambda t: (0, 0, 0)), out_piece, out_piece],
        out_shape=[jax.ShapeDtypeStruct(grads, BF16), out_shape, out_shape],
        compiler_params=params(40),
        cost_estimate=LIGHT,
        name="weight_grads",
    )(second, d_gate_up, d_ffn, hidden, *mixed, d_attn)


def first_kernel(
    at_ref, gate_ref, patch_ref, embed_ref, vec_ref, weight_ref, d_raw_ref, d_mid_ref, place_ref, out_sum_ref,
    unpatch_sum_ref, back_sums_ref, own_sums_ref, head_ref, text_head_ref, gains_ref, mod_ref, activation_ref,
    own_pack_ref, other_pack_ref, p0_ref, p1_ref, p2_ref, p3_ref,
    taps_acc, embed_acc, first_acc, shared_acc, qkv_acc, turned_acc,
):
    step = pl.program_id(0)
    last = pl.num_programs(0) - 1
    x = dot(patch_ref[...], embed_ref[...], (0, 0))
    scale = row_rms(x)
    x_normed = x * scale
    h = (x_normed * vec_ref[0:1]).astype(BF16)
    d_h = dot(d_raw_ref[0], weight_ref[0], (0, 1))
    for s in (1, 2):
        d_h = d_h + dot(d_raw_ref[s], weight_ref[s], (0, 1))

    @pl.when(step == 0)
    def _():
        qkv_acc[...] = jnp.zeros_like(qkv_acc)
        embed_acc[...] = jnp.zeros_like(embed_acc)
        first_acc[...] = jnp.zeros_like(first_acc)

    qkv_acc[...] += dot(joined(d_raw_ref), h, (1, 0)).reshape(qkv_acc.shape)
    first_acc[0:1] += jnp.sum(x_normed * d_h, axis=0, keepdims=True)
    d_first = (d_mid_ref[...].astype(F32) + row_rms_back(x, scale, vec_ref[0:1] * d_h)).astype(BF16)
    embed_acc[...] += dot(patch_ref[...], d_first, (1, 0))
    here = pl.ds(pl.multiple_of(step * PAIR, PAIR), PAIR)
    taps_acc[:, here] = dot(embed_ref[...], d_first, (1, 1))

    @pl.when(step == last)
    def _():
        part = p0_ref.shape[1] // 2
        for s in range(4):
            turned_acc[s] = (qkv_acc[s] if s < 3 else out_sum_ref[...]).T.astype(BF16)
        for dz, ref in enumerate((p0_ref, p1_ref, p2_ref, p3_ref)):
            z = lax.rem(at_ref[3] + dz, 4)
            for y in range(4):
                dy = lax.rem(y - at_ref[2] + 4, 4)
                first = pl.multiple_of((y * 4 + z) * part, part)
                pieces = [turned_acc[s, pl.ds(first, part), :] for s in range(4)]
                for k in range(2):
                    ref[dy, k * part : (k + 1) * part] = jnp.concatenate(
                        pieces[2 * k : 2 * k + 2], 1
                    )
        terms = jnp.concatenate(
            [first_acc[0:1], back_sums_ref[1:2], back_sums_ref[0:1], own_sums_ref[0:1]], 0
        )
        gates = [jnp.tanh(mod_ref[k : k + 1]) for k in (1, 3)]
        into = jnp.concatenate(
            [1.0 + mod_ref[0:1], gates[0], 1.0 + mod_ref[2:3], gates[1]], 0
        )
        d_gains = terms * into
        slope = jnp.concatenate(
            [jnp.ones_like(gates[0]), 1.0 - gates[0] * gates[0]] * 1
            + [jnp.ones_like(gates[0]), 1.0 - gates[1] * gates[1]],
            0,
        )
        d_modulation = terms * gains_ref[0:4] * slope
        heads = head_ref.shape[0]
        width = d_gains.shape[1]
        rows = [head_ref[h] for h in range(heads)], [text_head_ref[h] for h in range(heads)]
        own = jnp.concatenate(
            [
                jnp.concatenate([r[0:2] for r in rows[0]], 1),
                jnp.concatenate([r[0:1] for r in rows[1]], 1),
                jnp.zeros((5, heads * HD), F32),
            ],
            0,
        )
        own = jnp.concatenate([own, jnp.zeros((8, width - heads * HD), F32)], 1)
        row_at = 2 * at_ref[0] + at_ref[1]
        own = pltpu.roll(own, row_at * (heads * HD), 1)
        lane = lax.broadcasted_iota(jnp.int32, (1, width), 1)
        gate_row = jnp.zeros((1, width), F32)
        for h in range(heads):
            total = jnp.sum(rows[1][h][1:2], axis=1, keepdims=True)
            total = total * (1.0 - gate_ref[h] * gate_ref[h])
            gate_row = gate_row + jnp.where(lane == row_at * heads + h, total, 0.0)
        small = jnp.concatenate(
            [d_gains, own[0:3], gate_row, jnp.zeros((24, width), F32)], 0
        )
        for tile in range(12):
            lanes = slice(tile * 128, (tile + 1) * 128)
            first = tile * SHARED
            shared_acc[first : first + 144] = embed_acc[:, lanes].astype(BF16)
            shared_acc[first + 144 : first + 288] = unpatch_sum_ref[:, lanes].astype(BF16)
            shared_acc[first + 288 : first + SHARED] = small[:, lanes].astype(BF16)
        shared_acc[12 * SHARED :] = jnp.zeros((8 * CHUNK - 12 * SHARED, 128), BF16)
        latent = field_of(taps_acc[...], place_ref[...], -1)
        rows = [
            d_modulation[q : q + 1, tile * 128 : (tile + 1) * 128]
            for q in range(4)
            for tile in range(12)
        ]
        for r in range(ROWS):
            ahead = lax.rem(r // 2 - at_ref[0] + 4, 4)
            mods = jnp.concatenate(rows[6 * r : 6 * r + 6] + [jnp.zeros((10, 128), F32)], 0)
            piece = jnp.concatenate(
                [
                    shared_acc[r * CHUNK : (r + 1) * CHUNK],
                    activation_ref[r].astype(BF16),
                    latent[r].astype(BF16),
                    mods.astype(BF16),
                ],
                0,
            )

            @pl.when(at_ref[1] == r % 2)
            def _():
                own_pack_ref[ahead] = piece

            @pl.when(at_ref[1] != r % 2)
            def _():
                other_pack_ref[ahead] = piece


def first_back(
    at, gates, patches, embed, vec, weight, d_raw, d_mid, place, out_sum, unpatch_sum, back_sums, own_sums,
    head, text_head, gains, modulation, activation,
):
    width = embed.shape[1]
    part = weight.shape[2]
    pack = (4, CHUNK + 48, 128)
    grads = (4, 2 * width // COLS, 2 * part)
    rest = (place, out_sum, unpatch_sum, back_sums, own_sums, head, text_head, gains, modulation, activation)
    return pl.pallas_call(
        first_kernel,
        grid_spec=pltpu.PrefetchScalarGridSpec(
            num_scalar_prefetch=2,
            grid=(TOKENS // PAIR,),
            in_specs=[
                lane_block(144, PAIR),
                whole(embed.shape),
                whole(vec.shape),
                held(),
                pl.BlockSpec((3, part, PAIR), lambda t, *_: (0, 0, t)),
                row_block(PAIR, width),
            ]
            + [held()]
            + [whole(value.shape) for value in rest[1:]],
            out_specs=[pl.BlockSpec(pack, lambda t, *_: (0, 0, 0))] * 2
            + [pl.BlockSpec(grads, lambda t, *_: (0, 0, 0))] * 4,
            scratch_shapes=[
                pltpu.VMEM((144, TOKENS), F32),
                pltpu.VMEM((144, width), F32),
                pltpu.VMEM((8, width), F32),
                pltpu.VMEM((8 * CHUNK, 128), BF16),
                pltpu.VMEM((3, part, width), F32),
                pltpu.VMEM((4, width, part), BF16),
            ],
        ),
        out_shape=[jax.ShapeDtypeStruct(pack, BF16)] * 2 + [jax.ShapeDtypeStruct(grads, BF16)] * 4,
        compiler_params=params(58),
        cost_estimate=LIGHT,
        name="first_back",
    )(at, gates, patches, embed, vec, weight, d_raw, d_mid, *rest)


def local(
    latent, condition, caption, cap_len, cotangent, embed_weight, modulate_weight, norm_gains,
    cross_gate, qkv_weight, text_kv_weight, out_weight, gate_up_weight, down_weight, unpatch_weight,
):
    images, _, _, channels = latent.shape
    width = embed_weight.shape[3]
    local_width = qkv_weight.shape[2]
    heads = local_width // HD
    hidden_width = down_weight.shape[0]
    taps = 9 * channels
    row_at = lax.axis_index("row")
    col_at = lax.axis_index("col")
    at = jnp.stack([row_at // 2, row_at % 2, col_at // 4, col_at % 4]).astype(jnp.int32)
    tile = latent.shape[1] * latent.shape[2] * channels

    cond_low = jax.nn.silu(condition.astype(F32)).astype(BF16)
    mod_piece = jnp.dot(cond_low, modulate_weight, preferred_element_type=F32)
    mod_columns = mod_piece.shape[1]
    mod_high = mod_piece.astype(BF16)
    mod_low = (mod_piece - mod_high.astype(F32)).astype(BF16)

    packed = jnp.concatenate(
        [latent.reshape(images, tile), cotangent.reshape(images, tile), mod_high, mod_low], axis=1
    )
    packed = jnp.pad(packed, ((0, 0), (0, 2 * local_width - packed.shape[1])))

    head_piece = jnp.concatenate(
        [
            jnp.concatenate([qkv_weight[0], qkv_weight[1]], axis=1),
            jnp.concatenate([qkv_weight[2], out_weight.T], axis=1),
        ]
    )
    text_piece = jnp.concatenate([text_kv_weight[0], text_kv_weight[1]], axis=1)
    head_pieces = from_col(head_piece, along_y)
    text_pieces = from_col(text_piece, along_z)
    packed = lax.all_to_all(packed, "col", 0, 0, tiled=True)
    packed, *reached = lax.optimization_barrier((packed, *head_pieces, *text_pieces))
    head_pieces, text_pieces = reached[:4], reached[4:]
    packed = send_all(packed, "row")
    patches, cot_taps = image_taps(packed)
    head_pieces = from_col(jnp.stack(head_pieces), along_z)
    text_own = jnp.stack(text_pieces)
    text_beside = [lax.ppermute(text_own, "col", col_pairs(d, 0)) for d in (1, 3)]
    ffn_piece = jnp.concatenate([gate_up_weight[0], gate_up_weight[1], down_weight.T], axis=1)
    ffn_piece, patches, text_own, next_text, last_text, *head_pieces = lax.optimization_barrier(
        (ffn_piece, patches, text_own, *text_beside, *head_pieces)
    )
    ffn_whole = lax.all_gather(ffn_piece, "col", axis=0, tiled=True)
    text_apart = lax.ppermute(text_own, "col", col_pairs(2, 0))
    text_pieces = [text_own, next_text, text_apart, last_text]
    qkv_whole, out_rows = unpack_head(at, head_pieces)
    out_pieces = from_chips(out_rows)

    mod_at = 2 * tile
    modulation = packed[:, :, mod_at : mod_at + mod_columns].astype(F32)
    modulation = modulation + packed[:, :, mod_at + mod_columns : mod_at + 2 * mod_columns].astype(F32)
    modulation = modulation.reshape(4, width)
    attn_gate = jnp.tanh(modulation[1])
    ffn_gate = jnp.tanh(modulation[3])
    vec = jnp.stack(
        [
            norm_gains[0] * (1.0 + modulation[0]),
            norm_gains[1] * attn_gate,
            norm_gains[2] * (1.0 + modulation[2]),
            norm_gains[3] * ffn_gate,
        ]
    )
    vec = jnp.pad(vec, ((0, 4), (0, 0)))
    embed = embed_weight.reshape(taps, width)
    unpatch = unpatch_weight.transpose(0, 1, 3, 2).reshape(taps, width)
    raw = qkv_project(patches, embed, vec, qkv_whole)
    raw = raw.reshape(3, heads, HD, TOKENS)
    caption_rows = caption[0]
    text_raw = text_project(at, text_pieces, caption_rows)
    text_raw = text_raw.reshape(2, heads, HD, caption_rows.shape[0])
    head_gains = lax.dynamic_slice(norm_gains, (4, row_at * local_width), (3, local_width)).reshape(
        3, heads, HD, 1
    )
    head_gates = jnp.tanh(lax.dynamic_slice_in_dim(cross_gate, row_at * heads, heads))
    cap = lax.dynamic_slice_in_dim(cap_len, col_at, 1)
    table = jnp.asarray(rope_tables())
    mixed, lse = attend(raw, text_raw, head_gains, table, cap, head_gates)

    mixed_pieces = from_chips(mixed)
    reached = lax.optimization_barrier((*mixed_pieces, *out_pieces))
    mixed_whole = with_other_core(reached[:4])
    out_whole = with_other_core(reached[4:])
    attn, second, gate_up, hidden, ffn_own, ffn_other = forward(
        at, mixed_whole, out_whole, patches, embed, vec, ffn_whole
    )
    place = tile_places(False)
    cot_own = lax.dynamic_slice_in_dim(cot_taps, row_at * BLOCK, BLOCK, 1)
    d_ffn_own, ffn_out = own_grad(
        to_chips(sum_cores(ffn_own, ffn_other)), cot_own, unpatch, vec
    )
    d_ffn_near = from_chips(d_ffn_own)
    activation_field, unpatch_sum, own_sums = own_block(
        at, ffn_out, attn, patches, cot_taps, embed, unpatch, vec, place
    )
    d_ffn_near = lax.optimization_barrier((*d_ffn_near, activation_field))[:4]
    d_ffn, d_gate_up, d_attn, d_mid, mixed_own, mixed_other, back_sums = backward(
        at, with_other_core(d_ffn_near), ffn_whole, out_whole, gate_up, attn, patches, embed, cot_taps,
        unpatch, vec,
    )
    mixed_near = sum_cores(mixed_own, mixed_other)
    mixed_terms = to_chips(mixed_near)
    text_rows = text_kv_weight.shape[1]
    grads, out_near, out_far = weight_grads(
        after(second, *mixed_near), d_gate_up, d_ffn, hidden, mixed_whole, d_attn, text_rows
    )
    *mixed_terms, grads, out_near, out_far = lax.optimization_barrier(
        (*mixed_terms, grads, out_near, out_far)
    )
    d_mixed = sum(term.astype(F32) for term in mixed_terms).astype(BF16)
    d_mixed = d_mixed.reshape(heads, HD, TOKENS)
    out_near = sum_cores(out_near, out_far)
    out_apart = lax.ppermute(out_near[2], "row", row_pairs_to(2, 0))

    grads, dq_text, d_text_head = text_back(
        raw, text_raw, head_gains, table, lse, d_mixed, cap, head_gates, caption_rows,
        after(grads, *out_near),
    )
    dq_text, grads, out_apart, *out_near = lax.optimization_barrier(
        (dq_text, grads, out_apart, *out_near)
    )
    d_raw, d_head = attend_back(raw, head_gains, table, lse, d_mixed, dq_text)
    out_beside = [lax.ppermute(out_near[d], "row", row_pairs_to(d, 0)) for d in (1, 3)]
    d_raw, *out_terms = lax.optimization_barrier((d_raw, out_near[0], out_apart, *out_beside))
    out_sum = sum(term.astype(F32) for term in out_terms)
    d_raw = d_raw.reshape(3, local_width, TOKENS)
    own_pack, other_pack, *head_parts = first_back(
        at, head_gates, patches, embed, vec, qkv_whole, d_raw, d_mid, place, out_sum, unpatch_sum,
        back_sums, own_sums, d_head, d_text_head, norm_gains, modulation, activation_field,
    )
    beside = [lax.ppermute(head_parts[d], "col", col_pairs_to(0, d)) for d in (1, 3)]

    row_terms = to_chips(sum_cores(own_pack, other_pack))
    row_pack = sum(term.astype(F32) for term in row_terms)
    fields = row_pack[CHUNK : CHUNK + 2 * channels].T.reshape(COLS, 8, 2 * channels)
    mod_sums = row_pack[CHUNK + 2 * channels : CHUNK + 2 * channels + 6].reshape(COLS, 8, 6)
    fields = jnp.concatenate([fields, mod_sums], axis=2).astype(BF16)
    fields = jnp.pad(fields, ((0, 0), (0, 0), (0, 128 - fields.shape[2])))
    shared = row_pack[:CHUNK].astype(BF16).reshape(COLS, CHUNK // COLS, 128)
    col_pack = lax.all_to_all(jnp.concatenate([shared, fields], axis=1), "col", 0, 0)
    col_pack, left, right = lax.optimization_barrier((col_pack, *beside))
    shared = jnp.sum(col_pack[:, : CHUNK // COLS].astype(F32), axis=0)
    shared, apart = lax.optimization_barrier(
        (send_all(shared.astype(BF16), "col"), head_parts[2])
    )
    shared = send_all(shared, "row").reshape(-1, 128)
    apart = lax.ppermute(apart, "col", col_pairs_to(0, 2))
    head_near = sum(term.astype(F32) for term in (head_parts[0], left, apart, right)).astype(BF16)
    shared = shared[: 12 * SHARED].reshape(12, SHARED, 128).astype(F32)
    fields = col_pack[:, CHUNK // COLS :]
    activation = fields[:, :, :channels].reshape(latent.shape)
    latent_grad = fields[:, :, channels : 2 * channels].reshape(latent.shape)
    modulate_grad = lax.dot_general(
        cond_low.astype(F32),
        fields[:, :, 2 * channels : 2 * channels + 6].reshape(images, mod_columns).astype(F32),
        (((0,), (0,)), ((), ())),
        precision=lax.Precision.HIGHEST,
        preferred_element_type=F32,
    )
    embed_grad = shared[:, :taps].transpose(1, 0, 2).reshape(embed_weight.shape)
    unpatch_grad = shared[:, taps : 2 * taps].reshape(12, 3, 3, channels, 128)
    unpatch_grad = unpatch_grad.transpose(1, 2, 0, 4, 3).reshape(unpatch_weight.shape)
    gains_grad = shared[:, 2 * taps : 2 * taps + 7].transpose(1, 0, 2).reshape(7, width)
    gate_grad = shared[0, 2 * taps + 7, :HEADS]

    part = width // COLS
    grads = lax.psum_scatter(
        grads.reshape(-1, 2 * local_width), "col", scatter_dimension=0, tiled=True
    ).astype(F32)
    text_kv_grad = jnp.stack([grads[:text_rows, :local_width], grads[:text_rows, local_width:]])
    ffn_total = jnp.concatenate(
        [grads[first : first + part] for first in range(text_rows, grads.shape[0], part)], axis=1
    )
    gate_up_grad = jnp.stack(
        [ffn_total[:, :hidden_width], ffn_total[:, hidden_width : 2 * hidden_width]]
    )
    down_grad = ffn_total[:, 2 * hidden_width :].T
    head_terms, others = lax.optimization_barrier(
        (
            along_col(head_near, along_y),
            (
                activation, latent_grad, embed_grad, modulate_grad, gains_grad, gate_grad,
                text_kv_grad, gate_up_grad, down_grad, unpatch_grad,
            ),
        )
    )
    (
        activation, latent_grad, embed_grad, modulate_grad, gains_grad, gate_grad,
        text_kv_grad, gate_up_grad, down_grad, unpatch_grad,
    ) = others
    head_total = sum(term.astype(F32) for term in head_terms)
    first, second_half = head_total[:, :local_width], head_total[:, local_width:]
    qkv_grad = jnp.stack([first[:part], second_half[:part], first[part:]])
    out_grad = second_half[part:].T
    return (
        activation, latent_grad, embed_grad, modulate_grad, gains_grad, gate_grad,
        qkv_grad, text_kv_grad, out_grad, gate_up_grad, down_grad, unpatch_grad,
    )


def solution(mesh):
    placed = (
        P(None, "row", "col", None),
        P(),
        P("col", None, None),
        P(),
        P(None, "row", "col", None),
        P(),
        P(None, ("row", "col")),
        P(),
        P(),
        P(None, "col", "row"),
        P(None, "col", "row"),
        P("row", "col"),
        P(None, "col", "row"),
        P("row", "col"),
        P(),
    )
    return jax.shard_map(
        local,
        mesh=mesh,
        in_specs=placed,
        out_specs=(
            P(None, "row", "col", None),
            P(None, "row", "col", None),
            P(),
            P(None, ("row", "col")),
            P(),
            P(),
            P(None, "col", "row"),
            P(None, "col", "row"),
            P("row", "col"),
            P(None, "col", "row"),
            P("row", "col"),
            P(),
        ),
        check_vma=False,
    )
```
